32 devices in a mesh: groups: 2 (over y), blk: 4 (over z), len: 2 (over x), wall: 2 (over core).
Axes of the slice: x: 2, y: 2, z: 4, core: 2. Of those that a mesh axis runs over, the one named last changes fastest.
Arguments:
- adj_next: float32 [128, 64, 256], P(('groups', 'wall'), 'blk', 'len'), parts along dimension 0, may hold values from -6 to 6
- ion_slope: float32 [128, 64, 256], P(('groups', 'wall'), 'blk', 'len'), parts along dimension 0, may hold values from 0.1 to 3
- misfit: float32 [128, 64, 256], P(('groups', 'wall'), 'blk', 'len'), parts along dimension 0, may hold values from -8 to 8
- tissue_mask: int32 [128, 64, 256], P(('groups', 'wall'), 'blk', 'len'), parts along dimension 0, may hold values 0 or 1
- patch_ids: int32 [4, 64, 256], P(('groups', 'wall'), 'blk', 'len'), parts along dimension 0, may hold values from 0 to 31
- owner_map: int32 [64], P('groups'), parts along dimension 0, may hold values from 0 to 15, as said below
Outputs:
- adj_prev: float32 [128, 64, 256], P(('groups', 'wall'), 'blk', 'len'), parts along dimension 0
- potential: float32 [128, 64, 256], P(('groups', 'wall'), 'blk', 'len'), parts along dimension 0
- patch_grad: float32 [32, 2], P(('groups', 'blk', 'len', 'wall')), parts along dimension 0
The draws below stay inside these ranges and needn't reach their ends.
There are 2 independent parts, one for each index of `groups`. The reference program is written for one: setup_inputs(seed, part) draws one part's arguments, and reference() takes and returns one part's arrays. A program takes and returns all parts, laid end to end along the dimension named above; each array names one. Nothing has to cross between parts.
Inputs may be any that keep to these rules, and one draw needn't show every extreme that they name: `owner_map`: every device index owns exactly 2 patches.
All inputs are finite; a program needn't handle non-finite values. No bound on the sum of `tissue_mask` on one device may be relied on, other than what follows from the above.
Results may differ from the reference program's by a relative error of at most 0.00011.
Values sent between devices are 32-bit elements; how exact they have to be, the bound alone decides.
No kernel may reach another device: no remote copies, remote signals or barrier semaphores. Data moves between devices by JAX's collectives and lax.ppermute only.
A program may use at most 128 MiB of HBM per device.

```python
import math
import jax
import jax.numpy as jnp

CC = 16
CL = 128
LEVELS = 4
SWEEPS = 2
SLOTS = 2
NW = 64
NC = 64
NL = 256
ELECTRODES = 32
N_BLK = 4
N_LEN = 2
N_WALL = 2


def draw_misfit(key, part):
    key = jax.random.fold_in(key, 7)
    first = jax.random.fold_in(key, 0)
    return jnp.clip(jax.random.normal(first, (NW, NC, NL), jnp.float32), -5.0, 5.0)


def draw_owner_map(key, part):
    key = jax.random.fold_in(key, 11)
    order = jax.random.permutation(key, SLOTS * N_BLK * N_LEN * N_WALL)
    return (order // SLOTS).astype(jnp.int32)


def set_ends(entries, rng, smallest, high):
    dims = entries.shape
    place = [jax.random.randint(jax.random.fold_in(rng, axis), (), 0, dims[axis]) for axis in range(len(dims))]
    entries = entries.at[tuple(place)].set(smallest)
    longest = dims.index(max(dims))
    place[longest] = (place[longest] + 1) % dims[longest]
    return entries.at[tuple(place)].set(high)


def block_scale(key, shape, cuts, smallest, largest):
    def one(dim, parts):
        steps = jax.random.uniform(jax.random.fold_in(jax.random.fold_in(key, 6), dim), (parts,), jnp.float32, smallest / len(cuts), largest / len(cuts))
        return jnp.repeat(jnp.exp(steps), shape[dim] // parts).reshape((-1,) + (1,) * (len(shape) - dim - 1))

    factor_of = one(*cuts[0])
    for cut in cuts[1:]:
        factor_of = factor_of * one(*cut)
    return factor_of


def bell_draw(own_key, shape, width, bound, cuts=(), kind=jnp.bfloat16):
    drawn = width * jax.random.normal(own_key, shape, jnp.float32)
    if cuts:
        drawn = drawn * block_scale(own_key, shape, cuts, -0.22, 0.18)
    return jnp.clip(drawn, -bound, bound).astype(kind)


def setup_inputs(seed: int = 0, part: int = 0) -> dict:
    key_list = jax.random.split(jax.random.key(seed), 7)
    own_keys = jax.random.split(jax.random.fold_in(key_list[6], part), 7)
    return {
        "adj_next": bell_draw(own_keys[0], (NW, NC, NL), 1.0, 6.0, ((0, 2), (1, 4), (2, 2)), jnp.float32),
        "ion_slope": jnp.clip(jnp.exp(math.log(3.0) - 3.4011974 * jax.random.uniform(own_keys[1], (NW, NC, NL), jnp.float32) ** block_scale(own_keys[1], (NW, NC, NL), ((0, 2), (1, 4), (2, 2)), -0.2, 0.2)), 0.1, 3.0),
        "misfit": draw_misfit(jax.random.fold_in(jax.random.fold_in(key_list[6], part), 71), part),
        "tissue_mask": set_ends((jax.random.randint(own_keys[3], (NW, NC, NL), 0, 10) < 9).astype(jnp.int32), jax.random.fold_in(own_keys[3], 1), 0, 1),
        "patch_ids": set_ends(jax.random.randint(own_keys[4], (2, NC, NL), 0, ELECTRODES), jax.random.fold_in(own_keys[4], 1), 0, ELECTRODES - 1).astype(jnp.int32),
        "owner_map": draw_owner_map(jax.random.fold_in(jax.random.fold_in(key_list[6], part), 71), part),
    }


SI = (0.6, 1.0, 3.0)
SE = (0.8, 1.2, 2.0)
SHIFT = 0.002
OMEGA = 0.8
DT = 0.1


def stencil(center, wp, wm, cp, cm, lp, lm, coef):
    return coef[0] * (2.0 * center - wp - wm) + coef[1] * (2.0 * center - cp - cm) + coef[2] * (2.0 * center - lp - lm)


def neighbours(field):
    wpad = jnp.pad(field, ((1, 1), (0, 0), (0, 0)))
    cpad = jnp.concatenate([field[:, -1:], field, field[:, :1]], 1)
    lpad = jnp.pad(field, ((0, 0), (0, 0), (1, 1)))
    return wpad[2:], wpad[:-2], cpad[:, 2:], cpad[:, :-2], lpad[:, :, 2:], lpad[:, :, :-2]


def operate(field, coef):
    return stencil(field, *neighbours(field), coef)


def level_coef(level):
    return tuple((SI[i] + SE[i]) / 4.0 ** level for i in range(3))


def level_diag(level):
    return SHIFT + 2.0 * (SI[0] + SE[0] + SI[1] + SE[1] + SI[2] + SE[2]) / 4.0 ** level


def elliptic(field, level):
    return SHIFT * field + operate(field, level_coef(level))


def restrict(field):
    a, b, c = field.shape
    return field.reshape(a // 2, 2, b // 2, 2, c // 2, 2).mean(axis=(1, 3, 5))


def prolong(field):
    return jnp.repeat(jnp.repeat(jnp.repeat(field, 2, 0), 2, 1), 2, 2)


def vcycle(source):
    sources = [source]
    iterates = []
    for level in range(LEVELS - 1):
        guess = (OMEGA * sources[level]) / level_diag(level)
        left = sources[level] - elliptic(guess, level)
        iterates.append(guess)
        sources.append(restrict(left))
    last = LEVELS - 1
    guess = (OMEGA * sources[last]) / level_diag(last)
    for sweep in range(SWEEPS):
        guess = guess + (OMEGA * (sources[last] - elliptic(guess, last))) / level_diag(last)
    for level in range(LEVELS - 2, -1, -1):
        guess = iterates[level] + prolong(guess)
        guess = guess + (OMEGA * (sources[level] - elliptic(guess, level))) / level_diag(level)
    return guess


def reference(adj_next, ion_slope, misfit, tissue_mask, patch_ids, owner_map):
    maskf = tissue_mask.astype(jnp.float32)
    lam = adj_next - DT * maskf * (operate(adj_next, SI) + ion_slope * adj_next)
    source = operate(lam, SI) + misfit
    potential = vcycle(source)
    adj_prev = lam - DT * maskf * operate(potential, SI)
    surface = jnp.stack([potential[0], potential[-1]])
    electrodes = owner_map.shape[0]
    sums = jax.ops.segment_sum(surface.reshape(-1), patch_ids.reshape(-1), num_segments=electrodes)
    sums = sums * (1.0 / (2.0 * CC * CL / SLOTS) ** 0.5)
    owners = electrodes // SLOTS
    onehot = (owner_map[:, None] == jnp.arange(owners, dtype=jnp.int32)[None, :]).astype(jnp.int32)
    ranks = jnp.sum(onehot * (jnp.cumsum(onehot, axis=0) - onehot), axis=1).astype(jnp.int32)
    target = owner_map * SLOTS + ranks
    patch_grad = jnp.zeros((electrodes,), jnp.float32).at[target].set(sums).reshape(owners, SLOTS)
    return adj_prev, potential, patch_grad
```

```python
import functools

import jax
import jax.numpy as jnp
from jax import lax
from jax.experimental import pallas as pl
from jax.experimental.pallas import tpu as pltpu
from jax.sharding import PartitionSpec as P

SWEEPS = 2
SI = (0.6, 1.0, 3.0)
SE = (0.8, 1.2, 2.0)
SHIFT = 0.002
OMEGA = 0.8
DT = 0.1
H = 4
LANES = 128
HIGHEST = lax.Precision.HIGHEST
F32 = jnp.float32


def level_coef(level):
    return tuple((SI[i] + SE[i]) / 4.0**level for i in range(3))


def level_diag(level):
    return SHIFT + 2.0 * sum(level_coef(level))


def level_step(level):
    return OMEGA / level_diag(level)


def lane_of(shape):
    return lax.broadcasted_iota(jnp.int32, shape, len(shape) - 1)


def before(m, e):
    first = lane_of(m.shape) == 0
    rm, re = pltpu.roll(m, 1, 1), pltpu.roll(e, 1, 1)
    return jnp.where(first, re, rm), jnp.where(first, rm, re)


def after(m, e):
    last = lane_of(m.shape) == LANES - 1
    rm, re = pltpu.roll(m, LANES - 1, 1), pltpu.roll(e, LANES - 1, 1)
    return jnp.where(last, re, rm), jnp.where(last, rm, re)


def beside_lanes(m, e):
    bm, be = before(m, e)
    am, ae = after(m, e)
    return bm + am, be + ae


def beside_lanes_main(m, e):
    lane = lane_of(m.shape)
    left = jnp.where(lane == 0, pltpu.roll(e, 1, 1), pltpu.roll(m, 1, 1))
    right = jnp.where(lane == LANES - 1, pltpu.roll(e, LANES - 1, 1), pltpu.roll(m, LANES - 1, 1))
    return left + right


def beside_rows(x, row_before, row_after):
    rows = x.shape[0]
    row = lax.broadcasted_iota(jnp.int32, x.shape, 0)
    low = jnp.where(row == 0, row_before, pltpu.roll(x, 1, 0))
    high = jnp.where(row == rows - 1, row_after, pltpu.roll(x, rows - 1, 0))
    return low + high


def beside_dense(x):
    return pltpu.roll(x, 1, 0) + pltpu.roll(x, x.shape[0] - 1, 0)


def plane(ref, i, rows):
    return ref[pl.ds(pl.multiple_of(i * rows, rows), rows), :]


def set_plane(ref, i, rows, value):
    ref[pl.ds(pl.multiple_of(i * rows, rows), rows), :] = value


def loop(low, high, step, unroll):
    def wrapped(i, carry):
        step(i)
        return carry

    lax.fori_loop(low, high, wrapped, 0, unroll=min(unroll, high - low))


def pack_faces(n_len, adj, ion, mask, mis, wall_out, *outs):
    W, C, L = adj.shape
    arrays = (adj, ion, mask, mis)
    wall, length = lax.axis_index("wall"), lax.axis_index("len")
    base = jnp.where(wall == 0, W - H, 0)
    group = lane_of((C, LANES)) // H
    n_dir = 1 if n_len == 2 else 2
    strips, corners = outs[:n_dir], outs[n_dir:]
    turns = [jnp.where(length == 0, H, 0)] if n_dir == 1 else [H, 0]
    for d in range(n_dir):
        corner = jnp.zeros((C, LANES), F32)
        for a, ref in enumerate(arrays):
            strip = jnp.zeros((C, LANES), F32)
            for w in range(W):
                turned = pltpu.roll(ref[w].astype(F32), lax.rem(H * w + turns[d], LANES), 1)
                strip = jnp.where(group == w, turned, strip)
            strips[d][a] = strip
            for p in range(H):
                face = ref[base + p].astype(F32)
                if d == 0:
                    wall_out[a, p] = face
                slot = a * H + p
                turned = pltpu.roll(face, lax.rem(H * slot + turns[d], LANES), 1)
                corner = jnp.where(group == slot, turned, corner)
        corners[d][...] = corner


def spots(m_ref, e_ref, i, rows, coef):
    m, e = plane(m_ref, i, rows), plane(e_ref, i, rows)
    wm = plane(m_ref, i - 1, rows) + plane(m_ref, i + 1, rows)
    we = plane(e_ref, i - 1, rows) + plane(e_ref, i + 1, rows)
    lm, le = beside_lanes(m, e)
    cm, ce = beside_rows(m, 0.0, 0.0), beside_rows(e, 0.0, 0.0)
    double = 2.0 * sum(coef)
    dm = double * m - coef[0] * wm - coef[1] * cm - coef[2] * lm
    de = double * e - coef[0] * we - coef[1] * ce - coef[2] * le
    return m, e, dm, de


def sector(n_len, adj, ion, mask, mis, wall_in, *rest):
    W, C, L = adj.shape
    N = W + 2 * H
    n_dir = 1 if n_len == 2 else 2
    strips, corners, rest = rest[:n_dir], rest[n_dir : 2 * n_dir], rest[2 * n_dir :]
    qm, pm, pe, to_next, to_prev = rest[:5]
    xm, xe, qe = rest[5:9], rest[9:13], rest[13]
    wall, length = lax.axis_index("wall"), lax.axis_index("len")
    lane = lane_of((C, LANES))
    if n_dir == 1:
        offs, valid = [jnp.where(length == 0, 0, LANES - H)], [True]
    else:
        offs, valid = [0, LANES - H], [length < n_len - 1, length > 0]
    seen = [jnp.logical_and(lax.rem(lane - off + LANES, LANES) < H, ok) for off, ok in zip(offs, valid)]

    def rim(packed, base):
        out = jnp.zeros((C, LANES), F32)
        for d in range(n_dir):
            out = jnp.where(seen[d], pltpu.roll(packed[d], lax.rem(offs[d] - base + LANES, LANES), 1), out)
        return out

    here = jnp.where(wall == 0, N - H, 0)
    none = N - H - here
    zero = jnp.zeros((C, LANES), F32)
    for a, ref in enumerate((adj, ion, mask, mis)):
        packed = [strip[a] for strip in strips]
        for w in range(W):
            set_plane(xm[a], w + H, C, ref[w].astype(F32))
            set_plane(xe[a], w + H, C, rim(packed, H * w))
        packed = [corner[...] for corner in corners]
        for p in range(H):
            set_plane(xm[a], here + p, C, wall_in[a, p])
            set_plane(xe[a], here + p, C, rim(packed, H * (a * H + p)))
            set_plane(xm[a], none + p, C, zero)
            set_plane(xe[a], none + p, C, zero)
    for i in (0, N - 1):
        set_plane(qm, i, C, zero)
        set_plane(qe, i, C, zero)
    for i in (0, 1, N - 2, N - 1):
        set_plane(pm, i, C, zero)
        set_plane(pe, i, C, zero)

    def parabolic(i):
        m, e, dm, de = spots(xm[0], xe[0], i, C, SI)
        set_plane(qm, i, C, m - DT * plane(xm[2], i, C) * (dm + plane(xm[1], i, C) * m))
        set_plane(qe, i, C, e - DT * plane(xe[2], i, C) * (de + plane(xe[1], i, C) * e))

    loop(1, N - 1, parabolic, 2)

    def elliptic_source(i):
        m, e, dm, de = spots(qm, qe, i, C, SI)
        set_plane(pm, i, C, plane(xm[3], i, C) + dm)
        set_plane(pe, i, C, plane(xe[3], i, C) + de)

    loop(2, N - 2, elliptic_source, 2)

    pos_of = lane_of((8, LANES)) // 8
    tiles = N // 8
    for out, near, second in ((to_next, C - 1, C - 2), (to_prev, 0, 1)):
        for q, (m, r) in enumerate(((xm[0], near), (xm[2], near), (qm, near), (pm, near), (pm, second))):
            out[q * N : (q + 1) * N, :] = m[pl.ds(r, N, stride=C), :]
        packs = [jnp.zeros((8, LANES), F32), jnp.zeros((8, LANES), F32)]
        for q, e in enumerate((xe[0], xe[2], qe, pe)):
            dense = e[pl.ds(near, N, stride=C), :]
            for s in range(tiles):
                t = q * tiles + s
                turned = pltpu.roll(dense[8 * s : 8 * s + 8], (H + 8 * (t % 16)) % LANES, 1)
                packs[t // 16] = jnp.where(pos_of == t % 16, turned, packs[t // 16])
        out[5 * N : 5 * N + 8, :] = packs[0]
        out[5 * N + 8 : 5 * N + 16, :] = packs[1]


def unpacked(ref, N):
    lane = lane_of((8, LANES))
    rim = jnp.logical_or(lane < H, lane >= LANES - H)
    tiles = N // 8
    mains = [ref[q * N : (q + 1) * N, :] for q in range(5)]
    packs = [ref[5 * N : 5 * N + 8, :], ref[5 * N + 8 : 5 * N + 16, :]]
    rims = []
    for q in range(4):
        parts = []
        for s in range(tiles):
            t = q * tiles + s
            turned = pltpu.roll(packs[t // 16], (2 * LANES - H - 8 * (t % 16)) % LANES, 1)
            parts.append(jnp.where(rim, turned, 0.0))
        rims.append(jnp.concatenate(parts, 0))
    return [(mains[q], rims[q]) for q in range(4)] + [mains[4]]


def lateral(pair):
    m, e = pair
    lm, le = beside_lanes(m, e)
    double = 2.0 * sum(SI)
    return (
        double * m - SI[0] * beside_dense(m) - SI[2] * lm,
        double * e - SI[0] * beside_dense(e) - SI[2] * le,
    )


def rim_lanes(lane, length, n_len):
    return jnp.logical_or(
        jnp.logical_and(lane < H, length < n_len - 1),
        jnp.logical_and(lane >= LANES - H, length > 0),
    )


def source_rows(own, other):
    adj_o, mask_o, q_o, _, _ = own
    adj_n, mask_n, q_n, p_n, second_n = other
    step = DT * SI[1]
    delta_o = [step * mask_o[k] * adj_n[k] for k in range(2)]
    delta_n = [step * mask_n[k] * adj_o[k] for k in range(2)]
    lat_o, lat_n = lateral(delta_o), lateral(delta_n)
    near = [lat_o[k] - SI[1] * (q_n[k] + delta_n[k]) for k in range(2)]
    second = [-SI[1] * delta_o[k] for k in range(2)]
    halo = [p_n[k] + lat_n[k] - SI[1] * (q_o[k] + delta_o[k]) for k in range(2)]
    halo_second = second_n - SI[1] * delta_n[0]
    return near, second, halo, halo_second, delta_o[0]


def residual(electrodes, n_len, n_wall, pm, pe, ids, own_next, own_prev, from_next, from_prev, *rest):
    bm, be, rows_n, rows_p, message = rest[:5]
    surf, pairs, sums = rest[5:]
    _, C, L = ids.shape
    N = pm.shape[0] // C
    W = N - 2 * H
    wall, length = lax.axis_index("wall"), lax.axis_index("len")
    lane = lane_of((C, LANES))
    rim = rim_lanes(lane, length, n_len)

    def inside(i):
        w = wall * W + i - H
        return jnp.logical_and(w >= 0, w < n_wall * W)

    def clear(i):
        ok = inside(i)
        set_plane(bm, i, C, jnp.where(ok, plane(pm, i, C), 0.0))
        set_plane(be, i, C, jnp.where(jnp.logical_and(rim, ok), plane(pe, i, C), 0.0))

    loop(0, N, clear, 4)

    dense_lane = lane_of((N, LANES))
    ok_m = inside(lax.broadcasted_iota(jnp.int32, (N, LANES), 0))
    ok_e = jnp.logical_and(ok_m, rim_lanes(dense_lane, length, n_len))
    for own, other, out, near_at, second_at in (
        (own_next, from_next, rows_n, C - 1, C - 2),
        (own_prev, from_prev, rows_p, 0, 1),
    ):
        near, second, halo, halo_second, delta = source_rows(unpacked(own, N), unpacked(other, N))
        for k, (ref, ok) in enumerate(((bm, ok_m), (be, ok_e))):
            for at, extra in ((near_at, near[k]), (second_at, second[k])):
                spot = pl.ds(at, N, stride=C)
                ref[spot, :] = ref[spot, :] + jnp.where(ok, extra, 0.0)
        out[0] = jnp.where(ok_m, halo[0], 0.0)
        out[1] = jnp.where(ok_e, halo[1], 0.0)
        out[2] = jnp.where(ok_m, halo_second, 0.0)
        out[3] = delta

    coef, k0 = level_coef(0), level_step(0)

    def left(i):
        m, e = plane(bm, i, C), plane(be, i, C)
        wm = plane(bm, i - 1, C) + plane(bm, i + 1, C)
        cm = beside_rows(m, rows_p[0, pl.ds(i, 1), :], rows_n[0, pl.ds(i, 1), :])
        lm = beside_lanes_main(m, e)
        return (1.0 - OMEGA) * m + k0 * (coef[0] * wm + coef[1] * cm + coef[2] * lm)

    def pair(q):
        i = 2 * q + H
        first, second = left(i), left(i + 1)
        set_plane(pairs, q, C, first + second)

        @pl.when(q == 0)
        def _():
            surf[0] = first

        @pl.when(q == W // 2 - 1)
        def _():
            surf[1] = second

    loop(0, W // 2, pair, 2)

    half = W * C // 8
    z = pairs[pl.ds(0, 2 * half, stride=2), :] + pairs[pl.ds(1, 2 * half, stride=2), :]
    src = lax.broadcasted_iota(jnp.int32, (LANES, LANES), 0) // 2
    dst = lax.broadcasted_iota(jnp.int32, (LANES, LANES), 1)
    low = jnp.where(src == dst, 0.125, 0.0).astype(F32)
    high = jnp.where(src == dst - LANES // 2, 0.125, 0.0).astype(F32)
    message[0:half, :] = jnp.dot(z[:half], low, precision=HIGHEST, preferred_element_type=F32) + jnp.dot(
        z[half:], high, precision=HIGHEST, preferred_element_type=F32
    )
    patch = ids[0]
    message[half : half + C, :] = patch.astype(F32)

    b_surf = plane(bm, jnp.where(wall == 0, H, W + H - 1), C)
    y = k0 * (b_surf + jnp.where(wall == 0, surf[0], surf[1]))
    wide = sums.shape[0]
    sums[...] = jnp.zeros(sums.shape, F32)

    def one(e):
        sums[pl.ds(e, 1), :] = jnp.sum(jnp.where(patch == e, y, 0.0), axis=0, keepdims=True)

    loop(0, electrodes, one, 8)
    totals = lax.dot_general(
        jnp.ones((8, LANES), F32), sums[...], (((1,), (1,)), ((), ())), precision=HIGHEST, preferred_element_type=F32
    )
    message[half + C : half + C + 8, :] = jnp.zeros((8, LANES), F32)
    for t in range(wide // LANES):
        message[half + C + t : half + C + t + 1, :] = totals[0:1, t * LANES : (t + 1) * LANES]


def around(x, by):
    rows, lanes = x.shape
    lane = lane_of(x.shape)
    c = pltpu.roll(x, by, 0) + pltpu.roll(x, rows - by, 0)
    l = jnp.where(lane < by, 0.0, pltpu.roll(x, by, 1)) + jnp.where(
        lane >= lanes - by, 0.0, pltpu.roll(x, lanes - by, 1)
    )
    return c, l


def twins(x, by):
    rows, lanes = x.shape
    row = lax.broadcasted_iota(jnp.int32, x.shape, 0)
    lane = lane_of(x.shape)
    x = x + jnp.where((row & by) == 0, pltpu.roll(x, rows - by, 0), pltpu.roll(x, by, 0))
    return x + jnp.where((lane & by) == 0, pltpu.roll(x, lanes - by, 1), pltpu.roll(x, by, 1))


def solve(sizes, relative, electrodes, *refs):
    n_blk, n_len, n_wall = sizes
    count = n_len * n_wall
    blocks, refs = refs[:count], refs[count:]
    bm, be, rows_n, rows_p, qm, mask, owner, adj_prev, potential, patch_grad = refs[:10]
    b1, x1, b2, x2, b3, x3, wide_m, wide_e, thin, hx, xm, xe, hp, tm, te, sheet = refs[10:]
    W, C, L = mask.shape
    N = W + 2 * H
    W1, C1 = W // 2, C // 2
    planes, NC1, NL1 = b1.shape
    planes -= 2
    blk, length, wall = lax.axis_index("blk"), lax.axis_index("len"), lax.axis_index("wall")
    half = W1 // 2
    middle = LANES // 2
    lane8 = lane_of((C1, LANES))

    def blk_of(d):
        return lax.rem(blk - d + n_blk, n_blk) if relative else d

    def length_of(j):
        return (length + j) % n_len if n_len == 2 else j

    zero1 = jnp.zeros((NC1, NL1), F32)
    for ref in (b1, x1, b2, x2, b3, x3):
        ref[0] = zero1
        ref[ref.shape[0] - 1] = zero1

    for v in range(n_wall):
        wall_s = (wall + v) % n_wall
        mine = blocks[v * n_len : (v + 1) * n_len]

        def unpack(d):
            at = pl.ds(pl.multiple_of(C1 * blk_of(d), C1), C1)
            for t in range(n_len // 2):
                one, two = mine[2 * t], mine[2 * t + 1]
                for i in range(half):
                    a, b = one[d, i * C1 : (i + 1) * C1, :], two[d, i * C1 : (i + 1) * C1, :]
                    if n_len == 2:
                        a, b = jnp.where(length == 0, a, b), jnp.where(length == 0, b, a)
                    spot = 1 + wall_s * W1 + i
                    lanes = slice(t * LANES, (t + 1) * LANES)
                    b1[spot, at, lanes] = jnp.where(lane8 < middle, a, pltpu.roll(b, middle, 1))
                    b1[spot + half, at, lanes] = jnp.where(lane8 < middle, pltpu.roll(a, middle, 1), b)

        loop(0, n_blk, unpack, 4)

    def swept(x, wsum, b, level):
        coef, k = level_coef(level), level_step(level)
        c, l = around(x, 2 ** (level - 1))
        total = coef[0] * wsum + coef[1] * c + coef[2] * l
        return total, k

    def left(ref, i, level):
        b = ref[i]
        total, k = swept(b, ref[i - 1] + ref[i + 1], b, level)
        return (1.0 - OMEGA) * b + k * total

    def sweep(x_ref, b_ref, i, level):
        x = x_ref[i]
        total, k = swept(x, x_ref[i - 1] + x_ref[i + 1], None, level)
        return (1.0 - OMEGA) * x + k * (b_ref[i] + total)

    def down1(q):
        b2[1 + q] = 0.125 * twins(left(b1, 2 * q + 1, 1) + left(b1, 2 * q + 2, 1), 1)

    loop(0, planes // 2, down1, 4)

    def down2(q):
        b3[1 + q] = 0.125 * twins(left(b2, 2 * q + 1, 2) + left(b2, 2 * q + 2, 2), 2)

    loop(0, planes // 4, down2, 4)

    deep = planes // 8 * 2
    k3 = level_step(3)

    def start3(q):
        x3[1 + q] = k3 * b3[1 + q]

    loop(0, deep, start3, 8)
    for _ in range(SWEEPS):

        def sweep3(q):
            x2[1 + q] = sweep(x3, b3, 1 + q, 3)

        loop(0, deep, sweep3, 4)

        def back3(q):
            x3[1 + q] = x2[1 + q]

        loop(0, deep, back3, 8)

    k2 = level_step(2)

    def up2(q):
        coarse = x3[1 + q]
        x2[1 + 2 * q] = k2 * b2[1 + 2 * q] + coarse
        x2[2 + 2 * q] = k2 * b2[2 + 2 * q] + coarse

    loop(0, planes // 4, up2, 4)

    k1 = level_step(1)

    def up1(q):
        fine = sweep(x2, b2, 1 + q, 2)
        x1[1 + 2 * q] = k1 * b1[1 + 2 * q] + fine
        x1[2 + 2 * q] = k1 * b1[2 + 2 * q] + fine

    loop(0, planes // 2, up1, 4)

    def finish1(i):
        b1[1 + i] = sweep(x1, b1, 1 + i, 1)

    loop(0, planes, finish1, 4)

    lane = lane_of((NL1, LANES))
    source = lax.broadcasted_iota(jnp.int32, (NL1, LANES), 0)
    first = length * middle
    take_m = jnp.where(source == first + lane // 2, 1.0, 0.0).astype(F32)
    at_e = jnp.where(lane < H, middle + lane // 2, jnp.where(lane >= LANES - H, lane // 2 - middle, 4 * NL1))
    take_e = jnp.where(source == first + at_e, 1.0, 0.0).astype(F32)
    Q = W1 + 2

    def taken(sector_index, sel):
        rows = b1[pl.ds(wall * W1, Q), pl.ds(pl.multiple_of(sector_index * C1, C1), C1), :]
        return jnp.dot(rows.reshape(Q * C1, NL1), sel, precision=HIGHEST, preferred_element_type=F32)

    for wide, sel in ((wide_m, take_m), (wide_e, take_e)):
        value = taken(blk, sel)
        wide[pl.ds(0, Q * C1, stride=2), :] = value
        wide[pl.ds(1, Q * C1, stride=2), :] = value
    padded = 8 * ((Q + 7) // 8)
    thin[...] = jnp.zeros(thin.shape, F32)
    k0 = level_step(0)
    for side, (other, at, rows) in enumerate(
        ((lax.rem(blk + 1, n_blk), 0, rows_n), (lax.rem(blk + n_blk - 1, n_blk), C1 - 1, rows_p))
    ):
        for k, sel in enumerate((take_m, take_e)):
            thin[0 : Q * C1, :] = taken(other, sel)
            dense = thin[pl.ds(at, padded, stride=C1), :]
            hx[side, k] = jnp.zeros(hx.shape[2:], F32)
            hx[side, k, pl.ds(H - 2, padded, stride=2), :] = dense
            hx[side, k, pl.ds(H - 1, padded, stride=2), :] = dense

    def start0(i):
        q = (i - 2) // 2
        set_plane(xm, i, C, k0 * plane(bm, i, C) + plane(wide_m, q, C))
        set_plane(xe, i, C, k0 * plane(be, i, C) + plane(wide_e, q, C))

    loop(2, N - 2, start0, 4)
    for i in (0, 1, N - 2, N - 1):
        set_plane(xm, i, C, jnp.zeros((C, LANES), F32))
        set_plane(xe, i, C, jnp.zeros((C, LANES), F32))
    coef = level_coef(0)
    for side, (rows, at) in enumerate(((rows_n, C - 1), (rows_p, 0))):
        coarse = hx[side, 0, 0:N, :]
        near_m = k0 * rows[0] + coarse
        near_e = k0 * rows[1] + hx[side, 1, 0:N, :]
        far_m = k0 * rows[2] + coarse
        own = xm[pl.ds(at, N, stride=C), :]
        total = (
            coef[0] * beside_dense(near_m) + coef[1] * (far_m + own) + coef[2] * beside_lanes_main(near_m, near_e)
        )
        hp[side, 0] = near_m
        hp[side, 1] = near_e
        hp[side, 2] = (1.0 - OMEGA) * near_m + k0 * (rows[0] + total)

    rim = rim_lanes(lane_of((C, LANES)), length, n_len)

    def last(i):
        m, e = plane(xm, i, C), plane(xe, i, C)
        wm = plane(xm, i - 1, C) + plane(xm, i + 1, C)
        we = plane(xe, i - 1, C) + plane(xe, i + 1, C)
        lm, le = beside_lanes(m, e)
        at = pl.ds(i, 1)
        cm = beside_rows(m, hp[1, 0, at, :], hp[0, 0, at, :])
        ce = beside_rows(e, hp[1, 1, at, :], hp[0, 1, at, :])
        pm = (1.0 - OMEGA) * m + k0 * (plane(bm, i, C) + coef[0] * wm + coef[1] * cm + coef[2] * lm)
        pe = (1.0 - OMEGA) * e + k0 * (plane(be, i, C) + coef[0] * we + coef[1] * ce + coef[2] * le)
        w = wall * W + i - H
        ok = jnp.logical_and(w >= 0, w < n_wall * W)
        set_plane(tm, i, C, jnp.where(ok, pm, 0.0))
        set_plane(te, i, C, jnp.where(rim, pe, 0.0))

    loop(H - 1, N - H + 1, last, 2)

    row = lax.broadcasted_iota(jnp.int32, (C, LANES), 0)

    def finish0(w):
        i = w + H
        m, e = plane(tm, i, C), plane(te, i, C)
        at = pl.ds(i, 1)
        wm = plane(tm, i - 1, C) + plane(tm, i + 1, C)
        cm = beside_rows(m, hp[1, 2, at, :], hp[0, 2, at, :])
        lm = beside_lanes_main(m, e)
        lam = plane(qm, i, C)
        lam = lam + jnp.where(row == C - 1, rows_n[3, at, :], 0.0) + jnp.where(row == 0, rows_p[3, at, :], 0.0)
        moved = 2.0 * sum(SI) * m - SI[0] * wm - SI[1] * cm - SI[2] * lm
        adj_prev[w] = lam - DT * mask[w].astype(F32) * moved
        potential[w] = m

    loop(0, W, finish0, 2)

    NC, NL = sheet.shape[1:]
    twice_c = jnp.where(
        lax.broadcasted_iota(jnp.int32, (NC, NC1), 0) // 2 == lax.broadcasted_iota(jnp.int32, (NC, NC1), 1), 1.0, 0.0
    ).astype(F32)
    twice_l = jnp.where(
        lax.broadcasted_iota(jnp.int32, (NL1, NL), 1) // 2 == lax.broadcasted_iota(jnp.int32, (NL1, NL), 0), 1.0, 0.0
    ).astype(F32)
    for s, i in enumerate((1, planes)):
        p = jnp.dot(twice_c, b1[i], precision=HIGHEST, preferred_element_type=F32)
        p = jnp.dot(p, twice_l, precision=HIGHEST, preferred_element_type=F32)
        c, l = around(p, 1)
        sheet[s] = (1.0 - OMEGA) * p + k0 * (coef[0] * p + coef[1] * c + coef[2] * l)

    me = (blk * n_len + length) * n_wall + wall
    which = lax.broadcasted_iota(jnp.int32, (1, electrodes), 1).astype(F32)
    mine = owner[...] == me
    patches = (
        jnp.min(jnp.where(mine, which, float(electrodes))),
        jnp.max(jnp.where(mine, which, -1.0)),
    )
    spot = lax.broadcasted_iota(jnp.int32, (8, LANES), 0) * LANES + lane_of((8, LANES))
    spot = spot.astype(F32)
    start = half * C1
    totals = [jnp.zeros((C, LANES), F32) for _ in patches]
    small = [jnp.zeros((8, LANES), F32) for _ in patches]
    for v in range(n_wall):
        wall_s = (wall + v) % n_wall
        for j in range(n_len):
            ref = blocks[v * n_len + j]
            at_l = pl.ds(pl.multiple_of(length_of(j) * L, L), L)

            def add(d, carry):
                big, little = carry
                values = sheet[wall_s, pl.ds(pl.multiple_of(blk_of(d) * C, C), C), at_l]
                ids = ref[d, start : start + C, :]
                parts = ref[d, start + C : start + C + 8, :]
                big = [x + jnp.where(ids == e, values, 0.0) for x, e in zip(big, patches)]
                little = [x + jnp.where(spot == e, parts, 0.0) for x, e in zip(little, patches)]
                return big, little

            totals, small = lax.fori_loop(0, n_blk, add, (totals, small), unroll=min(4, n_blk))
    factor = 1.0 / (2.0 * C * L / 2) ** 0.5
    for r in range(2):
        patch_grad[0, r] = (jnp.sum(totals[r]) + jnp.sum(small[r])) * factor


def ring(x, axis, by):
    count = lax.axis_size(axis)
    return lax.ppermute(x, axis, [(i, (i + by) % count) for i in range(count)])


def call(kernel, outs, scratch, smem=(), **kwargs):
    specs = [pl.BlockSpec(memory_space=pltpu.SMEM if k in smem else pltpu.VMEM) for k in range(len(outs))]
    return pl.pallas_call(
        kernel,
        out_shape=[jax.ShapeDtypeStruct(shape, F32) for shape in outs],
        out_specs=specs,
        scratch_shapes=[pltpu.VMEM(shape, F32) for shape in scratch],
        compiler_params=pltpu.CompilerParams(vmem_limit_bytes=48 * 2**20),
        **kwargs,
    )


def body(adj_next, ion_slope, misfit, tissue_mask, patch_ids, owner_map):
    W, C, L = adj_next.shape
    n_blk, n_len, n_wall = lax.axis_size("blk"), lax.axis_size("len"), lax.axis_size("wall")
    electrodes = owner_map.shape[0]
    assert L == LANES and H * W == LANES and n_wall == 2 and electrodes == 2 * n_blk * n_len * n_wall
    N = W + 2 * H
    n_dir = 1 if n_len == 2 else 2
    raw = (adj_next, ion_slope, tissue_mask, misfit)

    faces = call(
        functools.partial(pack_faces, n_len), [(4, H, C, L)] + [(4, C, L)] * n_dir + [(C, L)] * n_dir, [], name="faces"
    )(*raw)
    wall_in = ring(faces[0], "wall", 1)
    if n_dir == 1:
        strips = [ring(faces[1], "len", 1)]
        corners = [across(faces[2])]
    else:
        strips = [ring(faces[2], "len", -1), ring(faces[1], "len", 1)]
        corners = [ring(ring(faces[4], "wall", 1), "len", -1), ring(ring(faces[3], "wall", 1), "len", 1)]

    field = (N * C, L)
    near = (5 * N + 16, L)
    qm, pm, pe, to_next, to_prev = call(
        functools.partial(sector, n_len), [field] * 3 + [near] * 2, [field] * 9, name="sector"
    )(*raw, wall_in, *strips, *corners)
    from_next = ring(to_prev, "blk", -1)
    from_prev = ring(to_next, "blk", 1)

    rows = (4, N, L)
    wide = LANES * ((electrodes + LANES - 1) // LANES)
    message = (W * C // 8 + C + 8, L)
    bm, be, rows_n, rows_p, mine = call(
        functools.partial(residual, electrodes, n_len, n_wall),
        [field, field, rows, rows, message],
        [(2, C, L), (W // 2 * C, L), (wide, L)],
        name="residual",
    )(pm, pe, patch_ids, to_next, to_prev, from_next, from_prev)

    relative = n_blk <= 4
    if relative:
        sector_blocks = jnp.stack([mine] + [ring(mine, "blk", d) for d in range(1, n_blk)])
    else:
        sector_blocks = lax.all_gather(mine, "blk")
    if n_len == 2:
        here = [sector_blocks, ring(sector_blocks, "len", 1)]
    else:
        gathered = lax.all_gather(sector_blocks, "len")
        here = [gathered[j] for j in range(n_len)]
    blocks = here + [ring(x, "wall", 1) for x in here]

    NC1, NL1 = n_blk * C // 2, n_len * L // 2
    planes = n_wall * W // 2
    grid1 = (planes + 2, NC1, NL1)
    grid2 = (planes // 2 + 2, NC1, NL1)
    grid3 = (planes // 4 + 2, NC1, NL1)
    Q = W // 2 + 2
    padded = 8 * ((Q + 7) // 8)
    scratch = [grid1, grid1, grid2, grid2, grid3, grid3]
    scratch += [(Q * C, L), (Q * C, L), (padded * C // 2, L), (2, 2, 2 * padded + 8, L)]
    scratch += [field, field, (2, 3, N, L), field, field, (2, n_blk * C, n_len * L)]
    adj_prev, potential, patch_grad = call(
        functools.partial(solve, (n_blk, n_len, n_wall), relative, electrodes),
        [(W, C, L), (W, C, L), (1, 2)],
        scratch,
        smem=(2,),
        name="solve",
    )(*blocks, bm, be, rows_n, rows_p, qm, tissue_mask, owner_map.reshape(1, electrodes))
    return adj_prev, potential, patch_grad


def across(x):
    n_wall = lax.axis_size("wall")
    pairs = [(l * n_wall + w, (1 - l) * n_wall + (w + 1) % n_wall) for l in range(2) for w in range(n_wall)]
    return lax.ppermute(x, ("len", "wall"), pairs)


def solution(mesh):
    field = P(("groups", "wall"), "blk", "len")
    return jax.shard_map(
        body,
        mesh=mesh,
        in_specs=(field, field, field, field, field, P("groups")),
        out_specs=(field, field, P(("groups", "blk", "len", "wall"), None)),
        check_vma=False,
    )
```

```python
import functools

import jax
import jax.numpy as jnp
from jax import lax
from jax.experimental import pallas as pl
from jax.experimental.pallas import tpu as pltpu
from jax.sharding import PartitionSpec as P

SWEEPS = 2
SI = (0.6, 1.0, 3.0)
SE = (0.8, 1.2, 2.0)
SHIFT = 0.002
OMEGA = 0.8
DT = 0.1
H = 4
LANES = 128
HIGHEST = lax.Precision.HIGHEST
F32 = jnp.float32


def level_coef(level):
    return tuple((SI[i] + SE[i]) / 4.0**level for i in range(3))


def level_diag(level):
    return SHIFT + 2.0 * sum(level_coef(level))


def level_step(level):
    return OMEGA / level_diag(level)


def lane_of(shape):
    return lax.broadcasted_iota(jnp.int32, shape, len(shape) - 1)


def before(m, e):
    first = lane_of(m.shape) == 0
    rm, re = pltpu.roll(m, 1, 1), pltpu.roll(e, 1, 1)
    return jnp.where(first, re, rm), jnp.where(first, rm, re)


def after(m, e):
    last = lane_of(m.shape) == LANES - 1
    rm, re = pltpu.roll(m, LANES - 1, 1), pltpu.roll(e, LANES - 1, 1)
    return jnp.where(last, re, rm), jnp.where(last, rm, re)


def beside_lanes(m, e):
    bm, be = before(m, e)
    am, ae = after(m, e)
    return bm + am, be + ae


def beside_lanes_main(m, e):
    lane = lane_of(m.shape)
    left = jnp.where(lane == 0, pltpu.roll(e, 1, 1), pltpu.roll(m, 1, 1))
    right = jnp.where(lane == LANES - 1, pltpu.roll(e, LANES - 1, 1), pltpu.roll(m, LANES - 1, 1))
    return left + right


def beside_rows(x, row_before, row_after):
    rows = x.shape[0]
    row = lax.broadcasted_iota(jnp.int32, x.shape, 0)
    low = jnp.where(row == 0, row_before, pltpu.roll(x, 1, 0))
    high = jnp.where(row == rows - 1, row_after, pltpu.roll(x, rows - 1, 0))
    return low + high


def beside_dense(x):
    return pltpu.roll(x, 1, 0) + pltpu.roll(x, x.shape[0] - 1, 0)


def plane(ref, i, rows):
    return ref[pl.ds(pl.multiple_of(i * rows, rows), rows), :]


def set_plane(ref, i, rows, value):
    ref[pl.ds(pl.multiple_of(i * rows, rows), rows), :] = value


def loop(low, high, step, unroll):
    def wrapped(i, carry):
        step(i)
        return carry

    lax.fori_loop(low, high, wrapped, 0, unroll=min(unroll, high - low))


FACES = (H, H - 1, H - 1, H - 2)


def face_planes(array):
    return FACES[array], sum(FACES[:array])


def pack_faces(n_len, adj, ion, mask, mis, *rest):
    n_dir = 1 if n_len == 2 else 2
    fields, wall_out, rest = rest[:4], rest[4], rest[5:]
    strips, corners = rest[:n_dir], rest[n_dir : 2 * n_dir]
    whole_mask, sems = rest[2 * n_dir :]
    cells = adj.shape[0]
    C = wall_out.shape[1]
    W = cells // C
    wall, length = lax.axis_index("wall"), lax.axis_index("len")
    targets = (fields[0], fields[1], whole_mask, fields[3])
    copies = []
    for a, (src, dst) in enumerate(zip((adj, ion, mask, mis), targets)):
        part = cells // 2
        for k in range(2):
            spot = pl.ds(k * part, part)
            copies.append(pltpu.make_async_copy(src.at[spot], dst.at[spot], sems.at[a, k]))
            copies[-1].start()

    base = jnp.where(wall == 0, W - H, 0)
    group = lane_of((C, LANES)) // H
    turns = [jnp.where(length == 0, H, 0)] if n_dir == 1 else [H, 0]
    corner = [jnp.zeros((C, LANES), F32) for _ in range(n_dir)]
    for a in (0, 1, 3, 2):
        copies[2 * a].wait()
        copies[2 * a + 1].wait()
        if a == 2:
            fields[2][...] = whole_mask[...].astype(F32)
        ref = fields[a]
        strip = [jnp.zeros((C, LANES), F32) for _ in range(n_dir)]
        for w in range(W):
            value = ref[w * C : (w + 1) * C, :]
            for d in range(n_dir):
                turned = pltpu.roll(value, lax.rem(H * w + turns[d], LANES), 1)
                strip[d] = jnp.where(group == w, turned, strip[d])
        for d in range(n_dir):
            strips[d][a] = strip[d]
        count, first = face_planes(a)
        for p in range(count):
            face = plane(ref, base + jnp.where(wall == 0, H - count, 0) + p, C)
            wall_out[first + p] = face
            slot = first + p
            for d in range(n_dir):
                turned = pltpu.roll(face, lax.rem(H * slot + turns[d], LANES), 1)
                corner[d] = jnp.where(group == slot, turned, corner[d])
    for d in range(n_dir):
        corners[d][...] = corner[d]


def dense(ref, row, N, C):
    return ref[pl.ds(row, N, stride=C), :]


def dense_pair(m, e, row, N, C):
    return dense(m, row, N, C), dense(e, row, N, C)


def dense_apply(pair, inner, outer, coef):
    m, e = pair
    lm, le = beside_lanes(m, e)
    double = 2.0 * sum(coef)
    out = [double * m - coef[0] * beside_dense(m) - coef[2] * lm, double * e - coef[0] * beside_dense(e) - coef[2] * le]
    for row in (inner, outer):
        if row is not None:
            out = [out[k] - coef[1] * row[k] for k in range(2)]
    return out


def boundary(n_len, C, xm0, xm1, xm2, xm3, wall_in, *rest):
    n_dir = 1 if n_len == 2 else 2
    strips, corners, rest = rest[:n_dir], rest[n_dir : 2 * n_dir], rest[2 * n_dir :]
    xm, xe, to_next, to_prev, own_rows = rest[:4], rest[4:8], rest[8], rest[9], rest[10]
    N = xm[0].shape[0] // C
    W = N - 2 * H
    wall, length = lax.axis_index("wall"), lax.axis_index("len")
    lane = lane_of((C, LANES))
    if n_dir == 1:
        offs, valid = [jnp.where(length == 0, 0, LANES - H)], [True]
    else:
        offs, valid = [0, LANES - H], [length < n_len - 1, length > 0]
    seen = [jnp.logical_and(lax.rem(lane - off + LANES, LANES) < H, ok) for off, ok in zip(offs, valid)]

    def rim(packed, base):
        out = jnp.zeros((C, LANES), F32)
        for d in range(n_dir):
            out = jnp.where(seen[d], pltpu.roll(packed[d], lax.rem(offs[d] - base + LANES, LANES), 1), out)
        return out

    zero = jnp.zeros((C, LANES), F32)
    last = N - H
    for a, own in enumerate((xm0, xm1, xm2, xm3)):
        packed = [strip[a] for strip in strips]
        for w in range(W):
            set_plane(xm[a], w + H, C, plane(own, w, C))
            set_plane(xe[a], w + H, C, rim(packed, H * w))
        packed = [corner[...] for corner in corners]
        for i in range(H):
            set_plane(xm[a], i, C, zero)
            set_plane(xe[a], i, C, zero)
            set_plane(xm[a], last + i, C, zero)
            set_plane(xe[a], last + i, C, zero)
        count, first = face_planes(a)
        here = jnp.where(wall == 0, last, H - count)
        for p in range(count):
            set_plane(xm[a], here + p, C, wall_in[first + p])
            set_plane(xe[a], here + p, C, rim(packed, H * (first + p)))

    pos_of = lane_of((8, LANES)) // 8
    tiles = N // 8
    for side, (out, order) in enumerate(((to_next, (C - 1, C - 2, C - 3, C - 4)), (to_prev, (0, 1, 2, 3)))):
        adj = [dense_pair(xm[0], xe[0], r, N, C) for r in order]
        mask = [dense_pair(xm[2], xe[2], r, N, C) for r in order[:3]]
        q = []
        for k in range(3):
            ion = dense_pair(xm[1], xe[1], order[k], N, C)
            moved = dense_apply(adj[k], adj[k + 1], adj[k - 1] if k else None, SI)
            q.append([adj[k][j] - DT * mask[k][j] * (moved[j] + ion[j] * adj[k][j]) for j in range(2)])
        near = dense_apply(q[0], q[1], None, SI)
        mis = dense_pair(xm[3], xe[3], order[0], N, C)
        near = [near[j] + mis[j] for j in range(2)]
        second = dense_apply(q[1], q[2], q[0], SI)[0] + dense(xm[3], order[1], N, C)
        mains = (adj[0][0], mask[0][0], q[0][0], near[0], second)
        for k, value in enumerate(mains):
            out[k * N : (k + 1) * N, :] = value
        packs = [jnp.zeros((8, LANES), F32), jnp.zeros((8, LANES), F32)]
        for k, value in enumerate((adj[0][1], mask[0][1], q[0][1], near[1])):
            for s in range(tiles):
                t = k * tiles + s
                turned = pltpu.roll(value[8 * s : 8 * s + 8], (H + 8 * (t % 16)) % LANES, 1)
                packs[t // 16] = jnp.where(pos_of == t % 16, turned, packs[t // 16])
        out[5 * N : 5 * N + 8, :] = packs[0]
        out[5 * N + 8 : 5 * N + 16, :] = packs[1]
        for k, pair in enumerate((adj[0], mask[0], q[0])):
            own_rows[side, 2 * k] = pair[0]
            own_rows[side, 2 * k + 1] = pair[1]


def spots(m_ref, e_ref, i, rows, coef):
    m, e = plane(m_ref, i, rows), plane(e_ref, i, rows)
    wm = plane(m_ref, i - 1, rows) + plane(m_ref, i + 1, rows)
    we = plane(e_ref, i - 1, rows) + plane(e_ref, i + 1, rows)
    lm, le = beside_lanes(m, e)
    cm, ce = beside_rows(m, 0.0, 0.0), beside_rows(e, 0.0, 0.0)
    double = 2.0 * sum(coef)
    dm = double * m - coef[0] * wm - coef[1] * cm - coef[2] * lm
    de = double * e - coef[0] * we - coef[1] * ce - coef[2] * le
    return m, e, dm, de


def rim_lanes(lane, length, n_len):
    return jnp.logical_or(
        jnp.logical_and(lane < H, length < n_len - 1),
        jnp.logical_and(lane >= LANES - H, length > 0),
    )


def inside(i, wall, W, n_wall):
    w = wall * W + i - H
    return jnp.logical_and(w >= 0, w < n_wall * W)


def halving():
    src = lax.broadcasted_iota(jnp.int32, (LANES, LANES), 0) // 2
    dst = lax.broadcasted_iota(jnp.int32, (LANES, LANES), 1)
    low = jnp.where(src == dst, 0.125, 0.0).astype(F32)
    high = jnp.where(src == dst - LANES // 2, 0.125, 0.0).astype(F32)
    return low, high


def precise(a, b):
    return jnp.dot(a, b, precision=HIGHEST, preferred_element_type=F32)


def sector(n_len, n_wall, C, xm0, xm1, xm2, xm3, xe0, xe1, xe2, xe3, qm, bm, be, coarse, surface, qe, pairs):
    xm, xe = (xm0, xm1, xm2, xm3), (xe0, xe1, xe2, xe3)
    N = qm.shape[0] // C
    W = N - 2 * H
    wall, length = lax.axis_index("wall"), lax.axis_index("len")
    rim = rim_lanes(lane_of((C, LANES)), length, n_len)
    zero = jnp.zeros((C, LANES), F32)
    for i in (0, N - 1):
        set_plane(qm, i, C, zero)
        set_plane(qe, i, C, zero)
    for i in (0, 1, N - 2, N - 1):
        set_plane(bm, i, C, zero)
        set_plane(be, i, C, zero)

    def parabolic(i):
        m, e, dm, de = spots(xm[0], xe[0], i, C, SI)
        set_plane(qm, i, C, m - DT * plane(xm[2], i, C) * (dm + plane(xm[1], i, C) * m))
        set_plane(qe, i, C, e - DT * plane(xe[2], i, C) * (de + plane(xe[1], i, C) * e))

    loop(1, N - 1, parabolic, 2)

    def elliptic_source(i):
        m, e, dm, de = spots(qm, qe, i, C, SI)
        ok = inside(i, wall, W, n_wall)
        set_plane(bm, i, C, jnp.where(ok, plane(xm[3], i, C) + dm, 0.0))
        set_plane(be, i, C, jnp.where(jnp.logical_and(rim, ok), plane(xe[3], i, C) + de, 0.0))

    loop(2, N - 2, elliptic_source, 2)

    coef, k0 = level_coef(0), level_step(0)

    def left(i):
        m, e = plane(bm, i, C), plane(be, i, C)
        wm = plane(bm, i - 1, C) + plane(bm, i + 1, C)
        cm = beside_rows(m, 0.0, 0.0)
        lm = beside_lanes_main(m, e)
        return m, (1.0 - OMEGA) * m + k0 * (coef[0] * wm + coef[1] * cm + coef[2] * lm)

    def pair(q):
        i = 2 * q + H
        m, first = left(i)
        n, second = left(i + 1)
        set_plane(pairs, q, C, first + second)

        @pl.when(jnp.logical_and(q == 0, wall == 0))
        def _():
            surface[...] = k0 * (m + first)

        @pl.when(jnp.logical_and(q == W // 2 - 1, wall == n_wall - 1))
        def _():
            surface[...] = k0 * (n + second)

    loop(0, W // 2, pair, 2)

    half = W * C // 8
    z = pairs[pl.ds(0, 2 * half, stride=2), :] + pairs[pl.ds(1, 2 * half, stride=2), :]
    low, high = halving()
    coarse[...] = precise(z[:half], low) + precise(z[half:], high)


def unpacked(ref, N):
    lane = lane_of((8, LANES))
    rim = jnp.logical_or(lane < H, lane >= LANES - H)
    tiles = N // 8
    mains = [ref[q * N : (q + 1) * N, :] for q in range(5)]
    packs = [ref[5 * N : 5 * N + 8, :], ref[5 * N + 8 : 5 * N + 16, :]]
    rims = []
    for q in range(4):
        parts = []
        for s in range(tiles):
            t = q * tiles + s
            turned = pltpu.roll(packs[t // 16], (2 * LANES - H - 8 * (t % 16)) % LANES, 1)
            parts.append(jnp.where(rim, turned, 0.0))
        rims.append(jnp.concatenate(parts, 0))
    return [(mains[q], rims[q]) for q in range(4)] + [mains[4]]


def lateral(pair):
    return dense_apply(pair, None, None, SI)


def source_rows(own, other):
    adj_o, mask_o, q_o = own
    adj_n, mask_n, q_n, p_n, second_n = other
    step = DT * SI[1]
    delta_o = [step * mask_o[k] * adj_n[k] for k in range(2)]
    delta_n = [step * mask_n[k] * adj_o[k] for k in range(2)]
    lat_o, lat_n = lateral(delta_o), lateral(delta_n)
    near = [lat_o[k] - SI[1] * (q_n[k] + delta_n[k]) for k in range(2)]
    second = [-SI[1] * delta_o[k] for k in range(2)]
    halo = [p_n[k] + lat_n[k] - SI[1] * (q_o[k] + delta_o[k]) for k in range(2)]
    halo_second = second_n - SI[1] * delta_n[0]
    return near, second, halo, halo_second, delta_o[0]


def correct(electrodes, n_len, n_wall, own_rows, from_next, from_prev, coarse, surface, ids, *rest):
    rows_n, rows_p, message = rest[:3]
    lines, sums = rest[3:]
    _, C, L = ids.shape
    N = own_rows.shape[2]
    W = N - 2 * H
    wall, length = lax.axis_index("wall"), lax.axis_index("len")
    ok_m = inside(lax.broadcasted_iota(jnp.int32, (N, LANES), 0), wall, W, n_wall)
    ok_e = jnp.logical_and(ok_m, rim_lanes(lane_of((N, LANES)), length, n_len))
    coef, k0 = level_coef(0), level_step(0)
    y = surface[...]
    row = lax.broadcasted_iota(jnp.int32, (C, LANES), 0)
    at = pl.ds(jnp.where(wall == 0, H, W + H - 1), 1)
    lows, highs = [], []
    W1, C1 = W // 2, C // 2
    for side, (other, out, order) in enumerate(
        ((from_next, rows_n, (C - 1, C - 2, C - 3)), (from_prev, rows_p, (0, 1, 2)))
    ):
        own = [(own_rows[side, 2 * k], own_rows[side, 2 * k + 1]) for k in range(3)]
        near, second, halo, halo_second, delta = source_rows(own, unpacked(other, N))
        near = [jnp.where(ok_m, near[0], 0.0), jnp.where(ok_e, near[1], 0.0)]
        second = [jnp.where(ok_m, second[0], 0.0), jnp.where(ok_e, second[1], 0.0)]
        out[0] = halo_m = jnp.where(ok_m, halo[0], 0.0)
        out[1] = jnp.where(ok_e, halo[1], 0.0)
        out[2] = jnp.where(ok_m, halo_second, 0.0)
        out[3] = delta
        out[4], out[5] = near
        out[6], out[7] = second

        def turned(pair, beside):
            m, e = pair
            return (1.0 - OMEGA) * m + k0 * (
                coef[0] * beside_dense(m) + coef[2] * beside_lanes_main(m, e) + coef[1] * beside
            )

        first = turned(near, second[0] + halo_m)
        next_one = turned(second, near[0])
        third = k0 * coef[1] * second[0]
        for k, change in enumerate((near[0] + first, second[0] + next_one, third)):
            lines[0] = change
            y = y + jnp.where(row == order[k], k0 * lines[0, at, :], 0.0)
        for change in (first + next_one, third):
            lines[0] = change
            both = lines[0, pl.ds(H, W1, stride=2), :] + lines[0, pl.ds(H + 1, W1, stride=2), :]
            lows.append(both[: W1 // 2])
            highs.append(both[W1 // 2 :])
    low, high = halving()
    add = precise(jnp.concatenate(lows, 0), low) + precise(jnp.concatenate(highs, 0), high)
    half = W * C // 8
    message[0:half, :] = coarse[...]
    for k, c1 in enumerate((C1 - 1, C1 - 2, 0, 1)):
        spot = pl.ds(c1, W1 // 2, stride=C1)
        message[spot, :] = message[spot, :] + add[k * (W1 // 2) : (k + 1) * (W1 // 2)]
    patch = ids[0]
    message[half : half + C, :] = patch.astype(F32)
    wide = sums.shape[0]
    if wide > electrodes:
        sums[...] = jnp.zeros(sums.shape, F32)

    def one(e):
        sums[pl.ds(e, 1), :] = jnp.sum(jnp.where(patch == e, y, 0.0), axis=0, keepdims=True)

    loop(0, electrodes, one, 8)
    totals = lax.dot_general(
        jnp.ones((8, LANES), F32), sums[...], (((1,), (1,)), ((), ())), precision=HIGHEST, preferred_element_type=F32
    )
    message[half + C : half + C + 8, :] = jnp.zeros((8, LANES), F32)
    for t in range(wide // LANES):
        message[half + C + t : half + C + t + 1, :] = totals[0:1, t * LANES : (t + 1) * LANES]


def source_part(n_blk, n_len, n_wall, C, electrodes, bm, be, rows_n, rows_p, qm, mask, owner, base_adj, base_pot, *rest):
    patches, fm, fe, tm, te, hp = rest
    N = bm.shape[0] // C
    W = N - 2 * H
    blk, length, wall = lax.axis_index("blk"), lax.axis_index("len"), lax.axis_index("wall")
    fm[...] = bm[...]
    fe[...] = be[...]
    for rows, near, second in ((rows_n, C - 1, C - 2), (rows_p, 0, 1)):
        for k, at in ((4, near), (6, second)):
            spot = pl.ds(at, N, stride=C)
            fm[spot, :] = fm[spot, :] + rows[k]
            fe[spot, :] = fe[spot, :] + rows[k + 1]
    coef, k0 = level_coef(0), level_step(0)
    rim = rim_lanes(lane_of((C, LANES)), length, n_len)

    def part(i):
        m, e = plane(fm, i, C), plane(fe, i, C)
        wm = plane(fm, i - 1, C) + plane(fm, i + 1, C)
        we = plane(fe, i - 1, C) + plane(fe, i + 1, C)
        lm, le = beside_lanes(m, e)
        at = pl.ds(i, 1)
        cm = beside_rows(m, rows_p[0, at, :], rows_n[0, at, :])
        ce = beside_rows(e, rows_p[1, at, :], rows_n[1, at, :])
        pm = k0 * ((2.0 - OMEGA) * m + k0 * (coef[0] * wm + coef[1] * cm + coef[2] * lm))
        pe = k0 * ((2.0 - OMEGA) * e + k0 * (coef[0] * we + coef[1] * ce + coef[2] * le))
        set_plane(tm, i, C, jnp.where(inside(i, wall, W, n_wall), pm, 0.0))
        set_plane(te, i, C, jnp.where(rim, pe, 0.0))

    loop(H - 1, N - H + 1, part, 2)
    for side, (rows, at) in enumerate(((rows_n, C - 1), (rows_p, 0))):
        m = rows[0]
        total = (
            coef[0] * beside_dense(m)
            + coef[1] * (rows[2] + dense(fm, at, N, C))
            + coef[2] * beside_lanes_main(m, rows[1])
        )
        hp[side] = k0 * ((2.0 - OMEGA) * m + k0 * total)
    row = lax.broadcasted_iota(jnp.int32, (C, LANES), 0)

    def finish(w):
        i = w + H
        m, e = plane(tm, i, C), plane(te, i, C)
        at = pl.ds(i, 1)
        wm = plane(tm, i - 1, C) + plane(tm, i + 1, C)
        cm = beside_rows(m, hp[1, at, :], hp[0, at, :])
        lm = beside_lanes_main(m, e)
        lam = plane(qm, i, C)
        lam = lam + jnp.where(row == C - 1, rows_n[3, at, :], 0.0) + jnp.where(row == 0, rows_p[3, at, :], 0.0)
        moved = 2.0 * sum(SI) * m - SI[0] * wm - SI[1] * cm - SI[2] * lm
        set_plane(base_adj, w, C, lam - DT * plane(mask, i, C) * moved)
        set_plane(base_pot, w, C, m)

    loop(0, W, finish, 2)

    me = (blk * n_len + length) * n_wall + wall
    which = lax.broadcasted_iota(jnp.int32, (1, electrodes), 1).astype(F32)
    mine = owner[...] == me
    patches[0:1, :] = jnp.full((1, LANES), jnp.min(jnp.where(mine, which, float(electrodes))))
    patches[1:2, :] = jnp.full((1, LANES), jnp.max(jnp.where(mine, which, -1.0)))
    patches[2:8, :] = jnp.zeros((6, LANES), F32)


def around(x, by):
    rows, lanes = x.shape
    lane = lane_of(x.shape)
    c = pltpu.roll(x, by, 0) + pltpu.roll(x, rows - by, 0)
    l = jnp.where(lane < by, 0.0, pltpu.roll(x, by, 1)) + jnp.where(
        lane >= lanes - by, 0.0, pltpu.roll(x, lanes - by, 1)
    )
    return c, l


def twins(x, by):
    rows, lanes = x.shape
    row = lax.broadcasted_iota(jnp.int32, x.shape, 0)
    lane = lane_of(x.shape)
    x = x + jnp.where((row & by) == 0, pltpu.roll(x, rows - by, 0), pltpu.roll(x, by, 0))
    return x + jnp.where((lane & by) == 0, pltpu.roll(x, lanes - by, 1), pltpu.roll(x, by, 1))


def solve(sizes, relative, C, W, *refs):
    n_blk, n_len, n_wall = sizes
    count = n_len * n_wall
    blocks, refs = refs[:count], refs[count:]
    base_adj, base_pot, mask, patches, adj_prev, potential, patch_grad = refs[:7]
    b1, x1, b2, x2, b3, x3, near, wide, pm, pe, tm, te, adj_out, pot_out, sheet, sems = refs[7:]
    L = LANES
    W1, C1 = W // 2, C // 2
    planes, NC1, NL1 = b1.shape
    planes -= 2
    blk, length, wall = lax.axis_index("blk"), lax.axis_index("len"), lax.axis_index("wall")
    half = W1 // 2
    middle = LANES // 2
    lane8 = lane_of((C1, LANES))
    often = 8 if NC1 * NL1 <= 4096 else 1

    def blk_of(d):
        return lax.rem(blk - d + n_blk, n_blk) if relative else d

    def length_of(j):
        return (length + j) % n_len if n_len == 2 else j

    zero1 = jnp.zeros((NC1, NL1), F32)
    for ref in (b1, x1, b2, x2, b3, x3):
        ref[0] = zero1
        ref[ref.shape[0] - 1] = zero1

    for v in range(n_wall):
        wall_s = (wall + v) % n_wall
        mine = blocks[v * n_len : (v + 1) * n_len]

        def unpack(d):
            at = pl.ds(pl.multiple_of(C1 * blk_of(d), C1), C1)
            for t in range(n_len // 2):
                one, two = mine[2 * t], mine[2 * t + 1]
                for i in range(half):
                    a, b = one[d, i * C1 : (i + 1) * C1, :], two[d, i * C1 : (i + 1) * C1, :]
                    if n_len == 2:
                        a, b = jnp.where(length == 0, a, b), jnp.where(length == 0, b, a)
                    spot = 1 + wall_s * W1 + i
                    lanes = slice(t * LANES, (t + 1) * LANES)
                    b1[spot, at, lanes] = jnp.where(lane8 < middle, a, pltpu.roll(b, middle, 1))
                    b1[spot + half, at, lanes] = jnp.where(lane8 < middle, pltpu.roll(a, middle, 1), b)

        loop(0, n_blk, unpack, 4)

    def total_of(x, wsum, level, by):
        coef = level_coef(level)
        c, l = around(x, by)
        return level_step(level) * (coef[0] * wsum + coef[1] * c + coef[2] * l)

    def left(ref, i, level):
        b = ref[i]
        return (1.0 - OMEGA) * b + total_of(b, ref[i - 1] + ref[i + 1], level, 2 ** (level - 1))

    def sweep(x_ref, b_ref, i, level):
        x = x_ref[i]
        total = total_of(x, x_ref[i - 1] + x_ref[i + 1], level, 2 ** (level - 1))
        return (1.0 - OMEGA) * x + level_step(level) * b_ref[i] + total

    def down1(q):
        b2[1 + q] = 0.125 * twins(left(b1, 2 * q + 1, 1) + left(b1, 2 * q + 2, 1), 1)

    loop(0, planes // 2, down1, often)

    def down2(q):
        b3[1 + q] = 0.125 * twins(left(b2, 2 * q + 1, 2) + left(b2, 2 * q + 2, 2), 2)

    loop(0, planes // 4, down2, often)

    deep = planes // 4
    k3 = level_step(3)

    def start3(q):
        x3[1 + q] = k3 * b3[1 + q]

    loop(0, deep, start3, often)
    for k in range(SWEEPS):
        from_ref, to_ref = (x3, x2) if k % 2 == 0 else (x2, x3)

        if k == 1:
            x2[1 + deep] = zero1

        def sweep3(q):
            to_ref[1 + q] = sweep(from_ref, b3, 1 + q, 3)

        loop(0, deep, sweep3, often)
    deepest = x3 if SWEEPS % 2 == 0 else x2
    assert deepest is x3
    k2 = level_step(2)

    def up2(q):
        coarse = x3[1 + q]
        x2[1 + 2 * q] = k2 * b2[1 + 2 * q] + coarse
        x2[2 + 2 * q] = k2 * b2[2 + 2 * q] + coarse

    loop(0, planes // 4, up2, often)

    k1 = level_step(1)

    def up1(q):
        fine = sweep(x2, b2, 1 + q, 2)
        x1[1 + 2 * q] = k1 * b1[1 + 2 * q] + fine
        x1[2 + 2 * q] = k1 * b1[2 + 2 * q] + fine

    loop(0, planes // 2, up1, often)

    Q = W1 + 2
    sectors = (blk, lax.rem(blk + 1, n_blk), lax.rem(blk + n_blk - 1, n_blk))
    spots3 = [pl.ds(pl.multiple_of(s * C1, C1), C1) for s in sectors]
    row8 = lax.broadcasted_iota(jnp.int32, (C1, NL1), 0)
    NR = 2 * C1

    def three(ref, i):
        return jnp.concatenate([ref[i, s, :] for s in spots3], 0)

    def finish1(q):
        i = wall * W1 + q
        x = three(x1, i)
        wsum = three(x1, jnp.maximum(i - 1, 0)) + three(x1, jnp.minimum(i + 1, planes + 1))
        value = (1.0 - OMEGA) * x + k1 * three(b1, i) + total_of(x, wsum, 1, 1)
        value = jnp.where(jnp.logical_and(i >= 1, i <= planes), value, 0.0)
        set_plane(near, 2 * q, C1, value[:C1])
        set_plane(near, 2 * q + 1, C1, jnp.where(row8 < 2, value[C1 : 2 * C1], value[2 * C1 :]))

    loop(0, Q, finish1, min(often, 6))

    lane = lane_of((NL1, LANES))
    source = lax.broadcasted_iota(jnp.int32, (NL1, LANES), 0)
    first = length * middle
    take_m = jnp.where(source == first + lane // 2, 1.0, 0.0).astype(F32)
    at_e = jnp.where(lane < H, middle + lane // 2, jnp.where(lane >= LANES - H, lane // 2 - middle, 4 * NL1))
    take_e = jnp.where(source == first + at_e, 1.0, 0.0).astype(F32)
    R = C + 8
    row8 = lax.broadcasted_iota(jnp.int32, (8, LANES), 0)
    for out, sel in ((pm, take_m), (pe, take_e)):
        value = precise(near[...], sel)
        wide[pl.ds(0, Q * NR, stride=2), :] = value
        wide[pl.ds(1, Q * NR, stride=2), :] = value
        for q in range(Q):
            base = 2 * NR * q
            out[R * q : R * q + C, :] = wide[base : base + C, :]
            out[R * q + C : R * (q + 1), :] = jnp.where(
                row8 < H, wide[base + C : base + C + 8, :], wide[base + 2 * NR - 8 : base + 2 * NR, :]
            )
    coef, k0 = level_coef(0), level_step(0)
    rim = rim_lanes(lane_of((R, LANES)), length, n_len)

    def rows_beside(x):
        return pltpu.roll(x, 1, 0) + pltpu.roll(x, x.shape[0] - 1, 0)

    def coarse_terms(q):
        m, e = plane(pm, q, R), plane(pe, q, R)
        lm, le = beside_lanes(m, e)
        gm = (1.0 - OMEGA) * m + k0 * (coef[0] * m + coef[1] * rows_beside(m) + coef[2] * lm)
        ge = (1.0 - OMEGA) * e + k0 * (coef[0] * e + coef[1] * rows_beside(e) + coef[2] * le)
        return gm, ge

    ks = k0 * coef[0]

    def put(t, gm, ge, other, ok):
        m = gm + ks * plane(pm, other, R)
        e = jnp.where(rim, ge + ks * plane(pe, other, R), 0.0)
        if ok is not None:
            m, e = jnp.where(ok, m, 0.0), jnp.where(ok, e, 0.0)
        set_plane(tm, t, R, m)
        set_plane(te, t, R, e)

    put(0, *coarse_terms(0), 1, wall > 0)
    put(W + 1, *coarse_terms(Q - 1), Q - 2, wall < n_wall - 1)

    def level0(q):
        gm, ge = coarse_terms(q)
        put(2 * q - 1, gm, ge, q - 1, None)
        put(2 * q, gm, ge, q + 1, None)
        for w in (2 * q - 2, 2 * q - 1):
            set_plane(pot_out, w, C, plane(base_pot, w, C) + plane(tm, w + 1, R)[:C])

    def finish0(w):
        m, e = plane(tm, w + 1, R), plane(te, w + 1, R)[:C]
        cm = rows_beside(m)[:C]
        m = m[:C]
        wm = plane(tm, w, R)[:C] + plane(tm, w + 2, R)[:C]
        lm = beside_lanes_main(m, e)
        moved = 2.0 * sum(SI) * m - SI[0] * wm - SI[1] * cm - SI[2] * lm
        set_plane(adj_out, w, C, plane(base_adj, w, C) - DT * plane(mask, w + H, C) * moved)

    parts = 2
    size = W // parts
    copies = []

    def send(src, dst, k, sem):
        spot = pl.ds(k * size * C, size * C)
        copies.append(pltpu.make_async_copy(src.at[spot], dst.at[spot], sem))
        copies[-1].start()

    for k in range(parts):
        loop(1 + k * W1 // parts, 1 + (k + 1) * W1 // parts, level0, 4)
        send(pot_out, potential, k, sems.at[0, k])
    for k in range(parts):
        loop(k * size, (k + 1) * size, finish0, 4)
        send(adj_out, adj_prev, k, sems.at[1, k])

    NC, NL = sheet.shape[1:]
    twice_c = jnp.where(
        lax.broadcasted_iota(jnp.int32, (NC, NC1), 0) // 2 == lax.broadcasted_iota(jnp.int32, (NC, NC1), 1), 1.0, 0.0
    ).astype(F32)
    twice_l = jnp.where(
        lax.broadcasted_iota(jnp.int32, (NL1, NL), 1) // 2 == lax.broadcasted_iota(jnp.int32, (NL1, NL), 0), 1.0, 0.0
    ).astype(F32)
    for s, i in enumerate((1, planes)):
        p = precise(precise(twice_c, sweep(x1, b1, i, 1)), twice_l)
        c, l = around(p, 1)
        sheet[s] = (1.0 - OMEGA) * p + k0 * (coef[0] * p + coef[1] * c + coef[2] * l)

    owned = [patches[r : r + 1, :] for r in range(2)]
    spot = lax.broadcasted_iota(jnp.int32, (8, LANES), 0) * LANES + lane_of((8, LANES))
    spot = spot.astype(F32)
    start = half * C1
    totals = [jnp.zeros((C, LANES), F32) for _ in owned]
    small = [jnp.zeros((8, LANES), F32) for _ in owned]
    for v in range(n_wall):
        wall_s = (wall + v) % n_wall
        for j in range(n_len):
            ref = blocks[v * n_len + j]
            at_l = pl.ds(pl.multiple_of(length_of(j) * L, L), L)

            def add(d, carry):
                big, little = carry
                values = sheet[wall_s, pl.ds(pl.multiple_of(blk_of(d) * C, C), C), at_l]
                ids = ref[d, start : start + C, :]
                parts = ref[d, start + C : start + C + 8, :]
                big = [x + jnp.where(ids == e, values, 0.0) for x, e in zip(big, owned)]
                little = [x + jnp.where(spot == e, parts, 0.0) for x, e in zip(little, owned)]
                return big, little

            totals, small = lax.fori_loop(0, n_blk, add, (totals, small), unroll=min(4, n_blk))
    factor = 1.0 / (2.0 * C * L / 2) ** 0.5
    for r in range(2):
        patch_grad[0, r] = (jnp.sum(totals[r]) + jnp.sum(small[r])) * factor
    for copy in copies:
        copy.wait()


def ring(x, axis, by):
    count = lax.axis_size(axis)
    return lax.ppermute(x, axis, [(i, (i + by) % count) for i in range(count)])


def across(x):
    n_wall = lax.axis_size("wall")
    pairs = [(l * n_wall + w, (1 - l) * n_wall + (w + 1) % n_wall) for l in range(2) for w in range(n_wall)]
    return lax.ppermute(x, ("len", "wall"), pairs)


def call(kernel, ins, outs, scratch, name, work=0):
    places = {"vmem": pltpu.VMEM, "smem": pltpu.SMEM, "any": pl.ANY}

    def specs(kinds):
        return [pl.BlockSpec(memory_space=places[kind]) for kind in kinds]

    cost = pl.CostEstimate(flops=work, bytes_accessed=work, transcendentals=0) if work else None
    return pl.pallas_call(
        kernel,
        out_shape=[jax.ShapeDtypeStruct(shape, F32) for shape, _ in outs],
        in_specs=specs(ins),
        out_specs=specs(kind for _, kind in outs),
        scratch_shapes=[pltpu.VMEM(shape, F32) if isinstance(shape, tuple) else shape for shape in scratch],
        compiler_params=pltpu.CompilerParams(vmem_limit_bytes=48 * 2**20),
        cost_estimate=cost,
        name=name,
    )


def body(adj_next, ion_slope, misfit, tissue_mask, patch_ids, owner_map):
    W, C, L = adj_next.shape
    n_blk, n_len, n_wall = lax.axis_size("blk"), lax.axis_size("len"), lax.axis_size("wall")
    electrodes = owner_map.shape[0]
    assert L == LANES and H * W == LANES and n_wall == 2 and electrodes == 2 * n_blk * n_len * n_wall
    N = W + 2 * H
    n_dir = 1 if n_len == 2 else 2
    cells = W * C
    vmem = "vmem"
    field, own = (N * C, L), (cells, L)
    raw = [x.reshape(cells, L) for x in (adj_next, ion_slope, tissue_mask, misfit)]

    *fields, wall_out = (faces := call(
        functools.partial(pack_faces, n_len),
        ["any"] * 4,
        [(own, vmem)] * 4
        + [((sum(FACES), C, L), vmem)]
        + [((4, C, L), vmem)] * n_dir
        + [((C, L), vmem)] * n_dir,
        [pltpu.VMEM(own, jnp.int32), pltpu.SemaphoreType.DMA((4, 2))],
        "faces",
    )(*raw))[:5]
    strip_out, corner_out = faces[5 : 5 + n_dir], faces[5 + n_dir :]
    wall_in = ring(wall_out, "wall", 1)
    if n_dir == 1:
        strips = [ring(strip_out[0], "len", 1)]
        corners = [across(corner_out[0])]
    else:
        strips = [ring(strip_out[1], "len", -1), ring(strip_out[0], "len", 1)]
        corners = [ring(ring(corner_out[1], "wall", 1), "len", -1), ring(ring(corner_out[0], "wall", 1), "len", 1)]

    near = (5 * N + 16, L)
    *fields, to_next, to_prev, own_rows = call(
        functools.partial(boundary, n_len, C),
        [vmem] * (5 + 2 * n_dir),
        [(field, vmem)] * 8 + [(near, vmem)] * 2 + [((2, 6, N, L), vmem)],
        [],
        "boundary",
    )(*fields, wall_in, *strips, *corners)
    from_next = ring(to_prev, "blk", -1)
    from_prev = ring(to_next, "blk", 1)
    qm, bm, be, coarse, surface = call(
        functools.partial(sector, n_len, n_wall, C),
        [vmem] * 8,
        [(field, vmem)] * 3 + [((cells // 8, L), vmem), ((C, L), vmem)],
        [field, (cells // 2, L)],
        "sector",
        work=16 * 10**6,
    )(*fields)

    rows = (8, N, L)
    wide = LANES * ((electrodes + LANES - 1) // LANES)
    message = (cells // 8 + C + 8, L)
    rows_n, rows_p, mine = call(
        functools.partial(correct, electrodes, n_len, n_wall),
        [vmem] * 6,
        [(rows, vmem), (rows, vmem), (message, vmem)],
        [(1, N, L), (wide, L)],
        "correct",
    )(own_rows, from_next, from_prev, coarse, surface, patch_ids)

    relative = n_blk <= 4
    if relative:
        sector_blocks = jnp.stack([mine] + [ring(mine, "blk", d) for d in range(1, n_blk)])
    else:
        sector_blocks = lax.all_gather(mine, "blk")
    if n_len == 2:
        here = [sector_blocks, ring(sector_blocks, "len", 1)]
    else:
        gathered = lax.all_gather(sector_blocks, "len")
        here = [gathered[j] for j in range(n_len)]
    blocks = here + [ring(x, "wall", 1) for x in here]

    base_adj, base_pot, patches = call(
        functools.partial(source_part, n_blk, n_len, n_wall, C, electrodes),
        [vmem] * 7,
        [(own, vmem), (own, vmem), ((8, L), vmem)],
        [field] * 4 + [(2, N, L)],
        "source_part",
        work=12 * 10**6,
    )(bm, be, rows_n, rows_p, qm, fields[2], owner_map.reshape(1, electrodes))

    NC1, NL1 = n_blk * C // 2, n_len * L // 2
    planes = n_wall * W // 2
    grids = [(planes // k + 2, NC1, NL1) for k in (1, 1, 2, 2, 4, 4)]
    Q = W // 2 + 2
    tall = (Q * (C + 8), L)
    taller = ((W + 2) * (C + 8), L)
    scratch = grids + [(Q * C, NL1), (2 * Q * C, L), tall, tall, taller, taller, own, own]
    scratch += [(2, n_blk * C, n_len * L), pltpu.SemaphoreType.DMA((2, 2))]
    adj_prev, potential, patch_grad = call(
        functools.partial(solve, (n_blk, n_len, n_wall), relative, C, W),
        [vmem] * (n_len * n_wall + 4),
        [(own, "any"), (own, "any"), ((1, 2), "smem")],
        scratch,
        "solve",
    )(*blocks, base_adj, base_pot, fields[2], patches)
    return adj_prev.reshape(W, C, L), potential.reshape(W, C, L), patch_grad


def solution(mesh):
    field = P(("groups", "wall"), "blk", "len")
    return jax.shard_map(
        body,
        mesh=mesh,
        in_specs=(field, field, field, field, field, P("groups")),
        out_specs=(field, field, P(("groups", "blk", "len", "wall"), None)),
        check_vma=False,
    )
```

```python
import functools

import jax
import jax.numpy as jnp
from jax import lax
from jax.experimental import pallas as pl
from jax.experimental.pallas import tpu as pltpu
from jax.sharding import PartitionSpec as P

SWEEPS = 2
SI = (0.6, 1.0, 3.0)
SE = (0.8, 1.2, 2.0)
SHIFT = 0.002
OMEGA = 0.8
DT = 0.1
H = 4
LANES = 128
HIGHEST = lax.Precision.HIGHEST
F32 = jnp.float32


def level_coef(level):
    return tuple((SI[i] + SE[i]) / 4.0**level for i in range(3))


def level_diag(level):
    return SHIFT + 2.0 * sum(level_coef(level))


def level_step(level):
    return OMEGA / level_diag(level)


def lane_of(shape):
    return lax.broadcasted_iota(jnp.int32, shape, len(shape) - 1)


def before(m, e):
    first = lane_of(m.shape) == 0
    rm, re = pltpu.roll(m, 1, 1), pltpu.roll(e, 1, 1)
    return jnp.where(first, re, rm), jnp.where(first, rm, re)


def after(m, e):
    last = lane_of(m.shape) == LANES - 1
    rm, re = pltpu.roll(m, LANES - 1, 1), pltpu.roll(e, LANES - 1, 1)
    return jnp.where(last, re, rm), jnp.where(last, rm, re)


def beside_lanes(m, e):
    bm, be = before(m, e)
    am, ae = after(m, e)
    return bm + am, be + ae


def beside_lanes_main(m, e):
    lane = lane_of(m.shape)
    left = jnp.where(lane == 0, pltpu.roll(e, 1, 1), pltpu.roll(m, 1, 1))
    right = jnp.where(lane == LANES - 1, pltpu.roll(e, LANES - 1, 1), pltpu.roll(m, LANES - 1, 1))
    return left + right


def beside_rows(x, row_before, row_after):
    rows = x.shape[0]
    row = lax.broadcasted_iota(jnp.int32, x.shape, 0)
    low = jnp.where(row == 0, row_before, pltpu.roll(x, 1, 0))
    high = jnp.where(row == rows - 1, row_after, pltpu.roll(x, rows - 1, 0))
    return low + high


def beside_dense(x):
    return pltpu.roll(x, 1, 0) + pltpu.roll(x, x.shape[0] - 1, 0)


def plane(ref, i, rows):
    return ref[pl.ds(pl.multiple_of(i * rows, rows), rows), :]


def set_plane(ref, i, rows, value):
    ref[pl.ds(pl.multiple_of(i * rows, rows), rows), :] = value


def loop(low, high, step, unroll):
    def wrapped(i, carry):
        step(i)
        return carry

    lax.fori_loop(low, high, wrapped, 0, unroll=min(unroll, high - low))


FACES = (H, H - 1, H - 1, H - 2)


def face_planes(array):
    return FACES[array], sum(FACES[:array])


def pack_faces(n_len, adj, ion, mask, mis, *rest):
    n_dir = 1 if n_len == 2 else 2
    fields, wall_out, rest = rest[:4], rest[4], rest[5:]
    strips, corners = rest[:n_dir], rest[n_dir : 2 * n_dir]
    whole_mask, sems = rest[2 * n_dir :]
    cells = adj.shape[0]
    C = wall_out.shape[1]
    W = cells // C
    wall, length = lax.axis_index("wall"), lax.axis_index("len")
    targets = (fields[0], fields[1], whole_mask, fields[3])
    copies = []
    for a, (src, dst) in enumerate(zip((adj, ion, mask, mis), targets)):
        part = cells // 2
        for k in range(2):
            spot = pl.ds(k * part, part)
            copies.append(pltpu.make_async_copy(src.at[spot], dst.at[spot], sems.at[a, k]))
            copies[-1].start()

    base = jnp.where(wall == 0, W - H, 0)
    group = lane_of((C, LANES)) // H
    turns = [jnp.where(length == 0, H, 0)] if n_dir == 1 else [H, 0]
    corner = [jnp.zeros((C, LANES), F32) for _ in range(n_dir)]
    for a in (0, 1, 3, 2):
        copies[2 * a].wait()
        copies[2 * a + 1].wait()
        if a == 2:
            fields[2][...] = whole_mask[...].astype(F32)
        ref = fields[a]
        strip = [jnp.zeros((C, LANES), F32) for _ in range(n_dir)]
        for w in range(W):
            value = ref[w * C : (w + 1) * C, :]
            for d in range(n_dir):
                turned = pltpu.roll(value, lax.rem(H * w + turns[d], LANES), 1)
                strip[d] = jnp.where(group == w, turned, strip[d])
        for d in range(n_dir):
            strips[d][a] = strip[d]
        count, first = face_planes(a)
        for p in range(count):
            face = plane(ref, base + jnp.where(wall == 0, H - count, 0) + p, C)
            wall_out[first + p] = face
            slot = first + p
            for d in range(n_dir):
                turned = pltpu.roll(face, lax.rem(H * slot + turns[d], LANES), 1)
                corner[d] = jnp.where(group == slot, turned, corner[d])
    for d in range(n_dir):
        corners[d][...] = corner[d]


def dense(ref, row, N, C):
    return ref[pl.ds(row, N, stride=C), :]


def dense_pair(m, e, row, N, C):
    return dense(m, row, N, C), dense(e, row, N, C)


def dense_apply(pair, inner, outer, coef):
    m, e = pair
    lm, le = beside_lanes(m, e)
    double = 2.0 * sum(coef)
    out = [double * m - coef[0] * beside_dense(m) - coef[2] * lm, double * e - coef[0] * beside_dense(e) - coef[2] * le]
    for row in (inner, outer):
        if row is not None:
            out = [out[k] - coef[1] * row[k] for k in range(2)]
    return out


def near_rows(n_dir, W):
    start, places = 8 * n_dir, []
    for reach in (0, 1, 2, 2, 3):
        places.append((start, H - reach, W + 2 * reach))
        start += W + 2 * reach
    assert start % 8 == 0
    return places


def rim_tiles(values):
    return [value[s : s + 8] for value in values for s in range(0, value.shape[0], 8)]


def boundary(n_len, C, xm0, xm1, xm2, xm3, wall_in, *rest):
    n_dir = 1 if n_len == 2 else 2
    strips, corners, rest = rest[:n_dir], rest[n_dir : 2 * n_dir], rest[2 * n_dir :]
    xm, xe, to_next, to_prev, own_rows = rest[:4], rest[4:8], rest[8], rest[9], rest[10]
    N = xm[0].shape[0] // C
    W = N - 2 * H
    wall, length = lax.axis_index("wall"), lax.axis_index("len")
    lane = lane_of((C, LANES))
    if n_dir == 1:
        offs, valid = [jnp.where(length == 0, 0, LANES - H)], [True]
    else:
        offs, valid = [0, LANES - H], [length < n_len - 1, length > 0]
    seen = [jnp.logical_and(lax.rem(lane - off + LANES, LANES) < H, ok) for off, ok in zip(offs, valid)]

    def rim(packed, base):
        out = jnp.zeros((C, LANES), F32)
        for d in range(n_dir):
            out = jnp.where(seen[d], pltpu.roll(packed[d], lax.rem(offs[d] - base + LANES, LANES), 1), out)
        return out

    zero = jnp.zeros((C, LANES), F32)
    last = N - H
    for a, own in enumerate((xm0, xm1, xm2, xm3)):
        packed = [strip[a] for strip in strips]
        for w in range(W):
            set_plane(xm[a], w + H, C, plane(own, w, C))
            set_plane(xe[a], w + H, C, rim(packed, H * w))
        packed = [corner[...] for corner in corners]
        for i in range(H):
            set_plane(xm[a], i, C, zero)
            set_plane(xe[a], i, C, zero)
            set_plane(xm[a], last + i, C, zero)
            set_plane(xe[a], last + i, C, zero)
        count, first = face_planes(a)
        here = jnp.where(wall == 0, last, H - count)
        for p in range(count):
            set_plane(xm[a], here + p, C, wall_in[first + p])
            set_plane(xe[a], here + p, C, rim(packed, H * (first + p)))

    for side, (out, order) in enumerate(((to_next, (C - 1, C - 2, C - 3, C - 4)), (to_prev, (0, 1, 2, 3)))):
        adj = [dense_pair(xm[0], xe[0], r, N, C) for r in order]
        mask = [dense_pair(xm[2], xe[2], r, N, C) for r in order[:3]]
        q = []
        for k in range(3):
            ion = dense_pair(xm[1], xe[1], order[k], N, C)
            moved = dense_apply(adj[k], adj[k + 1], adj[k - 1] if k else None, SI)
            q.append([adj[k][j] - DT * mask[k][j] * (moved[j] + ion[j] * adj[k][j]) for j in range(2)])
        near = dense_apply(q[0], q[1], None, SI)
        mis = dense_pair(xm[3], xe[3], order[0], N, C)
        near = [near[j] + mis[j] for j in range(2)]
        second = dense_apply(q[1], q[2], q[0], SI)[0] + dense(xm[3], order[1], N, C)
        for value, (start, first, count) in zip((second, near[0], q[0][0], mask[0][0], adj[0][0]), near_rows(n_dir, W)):
            out[start : start + count, :] = value[first : first + count]
        group = lane_of((8, LANES)) // (H * n_dir)
        shift = jnp.where(length == 0, 0, H) if n_dir == 1 else H
        packs = [jnp.zeros((8, LANES), F32) for _ in range(n_dir)]
        for t, tile in enumerate(rim_tiles((near[1], q[0][1], mask[0][1], adj[0][1]))):
            k, at = divmod(t, LANES // (H * n_dir))
            turned = pltpu.roll(tile, lax.rem(shift + H * n_dir * at, LANES), 1)
            packs[k] = jnp.where(group == at, turned, packs[k])
        for k in range(n_dir):
            out[8 * k : 8 * k + 8, :] = packs[k]
        for k, pair in enumerate((adj[0], mask[0], q[0])):
            own_rows[side, 2 * k] = pair[0]
            own_rows[side, 2 * k + 1] = pair[1]


def spots(m_ref, e_ref, i, rows, coef):
    m, e = plane(m_ref, i, rows), plane(e_ref, i, rows)
    wm = plane(m_ref, i - 1, rows) + plane(m_ref, i + 1, rows)
    we = plane(e_ref, i - 1, rows) + plane(e_ref, i + 1, rows)
    lm, le = beside_lanes(m, e)
    cm, ce = beside_rows(m, 0.0, 0.0), beside_rows(e, 0.0, 0.0)
    double = 2.0 * sum(coef)
    dm = double * m - coef[0] * wm - coef[1] * cm - coef[2] * lm
    de = double * e - coef[0] * we - coef[1] * ce - coef[2] * le
    return m, e, dm, de


def rim_lanes(lane, length, n_len):
    return jnp.logical_or(
        jnp.logical_and(lane < H, length < n_len - 1),
        jnp.logical_and(lane >= LANES - H, length > 0),
    )


def inside(i, wall, W, n_wall):
    w = wall * W + i - H
    return jnp.logical_and(w >= 0, w < n_wall * W)


def halving():
    src = lax.broadcasted_iota(jnp.int32, (LANES, LANES), 0) // 2
    dst = lax.broadcasted_iota(jnp.int32, (LANES, LANES), 1)
    low = jnp.where(src == dst, 0.125, 0.0).astype(F32)
    high = jnp.where(src == dst - LANES // 2, 0.125, 0.0).astype(F32)
    return low, high


def precise(a, b):
    return jnp.dot(a, b, precision=HIGHEST, preferred_element_type=F32)


def sector(n_len, n_wall, C, xm0, xm1, xm2, xm3, xe0, xe1, xe2, xe3, qm, bm, be, coarse, surface, qe, pairs):
    xm, xe = (xm0, xm1, xm2, xm3), (xe0, xe1, xe2, xe3)
    N = qm.shape[0] // C
    W = N - 2 * H
    wall, length = lax.axis_index("wall"), lax.axis_index("len")
    rim = rim_lanes(lane_of((C, LANES)), length, n_len)
    zero = jnp.zeros((C, LANES), F32)
    for i in (0, N - 1):
        set_plane(qm, i, C, zero)
        set_plane(qe, i, C, zero)
    for i in (0, 1, N - 2, N - 1):
        set_plane(bm, i, C, zero)
        set_plane(be, i, C, zero)

    def parabolic(i):
        m, e, dm, de = spots(xm[0], xe[0], i, C, SI)
        set_plane(qm, i, C, m - DT * plane(xm[2], i, C) * (dm + plane(xm[1], i, C) * m))
        set_plane(qe, i, C, e - DT * plane(xe[2], i, C) * (de + plane(xe[1], i, C) * e))

    loop(1, N - 1, parabolic, 2)

    def elliptic_source(i):
        m, e, dm, de = spots(qm, qe, i, C, SI)
        ok = inside(i, wall, W, n_wall)
        set_plane(bm, i, C, jnp.where(ok, plane(xm[3], i, C) + dm, 0.0))
        set_plane(be, i, C, jnp.where(jnp.logical_and(rim, ok), plane(xe[3], i, C) + de, 0.0))

    loop(2, N - 2, elliptic_source, 2)

    coef, k0 = level_coef(0), level_step(0)

    def left(i):
        m, e = plane(bm, i, C), plane(be, i, C)
        wm = plane(bm, i - 1, C) + plane(bm, i + 1, C)
        cm = beside_rows(m, 0.0, 0.0)
        lm = beside_lanes_main(m, e)
        return m, (1.0 - OMEGA) * m + k0 * (coef[0] * wm + coef[1] * cm + coef[2] * lm)

    def pair(q):
        i = 2 * q + H
        m, first = left(i)
        n, second = left(i + 1)
        set_plane(pairs, q, C, first + second)

        @pl.when(jnp.logical_and(q == 0, wall == 0))
        def _():
            surface[...] = k0 * (m + first)

        @pl.when(jnp.logical_and(q == W // 2 - 1, wall == n_wall - 1))
        def _():
            surface[...] = k0 * (n + second)

    loop(0, W // 2, pair, 2)

    half = W * C // 8
    z = pairs[pl.ds(0, 2 * half, stride=2), :] + pairs[pl.ds(1, 2 * half, stride=2), :]
    low, high = halving()
    coarse[...] = precise(z[:half], low) + precise(z[half:], high)


def unpacked(ref, n_len, length, N):
    n_dir = 1 if n_len == 2 else 2
    mains = []
    for start, first, count in near_rows(n_dir, N - 2 * H):
        begin = min(start - first, ref.shape[0] - N)
        value = ref[begin : begin + N, :]
        behind = start - first - begin
        mains.append(pltpu.roll(value, N - behind, 0) if behind else value)
    rim = rim_lanes(lane_of((8, LANES)), length, n_len)
    shift = jnp.where(length == 0, 0, H) if n_dir == 1 else H
    rims = []
    for k in range(4):
        parts = []
        for s in range(N // 8):
            pack, at = divmod(k * (N // 8) + s, LANES // (H * n_dir))
            back = lax.rem(2 * LANES - shift - H * n_dir * at, LANES)
            parts.append(jnp.where(rim, pltpu.roll(ref[8 * pack : 8 * pack + 8, :], back, 1), 0.0))
        rims.append(jnp.concatenate(parts, 0))
    second, near, q, mask, adj = mains
    return (adj, rims[3]), (mask, rims[2]), (q, rims[1]), (near, rims[0]), second


def lateral(pair):
    return dense_apply(pair, None, None, SI)


def source_rows(own, other):
    adj_o, mask_o, q_o = own
    adj_n, mask_n, q_n, p_n, second_n = other
    step = DT * SI[1]
    delta_o = [step * mask_o[k] * adj_n[k] for k in range(2)]
    delta_n = [step * mask_n[k] * adj_o[k] for k in range(2)]
    lat_o, lat_n = lateral(delta_o), lateral(delta_n)
    near = [lat_o[k] - SI[1] * (q_n[k] + delta_n[k]) for k in range(2)]
    second = [-SI[1] * delta_o[k] for k in range(2)]
    halo = [p_n[k] + lat_n[k] - SI[1] * (q_o[k] + delta_o[k]) for k in range(2)]
    halo_second = second_n - SI[1] * delta_n[0]
    return near, second, halo, halo_second, delta_o[0]


def correct(electrodes, n_len, n_wall, own_rows, from_next, from_prev, coarse, surface, ids, *rest):
    rows_n, rows_p, message = rest[:3]
    lines, sums = rest[3:]
    _, C, L = ids.shape
    N = own_rows.shape[2]
    W = N - 2 * H
    wall, length = lax.axis_index("wall"), lax.axis_index("len")
    ok_m = inside(lax.broadcasted_iota(jnp.int32, (N, LANES), 0), wall, W, n_wall)
    ok_e = jnp.logical_and(ok_m, rim_lanes(lane_of((N, LANES)), length, n_len))
    coef, k0 = level_coef(0), level_step(0)
    y = surface[...]
    row = lax.broadcasted_iota(jnp.int32, (C, LANES), 0)
    at = pl.ds(jnp.where(wall == 0, H, W + H - 1), 1)
    lows, highs = [], []
    W1, C1 = W // 2, C // 2
    for side, (other, out, order) in enumerate(
        ((from_next, rows_n, (C - 1, C - 2, C - 3)), (from_prev, rows_p, (0, 1, 2)))
    ):
        own = [(own_rows[side, 2 * k], own_rows[side, 2 * k + 1]) for k in range(3)]
        near, second, halo, halo_second, delta = source_rows(own, unpacked(other, n_len, length, N))
        near = [jnp.where(ok_m, near[0], 0.0), jnp.where(ok_e, near[1], 0.0)]
        second = [jnp.where(ok_m, second[0], 0.0), jnp.where(ok_e, second[1], 0.0)]
        out[0] = halo_m = jnp.where(ok_m, halo[0], 0.0)
        out[1] = jnp.where(ok_e, halo[1], 0.0)
        out[2] = jnp.where(ok_m, halo_second, 0.0)
        out[3] = delta
        out[4], out[5] = near
        out[6], out[7] = second

        def turned(pair, beside):
            m, e = pair
            return (1.0 - OMEGA) * m + k0 * (
                coef[0] * beside_dense(m) + coef[2] * beside_lanes_main(m, e) + coef[1] * beside
            )

        first = turned(near, second[0] + halo_m)
        next_one = turned(second, near[0])
        third = k0 * coef[1] * second[0]
        for k, change in enumerate((near[0] + first, second[0] + next_one, third)):
            lines[0] = change
            y = y + jnp.where(row == order[k], k0 * lines[0, at, :], 0.0)
        for change in (first + next_one, third):
            lines[0] = change
            both = lines[0, pl.ds(H, W1, stride=2), :] + lines[0, pl.ds(H + 1, W1, stride=2), :]
            lows.append(both[: W1 // 2])
            highs.append(both[W1 // 2 :])
    low, high = halving()
    add = precise(jnp.concatenate(lows, 0), low) + precise(jnp.concatenate(highs, 0), high)
    half = W * C // 8
    message[0:half, :] = coarse[...]
    for k, c1 in enumerate((C1 - 1, C1 - 2, 0, 1)):
        spot = pl.ds(c1, W1 // 2, stride=C1)
        message[spot, :] = message[spot, :] + add[k * (W1 // 2) : (k + 1) * (W1 // 2)]
    patch = ids[0]
    message[half : half + C, :] = patch.astype(F32)
    wide = sums.shape[0]
    if wide > electrodes:
        sums[...] = jnp.zeros(sums.shape, F32)

    def one(e):
        sums[pl.ds(e, 1), :] = jnp.sum(jnp.where(patch == e, y, 0.0), axis=0, keepdims=True)

    loop(0, electrodes, one, 8)
    totals = lax.dot_general(
        jnp.ones((8, LANES), F32), sums[...], (((1,), (1,)), ((), ())), precision=HIGHEST, preferred_element_type=F32
    )
    message[half + C : half + C + 8, :] = jnp.zeros((8, LANES), F32)
    for t in range(wide // LANES):
        message[half + C + t : half + C + t + 1, :] = totals[0:1, t * LANES : (t + 1) * LANES]


def source_part(n_blk, n_len, n_wall, C, electrodes, bm, be, rows_n, rows_p, qm, mask, owner, base_adj, base_pot, *rest):
    patches, fm, fe, tm, te, hp = rest
    N = bm.shape[0] // C
    W = N - 2 * H
    blk, length, wall = lax.axis_index("blk"), lax.axis_index("len"), lax.axis_index("wall")
    fm[...] = bm[...]
    fe[...] = be[...]
    for rows, near, second in ((rows_n, C - 1, C - 2), (rows_p, 0, 1)):
        for k, at in ((4, near), (6, second)):
            spot = pl.ds(at, N, stride=C)
            fm[spot, :] = fm[spot, :] + rows[k]
            fe[spot, :] = fe[spot, :] + rows[k + 1]
    coef, k0 = level_coef(0), level_step(0)
    rim = rim_lanes(lane_of((C, LANES)), length, n_len)

    def part(i):
        m, e = plane(fm, i, C), plane(fe, i, C)
        wm = plane(fm, i - 1, C) + plane(fm, i + 1, C)
        we = plane(fe, i - 1, C) + plane(fe, i + 1, C)
        lm, le = beside_lanes(m, e)
        at = pl.ds(i, 1)
        cm = beside_rows(m, rows_p[0, at, :], rows_n[0, at, :])
        ce = beside_rows(e, rows_p[1, at, :], rows_n[1, at, :])
        pm = k0 * ((2.0 - OMEGA) * m + k0 * (coef[0] * wm + coef[1] * cm + coef[2] * lm))
        pe = k0 * ((2.0 - OMEGA) * e + k0 * (coef[0] * we + coef[1] * ce + coef[2] * le))
        set_plane(tm, i, C, jnp.where(inside(i, wall, W, n_wall), pm, 0.0))
        set_plane(te, i, C, jnp.where(rim, pe, 0.0))

    loop(H - 1, N - H + 1, part, 2)
    for side, (rows, at) in enumerate(((rows_n, C - 1), (rows_p, 0))):
        m = rows[0]
        total = (
            coef[0] * beside_dense(m)
            + coef[1] * (rows[2] + dense(fm, at, N, C))
            + coef[2] * beside_lanes_main(m, rows[1])
        )
        hp[side] = k0 * ((2.0 - OMEGA) * m + k0 * total)
    row = lax.broadcasted_iota(jnp.int32, (C, LANES), 0)

    def finish(w):
        i = w + H
        m, e = plane(tm, i, C), plane(te, i, C)
        at = pl.ds(i, 1)
        wm = plane(tm, i - 1, C) + plane(tm, i + 1, C)
        cm = beside_rows(m, hp[1, at, :], hp[0, at, :])
        lm = beside_lanes_main(m, e)
        lam = plane(qm, i, C)
        lam = lam + jnp.where(row == C - 1, rows_n[3, at, :], 0.0) + jnp.where(row == 0, rows_p[3, at, :], 0.0)
        moved = 2.0 * sum(SI) * m - SI[0] * wm - SI[1] * cm - SI[2] * lm
        set_plane(base_adj, w, C, lam - DT * plane(mask, i, C) * moved)
        set_plane(base_pot, w, C, m)

    loop(0, W, finish, 2)

    me = (blk * n_len + length) * n_wall + wall
    which = lax.broadcasted_iota(jnp.int32, (1, electrodes), 1).astype(F32)
    mine = owner[...] == me
    patches[0:1, :] = jnp.full((1, LANES), jnp.min(jnp.where(mine, which, float(electrodes))))
    patches[1:2, :] = jnp.full((1, LANES), jnp.max(jnp.where(mine, which, -1.0)))
    patches[2:8, :] = jnp.zeros((6, LANES), F32)


def around(x, by):
    rows, lanes = x.shape
    lane = lane_of(x.shape)
    c = pltpu.roll(x, by, 0) + pltpu.roll(x, rows - by, 0)
    l = jnp.where(lane < by, 0.0, pltpu.roll(x, by, 1)) + jnp.where(
        lane >= lanes - by, 0.0, pltpu.roll(x, lanes - by, 1)
    )
    return c, l


def twins(x, by):
    rows, lanes = x.shape
    row = lax.broadcasted_iota(jnp.int32, x.shape, 0)
    lane = lane_of(x.shape)
    x = x + jnp.where((row & by) == 0, pltpu.roll(x, rows - by, 0), pltpu.roll(x, by, 0))
    return x + jnp.where((lane & by) == 0, pltpu.roll(x, lanes - by, 1), pltpu.roll(x, by, 1))


def solve(sizes, relative, C, W, *refs):
    n_blk, n_len, n_wall = sizes
    count = n_len * n_wall
    blocks, refs = refs[:count], refs[count:]
    base_adj, base_pot, mask, patches, adj_prev, potential, patch_grad = refs[:7]
    b1, x1, b2, x2, b3, x3, near, wide, pm, pe, tm, te, adj_out, pot_out, sheet, sems = refs[7:]
    L = LANES
    W1, C1 = W // 2, C // 2
    planes, NC1, NL1 = b1.shape
    planes -= 2
    blk, length, wall = lax.axis_index("blk"), lax.axis_index("len"), lax.axis_index("wall")
    half = W1 // 2
    middle = LANES // 2
    lane8 = lane_of((C1, LANES))
    often = 8 if NC1 * NL1 <= 4096 else 1

    def blk_of(d):
        return lax.rem(blk - d + n_blk, n_blk) if relative else d

    def length_of(j):
        return (length + j) % n_len if n_len == 2 else j

    zero1 = jnp.zeros((NC1, NL1), F32)
    for ref in (b1, x1, b2, x2, b3, x3):
        ref[0] = zero1
        ref[ref.shape[0] - 1] = zero1

    for v in range(n_wall):
        wall_s = (wall + v) % n_wall
        mine = blocks[v * n_len : (v + 1) * n_len]

        def unpack(d):
            at = pl.ds(pl.multiple_of(C1 * blk_of(d), C1), C1)
            for t in range(n_len // 2):
                one, two = mine[2 * t], mine[2 * t + 1]
                for i in range(half):
                    a, b = one[d, i * C1 : (i + 1) * C1, :], two[d, i * C1 : (i + 1) * C1, :]
                    if n_len == 2:
                        a, b = jnp.where(length == 0, a, b), jnp.where(length == 0, b, a)
                    spot = 1 + wall_s * W1 + i
                    lanes = slice(t * LANES, (t + 1) * LANES)
                    b1[spot, at, lanes] = jnp.where(lane8 < middle, a, pltpu.roll(b, middle, 1))
                    b1[spot + half, at, lanes] = jnp.where(lane8 < middle, pltpu.roll(a, middle, 1), b)

        loop(0, n_blk, unpack, 4)

    def total_of(x, wsum, level, by):
        coef = level_coef(level)
        c, l = around(x, by)
        return level_step(level) * (coef[0] * wsum + coef[1] * c + coef[2] * l)

    def left(ref, i, level):
        b = ref[i]
        return (1.0 - OMEGA) * b + total_of(b, ref[i - 1] + ref[i + 1], level, 2 ** (level - 1))

    def sweep(x_ref, b_ref, i, level):
        x = x_ref[i]
        total = total_of(x, x_ref[i - 1] + x_ref[i + 1], level, 2 ** (level - 1))
        return (1.0 - OMEGA) * x + level_step(level) * b_ref[i] + total

    def down1(q):
        b2[1 + q] = 0.125 * twins(left(b1, 2 * q + 1, 1) + left(b1, 2 * q + 2, 1), 1)

    loop(0, planes // 2, down1, often)

    def down2(q):
        b3[1 + q] = 0.125 * twins(left(b2, 2 * q + 1, 2) + left(b2, 2 * q + 2, 2), 2)

    loop(0, planes // 4, down2, often)

    deep = planes // 4
    k3 = level_step(3)

    def start3(q):
        x3[1 + q] = k3 * b3[1 + q]

    loop(0, deep, start3, often)
    for k in range(SWEEPS):
        from_ref, to_ref = (x3, x2) if k % 2 == 0 else (x2, x3)

        if k == 1:
            x2[1 + deep] = zero1

        def sweep3(q):
            to_ref[1 + q] = sweep(from_ref, b3, 1 + q, 3)

        loop(0, deep, sweep3, often)
    deepest = x3 if SWEEPS % 2 == 0 else x2
    assert deepest is x3
    k2 = level_step(2)

    def up2(q):
        coarse = x3[1 + q]
        x2[1 + 2 * q] = k2 * b2[1 + 2 * q] + coarse
        x2[2 + 2 * q] = k2 * b2[2 + 2 * q] + coarse

    loop(0, planes // 4, up2, often)

    k1 = level_step(1)

    def up1(q):
        fine = sweep(x2, b2, 1 + q, 2)
        x1[1 + 2 * q] = k1 * b1[1 + 2 * q] + fine
        x1[2 + 2 * q] = k1 * b1[2 + 2 * q] + fine

    loop(0, planes // 2, up1, often)

    Q = W1 + 2
    sectors = (blk, lax.rem(blk + 1, n_blk), lax.rem(blk + n_blk - 1, n_blk))
    spots3 = [pl.ds(pl.multiple_of(s * C1, C1), C1) for s in sectors]
    row8 = lax.broadcasted_iota(jnp.int32, (C1, NL1), 0)
    NR = 2 * C1

    def three(ref, i):
        return jnp.concatenate([ref[i, s, :] for s in spots3], 0)

    def finish1(q):
        i = wall * W1 + q
        x = three(x1, i)
        wsum = three(x1, jnp.maximum(i - 1, 0)) + three(x1, jnp.minimum(i + 1, planes + 1))
        value = (1.0 - OMEGA) * x + k1 * three(b1, i) + total_of(x, wsum, 1, 1)
        value = jnp.where(jnp.logical_and(i >= 1, i <= planes), value, 0.0)
        set_plane(near, 2 * q, C1, value[:C1])
        set_plane(near, 2 * q + 1, C1, jnp.where(row8 < 2, value[C1 : 2 * C1], value[2 * C1 :]))

    loop(0, Q, finish1, min(often, 6))

    lane = lane_of((NL1, LANES))
    source = lax.broadcasted_iota(jnp.int32, (NL1, LANES), 0)
    first = length * middle
    take_m = jnp.where(source == first + lane // 2, 1.0, 0.0).astype(F32)
    at_e = jnp.where(lane < H, middle + lane // 2, jnp.where(lane >= LANES - H, lane // 2 - middle, 4 * NL1))
    take_e = jnp.where(source == first + at_e, 1.0, 0.0).astype(F32)
    R = C + 8
    row8 = lax.broadcasted_iota(jnp.int32, (8, LANES), 0)
    for out, sel in ((pm, take_m), (pe, take_e)):
        value = precise(near[...], sel)
        wide[pl.ds(0, Q * NR, stride=2), :] = value
        wide[pl.ds(1, Q * NR, stride=2), :] = value
        for q in range(Q):
            base = 2 * NR * q
            out[R * q : R * q + C, :] = wide[base : base + C, :]
            out[R * q + C : R * (q + 1), :] = jnp.where(
                row8 < H, wide[base + C : base + C + 8, :], wide[base + 2 * NR - 8 : base + 2 * NR, :]
            )
    coef, k0 = level_coef(0), level_step(0)
    rim = rim_lanes(lane_of((R, LANES)), length, n_len)

    def rows_beside(x):
        return pltpu.roll(x, 1, 0) + pltpu.roll(x, x.shape[0] - 1, 0)

    def coarse_terms(q):
        m, e = plane(pm, q, R), plane(pe, q, R)
        lm, le = beside_lanes(m, e)
        gm = (1.0 - OMEGA) * m + k0 * (coef[0] * m + coef[1] * rows_beside(m) + coef[2] * lm)
        ge = (1.0 - OMEGA) * e + k0 * (coef[0] * e + coef[1] * rows_beside(e) + coef[2] * le)
        return gm, ge

    ks = k0 * coef[0]

    def put(t, gm, ge, other, ok):
        m = gm + ks * plane(pm, other, R)
        e = jnp.where(rim, ge + ks * plane(pe, other, R), 0.0)
        if ok is not None:
            m, e = jnp.where(ok, m, 0.0), jnp.where(ok, e, 0.0)
        set_plane(tm, t, R, m)
        set_plane(te, t, R, e)

    put(0, *coarse_terms(0), 1, wall > 0)
    put(W + 1, *coarse_terms(Q - 1), Q - 2, wall < n_wall - 1)

    def level0(q):
        gm, ge = coarse_terms(q)
        put(2 * q - 1, gm, ge, q - 1, None)
        put(2 * q, gm, ge, q + 1, None)
        for w in (2 * q - 2, 2 * q - 1):
            set_plane(pot_out, w, C, plane(base_pot, w, C) + plane(tm, w + 1, R)[:C])

    def finish0(w):
        m, e = plane(tm, w + 1, R), plane(te, w + 1, R)[:C]
        cm = rows_beside(m)[:C]
        m = m[:C]
        wm = plane(tm, w, R)[:C] + plane(tm, w + 2, R)[:C]
        lm = beside_lanes_main(m, e)
        moved = 2.0 * sum(SI) * m - SI[0] * wm - SI[1] * cm - SI[2] * lm
        set_plane(adj_out, w, C, plane(base_adj, w, C) - DT * plane(mask, w + H, C) * moved)

    parts = 2
    size = W // parts
    copies = []

    def send(src, dst, k, sem):
        spot = pl.ds(k * size * C, size * C)
        copies.append(pltpu.make_async_copy(src.at[spot], dst.at[spot], sem))
        copies[-1].start()

    for k in range(parts):
        loop(1 + k * W1 // parts, 1 + (k + 1) * W1 // parts, level0, 4)
        send(pot_out, potential, k, sems.at[0, k])
    for k in range(parts):
        loop(k * size, (k + 1) * size, finish0, 4)
        send(adj_out, adj_prev, k, sems.at[1, k])

    NC, NL = sheet.shape[1:]
    twice_c = jnp.where(
        lax.broadcasted_iota(jnp.int32, (NC, NC1), 0) // 2 == lax.broadcasted_iota(jnp.int32, (NC, NC1), 1), 1.0, 0.0
    ).astype(F32)
    twice_l = jnp.where(
        lax.broadcasted_iota(jnp.int32, (NL1, NL), 1) // 2 == lax.broadcasted_iota(jnp.int32, (NL1, NL), 0), 1.0, 0.0
    ).astype(F32)
    for s, i in enumerate((1, planes)):
        p = precise(precise(twice_c, sweep(x1, b1, i, 1)), twice_l)
        c, l = around(p, 1)
        sheet[s] = (1.0 - OMEGA) * p + k0 * (coef[0] * p + coef[1] * c + coef[2] * l)

    owned = [patches[r : r + 1, :] for r in range(2)]
    spot = lax.broadcasted_iota(jnp.int32, (8, LANES), 0) * LANES + lane_of((8, LANES))
    spot = spot.astype(F32)
    start = half * C1
    totals = [jnp.zeros((C, LANES), F32) for _ in owned]
    small = [jnp.zeros((8, LANES), F32) for _ in owned]
    for v in range(n_wall):
        wall_s = (wall + v) % n_wall
        for j in range(n_len):
            ref = blocks[v * n_len + j]
            at_l = pl.ds(pl.multiple_of(length_of(j) * L, L), L)

            def add(d, carry):
                big, little = carry
                values = sheet[wall_s, pl.ds(pl.multiple_of(blk_of(d) * C, C), C), at_l]
                ids = ref[d, start : start + C, :]
                parts = ref[d, start + C : start + C + 8, :]
                big = [x + jnp.where(ids == e, values, 0.0) for x, e in zip(big, owned)]
                little = [x + jnp.where(spot == e, parts, 0.0) for x, e in zip(little, owned)]
                return big, little

            totals, small = lax.fori_loop(0, n_blk, add, (totals, small), unroll=min(4, n_blk))
    factor = 1.0 / (2.0 * C * L / 2) ** 0.5
    for r in range(2):
        patch_grad[0, r] = (jnp.sum(totals[r]) + jnp.sum(small[r])) * factor
    for copy in copies:
        copy.wait()


def ring(x, axis, by):
    count = lax.axis_size(axis)
    return lax.ppermute(x, axis, [(i, (i + by) % count) for i in range(count)])


def across(x):
    n_wall = lax.axis_size("wall")
    pairs = [(l * n_wall + w, (1 - l) * n_wall + (w + 1) % n_wall) for l in range(2) for w in range(n_wall)]
    return lax.ppermute(x, ("len", "wall"), pairs)


def call(kernel, ins, outs, scratch, name, work=0, room=48):
    places = {"vmem": pltpu.VMEM, "smem": pltpu.SMEM, "any": pl.ANY, "hbm": pltpu.HBM}

    def specs(kinds):
        return [pl.BlockSpec(memory_space=places[kind]) for kind in kinds]

    cost = pl.CostEstimate(flops=work, bytes_accessed=work, transcendentals=0) if work else None
    return pl.pallas_call(
        kernel,
        out_shape=[jax.ShapeDtypeStruct(shape, F32) for shape, _ in outs],
        in_specs=specs(ins),
        out_specs=specs(kind for _, kind in outs),
        scratch_shapes=[pltpu.VMEM(shape, F32) if isinstance(shape, tuple) else shape for shape in scratch],
        compiler_params=pltpu.CompilerParams(vmem_limit_bytes=int(room * 2**20)),
        cost_estimate=cost,
        name=name,
    )


def body(adj_next, ion_slope, misfit, tissue_mask, patch_ids, owner_map):
    W, C, L = adj_next.shape
    n_blk, n_len, n_wall = lax.axis_size("blk"), lax.axis_size("len"), lax.axis_size("wall")
    electrodes = owner_map.shape[0]
    assert L == LANES and H * W == LANES and n_wall == 2 and electrodes == 2 * n_blk * n_len * n_wall
    N = W + 2 * H
    n_dir = 1 if n_len == 2 else 2
    cells = W * C
    vmem = "vmem"
    field, own = (N * C, L), (cells, L)
    raw = [x.reshape(cells, L) for x in (adj_next, ion_slope, tissue_mask, misfit)]

    *fields, wall_out = (faces := call(
        functools.partial(pack_faces, n_len),
        ["hbm"] * 4,
        [(own, vmem)] * 4
        + [((sum(FACES), C, L), vmem)]
        + [((4, C, L), vmem)] * n_dir
        + [((C, L), vmem)] * n_dir,
        [pltpu.VMEM(own, jnp.int32), pltpu.SemaphoreType.DMA((4, 2))],
        "faces",
        room=52.75,
    )(*raw))[:5]
    strip_out, corner_out = faces[5 : 5 + n_dir], faces[5 + n_dir :]
    wall_in = ring(wall_out, "wall", 1)
    if n_dir == 1:
        strips = [ring(strip_out[0], "len", 1)]
        corners = [across(corner_out[0])]
    else:
        strips = [ring(strip_out[1], "len", -1), ring(strip_out[0], "len", 1)]
        corners = [ring(ring(corner_out[1], "wall", 1), "len", -1), ring(ring(corner_out[0], "wall", 1), "len", 1)]

    near = (sum(near_rows(n_dir, W)[-1][::2]), L)
    *fields, to_next, to_prev, own_rows = call(
        functools.partial(boundary, n_len, C),
        [vmem] * (5 + 2 * n_dir),
        [(field, vmem)] * 8 + [(near, vmem)] * 2 + [((2, 6, N, L), vmem)],
        [],
        "boundary",
    )(*fields, wall_in, *strips, *corners)
    from_next = ring(to_prev, "blk", -1)
    from_prev = ring(to_next, "blk", 1)
    qm, bm, be, coarse, surface = call(
        functools.partial(sector, n_len, n_wall, C),
        [vmem] * 8,
        [(field, vmem)] * 3 + [((cells // 8, L), vmem), ((C, L), vmem)],
        [field, (cells // 2, L)],
        "sector",
        work=16 * 10**6,
    )(*fields)

    rows = (8, N, L)
    wide = LANES * ((electrodes + LANES - 1) // LANES)
    message = (cells // 8 + C + 8, L)
    rows_n, rows_p, mine = call(
        functools.partial(correct, electrodes, n_len, n_wall),
        [vmem] * 6,
        [(rows, vmem), (rows, vmem), (message, vmem)],
        [(1, N, L), (wide, L)],
        "correct",
    )(own_rows, from_next, from_prev, coarse, surface, patch_ids)

    relative = n_blk <= 4
    moved = [ring(mine, "blk", d) for d in range(1, n_blk)] if relative else [lax.all_gather(mine, "blk")]
    base_adj, base_pot, patches = call(
        functools.partial(source_part, n_blk, n_len, n_wall, C, electrodes),
        [vmem] * 7,
        [(own, vmem), (own, vmem), ((8, L), vmem)],
        [field] * 4 + [(2, N, L)],
        "source_part",
        work=12 * 10**6,
    )(bm, be, rows_n, rows_p, qm, fields[2], owner_map.reshape(1, electrodes))
    moved, base_adj = lax.optimization_barrier((moved, base_adj))
    sector_blocks = jnp.stack([mine] + moved) if relative else moved[0]
    if n_len == 2:
        here = [sector_blocks, ring(sector_blocks, "len", 1)]
    else:
        gathered = lax.all_gather(sector_blocks, "len")
        here = [gathered[j] for j in range(n_len)]
    blocks = here + [ring(x, "wall", 1) for x in here]

    NC1, NL1 = n_blk * C // 2, n_len * L // 2
    planes = n_wall * W // 2
    grids = [(planes // k + 2, NC1, NL1) for k in (1, 1, 2, 2, 4, 4)]
    Q = W // 2 + 2
    tall = (Q * (C + 8), L)
    taller = ((W + 2) * (C + 8), L)
    scratch = grids + [(Q * C, NL1), (2 * Q * C, L), tall, tall, taller, taller, own, own]
    scratch += [(2, n_blk * C, n_len * L), pltpu.SemaphoreType.DMA((2, 2))]
    adj_prev, potential, patch_grad = call(
        functools.partial(solve, (n_blk, n_len, n_wall), relative, C, W),
        [vmem] * (n_len * n_wall + 4),
        [(own, "any"), (own, "any"), ((1, 2), "smem")],
        scratch,
        "solve",
    )(*blocks, base_adj, base_pot, fields[2], patches)
    return adj_prev.reshape(W, C, L), potential.reshape(W, C, L), patch_grad


def solution(mesh):
    field = P(("groups", "wall"), "blk", "len")
    return jax.shard_map(
        body,
        mesh=mesh,
        in_specs=(field, field, field, field, field, P("groups")),
        out_specs=(field, field, P(("groups", "blk", "len", "wall"), None)),
        check_vma=False,
    )
```

```python
import functools

import jax
import jax.numpy as jnp
from jax import lax
from jax.experimental import pallas as pl
from jax.experimental.pallas import tpu as pltpu
from jax.sharding import PartitionSpec as P

SWEEPS = 2
SI = (0.6, 1.0, 3.0)
SE = (0.8, 1.2, 2.0)
SHIFT = 0.002
OMEGA = 0.8
DT = 0.1
H = 4
LANES = 128
HIGHEST = lax.Precision.HIGHEST
F32 = jnp.float32


def level_coef(level):
    return tuple((SI[i] + SE[i]) / 4.0**level for i in range(3))


def level_diag(level):
    return SHIFT + 2.0 * sum(level_coef(level))


def level_step(level):
    return OMEGA / level_diag(level)


def lane_of(shape):
    return lax.broadcasted_iota(jnp.int32, shape, len(shape) - 1)


def before(m, e):
    first = lane_of(m.shape) == 0
    rm, re = pltpu.roll(m, 1, 1), pltpu.roll(e, 1, 1)
    return jnp.where(first, re, rm), jnp.where(first, rm, re)


def after(m, e):
    last = lane_of(m.shape) == LANES - 1
    rm, re = pltpu.roll(m, LANES - 1, 1), pltpu.roll(e, LANES - 1, 1)
    return jnp.where(last, re, rm), jnp.where(last, rm, re)


def beside_lanes(m, e):
    bm, be = before(m, e)
    am, ae = after(m, e)
    return bm + am, be + ae


def beside_lanes_main(m, e):
    lane = lane_of(m.shape)
    left = jnp.where(lane == 0, pltpu.roll(e, 1, 1), pltpu.roll(m, 1, 1))
    right = jnp.where(lane == LANES - 1, pltpu.roll(e, LANES - 1, 1), pltpu.roll(m, LANES - 1, 1))
    return left + right


def beside_rows(x, row_before, row_after):
    rows = x.shape[0]
    row = lax.broadcasted_iota(jnp.int32, x.shape, 0)
    low = jnp.where(row == 0, row_before, pltpu.roll(x, 1, 0))
    high = jnp.where(row == rows - 1, row_after, pltpu.roll(x, rows - 1, 0))
    return low + high


def beside_dense(x):
    return pltpu.roll(x, 1, 0) + pltpu.roll(x, x.shape[0] - 1, 0)


def plane(ref, i, rows):
    return ref[pl.ds(pl.multiple_of(i * rows, rows), rows), :]


def set_plane(ref, i, rows, value):
    ref[pl.ds(pl.multiple_of(i * rows, rows), rows), :] = value


def loop(low, high, step, unroll):
    def wrapped(i, carry):
        step(i)
        return carry

    lax.fori_loop(low, high, wrapped, 0, unroll=min(unroll, high - low))


FACES = (H, H - 1, H - 1, H - 2)


def face_planes(array):
    return FACES[array], sum(FACES[:array])


def pack_faces(n_len, adj, ion, mask, mis, *rest):
    n_dir = 1 if n_len == 2 else 2
    fields, wall_out, rest = rest[:4], rest[4], rest[5:]
    strips, corners = rest[:n_dir], rest[n_dir : 2 * n_dir]
    whole_mask, sems = rest[2 * n_dir :]
    cells = adj.shape[0]
    C = wall_out.shape[1]
    W = cells // C
    wall, length = lax.axis_index("wall"), lax.axis_index("len")
    targets = (fields[0], fields[1], whole_mask, fields[3])
    copies = []
    for a, (src, dst) in enumerate(zip((adj, ion, mask, mis), targets)):
        part = cells // 2
        for k in range(2):
            spot = pl.ds(k * part, part)
            copies.append(pltpu.make_async_copy(src.at[spot], dst.at[spot], sems.at[a, k]))
            copies[-1].start()

    base = jnp.where(wall == 0, W - H, 0)
    group = lane_of((C, LANES)) // H
    turns = [jnp.where(length == 0, H, 0)] if n_dir == 1 else [H, 0]
    corner = [jnp.zeros((C, LANES), F32) for _ in range(n_dir)]
    for a in (0, 1, 3, 2):
        copies[2 * a].wait()
        copies[2 * a + 1].wait()
        if a == 2:
            fields[2][...] = whole_mask[...].astype(F32)
        ref = fields[a]
        strip = [jnp.zeros((C, LANES), F32) for _ in range(n_dir)]
        for w in range(W):
            value = ref[w * C : (w + 1) * C, :]
            for d in range(n_dir):
                turned = pltpu.roll(value, lax.rem(H * w + turns[d], LANES), 1)
                strip[d] = jnp.where(group == w, turned, strip[d])
        for d in range(n_dir):
            strips[d][a] = strip[d]
        count, first = face_planes(a)
        for p in range(count):
            face = plane(ref, base + jnp.where(wall == 0, H - count, 0) + p, C)
            wall_out[first + p] = face
            slot = first + p
            for d in range(n_dir):
                turned = pltpu.roll(face, lax.rem(H * slot + turns[d], LANES), 1)
                corner[d] = jnp.where(group == slot, turned, corner[d])
    for d in range(n_dir):
        corners[d][...] = corner[d]


def dense(ref, row, N, C):
    return ref[pl.ds(row, N, stride=C), :]


def dense_pair(m, e, row, N, C):
    return dense(m, row, N, C), dense(e, row, N, C)


def dense_apply(pair, inner, outer, coef):
    m, e = pair
    lm, le = beside_lanes(m, e)
    double = 2.0 * sum(coef)
    out = [double * m - coef[0] * beside_dense(m) - coef[2] * lm, double * e - coef[0] * beside_dense(e) - coef[2] * le]
    for row in (inner, outer):
        if row is not None:
            out = [out[k] - coef[1] * row[k] for k in range(2)]
    return out


def near_rows(n_dir, W):
    start, places = 8 * n_dir, []
    for reach in (0, 1, 2, 2, 3):
        places.append((start, H - reach, W + 2 * reach))
        start += W + 2 * reach
    assert start % 8 == 0
    return places


def rim_tiles(values):
    return [value[s : s + 8] for value in values for s in range(0, value.shape[0], 8)]


def boundary(n_len, C, xm0, xm1, xm2, xm3, wall_in, *rest):
    n_dir = 1 if n_len == 2 else 2
    strips, corners, rest = rest[:n_dir], rest[n_dir : 2 * n_dir], rest[2 * n_dir :]
    xm, xe, to_next, to_prev, own_rows = rest[:4], rest[4:8], rest[8], rest[9], rest[10]
    N = xm[0].shape[0] // C
    W = N - 2 * H
    wall, length = lax.axis_index("wall"), lax.axis_index("len")
    lane = lane_of((C, LANES))
    if n_dir == 1:
        offs, valid = [jnp.where(length == 0, 0, LANES - H)], [True]
    else:
        offs, valid = [0, LANES - H], [length < n_len - 1, length > 0]
    seen = [jnp.logical_and(lax.rem(lane - off + LANES, LANES) < H, ok) for off, ok in zip(offs, valid)]

    def rim(packed, base):
        out = jnp.zeros((C, LANES), F32)
        for d in range(n_dir):
            out = jnp.where(seen[d], pltpu.roll(packed[d], lax.rem(offs[d] - base + LANES, LANES), 1), out)
        return out

    zero = jnp.zeros((C, LANES), F32)
    last = N - H
    for a, own in enumerate((xm0, xm1, xm2, xm3)):
        packed = [strip[a] for strip in strips]
        for w in range(W):
            set_plane(xm[a], w + H, C, plane(own, w, C))
            set_plane(xe[a], w + H, C, rim(packed, H * w))
        packed = [corner[...] for corner in corners]
        for i in range(H):
            set_plane(xm[a], i, C, zero)
            set_plane(xe[a], i, C, zero)
            set_plane(xm[a], last + i, C, zero)
            set_plane(xe[a], last + i, C, zero)
        count, first = face_planes(a)
        here = jnp.where(wall == 0, last, H - count)
        for p in range(count):
            set_plane(xm[a], here + p, C, wall_in[first + p])
            set_plane(xe[a], here + p, C, rim(packed, H * (first + p)))

    for side, (out, order) in enumerate(((to_next, (C - 1, C - 2, C - 3, C - 4)), (to_prev, (0, 1, 2, 3)))):
        adj = [dense_pair(xm[0], xe[0], r, N, C) for r in order]
        mask = [dense_pair(xm[2], xe[2], r, N, C) for r in order[:3]]
        q = []
        for k in range(3):
            ion = dense_pair(xm[1], xe[1], order[k], N, C)
            moved = dense_apply(adj[k], adj[k + 1], adj[k - 1] if k else None, SI)
            q.append([adj[k][j] - DT * mask[k][j] * (moved[j] + ion[j] * adj[k][j]) for j in range(2)])
        near = dense_apply(q[0], q[1], None, SI)
        mis = dense_pair(xm[3], xe[3], order[0], N, C)
        near = [near[j] + mis[j] for j in range(2)]
        second = dense_apply(q[1], q[2], q[0], SI)[0] + dense(xm[3], order[1], N, C)
        for value, (start, first, count) in zip((second, near[0], q[0][0], mask[0][0], adj[0][0]), near_rows(n_dir, W)):
            out[start : start + count, :] = value[first : first + count]
        group = lane_of((8, LANES)) // (H * n_dir)
        shift = jnp.where(length == 0, 0, H) if n_dir == 1 else H
        packs = [jnp.zeros((8, LANES), F32) for _ in range(n_dir)]
        for t, tile in enumerate(rim_tiles((near[1], q[0][1], mask[0][1], adj[0][1]))):
            k, at = divmod(t, LANES // (H * n_dir))
            turned = pltpu.roll(tile, lax.rem(shift + H * n_dir * at, LANES), 1)
            packs[k] = jnp.where(group == at, turned, packs[k])
        for k in range(n_dir):
            out[8 * k : 8 * k + 8, :] = packs[k]
        for k, pair in enumerate((adj[0], mask[0], q[0])):
            own_rows[side, 2 * k] = pair[0]
            own_rows[side, 2 * k + 1] = pair[1]


def spots(m_ref, e_ref, i, rows, coef):
    m, e = plane(m_ref, i, rows), plane(e_ref, i, rows)
    wm = plane(m_ref, i - 1, rows) + plane(m_ref, i + 1, rows)
    we = plane(e_ref, i - 1, rows) + plane(e_ref, i + 1, rows)
    lm, le = beside_lanes(m, e)
    cm, ce = beside_rows(m, 0.0, 0.0), beside_rows(e, 0.0, 0.0)
    double = 2.0 * sum(coef)
    dm = double * m - coef[0] * wm - coef[1] * cm - coef[2] * lm
    de = double * e - coef[0] * we - coef[1] * ce - coef[2] * le
    return m, e, dm, de


def rim_lanes(lane, length, n_len):
    return jnp.logical_or(
        jnp.logical_and(lane < H, length < n_len - 1),
        jnp.logical_and(lane >= LANES - H, length > 0),
    )


def inside(i, wall, W, n_wall):
    w = wall * W + i - H
    return jnp.logical_and(w >= 0, w < n_wall * W)


def lanes_at(x, index):
    return jnp.take_along_axis(x, index, axis=1, mode="promise_in_bounds")


def rows_at(x, index):
    return jnp.take_along_axis(x, index, axis=0, mode="promise_in_bounds")


def halved(low, high):
    lane = lane_of(low.shape)
    even = 2 * lane % LANES
    pairs = [lanes_at(x, even) + lanes_at(x, even + 1) for x in (low, high)]
    return 0.125 * jnp.where(lane < LANES // 2, pairs[0], pairs[1])


def precise(a, b):
    return jnp.dot(a, b, precision=HIGHEST, preferred_element_type=F32)


def sector(n_len, n_wall, C, xm0, xm1, xm2, xm3, xe0, xe1, xe2, xe3, qm, bm, be, coarse, surface, qe, pairs):
    xm, xe = (xm0, xm1, xm2, xm3), (xe0, xe1, xe2, xe3)
    N = qm.shape[0] // C
    W = N - 2 * H
    wall, length = lax.axis_index("wall"), lax.axis_index("len")
    rim = rim_lanes(lane_of((C, LANES)), length, n_len)
    zero = jnp.zeros((C, LANES), F32)
    for i in (0, N - 1):
        set_plane(qm, i, C, zero)
        set_plane(qe, i, C, zero)
    for i in (0, 1, N - 2, N - 1):
        set_plane(bm, i, C, zero)
        set_plane(be, i, C, zero)

    def parabolic(i):
        m, e, dm, de = spots(xm[0], xe[0], i, C, SI)
        set_plane(qm, i, C, m - DT * plane(xm[2], i, C) * (dm + plane(xm[1], i, C) * m))
        set_plane(qe, i, C, e - DT * plane(xe[2], i, C) * (de + plane(xe[1], i, C) * e))

    loop(1, N - 1, parabolic, 2)

    def elliptic_source(i):
        m, e, dm, de = spots(qm, qe, i, C, SI)
        ok = inside(i, wall, W, n_wall)
        set_plane(bm, i, C, jnp.where(ok, plane(xm[3], i, C) + dm, 0.0))
        set_plane(be, i, C, jnp.where(jnp.logical_and(rim, ok), plane(xe[3], i, C) + de, 0.0))

    loop(2, N - 2, elliptic_source, 2)

    coef, k0 = level_coef(0), level_step(0)

    def left(i):
        m, e = plane(bm, i, C), plane(be, i, C)
        wm = plane(bm, i - 1, C) + plane(bm, i + 1, C)
        cm = beside_rows(m, 0.0, 0.0)
        lm = beside_lanes_main(m, e)
        return m, (1.0 - OMEGA) * m + k0 * (coef[0] * wm + coef[1] * cm + coef[2] * lm)

    def pair(q):
        i = 2 * q + H
        m, first = left(i)
        n, second = left(i + 1)
        set_plane(pairs, q, C, first + second)

        @pl.when(jnp.logical_and(q == 0, wall == 0))
        def _():
            surface[...] = k0 * (m + first)

        @pl.when(jnp.logical_and(q == W // 2 - 1, wall == n_wall - 1))
        def _():
            surface[...] = k0 * (n + second)

    loop(0, W // 2, pair, 2)

    half = W * C // 8
    z = pairs[pl.ds(0, 2 * half, stride=2), :] + pairs[pl.ds(1, 2 * half, stride=2), :]
    coarse[...] = halved(z[:half], z[half:])


def unpacked(ref, n_len, length, N):
    n_dir = 1 if n_len == 2 else 2
    mains = []
    for start, first, count in near_rows(n_dir, N - 2 * H):
        begin = min(start - first, ref.shape[0] - N)
        value = ref[begin : begin + N, :]
        behind = start - first - begin
        mains.append(pltpu.roll(value, N - behind, 0) if behind else value)
    rim = rim_lanes(lane_of((8, LANES)), length, n_len)
    shift = jnp.where(length == 0, 0, H) if n_dir == 1 else H
    rims = []
    for k in range(4):
        parts = []
        for s in range(N // 8):
            pack, at = divmod(k * (N // 8) + s, LANES // (H * n_dir))
            back = lax.rem(2 * LANES - shift - H * n_dir * at, LANES)
            parts.append(jnp.where(rim, pltpu.roll(ref[8 * pack : 8 * pack + 8, :], back, 1), 0.0))
        rims.append(jnp.concatenate(parts, 0))
    second, near, q, mask, adj = mains
    return (adj, rims[3]), (mask, rims[2]), (q, rims[1]), (near, rims[0]), second


def lateral(pair):
    return dense_apply(pair, None, None, SI)


def source_rows(own, other):
    adj_o, mask_o, q_o = own
    adj_n, mask_n, q_n, p_n, second_n = other
    step = DT * SI[1]
    delta_o = [step * mask_o[k] * adj_n[k] for k in range(2)]
    delta_n = [step * mask_n[k] * adj_o[k] for k in range(2)]
    lat_o, lat_n = lateral(delta_o), lateral(delta_n)
    near = [lat_o[k] - SI[1] * (q_n[k] + delta_n[k]) for k in range(2)]
    second = [-SI[1] * delta_o[k] for k in range(2)]
    halo = [p_n[k] + lat_n[k] - SI[1] * (q_o[k] + delta_o[k]) for k in range(2)]
    halo_second = second_n - SI[1] * delta_n[0]
    return near, second, halo, halo_second, delta_o[0]


def correct(electrodes, n_len, n_wall, own_rows, from_next, from_prev, coarse, surface, ids, *rest):
    rows_n, rows_p, message = rest[:3]
    lines, sums = rest[3:]
    _, C, L = ids.shape
    N = own_rows.shape[2]
    W = N - 2 * H
    wall, length = lax.axis_index("wall"), lax.axis_index("len")
    ok_m = inside(lax.broadcasted_iota(jnp.int32, (N, LANES), 0), wall, W, n_wall)
    ok_e = jnp.logical_and(ok_m, rim_lanes(lane_of((N, LANES)), length, n_len))
    coef, k0 = level_coef(0), level_step(0)
    y = surface[...]
    row = lax.broadcasted_iota(jnp.int32, (C, LANES), 0)
    at = pl.ds(jnp.where(wall == 0, H, W + H - 1), 1)
    lows, highs = [], []
    W1, C1 = W // 2, C // 2
    for side, (other, out, order) in enumerate(
        ((from_next, rows_n, (C - 1, C - 2, C - 3)), (from_prev, rows_p, (0, 1, 2)))
    ):
        own = [(own_rows[side, 2 * k], own_rows[side, 2 * k + 1]) for k in range(3)]
        near, second, halo, halo_second, delta = source_rows(own, unpacked(other, n_len, length, N))
        near = [jnp.where(ok_m, near[0], 0.0), jnp.where(ok_e, near[1], 0.0)]
        second = [jnp.where(ok_m, second[0], 0.0), jnp.where(ok_e, second[1], 0.0)]
        out[0] = halo_m = jnp.where(ok_m, halo[0], 0.0)
        out[1] = jnp.where(ok_e, halo[1], 0.0)
        out[2] = jnp.where(ok_m, halo_second, 0.0)
        out[3] = delta
        out[4], out[5] = near
        out[6], out[7] = second

        def turned(pair, beside):
            m, e = pair
            return (1.0 - OMEGA) * m + k0 * (
                coef[0] * beside_dense(m) + coef[2] * beside_lanes_main(m, e) + coef[1] * beside
            )

        first = turned(near, second[0] + halo_m)
        next_one = turned(second, near[0])
        third = k0 * coef[1] * second[0]
        for k, change in enumerate((near[0] + first, second[0] + next_one, third)):
            lines[0] = change
            y = y + jnp.where(row == order[k], k0 * lines[0, at, :], 0.0)
        for change in (first + next_one, third):
            lines[0] = change
            both = lines[0, pl.ds(H, W1, stride=2), :] + lines[0, pl.ds(H + 1, W1, stride=2), :]
            lows.append(both[: W1 // 2])
            highs.append(both[W1 // 2 :])
    add = halved(jnp.concatenate(lows, 0), jnp.concatenate(highs, 0))
    half = W * C // 8
    message[0:half, :] = coarse[...]
    for k, c1 in enumerate((C1 - 1, C1 - 2, 0, 1)):
        spot = pl.ds(c1, W1 // 2, stride=C1)
        message[spot, :] = message[spot, :] + add[k * (W1 // 2) : (k + 1) * (W1 // 2)]
    patch = ids[0]
    message[half : half + C, :] = patch.astype(F32)
    wide = sums.shape[0]
    if wide > electrodes:
        sums[...] = jnp.zeros(sums.shape, F32)

    def one(e):
        sums[pl.ds(e, 1), :] = jnp.sum(jnp.where(patch == e, y, 0.0), axis=0, keepdims=True)

    loop(0, electrodes, one, 8)
    totals = lax.dot_general(
        jnp.ones((8, LANES), F32), sums[...], (((1,), (1,)), ((), ())), precision=HIGHEST, preferred_element_type=F32
    )
    message[half + C : half + C + 8, :] = jnp.zeros((8, LANES), F32)
    for t in range(wide // LANES):
        message[half + C + t : half + C + t + 1, :] = totals[0:1, t * LANES : (t + 1) * LANES]


def source_part(n_blk, n_len, n_wall, C, electrodes, bm, be, rows_n, rows_p, qm, mask, owner, base_adj, base_pot, *rest):
    patches, fm, fe, tm, te, hp = rest
    N = bm.shape[0] // C
    W = N - 2 * H
    blk, length, wall = lax.axis_index("blk"), lax.axis_index("len"), lax.axis_index("wall")
    fm[...] = bm[...]
    fe[...] = be[...]
    for rows, near, second in ((rows_n, C - 1, C - 2), (rows_p, 0, 1)):
        for k, at in ((4, near), (6, second)):
            spot = pl.ds(at, N, stride=C)
            fm[spot, :] = fm[spot, :] + rows[k]
            fe[spot, :] = fe[spot, :] + rows[k + 1]
    coef, k0 = level_coef(0), level_step(0)
    rim = rim_lanes(lane_of((C, LANES)), length, n_len)

    def part(i):
        m, e = plane(fm, i, C), plane(fe, i, C)
        wm = plane(fm, i - 1, C) + plane(fm, i + 1, C)
        we = plane(fe, i - 1, C) + plane(fe, i + 1, C)
        lm, le = beside_lanes(m, e)
        at = pl.ds(i, 1)
        cm = beside_rows(m, rows_p[0, at, :], rows_n[0, at, :])
        ce = beside_rows(e, rows_p[1, at, :], rows_n[1, at, :])
        pm = k0 * ((2.0 - OMEGA) * m + k0 * (coef[0] * wm + coef[1] * cm + coef[2] * lm))
        pe = k0 * ((2.0 - OMEGA) * e + k0 * (coef[0] * we + coef[1] * ce + coef[2] * le))
        set_plane(tm, i, C, jnp.where(inside(i, wall, W, n_wall), pm, 0.0))
        set_plane(te, i, C, jnp.where(rim, pe, 0.0))

    loop(H - 1, N - H + 1, part, 2)
    for side, (rows, at) in enumerate(((rows_n, C - 1), (rows_p, 0))):
        m = rows[0]
        total = (
            coef[0] * beside_dense(m)
            + coef[1] * (rows[2] + dense(fm, at, N, C))
            + coef[2] * beside_lanes_main(m, rows[1])
        )
        hp[side] = k0 * ((2.0 - OMEGA) * m + k0 * total)
    row = lax.broadcasted_iota(jnp.int32, (C, LANES), 0)

    def finish(w):
        i = w + H
        m, e = plane(tm, i, C), plane(te, i, C)
        at = pl.ds(i, 1)
        wm = plane(tm, i - 1, C) + plane(tm, i + 1, C)
        cm = beside_rows(m, hp[1, at, :], hp[0, at, :])
        lm = beside_lanes_main(m, e)
        lam = plane(qm, i, C)
        lam = lam + jnp.where(row == C - 1, rows_n[3, at, :], 0.0) + jnp.where(row == 0, rows_p[3, at, :], 0.0)
        moved = 2.0 * sum(SI) * m - SI[0] * wm - SI[1] * cm - SI[2] * lm
        set_plane(base_adj, w, C, lam - DT * plane(mask, i, C) * moved)
        set_plane(base_pot, w, C, m)

    loop(0, W, finish, 2)

    me = (blk * n_len + length) * n_wall + wall
    which = lax.broadcasted_iota(jnp.int32, (1, electrodes), 1).astype(F32)
    mine = owner[...] == me
    patches[0:1, :] = jnp.full((1, LANES), jnp.min(jnp.where(mine, which, float(electrodes))))
    patches[1:2, :] = jnp.full((1, LANES), jnp.max(jnp.where(mine, which, -1.0)))
    patches[2:8, :] = jnp.zeros((6, LANES), F32)


def around(x, by):
    rows, lanes = x.shape
    lane = lane_of(x.shape)
    c = pltpu.roll(x, by, 0) + pltpu.roll(x, rows - by, 0)
    l = jnp.where(lane < by, 0.0, pltpu.roll(x, by, 1)) + jnp.where(
        lane >= lanes - by, 0.0, pltpu.roll(x, lanes - by, 1)
    )
    return c, l


def twins(x, by):
    rows, lanes = x.shape
    row = lax.broadcasted_iota(jnp.int32, x.shape, 0)
    lane = lane_of(x.shape)
    x = x + jnp.where((row & by) == 0, pltpu.roll(x, rows - by, 0), pltpu.roll(x, by, 0))
    return x + jnp.where((lane & by) == 0, pltpu.roll(x, lanes - by, 1), pltpu.roll(x, by, 1))


def solve(sizes, relative, quad, C, W, *refs):
    n_blk, n_len, n_wall = sizes
    count = 1 if quad else n_len * n_wall
    blocks, refs = refs[:count], refs[count:]
    if quad:
        blocks = [blocks[0].at[j * n_wall + v] for v in range(n_wall) for j in range(n_len)]
    base_adj, base_pot, mask, patches, adj_prev, potential, patch_grad = refs[:7]
    b1, x1, b2, x2, b3, x3, near, pm, pe, tm, te, adj_out, pot_out, sheet, sems = refs[7:]
    L = LANES
    W1, C1 = W // 2, C // 2
    planes, NC1, NL1 = b1.shape
    planes -= 2
    blk, length, wall = lax.axis_index("blk"), lax.axis_index("len"), lax.axis_index("wall")
    half = W1 // 2
    middle = LANES // 2
    lane8 = lane_of((C1, LANES))
    often = 8 if NC1 * NL1 <= 4096 else 1

    def blk_of(d):
        return lax.rem(blk - d + n_blk, n_blk) if relative else d

    def length_of(j):
        return (length + j) % n_len if n_len == 2 and not quad else j

    def wall_of(v):
        return v if quad else (wall + v) % n_wall

    zero1 = jnp.zeros((NC1, NL1), F32)
    for ref in (b1, x1, b2, x2, b3, x3):
        ref[0] = zero1
        ref[ref.shape[0] - 1] = zero1

    for v in range(n_wall):
        wall_s = wall_of(v)
        mine = blocks[v * n_len : (v + 1) * n_len]

        def unpack(d):
            at = pl.ds(pl.multiple_of(C1 * blk_of(d), C1), C1)
            for t in range(n_len // 2):
                one, two = mine[2 * t], mine[2 * t + 1]
                for i in range(half):
                    a, b = one[d, i * C1 : (i + 1) * C1, :], two[d, i * C1 : (i + 1) * C1, :]
                    if n_len == 2 and not quad:
                        a, b = jnp.where(length == 0, a, b), jnp.where(length == 0, b, a)
                    spot = 1 + wall_s * W1 + i
                    lanes = slice(t * LANES, (t + 1) * LANES)
                    b1[spot, at, lanes] = jnp.where(lane8 < middle, a, pltpu.roll(b, middle, 1))
                    b1[spot + half, at, lanes] = jnp.where(lane8 < middle, pltpu.roll(a, middle, 1), b)

        loop(0, n_blk, unpack, 4)

    def total_of(x, wsum, level, by):
        coef = level_coef(level)
        c, l = around(x, by)
        return level_step(level) * (coef[0] * wsum + coef[1] * c + coef[2] * l)

    def left(ref, i, level):
        b = ref[i]
        return (1.0 - OMEGA) * b + total_of(b, ref[i - 1] + ref[i + 1], level, 2 ** (level - 1))

    def sweep(x_ref, b_ref, i, level):
        x = x_ref[i]
        total = total_of(x, x_ref[i - 1] + x_ref[i + 1], level, 2 ** (level - 1))
        return (1.0 - OMEGA) * x + level_step(level) * b_ref[i] + total

    def down1(q):
        b2[1 + q] = 0.125 * twins(left(b1, 2 * q + 1, 1) + left(b1, 2 * q + 2, 1), 1)

    loop(0, planes // 2, down1, often)

    def down2(q):
        b3[1 + q] = 0.125 * twins(left(b2, 2 * q + 1, 2) + left(b2, 2 * q + 2, 2), 2)

    loop(0, planes // 4, down2, often)

    deep = planes // 4
    k3 = level_step(3)

    def start3(q):
        x3[1 + q] = k3 * b3[1 + q]

    loop(0, deep, start3, often)
    for k in range(SWEEPS):
        from_ref, to_ref = (x3, x2) if k % 2 == 0 else (x2, x3)

        if k == 1:
            x2[1 + deep] = zero1

        def sweep3(q):
            to_ref[1 + q] = sweep(from_ref, b3, 1 + q, 3)

        loop(0, deep, sweep3, often)
    deepest = x3 if SWEEPS % 2 == 0 else x2
    assert deepest is x3
    k2 = level_step(2)

    def up2(q):
        coarse = x3[1 + q]
        x2[1 + 2 * q] = k2 * b2[1 + 2 * q] + coarse
        x2[2 + 2 * q] = k2 * b2[2 + 2 * q] + coarse

    loop(0, planes // 4, up2, often)

    k1 = level_step(1)

    def up1(q):
        fine = sweep(x2, b2, 1 + q, 2)
        x1[1 + 2 * q] = k1 * b1[1 + 2 * q] + fine
        x1[2 + 2 * q] = k1 * b1[2 + 2 * q] + fine

    loop(0, planes // 2, up1, often)

    Q = W1 + 2
    sectors = (blk, lax.rem(blk + 1, n_blk), lax.rem(blk + n_blk - 1, n_blk))
    spots3 = [pl.ds(pl.multiple_of(s * C1, C1), C1) for s in sectors]
    row8 = lax.broadcasted_iota(jnp.int32, (C1, NL1), 0)

    def three(ref, i):
        return jnp.concatenate([ref[i, s, :] for s in spots3], 0)

    def finish1(q):
        i = wall * W1 + q
        x = three(x1, i)
        wsum = three(x1, jnp.maximum(i - 1, 0)) + three(x1, jnp.minimum(i + 1, planes + 1))
        value = (1.0 - OMEGA) * x + k1 * three(b1, i) + total_of(x, wsum, 1, 1)
        value = jnp.where(jnp.logical_and(i >= 1, i <= planes), value, 0.0)
        set_plane(near, 2 * q, C1, value[:C1])
        set_plane(near, 2 * q + 1, C1, jnp.where(row8 < 2, value[C1 : 2 * C1], value[2 * C1 :]))

    loop(0, Q, finish1, min(often, 6))

    first = length * middle
    R = C + 8
    row8 = lax.broadcasted_iota(jnp.int32, (8, LANES), 0)
    tile_lane = lane_of((8, LANES))
    at_e = jnp.where(tile_lane < H, middle + tile_lane // 2, tile_lane // 2 - middle)
    rim8 = rim_lanes(tile_lane, length, n_len)
    if NL1 == LANES:
        index_m, index_e = first + tile_lane // 2, jnp.clip(first + at_e, 0, LANES - 1)

        def spread(tile):
            return lanes_at(tile, index_m), jnp.where(rim8, lanes_at(tile, index_e), 0.0)

    else:
        source = lax.broadcasted_iota(jnp.int32, (NL1, LANES), 0)
        lane = lane_of((NL1, LANES))
        at_all = jnp.where(lane < H, middle + lane // 2, jnp.where(lane >= LANES - H, lane // 2 - middle, 4 * NL1))
        take_m = jnp.where(source == first + lane // 2, 1.0, 0.0).astype(F32)
        take_e = jnp.where(source == first + at_all, 1.0, 0.0).astype(F32)

        def spread(tile):
            return precise(tile, take_m), precise(tile, take_e)

    picks = (row8 // 2, H + row8 // 2, jnp.where(row8 < H, row8 // 2, H + row8 // 2))

    def fine_rows(q):
        own = spread(plane(near, 2 * q, C1))
        beside = spread(plane(near, 2 * q + 1, C1))
        for out, a, b in ((pm, own[0], beside[0]), (pe, own[1], beside[1])):
            parts = (rows_at(a, picks[0]), rows_at(a, picks[1]), rows_at(b, picks[2]))
            set_plane(out, q, R, jnp.concatenate(parts, 0))

    loop(0, Q, fine_rows, min(often, 6))
    coef, k0 = level_coef(0), level_step(0)
    rim = rim_lanes(lane_of((C, LANES)), length, n_len)

    def rows_beside(x):
        return pltpu.roll(x, 1, 0) + pltpu.roll(x, x.shape[0] - 1, 0)

    def coarse_terms(q):
        m, e = plane(pm, q, R), plane(pe, q, R)
        lm, le = beside_lanes(m, e)
        gm = (1.0 - OMEGA) * m + k0 * (coef[0] * m + coef[1] * rows_beside(m) + coef[2] * lm)
        ge = (1.0 - OMEGA) * e + k0 * (coef[0] * e + coef[1] * rows_beside(e) + coef[2] * le)
        return gm, ge[:C]

    ks = k0 * coef[0]

    def put_end(t, q, other, ok):
        set_plane(tm, t, R, jnp.where(ok, coarse_terms(q)[0] + ks * plane(pm, other, R), 0.0))

    put_end(0, 0, 1, wall > 0)
    put_end(W + 1, Q - 1, Q - 2, wall < n_wall - 1)

    def level0(q):
        gm, ge = coarse_terms(q)
        for t, other in ((2 * q - 1, q - 1), (2 * q, q + 1)):
            m = gm + ks * plane(pm, other, R)
            set_plane(tm, t, R, m)
            set_plane(te, t - 1, C, jnp.where(rim, ge + ks * plane(pe, other, R)[:C], 0.0))
            set_plane(pot_out, t - 1, C, plane(base_pot, t - 1, C) + m[:C])

    def finish0(w):
        m, e = plane(tm, w + 1, R), plane(te, w, C)
        cm = rows_beside(m)[:C]
        m = m[:C]
        wm = plane(tm, w, R)[:C] + plane(tm, w + 2, R)[:C]
        lm = beside_lanes_main(m, e)
        moved = 2.0 * sum(SI) * m - SI[0] * wm - SI[1] * cm - SI[2] * lm
        set_plane(adj_out, w, C, plane(base_adj, w, C) - DT * plane(mask, w + H, C) * moved)

    parts = 2
    size = W // parts
    copies = []

    def send(src, dst, k, sem):
        spot = pl.ds(k * size * C, size * C)
        copies.append(pltpu.make_async_copy(src.at[spot], dst.at[spot], sem))
        copies[-1].start()

    for k in range(parts):
        loop(1 + k * W1 // parts, 1 + (k + 1) * W1 // parts, level0, 4)
        send(pot_out, potential, k, sems.at[0, k])
    for k in range(parts):
        loop(k * size, (k + 1) * size, finish0, 4)
        send(adj_out, adj_prev, k, sems.at[1, k])

    NC, NL = sheet.shape[1:]

    def whole_fine(x):
        if NL1 == LANES:
            parts = []
            for t in range(0, NC1, 8):
                wide8 = [lanes_at(x[t : t + 8], tile_lane // 2 + k * middle) for k in range(2)]
                for pick in picks[:2]:
                    parts.append(jnp.concatenate([rows_at(v, pick) for v in wide8], 1))
            return jnp.concatenate(parts, 0)
        along_c = lax.broadcasted_iota(jnp.int32, (NC, NC1), 0) // 2
        along_l = lax.broadcasted_iota(jnp.int32, (NL1, NL), 1) // 2
        twice_c = jnp.where(along_c == lax.broadcasted_iota(jnp.int32, (NC, NC1), 1), 1.0, 0.0).astype(F32)
        twice_l = jnp.where(along_l == lax.broadcasted_iota(jnp.int32, (NL1, NL), 0), 1.0, 0.0).astype(F32)
        return precise(precise(twice_c, x), twice_l)

    for s, i in enumerate((1, planes)):
        p = whole_fine(sweep(x1, b1, i, 1))
        c, l = around(p, 1)
        sheet[s] = (1.0 - OMEGA) * p + k0 * (coef[0] * p + coef[1] * c + coef[2] * l)

    owned = [patches[r : r + 1, :] for r in range(2)]
    spot = lax.broadcasted_iota(jnp.int32, (8, LANES), 0) * LANES + lane_of((8, LANES))
    spot = spot.astype(F32)
    start = half * C1
    totals = [jnp.zeros((C, LANES), F32) for _ in owned]
    small = [jnp.zeros((8, LANES), F32) for _ in owned]
    for v in range(n_wall):
        wall_s = wall_of(v)
        for j in range(n_len):
            ref = blocks[v * n_len + j]
            at_l = pl.ds(pl.multiple_of(length_of(j) * L, L), L)

            def add(d, carry):
                big, little = carry
                values = sheet[wall_s, pl.ds(pl.multiple_of(blk_of(d) * C, C), C), at_l]
                ids = ref[d, start : start + C, :]
                parts = ref[d, start + C : start + C + 8, :]
                big = [x + jnp.where(ids == e, values, 0.0) for x, e in zip(big, owned)]
                little = [x + jnp.where(spot == e, parts, 0.0) for x, e in zip(little, owned)]
                return big, little

            totals, small = lax.fori_loop(0, n_blk, add, (totals, small), unroll=min(4, n_blk))
    factor = 1.0 / (2.0 * C * L / 2) ** 0.5
    for r in range(2):
        patch_grad[0, r] = (jnp.sum(totals[r]) + jnp.sum(small[r])) * factor
    for copy in copies:
        copy.wait()


def ring(x, axis, by):
    count = lax.axis_size(axis)
    return lax.ppermute(x, axis, [(i, (i + by) % count) for i in range(count)])


def across(x):
    n_wall = lax.axis_size("wall")
    pairs = [(l * n_wall + w, (1 - l) * n_wall + (w + 1) % n_wall) for l in range(2) for w in range(n_wall)]
    return lax.ppermute(x, ("len", "wall"), pairs)


def call(kernel, ins, outs, scratch, name, work=0, room=48):
    places = {"vmem": pltpu.VMEM, "smem": pltpu.SMEM, "any": pl.ANY, "hbm": pltpu.HBM}

    def specs(kinds):
        return [pl.BlockSpec(memory_space=places[kind]) for kind in kinds]

    cost = pl.CostEstimate(flops=work, bytes_accessed=work, transcendentals=0) if work else None
    return pl.pallas_call(
        kernel,
        out_shape=[jax.ShapeDtypeStruct(shape, F32) for shape, _ in outs],
        in_specs=specs(ins),
        out_specs=specs(kind for _, kind in outs),
        scratch_shapes=[pltpu.VMEM(shape, F32) if isinstance(shape, tuple) else shape for shape in scratch],
        compiler_params=pltpu.CompilerParams(vmem_limit_bytes=int(room * 2**20)),
        cost_estimate=cost,
        name=name,
    )


def body(adj_next, ion_slope, misfit, tissue_mask, patch_ids, owner_map):
    W, C, L = adj_next.shape
    n_blk, n_len, n_wall = lax.axis_size("blk"), lax.axis_size("len"), lax.axis_size("wall")
    electrodes = owner_map.shape[0]
    assert L == LANES and H * W == LANES and n_wall == 2 and electrodes == 2 * n_blk * n_len * n_wall
    N = W + 2 * H
    n_dir = 1 if n_len == 2 else 2
    cells = W * C
    vmem = "vmem"
    field, own = (N * C, L), (cells, L)
    raw = [x.reshape(cells, L) for x in (adj_next, ion_slope, tissue_mask, misfit)]

    *fields, wall_out = (faces := call(
        functools.partial(pack_faces, n_len),
        ["hbm"] * 4,
        [(own, vmem)] * 4
        + [((sum(FACES), C, L), vmem)]
        + [((4, C, L), vmem)] * n_dir
        + [((C, L), vmem)] * n_dir,
        [pltpu.VMEM(own, jnp.int32), pltpu.SemaphoreType.DMA((4, 2))],
        "faces",
        room=52.75,
    )(*raw))[:5]
    strip_out, corner_out = faces[5 : 5 + n_dir], faces[5 + n_dir :]
    wall_in = ring(wall_out, "wall", 1)
    if n_dir == 1:
        strips = [ring(strip_out[0], "len", 1)]
        corners = [across(corner_out[0])]
    else:
        strips = [ring(strip_out[1], "len", -1), ring(strip_out[0], "len", 1)]
        corners = [ring(ring(corner_out[1], "wall", 1), "len", -1), ring(ring(corner_out[0], "wall", 1), "len", 1)]

    near = (sum(near_rows(n_dir, W)[-1][::2]), L)
    *fields, to_next, to_prev, own_rows = call(
        functools.partial(boundary, n_len, C),
        [vmem] * (5 + 2 * n_dir),
        [(field, vmem)] * 8 + [(near, vmem)] * 2 + [((2, 6, N, L), vmem)],
        [],
        "boundary",
    )(*fields, wall_in, *strips, *corners)
    from_next = ring(to_prev, "blk", -1)
    from_prev = ring(to_next, "blk", 1)
    qm, bm, be, coarse, surface = call(
        functools.partial(sector, n_len, n_wall, C),
        [vmem] * 8,
        [(field, vmem)] * 3 + [((cells // 8, L), vmem), ((C, L), vmem)],
        [field, (cells // 2, L)],
        "sector",
        work=16 * 10**6,
    )(*fields)

    rows = (8, N, L)
    wide = LANES * ((electrodes + LANES - 1) // LANES)
    message = (cells // 8 + C + 8, L)
    rows_n, rows_p, mine = call(
        functools.partial(correct, electrodes, n_len, n_wall),
        [vmem] * 6,
        [(rows, vmem), (rows, vmem), (message, vmem)],
        [(1, N, L), (wide, L)],
        "correct",
    )(own_rows, from_next, from_prev, coarse, surface, patch_ids)

    relative = n_blk <= 4
    moved = [ring(mine, "blk", d) for d in range(1, n_blk)] if relative else [lax.all_gather(mine, "blk")]
    base_adj, base_pot, patches = call(
        functools.partial(source_part, n_blk, n_len, n_wall, C, electrodes),
        [vmem] * 7,
        [(own, vmem), (own, vmem), ((8, L), vmem)],
        [field] * 4 + [(2, N, L)],
        "source_part",
        work=12 * 10**6,
    )(bm, be, rows_n, rows_p, qm, fields[2], owner_map.reshape(1, electrodes))
    moved, base_adj = lax.optimization_barrier((moved, base_adj))
    sector_blocks = jnp.stack([mine] + moved) if relative else moved[0]
    quad = True
    blocks = [lax.all_gather(sector_blocks, ("len", "wall"))]

    NC1, NL1 = n_blk * C // 2, n_len * L // 2
    planes = n_wall * W // 2
    grids = [(planes // k + 2, NC1, NL1) for k in (1, 1, 2, 2, 4, 4)]
    Q = W // 2 + 2
    tall = (Q * (C + 8), L)
    taller = ((W + 2) * (C + 8), L)
    scratch = grids + [(Q * C, NL1), tall, tall, taller, own, own, own]
    scratch += [(2, n_blk * C, n_len * L), pltpu.SemaphoreType.DMA((2, 2))]
    adj_prev, potential, patch_grad = call(
        functools.partial(solve, (n_blk, n_len, n_wall), relative, quad, C, W),
        [vmem] * (len(blocks) + 4),
        [(own, "any"), (own, "any"), ((1, 2), "smem")],
        scratch,
        "solve",
        room=48 if NC1 * NL1 <= 4096 else 58,
    )(*blocks, base_adj, base_pot, fields[2], patches)
    return adj_prev.reshape(W, C, L), potential.reshape(W, C, L), patch_grad


def solution(mesh):
    field = P(("groups", "wall"), "blk", "len")
    return jax.shard_map(
        body,
        mesh=mesh,
        in_specs=(field, field, field, field, field, P("groups")),
        out_specs=(field, field, P(("groups", "blk", "len", "wall"), None)),
        check_vma=False,
    )
```

```python
import functools

import jax
import jax.numpy as jnp
from jax import lax
from jax.experimental import pallas as pl
from jax.experimental.pallas import tpu as pltpu
from jax.sharding import PartitionSpec as P

SI = (0.6, 1.0, 3.0)
SE = (0.8, 1.2, 2.0)
SHIFT = 0.002
OMEGA = 0.8
DT = 0.1
H = 4
LANES = 128
HIGHEST = lax.Precision.HIGHEST
F32 = jnp.float32


def level_coef(level):
    return tuple((SI[i] + SE[i]) / 4.0**level for i in range(3))


def level_diag(level):
    return SHIFT + 2.0 * sum(level_coef(level))


def level_step(level):
    return OMEGA / level_diag(level)


def lane_of(shape):
    return lax.broadcasted_iota(jnp.int32, shape, len(shape) - 1)


def before(m, e):
    first = lane_of(m.shape) == 0
    rm, re = pltpu.roll(m, 1, 1), pltpu.roll(e, 1, 1)
    return jnp.where(first, re, rm), jnp.where(first, rm, re)


def after(m, e):
    last = lane_of(m.shape) == LANES - 1
    rm, re = pltpu.roll(m, LANES - 1, 1), pltpu.roll(e, LANES - 1, 1)
    return jnp.where(last, re, rm), jnp.where(last, rm, re)


def beside_lanes(m, e):
    bm, be = before(m, e)
    am, ae = after(m, e)
    return bm + am, be + ae


def beside_lanes_main(m, e):
    lane = lane_of(m.shape)
    ends = lanes_at(e, LANES - 1 - lane)
    left = jnp.where(lane == 0, ends, pltpu.roll(m, 1, 1))
    right = jnp.where(lane == LANES - 1, ends, pltpu.roll(m, LANES - 1, 1))
    return left + right


def beside_rows(x, row_before, row_after):
    rows = x.shape[0]
    row = lax.broadcasted_iota(jnp.int32, x.shape, 0)
    low = jnp.where(row == 0, row_before, pltpu.roll(x, 1, 0))
    high = jnp.where(row == rows - 1, row_after, pltpu.roll(x, rows - 1, 0))
    return low + high


def beside_dense(x):
    return pltpu.roll(x, 1, 0) + pltpu.roll(x, x.shape[0] - 1, 0)


def plane(ref, i, rows):
    return ref[pl.ds(pl.multiple_of(i * rows, rows), rows), :]


def set_plane(ref, i, rows, value):
    ref[pl.ds(pl.multiple_of(i * rows, rows), rows), :] = value


def loop(low, high, step, unroll):
    def wrapped(i, carry):
        step(i)
        return carry

    lax.fori_loop(low, high, wrapped, 0, unroll=min(unroll, high - low))


FACES = (H, H - 1, H - 1, H - 2)


def face_planes(array):
    return FACES[array], sum(FACES[:array])


def pack_faces(n_len, adj, ion, mask, mis, *rest):
    n_dir = 1 if n_len == 2 else 2
    fields, wall_out, rest = rest[:4], rest[4], rest[5:]
    strips, corners = rest[:n_dir], rest[n_dir : 2 * n_dir]
    whole_mask, sems = rest[2 * n_dir :]
    cells = adj.shape[0]
    C = wall_out.shape[1]
    W = cells // C
    wall, length = lax.axis_index("wall"), lax.axis_index("len")
    targets = (fields[0], fields[1], whole_mask, fields[3])
    copies = []
    for a, (src, dst) in enumerate(zip((adj, ion, mask, mis), targets)):
        part = cells // 2
        for k in range(2):
            spot = pl.ds(k * part, part)
            copies.append(pltpu.make_async_copy(src.at[spot], dst.at[spot], sems.at[a, k]))
            copies[-1].start()

    base = jnp.where(wall == 0, W - H, 0)
    group = lane_of((C, LANES)) // H
    turns = [jnp.where(length == 0, H, 0)] if n_dir == 1 else [H, 0]
    corner = [jnp.zeros((C, LANES), F32) for _ in range(n_dir)]
    for a in (0, 1, 3, 2):
        copies[2 * a].wait()
        copies[2 * a + 1].wait()
        if a == 2:
            fields[2][...] = whole_mask[...].astype(F32)
        ref = fields[a]
        strip = [jnp.zeros((C, LANES), F32) for _ in range(n_dir)]
        for w in range(W):
            value = ref[w * C : (w + 1) * C, :]
            for d in range(n_dir):
                turned = pltpu.roll(value, lax.rem(H * w + turns[d], LANES), 1)
                strip[d] = jnp.where(group == w, turned, strip[d])
        for d in range(n_dir):
            strips[d][a] = strip[d]
        count, first = face_planes(a)
        for p in range(count):
            face = plane(ref, base + jnp.where(wall == 0, H - count, 0) + p, C)
            wall_out[first + p] = face
            slot = first + p
            for d in range(n_dir):
                turned = pltpu.roll(face, lax.rem(H * slot + turns[d], LANES), 1)
                corner[d] = jnp.where(group == slot, turned, corner[d])
    for d in range(n_dir):
        corners[d][...] = corner[d]


def dense(ref, row, N, C):
    return ref[pl.ds(row, N, stride=C), :]


def dense_pair(m, e, row, N, C):
    return dense(m, row, N, C), dense(e, row, N, C)


def dense_apply(pair, inner, outer, coef):
    m, e = pair
    lm, le = beside_lanes(m, e)
    double = 2.0 * sum(coef)
    out = [double * m - coef[0] * beside_dense(m) - coef[2] * lm, double * e - coef[0] * beside_dense(e) - coef[2] * le]
    for row in (inner, outer):
        if row is not None:
            out = [out[k] - coef[1] * row[k] for k in range(2)]
    return out


def near_rows(n_dir, W):
    start, places = 8 * n_dir, []
    for reach in (0, 1, 2, 2, 3):
        places.append((start, H - reach, W + 2 * reach))
        start += W + 2 * reach
    assert start % 8 == 0
    return places


def rim_tiles(values):
    return [value[s : s + 8] for value in values for s in range(0, value.shape[0], 8)]


def rim_places(n_len, length):
    if n_len == 2:
        return [(jnp.where(length == 0, 0, LANES - H), True)]
    return [(0, length < n_len - 1), (LANES - H, length > 0)]


def boundary(n_len, C, *refs):
    n_dir = 1 if n_len == 2 else 2
    raw, wall_in, refs = refs[:4], refs[4], refs[5:]
    strips, corners, refs = refs[:n_dir], refs[n_dir : 2 * n_dir], refs[2 * n_dir :]
    to_next, to_prev, own_rows, build = refs
    W = raw[0].shape[0] // C
    N = W + 2 * H
    wall, length = lax.axis_index("wall"), lax.axis_index("len")
    places = rim_places(n_len, length)

    def strip_rows(packed, first, count):
        lane, k = lane_of((count, LANES)), lax.broadcasted_iota(jnp.int32, (count, LANES), 0)
        out = jnp.zeros((count, LANES), F32)
        for row, (off, ok) in zip(packed, places):
            j = lax.rem(lane - off + LANES, LANES)
            index = jnp.clip(H * (first + k) + j, 0, LANES - 1)
            taken = lanes_at(jnp.broadcast_to(row, (count, LANES)), index)
            out = jnp.where(jnp.logical_and(j < H, ok), taken, out)
        return out

    slots = iter(range(build.shape[0]))

    def assembled(own, halo, count):
        ref = build.at[next(slots)]
        ref[0:8, :] = jnp.zeros((8, LANES), F32)
        ref[N - 8 : N, :] = jnp.zeros((8, LANES), F32)
        ref[H : H + W, :] = own
        ref[H - count : H, :] = jnp.where(wall == 0, 0.0, halo)
        ref[H + W : H + W + count, :] = jnp.where(wall == 0, halo, 0.0)
        return ref[...]

    def row_of(a, r):
        count, first = face_planes(a)
        halo = jnp.concatenate([wall_in[first + p, r : r + 1, :] for p in range(count)], 0)
        m = assembled(raw[a][pl.ds(r, W, stride=C), :], halo, count)
        own = strip_rows([strip[a, r : r + 1, :] for strip in strips], 0, W)
        halo = strip_rows([corner[r : r + 1, :] for corner in corners], first, 8)[:count]
        return m, assembled(own, halo, count)

    length_shift = jnp.where(length == 0, 0, H) if n_dir == 1 else H
    group = lane_of((8, LANES)) // (H * n_dir)
    for side, (out, order) in enumerate(((to_next, (C - 1, C - 2, C - 3, C - 4)), (to_prev, (0, 1, 2, 3)))):
        adj = [row_of(0, r) for r in order]
        mask = [row_of(2, r) for r in order[:3]]
        q = []
        for k in range(3):
            ion = row_of(1, order[k])
            moved = dense_apply(adj[k], adj[k + 1], adj[k - 1] if k else None, SI)
            q.append([adj[k][j] - DT * mask[k][j] * (moved[j] + ion[j] * adj[k][j]) for j in range(2)])
        near = dense_apply(q[0], q[1], None, SI)
        mis = row_of(3, order[0])
        near = [near[j] + mis[j] for j in range(2)]
        second = dense_apply(q[1], q[2], q[0], SI)[0] + row_of(3, order[1])[0]
        for value, (start, first, count) in zip((second, near[0], q[0][0], mask[0][0], adj[0][0]), near_rows(n_dir, W)):
            out[start : start + count, :] = value[first : first + count]
        packs = [jnp.zeros((8, LANES), F32) for _ in range(n_dir)]
        for t, tile in enumerate(rim_tiles((near[1], q[0][1], mask[0][1], adj[0][1]))):
            k, at = divmod(t, LANES // (H * n_dir))
            turned = pltpu.roll(tile, lax.rem(length_shift + H * n_dir * at, LANES), 1)
            packs[k] = jnp.where(group == at, turned, packs[k])
        for k in range(n_dir):
            out[8 * k : 8 * k + 8, :] = packs[k]
        for k, pair in enumerate((adj[0], mask[0], q[0])):
            own_rows[side, 2 * k] = pair[0]
            own_rows[side, 2 * k + 1] = pair[1]


def spots(m_ref, e_ref, i, rows, coef):
    m, e = plane(m_ref, i, rows), plane(e_ref, i, rows)
    wm = plane(m_ref, i - 1, rows) + plane(m_ref, i + 1, rows)
    we = plane(e_ref, i - 1, rows) + plane(e_ref, i + 1, rows)
    lm, le = beside_lanes(m, e)
    cm, ce = beside_rows(m, 0.0, 0.0), beside_rows(e, 0.0, 0.0)
    double = 2.0 * sum(coef)
    dm = double * m - coef[0] * wm - coef[1] * cm - coef[2] * lm
    de = double * e - coef[0] * we - coef[1] * ce - coef[2] * le
    return m, e, dm, de


def rim_lanes(lane, length, n_len):
    return jnp.logical_or(
        jnp.logical_and(lane < H, length < n_len - 1),
        jnp.logical_and(lane >= LANES - H, length > 0),
    )


def inside(i, wall, W, n_wall):
    w = wall * W + i - H
    return jnp.logical_and(w >= 0, w < n_wall * W)


def lanes_at(x, index):
    return jnp.take_along_axis(x, index, axis=1, mode="promise_in_bounds")


def rows_at(x, index):
    return jnp.take_along_axis(x, index, axis=0, mode="promise_in_bounds")


def halved(low, high):
    lane = lane_of(low.shape)
    even = 2 * lane % LANES
    pairs = [lanes_at(x, even) + lanes_at(x, even + 1) for x in (low, high)]
    return 0.125 * jnp.where(lane < LANES // 2, pairs[0], pairs[1])


def precise(a, b):
    return jnp.dot(a, b, precision=HIGHEST, preferred_element_type=F32)


def assemble(n_len, C, raw, wall_in, strips, corners, xm, xe):
    W = raw[0].shape[0] // C
    N = W + 2 * H
    wall, length = lax.axis_index("wall"), lax.axis_index("len")
    lane = lane_of((C, LANES))
    places = rim_places(n_len, length)
    seen = [jnp.logical_and(lax.rem(lane - off + LANES, LANES) < H, ok) for off, ok in places]

    def rim(packed, base):
        out = jnp.zeros((C, LANES), F32)
        for row, ok, (off, _) in zip(packed, seen, places):
            out = jnp.where(ok, pltpu.roll(row, lax.rem(off - base + LANES, LANES), 1), out)
        return out

    zero = jnp.zeros((C, LANES), F32)
    last = N - H
    for a, own in enumerate(raw):
        packed = [strip[a] for strip in strips]
        for w in range(W):
            set_plane(xm[a], w + H, C, plane(own, w, C))
            set_plane(xe[a], w + H, C, rim(packed, H * w))
        packed = [corner[...] for corner in corners]
        for i in range(H):
            for at in (i, last + i):
                set_plane(xm[a], at, C, zero)
                set_plane(xe[a], at, C, zero)
        count, first = face_planes(a)
        here = jnp.where(wall == 0, last, H - count)
        for p in range(count):
            set_plane(xm[a], here + p, C, wall_in[first + p])
            set_plane(xe[a], here + p, C, rim(packed, H * (first + p)))


def sector(n_len, n_wall, C, *refs):
    n_dir = 1 if n_len == 2 else 2
    raw, wall_in, refs = refs[:4], refs[4], refs[5:]
    strips, corners, refs = refs[:n_dir], refs[n_dir : 2 * n_dir], refs[2 * n_dir :]
    qm, bm, be, coarse, surface, qe, pairs = refs[:7]
    xm, xe = refs[7:11], refs[11:15]
    assemble(n_len, C, raw, wall_in, strips, corners, xm, xe)
    N = qm.shape[0] // C
    W = N - 2 * H
    wall, length = lax.axis_index("wall"), lax.axis_index("len")
    rim = rim_lanes(lane_of((C, LANES)), length, n_len)
    zero = jnp.zeros((C, LANES), F32)
    for i in (0, N - 1):
        set_plane(qm, i, C, zero)
        set_plane(qe, i, C, zero)
    for i in (0, 1, N - 2, N - 1):
        set_plane(bm, i, C, zero)
        set_plane(be, i, C, zero)

    def parabolic(i):
        m, e, dm, de = spots(xm[0], xe[0], i, C, SI)
        set_plane(qm, i, C, m - DT * plane(xm[2], i, C) * (dm + plane(xm[1], i, C) * m))
        set_plane(qe, i, C, e - DT * plane(xe[2], i, C) * (de + plane(xe[1], i, C) * e))

    loop(1, N - 1, parabolic, 2)

    def elliptic_source(i):
        m, e, dm, de = spots(qm, qe, i, C, SI)
        ok = inside(i, wall, W, n_wall)
        set_plane(bm, i, C, jnp.where(ok, plane(xm[3], i, C) + dm, 0.0))
        set_plane(be, i, C, jnp.where(jnp.logical_and(rim, ok), plane(xe[3], i, C) + de, 0.0))

    loop(2, N - 2, elliptic_source, 2)

    coef, k0 = level_coef(0), level_step(0)

    def left(i):
        m, e = plane(bm, i, C), plane(be, i, C)
        wm = plane(bm, i - 1, C) + plane(bm, i + 1, C)
        cm = beside_rows(m, 0.0, 0.0)
        lm = beside_lanes_main(m, e)
        return m, (1.0 - OMEGA) * m + k0 * (coef[0] * wm + coef[1] * cm + coef[2] * lm)

    def pair(q):
        i = 2 * q + H
        m, first = left(i)
        n, second = left(i + 1)
        set_plane(pairs, q, C, first + second)

        @pl.when(jnp.logical_and(q == 0, wall == 0))
        def _():
            surface[...] = k0 * (m + first)

        @pl.when(jnp.logical_and(q == W // 2 - 1, wall == n_wall - 1))
        def _():
            surface[...] = k0 * (n + second)

    loop(0, W // 2, pair, 2)

    half = W * C // 8
    z = pairs[pl.ds(0, 2 * half, stride=2), :] + pairs[pl.ds(1, 2 * half, stride=2), :]
    coarse[...] = halved(z[:half], z[half:])


def unpacked(ref, n_len, length, N):
    n_dir = 1 if n_len == 2 else 2
    mains = []
    for start, first, count in near_rows(n_dir, N - 2 * H):
        begin = min(start - first, ref.shape[0] - N)
        value = ref[begin : begin + N, :]
        behind = start - first - begin
        mains.append(pltpu.roll(value, N - behind, 0) if behind else value)
    rim = rim_lanes(lane_of((8, LANES)), length, n_len)
    shift = jnp.where(length == 0, 0, H) if n_dir == 1 else H
    rims = []
    for k in range(4):
        parts = []
        for s in range(N // 8):
            pack, at = divmod(k * (N // 8) + s, LANES // (H * n_dir))
            back = lax.rem(2 * LANES - shift - H * n_dir * at, LANES)
            parts.append(jnp.where(rim, pltpu.roll(ref[8 * pack : 8 * pack + 8, :], back, 1), 0.0))
        rims.append(jnp.concatenate(parts, 0))
    second, near, q, mask, adj = mains
    return (adj, rims[3]), (mask, rims[2]), (q, rims[1]), (near, rims[0]), second


def lateral(pair):
    return dense_apply(pair, None, None, SI)


def source_rows(own, other):
    adj_o, mask_o, q_o = own
    adj_n, mask_n, q_n, p_n, second_n = other
    step = DT * SI[1]
    delta_o = [step * mask_o[k] * adj_n[k] for k in range(2)]
    delta_n = [step * mask_n[k] * adj_o[k] for k in range(2)]
    lat_o, lat_n = lateral(delta_o), lateral(delta_n)
    near = [lat_o[k] - SI[1] * (q_n[k] + delta_n[k]) for k in range(2)]
    second = [-SI[1] * delta_o[k] for k in range(2)]
    halo = [p_n[k] + lat_n[k] - SI[1] * (q_o[k] + delta_o[k]) for k in range(2)]
    halo_second = second_n - SI[1] * delta_n[0]
    return near, second, halo, halo_second, delta_o[0]


def correct(electrodes, n_len, n_wall, own_rows, from_next, from_prev, coarse, surface, ids, *rest):
    rows_n, rows_p, message = rest[:3]
    lines, sums = rest[3:]
    _, C, L = ids.shape
    N = own_rows.shape[2]
    W = N - 2 * H
    wall, length = lax.axis_index("wall"), lax.axis_index("len")
    ok_m = inside(lax.broadcasted_iota(jnp.int32, (N, LANES), 0), wall, W, n_wall)
    ok_e = jnp.logical_and(ok_m, rim_lanes(lane_of((N, LANES)), length, n_len))
    coef, k0 = level_coef(0), level_step(0)
    y = surface[...]
    row = lax.broadcasted_iota(jnp.int32, (C, LANES), 0)
    at = pl.ds(jnp.where(wall == 0, H, W + H - 1), 1)
    lows, highs = [], []
    W1, C1 = W // 2, C // 2
    for side, (other, out, order) in enumerate(
        ((from_next, rows_n, (C - 1, C - 2, C - 3)), (from_prev, rows_p, (0, 1, 2)))
    ):
        own = [(own_rows[side, 2 * k], own_rows[side, 2 * k + 1]) for k in range(3)]
        near, second, halo, halo_second, delta = source_rows(own, unpacked(other, n_len, length, N))
        near = [jnp.where(ok_m, near[0], 0.0), jnp.where(ok_e, near[1], 0.0)]
        second = [jnp.where(ok_m, second[0], 0.0), jnp.where(ok_e, second[1], 0.0)]
        out[0] = halo_m = jnp.where(ok_m, halo[0], 0.0)
        out[1] = jnp.where(ok_e, halo[1], 0.0)
        out[2] = jnp.where(ok_m, halo_second, 0.0)
        out[3] = delta
        out[4], out[5] = near
        out[6], out[7] = second

        def turned(pair, beside):
            m, e = pair
            return (1.0 - OMEGA) * m + k0 * (
                coef[0] * beside_dense(m) + coef[2] * beside_lanes_main(m, e) + coef[1] * beside
            )

        first = turned(near, second[0] + halo_m)
        next_one = turned(second, near[0])
        third = k0 * coef[1] * second[0]
        for k, change in enumerate((near[0] + first, second[0] + next_one, third)):
            lines[0] = change
            y = y + jnp.where(row == order[k], k0 * lines[0, at, :], 0.0)
        for change in (first + next_one, third):
            lines[0] = change
            both = lines[0, pl.ds(H, W1, stride=2), :] + lines[0, pl.ds(H + 1, W1, stride=2), :]
            lows.append(both[: W1 // 2])
            highs.append(both[W1 // 2 :])
    add = halved(jnp.concatenate(lows, 0), jnp.concatenate(highs, 0))
    half = W * C // 8
    message[0:half, :] = coarse[...]
    for k, c1 in enumerate((C1 - 1, C1 - 2, 0, 1)):
        spot = pl.ds(c1, W1 // 2, stride=C1)
        message[spot, :] = message[spot, :] + add[k * (W1 // 2) : (k + 1) * (W1 // 2)]
    patch = ids[0]
    message[half : half + C, :] = patch.astype(F32)
    wide = sums.shape[0]
    if wide > electrodes:
        sums[...] = jnp.zeros(sums.shape, F32)

    def one(e):
        sums[pl.ds(e, 1), :] = jnp.sum(jnp.where(patch == e, y, 0.0), axis=0, keepdims=True)

    loop(0, electrodes, one, 8)
    totals = lax.dot_general(
        jnp.ones((8, LANES), F32), sums[...], (((1,), (1,)), ((), ())), precision=HIGHEST, preferred_element_type=F32
    )
    message[half + C : half + C + 8, :] = jnp.zeros((8, LANES), F32)
    for t in range(wide // LANES):
        message[half + C + t : half + C + t + 1, :] = totals[0:1, t * LANES : (t + 1) * LANES]


def source_part(n_blk, n_len, n_wall, C, electrodes, bm, be, rows_n, rows_p, qm, mask, owner, base_adj, base_pot, *rest):
    patches, fm, fe, tm, te, hp = rest
    N = bm.shape[0] // C
    W = N - 2 * H
    blk, length, wall = lax.axis_index("blk"), lax.axis_index("len"), lax.axis_index("wall")
    fm[...] = bm[...]
    fe[...] = be[...]
    for rows, near, second in ((rows_n, C - 1, C - 2), (rows_p, 0, 1)):
        for k, at in ((4, near), (6, second)):
            spot = pl.ds(at, N, stride=C)
            fm[spot, :] = fm[spot, :] + rows[k]
            fe[spot, :] = fe[spot, :] + rows[k + 1]
    coef, k0 = level_coef(0), level_step(0)
    rim = rim_lanes(lane_of((C, LANES)), length, n_len)

    def part(i):
        m, e = plane(fm, i, C), plane(fe, i, C)
        wm = plane(fm, i - 1, C) + plane(fm, i + 1, C)
        we = plane(fe, i - 1, C) + plane(fe, i + 1, C)
        lm, le = beside_lanes(m, e)
        at = pl.ds(i, 1)
        cm = beside_rows(m, rows_p[0, at, :], rows_n[0, at, :])
        ce = beside_rows(e, rows_p[1, at, :], rows_n[1, at, :])
        pm = k0 * ((2.0 - OMEGA) * m + k0 * (coef[0] * wm + coef[1] * cm + coef[2] * lm))
        pe = k0 * ((2.0 - OMEGA) * e + k0 * (coef[0] * we + coef[1] * ce + coef[2] * le))
        set_plane(tm, i, C, jnp.where(inside(i, wall, W, n_wall), pm, 0.0))
        set_plane(te, i, C, jnp.where(rim, pe, 0.0))

    loop(H - 1, N - H + 1, part, 2)
    for side, (rows, at) in enumerate(((rows_n, C - 1), (rows_p, 0))):
        m = rows[0]
        total = (
            coef[0] * beside_dense(m)
            + coef[1] * (rows[2] + dense(fm, at, N, C))
            + coef[2] * beside_lanes_main(m, rows[1])
        )
        hp[side] = k0 * ((2.0 - OMEGA) * m + k0 * total)
    row = lax.broadcasted_iota(jnp.int32, (C, LANES), 0)

    def finish(w):
        i = w + H
        m, e = plane(tm, i, C), plane(te, i, C)
        at = pl.ds(i, 1)
        wm = plane(tm, i - 1, C) + plane(tm, i + 1, C)
        cm = beside_rows(m, hp[1, at, :], hp[0, at, :])
        lm = beside_lanes_main(m, e)
        lam = plane(qm, i, C)
        lam = lam + jnp.where(row == C - 1, rows_n[3, at, :], 0.0) + jnp.where(row == 0, rows_p[3, at, :], 0.0)
        moved = 2.0 * sum(SI) * m - SI[0] * wm - SI[1] * cm - SI[2] * lm
        set_plane(base_adj, w, C, lam - DT * plane(mask, w, C) * moved)
        set_plane(base_pot, w, C, m)

    loop(0, W, finish, 2)

    me = (blk * n_len + length) * n_wall + wall
    which = lax.broadcasted_iota(jnp.int32, (1, electrodes), 1).astype(F32)
    mine = owner[...] == me
    patches[0:1, :] = jnp.full((1, LANES), jnp.min(jnp.where(mine, which, float(electrodes))))
    patches[1:2, :] = jnp.full((1, LANES), jnp.max(jnp.where(mine, which, -1.0)))
    patches[2:8, :] = jnp.zeros((6, LANES), F32)


def around(x, by):
    rows, lanes = x.shape
    lane = lane_of(x.shape)
    c = pltpu.roll(x, by, 0) + pltpu.roll(x, rows - by, 0)
    l = jnp.where(lane < by, 0.0, pltpu.roll(x, by, 1)) + jnp.where(
        lane >= lanes - by, 0.0, pltpu.roll(x, lanes - by, 1)
    )
    return c, l


def twins(x, by):
    rows, lanes = x.shape
    if lanes == LANES:
        index = lax.broadcasted_iota(jnp.int32, (8, LANES), 0) ^ by
        x = x + jnp.concatenate([rows_at(x[t : t + 8], index) for t in range(0, rows, 8)], 0)
        return x + lanes_at(x, lane_of(x.shape) ^ by)
    row = lax.broadcasted_iota(jnp.int32, x.shape, 0)
    lane = lane_of(x.shape)
    x = x + jnp.where((row & by) == 0, pltpu.roll(x, rows - by, 0), pltpu.roll(x, by, 0))
    return x + jnp.where((lane & by) == 0, pltpu.roll(x, lanes - by, 1), pltpu.roll(x, by, 1))


def solve(sizes, relative, C, W, *refs):
    n_blk, n_len, n_wall = sizes
    count = n_len * n_wall
    blocks, refs = refs[:count], refs[count:]
    base_adj, base_pot, mask, patches, adj_prev, potential, patch_grad = refs[:7]
    b1, x1, b2, x2, b3, x3, near, pm, pe, tm, te, adj_out, pot_out, sheet, sems = refs[7:]
    L = LANES
    W1, C1 = W // 2, C // 2
    planes, NC1, NL1 = b1.shape
    planes -= 2
    blk, length, wall = lax.axis_index("blk"), lax.axis_index("len"), lax.axis_index("wall")
    half = W1 // 2
    middle = LANES // 2
    lane8 = lane_of((C1, LANES))
    often = 8 if NC1 * NL1 <= 4096 else 1

    def blk_of(d):
        return lax.rem(blk - d + n_blk, n_blk) if relative else d

    def length_of(j):
        return (length + j) % n_len if n_len == 2 else j

    def wall_of(v):
        return (wall + v) % n_wall

    zero1 = jnp.zeros((NC1, NL1), F32)
    for ref in (b1, x1, b2, x2, b3, x3):
        ref[0] = zero1
        ref[ref.shape[0] - 1] = zero1

    for v in range(n_wall):
        wall_s = wall_of(v)
        mine = blocks[v * n_len : (v + 1) * n_len]

        def unpack(d):
            at = pl.ds(pl.multiple_of(C1 * blk_of(d), C1), C1)
            for t in range(n_len // 2):
                one, two = mine[2 * t], mine[2 * t + 1]
                for i in range(half):
                    a, b = one[d, i * C1 : (i + 1) * C1, :], two[d, i * C1 : (i + 1) * C1, :]
                    if n_len == 2:
                        a, b = jnp.where(length == 0, a, b), jnp.where(length == 0, b, a)
                    spot = 1 + wall_s * W1 + i
                    lanes = slice(t * LANES, (t + 1) * LANES)
                    b1[spot, at, lanes] = jnp.where(lane8 < middle, a, pltpu.roll(b, middle, 1))
                    b1[spot + half, at, lanes] = jnp.where(lane8 < middle, pltpu.roll(a, middle, 1), b)

        loop(0, n_blk, unpack, 4)

    def total_of(x, wsum, level, by):
        coef = level_coef(level)
        c, l = around(x, by)
        return level_step(level) * (coef[0] * wsum + coef[1] * c + coef[2] * l)

    def left_pair(ref, i, level):
        both = ref[i] + ref[i + 1]
        return (1.0 - OMEGA) * both + total_of(both, ref[i - 1] + both + ref[i + 2], level, 2 ** (level - 1))

    def sweep(x_ref, b_ref, i, level):
        x = x_ref[i]
        total = total_of(x, x_ref[i - 1] + x_ref[i + 1], level, 2 ** (level - 1))
        return (1.0 - OMEGA) * x + level_step(level) * b_ref[i] + total

    def down1(q):
        b2[1 + q] = 0.125 * twins(left_pair(b1, 2 * q + 1, 1), 1)

    loop(0, planes // 2, down1, often)

    def down2(q):
        b3[1 + q] = 0.125 * twins(left_pair(b2, 2 * q + 1, 2), 2)

    loop(0, planes // 4, down2, often)

    deep = planes // 4
    k3 = level_step(3)

    x2[1 + deep] = zero1

    def start3(q):
        b = b3[1 + q]
        x2[1 + q] = k3 * ((2.0 - OMEGA) * b + total_of(b, b3[q] + b3[2 + q], 3, 4))

    loop(0, deep, start3, often)

    def sweep3(q):
        x3[1 + q] = sweep(x2, b3, 1 + q, 3)

    loop(0, deep, sweep3, often)
    k2 = level_step(2)

    def up2(q):
        coarse = x3[1 + q]
        x2[1 + 2 * q] = k2 * b2[1 + 2 * q] + coarse
        x2[2 + 2 * q] = k2 * b2[2 + 2 * q] + coarse

    loop(0, planes // 4, up2, often)

    k1 = level_step(1)

    def up1(q):
        fine = sweep(x2, b2, 1 + q, 2)
        x1[1 + 2 * q] = k1 * b1[1 + 2 * q] + fine
        x1[2 + 2 * q] = k1 * b1[2 + 2 * q] + fine

    loop(0, planes // 2, up1, often)

    Q = W1 + 2
    sectors = (blk, lax.rem(blk + 1, n_blk), lax.rem(blk + n_blk - 1, n_blk))
    spots3 = [pl.ds(pl.multiple_of(s * C1, C1), C1) for s in sectors]
    row8 = lax.broadcasted_iota(jnp.int32, (C1, NL1), 0)

    def three(ref, i):
        return jnp.concatenate([ref[i, s, :] for s in spots3], 0)

    def finish1(q):
        i = wall * W1 + q
        x = three(x1, i)
        wsum = three(x1, jnp.maximum(i - 1, 0)) + three(x1, jnp.minimum(i + 1, planes + 1))
        value = (1.0 - OMEGA) * x + k1 * three(b1, i) + total_of(x, wsum, 1, 1)
        value = jnp.where(jnp.logical_and(i >= 1, i <= planes), value, 0.0)
        set_plane(near, 2 * q, C1, value[:C1])
        set_plane(near, 2 * q + 1, C1, jnp.where(row8 < 2, value[C1 : 2 * C1], value[2 * C1 :]))

    loop(0, Q, finish1, min(often, 6))

    first = length * middle
    R = C + 8
    row8 = lax.broadcasted_iota(jnp.int32, (8, LANES), 0)
    tile_lane = lane_of((8, LANES))
    at_e = jnp.where(tile_lane < H, middle + tile_lane // 2, tile_lane // 2 - middle)
    rim8 = rim_lanes(tile_lane, length, n_len)
    if NL1 == LANES:
        index_m, index_e = first + tile_lane // 2, jnp.clip(first + at_e, 0, LANES - 1)

        def spread(tile):
            return lanes_at(tile, index_m), jnp.where(rim8, lanes_at(tile, index_e), 0.0)

    else:
        source = lax.broadcasted_iota(jnp.int32, (NL1, LANES), 0)
        lane = lane_of((NL1, LANES))
        at_all = jnp.where(lane < H, middle + lane // 2, jnp.where(lane >= LANES - H, lane // 2 - middle, 4 * NL1))
        take_m = jnp.where(source == first + lane // 2, 1.0, 0.0).astype(F32)
        take_e = jnp.where(source == first + at_all, 1.0, 0.0).astype(F32)

        def spread(tile):
            return precise(tile, take_m), precise(tile, take_e)

    picks = (row8 // 2, H + row8 // 2, jnp.where(row8 < H, row8 // 2, H + row8 // 2))

    def fine_rows(q):
        own = spread(plane(near, 2 * q, C1))
        beside = spread(plane(near, 2 * q + 1, C1))
        for out, a, b in ((pm, own[0], beside[0]), (pe, own[1], beside[1])):
            parts = (rows_at(a, picks[0]), rows_at(a, picks[1]), rows_at(b, picks[2]))
            set_plane(out, q, R, jnp.concatenate(parts, 0))

    loop(0, Q, fine_rows, min(often, 6))
    coef, k0 = level_coef(0), level_step(0)
    rim = rim_lanes(lane_of((C, LANES)), length, n_len)

    def rows_beside(x):
        return pltpu.roll(x, 1, 0) + pltpu.roll(x, x.shape[0] - 1, 0)

    def coarse_terms(q):
        m, e = plane(pm, q, R), plane(pe, q, R)
        lm, le = beside_lanes(m, e)
        gm = (1.0 - OMEGA) * m + k0 * (coef[0] * m + coef[1] * rows_beside(m) + coef[2] * lm)
        ge = (1.0 - OMEGA) * e + k0 * (coef[0] * e + coef[1] * rows_beside(e) + coef[2] * le)
        return gm, ge[:C]

    ks = k0 * coef[0]

    def put_end(t, q, other, ok):
        set_plane(tm, t, R, jnp.where(ok, coarse_terms(q)[0] + ks * plane(pm, other, R), 0.0))

    put_end(0, 0, 1, wall > 0)
    put_end(W + 1, Q - 1, Q - 2, wall < n_wall - 1)

    def level0(q):
        gm, ge = coarse_terms(q)
        for t, other in ((2 * q - 1, q - 1), (2 * q, q + 1)):
            m = gm + ks * plane(pm, other, R)
            set_plane(tm, t, R, m)
            set_plane(te, t - 1, C, jnp.where(rim, ge + ks * plane(pe, other, R)[:C], 0.0))
            set_plane(pot_out, t - 1, C, plane(base_pot, t - 1, C) + m[:C])

    def finish0(w):
        m, e = plane(tm, w + 1, R), plane(te, w, C)
        cm = rows_beside(m)[:C]
        m = m[:C]
        wm = plane(tm, w, R)[:C] + plane(tm, w + 2, R)[:C]
        lm = beside_lanes_main(m, e)
        moved = 2.0 * sum(SI) * m - SI[0] * wm - SI[1] * cm - SI[2] * lm
        set_plane(adj_out, w, C, plane(base_adj, w, C) - DT * plane(mask, w, C) * moved)

    parts = 2
    size = W // parts
    copies = []

    def send(src, dst, k, sem):
        spot = pl.ds(k * size * C, size * C)
        copies.append(pltpu.make_async_copy(src.at[spot], dst.at[spot], sem))
        copies[-1].start()

    for k in range(parts):
        loop(1 + k * W1 // parts, 1 + (k + 1) * W1 // parts, level0, 4)
        send(pot_out, potential, k, sems.at[0, k])
    for k in range(parts):
        loop(k * size, (k + 1) * size, finish0, 4)
        send(adj_out, adj_prev, k, sems.at[1, k])

    NC, NL = sheet.shape[1:]

    def whole_fine(x):
        if NL1 == LANES:
            parts = []
            for t in range(0, NC1, 8):
                wide8 = [lanes_at(x[t : t + 8], tile_lane // 2 + k * middle) for k in range(2)]
                for pick in picks[:2]:
                    parts.append(jnp.concatenate([rows_at(v, pick) for v in wide8], 1))
            return jnp.concatenate(parts, 0)
        along_c = lax.broadcasted_iota(jnp.int32, (NC, NC1), 0) // 2
        along_l = lax.broadcasted_iota(jnp.int32, (NL1, NL), 1) // 2
        twice_c = jnp.where(along_c == lax.broadcasted_iota(jnp.int32, (NC, NC1), 1), 1.0, 0.0).astype(F32)
        twice_l = jnp.where(along_l == lax.broadcasted_iota(jnp.int32, (NL1, NL), 0), 1.0, 0.0).astype(F32)
        return precise(precise(twice_c, x), twice_l)

    for s, i in enumerate((1, planes)):
        p = whole_fine(sweep(x1, b1, i, 1))
        c, l = around(p, 1)
        sheet[s] = (1.0 - OMEGA) * p + k0 * (coef[0] * p + coef[1] * c + coef[2] * l)

    owned = [patches[r : r + 1, :] for r in range(2)]
    spot = lax.broadcasted_iota(jnp.int32, (8, LANES), 0) * LANES + lane_of((8, LANES))
    spot = spot.astype(F32)
    start = half * C1
    totals = [jnp.zeros((C, LANES), F32) for _ in owned]
    small = [jnp.zeros((8, LANES), F32) for _ in owned]
    for v in range(n_wall):
        wall_s = wall_of(v)
        for j in range(n_len):
            ref = blocks[v * n_len + j]
            at_l = pl.ds(pl.multiple_of(length_of(j) * L, L), L)

            def add(d, carry):
                big, little = carry
                values = sheet[wall_s, pl.ds(pl.multiple_of(blk_of(d) * C, C), C), at_l]
                ids = ref[d, start : start + C, :]
                parts = ref[d, start + C : start + C + 8, :]
                big = [x + jnp.where(ids == e, values, 0.0) for x, e in zip(big, owned)]
                little = [x + jnp.where(spot == e, parts, 0.0) for x, e in zip(little, owned)]
                return big, little

            totals, small = lax.fori_loop(0, n_blk, add, (totals, small), unroll=min(4, n_blk))
    factor = 1.0 / (2.0 * C * L / 2) ** 0.5
    for r in range(2):
        patch_grad[0, r] = (jnp.sum(totals[r]) + jnp.sum(small[r])) * factor
    for copy in copies:
        copy.wait()


def ring(x, axis, by):
    count = lax.axis_size(axis)
    return lax.ppermute(x, axis, [(i, (i + by) % count) for i in range(count)])


def across(x):
    n_wall = lax.axis_size("wall")
    pairs = [(l * n_wall + w, (1 - l) * n_wall + (w + 1) % n_wall) for l in range(2) for w in range(n_wall)]
    return lax.ppermute(x, ("len", "wall"), pairs)


def call(kernel, ins, outs, scratch, name, work=0, room=48):
    places = {"vmem": pltpu.VMEM, "smem": pltpu.SMEM, "any": pl.ANY, "hbm": pltpu.HBM}

    def specs(kinds):
        return [pl.BlockSpec(memory_space=places[kind]) for kind in kinds]

    cost = pl.CostEstimate(flops=work, bytes_accessed=work, transcendentals=0) if work else None
    return pl.pallas_call(
        kernel,
        out_shape=[jax.ShapeDtypeStruct(shape, F32) for shape, _ in outs],
        in_specs=specs(ins),
        out_specs=specs(kind for _, kind in outs),
        scratch_shapes=[pltpu.VMEM(shape, F32) if isinstance(shape, tuple) else shape for shape in scratch],
        compiler_params=pltpu.CompilerParams(vmem_limit_bytes=int(room * 2**20)),
        cost_estimate=cost,
        name=name,
    )


def body(adj_next, ion_slope, misfit, tissue_mask, patch_ids, owner_map):
    W, C, L = adj_next.shape
    n_blk, n_len, n_wall = lax.axis_size("blk"), lax.axis_size("len"), lax.axis_size("wall")
    electrodes = owner_map.shape[0]
    assert L == LANES and H * W == LANES and n_wall == 2 and electrodes == 2 * n_blk * n_len * n_wall
    N = W + 2 * H
    n_dir = 1 if n_len == 2 else 2
    cells = W * C
    vmem = "vmem"
    field, own = (N * C, L), (cells, L)
    raw = [x.reshape(cells, L) for x in (adj_next, ion_slope, tissue_mask, misfit)]

    *fields, wall_out = (faces := call(
        functools.partial(pack_faces, n_len),
        ["hbm"] * 4,
        [(own, vmem)] * 4
        + [((sum(FACES), C, L), vmem)]
        + [((4, C, L), vmem)] * n_dir
        + [((C, L), vmem)] * n_dir,
        [pltpu.VMEM(own, jnp.int32), pltpu.SemaphoreType.DMA((4, 2))],
        "faces",
        room=52.75,
    )(*raw))[:5]
    strip_out, corner_out = faces[5 : 5 + n_dir], faces[5 + n_dir :]
    wall_in = ring(wall_out, "wall", 1)
    if n_dir == 1:
        strips = [ring(strip_out[0], "len", 1)]
        corners = [across(corner_out[0])]
    else:
        strips = [ring(strip_out[1], "len", -1), ring(strip_out[0], "len", 1)]
        corners = [ring(ring(corner_out[1], "wall", 1), "len", -1), ring(ring(corner_out[0], "wall", 1), "len", 1)]

    near = (sum(near_rows(n_dir, W)[-1][::2]), L)
    halos = [wall_in, *strips, *corners]
    to_next, to_prev, own_rows = call(
        functools.partial(boundary, n_len, C),
        [vmem] * (5 + 2 * n_dir),
        [(near, vmem)] * 2 + [((2, 6, N, L), vmem)],
        [(48, N, L)],
        "boundary",
    )(*fields, *halos)
    from_next = ring(to_prev, "blk", -1)
    from_prev = ring(to_next, "blk", 1)
    qm, bm, be, coarse, surface = call(
        functools.partial(sector, n_len, n_wall, C),
        [vmem] * (5 + 2 * n_dir),
        [(field, vmem)] * 3 + [((cells // 8, L), vmem), ((C, L), vmem)],
        [field, (cells // 2, L)] + [field] * 8,
        "sector",
        work=16 * 10**6,
    )(*fields, *halos)

    rows = (8, N, L)
    wide = LANES * ((electrodes + LANES - 1) // LANES)
    message = (cells // 8 + C + 8, L)
    rows_n, rows_p, mine = call(
        functools.partial(correct, electrodes, n_len, n_wall),
        [vmem] * 6,
        [(rows, vmem), (rows, vmem), (message, vmem)],
        [(1, N, L), (wide, L)],
        "correct",
    )(own_rows, from_next, from_prev, coarse, surface, patch_ids)

    relative = n_blk <= 4
    moved = [ring(mine, "blk", d) for d in range(1, n_blk)] if relative else [lax.all_gather(mine, "blk")]
    base_adj, base_pot, patches = call(
        functools.partial(source_part, n_blk, n_len, n_wall, C, electrodes),
        [vmem] * 7,
        [(own, vmem), (own, vmem), ((8, L), vmem)],
        [field] * 4 + [(2, N, L)],
        "source_part",
        work=12 * 10**6,
    )(bm, be, rows_n, rows_p, qm, fields[2], owner_map.reshape(1, electrodes))
    moved, base_adj = lax.optimization_barrier((moved, base_adj))
    sector_blocks = jnp.stack([mine] + moved) if relative else moved[0]
    if n_len == 2:
        here = [sector_blocks, ring(sector_blocks, "len", 1)]
    else:
        gathered = lax.all_gather(sector_blocks, "len")
        here = [gathered[j] for j in range(n_len)]
    blocks = here + [ring(x, "wall", 1) for x in here]

    NC1, NL1 = n_blk * C // 2, n_len * L // 2
    planes = n_wall * W // 2
    grids = [(planes // k + 2, NC1, NL1) for k in (1, 1, 2, 2, 4, 4)]
    Q = W // 2 + 2
    tall = (Q * (C + 8), L)
    taller = ((W + 2) * (C + 8), L)
    scratch = grids + [(Q * C, NL1), tall, tall, taller, own, own, own]
    scratch += [(2, n_blk * C, n_len * L), pltpu.SemaphoreType.DMA((2, 2))]
    adj_prev, potential, patch_grad = call(
        functools.partial(solve, (n_blk, n_len, n_wall), relative, C, W),
        [vmem] * (len(blocks) + 4),
        [(own, "any"), (own, "any"), ((1, 2), "smem")],
        scratch,
        "solve",
        room=48 if NC1 * NL1 <= 4096 else 58,
    )(*blocks, base_adj, base_pot, fields[2], patches)
    return adj_prev.reshape(W, C, L), potential.reshape(W, C, L), patch_grad


def solution(mesh):
    field = P(("groups", "wall"), "blk", "len")
    return jax.shard_map(
        body,
        mesh=mesh,
        in_specs=(field, field, field, field, field, P("groups")),
        out_specs=(field, field, P(("groups", "blk", "len", "wall"), None)),
        check_vma=False,
    )
```

```python
import functools

import jax
import jax.numpy as jnp
from jax import lax
from jax.experimental import pallas as pl
from jax.experimental.pallas import tpu as pltpu
from jax.sharding import PartitionSpec as P

SI = (0.6, 1.0, 3.0)
SE = (0.8, 1.2, 2.0)
SHIFT = 0.002
OMEGA = 0.8
DT = 0.1
H = 4
LANES = 128
HIGHEST = lax.Precision.HIGHEST
F32 = jnp.float32


def level_coef(level):
    return tuple((SI[i] + SE[i]) / 4.0**level for i in range(3))


def level_diag(level):
    return SHIFT + 2.0 * sum(level_coef(level))


def level_step(level):
    return OMEGA / level_diag(level)


def lane_of(shape):
    return lax.broadcasted_iota(jnp.int32, shape, len(shape) - 1)


def before(m, e):
    first = lane_of(m.shape) == 0
    rm, re = pltpu.roll(m, 1, 1), pltpu.roll(e, 1, 1)
    return jnp.where(first, re, rm), jnp.where(first, rm, re)


def after(m, e):
    last = lane_of(m.shape) == LANES - 1
    rm, re = pltpu.roll(m, LANES - 1, 1), pltpu.roll(e, LANES - 1, 1)
    return jnp.where(last, re, rm), jnp.where(last, rm, re)


def beside_lanes(m, e):
    bm, be = before(m, e)
    am, ae = after(m, e)
    return bm + am, be + ae


def beside_lanes_main(m, e):
    lane = lane_of(m.shape)
    ends = lanes_at(e, LANES - 1 - lane)
    left = jnp.where(lane == 0, ends, pltpu.roll(m, 1, 1))
    right = jnp.where(lane == LANES - 1, ends, pltpu.roll(m, LANES - 1, 1))
    return left + right


def beside_rows(x, row_before, row_after):
    rows = x.shape[0]
    row = lax.broadcasted_iota(jnp.int32, x.shape, 0)
    low = jnp.where(row == 0, row_before, pltpu.roll(x, 1, 0))
    high = jnp.where(row == rows - 1, row_after, pltpu.roll(x, rows - 1, 0))
    return low + high


def beside_dense(x):
    return pltpu.roll(x, 1, 0) + pltpu.roll(x, x.shape[0] - 1, 0)


def plane(ref, i, rows):
    return ref[pl.ds(pl.multiple_of(i * rows, rows), rows), :]


def set_plane(ref, i, rows, value):
    ref[pl.ds(pl.multiple_of(i * rows, rows), rows), :] = value


def loop(low, high, step, unroll):
    def wrapped(i, carry):
        step(i)
        return carry

    lax.fori_loop(low, high, wrapped, 0, unroll=min(unroll, high - low))


FACES = (H, H - 1, H - 1, H - 2)


def face_planes(array):
    return FACES[array], sum(FACES[:array])


def pack_faces(n_len, adj, ion, mask, mis, *rest):
    n_dir = 1 if n_len == 2 else 2
    fields, wall_out, rest = rest[:4], rest[4], rest[5:]
    strips, corners = rest[:n_dir], rest[n_dir : 2 * n_dir]
    whole_mask, sems = rest[2 * n_dir :]
    cells = adj.shape[0]
    C = wall_out.shape[1]
    W = cells // C
    wall, length = lax.axis_index("wall"), lax.axis_index("len")
    targets = (fields[0], fields[1], whole_mask, fields[3])
    copies = []
    for a, (src, dst) in enumerate(zip((adj, ion, mask, mis), targets)):
        part = cells // 2
        for k in range(2):
            spot = pl.ds(k * part, part)
            copies.append(pltpu.make_async_copy(src.at[spot], dst.at[spot], sems.at[a, k]))
            copies[-1].start()

    base = jnp.where(wall == 0, W - H, 0)
    group = lane_of((C, LANES)) // H
    turns = [jnp.where(length == 0, H, 0)] if n_dir == 1 else [H, 0]
    corner = [jnp.zeros((C, LANES), F32) for _ in range(n_dir)]
    for a in (0, 1, 3, 2):
        copies[2 * a].wait()
        copies[2 * a + 1].wait()
        if a == 2:
            fields[2][...] = whole_mask[...].astype(F32)
        ref = fields[a]
        strip = [jnp.zeros((C, LANES), F32) for _ in range(n_dir)]
        for w in range(W):
            value = ref[w * C : (w + 1) * C, :]
            for d in range(n_dir):
                turned = pltpu.roll(value, lax.rem(H * w + turns[d], LANES), 1)
                strip[d] = jnp.where(group == w, turned, strip[d])
        for d in range(n_dir):
            strips[d][a] = strip[d]
        count, first = face_planes(a)
        for p in range(count):
            face = plane(ref, base + jnp.where(wall == 0, H - count, 0) + p, C)
            wall_out[first + p] = face
            slot = first + p
            for d in range(n_dir):
                turned = pltpu.roll(face, lax.rem(H * slot + turns[d], LANES), 1)
                corner[d] = jnp.where(group == slot, turned, corner[d])
    for d in range(n_dir):
        corners[d][...] = corner[d]


def dense(ref, row, N, C):
    return ref[pl.ds(row, N, stride=C), :]


def dense_pair(m, e, row, N, C):
    return dense(m, row, N, C), dense(e, row, N, C)


def dense_apply(pair, inner, outer, coef):
    m, e = pair
    lm, le = beside_lanes(m, e)
    double = 2.0 * sum(coef)
    out = [double * m - coef[0] * beside_dense(m) - coef[2] * lm, double * e - coef[0] * beside_dense(e) - coef[2] * le]
    for row in (inner, outer):
        if row is not None:
            out = [out[k] - coef[1] * row[k] for k in range(2)]
    return out


def near_rows(n_dir, W):
    start, places = 8 * n_dir, []
    for reach in (0, 1, 2, 2, 3):
        places.append((start, H - reach, W + 2 * reach))
        start += W + 2 * reach
    assert start % 8 == 0
    return places


def rim_tiles(values):
    return [value[s : s + 8] for value in values for s in range(0, value.shape[0], 8)]


def rim_places(n_len, length):
    if n_len == 2:
        return [(jnp.where(length == 0, 0, LANES - H), True)]
    return [(0, length < n_len - 1), (LANES - H, length > 0)]


def boundary(n_len, C, *refs):
    n_dir = 1 if n_len == 2 else 2
    raw, wall_in, refs = refs[:4], refs[4], refs[5:]
    strips, corners, refs = refs[:n_dir], refs[n_dir : 2 * n_dir], refs[2 * n_dir :]
    to_next, to_prev, own_rows, build = refs
    W = raw[0].shape[0] // C
    N = W + 2 * H
    wall, length = lax.axis_index("wall"), lax.axis_index("len")
    places = rim_places(n_len, length)

    def strip_rows(packed, first, count):
        lane, k = lane_of((count, LANES)), lax.broadcasted_iota(jnp.int32, (count, LANES), 0)
        out = jnp.zeros((count, LANES), F32)
        for row, (off, ok) in zip(packed, places):
            j = lax.rem(lane - off + LANES, LANES)
            index = jnp.clip(H * (first + k) + j, 0, LANES - 1)
            taken = lanes_at(jnp.broadcast_to(row, (count, LANES)), index)
            out = jnp.where(jnp.logical_and(j < H, ok), taken, out)
        return out

    slots = iter(range(build.shape[0]))

    def assembled(own, halo, count):
        ref = build.at[next(slots)]
        ref[0:8, :] = jnp.zeros((8, LANES), F32)
        ref[N - 8 : N, :] = jnp.zeros((8, LANES), F32)
        ref[H : H + W, :] = own
        ref[H - count : H, :] = jnp.where(wall == 0, 0.0, halo)
        ref[H + W : H + W + count, :] = jnp.where(wall == 0, halo, 0.0)
        return ref[...]

    def row_of(a, r):
        count, first = face_planes(a)
        halo = jnp.concatenate([wall_in[first + p, r : r + 1, :] for p in range(count)], 0)
        m = assembled(raw[a][pl.ds(r, W, stride=C), :], halo, count)
        own = strip_rows([strip[a, r : r + 1, :] for strip in strips], 0, W)
        halo = strip_rows([corner[r : r + 1, :] for corner in corners], first, 8)[:count]
        return m, assembled(own, halo, count)

    length_shift = jnp.where(length == 0, 0, H) if n_dir == 1 else H
    group = lane_of((8, LANES)) // (H * n_dir)
    for side, (out, order) in enumerate(((to_next, (C - 1, C - 2, C - 3, C - 4)), (to_prev, (0, 1, 2, 3)))):
        adj = [row_of(0, r) for r in order]
        mask = [row_of(2, r) for r in order[:3]]
        q = []
        for k in range(3):
            ion = row_of(1, order[k])
            moved = dense_apply(adj[k], adj[k + 1], adj[k - 1] if k else None, SI)
            q.append([adj[k][j] - DT * mask[k][j] * (moved[j] + ion[j] * adj[k][j]) for j in range(2)])
        near = dense_apply(q[0], q[1], None, SI)
        mis = row_of(3, order[0])
        near = [near[j] + mis[j] for j in range(2)]
        second = dense_apply(q[1], q[2], q[0], SI)[0] + row_of(3, order[1])[0]
        for value, (start, first, count) in zip((second, near[0], q[0][0], mask[0][0], adj[0][0]), near_rows(n_dir, W)):
            out[start : start + count, :] = value[first : first + count]
        packs = [jnp.zeros((8, LANES), F32) for _ in range(n_dir)]
        for t, tile in enumerate(rim_tiles((near[1], q[0][1], mask[0][1], adj[0][1]))):
            k, at = divmod(t, LANES // (H * n_dir))
            turned = pltpu.roll(tile, lax.rem(length_shift + H * n_dir * at, LANES), 1)
            packs[k] = jnp.where(group == at, turned, packs[k])
        for k in range(n_dir):
            out[8 * k : 8 * k + 8, :] = packs[k]
        for k, pair in enumerate((adj[0], mask[0], q[0])):
            own_rows[side, 2 * k] = pair[0]
            own_rows[side, 2 * k + 1] = pair[1]


def spots(m_ref, e_ref, i, rows, coef):
    m, e = plane(m_ref, i, rows), plane(e_ref, i, rows)
    wm = plane(m_ref, i - 1, rows) + plane(m_ref, i + 1, rows)
    we = plane(e_ref, i - 1, rows) + plane(e_ref, i + 1, rows)
    lm, le = beside_lanes(m, e)
    cm, ce = beside_rows(m, 0.0, 0.0), beside_rows(e, 0.0, 0.0)
    double = 2.0 * sum(coef)
    dm = double * m - coef[0] * wm - coef[1] * cm - coef[2] * lm
    de = double * e - coef[0] * we - coef[1] * ce - coef[2] * le
    return m, e, dm, de


def rim_lanes(lane, length, n_len):
    return jnp.logical_or(
        jnp.logical_and(lane < H, length < n_len - 1),
        jnp.logical_and(lane >= LANES - H, length > 0),
    )


def inside(i, wall, W, n_wall):
    w = wall * W + i - H
    return jnp.logical_and(w >= 0, w < n_wall * W)


def lanes_at(x, index):
    return jnp.take_along_axis(x, index, axis=1, mode="promise_in_bounds")


def rows_at(x, index):
    return jnp.take_along_axis(x, index, axis=0, mode="promise_in_bounds")


def halved(low, high):
    lane = lane_of(low.shape)
    even = 2 * lane % LANES
    pairs = [lanes_at(x, even) + lanes_at(x, even + 1) for x in (low, high)]
    return 0.125 * jnp.where(lane < LANES // 2, pairs[0], pairs[1])


def precise(a, b):
    return jnp.dot(a, b, precision=HIGHEST, preferred_element_type=F32)


def assemble(n_len, C, raw, wall_in, strips, corners, xm, xe):
    W = raw[0].shape[0] // C
    N = W + 2 * H
    wall, length = lax.axis_index("wall"), lax.axis_index("len")
    lane = lane_of((C, LANES))
    places = rim_places(n_len, length)
    seen = [jnp.logical_and(lax.rem(lane - off + LANES, LANES) < H, ok) for off, ok in places]

    def rim(packed, base):
        out = jnp.zeros((C, LANES), F32)
        for row, ok, (off, _) in zip(packed, seen, places):
            out = jnp.where(ok, pltpu.roll(row, lax.rem(off - base + LANES, LANES), 1), out)
        return out

    zero = jnp.zeros((C, LANES), F32)
    last = N - H
    for a, own in enumerate(raw):
        packed = [strip[a] for strip in strips]
        for w in range(W):
            set_plane(xm[a], w + H, C, plane(own, w, C))
            set_plane(xe[a], w + H, C, rim(packed, H * w))
        packed = [corner[...] for corner in corners]
        for i in range(H):
            for at in (i, last + i):
                set_plane(xm[a], at, C, zero)
                set_plane(xe[a], at, C, zero)
        count, first = face_planes(a)
        here = jnp.where(wall == 0, last, H - count)
        for p in range(count):
            set_plane(xm[a], here + p, C, wall_in[first + p])
            set_plane(xe[a], here + p, C, rim(packed, H * (first + p)))


def sector(n_len, n_wall, C, *refs):
    n_dir = 1 if n_len == 2 else 2
    raw, wall_in, refs = refs[:4], refs[4], refs[5:]
    strips, corners, refs = refs[:n_dir], refs[n_dir : 2 * n_dir], refs[2 * n_dir :]
    qm, bm, be, coarse, surface, qe, pairs = refs[:7]
    xm, xe = refs[7:11], refs[11:15]
    assemble(n_len, C, raw, wall_in, strips, corners, xm, xe)
    N = qm.shape[0] // C
    W = N - 2 * H
    wall, length = lax.axis_index("wall"), lax.axis_index("len")
    rim = rim_lanes(lane_of((C, LANES)), length, n_len)
    zero = jnp.zeros((C, LANES), F32)
    for i in (0, N - 1):
        set_plane(qm, i, C, zero)
        set_plane(qe, i, C, zero)
    for i in (0, 1, N - 2, N - 1):
        set_plane(bm, i, C, zero)
        set_plane(be, i, C, zero)

    def parabolic(i):
        m, e, dm, de = spots(xm[0], xe[0], i, C, SI)
        set_plane(qm, i, C, m - DT * plane(xm[2], i, C) * (dm + plane(xm[1], i, C) * m))
        set_plane(qe, i, C, e - DT * plane(xe[2], i, C) * (de + plane(xe[1], i, C) * e))

    loop(1, N - 1, parabolic, 2)

    def elliptic_source(i):
        m, e, dm, de = spots(qm, qe, i, C, SI)
        ok = inside(i, wall, W, n_wall)
        set_plane(bm, i, C, jnp.where(ok, plane(xm[3], i, C) + dm, 0.0))
        set_plane(be, i, C, jnp.where(jnp.logical_and(rim, ok), plane(xe[3], i, C) + de, 0.0))

    loop(2, N - 2, elliptic_source, 2)

    coef, k0 = level_coef(0), level_step(0)

    def left(i):
        m, e = plane(bm, i, C), plane(be, i, C)
        wm = plane(bm, i - 1, C) + plane(bm, i + 1, C)
        cm = beside_rows(m, 0.0, 0.0)
        lm = beside_lanes_main(m, e)
        return m, (1.0 - OMEGA) * m + k0 * (coef[0] * wm + coef[1] * cm + coef[2] * lm)

    def pair(q):
        i = 2 * q + H
        m, first = left(i)
        n, second = left(i + 1)
        set_plane(pairs, q, C, first + second)

        @pl.when(jnp.logical_and(q == 0, wall == 0))
        def _():
            surface[...] = k0 * (m + first)

        @pl.when(jnp.logical_and(q == W // 2 - 1, wall == n_wall - 1))
        def _():
            surface[...] = k0 * (n + second)

    loop(0, W // 2, pair, 2)

    half = W * C // 8
    z = pairs[pl.ds(0, 2 * half, stride=2), :] + pairs[pl.ds(1, 2 * half, stride=2), :]
    coarse[...] = halved(z[:half], z[half:])


def unpacked(ref, n_len, length, N):
    n_dir = 1 if n_len == 2 else 2
    mains = []
    for start, first, count in near_rows(n_dir, N - 2 * H):
        begin = min(start - first, ref.shape[0] - N)
        value = ref[begin : begin + N, :]
        behind = start - first - begin
        mains.append(pltpu.roll(value, N - behind, 0) if behind else value)
    rim = rim_lanes(lane_of((8, LANES)), length, n_len)
    shift = jnp.where(length == 0, 0, H) if n_dir == 1 else H
    rims = []
    for k in range(4):
        parts = []
        for s in range(N // 8):
            pack, at = divmod(k * (N // 8) + s, LANES // (H * n_dir))
            back = lax.rem(2 * LANES - shift - H * n_dir * at, LANES)
            parts.append(jnp.where(rim, pltpu.roll(ref[8 * pack : 8 * pack + 8, :], back, 1), 0.0))
        rims.append(jnp.concatenate(parts, 0))
    second, near, q, mask, adj = mains
    return (adj, rims[3]), (mask, rims[2]), (q, rims[1]), (near, rims[0]), second


def lateral(pair):
    return dense_apply(pair, None, None, SI)


def source_rows(own, other):
    adj_o, mask_o, q_o = own
    adj_n, mask_n, q_n, p_n, second_n = other
    step = DT * SI[1]
    delta_o = [step * mask_o[k] * adj_n[k] for k in range(2)]
    delta_n = [step * mask_n[k] * adj_o[k] for k in range(2)]
    lat_o, lat_n = lateral(delta_o), lateral(delta_n)
    near = [lat_o[k] - SI[1] * (q_n[k] + delta_n[k]) for k in range(2)]
    second = [-SI[1] * delta_o[k] for k in range(2)]
    halo = [p_n[k] + lat_n[k] - SI[1] * (q_o[k] + delta_o[k]) for k in range(2)]
    halo_second = second_n - SI[1] * delta_n[0]
    return near, second, halo, halo_second, delta_o[0]


def correct(electrodes, n_len, n_wall, own_rows, from_next, from_prev, coarse, surface, ids, *rest):
    rows_n, rows_p, message = rest[:3]
    lines, sums = rest[3:]
    _, C, L = ids.shape
    N = own_rows.shape[2]
    W = N - 2 * H
    wall, length = lax.axis_index("wall"), lax.axis_index("len")
    ok_m = inside(lax.broadcasted_iota(jnp.int32, (N, LANES), 0), wall, W, n_wall)
    ok_e = jnp.logical_and(ok_m, rim_lanes(lane_of((N, LANES)), length, n_len))
    coef, k0 = level_coef(0), level_step(0)
    y = surface[...]
    row = lax.broadcasted_iota(jnp.int32, (C, LANES), 0)
    at = pl.ds(jnp.where(wall == 0, H, W + H - 1), 1)
    lows, highs = [], []
    W1, C1 = W // 2, C // 2
    for side, (other, out, order) in enumerate(
        ((from_next, rows_n, (C - 1, C - 2, C - 3)), (from_prev, rows_p, (0, 1, 2)))
    ):
        own = [(own_rows[side, 2 * k], own_rows[side, 2 * k + 1]) for k in range(3)]
        near, second, halo, halo_second, delta = source_rows(own, unpacked(other, n_len, length, N))
        near = [jnp.where(ok_m, near[0], 0.0), jnp.where(ok_e, near[1], 0.0)]
        second = [jnp.where(ok_m, second[0], 0.0), jnp.where(ok_e, second[1], 0.0)]
        out[0] = halo_m = jnp.where(ok_m, halo[0], 0.0)
        out[1] = jnp.where(ok_e, halo[1], 0.0)
        out[2] = jnp.where(ok_m, halo_second, 0.0)
        out[3] = delta
        out[4], out[5] = near
        out[6], out[7] = second

        def turned(pair, beside):
            m, e = pair
            return (1.0 - OMEGA) * m + k0 * (
                coef[0] * beside_dense(m) + coef[2] * beside_lanes_main(m, e) + coef[1] * beside
            )

        first = turned(near, second[0] + halo_m)
        next_one = turned(second, near[0])
        third = k0 * coef[1] * second[0]
        for k, change in enumerate((near[0] + first, second[0] + next_one, third)):
            lines[0] = change
            y = y + jnp.where(row == order[k], k0 * lines[0, at, :], 0.0)
        for change in (first + next_one, third):
            lines[0] = change
            both = lines[0, pl.ds(H, W1, stride=2), :] + lines[0, pl.ds(H + 1, W1, stride=2), :]
            lows.append(both[: W1 // 2])
            highs.append(both[W1 // 2 :])
    add = halved(jnp.concatenate(lows, 0), jnp.concatenate(highs, 0))
    half = W * C // 8
    message[0:half, :] = coarse[...]
    for k, c1 in enumerate((C1 - 1, C1 - 2, 0, 1)):
        spot = pl.ds(c1, W1 // 2, stride=C1)
        message[spot, :] = message[spot, :] + add[k * (W1 // 2) : (k + 1) * (W1 // 2)]
    patch = ids[0]
    message[half : half + C, :] = patch.astype(F32)
    wide = sums.shape[0]
    if wide > electrodes:
        sums[...] = jnp.zeros(sums.shape, F32)

    def one(e):
        sums[pl.ds(e, 1), :] = jnp.sum(jnp.where(patch == e, y, 0.0), axis=0, keepdims=True)

    loop(0, electrodes, one, 8)
    totals = lax.dot_general(
        jnp.ones((8, LANES), F32), sums[...], (((1,), (1,)), ((), ())), precision=HIGHEST, preferred_element_type=F32
    )
    message[half + C : half + C + 8, :] = jnp.zeros((8, LANES), F32)
    for t in range(wide // LANES):
        message[half + C + t : half + C + t + 1, :] = totals[0:1, t * LANES : (t + 1) * LANES]


def source_part(n_blk, n_len, n_wall, C, electrodes, bm, be, rows_n, rows_p, qm, mask, owner, base_adj, base_pot, *rest):
    patches, fm, fe, tm, te, hp = rest
    N = bm.shape[0] // C
    W = N - 2 * H
    blk, length, wall = lax.axis_index("blk"), lax.axis_index("len"), lax.axis_index("wall")
    fm[...] = bm[...]
    fe[...] = be[...]
    for rows, near, second in ((rows_n, C - 1, C - 2), (rows_p, 0, 1)):
        for k, at in ((4, near), (6, second)):
            spot = pl.ds(at, N, stride=C)
            fm[spot, :] = fm[spot, :] + rows[k]
            fe[spot, :] = fe[spot, :] + rows[k + 1]
    coef, k0 = level_coef(0), level_step(0)
    rim = rim_lanes(lane_of((C, LANES)), length, n_len)

    def part(i):
        m, e = plane(fm, i, C), plane(fe, i, C)
        wm = plane(fm, i - 1, C) + plane(fm, i + 1, C)
        we = plane(fe, i - 1, C) + plane(fe, i + 1, C)
        lm, le = beside_lanes(m, e)
        at = pl.ds(i, 1)
        cm = beside_rows(m, rows_p[0, at, :], rows_n[0, at, :])
        ce = beside_rows(e, rows_p[1, at, :], rows_n[1, at, :])
        pm = k0 * ((2.0 - OMEGA) * m + k0 * (coef[0] * wm + coef[1] * cm + coef[2] * lm))
        pe = k0 * ((2.0 - OMEGA) * e + k0 * (coef[0] * we + coef[1] * ce + coef[2] * le))
        set_plane(tm, i, C, jnp.where(inside(i, wall, W, n_wall), pm, 0.0))
        set_plane(te, i, C, jnp.where(rim, pe, 0.0))

    loop(H - 1, N - H + 1, part, 2)
    for side, (rows, at) in enumerate(((rows_n, C - 1), (rows_p, 0))):
        m = rows[0]
        total = (
            coef[0] * beside_dense(m)
            + coef[1] * (rows[2] + dense(fm, at, N, C))
            + coef[2] * beside_lanes_main(m, rows[1])
        )
        hp[side] = k0 * ((2.0 - OMEGA) * m + k0 * total)
    row = lax.broadcasted_iota(jnp.int32, (C, LANES), 0)

    def finish(w):
        i = w + H
        m, e = plane(tm, i, C), plane(te, i, C)
        at = pl.ds(i, 1)
        wm = plane(tm, i - 1, C) + plane(tm, i + 1, C)
        cm = beside_rows(m, hp[1, at, :], hp[0, at, :])
        lm = beside_lanes_main(m, e)
        lam = plane(qm, i, C)
        lam = lam + jnp.where(row == C - 1, rows_n[3, at, :], 0.0) + jnp.where(row == 0, rows_p[3, at, :], 0.0)
        moved = 2.0 * sum(SI) * m - SI[0] * wm - SI[1] * cm - SI[2] * lm
        set_plane(base_adj, w, C, lam - DT * plane(mask, w, C) * moved)
        set_plane(base_pot, w, C, m)

    loop(0, W, finish, 2)

    me = (blk * n_len + length) * n_wall + wall
    which = lax.broadcasted_iota(jnp.int32, (1, electrodes), 1).astype(F32)
    mine = owner[...] == me
    patches[0:1, :] = jnp.full((1, LANES), jnp.min(jnp.where(mine, which, float(electrodes))))
    patches[1:2, :] = jnp.full((1, LANES), jnp.max(jnp.where(mine, which, -1.0)))
    patches[2:8, :] = jnp.zeros((6, LANES), F32)


def around(x, by):
    rows, lanes = x.shape
    lane = lane_of(x.shape)
    c = pltpu.roll(x, by, 0) + pltpu.roll(x, rows - by, 0)
    l = jnp.where(lane < by, 0.0, pltpu.roll(x, by, 1)) + jnp.where(
        lane >= lanes - by, 0.0, pltpu.roll(x, lanes - by, 1)
    )
    return c, l


def twins(x, by):
    rows, lanes = x.shape
    if lanes == LANES:
        index = lax.broadcasted_iota(jnp.int32, (8, LANES), 0) ^ by
        x = x + jnp.concatenate([rows_at(x[t : t + 8], index) for t in range(0, rows, 8)], 0)
        return x + lanes_at(x, lane_of(x.shape) ^ by)
    row = lax.broadcasted_iota(jnp.int32, x.shape, 0)
    lane = lane_of(x.shape)
    x = x + jnp.where((row & by) == 0, pltpu.roll(x, rows - by, 0), pltpu.roll(x, by, 0))
    return x + jnp.where((lane & by) == 0, pltpu.roll(x, lanes - by, 1), pltpu.roll(x, by, 1))


def solve(sizes, relative, C, W, *refs):
    n_blk, n_len, n_wall = sizes
    count = n_len * n_wall
    blocks, refs = refs[:count], refs[count:]
    base_adj, base_pot, mask, patches, adj_prev, potential, patch_grad = refs[:7]
    b1, x1, b2, x2, b3, x3, near, pm, pe, tm, te, adj_out, pot_out, sheet, sems = refs[7:]
    L = LANES
    W1, C1 = W // 2, C // 2
    planes, NC1, NL1 = b1.shape
    planes -= 2
    blk, length, wall = lax.axis_index("blk"), lax.axis_index("len"), lax.axis_index("wall")
    half = W1 // 2
    middle = LANES // 2
    lane8 = lane_of((C1, LANES))
    often = 8 if NC1 * NL1 <= 4096 else 1

    def blk_of(d):
        return lax.rem(blk - d + n_blk, n_blk) if relative else d

    def length_of(j):
        return (length + j) % n_len if n_len == 2 else j

    def wall_of(v):
        return (wall + v) % n_wall

    zero1 = jnp.zeros((NC1, NL1), F32)
    for ref in (b1, x1, b2, x2, b3, x3):
        ref[0] = zero1
        ref[ref.shape[0] - 1] = zero1

    for v in range(n_wall):
        wall_s = wall_of(v)
        mine = blocks[v * n_len : (v + 1) * n_len]

        def unpack(d):
            at = pl.ds(pl.multiple_of(C1 * blk_of(d), C1), C1)
            for t in range(n_len // 2):
                one, two = mine[2 * t], mine[2 * t + 1]
                for i in range(half):
                    a, b = one[d, i * C1 : (i + 1) * C1, :], two[d, i * C1 : (i + 1) * C1, :]
                    if n_len == 2:
                        a, b = jnp.where(length == 0, a, b), jnp.where(length == 0, b, a)
                    spot = 1 + wall_s * W1 + i
                    lanes = slice(t * LANES, (t + 1) * LANES)
                    b1[spot, at, lanes] = jnp.where(lane8 < middle, a, pltpu.roll(b, middle, 1))
                    b1[spot + half, at, lanes] = jnp.where(lane8 < middle, pltpu.roll(a, middle, 1), b)

        loop(0, n_blk, unpack, 4)

    def total_of(x, wsum, level, by):
        coef = level_coef(level)
        c, l = around(x, by)
        return level_step(level) * (coef[0] * wsum + coef[1] * c + coef[2] * l)

    def left_pair(ref, i, level):
        both = ref[i] + ref[i + 1]
        return (1.0 - OMEGA) * both + total_of(both, ref[i - 1] + both + ref[i + 2], level, 2 ** (level - 1))

    def sweep(x_ref, b_ref, i, level):
        x = x_ref[i]
        total = total_of(x, x_ref[i - 1] + x_ref[i + 1], level, 2 ** (level - 1))
        return (1.0 - OMEGA) * x + level_step(level) * b_ref[i] + total

    def down1(q):
        b2[1 + q] = 0.125 * twins(left_pair(b1, 2 * q + 1, 1), 1)

    loop(0, planes // 2, down1, often)

    def down2(q):
        b3[1 + q] = 0.125 * twins(left_pair(b2, 2 * q + 1, 2), 2)

    loop(0, planes // 4, down2, often)

    deep = planes // 4
    k3 = level_step(3)

    x2[1 + deep] = zero1

    def start3(q):
        b = b3[1 + q]
        x2[1 + q] = k3 * ((2.0 - OMEGA) * b + total_of(b, b3[q] + b3[2 + q], 3, 4))

    loop(0, deep, start3, often)

    def sweep3(q):
        x3[1 + q] = sweep(x2, b3, 1 + q, 3)

    loop(0, deep, sweep3, often)
    k2 = level_step(2)

    def up2(q):
        coarse = x3[1 + q]
        x2[1 + 2 * q] = k2 * b2[1 + 2 * q] + coarse
        x2[2 + 2 * q] = k2 * b2[2 + 2 * q] + coarse

    loop(0, planes // 4, up2, often)

    k1 = level_step(1)

    def up1(q):
        fine = sweep(x2, b2, 1 + q, 2)
        x1[1 + 2 * q] = k1 * b1[1 + 2 * q] + fine
        x1[2 + 2 * q] = k1 * b1[2 + 2 * q] + fine

    loop(0, planes // 2, up1, often)

    Q = W1 + 2
    sectors = (blk, lax.rem(blk + 1, n_blk), lax.rem(blk + n_blk - 1, n_blk))
    spots3 = [pl.ds(pl.multiple_of(s * C1, C1), C1) for s in sectors]
    row8 = lax.broadcasted_iota(jnp.int32, (C1, NL1), 0)

    def three(ref, i):
        return jnp.concatenate([ref[i, s, :] for s in spots3], 0)

    def finish1(q):
        i = wall * W1 + q
        x = three(x1, i)
        wsum = three(x1, jnp.maximum(i - 1, 0)) + three(x1, jnp.minimum(i + 1, planes + 1))
        value = (1.0 - OMEGA) * x + k1 * three(b1, i) + total_of(x, wsum, 1, 1)
        value = jnp.where(jnp.logical_and(i >= 1, i <= planes), value, 0.0)
        set_plane(near, 2 * q, C1, value[:C1])
        set_plane(near, 2 * q + 1, C1, jnp.where(row8 < 2, value[C1 : 2 * C1], value[2 * C1 :]))

    loop(0, Q, finish1, min(often, 6))

    first = length * middle
    R = C + 8
    row8 = lax.broadcasted_iota(jnp.int32, (8, LANES), 0)
    tile_lane = lane_of((8, LANES))
    at_e = jnp.where(tile_lane < H, middle + tile_lane // 2, tile_lane // 2 - middle)
    rim8 = rim_lanes(tile_lane, length, n_len)
    if NL1 == LANES:
        index_m, index_e = first + tile_lane // 2, jnp.clip(first + at_e, 0, LANES - 1)

        def spread(tile):
            return lanes_at(tile, index_m), jnp.where(rim8, lanes_at(tile, index_e), 0.0)

    else:
        source = lax.broadcasted_iota(jnp.int32, (NL1, LANES), 0)
        lane = lane_of((NL1, LANES))
        at_all = jnp.where(lane < H, middle + lane // 2, jnp.where(lane >= LANES - H, lane // 2 - middle, 4 * NL1))
        take_m = jnp.where(source == first + lane // 2, 1.0, 0.0).astype(F32)
        take_e = jnp.where(source == first + at_all, 1.0, 0.0).astype(F32)

        def spread(tile):
            return precise(tile, take_m), precise(tile, take_e)

    picks = (row8 // 2, H + row8 // 2, jnp.where(row8 < H, row8 // 2, H + row8 // 2))

    def fine_rows(q):
        own = spread(plane(near, 2 * q, C1))
        beside = spread(plane(near, 2 * q + 1, C1))
        for out, a, b in ((pm, own[0], beside[0]), (pe, own[1], beside[1])):
            parts = (rows_at(a, picks[0]), rows_at(a, picks[1]), rows_at(b, picks[2]))
            set_plane(out, q, R, jnp.concatenate(parts, 0))

    loop(0, Q, fine_rows, min(often, 6))
    coef, k0 = level_coef(0), level_step(0)
    rim = rim_lanes(lane_of((C, LANES)), length, n_len)

    def rows_beside(x):
        return pltpu.roll(x, 1, 0) + pltpu.roll(x, x.shape[0] - 1, 0)

    def coarse_terms(q):
        m, e = plane(pm, q, R), plane(pe, q, R)
        lm, le = beside_lanes(m, e)
        gm = (1.0 - OMEGA) * m + k0 * (coef[0] * m + coef[1] * rows_beside(m) + coef[2] * lm)
        ge = (1.0 - OMEGA) * e + k0 * (coef[0] * e + coef[1] * rows_beside(e) + coef[2] * le)
        return gm, ge[:C]

    ks = k0 * coef[0]

    def put_end(t, q, other, ok):
        set_plane(tm, t, R, jnp.where(ok, coarse_terms(q)[0] + ks * plane(pm, other, R), 0.0))

    put_end(0, 0, 1, wall > 0)
    put_end(W + 1, Q - 1, Q - 2, wall < n_wall - 1)

    def level0(q):
        gm, ge = coarse_terms(q)
        for t, other in ((2 * q - 1, q - 1), (2 * q, q + 1)):
            m = gm + ks * plane(pm, other, R)
            set_plane(tm, t, R, m)
            set_plane(te, t - 1, C, jnp.where(rim, ge + ks * plane(pe, other, R)[:C], 0.0))
            set_plane(pot_out, t - 1, C, plane(base_pot, t - 1, C) + m[:C])

    def finish0(w):
        m, e = plane(tm, w + 1, R), plane(te, w, C)
        cm = rows_beside(m)[:C]
        m = m[:C]
        wm = plane(tm, w, R)[:C] + plane(tm, w + 2, R)[:C]
        lm = beside_lanes_main(m, e)
        moved = 2.0 * sum(SI) * m - SI[0] * wm - SI[1] * cm - SI[2] * lm
        set_plane(adj_out, w, C, plane(base_adj, w, C) - DT * plane(mask, w, C) * moved)

    parts = 2
    size = W // parts
    copies = []

    def send(src, dst, k, sem):
        spot = pl.ds(k * size * C, size * C)
        copies.append(pltpu.make_async_copy(src.at[spot], dst.at[spot], sem))
        copies[-1].start()

    for k in range(parts):
        loop(1 + k * W1 // parts, 1 + (k + 1) * W1 // parts, level0, 4)
        send(pot_out, potential, k, sems.at[0, k])
    for k in range(parts):
        loop(k * size, (k + 1) * size, finish0, 4)
        send(adj_out, adj_prev, k, sems.at[1, k])

    NC, NL = sheet.shape[1:]

    def whole_fine(x):
        if NL1 == LANES:
            parts = []
            for t in range(0, NC1, 8):
                wide8 = [lanes_at(x[t : t + 8], tile_lane // 2 + k * middle) for k in range(2)]
                for pick in picks[:2]:
                    parts.append(jnp.concatenate([rows_at(v, pick) for v in wide8], 1))
            return jnp.concatenate(parts, 0)
        along_c = lax.broadcasted_iota(jnp.int32, (NC, NC1), 0) // 2
        along_l = lax.broadcasted_iota(jnp.int32, (NL1, NL), 1) // 2
        twice_c = jnp.where(along_c == lax.broadcasted_iota(jnp.int32, (NC, NC1), 1), 1.0, 0.0).astype(F32)
        twice_l = jnp.where(along_l == lax.broadcasted_iota(jnp.int32, (NL1, NL), 0), 1.0, 0.0).astype(F32)
        return precise(precise(twice_c, x), twice_l)

    for s, i in enumerate((1, planes)):
        p = whole_fine(sweep(x1, b1, i, 1))
        c, l = around(p, 1)
        sheet[s] = (1.0 - OMEGA) * p + k0 * (coef[0] * p + coef[1] * c + coef[2] * l)

    owned = [patches[r : r + 1, :] for r in range(2)]
    spot = lax.broadcasted_iota(jnp.int32, (8, LANES), 0) * LANES + lane_of((8, LANES))
    spot = spot.astype(F32)
    start = half * C1
    totals = [jnp.zeros((C, LANES), F32) for _ in owned]
    small = [jnp.zeros((8, LANES), F32) for _ in owned]
    for v in range(n_wall):
        wall_s = wall_of(v)
        for j in range(n_len):
            ref = blocks[v * n_len + j]
            at_l = pl.ds(pl.multiple_of(length_of(j) * L, L), L)

            def add(d, carry):
                big, little = carry
                values = sheet[wall_s, pl.ds(pl.multiple_of(blk_of(d) * C, C), C), at_l]
                ids = ref[d, start : start + C, :]
                parts = ref[d, start + C : start + C + 8, :]
                big = [x + jnp.where(ids == e, values, 0.0) for x, e in zip(big, owned)]
                little = [x + jnp.where(spot == e, parts, 0.0) for x, e in zip(little, owned)]
                return big, little

            totals, small = lax.fori_loop(0, n_blk, add, (totals, small), unroll=min(4, n_blk))
    factor = 1.0 / (2.0 * C * L / 2) ** 0.5
    for r in range(2):
        patch_grad[0, r] = (jnp.sum(totals[r]) + jnp.sum(small[r])) * factor
    for copy in copies:
        copy.wait()


def ring(x, axis, by):
    count = lax.axis_size(axis)
    return lax.ppermute(x, axis, [(i, (i + by) % count) for i in range(count)])


def across(x):
    n_wall = lax.axis_size("wall")
    pairs = [(l * n_wall + w, (1 - l) * n_wall + (w + 1) % n_wall) for l in range(2) for w in range(n_wall)]
    return lax.ppermute(x, ("len", "wall"), pairs)


def call(kernel, ins, outs, scratch, name, work=0, room=48):
    places = {"vmem": pltpu.VMEM, "smem": pltpu.SMEM, "any": pl.ANY, "hbm": pltpu.HBM}

    def specs(kinds):
        return [pl.BlockSpec(memory_space=places[kind]) for kind in kinds]

    cost = pl.CostEstimate(flops=work, bytes_accessed=work, transcendentals=0) if work else None
    return pl.pallas_call(
        kernel,
        out_shape=[jax.ShapeDtypeStruct(shape, F32) for shape, _ in outs],
        in_specs=specs(ins),
        out_specs=specs(kind for _, kind in outs),
        scratch_shapes=[pltpu.VMEM(shape, F32) if isinstance(shape, tuple) else shape for shape in scratch],
        compiler_params=pltpu.CompilerParams(vmem_limit_bytes=int(room * 2**20)),
        cost_estimate=cost,
        name=name,
    )


def body(adj_next, ion_slope, misfit, tissue_mask, patch_ids, owner_map):
    W, C, L = adj_next.shape
    n_blk, n_len, n_wall = lax.axis_size("blk"), lax.axis_size("len"), lax.axis_size("wall")
    electrodes = owner_map.shape[0]
    assert L == LANES and H * W == LANES and n_wall == 2 and electrodes == 2 * n_blk * n_len * n_wall
    N = W + 2 * H
    n_dir = 1 if n_len == 2 else 2
    cells = W * C
    vmem = "vmem"
    field, own = (N * C, L), (cells, L)
    raw = [x.reshape(cells, L) for x in (adj_next, ion_slope, tissue_mask, misfit)]

    *fields, wall_out = (faces := call(
        functools.partial(pack_faces, n_len),
        ["hbm"] * 4,
        [(own, vmem)] * 4
        + [((sum(FACES), C, L), vmem)]
        + [((4, C, L), vmem)] * n_dir
        + [((C, L), vmem)] * n_dir,
        [pltpu.VMEM(own, jnp.int32), pltpu.SemaphoreType.DMA((4, 2))],
        "faces",
        room=52.75,
    )(*raw))[:5]
    strip_out, corner_out = faces[5 : 5 + n_dir], faces[5 + n_dir :]
    wall_in = ring(wall_out, "wall", 1)
    if n_dir == 1:
        strips = [ring(strip_out[0], "len", 1)]
        corners = [across(corner_out[0])]
    else:
        strips = [ring(strip_out[1], "len", -1), ring(strip_out[0], "len", 1)]
        corners = [ring(ring(corner_out[1], "wall", 1), "len", -1), ring(ring(corner_out[0], "wall", 1), "len", 1)]

    near = (sum(near_rows(n_dir, W)[-1][::2]), L)
    halos = [wall_in, *strips, *corners]
    to_next, to_prev, own_rows = call(
        functools.partial(boundary, n_len, C),
        [vmem] * (5 + 2 * n_dir),
        [(near, vmem)] * 2 + [((2, 6, N, L), vmem)],
        [(48, N, L)],
        "boundary",
    )(*fields, *halos)
    from_next = ring(to_prev, "blk", -1)
    from_prev = ring(to_next, "blk", 1)
    qm, bm, be, coarse, surface = call(
        functools.partial(sector, n_len, n_wall, C),
        [vmem] * (5 + 2 * n_dir),
        [(field, vmem)] * 3 + [((cells // 8, L), vmem), ((C, L), vmem)],
        [field, (cells // 2, L)] + [field] * 8,
        "sector",
        work=16 * 10**6,
    )(*fields, *halos)

    rows = (8, N, L)
    wide = LANES * ((electrodes + LANES - 1) // LANES)
    message = (cells // 8 + C + 8, L)
    rows_n, rows_p, mine = call(
        functools.partial(correct, electrodes, n_len, n_wall),
        [vmem] * 6,
        [(rows, vmem), (rows, vmem), (message, vmem)],
        [(1, N, L), (wide, L)],
        "correct",
    )(own_rows, from_next, from_prev, coarse, surface, patch_ids)

    relative = False
    moved = [ring(mine, "blk", d) for d in range(1, n_blk)] if relative else [lax.all_gather(mine, "blk")]
    base_adj, base_pot, patches = call(
        functools.partial(source_part, n_blk, n_len, n_wall, C, electrodes),
        [vmem] * 7,
        [(own, vmem), (own, vmem), ((8, L), vmem)],
        [field] * 4 + [(2, N, L)],
        "source_part",
        work=12 * 10**6,
    )(bm, be, rows_n, rows_p, qm, fields[2], owner_map.reshape(1, electrodes))
    sector_blocks = jnp.stack([mine] + moved) if relative else moved[0]
    if n_len == 2:
        here = [sector_blocks, ring(sector_blocks, "len", 1)]
        here[1], base_adj = lax.optimization_barrier((here[1], base_adj))
    else:
        gathered = lax.all_gather(sector_blocks, "len")
        here = [gathered[j] for j in range(n_len)]
    blocks = here + [ring(x, "wall", 1) for x in here]

    NC1, NL1 = n_blk * C // 2, n_len * L // 2
    planes = n_wall * W // 2
    grids = [(planes // k + 2, NC1, NL1) for k in (1, 1, 2, 2, 4, 4)]
    Q = W // 2 + 2
    tall = (Q * (C + 8), L)
    taller = ((W + 2) * (C + 8), L)
    scratch = grids + [(Q * C, NL1), tall, tall, taller, own, own, own]
    scratch += [(2, n_blk * C, n_len * L), pltpu.SemaphoreType.DMA((2, 2))]
    adj_prev, potential, patch_grad = call(
        functools.partial(solve, (n_blk, n_len, n_wall), relative, C, W),
        [vmem] * (len(blocks) + 4),
        [(own, "any"), (own, "any"), ((1, 2), "smem")],
        scratch,
        "solve",
        room=48 if NC1 * NL1 <= 4096 else 58,
    )(*blocks, base_adj, base_pot, fields[2], patches)
    return adj_prev.reshape(W, C, L), potential.reshape(W, C, L), patch_grad


def solution(mesh):
    field = P(("groups", "wall"), "blk", "len")
    return jax.shard_map(
        body,
        mesh=mesh,
        in_specs=(field, field, field, field, field, P("groups")),
        out_specs=(field, field, P(("groups", "blk", "len", "wall"), None)),
        check_vma=False,
    )
```

```python
import functools

import jax
import jax.numpy as jnp
from jax import lax
from jax.experimental import pallas as pl
from jax.experimental.pallas import tpu as pltpu
from jax.sharding import PartitionSpec as P

SI = (0.6, 1.0, 3.0)
SE = (0.8, 1.2, 2.0)
SHIFT = 0.002
OMEGA = 0.8
DT = 0.1
H = 4
LANES = 128
HIGHEST = lax.Precision.HIGHEST
F32 = jnp.float32


def level_coef(level):
    return tuple((SI[i] + SE[i]) / 4.0**level for i in range(3))


def level_diag(level):
    return SHIFT + 2.0 * sum(level_coef(level))


def level_step(level):
    return OMEGA / level_diag(level)


def lane_of(shape):
    return lax.broadcasted_iota(jnp.int32, shape, len(shape) - 1)


def before(m, e):
    first = lane_of(m.shape) == 0
    rm, re = pltpu.roll(m, 1, 1), pltpu.roll(e, 1, 1)
    return jnp.where(first, re, rm), jnp.where(first, rm, re)


def after(m, e):
    last = lane_of(m.shape) == LANES - 1
    rm, re = pltpu.roll(m, LANES - 1, 1), pltpu.roll(e, LANES - 1, 1)
    return jnp.where(last, re, rm), jnp.where(last, rm, re)


def beside_lanes(m, e):
    bm, be = before(m, e)
    am, ae = after(m, e)
    return bm + am, be + ae


def beside_lanes_main(m, e):
    lane = lane_of(m.shape)
    ends = lanes_at(e, LANES - 1 - lane)
    left = jnp.where(lane == 0, ends, pltpu.roll(m, 1, 1))
    right = jnp.where(lane == LANES - 1, ends, pltpu.roll(m, LANES - 1, 1))
    return left + right


def beside_rows(x, row_before, row_after):
    rows = x.shape[0]
    row = lax.broadcasted_iota(jnp.int32, x.shape, 0)
    low = jnp.where(row == 0, row_before, pltpu.roll(x, 1, 0))
    high = jnp.where(row == rows - 1, row_after, pltpu.roll(x, rows - 1, 0))
    return low + high


def beside_dense(x):
    return pltpu.roll(x, 1, 0) + pltpu.roll(x, x.shape[0] - 1, 0)


def plane(ref, i, rows):
    return ref[pl.ds(pl.multiple_of(i * rows, rows), rows), :]


def set_plane(ref, i, rows, value):
    ref[pl.ds(pl.multiple_of(i * rows, rows), rows), :] = value


def loop(low, high, step, unroll):
    def wrapped(i, carry):
        step(i)
        return carry

    lax.fori_loop(low, high, wrapped, 0, unroll=min(unroll, high - low))


FACES = (H, H - 1, H - 1, H - 2)


def face_planes(array):
    return FACES[array], sum(FACES[:array])


def pack_faces(n_len, adj, ion, mask, mis, *rest):
    n_dir = 1 if n_len == 2 else 2
    fields, wall_out, rest = rest[:4], rest[4], rest[5:]
    strips, corners = rest[:n_dir], rest[n_dir : 2 * n_dir]
    whole_mask, sems = rest[2 * n_dir :]
    cells = adj.shape[0]
    C = wall_out.shape[1]
    W = cells // C
    wall, length = lax.axis_index("wall"), lax.axis_index("len")
    targets = (fields[0], fields[1], whole_mask, fields[3])
    copies = []
    for a, (src, dst) in enumerate(zip((adj, ion, mask, mis), targets)):
        part = cells // 2
        for k in range(2):
            spot = pl.ds(k * part, part)
            copies.append(pltpu.make_async_copy(src.at[spot], dst.at[spot], sems.at[a, k]))
            copies[-1].start()

    base = jnp.where(wall == 0, W - H, 0)
    group = lane_of((C, LANES)) // H
    turns = [jnp.where(length == 0, H, 0)] if n_dir == 1 else [H, 0]
    corner = [jnp.zeros((C, LANES), F32) for _ in range(n_dir)]
    for a in (0, 1, 3, 2):
        copies[2 * a].wait()
        copies[2 * a + 1].wait()
        if a == 2:
            fields[2][...] = whole_mask[...].astype(F32)
        ref = fields[a]
        strip = [jnp.zeros((C, LANES), F32) for _ in range(n_dir)]
        for w in range(W):
            value = ref[w * C : (w + 1) * C, :]
            for d in range(n_dir):
                turned = pltpu.roll(value, lax.rem(H * w + turns[d], LANES), 1)
                strip[d] = jnp.where(group == w, turned, strip[d])
        for d in range(n_dir):
            strips[d][a] = strip[d]
        count, first = face_planes(a)
        for p in range(count):
            face = plane(ref, base + jnp.where(wall == 0, H - count, 0) + p, C)
            wall_out[first + p] = face
            slot = first + p
            for d in range(n_dir):
                turned = pltpu.roll(face, lax.rem(H * slot + turns[d], LANES), 1)
                corner[d] = jnp.where(group == slot, turned, corner[d])
    for d in range(n_dir):
        corners[d][...] = corner[d]


def dense(ref, row, N, C):
    return ref[pl.ds(row, N, stride=C), :]


def dense_pair(m, e, row, N, C):
    return dense(m, row, N, C), dense(e, row, N, C)


def dense_apply(pair, inner, outer, coef):
    m, e = pair
    lm, le = beside_lanes(m, e)
    double = 2.0 * sum(coef)
    out = [double * m - coef[0] * beside_dense(m) - coef[2] * lm, double * e - coef[0] * beside_dense(e) - coef[2] * le]
    for row in (inner, outer):
        if row is not None:
            out = [out[k] - coef[1] * row[k] for k in range(2)]
    return out


def near_rows(n_dir, W):
    start, places = 8 * n_dir, []
    for reach in (0, 1, 2, 2, 3):
        places.append((start, H - reach, W + 2 * reach))
        start += W + 2 * reach
    assert start % 8 == 0
    return places


def rim_tiles(values):
    return [value[s : s + 8] for value in values for s in range(0, value.shape[0], 8)]


def rim_places(n_len, length):
    if n_len == 2:
        return [(jnp.where(length == 0, 0, LANES - H), True)]
    return [(0, length < n_len - 1), (LANES - H, length > 0)]


def boundary(n_len, C, *refs):
    n_dir = 1 if n_len == 2 else 2
    raw, wall_in, refs = refs[:4], refs[4], refs[5:]
    strips, corners, refs = refs[:n_dir], refs[n_dir : 2 * n_dir], refs[2 * n_dir :]
    to_next, to_prev, own_rows, build = refs
    W = raw[0].shape[0] // C
    N = W + 2 * H
    wall, length = lax.axis_index("wall"), lax.axis_index("len")
    places = rim_places(n_len, length)

    def strip_rows(packed, first, count):
        lane, k = lane_of((count, LANES)), lax.broadcasted_iota(jnp.int32, (count, LANES), 0)
        out = jnp.zeros((count, LANES), F32)
        for row, (off, ok) in zip(packed, places):
            j = lax.rem(lane - off + LANES, LANES)
            index = jnp.clip(H * (first + k) + j, 0, LANES - 1)
            taken = lanes_at(jnp.broadcast_to(row, (count, LANES)), index)
            out = jnp.where(jnp.logical_and(j < H, ok), taken, out)
        return out

    slots = iter(range(build.shape[0]))

    def assembled(own, halo, count):
        ref = build.at[next(slots)]
        ref[0:8, :] = jnp.zeros((8, LANES), F32)
        ref[N - 8 : N, :] = jnp.zeros((8, LANES), F32)
        ref[H : H + W, :] = own
        ref[H - count : H, :] = jnp.where(wall == 0, 0.0, halo)
        ref[H + W : H + W + count, :] = jnp.where(wall == 0, halo, 0.0)
        return ref[...]

    def row_of(a, r):
        count, first = face_planes(a)
        halo = jnp.concatenate([wall_in[first + p, r : r + 1, :] for p in range(count)], 0)
        m = assembled(raw[a][pl.ds(r, W, stride=C), :], halo, count)
        own = strip_rows([strip[a, r : r + 1, :] for strip in strips], 0, W)
        halo = strip_rows([corner[r : r + 1, :] for corner in corners], first, 8)[:count]
        return m, assembled(own, halo, count)

    length_shift = jnp.where(length == 0, 0, H) if n_dir == 1 else H
    group = lane_of((8, LANES)) // (H * n_dir)
    for side, (out, order) in enumerate(((to_next, (C - 1, C - 2, C - 3, C - 4)), (to_prev, (0, 1, 2, 3)))):
        adj = [row_of(0, r) for r in order]
        mask = [row_of(2, r) for r in order[:3]]
        q = []
        for k in range(3):
            ion = row_of(1, order[k])
            moved = dense_apply(adj[k], adj[k + 1], adj[k - 1] if k else None, SI)
            q.append([adj[k][j] - DT * mask[k][j] * (moved[j] + ion[j] * adj[k][j]) for j in range(2)])
        near = dense_apply(q[0], q[1], None, SI)
        mis = row_of(3, order[0])
        near = [near[j] + mis[j] for j in range(2)]
        second = dense_apply(q[1], q[2], q[0], SI)[0] + row_of(3, order[1])[0]
        for value, (start, first, count) in zip((second, near[0], q[0][0], mask[0][0], adj[0][0]), near_rows(n_dir, W)):
            out[start : start + count, :] = value[first : first + count]
        packs = [jnp.zeros((8, LANES), F32) for _ in range(n_dir)]
        for t, tile in enumerate(rim_tiles((near[1], q[0][1], mask[0][1], adj[0][1]))):
            k, at = divmod(t, LANES // (H * n_dir))
            turned = pltpu.roll(tile, lax.rem(length_shift + H * n_dir * at, LANES), 1)
            packs[k] = jnp.where(group == at, turned, packs[k])
        for k in range(n_dir):
            out[8 * k : 8 * k + 8, :] = packs[k]
        for k, pair in enumerate((adj[0], mask[0], q[0])):
            own_rows[side, 2 * k] = pair[0]
            own_rows[side, 2 * k + 1] = pair[1]


def spots(m_ref, e_ref, i, rows, coef):
    m, e = plane(m_ref, i, rows), plane(e_ref, i, rows)
    wm = plane(m_ref, i - 1, rows) + plane(m_ref, i + 1, rows)
    we = plane(e_ref, i - 1, rows) + plane(e_ref, i + 1, rows)
    lm, le = beside_lanes(m, e)
    cm, ce = beside_rows(m, 0.0, 0.0), beside_rows(e, 0.0, 0.0)
    double = 2.0 * sum(coef)
    dm = double * m - coef[0] * wm - coef[1] * cm - coef[2] * lm
    de = double * e - coef[0] * we - coef[1] * ce - coef[2] * le
    return m, e, dm, de


def rim_lanes(lane, length, n_len):
    return jnp.logical_or(
        jnp.logical_and(lane < H, length < n_len - 1),
        jnp.logical_and(lane >= LANES - H, length > 0),
    )


def inside(i, wall, W, n_wall):
    w = wall * W + i - H
    return jnp.logical_and(w >= 0, w < n_wall * W)


def lanes_at(x, index):
    return jnp.take_along_axis(x, index, axis=1, mode="promise_in_bounds")


def rows_at(x, index):
    return jnp.take_along_axis(x, index, axis=0, mode="promise_in_bounds")


def halved(low, high):
    lane = lane_of(low.shape)
    even = 2 * lane % LANES
    pairs = [lanes_at(x, even) + lanes_at(x, even + 1) for x in (low, high)]
    return 0.125 * jnp.where(lane < LANES // 2, pairs[0], pairs[1])


def precise(a, b):
    return jnp.dot(a, b, precision=HIGHEST, preferred_element_type=F32)


def assemble(n_len, C, raw, wall_in, strips, corners, xm, xe):
    W = raw[0].shape[0] // C
    N = W + 2 * H
    wall, length = lax.axis_index("wall"), lax.axis_index("len")
    lane = lane_of((C, LANES))
    places = rim_places(n_len, length)
    seen = [jnp.logical_and(lax.rem(lane - off + LANES, LANES) < H, ok) for off, ok in places]

    def rim(packed, base):
        out = jnp.zeros((C, LANES), F32)
        for row, ok, (off, _) in zip(packed, seen, places):
            out = jnp.where(ok, pltpu.roll(row, lax.rem(off - base + LANES, LANES), 1), out)
        return out

    zero = jnp.zeros((C, LANES), F32)
    last = N - H
    for a, own in enumerate(raw):
        packed = [strip[a] for strip in strips]
        for w in range(W):
            set_plane(xm[a], w + H, C, plane(own, w, C))
            set_plane(xe[a], w + H, C, rim(packed, H * w))
        packed = [corner[...] for corner in corners]
        for i in range(H):
            for at in (i, last + i):
                set_plane(xm[a], at, C, zero)
                set_plane(xe[a], at, C, zero)
        count, first = face_planes(a)
        here = jnp.where(wall == 0, last, H - count)
        for p in range(count):
            set_plane(xm[a], here + p, C, wall_in[first + p])
            set_plane(xe[a], here + p, C, rim(packed, H * (first + p)))


def sector(n_len, n_wall, C, *refs):
    n_dir = 1 if n_len == 2 else 2
    raw, wall_in, refs = refs[:4], refs[4], refs[5:]
    strips, corners, refs = refs[:n_dir], refs[n_dir : 2 * n_dir], refs[2 * n_dir :]
    qm, bm, be, coarse, surface, qe, pairs = refs[:7]
    xm, xe = refs[7:11], refs[11:15]
    assemble(n_len, C, raw, wall_in, strips, corners, xm, xe)
    N = qm.shape[0] // C
    W = N - 2 * H
    wall, length = lax.axis_index("wall"), lax.axis_index("len")
    rim = rim_lanes(lane_of((C, LANES)), length, n_len)
    zero = jnp.zeros((C, LANES), F32)
    for i in (0, N - 1):
        set_plane(qm, i, C, zero)
        set_plane(qe, i, C, zero)
    for i in (0, 1, N - 2, N - 1):
        set_plane(bm, i, C, zero)
        set_plane(be, i, C, zero)

    def parabolic(i):
        m, e, dm, de = spots(xm[0], xe[0], i, C, SI)
        set_plane(qm, i, C, m - DT * plane(xm[2], i, C) * (dm + plane(xm[1], i, C) * m))
        set_plane(qe, i, C, e - DT * plane(xe[2], i, C) * (de + plane(xe[1], i, C) * e))

    loop(1, N - 1, parabolic, 2)

    def elliptic_source(i):
        m, e, dm, de = spots(qm, qe, i, C, SI)
        ok = inside(i, wall, W, n_wall)
        set_plane(bm, i, C, jnp.where(ok, plane(xm[3], i, C) + dm, 0.0))
        set_plane(be, i, C, jnp.where(jnp.logical_and(rim, ok), plane(xe[3], i, C) + de, 0.0))

    loop(2, N - 2, elliptic_source, 2)

    coef, k0 = level_coef(0), level_step(0)

    def left(i):
        m, e = plane(bm, i, C), plane(be, i, C)
        wm = plane(bm, i - 1, C) + plane(bm, i + 1, C)
        cm = beside_rows(m, 0.0, 0.0)
        lm = beside_lanes_main(m, e)
        return m, (1.0 - OMEGA) * m + k0 * (coef[0] * wm + coef[1] * cm + coef[2] * lm)

    def pair(q):
        i = 2 * q + H
        m, first = left(i)
        n, second = left(i + 1)
        set_plane(pairs, q, C, first + second)

        @pl.when(jnp.logical_and(q == 0, wall == 0))
        def _():
            surface[...] = k0 * (m + first)

        @pl.when(jnp.logical_and(q == W // 2 - 1, wall == n_wall - 1))
        def _():
            surface[...] = k0 * (n + second)

    loop(0, W // 2, pair, 2)

    half = W * C // 8
    z = pairs[pl.ds(0, 2 * half, stride=2), :] + pairs[pl.ds(1, 2 * half, stride=2), :]
    coarse[...] = halved(z[:half], z[half:])


def unpacked(ref, n_len, length, N):
    n_dir = 1 if n_len == 2 else 2
    mains = []
    for start, first, count in near_rows(n_dir, N - 2 * H):
        begin = min(start - first, ref.shape[0] - N)
        value = ref[begin : begin + N, :]
        behind = start - first - begin
        mains.append(pltpu.roll(value, N - behind, 0) if behind else value)
    rim = rim_lanes(lane_of((8, LANES)), length, n_len)
    shift = jnp.where(length == 0, 0, H) if n_dir == 1 else H
    rims = []
    for k in range(4):
        parts = []
        for s in range(N // 8):
            pack, at = divmod(k * (N // 8) + s, LANES // (H * n_dir))
            back = lax.rem(2 * LANES - shift - H * n_dir * at, LANES)
            parts.append(jnp.where(rim, pltpu.roll(ref[8 * pack : 8 * pack + 8, :], back, 1), 0.0))
        rims.append(jnp.concatenate(parts, 0))
    second, near, q, mask, adj = mains
    return (adj, rims[3]), (mask, rims[2]), (q, rims[1]), (near, rims[0]), second


def lateral(pair):
    return dense_apply(pair, None, None, SI)


def source_rows(own, other):
    adj_o, mask_o, q_o = own
    adj_n, mask_n, q_n, p_n, second_n = other
    step = DT * SI[1]
    delta_o = [step * mask_o[k] * adj_n[k] for k in range(2)]
    delta_n = [step * mask_n[k] * adj_o[k] for k in range(2)]
    lat_o, lat_n = lateral(delta_o), lateral(delta_n)
    near = [lat_o[k] - SI[1] * (q_n[k] + delta_n[k]) for k in range(2)]
    second = [-SI[1] * delta_o[k] for k in range(2)]
    halo = [p_n[k] + lat_n[k] - SI[1] * (q_o[k] + delta_o[k]) for k in range(2)]
    halo_second = second_n - SI[1] * delta_n[0]
    return near, second, halo, halo_second, delta_o[0]


def correct(electrodes, n_len, n_wall, own_rows, from_next, from_prev, coarse, surface, ids, *rest):
    rows_n, rows_p, message = rest[:3]
    lines, sums = rest[3:]
    _, C, L = ids.shape
    N = own_rows.shape[2]
    W = N - 2 * H
    wall, length = lax.axis_index("wall"), lax.axis_index("len")
    ok_m = inside(lax.broadcasted_iota(jnp.int32, (N, LANES), 0), wall, W, n_wall)
    ok_e = jnp.logical_and(ok_m, rim_lanes(lane_of((N, LANES)), length, n_len))
    coef, k0 = level_coef(0), level_step(0)
    y = surface[...]
    row = lax.broadcasted_iota(jnp.int32, (C, LANES), 0)
    at = pl.ds(jnp.where(wall == 0, H, W + H - 1), 1)
    lows, highs = [], []
    W1, C1 = W // 2, C // 2
    for side, (other, out, order) in enumerate(
        ((from_next, rows_n, (C - 1, C - 2, C - 3)), (from_prev, rows_p, (0, 1, 2)))
    ):
        own = [(own_rows[side, 2 * k], own_rows[side, 2 * k + 1]) for k in range(3)]
        near, second, halo, halo_second, delta = source_rows(own, unpacked(other, n_len, length, N))
        near = [jnp.where(ok_m, near[0], 0.0), jnp.where(ok_e, near[1], 0.0)]
        second = [jnp.where(ok_m, second[0], 0.0), jnp.where(ok_e, second[1], 0.0)]
        out[0] = halo_m = jnp.where(ok_m, halo[0], 0.0)
        out[1] = jnp.where(ok_e, halo[1], 0.0)
        out[2] = jnp.where(ok_m, halo_second, 0.0)
        out[3] = delta
        out[4], out[5] = near
        out[6], out[7] = second

        def turned(pair, beside):
            m, e = pair
            return (1.0 - OMEGA) * m + k0 * (
                coef[0] * beside_dense(m) + coef[2] * beside_lanes_main(m, e) + coef[1] * beside
            )

        first = turned(near, second[0] + halo_m)
        next_one = turned(second, near[0])
        third = k0 * coef[1] * second[0]
        for k, change in enumerate((near[0] + first, second[0] + next_one, third)):
            lines[0] = change
            y = y + jnp.where(row == order[k], k0 * lines[0, at, :], 0.0)
        for change in (first + next_one, third):
            lines[0] = change
            both = lines[0, pl.ds(H, W1, stride=2), :] + lines[0, pl.ds(H + 1, W1, stride=2), :]
            lows.append(both[: W1 // 2])
            highs.append(both[W1 // 2 :])
    add = halved(jnp.concatenate(lows, 0), jnp.concatenate(highs, 0))
    half = W * C // 8
    message[0:half, :] = coarse[...]
    for k, c1 in enumerate((C1 - 1, C1 - 2, 0, 1)):
        spot = pl.ds(c1, W1 // 2, stride=C1)
        message[spot, :] = message[spot, :] + add[k * (W1 // 2) : (k + 1) * (W1 // 2)]
    patch = ids[0]
    message[half : half + C, :] = patch.astype(F32)
    wide = sums.shape[0]
    if wide > electrodes:
        sums[...] = jnp.zeros(sums.shape, F32)

    def one(e):
        sums[pl.ds(e, 1), :] = jnp.sum(jnp.where(patch == e, y, 0.0), axis=0, keepdims=True)

    loop(0, electrodes, one, 8)
    totals = lax.dot_general(
        jnp.ones((8, LANES), F32), sums[...], (((1,), (1,)), ((), ())), precision=HIGHEST, preferred_element_type=F32
    )
    message[half + C : half + C + 8, :] = jnp.zeros((8, LANES), F32)
    for t in range(wide // LANES):
        message[half + C + t : half + C + t + 1, :] = totals[0:1, t * LANES : (t + 1) * LANES]


def source_part(n_blk, n_len, n_wall, C, electrodes, bm, be, rows_n, rows_p, qm, mask, owner, base_adj, base_pot, *rest):
    patches, fm, fe, tm, te, hp = rest
    N = bm.shape[0] // C
    W = N - 2 * H
    blk, length, wall = lax.axis_index("blk"), lax.axis_index("len"), lax.axis_index("wall")
    fm[...] = bm[...]
    fe[...] = be[...]
    for rows, near, second in ((rows_n, C - 1, C - 2), (rows_p, 0, 1)):
        for k, at in ((4, near), (6, second)):
            spot = pl.ds(at, N, stride=C)
            fm[spot, :] = fm[spot, :] + rows[k]
            fe[spot, :] = fe[spot, :] + rows[k + 1]
    coef, k0 = level_coef(0), level_step(0)
    rim = rim_lanes(lane_of((C, LANES)), length, n_len)

    def part(i):
        m, e = plane(fm, i, C), plane(fe, i, C)
        wm = plane(fm, i - 1, C) + plane(fm, i + 1, C)
        we = plane(fe, i - 1, C) + plane(fe, i + 1, C)
        lm, le = beside_lanes(m, e)
        at = pl.ds(i, 1)
        cm = beside_rows(m, rows_p[0, at, :], rows_n[0, at, :])
        ce = beside_rows(e, rows_p[1, at, :], rows_n[1, at, :])
        pm = k0 * ((2.0 - OMEGA) * m + k0 * (coef[0] * wm + coef[1] * cm + coef[2] * lm))
        pe = k0 * ((2.0 - OMEGA) * e + k0 * (coef[0] * we + coef[1] * ce + coef[2] * le))
        set_plane(tm, i, C, jnp.where(inside(i, wall, W, n_wall), pm, 0.0))
        set_plane(te, i, C, jnp.where(rim, pe, 0.0))

    loop(H - 1, N - H + 1, part, 2)
    for side, (rows, at) in enumerate(((rows_n, C - 1), (rows_p, 0))):
        m = rows[0]
        total = (
            coef[0] * beside_dense(m)
            + coef[1] * (rows[2] + dense(fm, at, N, C))
            + coef[2] * beside_lanes_main(m, rows[1])
        )
        hp[side] = k0 * ((2.0 - OMEGA) * m + k0 * total)
    row = lax.broadcasted_iota(jnp.int32, (C, LANES), 0)

    def finish(w):
        i = w + H
        m, e = plane(tm, i, C), plane(te, i, C)
        at = pl.ds(i, 1)
        wm = plane(tm, i - 1, C) + plane(tm, i + 1, C)
        cm = beside_rows(m, hp[1, at, :], hp[0, at, :])
        lm = beside_lanes_main(m, e)
        lam = plane(qm, i, C)
        lam = lam + jnp.where(row == C - 1, rows_n[3, at, :], 0.0) + jnp.where(row == 0, rows_p[3, at, :], 0.0)
        moved = 2.0 * sum(SI) * m - SI[0] * wm - SI[1] * cm - SI[2] * lm
        set_plane(base_adj, w, C, lam - DT * plane(mask, w, C) * moved)
        set_plane(base_pot, w, C, m)

    loop(0, W, finish, 2)

    me = (blk * n_len + length) * n_wall + wall
    which = lax.broadcasted_iota(jnp.int32, (1, electrodes), 1).astype(F32)
    mine = owner[...] == me
    patches[0:1, :] = jnp.full((1, LANES), jnp.min(jnp.where(mine, which, float(electrodes))))
    patches[1:2, :] = jnp.full((1, LANES), jnp.max(jnp.where(mine, which, -1.0)))
    patches[2:8, :] = jnp.zeros((6, LANES), F32)


def halves(shape):
    lane = lane_of(shape)
    return lane, lane % (LANES // 2)


def compact(C, W, blocks, out, sheet1, coarse2):
    n_blk = blocks.shape[0]
    W1, C1 = W // 2, C // 2
    half, start, middle = W1 // 2, W1 // 2 * C1, LANES // 2
    blk, length, wall = lax.axis_index("blk"), lax.axis_index("len"), lax.axis_index("wall")
    sums = jnp.zeros((8, LANES), F32)
    for d in range(n_blk):
        b = lax.rem(blk - d + n_blk, n_blk)
        for i in range(half):
            sheet1[i, pl.ds(pl.multiple_of(C1 * b, C1), C1), :] = blocks[d, i * C1 : (i + 1) * C1, :]
        out[pl.ds(pl.multiple_of(96 + C * b, C), C), :] = blocks[d, start : start + C, :]
        sums = sums + blocks[d, start + C : start + C + 8, :]
    out[160:168, :] = sums
    NC1 = sheet1.shape[1]
    lane, at = halves((NC1, LANES))
    low = lane < middle
    coef, k1 = level_coef(1), level_step(1)
    ends = pltpu.roll(sheet1[half - 1], middle, 1), pltpu.roll(sheet1[0], middle, 1)
    for q in range(half // 2):
        both = sheet1[2 * q] + sheet1[2 * q + 1]
        prev = sheet1[2 * q - 1] if q else jnp.where(low, 0.0, ends[0])
        after_it = sheet1[2 * q + 2] if 2 * q + 2 < half else jnp.where(low, ends[1], 0.0)
        c = pltpu.roll(both, 1, 0) + pltpu.roll(both, NC1 - 1, 0)
        l = jnp.where(at == 0, 0.0, pltpu.roll(both, 1, 1)) + jnp.where(
            at == middle - 1, 0.0, pltpu.roll(both, LANES - 1, 1)
        )
        left = (1.0 - OMEGA) * both + k1 * (coef[0] * (prev + both + after_it) + coef[1] * c + coef[2] * l)
        coarse2[q] = 0.125 * twins(left, 1)
    coarse2[half // 2] = 0.125 * twins(jnp.where(wall == 0, sheet1[half - 1], sheet1[0]), 1)
    rows2 = NC1 // 2
    lane2, at2 = halves((rows2, LANES))
    pick = lane2 - at2 + 2 * (at2 % (middle // 2))
    for p in range(half // 4):
        pair = [lanes_at(coarse2[2 * p + k, pl.ds(0, rows2, stride=2), :], pick) for k in range(2)]
        out[rows2 * p : rows2 * (p + 1), :] = jnp.where(at2 < middle // 2, pair[0], pair[1])
    beside = jnp.zeros((NC1, LANES), F32)
    base = jnp.where(length == 0, middle - H, 0)
    for i in range(half):
        turned = pltpu.roll(sheet1[i], lax.rem(H * i - base + LANES, LANES), 1)
        beside = jnp.where(at // H == i, turned, beside)
    out[32 : 32 + NC1, :] = beside
    face = coarse2[half // 2, pl.ds(0, rows2, stride=2), :]
    face = lanes_at(face, jnp.where(wall == 0, middle, 0) + 2 * (at2 % (middle // 2)))
    inner = jnp.logical_and(lane2 >= middle // 2, lane2 < middle)
    out[32 : 32 + rows2, :] = jnp.where(inner, face, beside[:rows2])
    inner_surface = jnp.where(low, sheet1[0], pltpu.roll(sheet1[1], middle, 1))
    outer_surface = jnp.where(low, pltpu.roll(sheet1[half - 2], middle, 1), sheet1[half - 1])
    out[64 : 64 + NC1, :] = jnp.where(wall == 0, inner_surface, outer_surface)


def around(x, by):
    rows, lanes = x.shape
    lane = lane_of(x.shape)
    c = pltpu.roll(x, by, 0) + pltpu.roll(x, rows - by, 0)
    l = jnp.where(lane < by, 0.0, pltpu.roll(x, by, 1)) + jnp.where(
        lane >= lanes - by, 0.0, pltpu.roll(x, lanes - by, 1)
    )
    return c, l


def twins(x, by):
    rows, lanes = x.shape
    if lanes == LANES:
        index = lax.broadcasted_iota(jnp.int32, (8, LANES), 0) ^ by
        x = x + jnp.concatenate([rows_at(x[t : t + 8], index) for t in range(0, rows, 8)], 0)
        return x + lanes_at(x, lane_of(x.shape) ^ by)
    row = lax.broadcasted_iota(jnp.int32, x.shape, 0)
    lane = lane_of(x.shape)
    x = x + jnp.where((row & by) == 0, pltpu.roll(x, rows - by, 0), pltpu.roll(x, by, 0))
    return x + jnp.where((lane & by) == 0, pltpu.roll(x, lanes - by, 1), pltpu.roll(x, by, 1))


def solve(sizes, relative, compacted, C, W, *refs):
    n_blk, n_len, n_wall = sizes
    count = n_len * n_wall
    blocks, refs = refs[:count], refs[count:]
    base_adj, base_pot, mask, patches, adj_prev, potential, patch_grad = refs[:7]
    b1, x1, b2, x2, b3, x3, near, pm, pe, tm, te, adj_out, pot_out, sheet, both_walls, sems = refs[7:]
    L = LANES
    W1, C1 = W // 2, C // 2
    planes, NC1, NL1 = b1.shape
    planes -= 2
    blk, length, wall = lax.axis_index("blk"), lax.axis_index("len"), lax.axis_index("wall")
    half = W1 // 2
    middle = LANES // 2
    lane8 = lane_of((C1, LANES))
    often = 8 if NC1 * NL1 <= 4096 else 1

    def blk_of(d):
        return lax.rem(blk - d + n_blk, n_blk) if relative else d

    def length_of(j):
        return (length + j) % n_len if n_len == 2 else j

    def wall_of(v):
        return (wall + v) % n_wall

    zero1 = jnp.zeros((NC1, NL1), F32)
    for ref in (b1, x1, b2, x2, b3, x3):
        ref[0] = zero1
        ref[ref.shape[0] - 1] = zero1

    if not compacted:
        for v in range(n_wall):
            wall_s = wall_of(v)
            mine = blocks[v * n_len : (v + 1) * n_len]

            def unpack(d):
                at = pl.ds(pl.multiple_of(C1 * blk_of(d), C1), C1)
                for t in range(n_len // 2):
                    one, two = mine[2 * t], mine[2 * t + 1]
                    for i in range(half):
                        a, b = one[d, i * C1 : (i + 1) * C1, :], two[d, i * C1 : (i + 1) * C1, :]
                        if n_len == 2:
                            a, b = jnp.where(length == 0, a, b), jnp.where(length == 0, b, a)
                        spot = 1 + wall_s * W1 + i
                        lanes = slice(t * LANES, (t + 1) * LANES)
                        b1[spot, at, lanes] = jnp.where(lane8 < middle, a, pltpu.roll(b, middle, 1))
                        b1[spot + half, at, lanes] = jnp.where(lane8 < middle, pltpu.roll(a, middle, 1), b)

            loop(0, n_blk, unpack, 4)
    if compacted:
        lane8 = lane_of((C1, LANES))
        here8 = lane8 // middle == length
        face_lane = jnp.where(length == 0, middle, middle - H)
        near8 = jnp.logical_and(lane8 >= face_lane, lane8 < face_lane + H)
        for v in range(n_wall):
            wall_s = wall_of(v)
            own, other = blocks[2 * v], blocks[2 * v + 1]
            for d in range(n_blk):
                row = pl.multiple_of(C1 * blk_of(d), C1)
                at = pl.ds(row, C1)
                beside = other[pl.ds(32 + row, C1), :]
                for i in range(half):
                    a = own[d, i * C1 : (i + 1) * C1, :]
                    b = pltpu.roll(a, middle, 1)
                    for k, value in enumerate((jnp.where(length == 0, a, b), jnp.where(length == 0, b, a))):
                        turn = lax.rem(face_lane - H * i - middle * k + 2 * LANES, LANES)
                        rest = jnp.where(near8, pltpu.roll(beside, turn, 1), 0.0)
                        b1[1 + wall_s * W1 + i + half * k, at, :] = jnp.where(here8, value, rest)
            surface = other[64 : 64 + NC1, :]
            turned = pltpu.roll(surface, middle, 1)
            spot = jnp.where(wall_s == 0, 1, planes - 1)
            here = lane_of((NC1, LANES)) // middle == length
            b1[spot] = jnp.where(here, b1[spot], jnp.where(length == 0, turned, surface))
            b1[spot + 1] = jnp.where(here, b1[spot + 1], jnp.where(length == 0, surface, turned))
        for k in range(2):
            both_walls[k] = jnp.where(wall == k, blocks[1][0:48, :], blocks[3][0:48, :])
        tile_lane8 = lane_of((8, LANES)) % middle // 2
        row_of_8 = lax.broadcasted_iota(jnp.int32, (8, LANES), 0) // 2

        def widened(w, first, t, lane):
            tile = both_walls[w, first + 8 * (t // 2) : first + 8 * (t // 2) + 8, :]
            return lanes_at(rows_at(tile, 4 * (t % 2) + row_of_8), lane + tile_lane8)

        for w2 in range(planes // 2):
            w, q = divmod(w2, half)
            high, q = divmod(q, half // 2)
            for t in range(NC1 // 8):
                value = widened(w, NC1 // 2 * (q // 2), t, middle // 2 * (q % 2) + middle * high)
                if w2 in (half - 1, half):
                    value = value + level_step(1) * level_coef(1)[0] * widened(1 - w, 32, t, middle // 2)
                b2[1 + w2, 8 * t : 8 * t + 8, :] = value

    def total_of(x, wsum, level, by):
        coef = level_coef(level)
        c, l = around(x, by)
        return level_step(level) * (coef[0] * wsum + coef[1] * c + coef[2] * l)

    def left_pair(ref, i, level):
        both = ref[i] + ref[i + 1]
        return (1.0 - OMEGA) * both + total_of(both, ref[i - 1] + both + ref[i + 2], level, 2 ** (level - 1))

    def sweep(x_ref, b_ref, i, level):
        x = x_ref[i]
        total = total_of(x, x_ref[i - 1] + x_ref[i + 1], level, 2 ** (level - 1))
        return (1.0 - OMEGA) * x + level_step(level) * b_ref[i] + total

    lane1 = lane_of((NC1, NL1))
    exact = jnp.logical_or(lane1 // middle == length, lane1 // 2 == jnp.where(length == 0, middle // 2, middle // 2 - 1))

    def down1(q):
        value = 0.125 * twins(left_pair(b1, 2 * q + 1, 1), 1)
        b2[1 + q] = jnp.where(exact, value, b2[1 + q]) if compacted else value

    loop(0, planes // 2, down1, often)

    def down2(q):
        b3[1 + q] = 0.125 * twins(left_pair(b2, 2 * q + 1, 2), 2)

    loop(0, planes // 4, down2, often)

    deep = planes // 4
    k3 = level_step(3)

    x2[1 + deep] = zero1

    def start3(q):
        b = b3[1 + q]
        x2[1 + q] = k3 * ((2.0 - OMEGA) * b + total_of(b, b3[q] + b3[2 + q], 3, 4))

    loop(0, deep, start3, often)

    def sweep3(q):
        x3[1 + q] = sweep(x2, b3, 1 + q, 3)

    loop(0, deep, sweep3, often)
    k2 = level_step(2)

    def up2(q):
        coarse = x3[1 + q]
        x2[1 + 2 * q] = k2 * b2[1 + 2 * q] + coarse
        x2[2 + 2 * q] = k2 * b2[2 + 2 * q] + coarse

    loop(0, planes // 4, up2, often)

    k1 = level_step(1)

    def up1(q):
        fine = sweep(x2, b2, 1 + q, 2)
        x1[1 + 2 * q] = k1 * b1[1 + 2 * q] + fine
        x1[2 + 2 * q] = k1 * b1[2 + 2 * q] + fine

    loop(0, planes // 2, up1, often)

    Q = W1 + 2
    sectors = (blk, lax.rem(blk + 1, n_blk), lax.rem(blk + n_blk - 1, n_blk))
    spots3 = [pl.ds(pl.multiple_of(s * C1, C1), C1) for s in sectors]
    row8 = lax.broadcasted_iota(jnp.int32, (C1, NL1), 0)

    def three(ref, i):
        return jnp.concatenate([ref[i, s, :] for s in spots3], 0)

    def finish1(q):
        i = wall * W1 + q
        x = three(x1, i)
        wsum = three(x1, jnp.maximum(i - 1, 0)) + three(x1, jnp.minimum(i + 1, planes + 1))
        value = (1.0 - OMEGA) * x + k1 * three(b1, i) + total_of(x, wsum, 1, 1)
        value = jnp.where(jnp.logical_and(i >= 1, i <= planes), value, 0.0)
        set_plane(near, 2 * q, C1, value[:C1])
        set_plane(near, 2 * q + 1, C1, jnp.where(row8 < 2, value[C1 : 2 * C1], value[2 * C1 :]))

    loop(0, Q, finish1, min(often, 6))

    first = length * middle
    R = C + 8
    row8 = lax.broadcasted_iota(jnp.int32, (8, LANES), 0)
    tile_lane = lane_of((8, LANES))
    at_e = jnp.where(tile_lane < H, middle + tile_lane // 2, tile_lane // 2 - middle)
    rim8 = rim_lanes(tile_lane, length, n_len)
    if NL1 == LANES:
        index_m, index_e = first + tile_lane // 2, jnp.clip(first + at_e, 0, LANES - 1)

        def spread(tile):
            return lanes_at(tile, index_m), jnp.where(rim8, lanes_at(tile, index_e), 0.0)

    else:
        source = lax.broadcasted_iota(jnp.int32, (NL1, LANES), 0)
        lane = lane_of((NL1, LANES))
        at_all = jnp.where(lane < H, middle + lane // 2, jnp.where(lane >= LANES - H, lane // 2 - middle, 4 * NL1))
        take_m = jnp.where(source == first + lane // 2, 1.0, 0.0).astype(F32)
        take_e = jnp.where(source == first + at_all, 1.0, 0.0).astype(F32)

        def spread(tile):
            return precise(tile, take_m), precise(tile, take_e)

    picks = (row8 // 2, H + row8 // 2, jnp.where(row8 < H, row8 // 2, H + row8 // 2))

    def fine_rows(q):
        own = spread(plane(near, 2 * q, C1))
        beside = spread(plane(near, 2 * q + 1, C1))
        for out, a, b in ((pm, own[0], beside[0]), (pe, own[1], beside[1])):
            parts = (rows_at(a, picks[0]), rows_at(a, picks[1]), rows_at(b, picks[2]))
            set_plane(out, q, R, jnp.concatenate(parts, 0))

    loop(0, Q, fine_rows, min(often, 6))
    coef, k0 = level_coef(0), level_step(0)
    rim = rim_lanes(lane_of((C, LANES)), length, n_len)

    def rows_beside(x):
        return pltpu.roll(x, 1, 0) + pltpu.roll(x, x.shape[0] - 1, 0)

    def coarse_terms(q):
        m, e = plane(pm, q, R), plane(pe, q, R)
        lm, le = beside_lanes(m, e)
        gm = (1.0 - OMEGA) * m + k0 * (coef[0] * m + coef[1] * rows_beside(m) + coef[2] * lm)
        ge = (1.0 - OMEGA) * e + k0 * (coef[0] * e + coef[1] * rows_beside(e) + coef[2] * le)
        return gm, ge[:C]

    ks = k0 * coef[0]

    def put_end(t, q, other, ok):
        set_plane(tm, t, R, jnp.where(ok, coarse_terms(q)[0] + ks * plane(pm, other, R), 0.0))

    put_end(0, 0, 1, wall > 0)
    put_end(W + 1, Q - 1, Q - 2, wall < n_wall - 1)

    def level0(q):
        gm, ge = coarse_terms(q)
        for t, other in ((2 * q - 1, q - 1), (2 * q, q + 1)):
            m = gm + ks * plane(pm, other, R)
            set_plane(tm, t, R, m)
            set_plane(te, t - 1, C, jnp.where(rim, ge + ks * plane(pe, other, R)[:C], 0.0))
            set_plane(pot_out, t - 1, C, plane(base_pot, t - 1, C) + m[:C])

    def finish0(w):
        m, e = plane(tm, w + 1, R), plane(te, w, C)
        cm = rows_beside(m)[:C]
        m = m[:C]
        wm = plane(tm, w, R)[:C] + plane(tm, w + 2, R)[:C]
        lm = beside_lanes_main(m, e)
        moved = 2.0 * sum(SI) * m - SI[0] * wm - SI[1] * cm - SI[2] * lm
        set_plane(adj_out, w, C, plane(base_adj, w, C) - DT * plane(mask, w, C) * moved)

    parts = 2
    size = W // parts
    copies = []

    def send(src, dst, k, sem):
        spot = pl.ds(k * size * C, size * C)
        copies.append(pltpu.make_async_copy(src.at[spot], dst.at[spot], sem))
        copies[-1].start()

    for k in range(parts):
        loop(1 + k * W1 // parts, 1 + (k + 1) * W1 // parts, level0, 4)
        send(pot_out, potential, k, sems.at[0, k])
    for k in range(parts):
        loop(k * size, (k + 1) * size, finish0, 4)
        send(adj_out, adj_prev, k, sems.at[1, k])

    NC, NL = sheet.shape[1:]

    def whole_fine(x):
        if NL1 == LANES:
            parts = []
            for t in range(0, NC1, 8):
                wide8 = [lanes_at(x[t : t + 8], tile_lane // 2 + k * middle) for k in range(2)]
                for pick in picks[:2]:
                    parts.append(jnp.concatenate([rows_at(v, pick) for v in wide8], 1))
            return jnp.concatenate(parts, 0)
        along_c = lax.broadcasted_iota(jnp.int32, (NC, NC1), 0) // 2
        along_l = lax.broadcasted_iota(jnp.int32, (NL1, NL), 1) // 2
        twice_c = jnp.where(along_c == lax.broadcasted_iota(jnp.int32, (NC, NC1), 1), 1.0, 0.0).astype(F32)
        twice_l = jnp.where(along_l == lax.broadcasted_iota(jnp.int32, (NL1, NL), 0), 1.0, 0.0).astype(F32)
        return precise(precise(twice_c, x), twice_l)

    for s, i in enumerate((1, planes)):
        p = whole_fine(sweep(x1, b1, i, 1))
        c, l = around(p, 1)
        sheet[s] = (1.0 - OMEGA) * p + k0 * (coef[0] * p + coef[1] * c + coef[2] * l)

    owned = [patches[r : r + 1, :] for r in range(2)]
    spot = lax.broadcasted_iota(jnp.int32, (8, LANES), 0) * LANES + lane_of((8, LANES))
    spot = spot.astype(F32)
    start = half * C1
    totals = [jnp.zeros((C, LANES), F32) for _ in owned]
    small = [jnp.zeros((8, LANES), F32) for _ in owned]
    for v in range(n_wall):
        wall_s = wall_of(v)
        for j in range(n_len):
            ref = blocks[v * n_len + j]
            at_l = pl.ds(pl.multiple_of(length_of(j) * L, L), L)
            if compacted and j == 1:
                for b in range(n_blk):
                    values = sheet[wall_s, b * C : (b + 1) * C, at_l]
                    ids = ref[96 + b * C : 96 + (b + 1) * C, :]
                    totals = [x + jnp.where(ids == e, values, 0.0) for x, e in zip(totals, owned)]
                small = [x + jnp.where(spot == e, ref[160:168, :], 0.0) for x, e in zip(small, owned)]
                continue

            def add(d, carry):
                big, little = carry
                values = sheet[wall_s, pl.ds(pl.multiple_of(blk_of(d) * C, C), C), at_l]
                ids = ref[d, start : start + C, :]
                parts = ref[d, start + C : start + C + 8, :]
                big = [x + jnp.where(ids == e, values, 0.0) for x, e in zip(big, owned)]
                little = [x + jnp.where(spot == e, parts, 0.0) for x, e in zip(little, owned)]
                return big, little

            totals, small = lax.fori_loop(0, n_blk, add, (totals, small), unroll=min(4, n_blk))
    factor = 1.0 / (2.0 * C * L / 2) ** 0.5
    for r in range(2):
        patch_grad[0, r] = (jnp.sum(totals[r]) + jnp.sum(small[r])) * factor
    for copy in copies:
        copy.wait()


def ring(x, axis, by):
    count = lax.axis_size(axis)
    return lax.ppermute(x, axis, [(i, (i + by) % count) for i in range(count)])


def across(x):
    n_wall = lax.axis_size("wall")
    pairs = [(l * n_wall + w, (1 - l) * n_wall + (w + 1) % n_wall) for l in range(2) for w in range(n_wall)]
    return lax.ppermute(x, ("len", "wall"), pairs)


def call(kernel, ins, outs, scratch, name, work=0, room=48):
    places = {"vmem": pltpu.VMEM, "smem": pltpu.SMEM, "any": pl.ANY, "hbm": pltpu.HBM}

    def specs(kinds):
        return [pl.BlockSpec(memory_space=places[kind]) for kind in kinds]

    cost = pl.CostEstimate(flops=work, bytes_accessed=work, transcendentals=0) if work else None
    return pl.pallas_call(
        kernel,
        out_shape=[jax.ShapeDtypeStruct(shape, F32) for shape, _ in outs],
        in_specs=specs(ins),
        out_specs=specs(kind for _, kind in outs),
        scratch_shapes=[pltpu.VMEM(shape, F32) if isinstance(shape, tuple) else shape for shape in scratch],
        compiler_params=pltpu.CompilerParams(vmem_limit_bytes=int(room * 2**20)),
        cost_estimate=cost,
        name=name,
    )


def body(adj_next, ion_slope, misfit, tissue_mask, patch_ids, owner_map):
    W, C, L = adj_next.shape
    n_blk, n_len, n_wall = lax.axis_size("blk"), lax.axis_size("len"), lax.axis_size("wall")
    electrodes = owner_map.shape[0]
    assert L == LANES and H * W == LANES and n_wall == 2 and electrodes == 2 * n_blk * n_len * n_wall
    N = W + 2 * H
    n_dir = 1 if n_len == 2 else 2
    cells = W * C
    vmem = "vmem"
    field, own = (N * C, L), (cells, L)
    raw = [x.reshape(cells, L) for x in (adj_next, ion_slope, tissue_mask, misfit)]

    *fields, wall_out = (faces := call(
        functools.partial(pack_faces, n_len),
        ["hbm"] * 4,
        [(own, vmem)] * 4
        + [((sum(FACES), C, L), vmem)]
        + [((4, C, L), vmem)] * n_dir
        + [((C, L), vmem)] * n_dir,
        [pltpu.VMEM(own, jnp.int32), pltpu.SemaphoreType.DMA((4, 2))],
        "faces",
        room=52.75,
    )(*raw))[:5]
    strip_out, corner_out = faces[5 : 5 + n_dir], faces[5 + n_dir :]
    wall_in = ring(wall_out, "wall", 1)
    if n_dir == 1:
        strips = [ring(strip_out[0], "len", 1)]
        corners = [across(corner_out[0])]
    else:
        strips = [ring(strip_out[1], "len", -1), ring(strip_out[0], "len", 1)]
        corners = [ring(ring(corner_out[1], "wall", 1), "len", -1), ring(ring(corner_out[0], "wall", 1), "len", 1)]

    near = (sum(near_rows(n_dir, W)[-1][::2]), L)
    halos = [wall_in, *strips, *corners]
    to_next, to_prev, own_rows = call(
        functools.partial(boundary, n_len, C),
        [vmem] * (5 + 2 * n_dir),
        [(near, vmem)] * 2 + [((2, 6, N, L), vmem)],
        [(48, N, L)],
        "boundary",
    )(*fields, *halos)
    from_next = ring(to_prev, "blk", -1)
    from_prev = ring(to_next, "blk", 1)
    qm, bm, be, coarse, surface = call(
        functools.partial(sector, n_len, n_wall, C),
        [vmem] * (5 + 2 * n_dir),
        [(field, vmem)] * 3 + [((cells // 8, L), vmem), ((C, L), vmem)],
        [field, (cells // 2, L)] + [field] * 8,
        "sector",
        work=16 * 10**6,
    )(*fields, *halos)

    rows = (8, N, L)
    wide = LANES * ((electrodes + LANES - 1) // LANES)
    message = (cells // 8 + C + 8, L)
    rows_n, rows_p, mine = call(
        functools.partial(correct, electrodes, n_len, n_wall),
        [vmem] * 6,
        [(rows, vmem), (rows, vmem), (message, vmem)],
        [(1, N, L), (wide, L)],
        "correct",
    )(own_rows, from_next, from_prev, coarse, surface, patch_ids)

    relative = n_blk <= 4
    moved = [ring(mine, "blk", d) for d in range(1, n_blk)] if relative else [lax.all_gather(mine, "blk")]
    base_adj, base_pot, patches = call(
        functools.partial(source_part, n_blk, n_len, n_wall, C, electrodes),
        [vmem] * 7,
        [(own, vmem), (own, vmem), ((8, L), vmem)],
        [field] * 4 + [(2, N, L)],
        "source_part",
        work=12 * 10**6,
    )(bm, be, rows_n, rows_p, qm, fields[2], owner_map.reshape(1, electrodes))
    moved, base_adj = lax.optimization_barrier((moved, base_adj))
    sector_blocks = jnp.stack([mine] + moved) if relative else moved[0]
    compacted = (n_blk, n_len, C, W) == (4, 2, 16, 32)
    if compacted:
        (brief,) = call(
            functools.partial(compact, C, W),
            [vmem],
            [((168, L), vmem)],
            [(W // 4, n_blk * C // 2, L), (W // 8 + 1, n_blk * C // 2, L)],
            "compact",
        )(sector_blocks)
        here = [sector_blocks, ring(brief, "len", 1)]
    elif n_len == 2:
        here = [sector_blocks, ring(sector_blocks, "len", 1)]
    else:
        gathered = lax.all_gather(sector_blocks, "len")
        here = [gathered[j] for j in range(n_len)]
    blocks = here + [ring(x, "wall", 1) for x in here]

    NC1, NL1 = n_blk * C // 2, n_len * L // 2
    planes = n_wall * W // 2
    grids = [(planes // k + 2, NC1, NL1) for k in (1, 1, 2, 2, 4, 4)]
    Q = W // 2 + 2
    tall = (Q * (C + 8), L)
    taller = ((W + 2) * (C + 8), L)
    scratch = grids + [(Q * C, NL1), tall, tall, taller, own, own, own]
    scratch += [(2, n_blk * C, n_len * L), (2, 48, L), pltpu.SemaphoreType.DMA((2, 2))]
    adj_prev, potential, patch_grad = call(
        functools.partial(solve, (n_blk, n_len, n_wall), relative, compacted, C, W),
        [vmem] * (len(blocks) + 4),
        [(own, "any"), (own, "any"), ((1, 2), "smem")],
        scratch,
        "solve",
        room=48 if NC1 * NL1 <= 4096 else 58,
    )(*blocks, base_adj, base_pot, fields[2], patches)
    return adj_prev.reshape(W, C, L), potential.reshape(W, C, L), patch_grad


def solution(mesh):
    field = P(("groups", "wall"), "blk", "len")
    return jax.shard_map(
        body,
        mesh=mesh,
        in_specs=(field, field, field, field, field, P("groups")),
        out_specs=(field, field, P(("groups", "blk", "len", "wall"), None)),
        check_vma=False,
    )
```

```python
import functools

import jax
import jax.numpy as jnp
from jax import lax
from jax.experimental import pallas as pl
from jax.experimental.pallas import tpu as pltpu
from jax.sharding import PartitionSpec as P

SI = (0.6, 1.0, 3.0)
SE = (0.8, 1.2, 2.0)
SHIFT = 0.002
OMEGA = 0.8
DT = 0.1
H = 4
LANES = 128
HIGHEST = lax.Precision.HIGHEST
F32 = jnp.float32


def level_coef(level):
    return tuple((SI[i] + SE[i]) / 4.0**level for i in range(3))


def level_diag(level):
    return SHIFT + 2.0 * sum(level_coef(level))


def level_step(level):
    return OMEGA / level_diag(level)


def lane_of(shape):
    return lax.broadcasted_iota(jnp.int32, shape, len(shape) - 1)


def before(m, e):
    first = lane_of(m.shape) == 0
    rm, re = pltpu.roll(m, 1, 1), pltpu.roll(e, 1, 1)
    return jnp.where(first, re, rm), jnp.where(first, rm, re)


def after(m, e):
    last = lane_of(m.shape) == LANES - 1
    rm, re = pltpu.roll(m, LANES - 1, 1), pltpu.roll(e, LANES - 1, 1)
    return jnp.where(last, re, rm), jnp.where(last, rm, re)


def beside_lanes(m, e):
    bm, be = before(m, e)
    am, ae = after(m, e)
    return bm + am, be + ae


def beside_lanes_main(m, e):
    lane = lane_of(m.shape)
    ends = lanes_at(e, LANES - 1 - lane)
    left = jnp.where(lane == 0, ends, pltpu.roll(m, 1, 1))
    right = jnp.where(lane == LANES - 1, ends, pltpu.roll(m, LANES - 1, 1))
    return left + right


def beside_rows(x, row_before, row_after):
    rows = x.shape[0]
    row = lax.broadcasted_iota(jnp.int32, x.shape, 0)
    low = jnp.where(row == 0, row_before, pltpu.roll(x, 1, 0))
    high = jnp.where(row == rows - 1, row_after, pltpu.roll(x, rows - 1, 0))
    return low + high


def beside_dense(x):
    return pltpu.roll(x, 1, 0) + pltpu.roll(x, x.shape[0] - 1, 0)


def plane(ref, i, rows):
    return ref[pl.ds(pl.multiple_of(i * rows, rows), rows), :]


def set_plane(ref, i, rows, value):
    ref[pl.ds(pl.multiple_of(i * rows, rows), rows), :] = value


def loop(low, high, step, unroll):
    def wrapped(i, carry):
        step(i)
        return carry

    lax.fori_loop(low, high, wrapped, 0, unroll=min(unroll, high - low))


FACES = (H, H - 1, H - 1, H - 2)


def face_planes(array):
    return FACES[array], sum(FACES[:array])


def pack_faces(n_len, adj, ion, mask, mis, *rest):
    n_dir = 1 if n_len == 2 else 2
    fields, wall_out, rest = rest[:4], rest[4], rest[5:]
    strips, corners = rest[:n_dir], rest[n_dir : 2 * n_dir]
    whole_mask, sems = rest[2 * n_dir :]
    cells = adj.shape[0]
    C = wall_out.shape[1]
    W = cells // C
    wall, length = lax.axis_index("wall"), lax.axis_index("len")
    targets = (fields[0], fields[1], whole_mask, fields[3])
    copies = []
    for a, (src, dst) in enumerate(zip((adj, ion, mask, mis), targets)):
        part = cells // 4
        for k in range(4):
            spot = pl.ds(k * part, part)
            copies.append(pltpu.make_async_copy(src.at[spot], dst.at[spot], sems.at[a, k]))
            copies[-1].start()

    base = jnp.where(wall == 0, W - H, 0)
    group = lane_of((C, LANES)) // H
    turns = [jnp.where(length == 0, H, 0)] if n_dir == 1 else [H, 0]
    corner = [jnp.zeros((C, LANES), F32) for _ in range(n_dir)]
    for a in (0, 1, 3, 2):
        for k in range(4):
            copies[4 * a + k].wait()
        if a == 2:
            fields[2][...] = whole_mask[...].astype(F32)
        ref = fields[a]
        strip = [jnp.zeros((C, LANES), F32) for _ in range(n_dir)]
        for w in range(W):
            value = ref[w * C : (w + 1) * C, :]
            for d in range(n_dir):
                turned = pltpu.roll(value, lax.rem(H * w + turns[d], LANES), 1)
                strip[d] = jnp.where(group == w, turned, strip[d])
        for d in range(n_dir):
            strips[d][a] = strip[d]
        count, first = face_planes(a)
        for p in range(count):
            face = plane(ref, base + jnp.where(wall == 0, H - count, 0) + p, C)
            wall_out[first + p] = face
            slot = first + p
            for d in range(n_dir):
                turned = pltpu.roll(face, lax.rem(H * slot + turns[d], LANES), 1)
                corner[d] = jnp.where(group == slot, turned, corner[d])
    for d in range(n_dir):
        corners[d][...] = corner[d]


def dense(ref, row, N, C):
    return ref[pl.ds(row, N, stride=C), :]


def dense_pair(m, e, row, N, C):
    return dense(m, row, N, C), dense(e, row, N, C)


def dense_apply(pair, inner, outer, coef):
    m, e = pair
    lm, le = beside_lanes(m, e)
    double = 2.0 * sum(coef)
    out = [double * m - coef[0] * beside_dense(m) - coef[2] * lm, double * e - coef[0] * beside_dense(e) - coef[2] * le]
    for row in (inner, outer):
        if row is not None:
            out = [out[k] - coef[1] * row[k] for k in range(2)]
    return out


def near_rows(n_dir, W):
    start, places = 8 * n_dir, []
    for reach in (0, 1, 2, 2, 3):
        places.append((start, H - reach, W + 2 * reach))
        start += W + 2 * reach
    assert start % 8 == 0
    return places


def rim_tiles(values):
    return [value[s : s + 8] for value in values for s in range(0, value.shape[0], 8)]


def rim_places(n_len, length):
    if n_len == 2:
        return [(jnp.where(length == 0, 0, LANES - H), True)]
    return [(0, length < n_len - 1), (LANES - H, length > 0)]


def boundary(n_len, C, *refs):
    n_dir = 1 if n_len == 2 else 2
    raw, wall_in, refs = refs[:4], refs[4], refs[5:]
    strips, corners, refs = refs[:n_dir], refs[n_dir : 2 * n_dir], refs[2 * n_dir :]
    to_next, to_prev, own_rows, build = refs
    W = raw[0].shape[0] // C
    N = W + 2 * H
    wall, length = lax.axis_index("wall"), lax.axis_index("len")
    places = rim_places(n_len, length)

    def strip_rows(packed, first, count):
        lane, k = lane_of((count, LANES)), lax.broadcasted_iota(jnp.int32, (count, LANES), 0)
        out = jnp.zeros((count, LANES), F32)
        for row, (off, ok) in zip(packed, places):
            j = lax.rem(lane - off + LANES, LANES)
            index = jnp.clip(H * (first + k) + j, 0, LANES - 1)
            taken = lanes_at(jnp.broadcast_to(row, (count, LANES)), index)
            out = jnp.where(jnp.logical_and(j < H, ok), taken, out)
        return out

    slots = iter(range(build.shape[0]))

    def assembled(own, halo, count):
        ref = build.at[next(slots)]
        ref[0:8, :] = jnp.zeros((8, LANES), F32)
        ref[N - 8 : N, :] = jnp.zeros((8, LANES), F32)
        ref[H : H + W, :] = own
        ref[H - count : H, :] = jnp.where(wall == 0, 0.0, halo)
        ref[H + W : H + W + count, :] = jnp.where(wall == 0, halo, 0.0)
        return ref[...]

    def row_of(a, r):
        count, first = face_planes(a)
        halo = jnp.concatenate([wall_in[first + p, r : r + 1, :] for p in range(count)], 0)
        m = assembled(raw[a][pl.ds(r, W, stride=C), :], halo, count)
        own = strip_rows([strip[a, r : r + 1, :] for strip in strips], 0, W)
        halo = strip_rows([corner[r : r + 1, :] for corner in corners], first, 8)[:count]
        return m, assembled(own, halo, count)

    length_shift = jnp.where(length == 0, 0, H) if n_dir == 1 else H
    group = lane_of((8, LANES)) // (H * n_dir)
    for side, (out, order) in enumerate(((to_next, (C - 1, C - 2, C - 3, C - 4)), (to_prev, (0, 1, 2, 3)))):
        adj = [row_of(0, r) for r in order]
        mask = [row_of(2, r) for r in order[:3]]
        q = []
        for k in range(3):
            ion = row_of(1, order[k])
            moved = dense_apply(adj[k], adj[k + 1], adj[k - 1] if k else None, SI)
            q.append([adj[k][j] - DT * mask[k][j] * (moved[j] + ion[j] * adj[k][j]) for j in range(2)])
        near = dense_apply(q[0], q[1], None, SI)
        mis = row_of(3, order[0])
        near = [near[j] + mis[j] for j in range(2)]
        second = dense_apply(q[1], q[2], q[0], SI)[0] + row_of(3, order[1])[0]
        for value, (start, first, count) in zip((second, near[0], q[0][0], mask[0][0], adj[0][0]), near_rows(n_dir, W)):
            out[start : start + count, :] = value[first : first + count]
        packs = [jnp.zeros((8, LANES), F32) for _ in range(n_dir)]
        for t, tile in enumerate(rim_tiles((near[1], q[0][1], mask[0][1], adj[0][1]))):
            k, at = divmod(t, LANES // (H * n_dir))
            turned = pltpu.roll(tile, lax.rem(length_shift + H * n_dir * at, LANES), 1)
            packs[k] = jnp.where(group == at, turned, packs[k])
        for k in range(n_dir):
            out[8 * k : 8 * k + 8, :] = packs[k]
        for k, pair in enumerate((adj[0], mask[0], q[0])):
            own_rows[side, 2 * k] = pair[0]
            own_rows[side, 2 * k + 1] = pair[1]


def spots(m_ref, e_ref, i, rows, coef):
    m, e = plane(m_ref, i, rows), plane(e_ref, i, rows)
    wm = plane(m_ref, i - 1, rows) + plane(m_ref, i + 1, rows)
    we = plane(e_ref, i - 1, rows) + plane(e_ref, i + 1, rows)
    lm, le = beside_lanes(m, e)
    cm, ce = beside_rows(m, 0.0, 0.0), beside_rows(e, 0.0, 0.0)
    double = 2.0 * sum(coef)
    dm = double * m - coef[0] * wm - coef[1] * cm - coef[2] * lm
    de = double * e - coef[0] * we - coef[1] * ce - coef[2] * le
    return m, e, dm, de


def rim_lanes(lane, length, n_len):
    return jnp.logical_or(
        jnp.logical_and(lane < H, length < n_len - 1),
        jnp.logical_and(lane >= LANES - H, length > 0),
    )


def inside(i, wall, W, n_wall):
    w = wall * W + i - H
    return jnp.logical_and(w >= 0, w < n_wall * W)


def lanes_at(x, index):
    return jnp.take_along_axis(x, index, axis=1, mode="promise_in_bounds")


def rows_at(x, index):
    return jnp.take_along_axis(x, index, axis=0, mode="promise_in_bounds")


def halved(low, high):
    lane = lane_of(low.shape)
    even = 2 * lane % LANES
    pairs = [lanes_at(x, even) + lanes_at(x, even + 1) for x in (low, high)]
    return 0.125 * jnp.where(lane < LANES // 2, pairs[0], pairs[1])


def precise(a, b):
    return jnp.dot(a, b, precision=HIGHEST, preferred_element_type=F32)


def assemble(n_len, C, raw, wall_in, strips, corners, xm, xe):
    W = raw[0].shape[0] // C
    N = W + 2 * H
    wall, length = lax.axis_index("wall"), lax.axis_index("len")
    lane = lane_of((C, LANES))
    places = rim_places(n_len, length)
    seen = [jnp.logical_and(lax.rem(lane - off + LANES, LANES) < H, ok) for off, ok in places]

    def rim(packed, base):
        out = jnp.zeros((C, LANES), F32)
        for row, ok, (off, _) in zip(packed, seen, places):
            out = jnp.where(ok, pltpu.roll(row, lax.rem(off - base + LANES, LANES), 1), out)
        return out

    zero = jnp.zeros((C, LANES), F32)
    last = N - H
    for a, own in enumerate(raw):
        packed = [strip[a] for strip in strips]
        for w in range(W):
            set_plane(xm[a], w + H, C, plane(own, w, C))
            set_plane(xe[a], w + H, C, rim(packed, H * w))
        packed = [corner[...] for corner in corners]
        for i in range(H):
            for at in (i, last + i):
                set_plane(xm[a], at, C, zero)
                set_plane(xe[a], at, C, zero)
        count, first = face_planes(a)
        here = jnp.where(wall == 0, last, H - count)
        for p in range(count):
            set_plane(xm[a], here + p, C, wall_in[first + p])
            set_plane(xe[a], here + p, C, rim(packed, H * (first + p)))


def sector(n_len, n_wall, C, electrodes, *refs):
    n_dir = 1 if n_len == 2 else 2
    raw, wall_in, refs = refs[:4], refs[4], refs[5:]
    strips, corners, refs = refs[:n_dir], refs[n_dir : 2 * n_dir], refs[2 * n_dir :]
    owner, qm, bm, be, coarse, surface, patches, qe, pairs = refs[:9]
    xm, xe = refs[9:13], refs[13:17]
    assemble(n_len, C, raw, wall_in, strips, corners, xm, xe)
    N = qm.shape[0] // C
    W = N - 2 * H
    wall, length = lax.axis_index("wall"), lax.axis_index("len")
    rim = rim_lanes(lane_of((C, LANES)), length, n_len)
    zero = jnp.zeros((C, LANES), F32)
    for i in (0, N - 1):
        set_plane(qm, i, C, zero)
        set_plane(qe, i, C, zero)
    for i in (0, 1, N - 2, N - 1):
        set_plane(bm, i, C, zero)
        set_plane(be, i, C, zero)

    def parabolic(i):
        m, e, dm, de = spots(xm[0], xe[0], i, C, SI)
        set_plane(qm, i, C, m - DT * plane(xm[2], i, C) * (dm + plane(xm[1], i, C) * m))
        set_plane(qe, i, C, e - DT * plane(xe[2], i, C) * (de + plane(xe[1], i, C) * e))

    loop(1, N - 1, parabolic, 2)

    def elliptic_source(i):
        m, e, dm, de = spots(qm, qe, i, C, SI)
        ok = inside(i, wall, W, n_wall)
        set_plane(bm, i, C, jnp.where(ok, plane(xm[3], i, C) + dm, 0.0))
        set_plane(be, i, C, jnp.where(jnp.logical_and(rim, ok), plane(xe[3], i, C) + de, 0.0))

    loop(2, N - 2, elliptic_source, 2)

    coef, k0 = level_coef(0), level_step(0)

    def left(i):
        m, e = plane(bm, i, C), plane(be, i, C)
        wm = plane(bm, i - 1, C) + plane(bm, i + 1, C)
        cm = beside_rows(m, 0.0, 0.0)
        lm = beside_lanes_main(m, e)
        return m, (1.0 - OMEGA) * m + k0 * (coef[0] * wm + coef[1] * cm + coef[2] * lm)

    def pair(q):
        i = 2 * q + H
        m, first = left(i)
        n, second = left(i + 1)
        set_plane(pairs, q, C, first + second)

        @pl.when(jnp.logical_and(q == 0, wall == 0))
        def _():
            surface[...] = k0 * (m + first)

        @pl.when(jnp.logical_and(q == W // 2 - 1, wall == n_wall - 1))
        def _():
            surface[...] = k0 * (n + second)

    loop(0, W // 2, pair, 2)

    half = W * C // 8
    z = pairs[pl.ds(0, 2 * half, stride=2), :] + pairs[pl.ds(1, 2 * half, stride=2), :]
    coarse[...] = halved(z[:half], z[half:])

    blk = lax.axis_index("blk")
    me = (blk * n_len + length) * n_wall + wall
    which = lax.broadcasted_iota(jnp.int32, (1, electrodes), 1).astype(F32)
    mine = owner[...] == me
    patches[0:1, :] = jnp.full((1, LANES), jnp.min(jnp.where(mine, which, float(electrodes))))
    patches[1:2, :] = jnp.full((1, LANES), jnp.max(jnp.where(mine, which, -1.0)))
    patches[2:8, :] = jnp.zeros((6, LANES), F32)


def unpacked(ref, n_len, length, N):
    n_dir = 1 if n_len == 2 else 2
    mains = []
    for start, first, count in near_rows(n_dir, N - 2 * H):
        begin = min(start - first, ref.shape[0] - N)
        value = ref[begin : begin + N, :]
        behind = start - first - begin
        mains.append(pltpu.roll(value, N - behind, 0) if behind else value)
    rim = rim_lanes(lane_of((8, LANES)), length, n_len)
    shift = jnp.where(length == 0, 0, H) if n_dir == 1 else H
    rims = []
    for k in range(4):
        parts = []
        for s in range(N // 8):
            pack, at = divmod(k * (N // 8) + s, LANES // (H * n_dir))
            back = lax.rem(2 * LANES - shift - H * n_dir * at, LANES)
            parts.append(jnp.where(rim, pltpu.roll(ref[8 * pack : 8 * pack + 8, :], back, 1), 0.0))
        rims.append(jnp.concatenate(parts, 0))
    second, near, q, mask, adj = mains
    return (adj, rims[3]), (mask, rims[2]), (q, rims[1]), (near, rims[0]), second


def lateral(pair):
    return dense_apply(pair, None, None, SI)


def source_rows(own, other):
    adj_o, mask_o, q_o = own
    adj_n, mask_n, q_n, p_n, second_n = other
    step = DT * SI[1]
    delta_o = [step * mask_o[k] * adj_n[k] for k in range(2)]
    delta_n = [step * mask_n[k] * adj_o[k] for k in range(2)]
    lat_o, lat_n = lateral(delta_o), lateral(delta_n)
    near = [lat_o[k] - SI[1] * (q_n[k] + delta_n[k]) for k in range(2)]
    second = [-SI[1] * delta_o[k] for k in range(2)]
    halo = [p_n[k] + lat_n[k] - SI[1] * (q_o[k] + delta_o[k]) for k in range(2)]
    halo_second = second_n - SI[1] * delta_n[0]
    return near, second, halo, halo_second, delta_o[0]


def correct(electrodes, n_len, n_wall, own_rows, from_next, from_prev, coarse, surface, ids, *rest):
    rows_n, rows_p, message = rest[:3]
    lines, sums = rest[3:]
    _, C, L = ids.shape
    N = own_rows.shape[2]
    W = N - 2 * H
    wall, length = lax.axis_index("wall"), lax.axis_index("len")
    ok_m = inside(lax.broadcasted_iota(jnp.int32, (N, LANES), 0), wall, W, n_wall)
    ok_e = jnp.logical_and(ok_m, rim_lanes(lane_of((N, LANES)), length, n_len))
    coef, k0 = level_coef(0), level_step(0)
    y = surface[...]
    row = lax.broadcasted_iota(jnp.int32, (C, LANES), 0)
    at = pl.ds(jnp.where(wall == 0, H, W + H - 1), 1)
    lows, highs = [], []
    W1, C1 = W // 2, C // 2
    for side, (other, out, order) in enumerate(
        ((from_next, rows_n, (C - 1, C - 2, C - 3)), (from_prev, rows_p, (0, 1, 2)))
    ):
        own = [(own_rows[side, 2 * k], own_rows[side, 2 * k + 1]) for k in range(3)]
        near, second, halo, halo_second, delta = source_rows(own, unpacked(other, n_len, length, N))
        near = [jnp.where(ok_m, near[0], 0.0), jnp.where(ok_e, near[1], 0.0)]
        second = [jnp.where(ok_m, second[0], 0.0), jnp.where(ok_e, second[1], 0.0)]
        out[0] = halo_m = jnp.where(ok_m, halo[0], 0.0)
        out[1] = jnp.where(ok_e, halo[1], 0.0)
        out[2] = jnp.where(ok_m, halo_second, 0.0)
        out[3] = delta
        out[4], out[5] = near
        out[6], out[7] = second

        def turned(pair, beside):
            m, e = pair
            return (1.0 - OMEGA) * m + k0 * (
                coef[0] * beside_dense(m) + coef[2] * beside_lanes_main(m, e) + coef[1] * beside
            )

        first = turned(near, second[0] + halo_m)
        next_one = turned(second, near[0])
        third = k0 * coef[1] * second[0]
        for k, change in enumerate((near[0] + first, second[0] + next_one, third)):
            lines[0] = change
            y = y + jnp.where(row == order[k], k0 * lines[0, at, :], 0.0)
        for change in (first + next_one, third):
            lines[0] = change
            both = lines[0, pl.ds(H, W1, stride=2), :] + lines[0, pl.ds(H + 1, W1, stride=2), :]
            lows.append(both[: W1 // 2])
            highs.append(both[W1 // 2 :])
    add = halved(jnp.concatenate(lows, 0), jnp.concatenate(highs, 0))
    half = W * C // 8
    message[0:half, :] = coarse[...]
    for k, c1 in enumerate((C1 - 1, C1 - 2, 0, 1)):
        spot = pl.ds(c1, W1 // 2, stride=C1)
        message[spot, :] = message[spot, :] + add[k * (W1 // 2) : (k + 1) * (W1 // 2)]
    patch = ids[0]
    message[half : half + C, :] = patch.astype(F32)
    wide = sums.shape[0]
    if wide > electrodes:
        sums[...] = jnp.zeros(sums.shape, F32)

    def one(e):
        sums[pl.ds(e, 1), :] = jnp.sum(jnp.where(patch == e, y, 0.0), axis=0, keepdims=True)

    loop(0, electrodes, one, 8)
    totals = lax.dot_general(
        jnp.ones((8, LANES), F32), sums[...], (((1,), (1,)), ((), ())), precision=HIGHEST, preferred_element_type=F32
    )
    message[half + C : half + C + 8, :] = jnp.zeros((8, LANES), F32)
    for t in range(wide // LANES):
        message[half + C + t : half + C + t + 1, :] = totals[0:1, t * LANES : (t + 1) * LANES]


def source_part(n_len, n_wall, C, bm, be, rows_n, rows_p, qm, mask, base_adj, base_pot, fm, fe, tm, te, hp):
    N = bm.shape[0] // C
    W = N - 2 * H
    length, wall = lax.axis_index("len"), lax.axis_index("wall")
    fm[...] = bm[...]
    fe[...] = be[...]
    for rows, near, second in ((rows_n, C - 1, C - 2), (rows_p, 0, 1)):
        for k, at in ((4, near), (6, second)):
            spot = pl.ds(at, N, stride=C)
            fm[spot, :] = fm[spot, :] + rows[k]
            fe[spot, :] = fe[spot, :] + rows[k + 1]
    coef, k0 = level_coef(0), level_step(0)
    rim = rim_lanes(lane_of((C, LANES)), length, n_len)

    def part(i):
        m, e = plane(fm, i, C), plane(fe, i, C)
        wm = plane(fm, i - 1, C) + plane(fm, i + 1, C)
        we = plane(fe, i - 1, C) + plane(fe, i + 1, C)
        lm, le = beside_lanes(m, e)
        at = pl.ds(i, 1)
        cm = beside_rows(m, rows_p[0, at, :], rows_n[0, at, :])
        ce = beside_rows(e, rows_p[1, at, :], rows_n[1, at, :])
        pm = k0 * ((2.0 - OMEGA) * m + k0 * (coef[0] * wm + coef[1] * cm + coef[2] * lm))
        pe = k0 * ((2.0 - OMEGA) * e + k0 * (coef[0] * we + coef[1] * ce + coef[2] * le))
        set_plane(tm, i, C, jnp.where(inside(i, wall, W, n_wall), pm, 0.0))
        set_plane(te, i, C, jnp.where(rim, pe, 0.0))

    loop(H - 1, N - H + 1, part, 2)
    for side, (rows, at) in enumerate(((rows_n, C - 1), (rows_p, 0))):
        m = rows[0]
        total = (
            coef[0] * beside_dense(m)
            + coef[1] * (rows[2] + dense(fm, at, N, C))
            + coef[2] * beside_lanes_main(m, rows[1])
        )
        hp[side] = k0 * ((2.0 - OMEGA) * m + k0 * total)
    row = lax.broadcasted_iota(jnp.int32, (C, LANES), 0)

    def finish(w):
        i = w + H
        m, e = plane(tm, i, C), plane(te, i, C)
        at = pl.ds(i, 1)
        wm = plane(tm, i - 1, C) + plane(tm, i + 1, C)
        cm = beside_rows(m, hp[1, at, :], hp[0, at, :])
        lm = beside_lanes_main(m, e)
        lam = plane(qm, i, C)
        lam = lam + jnp.where(row == C - 1, rows_n[3, at, :], 0.0) + jnp.where(row == 0, rows_p[3, at, :], 0.0)
        moved = 2.0 * sum(SI) * m - SI[0] * wm - SI[1] * cm - SI[2] * lm
        set_plane(base_adj, w, C, lam - DT * plane(mask, w, C) * moved)
        set_plane(base_pot, w, C, m)

    loop(0, W, finish, 2)


def halves(shape):
    lane = lane_of(shape)
    return lane, lane % (LANES // 2)


def compact(C, W, blocks, out, sheet1, coarse2):
    n_blk = blocks.shape[0]
    W1, C1 = W // 2, C // 2
    half, start, middle = W1 // 2, W1 // 2 * C1, LANES // 2
    blk, length, wall = lax.axis_index("blk"), lax.axis_index("len"), lax.axis_index("wall")
    sums = jnp.zeros((8, LANES), F32)
    for d in range(n_blk):
        b = lax.rem(blk - d + n_blk, n_blk)
        for i in range(half):
            sheet1[i, pl.ds(pl.multiple_of(C1 * b, C1), C1), :] = blocks[d, i * C1 : (i + 1) * C1, :]
        out[pl.ds(pl.multiple_of(96 + C * b, C), C), :] = blocks[d, start : start + C, :]
        sums = sums + blocks[d, start + C : start + C + 8, :]
    out[160:168, :] = sums
    NC1 = sheet1.shape[1]
    lane, at = halves((NC1, LANES))
    low = lane < middle
    coef, k1 = level_coef(1), level_step(1)
    ends = pltpu.roll(sheet1[half - 1], middle, 1), pltpu.roll(sheet1[0], middle, 1)
    for q in range(half // 2):
        both = sheet1[2 * q] + sheet1[2 * q + 1]
        prev = sheet1[2 * q - 1] if q else jnp.where(low, 0.0, ends[0])
        after_it = sheet1[2 * q + 2] if 2 * q + 2 < half else jnp.where(low, ends[1], 0.0)
        c = pltpu.roll(both, 1, 0) + pltpu.roll(both, NC1 - 1, 0)
        l = jnp.where(at == 0, 0.0, pltpu.roll(both, 1, 1)) + jnp.where(
            at == middle - 1, 0.0, pltpu.roll(both, LANES - 1, 1)
        )
        left = (1.0 - OMEGA) * both + k1 * (coef[0] * (prev + both + after_it) + coef[1] * c + coef[2] * l)
        coarse2[q] = 0.125 * twins(left, 1)
    coarse2[half // 2] = 0.125 * twins(jnp.where(wall == 0, sheet1[half - 1], sheet1[0]), 1)
    rows2 = NC1 // 2
    lane2, at2 = halves((rows2, LANES))
    pick = lane2 - at2 + 2 * (at2 % (middle // 2))
    for p in range(half // 4):
        pair = [lanes_at(coarse2[2 * p + k, pl.ds(0, rows2, stride=2), :], pick) for k in range(2)]
        out[rows2 * p : rows2 * (p + 1), :] = jnp.where(at2 < middle // 2, pair[0], pair[1])
    beside = jnp.zeros((NC1, LANES), F32)
    base = jnp.where(length == 0, middle - H, 0)
    for i in range(half):
        turned = pltpu.roll(sheet1[i], lax.rem(H * i - base + LANES, LANES), 1)
        beside = jnp.where(at // H == i, turned, beside)
    out[32 : 32 + NC1, :] = beside
    face = coarse2[half // 2, pl.ds(0, rows2, stride=2), :]
    face = lanes_at(face, jnp.where(wall == 0, middle, 0) + 2 * (at2 % (middle // 2)))
    inner = jnp.logical_and(lane2 >= middle // 2, lane2 < middle)
    out[32 : 32 + rows2, :] = jnp.where(inner, face, beside[:rows2])
    inner_surface = jnp.where(low, sheet1[0], pltpu.roll(sheet1[1], middle, 1))
    outer_surface = jnp.where(low, pltpu.roll(sheet1[half - 2], middle, 1), sheet1[half - 1])
    out[64 : 64 + NC1, :] = jnp.where(wall == 0, inner_surface, outer_surface)


def around(x, by):
    rows, lanes = x.shape
    lane = lane_of(x.shape)
    c = pltpu.roll(x, by, 0) + pltpu.roll(x, rows - by, 0)
    l = jnp.where(lane < by, 0.0, pltpu.roll(x, by, 1)) + jnp.where(
        lane >= lanes - by, 0.0, pltpu.roll(x, lanes - by, 1)
    )
    return c, l


def twins(x, by):
    rows, lanes = x.shape
    if lanes == LANES:
        index = lax.broadcasted_iota(jnp.int32, (8, LANES), 0) ^ by
        x = x + jnp.concatenate([rows_at(x[t : t + 8], index) for t in range(0, rows, 8)], 0)
        return x + lanes_at(x, lane_of(x.shape) ^ by)
    row = lax.broadcasted_iota(jnp.int32, x.shape, 0)
    lane = lane_of(x.shape)
    x = x + jnp.where((row & by) == 0, pltpu.roll(x, rows - by, 0), pltpu.roll(x, by, 0))
    return x + jnp.where((lane & by) == 0, pltpu.roll(x, lanes - by, 1), pltpu.roll(x, by, 1))


def solve(sizes, relative, compacted, C, W, *refs):
    n_blk, n_len, n_wall = sizes
    count = n_len * n_wall
    blocks, refs = refs[:count], refs[count:]
    base_adj, base_pot, mask, patches, adj_prev, potential, patch_grad = refs[:7]
    b1, x1, b2, x2, b3, x3, near, pm, pe, tm, te, adj_out, pot_out, sheet, both_walls, sems = refs[7:]
    L = LANES
    W1, C1 = W // 2, C // 2
    planes, NC1, NL1 = b1.shape
    planes -= 2
    blk, length, wall = lax.axis_index("blk"), lax.axis_index("len"), lax.axis_index("wall")
    half = W1 // 2
    middle = LANES // 2
    lane8 = lane_of((C1, LANES))
    often = 8 if NC1 * NL1 <= 4096 else 1

    def blk_of(d):
        return lax.rem(blk - d + n_blk, n_blk) if relative else d

    def length_of(j):
        return (length + j) % n_len if n_len == 2 else j

    def wall_of(v):
        return (wall + v) % n_wall

    zero1 = jnp.zeros((NC1, NL1), F32)
    for ref in (b1, x1, b2, x2, b3, x3):
        ref[0] = zero1
        ref[ref.shape[0] - 1] = zero1

    if not compacted:
        for v in range(n_wall):
            wall_s = wall_of(v)
            mine = blocks[v * n_len : (v + 1) * n_len]

            def unpack(d):
                at = pl.ds(pl.multiple_of(C1 * blk_of(d), C1), C1)
                for t in range(n_len // 2):
                    one, two = mine[2 * t], mine[2 * t + 1]
                    for i in range(half):
                        a, b = one[d, i * C1 : (i + 1) * C1, :], two[d, i * C1 : (i + 1) * C1, :]
                        if n_len == 2:
                            a, b = jnp.where(length == 0, a, b), jnp.where(length == 0, b, a)
                        spot = 1 + wall_s * W1 + i
                        lanes = slice(t * LANES, (t + 1) * LANES)
                        b1[spot, at, lanes] = jnp.where(lane8 < middle, a, pltpu.roll(b, middle, 1))
                        b1[spot + half, at, lanes] = jnp.where(lane8 < middle, pltpu.roll(a, middle, 1), b)

            loop(0, n_blk, unpack, 4)
    if compacted:
        lane8 = lane_of((C1, LANES))
        here8 = lane8 // middle == length
        face_lane = jnp.where(length == 0, middle, middle - H)
        near8 = jnp.logical_and(lane8 >= face_lane, lane8 < face_lane + H)
        for v in range(n_wall):
            wall_s = wall_of(v)
            own, other = blocks[2 * v], blocks[2 * v + 1]
            for d in range(n_blk):
                row = pl.multiple_of(C1 * blk_of(d), C1)
                at = pl.ds(row, C1)
                beside = other[pl.ds(32 + row, C1), :]
                for i in range(half):
                    a = own[d, i * C1 : (i + 1) * C1, :]
                    b = pltpu.roll(a, middle, 1)
                    for k, value in enumerate((jnp.where(length == 0, a, b), jnp.where(length == 0, b, a))):
                        turn = lax.rem(face_lane - H * i - middle * k + 2 * LANES, LANES)
                        rest = jnp.where(near8, pltpu.roll(beside, turn, 1), 0.0)
                        b1[1 + wall_s * W1 + i + half * k, at, :] = jnp.where(here8, value, rest)
            surface = other[64 : 64 + NC1, :]
            turned = pltpu.roll(surface, middle, 1)
            spot = jnp.where(wall_s == 0, 1, planes - 1)
            here = lane_of((NC1, LANES)) // middle == length
            b1[spot] = jnp.where(here, b1[spot], jnp.where(length == 0, turned, surface))
            b1[spot + 1] = jnp.where(here, b1[spot + 1], jnp.where(length == 0, surface, turned))
        for k in range(2):
            both_walls[k] = jnp.where(wall == k, blocks[1][0:48, :], blocks[3][0:48, :])
        tile_lane8 = lane_of((8, LANES)) % middle // 2
        row_of_8 = lax.broadcasted_iota(jnp.int32, (8, LANES), 0) // 2

        def widened(w, first, t, lane):
            tile = both_walls[w, first + 8 * (t // 2) : first + 8 * (t // 2) + 8, :]
            return lanes_at(rows_at(tile, 4 * (t % 2) + row_of_8), lane + tile_lane8)

        for w2 in range(planes // 2):
            w, q = divmod(w2, half)
            high, q = divmod(q, half // 2)
            for t in range(NC1 // 8):
                value = widened(w, NC1 // 2 * (q // 2), t, middle // 2 * (q % 2) + middle * high)
                if w2 in (half - 1, half):
                    value = value + level_step(1) * level_coef(1)[0] * widened(1 - w, 32, t, middle // 2)
                b2[1 + w2, 8 * t : 8 * t + 8, :] = value

    def total_of(x, wsum, level, by):
        coef = level_coef(level)
        c, l = around(x, by)
        return level_step(level) * (coef[0] * wsum + coef[1] * c + coef[2] * l)

    def left_pair(ref, i, level):
        both = ref[i] + ref[i + 1]
        return (1.0 - OMEGA) * both + total_of(both, ref[i - 1] + both + ref[i + 2], level, 2 ** (level - 1))

    def sweep(x_ref, b_ref, i, level):
        x = x_ref[i]
        total = total_of(x, x_ref[i - 1] + x_ref[i + 1], level, 2 ** (level - 1))
        return (1.0 - OMEGA) * x + level_step(level) * b_ref[i] + total

    lane1 = lane_of((NC1, NL1))
    exact = jnp.logical_or(lane1 // middle == length, lane1 // 2 == jnp.where(length == 0, middle // 2, middle // 2 - 1))

    def down1(q):
        value = 0.125 * twins(left_pair(b1, 2 * q + 1, 1), 1)
        b2[1 + q] = jnp.where(exact, value, b2[1 + q]) if compacted else value

    loop(0, planes // 2, down1, often)

    def down2(q):
        b3[1 + q] = 0.125 * twins(left_pair(b2, 2 * q + 1, 2), 2)

    loop(0, planes // 4, down2, often)

    deep = planes // 4
    k3 = level_step(3)

    x2[1 + deep] = zero1

    def start3(q):
        b = b3[1 + q]
        x2[1 + q] = k3 * ((2.0 - OMEGA) * b + total_of(b, b3[q] + b3[2 + q], 3, 4))

    loop(0, deep, start3, often)

    def sweep3(q):
        x3[1 + q] = sweep(x2, b3, 1 + q, 3)

    loop(0, deep, sweep3, often)
    k2 = level_step(2)

    def up2(q):
        coarse = x3[1 + q]
        x2[1 + 2 * q] = k2 * b2[1 + 2 * q] + coarse
        x2[2 + 2 * q] = k2 * b2[2 + 2 * q] + coarse

    loop(0, planes // 4, up2, often)

    k1 = level_step(1)

    def up1(q):
        fine = sweep(x2, b2, 1 + q, 2)
        x1[1 + 2 * q] = k1 * b1[1 + 2 * q] + fine
        x1[2 + 2 * q] = k1 * b1[2 + 2 * q] + fine

    loop(0, planes // 2, up1, often)

    Q = W1 + 2
    sectors = (blk, lax.rem(blk + 1, n_blk), lax.rem(blk + n_blk - 1, n_blk))
    spots3 = [pl.ds(pl.multiple_of(s * C1, C1), C1) for s in sectors]
    row8 = lax.broadcasted_iota(jnp.int32, (C1, NL1), 0)

    def three(ref, i):
        return jnp.concatenate([ref[i, s, :] for s in spots3], 0)

    def finish1(q):
        i = wall * W1 + q
        x = three(x1, i)
        wsum = three(x1, jnp.maximum(i - 1, 0)) + three(x1, jnp.minimum(i + 1, planes + 1))
        value = (1.0 - OMEGA) * x + k1 * three(b1, i) + total_of(x, wsum, 1, 1)
        value = jnp.where(jnp.logical_and(i >= 1, i <= planes), value, 0.0)
        set_plane(near, 2 * q, C1, value[:C1])
        set_plane(near, 2 * q + 1, C1, jnp.where(row8 < 2, value[C1 : 2 * C1], value[2 * C1 :]))

    loop(0, Q, finish1, min(often, 6))

    first = length * middle
    R = C + 8
    row8 = lax.broadcasted_iota(jnp.int32, (8, LANES), 0)
    tile_lane = lane_of((8, LANES))
    at_e = jnp.where(tile_lane < H, middle + tile_lane // 2, tile_lane // 2 - middle)
    rim8 = rim_lanes(tile_lane, length, n_len)
    if NL1 == LANES:
        index_m, index_e = first + tile_lane // 2, jnp.clip(first + at_e, 0, LANES - 1)

        def spread(tile):
            return lanes_at(tile, index_m), jnp.where(rim8, lanes_at(tile, index_e), 0.0)

    else:
        source = lax.broadcasted_iota(jnp.int32, (NL1, LANES), 0)
        lane = lane_of((NL1, LANES))
        at_all = jnp.where(lane < H, middle + lane // 2, jnp.where(lane >= LANES - H, lane // 2 - middle, 4 * NL1))
        take_m = jnp.where(source == first + lane // 2, 1.0, 0.0).astype(F32)
        take_e = jnp.where(source == first + at_all, 1.0, 0.0).astype(F32)

        def spread(tile):
            return precise(tile, take_m), precise(tile, take_e)

    picks = (row8 // 2, H + row8 // 2)
    ends = jnp.where(row8 < H, 6 + row8 // 2, row8 // 2 - 2)

    def fine_rows(q):
        own = spread(plane(near, 2 * q, C1))
        beside = spread(plane(near, 2 * q + 1, C1))
        for out, a, b in ((pm, own[0], beside[0]), (pe, own[1], beside[1])):
            parts = (jnp.where(row8 < 6, a, b), a, jnp.where(row8 < 2, b, a))
            index = (ends, 2 + row8 // 2, ends)
            for k in range(3):
                out[pl.ds(pl.multiple_of(8 + R * q + 8 * k, 8), 8), :] = rows_at(parts[k], index[k])

    loop(0, Q, fine_rows, min(often, 6))
    for ref in (pm, pe):
        ref[0:8, :] = jnp.zeros((8, LANES), F32)
        ref[8 + R * Q : 16 + R * Q, :] = jnp.zeros((8, LANES), F32)
    coef, k0 = level_coef(0), level_step(0)
    def fine(ref, t, by=0, count=R):
        return ref[pl.ds(8 + R * t + by, count), :]

    def coarse_terms(q):
        out = []
        sides = beside_lanes(fine(pm, q), fine(pe, q))
        for ref, l in zip((pm, pe), sides):
            x = fine(ref, q)
            c = fine(ref, q, -1) + fine(ref, q, 1)
            out.append((1.0 - OMEGA) * x + k0 * (coef[0] * x + coef[1] * c + coef[2] * l))
        return out

    ks = k0 * coef[0]

    def set_fine(ref, t, value):
        ref[pl.ds(pl.multiple_of(8 + R * t, 8), R), :] = value

    def put_end(t, q, other, ok):
        set_fine(tm, t, jnp.where(ok, coarse_terms(q)[0] + ks * fine(pm, other), 0.0))

    put_end(0, 0, 1, wall > 0)
    put_end(W + 1, Q - 1, Q - 2, wall < n_wall - 1)
    rim = rim_lanes(lane_of((R, LANES)), length, n_len)

    def level0(q):
        gm, ge = coarse_terms(q)
        for t, other in ((2 * q - 1, q - 1), (2 * q, q + 1)):
            set_fine(tm, t, gm + ks * fine(pm, other))
            set_fine(te, t, jnp.where(rim, ge + ks * fine(pe, other), 0.0))

    loop(1, 1 + W1, level0, 4)

    def finish0(w):
        t = w + 1
        m, e = fine(tm, t, H, C), fine(te, t, H, C)
        cm = fine(tm, t, H - 1, C) + fine(tm, t, H + 1, C)
        wm = fine(tm, t - 1, H, C) + fine(tm, t + 1, H, C)
        lm = beside_lanes_main(m, e)
        moved = 2.0 * sum(SI) * m - SI[0] * wm - SI[1] * cm - SI[2] * lm
        set_plane(adj_out, w, C, plane(base_adj, w, C) - DT * plane(mask, w, C) * moved)
        set_plane(pot_out, w, C, plane(base_pot, w, C) + m)

    parts = 2
    size = W // parts
    copies = []
    for k in range(parts):
        loop(k * size, (k + 1) * size, finish0, 4)
        spot = pl.ds(k * size * C, size * C)
        for n, (src, dst) in enumerate(((adj_out, adj_prev), (pot_out, potential))):
            copies.append(pltpu.make_async_copy(src.at[spot], dst.at[spot], sems.at[n, k]))
            copies[-1].start()

    NC, NL = sheet.shape[1:]

    def whole_fine(x):
        if NL1 == LANES:
            parts = []
            for t in range(0, NC1, 8):
                wide8 = [lanes_at(x[t : t + 8], tile_lane // 2 + k * middle) for k in range(2)]
                for pick in picks[:2]:
                    parts.append(jnp.concatenate([rows_at(v, pick) for v in wide8], 1))
            return jnp.concatenate(parts, 0)
        along_c = lax.broadcasted_iota(jnp.int32, (NC, NC1), 0) // 2
        along_l = lax.broadcasted_iota(jnp.int32, (NL1, NL), 1) // 2
        twice_c = jnp.where(along_c == lax.broadcasted_iota(jnp.int32, (NC, NC1), 1), 1.0, 0.0).astype(F32)
        twice_l = jnp.where(along_l == lax.broadcasted_iota(jnp.int32, (NL1, NL), 0), 1.0, 0.0).astype(F32)
        return precise(precise(twice_c, x), twice_l)

    for s, i in enumerate((1, planes)):
        p = whole_fine(sweep(x1, b1, i, 1))
        c, l = around(p, 1)
        sheet[s] = (1.0 - OMEGA) * p + k0 * (coef[0] * p + coef[1] * c + coef[2] * l)

    owned = [patches[r : r + 1, :] for r in range(2)]
    spot = lax.broadcasted_iota(jnp.int32, (8, LANES), 0) * LANES + lane_of((8, LANES))
    spot = spot.astype(F32)
    start = half * C1
    totals = [jnp.zeros((C, LANES), F32) for _ in owned]
    small = [jnp.zeros((8, LANES), F32) for _ in owned]
    for v in range(n_wall):
        wall_s = wall_of(v)
        for j in range(n_len):
            ref = blocks[v * n_len + j]
            at_l = pl.ds(pl.multiple_of(length_of(j) * L, L), L)
            if compacted and j == 1:
                for b in range(n_blk):
                    values = sheet[wall_s, b * C : (b + 1) * C, at_l]
                    ids = ref[96 + b * C : 96 + (b + 1) * C, :]
                    totals = [x + jnp.where(ids == e, values, 0.0) for x, e in zip(totals, owned)]
                small = [x + jnp.where(spot == e, ref[160:168, :], 0.0) for x, e in zip(small, owned)]
                continue

            def add(d, carry):
                big, little = carry
                values = sheet[wall_s, pl.ds(pl.multiple_of(blk_of(d) * C, C), C), at_l]
                ids = ref[d, start : start + C, :]
                parts = ref[d, start + C : start + C + 8, :]
                big = [x + jnp.where(ids == e, values, 0.0) for x, e in zip(big, owned)]
                little = [x + jnp.where(spot == e, parts, 0.0) for x, e in zip(little, owned)]
                return big, little

            totals, small = lax.fori_loop(0, n_blk, add, (totals, small), unroll=min(4, n_blk))
    factor = 1.0 / (2.0 * C * L / 2) ** 0.5
    for r in range(2):
        patch_grad[0, r] = (jnp.sum(totals[r]) + jnp.sum(small[r])) * factor
    for copy in copies:
        copy.wait()


def ring(x, axis, by):
    count = lax.axis_size(axis)
    return lax.ppermute(x, axis, [(i, (i + by) % count) for i in range(count)])


def across(x):
    n_wall = lax.axis_size("wall")
    pairs = [(l * n_wall + w, (1 - l) * n_wall + (w + 1) % n_wall) for l in range(2) for w in range(n_wall)]
    return lax.ppermute(x, ("len", "wall"), pairs)


def call(kernel, ins, outs, scratch, name, work=0, room=48):
    places = {"vmem": pltpu.VMEM, "smem": pltpu.SMEM, "any": pl.ANY, "hbm": pltpu.HBM}

    def specs(kinds):
        return [pl.BlockSpec(memory_space=places[kind]) for kind in kinds]

    cost = pl.CostEstimate(flops=work, bytes_accessed=work, transcendentals=0) if work else None
    return pl.pallas_call(
        kernel,
        out_shape=[jax.ShapeDtypeStruct(shape, F32) for shape, _ in outs],
        in_specs=specs(ins),
        out_specs=specs(kind for _, kind in outs),
        scratch_shapes=[pltpu.VMEM(shape, F32) if isinstance(shape, tuple) else shape for shape in scratch],
        compiler_params=pltpu.CompilerParams(vmem_limit_bytes=int(room * 2**20)),
        cost_estimate=cost,
        name=name,
    )


def body(adj_next, ion_slope, misfit, tissue_mask, patch_ids, owner_map):
    W, C, L = adj_next.shape
    n_blk, n_len, n_wall = lax.axis_size("blk"), lax.axis_size("len"), lax.axis_size("wall")
    electrodes = owner_map.shape[0]
    assert L == LANES and H * W == LANES and n_wall == 2 and electrodes == 2 * n_blk * n_len * n_wall
    N = W + 2 * H
    n_dir = 1 if n_len == 2 else 2
    cells = W * C
    vmem = "vmem"
    field, own = (N * C, L), (cells, L)
    raw = [x.reshape(cells, L) for x in (adj_next, ion_slope, tissue_mask, misfit)]

    *fields, wall_out = (faces := call(
        functools.partial(pack_faces, n_len),
        ["hbm"] * 4,
        [(own, vmem)] * 4
        + [((sum(FACES), C, L), vmem)]
        + [((4, C, L), vmem)] * n_dir
        + [((C, L), vmem)] * n_dir,
        [pltpu.VMEM(own, jnp.int32), pltpu.SemaphoreType.DMA((4, 4))],
        "faces",
        room=52.75,
    )(*raw))[:5]
    strip_out, corner_out = faces[5 : 5 + n_dir], faces[5 + n_dir :]
    wall_in = ring(wall_out, "wall", 1)
    if n_dir == 1:
        strips = [ring(strip_out[0], "len", 1)]
        corners = [across(corner_out[0])]
    else:
        strips = [ring(strip_out[1], "len", -1), ring(strip_out[0], "len", 1)]
        corners = [ring(ring(corner_out[1], "wall", 1), "len", -1), ring(ring(corner_out[0], "wall", 1), "len", 1)]

    near = (sum(near_rows(n_dir, W)[-1][::2]), L)
    halos = [wall_in, *strips, *corners]
    to_next, to_prev, own_rows = call(
        functools.partial(boundary, n_len, C),
        [vmem] * (5 + 2 * n_dir),
        [(near, vmem)] * 2 + [((2, 6, N, L), vmem)],
        [(48, N, L)],
        "boundary",
    )(*fields, *halos)
    from_next = ring(to_prev, "blk", -1)
    from_prev = ring(to_next, "blk", 1)
    qm, bm, be, coarse, surface, patches = call(
        functools.partial(sector, n_len, n_wall, C, electrodes),
        [vmem] * (6 + 2 * n_dir),
        [(field, vmem)] * 3 + [((cells // 8, L), vmem), ((C, L), vmem), ((8, L), vmem)],
        [field, (cells // 2, L)] + [field] * 8,
        "sector",
        work=16 * 10**6,
    )(*fields, *halos, owner_map.reshape(1, electrodes))

    rows = (8, N, L)
    wide = LANES * ((electrodes + LANES - 1) // LANES)
    message = (cells // 8 + C + 8, L)
    rows_n, rows_p, mine = call(
        functools.partial(correct, electrodes, n_len, n_wall),
        [vmem] * 6,
        [(rows, vmem), (rows, vmem), (message, vmem)],
        [(1, N, L), (wide, L)],
        "correct",
    )(own_rows, from_next, from_prev, coarse, surface, patch_ids)

    relative = n_blk <= 4
    moved = [ring(mine, "blk", d) for d in range(1, n_blk)] if relative else [lax.all_gather(mine, "blk")]
    base_adj, base_pot = call(
        functools.partial(source_part, n_len, n_wall, C),
        [vmem] * 6,
        [(own, vmem), (own, vmem)],
        [field] * 4 + [(2, N, L)],
        "source_part",
        work=12 * 10**6,
    )(bm, be, rows_n, rows_p, qm, fields[2])
    moved, base_adj = lax.optimization_barrier((moved, base_adj))
    sector_blocks = jnp.stack([mine] + moved) if relative else moved[0]
    compacted = (n_blk, n_len, C, W) == (4, 2, 16, 32)
    if compacted:
        (brief,) = call(
            functools.partial(compact, C, W),
            [vmem],
            [((168, L), vmem)],
            [(W // 4, n_blk * C // 2, L), (W // 8 + 1, n_blk * C // 2, L)],
            "compact",
        )(sector_blocks)
        brief, sector_blocks = lax.optimization_barrier((brief, sector_blocks))
        here = [sector_blocks, ring(brief, "len", 1)]
    elif n_len == 2:
        here = [sector_blocks, ring(sector_blocks, "len", 1)]
    else:
        gathered = lax.all_gather(sector_blocks, "len")
        here = [gathered[j] for j in range(n_len)]
    blocks = here + [ring(x, "wall", 1) for x in here]

    NC1, NL1 = n_blk * C // 2, n_len * L // 2
    planes = n_wall * W // 2
    grids = [(planes // k + 2, NC1, NL1) for k in (1, 1, 2, 2, 4, 4)]
    Q = W // 2 + 2
    tall = (Q * (C + 8) + 16, L)
    taller = ((W + 2) * (C + 8) + 16, L)
    scratch = grids + [(Q * C, NL1), tall, tall, taller, taller, own, own]
    scratch += [(2, n_blk * C, n_len * L), (2, 48, L), pltpu.SemaphoreType.DMA((2, 2))]
    adj_prev, potential, patch_grad = call(
        functools.partial(solve, (n_blk, n_len, n_wall), relative, compacted, C, W),
        [vmem] * (len(blocks) + 4),
        [(own, "any"), (own, "any"), ((1, 2), "smem")],
        scratch,
        "solve",
        room=48 if NC1 * NL1 <= 4096 else 58,
    )(*blocks, base_adj, base_pot, fields[2], patches)
    return adj_prev.reshape(W, C, L), potential.reshape(W, C, L), patch_grad


def solution(mesh):
    field = P(("groups", "wall"), "blk", "len")
    return jax.shard_map(
        body,
        mesh=mesh,
        in_specs=(field, field, field, field, field, P("groups")),
        out_specs=(field, field, P(("groups", "blk", "len", "wall"), None)),
        check_vma=False,
    )
```

```python
import functools

import jax
import jax.numpy as jnp
from jax import lax
from jax.experimental import pallas as pl
from jax.experimental.pallas import tpu as pltpu
from jax.sharding import PartitionSpec as P

SI = (0.6, 1.0, 3.0)
SE = (0.8, 1.2, 2.0)
SHIFT = 0.002
OMEGA = 0.8
DT = 0.1
H = 4
LANES = 128
HIGHEST = lax.Precision.HIGHEST
F32 = jnp.float32


def level_coef(level):
    return tuple((SI[i] + SE[i]) / 4.0**level for i in range(3))


def level_diag(level):
    return SHIFT + 2.0 * sum(level_coef(level))


def level_step(level):
    return OMEGA / level_diag(level)


def lane_of(shape):
    return lax.broadcasted_iota(jnp.int32, shape, len(shape) - 1)


def before(m, e):
    first = lane_of(m.shape) == 0
    rm, re = pltpu.roll(m, 1, 1), pltpu.roll(e, 1, 1)
    return jnp.where(first, re, rm), jnp.where(first, rm, re)


def after(m, e):
    last = lane_of(m.shape) == LANES - 1
    rm, re = pltpu.roll(m, LANES - 1, 1), pltpu.roll(e, LANES - 1, 1)
    return jnp.where(last, re, rm), jnp.where(last, rm, re)


def beside_lanes(m, e):
    bm, be = before(m, e)
    am, ae = after(m, e)
    return bm + am, be + ae


def beside_lanes_main(m, e):
    lane = lane_of(m.shape)
    ends = lanes_at(e, LANES - 1 - lane)
    left = jnp.where(lane == 0, ends, pltpu.roll(m, 1, 1))
    right = jnp.where(lane == LANES - 1, ends, pltpu.roll(m, LANES - 1, 1))
    return left + right


def beside_rows(x, row_before, row_after):
    rows = x.shape[0]
    row = lax.broadcasted_iota(jnp.int32, x.shape, 0)
    low = jnp.where(row == 0, row_before, pltpu.roll(x, 1, 0))
    high = jnp.where(row == rows - 1, row_after, pltpu.roll(x, rows - 1, 0))
    return low + high


def beside_dense(x):
    return pltpu.roll(x, 1, 0) + pltpu.roll(x, x.shape[0] - 1, 0)


def plane(ref, i, rows):
    return ref[pl.ds(pl.multiple_of(i * rows, rows), rows), :]


def set_plane(ref, i, rows, value):
    ref[pl.ds(pl.multiple_of(i * rows, rows), rows), :] = value


def loop(low, high, step, unroll):
    def wrapped(i, carry):
        step(i)
        return carry

    lax.fori_loop(low, high, wrapped, 0, unroll=min(unroll, high - low))


FACES = (H, H - 1, H - 1, H - 2)


def face_planes(array):
    return FACES[array], sum(FACES[:array])


def pack_faces(n_len, adj, ion, mask, mis, *rest):
    n_dir = 1 if n_len == 2 else 2
    fields, wall_out, rest = rest[:4], rest[4], rest[5:]
    strips, corners = rest[:n_dir], rest[n_dir : 2 * n_dir]
    whole_mask, sems = rest[2 * n_dir :]
    cells = adj.shape[0]
    C = wall_out.shape[1]
    W = cells // C
    wall, length = lax.axis_index("wall"), lax.axis_index("len")
    targets = (fields[0], fields[1], whole_mask, fields[3])
    copies = []
    for a, (src, dst) in enumerate(zip((adj, ion, mask, mis), targets)):
        part = cells // 4
        for k in range(4):
            spot = pl.ds(k * part, part)
            copies.append(pltpu.make_async_copy(src.at[spot], dst.at[spot], sems.at[a, k]))
            copies[-1].start()

    base = jnp.where(wall == 0, W - H, 0)
    group = lane_of((C, LANES)) // H
    turns = [jnp.where(length == 0, H, 0)] if n_dir == 1 else [H, 0]
    corner = [jnp.zeros((C, LANES), F32) for _ in range(n_dir)]
    for a in (0, 1, 3, 2):
        for k in range(4):
            copies[4 * a + k].wait()
        if a == 2:
            fields[2][...] = whole_mask[...].astype(F32)
        ref = fields[a]
        strip = [jnp.zeros((C, LANES), F32) for _ in range(n_dir)]
        for w in range(W):
            value = ref[w * C : (w + 1) * C, :]
            for d in range(n_dir):
                turned = pltpu.roll(value, lax.rem(H * w + turns[d], LANES), 1)
                strip[d] = jnp.where(group == w, turned, strip[d])
        for d in range(n_dir):
            strips[d][a] = strip[d]
        count, first = face_planes(a)
        for p in range(count):
            face = plane(ref, base + jnp.where(wall == 0, H - count, 0) + p, C)
            wall_out[first + p] = face
            slot = first + p
            for d in range(n_dir):
                turned = pltpu.roll(face, lax.rem(H * slot + turns[d], LANES), 1)
                corner[d] = jnp.where(group == slot, turned, corner[d])
    for d in range(n_dir):
        corners[d][...] = corner[d]


def dense(ref, row, N, C):
    return ref[pl.ds(row, N, stride=C), :]


def dense_pair(m, e, row, N, C):
    return dense(m, row, N, C), dense(e, row, N, C)


def dense_apply(pair, inner, outer, coef):
    m, e = pair
    lm, le = beside_lanes(m, e)
    double = 2.0 * sum(coef)
    out = [double * m - coef[0] * beside_dense(m) - coef[2] * lm, double * e - coef[0] * beside_dense(e) - coef[2] * le]
    for row in (inner, outer):
        if row is not None:
            out = [out[k] - coef[1] * row[k] for k in range(2)]
    return out


def near_rows(n_dir, W):
    start, places = 8 * n_dir, []
    for reach in (0, 1, 2, 2, 3):
        places.append((start, H - reach, W + 2 * reach))
        start += W + 2 * reach
    assert start % 8 == 0
    return places


def rim_tiles(values):
    return [value[s : s + 8] for value in values for s in range(0, value.shape[0], 8)]


def rim_places(n_len, length):
    if n_len == 2:
        return [(jnp.where(length == 0, 0, LANES - H), True)]
    return [(0, length < n_len - 1), (LANES - H, length > 0)]


def boundary(n_len, C, *refs):
    n_dir = 1 if n_len == 2 else 2
    raw, wall_in, refs = refs[:4], refs[4], refs[5:]
    strips, corners, refs = refs[:n_dir], refs[n_dir : 2 * n_dir], refs[2 * n_dir :]
    to_next, to_prev, own_rows, build = refs
    W = raw[0].shape[0] // C
    N = W + 2 * H
    wall, length = lax.axis_index("wall"), lax.axis_index("len")
    places = rim_places(n_len, length)

    def strip_rows(packed, first, count):
        lane, k = lane_of((count, LANES)), lax.broadcasted_iota(jnp.int32, (count, LANES), 0)
        out = jnp.zeros((count, LANES), F32)
        for row, (off, ok) in zip(packed, places):
            j = lax.rem(lane - off + LANES, LANES)
            index = jnp.clip(H * (first + k) + j, 0, LANES - 1)
            taken = lanes_at(jnp.broadcast_to(row, (count, LANES)), index)
            out = jnp.where(jnp.logical_and(j < H, ok), taken, out)
        return out

    slots = iter(range(build.shape[0]))

    def assembled(own, halo, count):
        ref = build.at[next(slots)]
        ref[0:8, :] = jnp.zeros((8, LANES), F32)
        ref[N - 8 : N, :] = jnp.zeros((8, LANES), F32)
        ref[H : H + W, :] = own
        ref[H - count : H, :] = jnp.where(wall == 0, 0.0, halo)
        ref[H + W : H + W + count, :] = jnp.where(wall == 0, halo, 0.0)
        return ref[...]

    def row_of(a, r):
        count, first = face_planes(a)
        halo = jnp.concatenate([wall_in[first + p, r : r + 1, :] for p in range(count)], 0)
        m = assembled(raw[a][pl.ds(r, W, stride=C), :], halo, count)
        own = strip_rows([strip[a, r : r + 1, :] for strip in strips], 0, W)
        halo = strip_rows([corner[r : r + 1, :] for corner in corners], first, 8)[:count]
        return m, assembled(own, halo, count)

    length_shift = jnp.where(length == 0, 0, H) if n_dir == 1 else H
    group = lane_of((8, LANES)) // (H * n_dir)
    for side, (out, order) in enumerate(((to_next, (C - 1, C - 2, C - 3, C - 4)), (to_prev, (0, 1, 2, 3)))):
        adj = [row_of(0, r) for r in order]
        mask = [row_of(2, r) for r in order[:3]]
        q = []
        for k in range(3):
            ion = row_of(1, order[k])
            moved = dense_apply(adj[k], adj[k + 1], adj[k - 1] if k else None, SI)
            q.append([adj[k][j] - DT * mask[k][j] * (moved[j] + ion[j] * adj[k][j]) for j in range(2)])
        near = dense_apply(q[0], q[1], None, SI)
        mis = row_of(3, order[0])
        near = [near[j] + mis[j] for j in range(2)]
        second = dense_apply(q[1], q[2], q[0], SI)[0] + row_of(3, order[1])[0]
        for value, (start, first, count) in zip((second, near[0], q[0][0], mask[0][0], adj[0][0]), near_rows(n_dir, W)):
            out[start : start + count, :] = value[first : first + count]
        packs = [jnp.zeros((8, LANES), F32) for _ in range(n_dir)]
        for t, tile in enumerate(rim_tiles((near[1], q[0][1], mask[0][1], adj[0][1]))):
            k, at = divmod(t, LANES // (H * n_dir))
            turned = pltpu.roll(tile, lax.rem(length_shift + H * n_dir * at, LANES), 1)
            packs[k] = jnp.where(group == at, turned, packs[k])
        for k in range(n_dir):
            out[8 * k : 8 * k + 8, :] = packs[k]
        for k, pair in enumerate((adj[0], mask[0], q[0])):
            own_rows[side, 2 * k] = pair[0]
            own_rows[side, 2 * k + 1] = pair[1]


def spots(m_ref, e_ref, i, rows, coef):
    m, e = plane(m_ref, i, rows), plane(e_ref, i, rows)
    wm = plane(m_ref, i - 1, rows) + plane(m_ref, i + 1, rows)
    we = plane(e_ref, i - 1, rows) + plane(e_ref, i + 1, rows)
    lm, le = beside_lanes(m, e)
    cm, ce = beside_rows(m, 0.0, 0.0), beside_rows(e, 0.0, 0.0)
    double = 2.0 * sum(coef)
    dm = double * m - coef[0] * wm - coef[1] * cm - coef[2] * lm
    de = double * e - coef[0] * we - coef[1] * ce - coef[2] * le
    return m, e, dm, de


def rim_lanes(lane, length, n_len):
    return jnp.logical_or(
        jnp.logical_and(lane < H, length < n_len - 1),
        jnp.logical_and(lane >= LANES - H, length > 0),
    )


def inside(i, wall, W, n_wall):
    w = wall * W + i - H
    return jnp.logical_and(w >= 0, w < n_wall * W)


def lanes_at(x, index):
    return jnp.take_along_axis(x, index, axis=1, mode="promise_in_bounds")


def rows_at(x, index):
    return jnp.take_along_axis(x, index, axis=0, mode="promise_in_bounds")


def halved(low, high):
    lane = lane_of(low.shape)
    even = 2 * lane % LANES
    pairs = [lanes_at(x, even) + lanes_at(x, even + 1) for x in (low, high)]
    return 0.125 * jnp.where(lane < LANES // 2, pairs[0], pairs[1])


def precise(a, b):
    return jnp.dot(a, b, precision=HIGHEST, preferred_element_type=F32)


def assemble(n_len, C, raw, wall_in, strips, corners, xm, xe):
    W = raw[0].shape[0] // C
    N = W + 2 * H
    wall, length = lax.axis_index("wall"), lax.axis_index("len")
    lane = lane_of((C, LANES))
    places = rim_places(n_len, length)
    seen = [jnp.logical_and(lax.rem(lane - off + LANES, LANES) < H, ok) for off, ok in places]

    def rim(packed, base):
        out = jnp.zeros((C, LANES), F32)
        for row, ok, (off, _) in zip(packed, seen, places):
            out = jnp.where(ok, pltpu.roll(row, lax.rem(off - base + LANES, LANES), 1), out)
        return out

    zero = jnp.zeros((C, LANES), F32)
    last = N - H
    for a, own in enumerate(raw):
        packed = [strip[a] for strip in strips]
        for w in range(W):
            set_plane(xm[a], w + H, C, plane(own, w, C))
            set_plane(xe[a], w + H, C, rim(packed, H * w))
        packed = [corner[...] for corner in corners]
        for i in range(H):
            for at in (i, last + i):
                set_plane(xm[a], at, C, zero)
                set_plane(xe[a], at, C, zero)
        count, first = face_planes(a)
        here = jnp.where(wall == 0, last, H - count)
        for p in range(count):
            set_plane(xm[a], here + p, C, wall_in[first + p])
            set_plane(xe[a], here + p, C, rim(packed, H * (first + p)))


def sector(n_len, n_wall, C, electrodes, *refs):
    n_dir = 1 if n_len == 2 else 2
    raw, wall_in, refs = refs[:4], refs[4], refs[5:]
    strips, corners, refs = refs[:n_dir], refs[n_dir : 2 * n_dir], refs[2 * n_dir :]
    owner, qm, bm, be, coarse, surface, patches, qe, pairs = refs[:9]
    xm, xe = refs[9:13], refs[13:17]
    assemble(n_len, C, raw, wall_in, strips, corners, xm, xe)
    N = qm.shape[0] // C
    W = N - 2 * H
    wall, length = lax.axis_index("wall"), lax.axis_index("len")
    rim = rim_lanes(lane_of((C, LANES)), length, n_len)
    zero = jnp.zeros((C, LANES), F32)
    for i in (0, N - 1):
        set_plane(qm, i, C, zero)
        set_plane(qe, i, C, zero)
    for i in (0, 1, N - 2, N - 1):
        set_plane(bm, i, C, zero)
        set_plane(be, i, C, zero)

    def parabolic(i):
        m, e, dm, de = spots(xm[0], xe[0], i, C, SI)
        set_plane(qm, i, C, m - DT * plane(xm[2], i, C) * (dm + plane(xm[1], i, C) * m))
        set_plane(qe, i, C, e - DT * plane(xe[2], i, C) * (de + plane(xe[1], i, C) * e))

    loop(1, N - 1, parabolic, 2)

    def elliptic_source(i):
        m, e, dm, de = spots(qm, qe, i, C, SI)
        ok = inside(i, wall, W, n_wall)
        set_plane(bm, i, C, jnp.where(ok, plane(xm[3], i, C) + dm, 0.0))
        set_plane(be, i, C, jnp.where(jnp.logical_and(rim, ok), plane(xe[3], i, C) + de, 0.0))

    loop(2, N - 2, elliptic_source, 2)

    coef, k0 = level_coef(0), level_step(0)

    def left(i):
        m, e = plane(bm, i, C), plane(be, i, C)
        wm = plane(bm, i - 1, C) + plane(bm, i + 1, C)
        cm = beside_rows(m, 0.0, 0.0)
        lm = beside_lanes_main(m, e)
        return m, (1.0 - OMEGA) * m + k0 * (coef[0] * wm + coef[1] * cm + coef[2] * lm)

    def pair(q):
        i = 2 * q + H
        m, first = left(i)
        n, second = left(i + 1)
        set_plane(pairs, q, C, first + second)

        @pl.when(jnp.logical_and(q == 0, wall == 0))
        def _():
            surface[...] = k0 * (m + first)

        @pl.when(jnp.logical_and(q == W // 2 - 1, wall == n_wall - 1))
        def _():
            surface[...] = k0 * (n + second)

    loop(0, W // 2, pair, 2)

    half = W * C // 8
    z = pairs[pl.ds(0, 2 * half, stride=2), :] + pairs[pl.ds(1, 2 * half, stride=2), :]
    coarse[...] = halved(z[:half], z[half:])

    blk = lax.axis_index("blk")
    me = (blk * n_len + length) * n_wall + wall
    which = lax.broadcasted_iota(jnp.int32, (1, electrodes), 1).astype(F32)
    mine = owner[...] == me
    patches[0:1, :] = jnp.full((1, LANES), jnp.min(jnp.where(mine, which, float(electrodes))))
    patches[1:2, :] = jnp.full((1, LANES), jnp.max(jnp.where(mine, which, -1.0)))
    patches[2:8, :] = jnp.zeros((6, LANES), F32)


def unpacked(ref, n_len, length, N):
    n_dir = 1 if n_len == 2 else 2
    mains = []
    for start, first, count in near_rows(n_dir, N - 2 * H):
        begin = min(start - first, ref.shape[0] - N)
        value = ref[begin : begin + N, :]
        behind = start - first - begin
        mains.append(pltpu.roll(value, N - behind, 0) if behind else value)
    rim = rim_lanes(lane_of((8, LANES)), length, n_len)
    shift = jnp.where(length == 0, 0, H) if n_dir == 1 else H
    rims = []
    for k in range(4):
        parts = []
        for s in range(N // 8):
            pack, at = divmod(k * (N // 8) + s, LANES // (H * n_dir))
            back = lax.rem(2 * LANES - shift - H * n_dir * at, LANES)
            parts.append(jnp.where(rim, pltpu.roll(ref[8 * pack : 8 * pack + 8, :], back, 1), 0.0))
        rims.append(jnp.concatenate(parts, 0))
    second, near, q, mask, adj = mains
    return (adj, rims[3]), (mask, rims[2]), (q, rims[1]), (near, rims[0]), second


def lateral(pair):
    return dense_apply(pair, None, None, SI)


def source_rows(own, other):
    adj_o, mask_o, q_o = own
    adj_n, mask_n, q_n, p_n, second_n = other
    step = DT * SI[1]
    delta_o = [step * mask_o[k] * adj_n[k] for k in range(2)]
    delta_n = [step * mask_n[k] * adj_o[k] for k in range(2)]
    lat_o, lat_n = lateral(delta_o), lateral(delta_n)
    near = [lat_o[k] - SI[1] * (q_n[k] + delta_n[k]) for k in range(2)]
    second = [-SI[1] * delta_o[k] for k in range(2)]
    halo = [p_n[k] + lat_n[k] - SI[1] * (q_o[k] + delta_o[k]) for k in range(2)]
    halo_second = second_n - SI[1] * delta_n[0]
    return near, second, halo, halo_second, delta_o[0]


def correct(electrodes, n_len, n_wall, own_rows, from_next, from_prev, coarse, surface, ids, *rest):
    rows_n, rows_p, message = rest[:3]
    lines, sums = rest[3:]
    _, C, L = ids.shape
    N = own_rows.shape[2]
    W = N - 2 * H
    wall, length = lax.axis_index("wall"), lax.axis_index("len")
    ok_m = inside(lax.broadcasted_iota(jnp.int32, (N, LANES), 0), wall, W, n_wall)
    ok_e = jnp.logical_and(ok_m, rim_lanes(lane_of((N, LANES)), length, n_len))
    coef, k0 = level_coef(0), level_step(0)
    y = surface[...]
    row = lax.broadcasted_iota(jnp.int32, (C, LANES), 0)
    at = pl.ds(jnp.where(wall == 0, H, W + H - 1), 1)
    lows, highs = [], []
    W1, C1 = W // 2, C // 2
    for side, (other, out, order) in enumerate(
        ((from_next, rows_n, (C - 1, C - 2, C - 3)), (from_prev, rows_p, (0, 1, 2)))
    ):
        own = [(own_rows[side, 2 * k], own_rows[side, 2 * k + 1]) for k in range(3)]
        near, second, halo, halo_second, delta = source_rows(own, unpacked(other, n_len, length, N))
        near = [jnp.where(ok_m, near[0], 0.0), jnp.where(ok_e, near[1], 0.0)]
        second = [jnp.where(ok_m, second[0], 0.0), jnp.where(ok_e, second[1], 0.0)]
        out[0] = halo_m = jnp.where(ok_m, halo[0], 0.0)
        out[1] = jnp.where(ok_e, halo[1], 0.0)
        out[2] = jnp.where(ok_m, halo_second, 0.0)
        out[3] = delta
        out[4], out[5] = near
        out[6], out[7] = second

        def turned(pair, beside):
            m, e = pair
            return (1.0 - OMEGA) * m + k0 * (
                coef[0] * beside_dense(m) + coef[2] * beside_lanes_main(m, e) + coef[1] * beside
            )

        first = turned(near, second[0] + halo_m)
        next_one = turned(second, near[0])
        third = k0 * coef[1] * second[0]
        for k, change in enumerate((near[0] + first, second[0] + next_one, third)):
            lines[0] = change
            y = y + jnp.where(row == order[k], k0 * lines[0, at, :], 0.0)
        for change in (first + next_one, third):
            lines[0] = change
            both = lines[0, pl.ds(H, W1, stride=2), :] + lines[0, pl.ds(H + 1, W1, stride=2), :]
            lows.append(both[: W1 // 2])
            highs.append(both[W1 // 2 :])
    add = halved(jnp.concatenate(lows, 0), jnp.concatenate(highs, 0))
    half = W * C // 8
    message[0:half, :] = coarse[...]
    for k, c1 in enumerate((C1 - 1, C1 - 2, 0, 1)):
        spot = pl.ds(c1, W1 // 2, stride=C1)
        message[spot, :] = message[spot, :] + add[k * (W1 // 2) : (k + 1) * (W1 // 2)]
    patch = ids[0]
    message[half : half + C, :] = patch.astype(F32)
    wide = sums.shape[0]
    if wide > electrodes:
        sums[...] = jnp.zeros(sums.shape, F32)

    def one(e):
        sums[pl.ds(e, 1), :] = jnp.sum(jnp.where(patch == e, y, 0.0), axis=0, keepdims=True)

    loop(0, electrodes, one, 8)
    totals = lax.dot_general(
        jnp.ones((8, LANES), F32), sums[...], (((1,), (1,)), ((), ())), precision=HIGHEST, preferred_element_type=F32
    )
    message[half + C : half + C + 8, :] = jnp.zeros((8, LANES), F32)
    for t in range(wide // LANES):
        message[half + C + t : half + C + t + 1, :] = totals[0:1, t * LANES : (t + 1) * LANES]


def source_part(n_len, n_wall, C, bm, be, rows_n, rows_p, qm, mask, base_adj, base_pot, fm, fe, tm, te, hp):
    N = bm.shape[0] // C
    W = N - 2 * H
    length, wall = lax.axis_index("len"), lax.axis_index("wall")
    fm[...] = bm[...]
    fe[...] = be[...]
    for rows, near, second in ((rows_n, C - 1, C - 2), (rows_p, 0, 1)):
        for k, at in ((4, near), (6, second)):
            spot = pl.ds(at, N, stride=C)
            fm[spot, :] = fm[spot, :] + rows[k]
            fe[spot, :] = fe[spot, :] + rows[k + 1]
    coef, k0 = level_coef(0), level_step(0)
    rim = rim_lanes(lane_of((C, LANES)), length, n_len)

    def part(i):
        m, e = plane(fm, i, C), plane(fe, i, C)
        wm = plane(fm, i - 1, C) + plane(fm, i + 1, C)
        we = plane(fe, i - 1, C) + plane(fe, i + 1, C)
        lm, le = beside_lanes(m, e)
        at = pl.ds(i, 1)
        cm = beside_rows(m, rows_p[0, at, :], rows_n[0, at, :])
        ce = beside_rows(e, rows_p[1, at, :], rows_n[1, at, :])
        pm = k0 * ((2.0 - OMEGA) * m + k0 * (coef[0] * wm + coef[1] * cm + coef[2] * lm))
        pe = k0 * ((2.0 - OMEGA) * e + k0 * (coef[0] * we + coef[1] * ce + coef[2] * le))
        set_plane(tm, i, C, jnp.where(inside(i, wall, W, n_wall), pm, 0.0))
        set_plane(te, i, C, jnp.where(rim, pe, 0.0))

    loop(H - 1, N - H + 1, part, 2)
    for side, (rows, at) in enumerate(((rows_n, C - 1), (rows_p, 0))):
        m = rows[0]
        total = (
            coef[0] * beside_dense(m)
            + coef[1] * (rows[2] + dense(fm, at, N, C))
            + coef[2] * beside_lanes_main(m, rows[1])
        )
        hp[side] = k0 * ((2.0 - OMEGA) * m + k0 * total)
    row = lax.broadcasted_iota(jnp.int32, (C, LANES), 0)

    def finish(w):
        i = w + H
        m, e = plane(tm, i, C), plane(te, i, C)
        at = pl.ds(i, 1)
        wm = plane(tm, i - 1, C) + plane(tm, i + 1, C)
        cm = beside_rows(m, hp[1, at, :], hp[0, at, :])
        lm = beside_lanes_main(m, e)
        lam = plane(qm, i, C)
        lam = lam + jnp.where(row == C - 1, rows_n[3, at, :], 0.0) + jnp.where(row == 0, rows_p[3, at, :], 0.0)
        moved = 2.0 * sum(SI) * m - SI[0] * wm - SI[1] * cm - SI[2] * lm
        set_plane(base_adj, w, C, lam - DT * plane(mask, w, C) * moved)
        set_plane(base_pot, w, C, m)

    loop(0, W, finish, 2)


def halves(shape):
    lane = lane_of(shape)
    return lane, lane % (LANES // 2)


def compact(C, W, blocks, out, wall_out, sheet1, coarse2):
    n_blk = blocks.shape[0]
    W1, C1 = W // 2, C // 2
    half, start, middle = W1 // 2, W1 // 2 * C1, LANES // 2
    blk, length, wall = lax.axis_index("blk"), lax.axis_index("len"), lax.axis_index("wall")
    sums = jnp.zeros((8, LANES), F32)
    for d in range(n_blk):
        b = lax.rem(blk - d + n_blk, n_blk)
        for i in range(half):
            sheet1[i, pl.ds(pl.multiple_of(C1 * b, C1), C1), :] = blocks[d, i * C1 : (i + 1) * C1, :]
        out[pl.ds(pl.multiple_of(96 + C * b, C), C), :] = blocks[d, start : start + C, :]
        sums = sums + blocks[d, start + C : start + C + 8, :]
    out[160:168, :] = sums
    NC1 = sheet1.shape[1]
    lane, at = halves((NC1, LANES))
    low = lane < middle
    coef, k1 = level_coef(1), level_step(1)
    ends = pltpu.roll(sheet1[half - 1], middle, 1), pltpu.roll(sheet1[0], middle, 1)
    for q in range(half // 2):
        both = sheet1[2 * q] + sheet1[2 * q + 1]
        prev = sheet1[2 * q - 1] if q else jnp.where(low, 0.0, ends[0])
        after_it = sheet1[2 * q + 2] if 2 * q + 2 < half else jnp.where(low, ends[1], 0.0)
        c = pltpu.roll(both, 1, 0) + pltpu.roll(both, NC1 - 1, 0)
        l = jnp.where(at == 0, 0.0, pltpu.roll(both, 1, 1)) + jnp.where(
            at == middle - 1, 0.0, pltpu.roll(both, LANES - 1, 1)
        )
        left = (1.0 - OMEGA) * both + k1 * (coef[0] * (prev + both + after_it) + coef[1] * c + coef[2] * l)
        coarse2[q] = 0.125 * twins(left, 1)
    coarse2[half // 2] = 0.125 * twins(jnp.where(wall == 0, sheet1[half - 1], sheet1[0]), 1)
    rows2 = NC1 // 2
    lane2, at2 = halves((rows2, LANES))
    pick = lane2 - at2 + 2 * (at2 % (middle // 2))
    for p in range(half // 4):
        pair = [lanes_at(coarse2[2 * p + k, pl.ds(0, rows2, stride=2), :], pick) for k in range(2)]
        out[rows2 * p : rows2 * (p + 1), :] = jnp.where(at2 < middle // 2, pair[0], pair[1])
    beside = jnp.zeros((NC1, LANES), F32)
    base = jnp.where(length == 0, middle - H, 0)
    for i in range(half):
        turned = pltpu.roll(sheet1[i], lax.rem(H * i - base + LANES, LANES), 1)
        beside = jnp.where(at // H == i, turned, beside)
    index = lax.broadcasted_iota(jnp.int32, (8, LANES), 0) ^ 1
    line = beside + jnp.concatenate([rows_at(beside[t : t + 8], index) for t in range(0, NC1, 8)], 0)
    line = 0.125 * (line + pltpu.roll(line, LANES - H, 1))
    m = lane - 96
    spot = jnp.where(m < H, 8 * m, middle + 8 * (m - H)) + jnp.where(length == 0, H - 1, 0)
    line = lanes_at(line, jnp.clip(spot, 0, LANES - 1))
    beside = jnp.where(jnp.logical_and(m >= 0, m < 8), line, beside)
    out[32 : 32 + NC1, :] = beside
    face = coarse2[half // 2, pl.ds(0, rows2, stride=2), :]
    face = lanes_at(face, jnp.where(wall == 0, middle, 0) + 2 * (at2 % (middle // 2)))
    inner = jnp.logical_and(lane2 >= middle // 2, lane2 < middle)
    out[32 : 32 + rows2, :] = jnp.where(inner, face, beside[:rows2])
    inner_surface = jnp.where(low, sheet1[0], pltpu.roll(sheet1[1], middle, 1))
    outer_surface = jnp.where(low, pltpu.roll(sheet1[half - 2], middle, 1), sheet1[half - 1])
    out[64 : 64 + NC1, :] = jnp.where(wall == 0, inner_surface, outer_surface)
    wall_out[0:168, :] = out[...]
    last = jnp.where(low, pltpu.roll(sheet1[half - 1], middle, 1), sheet1[half - 2])
    wall_out[168 : 168 + NC1, :] = jnp.where(wall == 0, last, inner_surface)


def around(x, by):
    rows, lanes = x.shape
    lane = lane_of(x.shape)
    c = pltpu.roll(x, by, 0) + pltpu.roll(x, rows - by, 0)
    l = jnp.where(lane < by, 0.0, pltpu.roll(x, by, 1)) + jnp.where(
        lane >= lanes - by, 0.0, pltpu.roll(x, lanes - by, 1)
    )
    return c, l


def twins(x, by):
    rows, lanes = x.shape
    if lanes == LANES:
        index = lax.broadcasted_iota(jnp.int32, (8, LANES), 0) ^ by
        x = x + jnp.concatenate([rows_at(x[t : t + 8], index) for t in range(0, rows, 8)], 0)
        return x + lanes_at(x, lane_of(x.shape) ^ by)
    row = lax.broadcasted_iota(jnp.int32, x.shape, 0)
    lane = lane_of(x.shape)
    x = x + jnp.where((row & by) == 0, pltpu.roll(x, rows - by, 0), pltpu.roll(x, by, 0))
    return x + jnp.where((lane & by) == 0, pltpu.roll(x, lanes - by, 1), pltpu.roll(x, by, 1))


def solve(sizes, relative, compacted, C, W, *refs):
    n_blk, n_len, n_wall = sizes
    count = n_len * n_wall + compacted
    blocks, refs = refs[:count], refs[count:]
    base_adj, base_pot, mask, patches, adj_prev, potential, patch_grad = refs[:7]
    b1, x1, b2, x2, b3, x3, near, pm, pe, tm, te, adj_out, pot_out, sheet, briefs, sems = refs[7:]
    L = LANES
    W1, C1 = W // 2, C // 2
    planes, NC1, NL1 = b1.shape
    planes -= 2
    blk, length, wall = lax.axis_index("blk"), lax.axis_index("len"), lax.axis_index("wall")
    half = W1 // 2
    middle = LANES // 2
    lane8 = lane_of((C1, LANES))
    often = 8 if NC1 * NL1 <= 4096 else 1

    def blk_of(d):
        return lax.rem(blk - d + n_blk, n_blk) if relative else d

    def length_of(j):
        return (length + j) % n_len if n_len == 2 else j

    def wall_of(v):
        return (wall + v) % n_wall

    zero1 = jnp.zeros((NC1, NL1), F32)
    for ref in (b1, x1, b2, x2, b3, x3):
        ref[0] = zero1
        ref[ref.shape[0] - 1] = zero1

    if not compacted:
        for v in range(n_wall):
            wall_s = wall_of(v)
            mine = blocks[v * n_len : (v + 1) * n_len]

            def unpack(d):
                at = pl.ds(pl.multiple_of(C1 * blk_of(d), C1), C1)
                for t in range(n_len // 2):
                    one, two = mine[2 * t], mine[2 * t + 1]
                    for i in range(half):
                        a, b = one[d, i * C1 : (i + 1) * C1, :], two[d, i * C1 : (i + 1) * C1, :]
                        if n_len == 2:
                            a, b = jnp.where(length == 0, a, b), jnp.where(length == 0, b, a)
                        spot = 1 + wall_s * W1 + i
                        lanes = slice(t * LANES, (t + 1) * LANES)
                        b1[spot, at, lanes] = jnp.where(lane8 < middle, a, pltpu.roll(b, middle, 1))
                        b1[spot + half, at, lanes] = jnp.where(lane8 < middle, pltpu.roll(a, middle, 1), b)

            loop(0, n_blk, unpack, 4)
    if compacted:
        stack, len_brief, wall_brief, both_brief, own_brief = blocks
        lane8 = lane_of((C1, LANES))
        here8 = lane8 // middle == length
        here = lane_of((NC1, LANES)) // middle == length
        face_lane = jnp.where(length == 0, middle, middle - H)
        near8 = jnp.logical_and(lane8 >= face_lane, lane8 < face_lane + H)
        at_face = jnp.logical_and(lane_of((NC1, LANES)) >= face_lane, lane_of((NC1, LANES)) < face_lane + H)
        for d in range(n_blk):
            row = pl.multiple_of(C1 * blk_of(d), C1)
            beside = len_brief[pl.ds(32 + row, C1), :]
            for i in range(half):
                a = stack[d, i * C1 : (i + 1) * C1, :]
                b = pltpu.roll(a, middle, 1)
                for k, value in enumerate((jnp.where(length == 0, a, b), jnp.where(length == 0, b, a))):
                    turn = lax.rem(face_lane - H * i - middle * k + 2 * LANES, LANES)
                    rest = jnp.where(near8, pltpu.roll(beside, turn, 1), 0.0)
                    b1[1 + wall * W1 + i + half * k, pl.ds(row, C1), :] = jnp.where(here8, value, rest)

        def two_planes(tile):
            turned = pltpu.roll(tile, middle, 1)
            return jnp.where(length == 0, tile, turned), jnp.where(length == 0, turned, tile)

        beyond = two_planes(wall_brief[168 : 168 + NC1, :])
        beside = both_brief[32 : 32 + NC1, :]
        for k in range(2):
            off = jnp.where(wall == 0, H * k, middle + H * (half - 1 - k))
            rest = jnp.where(at_face, pltpu.roll(beside, lax.rem(face_lane - off + 2 * LANES, LANES), 1), 0.0)
            b1[jnp.where(wall == 0, 1 + W1 + k, W1 - k)] = jnp.where(here, beyond[k], rest)
        for k in range(2):
            theirs = two_planes(len_brief[64 : 64 + NC1, :])[1 - k]
            spot = jnp.where(wall == 0, 1, planes - 1) + k
            b1[spot] = jnp.where(here, b1[spot], theirs)
            ours = two_planes(wall_brief[64 : 64 + NC1, :])[k]
            theirs = two_planes(both_brief[64 : 64 + NC1, :])[1 - k]
            b1[jnp.where(wall == 0, planes - 1, 1) + k] = jnp.where(here, ours, theirs)
        for k in range(2):
            briefs[0, k] = jnp.where(wall == k, own_brief[0:64, :], wall_brief[0:64, :])
            briefs[1, k] = jnp.where(wall == k, len_brief[0:64, :], both_brief[0:64, :])
        tile_lane8 = lane_of((8, LANES)) % middle // 2
        row_of_8 = lax.broadcasted_iota(jnp.int32, (8, LANES), 0) // 2
        here_8 = lane_of((8, LANES)) // middle == length
        mine8 = lane_of((8, LANES)) // 2 == jnp.where(length == 0, middle // 2 - 1, middle // 2)
        other8 = lane_of((8, LANES)) // 2 == jnp.where(length == 0, middle // 2, middle // 2 - 1)
        coef1 = [level_step(1) * x for x in level_coef(1)]
        tiles2 = {}

        def widened(w, first, t, start):
            key = (w, first, t)
            if key not in tiles2:
                at = first + 8 * (t // 2)
                tiles2[key] = [rows_at(briefs[h, w, at : at + 8, :], 4 * (t % 2) + row_of_8) for h in range(2)]
            return jnp.where(here_8, *[lanes_at(x, start + tile_lane8) for x in tiles2[key]])

        for w in range(n_wall):
            for t in range(NC1 // 8):
                lines = [briefs[h, w, 32 + 8 * t : 40 + 8 * t, :] for h in range(2)]
                lines = jnp.where(lane_of((8, LANES)) < 104, lines[0], pltpu.roll(lines[1], 8, 1))
                for k in range(half):
                    high, q = divmod(k, half // 2)
                    value = widened(w, NC1 // 2 * (q // 2), t, middle // 2 * (q % 2) + middle * high)
                    index = jnp.where(mine8, 104 + k, jnp.where(other8, 96 + k, LANES - 1))
                    value = value + coef1[2] * lanes_at(lines, index)
                    if k == (half - 1 if w == 0 else 0):
                        value = value + coef1[0] * widened(1 - w, 32, t, middle // 2)
                    b2[1 + w * half + k, 8 * t : 8 * t + 8, :] = value

    def total_of(x, wsum, level, by):
        coef = level_coef(level)
        c, l = around(x, by)
        return level_step(level) * (coef[0] * wsum + coef[1] * c + coef[2] * l)

    def left_pair(ref, i, level):
        both = ref[i] + ref[i + 1]
        return (1.0 - OMEGA) * both + total_of(both, ref[i - 1] + both + ref[i + 2], level, 2 ** (level - 1))

    def sweep(x_ref, b_ref, i, level):
        x = x_ref[i]
        total = total_of(x, x_ref[i - 1] + x_ref[i + 1], level, 2 ** (level - 1))
        return (1.0 - OMEGA) * x + level_step(level) * b_ref[i] + total

    def down1(q):
        b2[1 + q] = 0.125 * twins(left_pair(b1, 2 * q + 1, 1), 1)

    if not compacted:
        loop(0, planes // 2, down1, often)

    def down2(q):
        b3[1 + q] = 0.125 * twins(left_pair(b2, 2 * q + 1, 2), 2)

    loop(0, planes // 4, down2, often)

    deep = planes // 4
    k3 = level_step(3)

    x2[1 + deep] = zero1

    def start3(q):
        b = b3[1 + q]
        x2[1 + q] = k3 * ((2.0 - OMEGA) * b + total_of(b, b3[q] + b3[2 + q], 3, 4))

    loop(0, deep, start3, often)

    def sweep3(q):
        x3[1 + q] = sweep(x2, b3, 1 + q, 3)

    loop(0, deep, sweep3, often)
    k2 = level_step(2)

    def up2(q):
        coarse = x3[1 + q]
        x2[1 + 2 * q] = k2 * b2[1 + 2 * q] + coarse
        x2[2 + 2 * q] = k2 * b2[2 + 2 * q] + coarse

    loop(0, planes // 4, up2, often)

    k1 = level_step(1)

    def up1(q):
        fine = sweep(x2, b2, 1 + q, 2)
        x1[1 + 2 * q] = k1 * b1[1 + 2 * q] + fine
        x1[2 + 2 * q] = k1 * b1[2 + 2 * q] + fine

    if compacted:
        loop(0, half, lambda q: up1(half * wall + q), often)
        up1(half - wall)
        up1((planes // 2 - 1) * (1 - wall))
    else:
        loop(0, planes // 2, up1, often)

    Q = W1 + 2
    sectors = (blk, lax.rem(blk + 1, n_blk), lax.rem(blk + n_blk - 1, n_blk))
    spots3 = [pl.ds(pl.multiple_of(s * C1, C1), C1) for s in sectors]
    row8 = lax.broadcasted_iota(jnp.int32, (C1, NL1), 0)

    def three(ref, i):
        return jnp.concatenate([ref[i, s, :] for s in spots3], 0)

    def finish1(q):
        i = wall * W1 + q
        x = three(x1, i)
        wsum = three(x1, jnp.maximum(i - 1, 0)) + three(x1, jnp.minimum(i + 1, planes + 1))
        value = (1.0 - OMEGA) * x + k1 * three(b1, i) + total_of(x, wsum, 1, 1)
        value = jnp.where(jnp.logical_and(i >= 1, i <= planes), value, 0.0)
        set_plane(near, 2 * q, C1, value[:C1])
        set_plane(near, 2 * q + 1, C1, jnp.where(row8 < 2, value[C1 : 2 * C1], value[2 * C1 :]))

    loop(0, Q, finish1, min(often, 6))

    first = length * middle
    R = C + 8
    row8 = lax.broadcasted_iota(jnp.int32, (8, LANES), 0)
    tile_lane = lane_of((8, LANES))
    at_e = jnp.where(tile_lane < H, middle + tile_lane // 2, tile_lane // 2 - middle)
    rim8 = rim_lanes(tile_lane, length, n_len)
    if NL1 == LANES:
        index_m, index_e = first + tile_lane // 2, jnp.clip(first + at_e, 0, LANES - 1)

        def spread(tile):
            return lanes_at(tile, index_m), jnp.where(rim8, lanes_at(tile, index_e), 0.0)

    else:
        source = lax.broadcasted_iota(jnp.int32, (NL1, LANES), 0)
        lane = lane_of((NL1, LANES))
        at_all = jnp.where(lane < H, middle + lane // 2, jnp.where(lane >= LANES - H, lane // 2 - middle, 4 * NL1))
        take_m = jnp.where(source == first + lane // 2, 1.0, 0.0).astype(F32)
        take_e = jnp.where(source == first + at_all, 1.0, 0.0).astype(F32)

        def spread(tile):
            return precise(tile, take_m), precise(tile, take_e)

    picks = (row8 // 2, H + row8 // 2)
    ends = jnp.where(row8 < H, 6 + row8 // 2, row8 // 2 - 2)

    def fine_rows(q):
        own = spread(plane(near, 2 * q, C1))
        beside = spread(plane(near, 2 * q + 1, C1))
        for out, a, b in ((pm, own[0], beside[0]), (pe, own[1], beside[1])):
            parts = (jnp.where(row8 < 6, a, b), a, jnp.where(row8 < 2, b, a))
            index = (ends, 2 + row8 // 2, ends)
            for k in range(3):
                out[pl.ds(pl.multiple_of(8 + R * q + 8 * k, 8), 8), :] = rows_at(parts[k], index[k])

    loop(0, Q, fine_rows, min(often, 6))
    for ref in (pm, pe):
        ref[0:8, :] = jnp.zeros((8, LANES), F32)
        ref[8 + R * Q : 16 + R * Q, :] = jnp.zeros((8, LANES), F32)
    coef, k0 = level_coef(0), level_step(0)
    def fine(ref, t, by=0, count=R):
        return ref[pl.ds(8 + R * t + by, count), :]

    def coarse_terms(q):
        out = []
        sides = beside_lanes(fine(pm, q), fine(pe, q))
        for ref, l in zip((pm, pe), sides):
            x = fine(ref, q)
            c = fine(ref, q, -1) + fine(ref, q, 1)
            out.append((1.0 - OMEGA) * x + k0 * (coef[0] * x + coef[1] * c + coef[2] * l))
        return out

    ks = k0 * coef[0]

    def set_fine(ref, t, value):
        ref[pl.ds(pl.multiple_of(8 + R * t, 8), R), :] = value

    def put_end(t, q, other, ok):
        set_fine(tm, t, jnp.where(ok, coarse_terms(q)[0] + ks * fine(pm, other), 0.0))

    put_end(0, 0, 1, wall > 0)
    put_end(W + 1, Q - 1, Q - 2, wall < n_wall - 1)
    rim = rim_lanes(lane_of((R, LANES)), length, n_len)

    def level0(q):
        gm, ge = coarse_terms(q)
        for t, other in ((2 * q - 1, q - 1), (2 * q, q + 1)):
            set_fine(tm, t, gm + ks * fine(pm, other))
            set_fine(te, t, jnp.where(rim, ge + ks * fine(pe, other), 0.0))

    loop(1, 1 + W1, level0, 4)

    def finish0(w):
        t = w + 1
        m, e = fine(tm, t, H, C), fine(te, t, H, C)
        cm = fine(tm, t, H - 1, C) + fine(tm, t, H + 1, C)
        wm = fine(tm, t - 1, H, C) + fine(tm, t + 1, H, C)
        lm = beside_lanes_main(m, e)
        moved = 2.0 * sum(SI) * m - SI[0] * wm - SI[1] * cm - SI[2] * lm
        set_plane(adj_out, w, C, plane(base_adj, w, C) - DT * plane(mask, w, C) * moved)
        set_plane(pot_out, w, C, plane(base_pot, w, C) + m)

    parts = 2
    size = W // parts
    copies = []
    for k in range(parts):
        loop(k * size, (k + 1) * size, finish0, 4)
        spot = pl.ds(k * size * C, size * C)
        for n, (src, dst) in enumerate(((adj_out, adj_prev), (pot_out, potential))):
            copies.append(pltpu.make_async_copy(src.at[spot], dst.at[spot], sems.at[n, k]))
            copies[-1].start()

    NC, NL = sheet.shape[1:]

    def whole_fine(x):
        if NL1 == LANES:
            parts = []
            for t in range(0, NC1, 8):
                wide8 = [lanes_at(x[t : t + 8], tile_lane // 2 + k * middle) for k in range(2)]
                for pick in picks[:2]:
                    parts.append(jnp.concatenate([rows_at(v, pick) for v in wide8], 1))
            return jnp.concatenate(parts, 0)
        along_c = lax.broadcasted_iota(jnp.int32, (NC, NC1), 0) // 2
        along_l = lax.broadcasted_iota(jnp.int32, (NL1, NL), 1) // 2
        twice_c = jnp.where(along_c == lax.broadcasted_iota(jnp.int32, (NC, NC1), 1), 1.0, 0.0).astype(F32)
        twice_l = jnp.where(along_l == lax.broadcasted_iota(jnp.int32, (NL1, NL), 0), 1.0, 0.0).astype(F32)
        return precise(precise(twice_c, x), twice_l)

    for s, i in enumerate((1, planes)):
        p = whole_fine(sweep(x1, b1, i, 1))
        c, l = around(p, 1)
        sheet[s] = (1.0 - OMEGA) * p + k0 * (coef[0] * p + coef[1] * c + coef[2] * l)

    owned = [patches[r : r + 1, :] for r in range(2)]
    spot = lax.broadcasted_iota(jnp.int32, (8, LANES), 0) * LANES + lane_of((8, LANES))
    spot = spot.astype(F32)
    start = half * C1
    totals = [jnp.zeros((C, LANES), F32) for _ in owned]
    small = [jnp.zeros((8, LANES), F32) for _ in owned]
    for v in range(n_wall):
        wall_s = wall_of(v)
        for j in range(n_len):
            ref = blocks[v * n_len + j]
            at_l = pl.ds(pl.multiple_of(length_of(j) * L, L), L)
            if compacted and v + j:
                for b in range(n_blk):
                    values = sheet[wall_s, b * C : (b + 1) * C, at_l]
                    ids = ref[96 + b * C : 96 + (b + 1) * C, :]
                    totals = [x + jnp.where(ids == e, values, 0.0) for x, e in zip(totals, owned)]
                small = [x + jnp.where(spot == e, ref[160:168, :], 0.0) for x, e in zip(small, owned)]
                continue

            def add(d, carry):
                big, little = carry
                values = sheet[wall_s, pl.ds(pl.multiple_of(blk_of(d) * C, C), C), at_l]
                ids = ref[d, start : start + C, :]
                parts = ref[d, start + C : start + C + 8, :]
                big = [x + jnp.where(ids == e, values, 0.0) for x, e in zip(big, owned)]
                little = [x + jnp.where(spot == e, parts, 0.0) for x, e in zip(little, owned)]
                return big, little

            totals, small = lax.fori_loop(0, n_blk, add, (totals, small), unroll=min(4, n_blk))
    factor = 1.0 / (2.0 * C * L / 2) ** 0.5
    for r in range(2):
        patch_grad[0, r] = (jnp.sum(totals[r]) + jnp.sum(small[r])) * factor
    for copy in copies:
        copy.wait()


def ring(x, axis, by):
    count = lax.axis_size(axis)
    return lax.ppermute(x, axis, [(i, (i + by) % count) for i in range(count)])


def across(x):
    n_wall = lax.axis_size("wall")
    pairs = [(l * n_wall + w, (1 - l) * n_wall + (w + 1) % n_wall) for l in range(2) for w in range(n_wall)]
    return lax.ppermute(x, ("len", "wall"), pairs)


def call(kernel, ins, outs, scratch, name, work=0, room=48):
    places = {"vmem": pltpu.VMEM, "smem": pltpu.SMEM, "any": pl.ANY, "hbm": pltpu.HBM}

    def specs(kinds):
        return [pl.BlockSpec(memory_space=places[kind]) for kind in kinds]

    cost = pl.CostEstimate(flops=work, bytes_accessed=work, transcendentals=0) if work else None
    return pl.pallas_call(
        kernel,
        out_shape=[jax.ShapeDtypeStruct(shape, F32) for shape, _ in outs],
        in_specs=specs(ins),
        out_specs=specs(kind for _, kind in outs),
        scratch_shapes=[pltpu.VMEM(shape, F32) if isinstance(shape, tuple) else shape for shape in scratch],
        compiler_params=pltpu.CompilerParams(vmem_limit_bytes=int(room * 2**20)),
        cost_estimate=cost,
        name=name,
    )


def body(adj_next, ion_slope, misfit, tissue_mask, patch_ids, owner_map):
    W, C, L = adj_next.shape
    n_blk, n_len, n_wall = lax.axis_size("blk"), lax.axis_size("len"), lax.axis_size("wall")
    electrodes = owner_map.shape[0]
    assert L == LANES and H * W == LANES and n_wall == 2 and electrodes == 2 * n_blk * n_len * n_wall
    N = W + 2 * H
    n_dir = 1 if n_len == 2 else 2
    cells = W * C
    vmem = "vmem"
    field, own = (N * C, L), (cells, L)
    raw = [x.reshape(cells, L) for x in (adj_next, ion_slope, tissue_mask, misfit)]

    *fields, wall_out = (faces := call(
        functools.partial(pack_faces, n_len),
        ["hbm"] * 4,
        [(own, vmem)] * 4
        + [((sum(FACES), C, L), vmem)]
        + [((4, C, L), vmem)] * n_dir
        + [((C, L), vmem)] * n_dir,
        [pltpu.VMEM(own, jnp.int32), pltpu.SemaphoreType.DMA((4, 4))],
        "faces",
        room=52.75,
    )(*raw))[:5]
    strip_out, corner_out = faces[5 : 5 + n_dir], faces[5 + n_dir :]
    wall_in = ring(wall_out, "wall", 1)
    if n_dir == 1:
        strips = [ring(strip_out[0], "len", 1)]
        corners = [across(corner_out[0])]
    else:
        strips = [ring(strip_out[1], "len", -1), ring(strip_out[0], "len", 1)]
        corners = [ring(ring(corner_out[1], "wall", 1), "len", -1), ring(ring(corner_out[0], "wall", 1), "len", 1)]

    near = (sum(near_rows(n_dir, W)[-1][::2]), L)
    halos = [wall_in, *strips, *corners]
    to_next, to_prev, own_rows = call(
        functools.partial(boundary, n_len, C),
        [vmem] * (5 + 2 * n_dir),
        [(near, vmem)] * 2 + [((2, 6, N, L), vmem)],
        [(48, N, L)],
        "boundary",
    )(*fields, *halos)
    from_next = ring(to_prev, "blk", -1)
    from_prev = ring(to_next, "blk", 1)
    qm, bm, be, coarse, surface, patches = call(
        functools.partial(sector, n_len, n_wall, C, electrodes),
        [vmem] * (6 + 2 * n_dir),
        [(field, vmem)] * 3 + [((cells // 8, L), vmem), ((C, L), vmem), ((8, L), vmem)],
        [field, (cells // 2, L)] + [field] * 8,
        "sector",
        work=16 * 10**6,
    )(*fields, *halos, owner_map.reshape(1, electrodes))

    rows = (8, N, L)
    wide = LANES * ((electrodes + LANES - 1) // LANES)
    message = (cells // 8 + C + 8, L)
    rows_n, rows_p, mine = call(
        functools.partial(correct, electrodes, n_len, n_wall),
        [vmem] * 6,
        [(rows, vmem), (rows, vmem), (message, vmem)],
        [(1, N, L), (wide, L)],
        "correct",
    )(own_rows, from_next, from_prev, coarse, surface, patch_ids)

    relative = n_blk <= 4
    moved = [ring(mine, "blk", d) for d in range(1, n_blk)] if relative else [lax.all_gather(mine, "blk")]
    base_adj, base_pot = call(
        functools.partial(source_part, n_len, n_wall, C),
        [vmem] * 6,
        [(own, vmem), (own, vmem)],
        [field] * 4 + [(2, N, L)],
        "source_part",
        work=12 * 10**6,
    )(bm, be, rows_n, rows_p, qm, fields[2])
    moved, base_adj = lax.optimization_barrier((moved, base_adj))
    sector_blocks = jnp.stack([mine] + moved) if relative else moved[0]
    compacted = (n_blk, n_len, C, W) == (4, 2, 16, 32)
    if compacted:
        brief, across_wall = call(
            functools.partial(compact, C, W),
            [vmem],
            [((168, L), vmem), ((200, L), vmem)],
            [(W // 4, n_blk * C // 2, L), (W // 8 + 1, n_blk * C // 2, L)],
            "compact",
        )(sector_blocks)
        len_brief = ring(brief, "len", 1)
        blocks = [sector_blocks, len_brief, ring(across_wall, "wall", 1), ring(len_brief, "wall", 1), brief]
    elif n_len == 2:
        here = [sector_blocks, ring(sector_blocks, "len", 1)]
    else:
        gathered = lax.all_gather(sector_blocks, "len")
        here = [gathered[j] for j in range(n_len)]
    if not compacted:
        blocks = here + [ring(x, "wall", 1) for x in here]

    NC1, NL1 = n_blk * C // 2, n_len * L // 2
    planes = n_wall * W // 2
    grids = [(planes // k + 2, NC1, NL1) for k in (1, 1, 2, 2, 4, 4)]
    Q = W // 2 + 2
    tall = (Q * (C + 8) + 16, L)
    taller = ((W + 2) * (C + 8) + 16, L)
    scratch = grids + [(Q * C, NL1), tall, tall, taller, taller, own, own]
    scratch += [(2, n_blk * C, n_len * L), (2, 2, 64, L), pltpu.SemaphoreType.DMA((2, 2))]
    adj_prev, potential, patch_grad = call(
        functools.partial(solve, (n_blk, n_len, n_wall), relative, compacted, C, W),
        [vmem] * (len(blocks) + 4),
        [(own, "any"), (own, "any"), ((1, 2), "smem")],
        scratch,
        "solve",
        room=48 if NC1 * NL1 <= 4096 else 58,
    )(*blocks, base_adj, base_pot, fields[2], patches)
    return adj_prev.reshape(W, C, L), potential.reshape(W, C, L), patch_grad


def solution(mesh):
    field = P(("groups", "wall"), "blk", "len")
    return jax.shard_map(
        body,
        mesh=mesh,
        in_specs=(field, field, field, field, field, P("groups")),
        out_specs=(field, field, P(("groups", "blk", "len", "wall"), None)),
        check_vma=False,
    )
```

```python
import functools

import jax
import jax.numpy as jnp
from jax import lax
from jax.experimental import pallas as pl
from jax.experimental.pallas import tpu as pltpu
from jax.sharding import PartitionSpec as P

SI = (0.6, 1.0, 3.0)
SE = (0.8, 1.2, 2.0)
SHIFT = 0.002
OMEGA = 0.8
DT = 0.1
H = 4
LANES = 128
HIGHEST = lax.Precision.HIGHEST
F32 = jnp.float32


def level_coef(level):
    return tuple((SI[i] + SE[i]) / 4.0**level for i in range(3))


def level_diag(level):
    return SHIFT + 2.0 * sum(level_coef(level))


def level_step(level):
    return OMEGA / level_diag(level)


def lane_of(shape):
    return lax.broadcasted_iota(jnp.int32, shape, len(shape) - 1)


def before(m, e):
    first = lane_of(m.shape) == 0
    rm, re = pltpu.roll(m, 1, 1), pltpu.roll(e, 1, 1)
    return jnp.where(first, re, rm), jnp.where(first, rm, re)


def after(m, e):
    last = lane_of(m.shape) == LANES - 1
    rm, re = pltpu.roll(m, LANES - 1, 1), pltpu.roll(e, LANES - 1, 1)
    return jnp.where(last, re, rm), jnp.where(last, rm, re)


def beside_lanes(m, e):
    bm, be = before(m, e)
    am, ae = after(m, e)
    return bm + am, be + ae


def beside_lanes_main(m, e):
    lane = lane_of(m.shape)
    ends = lanes_at(e, LANES - 1 - lane)
    left = jnp.where(lane == 0, ends, pltpu.roll(m, 1, 1))
    right = jnp.where(lane == LANES - 1, ends, pltpu.roll(m, LANES - 1, 1))
    return left + right


def beside_rows(x, row_before, row_after):
    rows = x.shape[0]
    row = lax.broadcasted_iota(jnp.int32, x.shape, 0)
    low = jnp.where(row == 0, row_before, pltpu.roll(x, 1, 0))
    high = jnp.where(row == rows - 1, row_after, pltpu.roll(x, rows - 1, 0))
    return low + high


def beside_dense(x):
    return pltpu.roll(x, 1, 0) + pltpu.roll(x, x.shape[0] - 1, 0)


def plane(ref, i, rows):
    return ref[pl.ds(pl.multiple_of(i * rows, rows), rows), :]


def set_plane(ref, i, rows, value):
    ref[pl.ds(pl.multiple_of(i * rows, rows), rows), :] = value


def loop(low, high, step, unroll):
    def wrapped(i, carry):
        step(i)
        return carry

    lax.fori_loop(low, high, wrapped, 0, unroll=min(unroll, high - low))


FACES = (H, H - 1, H - 1, H - 2)


def face_planes(array):
    return FACES[array], sum(FACES[:array])


def pack_faces(n_len, adj, ion, mask, mis, *rest):
    n_dir = 1 if n_len == 2 else 2
    fields, wall_out, rest = rest[:4], rest[4], rest[5:]
    strips, corners = rest[:n_dir], rest[n_dir : 2 * n_dir]
    whole_mask, sems = rest[2 * n_dir :]
    cells = adj.shape[0]
    C = wall_out.shape[1]
    W = cells // C
    wall, length = lax.axis_index("wall"), lax.axis_index("len")
    targets = (fields[0], fields[1], whole_mask, fields[3])
    copies = []
    for a, (src, dst) in enumerate(zip((adj, ion, mask, mis), targets)):
        part = cells // 4
        for k in range(4):
            spot = pl.ds(k * part, part)
            copies.append(pltpu.make_async_copy(src.at[spot], dst.at[spot], sems.at[a, k]))
            copies[-1].start()

    base = jnp.where(wall == 0, W - H, 0)
    group = lane_of((C, LANES)) // H
    turns = [jnp.where(length == 0, H, 0)] if n_dir == 1 else [H, 0]
    corner = [jnp.zeros((C, LANES), F32) for _ in range(n_dir)]
    for a in (0, 1, 3, 2):
        for k in range(4):
            copies[4 * a + k].wait()
        if a == 2:
            fields[2][...] = whole_mask[...].astype(F32)
        ref = fields[a]
        strip = [jnp.zeros((C, LANES), F32) for _ in range(n_dir)]
        for w in range(W):
            value = ref[w * C : (w + 1) * C, :]
            for d in range(n_dir):
                turned = pltpu.roll(value, lax.rem(H * w + turns[d], LANES), 1)
                strip[d] = jnp.where(group == w, turned, strip[d])
        for d in range(n_dir):
            strips[d][a] = strip[d]
        count, first = face_planes(a)
        for p in range(count):
            face = plane(ref, base + jnp.where(wall == 0, H - count, 0) + p, C)
            wall_out[first + p] = face
            slot = first + p
            for d in range(n_dir):
                turned = pltpu.roll(face, lax.rem(H * slot + turns[d], LANES), 1)
                corner[d] = jnp.where(group == slot, turned, corner[d])
    for d in range(n_dir):
        corners[d][...] = corner[d]


def dense(ref, row, N, C):
    return ref[pl.ds(row, N, stride=C), :]


def dense_pair(m, e, row, N, C):
    return dense(m, row, N, C), dense(e, row, N, C)


def dense_apply(pair, inner, outer, coef):
    m, e = pair
    lm, le = beside_lanes(m, e)
    double = 2.0 * sum(coef)
    out = [double * m - coef[0] * beside_dense(m) - coef[2] * lm, double * e - coef[0] * beside_dense(e) - coef[2] * le]
    for row in (inner, outer):
        if row is not None:
            out = [out[k] - coef[1] * row[k] for k in range(2)]
    return out


def near_rows(n_dir, W):
    start, places = 8 * n_dir, []
    for reach in (0, 1, 2, 2, 3):
        places.append((start, H - reach, W + 2 * reach))
        start += W + 2 * reach
    assert start % 8 == 0
    return places


def rim_tiles(values):
    return [value[s : s + 8] for value in values for s in range(0, value.shape[0], 8)]


def rim_places(n_len, length):
    if n_len == 2:
        return [(jnp.where(length == 0, 0, LANES - H), True)]
    return [(0, length < n_len - 1), (LANES - H, length > 0)]


def boundary(n_len, C, *refs):
    n_dir = 1 if n_len == 2 else 2
    raw, wall_in, refs = refs[:4], refs[4], refs[5:]
    strips, corners, refs = refs[:n_dir], refs[n_dir : 2 * n_dir], refs[2 * n_dir :]
    to_next, to_prev, own_rows, build = refs
    W = raw[0].shape[0] // C
    N = W + 2 * H
    wall, length = lax.axis_index("wall"), lax.axis_index("len")
    places = rim_places(n_len, length)

    def strip_rows(packed, first, count):
        lane, k = lane_of((count, LANES)), lax.broadcasted_iota(jnp.int32, (count, LANES), 0)
        out = jnp.zeros((count, LANES), F32)
        for row, (off, ok) in zip(packed, places):
            j = lax.rem(lane - off + LANES, LANES)
            index = jnp.clip(H * (first + k) + j, 0, LANES - 1)
            taken = lanes_at(jnp.broadcast_to(row, (count, LANES)), index)
            out = jnp.where(jnp.logical_and(j < H, ok), taken, out)
        return out

    slots = iter(range(build.shape[0]))

    def assembled(own, halo, count):
        ref = build.at[next(slots)]
        ref[0:8, :] = jnp.zeros((8, LANES), F32)
        ref[N - 8 : N, :] = jnp.zeros((8, LANES), F32)
        ref[H : H + W, :] = own
        ref[H - count : H, :] = jnp.where(wall == 0, 0.0, halo)
        ref[H + W : H + W + count, :] = jnp.where(wall == 0, halo, 0.0)
        return ref[...]

    def row_of(a, r):
        count, first = face_planes(a)
        halo = jnp.concatenate([wall_in[first + p, r : r + 1, :] for p in range(count)], 0)
        m = assembled(raw[a][pl.ds(r, W, stride=C), :], halo, count)
        own = strip_rows([strip[a, r : r + 1, :] for strip in strips], 0, W)
        halo = strip_rows([corner[r : r + 1, :] for corner in corners], first, 8)[:count]
        return m, assembled(own, halo, count)

    length_shift = jnp.where(length == 0, 0, H) if n_dir == 1 else H
    group = lane_of((8, LANES)) // (H * n_dir)
    for side, (out, order) in enumerate(((to_next, (C - 1, C - 2, C - 3, C - 4)), (to_prev, (0, 1, 2, 3)))):
        adj = [row_of(0, r) for r in order]
        mask = [row_of(2, r) for r in order[:3]]
        q = []
        for k in range(3):
            ion = row_of(1, order[k])
            moved = dense_apply(adj[k], adj[k + 1], adj[k - 1] if k else None, SI)
            q.append([adj[k][j] - DT * mask[k][j] * (moved[j] + ion[j] * adj[k][j]) for j in range(2)])
        near = dense_apply(q[0], q[1], None, SI)
        mis = row_of(3, order[0])
        near = [near[j] + mis[j] for j in range(2)]
        second = dense_apply(q[1], q[2], q[0], SI)[0] + row_of(3, order[1])[0]
        for value, (start, first, count) in zip((second, near[0], q[0][0], mask[0][0], adj[0][0]), near_rows(n_dir, W)):
            out[start : start + count, :] = value[first : first + count]
        packs = [jnp.zeros((8, LANES), F32) for _ in range(n_dir)]
        for t, tile in enumerate(rim_tiles((near[1], q[0][1], mask[0][1], adj[0][1]))):
            k, at = divmod(t, LANES // (H * n_dir))
            turned = pltpu.roll(tile, lax.rem(length_shift + H * n_dir * at, LANES), 1)
            packs[k] = jnp.where(group == at, turned, packs[k])
        for k in range(n_dir):
            out[8 * k : 8 * k + 8, :] = packs[k]
        for k, pair in enumerate((adj[0], mask[0], q[0])):
            own_rows[side, 2 * k] = pair[0]
            own_rows[side, 2 * k + 1] = pair[1]


def spots(m_ref, e_ref, i, rows, coef):
    m, e = plane(m_ref, i, rows), plane(e_ref, i, rows)
    wm = plane(m_ref, i - 1, rows) + plane(m_ref, i + 1, rows)
    we = plane(e_ref, i - 1, rows) + plane(e_ref, i + 1, rows)
    lm, le = beside_lanes(m, e)
    cm, ce = beside_rows(m, 0.0, 0.0), beside_rows(e, 0.0, 0.0)
    double = 2.0 * sum(coef)
    dm = double * m - coef[0] * wm - coef[1] * cm - coef[2] * lm
    de = double * e - coef[0] * we - coef[1] * ce - coef[2] * le
    return m, e, dm, de


def rim_lanes(lane, length, n_len):
    return jnp.logical_or(
        jnp.logical_and(lane < H, length < n_len - 1),
        jnp.logical_and(lane >= LANES - H, length > 0),
    )


def inside(i, wall, W, n_wall):
    w = wall * W + i - H
    return jnp.logical_and(w >= 0, w < n_wall * W)


def lanes_at(x, index):
    return jnp.take_along_axis(x, index, axis=1, mode="promise_in_bounds")


def rows_at(x, index):
    return jnp.take_along_axis(x, index, axis=0, mode="promise_in_bounds")


def halved(low, high):
    lane = lane_of(low.shape)
    even = 2 * lane % LANES
    pairs = [lanes_at(x, even) + lanes_at(x, even + 1) for x in (low, high)]
    return 0.125 * jnp.where(lane < LANES // 2, pairs[0], pairs[1])


def precise(a, b):
    return jnp.dot(a, b, precision=HIGHEST, preferred_element_type=F32)


def assemble(n_len, C, raw, wall_in, strips, corners, xm, xe):
    W = raw[0].shape[0] // C
    N = W + 2 * H
    wall, length = lax.axis_index("wall"), lax.axis_index("len")
    lane = lane_of((C, LANES))
    places = rim_places(n_len, length)
    seen = [jnp.logical_and(lax.rem(lane - off + LANES, LANES) < H, ok) for off, ok in places]

    def rim(packed, base):
        out = jnp.zeros((C, LANES), F32)
        for row, ok, (off, _) in zip(packed, seen, places):
            out = jnp.where(ok, pltpu.roll(row, lax.rem(off - base + LANES, LANES), 1), out)
        return out

    zero = jnp.zeros((C, LANES), F32)
    last = N - H
    for a, own in enumerate(raw):
        packed = [strip[a] for strip in strips]
        for w in range(W):
            set_plane(xm[a], w + H, C, plane(own, w, C))
            set_plane(xe[a], w + H, C, rim(packed, H * w))
        packed = [corner[...] for corner in corners]
        for i in range(H):
            for at in (i, last + i):
                set_plane(xm[a], at, C, zero)
                set_plane(xe[a], at, C, zero)
        count, first = face_planes(a)
        here = jnp.where(wall == 0, last, H - count)
        for p in range(count):
            set_plane(xm[a], here + p, C, wall_in[first + p])
            set_plane(xe[a], here + p, C, rim(packed, H * (first + p)))


def sector(n_len, n_wall, C, electrodes, *refs):
    n_dir = 1 if n_len == 2 else 2
    raw, wall_in, refs = refs[:4], refs[4], refs[5:]
    strips, corners, refs = refs[:n_dir], refs[n_dir : 2 * n_dir], refs[2 * n_dir :]
    owner, qm, bm, be, coarse, surface, patches, qe, pairs = refs[:9]
    xm, xe = refs[9:13], refs[13:17]
    assemble(n_len, C, raw, wall_in, strips, corners, xm, xe)
    N = qm.shape[0] // C
    W = N - 2 * H
    wall, length = lax.axis_index("wall"), lax.axis_index("len")
    rim = rim_lanes(lane_of((C, LANES)), length, n_len)
    zero = jnp.zeros((C, LANES), F32)
    for i in (0, N - 1):
        set_plane(qm, i, C, zero)
        set_plane(qe, i, C, zero)
    for i in (0, 1, N - 2, N - 1):
        set_plane(bm, i, C, zero)
        set_plane(be, i, C, zero)

    def parabolic(i):
        m, e, dm, de = spots(xm[0], xe[0], i, C, SI)
        set_plane(qm, i, C, m - DT * plane(xm[2], i, C) * (dm + plane(xm[1], i, C) * m))
        set_plane(qe, i, C, e - DT * plane(xe[2], i, C) * (de + plane(xe[1], i, C) * e))

    loop(1, N - 1, parabolic, 2)

    def elliptic_source(i):
        m, e, dm, de = spots(qm, qe, i, C, SI)
        ok = inside(i, wall, W, n_wall)
        set_plane(bm, i, C, jnp.where(ok, plane(xm[3], i, C) + dm, 0.0))
        set_plane(be, i, C, jnp.where(jnp.logical_and(rim, ok), plane(xe[3], i, C) + de, 0.0))

    loop(2, N - 2, elliptic_source, 2)

    coef, k0 = level_coef(0), level_step(0)

    def left(i):
        m, e = plane(bm, i, C), plane(be, i, C)
        wm = plane(bm, i - 1, C) + plane(bm, i + 1, C)
        cm = beside_rows(m, 0.0, 0.0)
        lm = beside_lanes_main(m, e)
        return m, (1.0 - OMEGA) * m + k0 * (coef[0] * wm + coef[1] * cm + coef[2] * lm)

    def pair(q):
        i = 2 * q + H
        m, first = left(i)
        n, second = left(i + 1)
        set_plane(pairs, q, C, first + second)

        @pl.when(jnp.logical_and(q == 0, wall == 0))
        def _():
            surface[...] = k0 * (m + first)

        @pl.when(jnp.logical_and(q == W // 2 - 1, wall == n_wall - 1))
        def _():
            surface[...] = k0 * (n + second)

    loop(0, W // 2, pair, 2)

    half = W * C // 8
    z = pairs[pl.ds(0, 2 * half, stride=2), :] + pairs[pl.ds(1, 2 * half, stride=2), :]
    coarse[...] = halved(z[:half], z[half:])

    blk = lax.axis_index("blk")
    me = (blk * n_len + length) * n_wall + wall
    which = lax.broadcasted_iota(jnp.int32, (1, electrodes), 1).astype(F32)
    mine = owner[...] == me
    patches[0:1, :] = jnp.full((1, LANES), jnp.min(jnp.where(mine, which, float(electrodes))))
    patches[1:2, :] = jnp.full((1, LANES), jnp.max(jnp.where(mine, which, -1.0)))
    patches[2:8, :] = jnp.zeros((6, LANES), F32)


def unpacked(ref, n_len, length, N):
    n_dir = 1 if n_len == 2 else 2
    mains = []
    for start, first, count in near_rows(n_dir, N - 2 * H):
        begin = min(start - first, ref.shape[0] - N)
        value = ref[begin : begin + N, :]
        behind = start - first - begin
        mains.append(pltpu.roll(value, N - behind, 0) if behind else value)
    rim = rim_lanes(lane_of((8, LANES)), length, n_len)
    shift = jnp.where(length == 0, 0, H) if n_dir == 1 else H
    rims = []
    for k in range(4):
        parts = []
        for s in range(N // 8):
            pack, at = divmod(k * (N // 8) + s, LANES // (H * n_dir))
            back = lax.rem(2 * LANES - shift - H * n_dir * at, LANES)
            parts.append(jnp.where(rim, pltpu.roll(ref[8 * pack : 8 * pack + 8, :], back, 1), 0.0))
        rims.append(jnp.concatenate(parts, 0))
    second, near, q, mask, adj = mains
    return (adj, rims[3]), (mask, rims[2]), (q, rims[1]), (near, rims[0]), second


def lateral(pair):
    return dense_apply(pair, None, None, SI)


def source_rows(own, other):
    adj_o, mask_o, q_o = own
    adj_n, mask_n, q_n, p_n, second_n = other
    step = DT * SI[1]
    delta_o = [step * mask_o[k] * adj_n[k] for k in range(2)]
    delta_n = [step * mask_n[k] * adj_o[k] for k in range(2)]
    lat_o, lat_n = lateral(delta_o), lateral(delta_n)
    near = [lat_o[k] - SI[1] * (q_n[k] + delta_n[k]) for k in range(2)]
    second = [-SI[1] * delta_o[k] for k in range(2)]
    halo = [p_n[k] + lat_n[k] - SI[1] * (q_o[k] + delta_o[k]) for k in range(2)]
    halo_second = second_n - SI[1] * delta_n[0]
    return near, second, halo, halo_second, delta_o[0]


def correct(electrodes, n_len, n_wall, own_rows, from_next, from_prev, coarse, surface, ids, *rest):
    rows_n, rows_p, message = rest[:3]
    lines, sums = rest[3:]
    _, C, L = ids.shape
    N = own_rows.shape[2]
    W = N - 2 * H
    wall, length = lax.axis_index("wall"), lax.axis_index("len")
    ok_m = inside(lax.broadcasted_iota(jnp.int32, (N, LANES), 0), wall, W, n_wall)
    ok_e = jnp.logical_and(ok_m, rim_lanes(lane_of((N, LANES)), length, n_len))
    coef, k0 = level_coef(0), level_step(0)
    y = surface[...]
    row = lax.broadcasted_iota(jnp.int32, (C, LANES), 0)
    at = pl.ds(jnp.where(wall == 0, H, W + H - 1), 1)
    lows, highs = [], []
    W1, C1 = W // 2, C // 2
    for side, (other, out, order) in enumerate(
        ((from_next, rows_n, (C - 1, C - 2, C - 3)), (from_prev, rows_p, (0, 1, 2)))
    ):
        own = [(own_rows[side, 2 * k], own_rows[side, 2 * k + 1]) for k in range(3)]
        near, second, halo, halo_second, delta = source_rows(own, unpacked(other, n_len, length, N))
        near = [jnp.where(ok_m, near[0], 0.0), jnp.where(ok_e, near[1], 0.0)]
        second = [jnp.where(ok_m, second[0], 0.0), jnp.where(ok_e, second[1], 0.0)]
        out[0] = halo_m = jnp.where(ok_m, halo[0], 0.0)
        out[1] = jnp.where(ok_e, halo[1], 0.0)
        out[2] = jnp.where(ok_m, halo_second, 0.0)
        out[3] = delta
        out[4], out[5] = near
        out[6], out[7] = second

        def turned(pair, beside):
            m, e = pair
            return (1.0 - OMEGA) * m + k0 * (
                coef[0] * beside_dense(m) + coef[2] * beside_lanes_main(m, e) + coef[1] * beside
            )

        first = turned(near, second[0] + halo_m)
        next_one = turned(second, near[0])
        third = k0 * coef[1] * second[0]
        for k, change in enumerate((near[0] + first, second[0] + next_one, third)):
            lines[0] = change
            y = y + jnp.where(row == order[k], k0 * lines[0, at, :], 0.0)
        for change in (first + next_one, third):
            lines[0] = change
            both = lines[0, pl.ds(H, W1, stride=2), :] + lines[0, pl.ds(H + 1, W1, stride=2), :]
            lows.append(both[: W1 // 2])
            highs.append(both[W1 // 2 :])
    add = halved(jnp.concatenate(lows, 0), jnp.concatenate(highs, 0))
    half = W * C // 8
    message[0:half, :] = coarse[...]
    for k, c1 in enumerate((C1 - 1, C1 - 2, 0, 1)):
        spot = pl.ds(c1, W1 // 2, stride=C1)
        message[spot, :] = message[spot, :] + add[k * (W1 // 2) : (k + 1) * (W1 // 2)]
    patch = ids[0]
    message[half : half + C, :] = patch.astype(F32)
    wide = sums.shape[0]
    if wide > electrodes:
        sums[...] = jnp.zeros(sums.shape, F32)

    def one(e):
        sums[pl.ds(e, 1), :] = jnp.sum(jnp.where(patch == e, y, 0.0), axis=0, keepdims=True)

    loop(0, electrodes, one, 8)
    totals = lax.dot_general(
        jnp.ones((8, LANES), F32), sums[...], (((1,), (1,)), ((), ())), precision=HIGHEST, preferred_element_type=F32
    )
    message[half + C : half + C + 8, :] = jnp.zeros((8, LANES), F32)
    for t in range(wide // LANES):
        message[half + C + t : half + C + t + 1, :] = totals[0:1, t * LANES : (t + 1) * LANES]


def source_part(n_len, n_wall, C, bm, be, rows_n, rows_p, qm, mask, base_adj, base_pot, fm, fe, tm, te, hp):
    N = bm.shape[0] // C
    W = N - 2 * H
    length, wall = lax.axis_index("len"), lax.axis_index("wall")
    fm[...] = bm[...]
    fe[...] = be[...]
    for rows, near, second in ((rows_n, C - 1, C - 2), (rows_p, 0, 1)):
        for k, at in ((4, near), (6, second)):
            spot = pl.ds(at, N, stride=C)
            fm[spot, :] = fm[spot, :] + rows[k]
            fe[spot, :] = fe[spot, :] + rows[k + 1]
    coef, k0 = level_coef(0), level_step(0)
    rim = rim_lanes(lane_of((C, LANES)), length, n_len)

    def part(i):
        m, e = plane(fm, i, C), plane(fe, i, C)
        wm = plane(fm, i - 1, C) + plane(fm, i + 1, C)
        we = plane(fe, i - 1, C) + plane(fe, i + 1, C)
        lm, le = beside_lanes(m, e)
        at = pl.ds(i, 1)
        cm = beside_rows(m, rows_p[0, at, :], rows_n[0, at, :])
        ce = beside_rows(e, rows_p[1, at, :], rows_n[1, at, :])
        pm = k0 * ((2.0 - OMEGA) * m + k0 * (coef[0] * wm + coef[1] * cm + coef[2] * lm))
        pe = k0 * ((2.0 - OMEGA) * e + k0 * (coef[0] * we + coef[1] * ce + coef[2] * le))
        set_plane(tm, i, C, jnp.where(inside(i, wall, W, n_wall), pm, 0.0))
        set_plane(te, i, C, jnp.where(rim, pe, 0.0))

    loop(H - 1, N - H + 1, part, 2)
    for side, (rows, at) in enumerate(((rows_n, C - 1), (rows_p, 0))):
        m = rows[0]
        total = (
            coef[0] * beside_dense(m)
            + coef[1] * (rows[2] + dense(fm, at, N, C))
            + coef[2] * beside_lanes_main(m, rows[1])
        )
        hp[side] = k0 * ((2.0 - OMEGA) * m + k0 * total)
    row = lax.broadcasted_iota(jnp.int32, (C, LANES), 0)

    def finish(w):
        i = w + H
        m, e = plane(tm, i, C), plane(te, i, C)
        at = pl.ds(i, 1)
        wm = plane(tm, i - 1, C) + plane(tm, i + 1, C)
        cm = beside_rows(m, hp[1, at, :], hp[0, at, :])
        lm = beside_lanes_main(m, e)
        lam = plane(qm, i, C)
        lam = lam + jnp.where(row == C - 1, rows_n[3, at, :], 0.0) + jnp.where(row == 0, rows_p[3, at, :], 0.0)
        moved = 2.0 * sum(SI) * m - SI[0] * wm - SI[1] * cm - SI[2] * lm
        set_plane(base_adj, w, C, lam - DT * plane(mask, w, C) * moved)
        set_plane(base_pot, w, C, m)

    loop(0, W, finish, 2)


def halves(shape):
    lane = lane_of(shape)
    return lane, lane % (LANES // 2)


def compact(C, W, blocks, out, wall_out, sheet1, coarse2):
    n_blk = blocks.shape[0]
    W1, C1 = W // 2, C // 2
    half, start, middle = W1 // 2, W1 // 2 * C1, LANES // 2
    blk, length, wall = lax.axis_index("blk"), lax.axis_index("len"), lax.axis_index("wall")
    sums = jnp.zeros((8, LANES), F32)
    for d in range(n_blk):
        b = lax.rem(blk - d + n_blk, n_blk)
        for i in range(half):
            sheet1[i, pl.ds(pl.multiple_of(C1 * b, C1), C1), :] = blocks[d, i * C1 : (i + 1) * C1, :]
        out[pl.ds(pl.multiple_of(96 + C * b, C), C), :] = blocks[d, start : start + C, :]
        sums = sums + blocks[d, start + C : start + C + 8, :]
    out[160:168, :] = sums
    NC1 = sheet1.shape[1]
    lane, at = halves((NC1, LANES))
    low = lane < middle
    coef, k1 = level_coef(1), level_step(1)
    ends = pltpu.roll(sheet1[half - 1], middle, 1), pltpu.roll(sheet1[0], middle, 1)
    for q in range(half // 2):
        both = sheet1[2 * q] + sheet1[2 * q + 1]
        prev = sheet1[2 * q - 1] if q else jnp.where(low, 0.0, ends[0])
        after_it = sheet1[2 * q + 2] if 2 * q + 2 < half else jnp.where(low, ends[1], 0.0)
        c = pltpu.roll(both, 1, 0) + pltpu.roll(both, NC1 - 1, 0)
        l = jnp.where(at == 0, 0.0, pltpu.roll(both, 1, 1)) + jnp.where(
            at == middle - 1, 0.0, pltpu.roll(both, LANES - 1, 1)
        )
        left = (1.0 - OMEGA) * both + k1 * (coef[0] * (prev + both + after_it) + coef[1] * c + coef[2] * l)
        coarse2[q] = 0.125 * twins(left, 1)
    coarse2[half // 2] = 0.125 * twins(jnp.where(wall == 0, sheet1[half - 1], sheet1[0]), 1)
    rows2 = NC1 // 2
    lane2, at2 = halves((rows2, LANES))
    pick = lane2 - at2 + 2 * (at2 % (middle // 2))
    for p in range(half // 4):
        pair = [lanes_at(coarse2[2 * p + k, pl.ds(0, rows2, stride=2), :], pick) for k in range(2)]
        out[rows2 * p : rows2 * (p + 1), :] = jnp.where(at2 < middle // 2, pair[0], pair[1])
    beside = jnp.zeros((NC1, LANES), F32)
    base = jnp.where(length == 0, middle - H, 0)
    for i in range(half):
        turned = pltpu.roll(sheet1[i], lax.rem(H * i - base + LANES, LANES), 1)
        beside = jnp.where(at // H == i, turned, beside)
    index = lax.broadcasted_iota(jnp.int32, (8, LANES), 0) ^ 1
    line = beside + jnp.concatenate([rows_at(beside[t : t + 8], index) for t in range(0, NC1, 8)], 0)
    line = 0.125 * (line + pltpu.roll(line, LANES - H, 1))
    m = lane - 96
    spot = jnp.where(m < H, 8 * m, middle + 8 * (m - H)) + jnp.where(length == 0, H - 1, 0)
    line = lanes_at(line, jnp.clip(spot, 0, LANES - 1))
    beside = jnp.where(jnp.logical_and(m >= 0, m < 8), line, beside)
    out[32 : 32 + NC1, :] = beside
    face = coarse2[half // 2, pl.ds(0, rows2, stride=2), :]
    face = lanes_at(face, jnp.where(wall == 0, middle, 0) + 2 * (at2 % (middle // 2)))
    inner = jnp.logical_and(lane2 >= middle // 2, lane2 < middle)
    out[32 : 32 + rows2, :] = jnp.where(inner, face, beside[:rows2])
    inner_surface = jnp.where(low, sheet1[0], pltpu.roll(sheet1[1], middle, 1))
    outer_surface = jnp.where(low, pltpu.roll(sheet1[half - 2], middle, 1), sheet1[half - 1])
    out[64 : 64 + NC1, :] = jnp.where(wall == 0, inner_surface, outer_surface)
    wall_out[0:168, :] = out[...]
    last = jnp.where(low, pltpu.roll(sheet1[half - 1], middle, 1), sheet1[half - 2])
    wall_out[168 : 168 + NC1, :] = jnp.where(wall == 0, last, inner_surface)


def around(x, by):
    rows, lanes = x.shape
    lane = lane_of(x.shape)
    c = pltpu.roll(x, by, 0) + pltpu.roll(x, rows - by, 0)
    l = jnp.where(lane < by, 0.0, pltpu.roll(x, by, 1)) + jnp.where(
        lane >= lanes - by, 0.0, pltpu.roll(x, lanes - by, 1)
    )
    return c, l


def twins(x, by):
    rows, lanes = x.shape
    if lanes == LANES:
        index = lax.broadcasted_iota(jnp.int32, (8, LANES), 0) ^ by
        x = x + jnp.concatenate([rows_at(x[t : t + 8], index) for t in range(0, rows, 8)], 0)
        return x + lanes_at(x, lane_of(x.shape) ^ by)
    row = lax.broadcasted_iota(jnp.int32, x.shape, 0)
    lane = lane_of(x.shape)
    x = x + jnp.where((row & by) == 0, pltpu.roll(x, rows - by, 0), pltpu.roll(x, by, 0))
    return x + jnp.where((lane & by) == 0, pltpu.roll(x, lanes - by, 1), pltpu.roll(x, by, 1))


def solve(sizes, relative, compacted, C, W, *refs):
    n_blk, n_len, n_wall = sizes
    count = n_len * n_wall + compacted
    blocks, refs = refs[:count], refs[count:]
    base_adj, base_pot, mask, patches, adj_prev, potential, patch_grad = refs[:7]
    b1, x1, b2, x2, b3, x3, near, pm, pe, tm, te, adj_out, pot_out, sheet, briefs, sems = refs[7:]
    L = LANES
    W1, C1 = W // 2, C // 2
    planes, NC1, NL1 = b1.shape
    planes -= 2
    blk, length, wall = lax.axis_index("blk"), lax.axis_index("len"), lax.axis_index("wall")
    half = W1 // 2
    middle = LANES // 2
    lane8 = lane_of((C1, LANES))
    often = 8 if NC1 * NL1 <= 4096 else 1

    def blk_of(d):
        return lax.rem(blk - d + n_blk, n_blk) if relative else d

    def length_of(j):
        return (length + j) % n_len if n_len == 2 else j

    def wall_of(v):
        return (wall + v) % n_wall

    zero1 = jnp.zeros((NC1, NL1), F32)
    for ref in (b1, x1, b2, x2, b3, x3):
        ref[0] = zero1
        ref[ref.shape[0] - 1] = zero1

    if not compacted:
        for v in range(n_wall):
            wall_s = wall_of(v)
            mine = blocks[v * n_len : (v + 1) * n_len]

            def unpack(d):
                at = pl.ds(pl.multiple_of(C1 * blk_of(d), C1), C1)
                for t in range(n_len // 2):
                    one, two = mine[2 * t], mine[2 * t + 1]
                    for i in range(half):
                        a, b = one[d, i * C1 : (i + 1) * C1, :], two[d, i * C1 : (i + 1) * C1, :]
                        if n_len == 2:
                            a, b = jnp.where(length == 0, a, b), jnp.where(length == 0, b, a)
                        spot = 1 + wall_s * W1 + i
                        lanes = slice(t * LANES, (t + 1) * LANES)
                        b1[spot, at, lanes] = jnp.where(lane8 < middle, a, pltpu.roll(b, middle, 1))
                        b1[spot + half, at, lanes] = jnp.where(lane8 < middle, pltpu.roll(a, middle, 1), b)

            loop(0, n_blk, unpack, 4)
    if compacted:
        stack, len_brief, wall_brief, both_brief, own_brief = blocks
        lane8 = lane_of((C1, LANES))
        here8 = lane8 // middle == length
        here = lane_of((NC1, LANES)) // middle == length
        face_lane = jnp.where(length == 0, middle, middle - H)
        near8 = jnp.logical_and(lane8 >= face_lane, lane8 < face_lane + H)
        at_face = jnp.logical_and(lane_of((NC1, LANES)) >= face_lane, lane_of((NC1, LANES)) < face_lane + H)
        for d in range(n_blk):
            row = pl.multiple_of(C1 * blk_of(d), C1)
            beside = len_brief[pl.ds(32 + row, C1), :]
            for i in range(half):
                a = stack[d, i * C1 : (i + 1) * C1, :]
                b = pltpu.roll(a, middle, 1)
                for k, value in enumerate((jnp.where(length == 0, a, b), jnp.where(length == 0, b, a))):
                    turn = lax.rem(face_lane - H * i - middle * k + 2 * LANES, LANES)
                    rest = jnp.where(near8, pltpu.roll(beside, turn, 1), 0.0)
                    b1[1 + wall * W1 + i + half * k, pl.ds(row, C1), :] = jnp.where(here8, value, rest)

        def two_planes(tile):
            turned = pltpu.roll(tile, middle, 1)
            return jnp.where(length == 0, tile, turned), jnp.where(length == 0, turned, tile)

        beyond = two_planes(wall_brief[168 : 168 + NC1, :])
        beside = both_brief[32 : 32 + NC1, :]
        for k in range(2):
            off = jnp.where(wall == 0, H * k, middle + H * (half - 1 - k))
            rest = jnp.where(at_face, pltpu.roll(beside, lax.rem(face_lane - off + 2 * LANES, LANES), 1), 0.0)
            b1[jnp.where(wall == 0, 1 + W1 + k, W1 - k)] = jnp.where(here, beyond[k], rest)
        for k in range(2):
            theirs = two_planes(len_brief[64 : 64 + NC1, :])[1 - k]
            spot = jnp.where(wall == 0, 1, planes - 1) + k
            b1[spot] = jnp.where(here, b1[spot], theirs)
            ours = two_planes(wall_brief[64 : 64 + NC1, :])[k]
            theirs = two_planes(both_brief[64 : 64 + NC1, :])[1 - k]
            b1[jnp.where(wall == 0, planes - 1, 1) + k] = jnp.where(here, ours, theirs)
        first_half = length == 0
        for k in range(2):
            ours = jnp.where(wall == k, own_brief[0:64, :], wall_brief[0:64, :])
            theirs = jnp.where(wall == k, len_brief[0:64, :], both_brief[0:64, :])
            briefs[0, k] = jnp.where(first_half, ours, theirs)
            briefs[1, k] = jnp.where(first_half, theirs, ours)
        lane_8 = lane_of((8, LANES))
        quarter = middle // 2
        left_quarter = lane_8 % middle < quarter
        pairs_index = [lane_8 // 2, middle + lane_8 // 2]
        facing = jnp.logical_and(lane_8 >= middle - 2, lane_8 < middle + 2)
        coef1 = [level_step(1) * x for x in level_coef(1)]
        rows2 = NC1 // 2

        def merged(w, start):
            one, two = briefs[0, w, start : start + 8, :], briefs[1, w, start : start + 8, :]
            even = jnp.where(left_quarter, one, pltpu.roll(two, quarter, 1))
            odd = jnp.where(left_quarter, pltpu.roll(one, LANES - quarter, 1), two)
            return even, odd

        for w in range(n_wall):
            for t in range(rows2 // 8):
                lines = [briefs[h, w, pl.ds(32 + 16 * t, 8, stride=2), :] for h in range(2)]
                lines = [lanes_at(x, jnp.minimum(96 + lane_8 // 4, LANES - 1)) for x in lines]
                lines = coef1[2] * jnp.where(lane_8 % 4 < 2, lines[1], lines[0])
                for p in range(half // 4):
                    tiles = merged(w, rows2 * p + 8 * t)
                    for odd in range(2):
                        for high in range(2):
                            k = 2 * p + odd + half // 2 * high
                            value = lanes_at(tiles[odd], pairs_index[high])
                            line = pltpu.roll(lines, middle - 2 - 4 * k, 1)
                            value = value + jnp.where(facing, line, 0.0)
                            if k == (half - 1 if w == 0 else 0):
                                value = value + coef1[0] * lanes_at(merged(1 - w, 32 + 8 * t)[1], pairs_index[0])
                            for r in range(2):
                                b2[1 + w * half + k, pl.ds(16 * t + r, 8, stride=2), :] = value

    def total_of(x, wsum, level, by):
        coef = level_coef(level)
        c, l = around(x, by)
        return level_step(level) * (coef[0] * wsum + coef[1] * c + coef[2] * l)

    def left_pair(ref, i, level):
        both = ref[i] + ref[i + 1]
        return (1.0 - OMEGA) * both + total_of(both, ref[i - 1] + both + ref[i + 2], level, 2 ** (level - 1))

    def sweep(x_ref, b_ref, i, level):
        x = x_ref[i]
        total = total_of(x, x_ref[i - 1] + x_ref[i + 1], level, 2 ** (level - 1))
        return (1.0 - OMEGA) * x + level_step(level) * b_ref[i] + total

    def down1(q):
        b2[1 + q] = 0.125 * twins(left_pair(b1, 2 * q + 1, 1), 1)

    if not compacted:
        loop(0, planes // 2, down1, often)

    def down2(q):
        b3[1 + q] = 0.125 * twins(left_pair(b2, 2 * q + 1, 2), 2)

    loop(0, planes // 4, down2, often)

    deep = planes // 4
    k3 = level_step(3)

    x2[1 + deep] = zero1

    def start3(q):
        b = b3[1 + q]
        x2[1 + q] = k3 * ((2.0 - OMEGA) * b + total_of(b, b3[q] + b3[2 + q], 3, 4))

    loop(0, deep, start3, often)

    def sweep3(q):
        x3[1 + q] = sweep(x2, b3, 1 + q, 3)

    loop(0, deep, sweep3, often)
    k2 = level_step(2)

    def up2(q):
        coarse = x3[1 + q]
        x2[1 + 2 * q] = k2 * b2[1 + 2 * q] + coarse
        x2[2 + 2 * q] = k2 * b2[2 + 2 * q] + coarse

    loop(0, planes // 4, up2, often)

    k1 = level_step(1)

    def up1(q):
        fine = sweep(x2, b2, 1 + q, 2)
        x1[1 + 2 * q] = k1 * b1[1 + 2 * q] + fine
        x1[2 + 2 * q] = k1 * b1[2 + 2 * q] + fine

    if compacted:
        loop(0, half, lambda q: up1(half * wall + q), often)
        up1(half - wall)
        up1((planes // 2 - 1) * (1 - wall))
    else:
        loop(0, planes // 2, up1, often)

    Q = W1 + 2
    sectors = (blk, lax.rem(blk + 1, n_blk), lax.rem(blk + n_blk - 1, n_blk))
    spots3 = [pl.ds(pl.multiple_of(s * C1, C1), C1) for s in sectors]
    row8 = lax.broadcasted_iota(jnp.int32, (C1, NL1), 0)

    def three(ref, i):
        return jnp.concatenate([ref[i, s, :] for s in spots3], 0)

    def finish1(q):
        i = wall * W1 + q
        x = three(x1, i)
        wsum = three(x1, jnp.maximum(i - 1, 0)) + three(x1, jnp.minimum(i + 1, planes + 1))
        value = (1.0 - OMEGA) * x + k1 * three(b1, i) + total_of(x, wsum, 1, 1)
        value = jnp.where(jnp.logical_and(i >= 1, i <= planes), value, 0.0)
        set_plane(near, 2 * q, C1, value[:C1])
        set_plane(near, 2 * q + 1, C1, jnp.where(row8 < 2, value[C1 : 2 * C1], value[2 * C1 :]))

    loop(0, Q, finish1, min(often, 6))

    first = length * middle
    R = C + 8
    row8 = lax.broadcasted_iota(jnp.int32, (8, LANES), 0)
    tile_lane = lane_of((8, LANES))
    at_e = jnp.where(tile_lane < H, middle + tile_lane // 2, tile_lane // 2 - middle)
    rim8 = rim_lanes(tile_lane, length, n_len)
    if NL1 == LANES:
        index_m, index_e = first + tile_lane // 2, jnp.clip(first + at_e, 0, LANES - 1)

        def spread(tile):
            return lanes_at(tile, index_m), jnp.where(rim8, lanes_at(tile, index_e), 0.0)

    else:
        source = lax.broadcasted_iota(jnp.int32, (NL1, LANES), 0)
        lane = lane_of((NL1, LANES))
        at_all = jnp.where(lane < H, middle + lane // 2, jnp.where(lane >= LANES - H, lane // 2 - middle, 4 * NL1))
        take_m = jnp.where(source == first + lane // 2, 1.0, 0.0).astype(F32)
        take_e = jnp.where(source == first + at_all, 1.0, 0.0).astype(F32)

        def spread(tile):
            return precise(tile, take_m), precise(tile, take_e)

    picks = (row8 // 2, H + row8 // 2)
    ends = jnp.where(row8 < H, 6 + row8 // 2, row8 // 2 - 2)

    def fine_rows(q):
        own = spread(plane(near, 2 * q, C1))
        beside = spread(plane(near, 2 * q + 1, C1))
        for out, a, b in ((pm, own[0], beside[0]), (pe, own[1], beside[1])):
            parts = (jnp.where(row8 < 6, a, b), a, jnp.where(row8 < 2, b, a))
            index = (ends, 2 + row8 // 2, ends)
            for k in range(3):
                out[pl.ds(pl.multiple_of(8 + R * q + 8 * k, 8), 8), :] = rows_at(parts[k], index[k])

    loop(0, Q, fine_rows, min(often, 6))
    for ref in (pm, pe):
        ref[0:8, :] = jnp.zeros((8, LANES), F32)
        ref[8 + R * Q : 16 + R * Q, :] = jnp.zeros((8, LANES), F32)
    coef, k0 = level_coef(0), level_step(0)
    def fine(ref, t, by=0, count=R):
        return ref[pl.ds(8 + R * t + by, count), :]

    def coarse_terms(q):
        out = []
        sides = beside_lanes(fine(pm, q), fine(pe, q))
        for ref, l in zip((pm, pe), sides):
            x = fine(ref, q)
            c = fine(ref, q, -1) + fine(ref, q, 1)
            out.append((1.0 - OMEGA) * x + k0 * (coef[0] * x + coef[1] * c + coef[2] * l))
        return out

    ks = k0 * coef[0]

    def set_fine(ref, t, value):
        ref[pl.ds(pl.multiple_of(8 + R * t, 8), R), :] = value

    def put_end(t, q, other, ok):
        set_fine(tm, t, jnp.where(ok, coarse_terms(q)[0] + ks * fine(pm, other), 0.0))

    put_end(0, 0, 1, wall > 0)
    put_end(W + 1, Q - 1, Q - 2, wall < n_wall - 1)
    rim = rim_lanes(lane_of((R, LANES)), length, n_len)

    def level0(q):
        gm, ge = coarse_terms(q)
        for t, other in ((2 * q - 1, q - 1), (2 * q, q + 1)):
            set_fine(tm, t, gm + ks * fine(pm, other))
            set_fine(te, t, jnp.where(rim, ge + ks * fine(pe, other), 0.0))

    loop(1, 1 + W1, level0, 4)

    def finish0(w):
        t = w + 1
        m, e = fine(tm, t, H, C), fine(te, t, H, C)
        cm = fine(tm, t, H - 1, C) + fine(tm, t, H + 1, C)
        wm = fine(tm, t - 1, H, C) + fine(tm, t + 1, H, C)
        lm = beside_lanes_main(m, e)
        moved = 2.0 * sum(SI) * m - SI[0] * wm - SI[1] * cm - SI[2] * lm
        set_plane(adj_out, w, C, plane(base_adj, w, C) - DT * plane(mask, w, C) * moved)
        set_plane(pot_out, w, C, plane(base_pot, w, C) + m)

    parts = 2
    size = W // parts
    copies = []
    for k in range(parts):
        loop(k * size, (k + 1) * size, finish0, 4)
        spot = pl.ds(k * size * C, size * C)
        for n, (src, dst) in enumerate(((adj_out, adj_prev), (pot_out, potential))):
            copies.append(pltpu.make_async_copy(src.at[spot], dst.at[spot], sems.at[n, k]))
            copies[-1].start()

    NC, NL = sheet.shape[1:]

    def whole_fine(x):
        if NL1 == LANES:
            parts = []
            for t in range(0, NC1, 8):
                wide8 = [lanes_at(x[t : t + 8], tile_lane // 2 + k * middle) for k in range(2)]
                for pick in picks[:2]:
                    parts.append(jnp.concatenate([rows_at(v, pick) for v in wide8], 1))
            return jnp.concatenate(parts, 0)
        along_c = lax.broadcasted_iota(jnp.int32, (NC, NC1), 0) // 2
        along_l = lax.broadcasted_iota(jnp.int32, (NL1, NL), 1) // 2
        twice_c = jnp.where(along_c == lax.broadcasted_iota(jnp.int32, (NC, NC1), 1), 1.0, 0.0).astype(F32)
        twice_l = jnp.where(along_l == lax.broadcasted_iota(jnp.int32, (NL1, NL), 0), 1.0, 0.0).astype(F32)
        return precise(precise(twice_c, x), twice_l)

    for s, i in enumerate((1, planes)):
        p = whole_fine(sweep(x1, b1, i, 1))
        c, l = around(p, 1)
        sheet[s] = (1.0 - OMEGA) * p + k0 * (coef[0] * p + coef[1] * c + coef[2] * l)

    owned = [patches[r : r + 1, :] for r in range(2)]
    spot = lax.broadcasted_iota(jnp.int32, (8, LANES), 0) * LANES + lane_of((8, LANES))
    spot = spot.astype(F32)
    start = half * C1
    totals = [jnp.zeros((C, LANES), F32) for _ in owned]
    small = [jnp.zeros((8, LANES), F32) for _ in owned]
    for v in range(n_wall):
        wall_s = wall_of(v)
        for j in range(n_len):
            ref = blocks[v * n_len + j]
            at_l = pl.ds(pl.multiple_of(length_of(j) * L, L), L)
            if compacted and v + j:
                for b in range(n_blk):
                    values = sheet[wall_s, b * C : (b + 1) * C, at_l]
                    ids = ref[96 + b * C : 96 + (b + 1) * C, :]
                    totals = [x + jnp.where(ids == e, values, 0.0) for x, e in zip(totals, owned)]
                small = [x + jnp.where(spot == e, ref[160:168, :], 0.0) for x, e in zip(small, owned)]
                continue

            def add(d, carry):
                big, little = carry
                values = sheet[wall_s, pl.ds(pl.multiple_of(blk_of(d) * C, C), C), at_l]
                ids = ref[d, start : start + C, :]
                parts = ref[d, start + C : start + C + 8, :]
                big = [x + jnp.where(ids == e, values, 0.0) for x, e in zip(big, owned)]
                little = [x + jnp.where(spot == e, parts, 0.0) for x, e in zip(little, owned)]
                return big, little

            totals, small = lax.fori_loop(0, n_blk, add, (totals, small), unroll=min(4, n_blk))
    factor = 1.0 / (2.0 * C * L / 2) ** 0.5
    for r in range(2):
        patch_grad[0, r] = (jnp.sum(totals[r]) + jnp.sum(small[r])) * factor
    for copy in copies:
        copy.wait()


def ring(x, axis, by):
    count = lax.axis_size(axis)
    return lax.ppermute(x, axis, [(i, (i + by) % count) for i in range(count)])


def across(x):
    n_wall = lax.axis_size("wall")
    pairs = [(l * n_wall + w, (1 - l) * n_wall + (w + 1) % n_wall) for l in range(2) for w in range(n_wall)]
    return lax.ppermute(x, ("len", "wall"), pairs)


def call(kernel, ins, outs, scratch, name, work=0, room=48):
    places = {"vmem": pltpu.VMEM, "smem": pltpu.SMEM, "any": pl.ANY, "hbm": pltpu.HBM}

    def specs(kinds):
        return [pl.BlockSpec(memory_space=places[kind]) for kind in kinds]

    cost = pl.CostEstimate(flops=work, bytes_accessed=work, transcendentals=0) if work else None
    return pl.pallas_call(
        kernel,
        out_shape=[jax.ShapeDtypeStruct(shape, F32) for shape, _ in outs],
        in_specs=specs(ins),
        out_specs=specs(kind for _, kind in outs),
        scratch_shapes=[pltpu.VMEM(shape, F32) if isinstance(shape, tuple) else shape for shape in scratch],
        compiler_params=pltpu.CompilerParams(vmem_limit_bytes=int(room * 2**20)),
        cost_estimate=cost,
        name=name,
    )


def body(adj_next, ion_slope, misfit, tissue_mask, patch_ids, owner_map):
    W, C, L = adj_next.shape
    n_blk, n_len, n_wall = lax.axis_size("blk"), lax.axis_size("len"), lax.axis_size("wall")
    electrodes = owner_map.shape[0]
    assert L == LANES and H * W == LANES and n_wall == 2 and electrodes == 2 * n_blk * n_len * n_wall
    N = W + 2 * H
    n_dir = 1 if n_len == 2 else 2
    cells = W * C
    vmem = "vmem"
    field, own = (N * C, L), (cells, L)
    raw = [x.reshape(cells, L) for x in (adj_next, ion_slope, tissue_mask, misfit)]

    *fields, wall_out = (faces := call(
        functools.partial(pack_faces, n_len),
        ["hbm"] * 4,
        [(own, vmem)] * 4
        + [((sum(FACES), C, L), vmem)]
        + [((4, C, L), vmem)] * n_dir
        + [((C, L), vmem)] * n_dir,
        [pltpu.VMEM(own, jnp.int32), pltpu.SemaphoreType.DMA((4, 4))],
        "faces",
        room=52.75,
    )(*raw))[:5]
    strip_out, corner_out = faces[5 : 5 + n_dir], faces[5 + n_dir :]
    wall_in = ring(wall_out, "wall", 1)
    if n_dir == 1:
        strips = [ring(strip_out[0], "len", 1)]
        corners = [across(corner_out[0])]
    else:
        strips = [ring(strip_out[1], "len", -1), ring(strip_out[0], "len", 1)]
        corners = [ring(ring(corner_out[1], "wall", 1), "len", -1), ring(ring(corner_out[0], "wall", 1), "len", 1)]

    near = (sum(near_rows(n_dir, W)[-1][::2]), L)
    halos = [wall_in, *strips, *corners]
    to_next, to_prev, own_rows = call(
        functools.partial(boundary, n_len, C),
        [vmem] * (5 + 2 * n_dir),
        [(near, vmem)] * 2 + [((2, 6, N, L), vmem)],
        [(48, N, L)],
        "boundary",
    )(*fields, *halos)
    from_next = ring(to_prev, "blk", -1)
    from_prev = ring(to_next, "blk", 1)
    qm, bm, be, coarse, surface, patches = call(
        functools.partial(sector, n_len, n_wall, C, electrodes),
        [vmem] * (6 + 2 * n_dir),
        [(field, vmem)] * 3 + [((cells // 8, L), vmem), ((C, L), vmem), ((8, L), vmem)],
        [field, (cells // 2, L)] + [field] * 8,
        "sector",
        work=16 * 10**6,
    )(*fields, *halos, owner_map.reshape(1, electrodes))

    rows = (8, N, L)
    wide = LANES * ((electrodes + LANES - 1) // LANES)
    message = (cells // 8 + C + 8, L)
    rows_n, rows_p, mine = call(
        functools.partial(correct, electrodes, n_len, n_wall),
        [vmem] * 6,
        [(rows, vmem), (rows, vmem), (message, vmem)],
        [(1, N, L), (wide, L)],
        "correct",
    )(own_rows, from_next, from_prev, coarse, surface, patch_ids)

    relative = n_blk <= 4
    moved = [ring(mine, "blk", d) for d in range(1, n_blk)] if relative else [lax.all_gather(mine, "blk")]
    base_adj, base_pot = call(
        functools.partial(source_part, n_len, n_wall, C),
        [vmem] * 6,
        [(own, vmem), (own, vmem)],
        [field] * 4 + [(2, N, L)],
        "source_part",
        work=12 * 10**6,
    )(bm, be, rows_n, rows_p, qm, fields[2])
    moved, base_adj = lax.optimization_barrier((moved, base_adj))
    sector_blocks = jnp.stack([mine] + moved) if relative else moved[0]
    compacted = (n_blk, n_len, C, W) == (4, 2, 16, 32)
    if compacted:
        brief, across_wall = call(
            functools.partial(compact, C, W),
            [vmem],
            [((168, L), vmem), ((200, L), vmem)],
            [(W // 4, n_blk * C // 2, L), (W // 8 + 1, n_blk * C // 2, L)],
            "compact",
        )(sector_blocks)
        len_brief = ring(brief, "len", 1)
        blocks = [sector_blocks, len_brief, ring(across_wall, "wall", 1), ring(len_brief, "wall", 1), brief]
    elif n_len == 2:
        here = [sector_blocks, ring(sector_blocks, "len", 1)]
    else:
        gathered = lax.all_gather(sector_blocks, "len")
        here = [gathered[j] for j in range(n_len)]
    if not compacted:
        blocks = here + [ring(x, "wall", 1) for x in here]

    NC1, NL1 = n_blk * C // 2, n_len * L // 2
    planes = n_wall * W // 2
    grids = [(planes // k + 2, NC1, NL1) for k in (1, 1, 2, 2, 4, 4)]
    Q = W // 2 + 2
    tall = (Q * (C + 8) + 16, L)
    taller = ((W + 2) * (C + 8) + 16, L)
    scratch = grids + [(Q * C, NL1), tall, tall, taller, taller, own, own]
    scratch += [(2, n_blk * C, n_len * L), (2, 2, 64, L), pltpu.SemaphoreType.DMA((2, 2))]
    adj_prev, potential, patch_grad = call(
        functools.partial(solve, (n_blk, n_len, n_wall), relative, compacted, C, W),
        [vmem] * (len(blocks) + 4),
        [(own, "any"), (own, "any"), ((1, 2), "smem")],
        scratch,
        "solve",
        room=48 if NC1 * NL1 <= 4096 else 58,
    )(*blocks, base_adj, base_pot, fields[2], patches)
    return adj_prev.reshape(W, C, L), potential.reshape(W, C, L), patch_grad


def solution(mesh):
    field = P(("groups", "wall"), "blk", "len")
    return jax.shard_map(
        body,
        mesh=mesh,
        in_specs=(field, field, field, field, field, P("groups")),
        out_specs=(field, field, P(("groups", "blk", "len", "wall"), None)),
        check_vma=False,
    )
```

```python
import functools

import jax
import jax.numpy as jnp
from jax import lax
from jax.experimental import pallas as pl
from jax.experimental.pallas import tpu as pltpu
from jax.sharding import PartitionSpec as P

SI = (0.6, 1.0, 3.0)
SE = (0.8, 1.2, 2.0)
SHIFT = 0.002
OMEGA = 0.8
DT = 0.1
H = 4
LANES = 128
HIGHEST = lax.Precision.HIGHEST
F32 = jnp.float32


def level_coef(level):
    return tuple((SI[i] + SE[i]) / 4.0**level for i in range(3))


def level_diag(level):
    return SHIFT + 2.0 * sum(level_coef(level))


def level_step(level):
    return OMEGA / level_diag(level)


def lane_of(shape):
    return lax.broadcasted_iota(jnp.int32, shape, len(shape) - 1)


def before(m, e):
    first = lane_of(m.shape) == 0
    rm, re = pltpu.roll(m, 1, 1), pltpu.roll(e, 1, 1)
    return jnp.where(first, re, rm), jnp.where(first, rm, re)


def after(m, e):
    last = lane_of(m.shape) == LANES - 1
    rm, re = pltpu.roll(m, LANES - 1, 1), pltpu.roll(e, LANES - 1, 1)
    return jnp.where(last, re, rm), jnp.where(last, rm, re)


def beside_lanes(m, e):
    bm, be = before(m, e)
    am, ae = after(m, e)
    return bm + am, be + ae


def beside_lanes_main(m, e):
    lane = lane_of(m.shape)
    ends = lanes_at(e, LANES - 1 - lane)
    left = jnp.where(lane == 0, ends, pltpu.roll(m, 1, 1))
    right = jnp.where(lane == LANES - 1, ends, pltpu.roll(m, LANES - 1, 1))
    return left + right


def beside_rows(x, row_before, row_after):
    rows = x.shape[0]
    row = lax.broadcasted_iota(jnp.int32, x.shape, 0)
    low = jnp.where(row == 0, row_before, pltpu.roll(x, 1, 0))
    high = jnp.where(row == rows - 1, row_after, pltpu.roll(x, rows - 1, 0))
    return low + high


def beside_dense(x):
    return pltpu.roll(x, 1, 0) + pltpu.roll(x, x.shape[0] - 1, 0)


def plane(ref, i, rows):
    return ref[pl.ds(pl.multiple_of(i * rows, rows), rows), :]


def set_plane(ref, i, rows, value):
    ref[pl.ds(pl.multiple_of(i * rows, rows), rows), :] = value


def loop(low, high, step, unroll):
    def wrapped(i, carry):
        step(i)
        return carry

    lax.fori_loop(low, high, wrapped, 0, unroll=min(unroll, high - low))


FACES = (H, H - 1, H - 1, H - 2)


def face_planes(array):
    return FACES[array], sum(FACES[:array])


def pack_faces(n_len, adj, ion, mask, mis, *rest):
    n_dir = 1 if n_len == 2 else 2
    fields, wall_out, rest = rest[:4], rest[4], rest[5:]
    strips, corners = rest[:n_dir], rest[n_dir : 2 * n_dir]
    whole_mask, sems = rest[2 * n_dir :]
    cells = adj.shape[0]
    C = wall_out.shape[1]
    W = cells // C
    wall, length = lax.axis_index("wall"), lax.axis_index("len")
    targets = (fields[0], fields[1], whole_mask, fields[3])
    copies = []
    for a, (src, dst) in enumerate(zip((adj, ion, mask, mis), targets)):
        part = cells // 4
        for k in range(4):
            spot = pl.ds(k * part, part)
            copies.append(pltpu.make_async_copy(src.at[spot], dst.at[spot], sems.at[a, k]))
            copies[-1].start()

    base = jnp.where(wall == 0, W - H, 0)
    group = lane_of((C, LANES)) // H
    turns = [jnp.where(length == 0, H, 0)] if n_dir == 1 else [H, 0]
    corner = [jnp.zeros((C, LANES), F32) for _ in range(n_dir)]
    for a in (0, 1, 3, 2):
        for k in range(4):
            copies[4 * a + k].wait()
        if a == 2:
            fields[2][...] = whole_mask[...].astype(F32)
        ref = fields[a]
        strip = [jnp.zeros((C, LANES), F32) for _ in range(n_dir)]
        for w in range(W):
            value = ref[w * C : (w + 1) * C, :]
            for d in range(n_dir):
                turned = pltpu.roll(value, lax.rem(H * w + turns[d], LANES), 1)
                strip[d] = jnp.where(group == w, turned, strip[d])
        for d in range(n_dir):
            strips[d][a] = strip[d]
        count, first = face_planes(a)
        for p in range(count):
            face = plane(ref, base + jnp.where(wall == 0, H - count, 0) + p, C)
            wall_out[first + p] = face
            slot = first + p
            for d in range(n_dir):
                turned = pltpu.roll(face, lax.rem(H * slot + turns[d], LANES), 1)
                corner[d] = jnp.where(group == slot, turned, corner[d])
    for d in range(n_dir):
        corners[d][...] = corner[d]


def dense(ref, row, N, C):
    return ref[pl.ds(row, N, stride=C), :]


def dense_pair(m, e, row, N, C):
    return dense(m, row, N, C), dense(e, row, N, C)


def dense_apply(pair, inner, outer, coef):
    m, e = pair
    lm, le = beside_lanes(m, e)
    double = 2.0 * sum(coef)
    out = [double * m - coef[0] * beside_dense(m) - coef[2] * lm, double * e - coef[0] * beside_dense(e) - coef[2] * le]
    for row in (inner, outer):
        if row is not None:
            out = [out[k] - coef[1] * row[k] for k in range(2)]
    return out


def near_rows(n_dir, W):
    start, places = 8 * n_dir, []
    for reach in (0, 1, 2, 2, 3):
        places.append((start, H - reach, W + 2 * reach))
        start += W + 2 * reach
    assert start % 8 == 0
    return places


def rim_tiles(values):
    return [value[s : s + 8] for value in values for s in range(0, value.shape[0], 8)]


def rim_places(n_len, length):
    if n_len == 2:
        return [(jnp.where(length == 0, 0, LANES - H), True)]
    return [(0, length < n_len - 1), (LANES - H, length > 0)]


def boundary(n_len, C, *refs):
    n_dir = 1 if n_len == 2 else 2
    raw, wall_in, refs = refs[:4], refs[4], refs[5:]
    strips, corners, refs = refs[:n_dir], refs[n_dir : 2 * n_dir], refs[2 * n_dir :]
    to_next, to_prev, own_rows, build = refs
    W = raw[0].shape[0] // C
    N = W + 2 * H
    wall, length = lax.axis_index("wall"), lax.axis_index("len")
    places = rim_places(n_len, length)

    def strip_rows(packed, first, count):
        lane, k = lane_of((count, LANES)), lax.broadcasted_iota(jnp.int32, (count, LANES), 0)
        out = jnp.zeros((count, LANES), F32)
        for row, (off, ok) in zip(packed, places):
            j = lax.rem(lane - off + LANES, LANES)
            index = jnp.clip(H * (first + k) + j, 0, LANES - 1)
            taken = lanes_at(jnp.broadcast_to(row, (count, LANES)), index)
            out = jnp.where(jnp.logical_and(j < H, ok), taken, out)
        return out

    slots = iter(range(build.shape[0]))

    def assembled(own, halo, count):
        ref = build.at[next(slots)]
        ref[0:8, :] = jnp.zeros((8, LANES), F32)
        ref[N - 8 : N, :] = jnp.zeros((8, LANES), F32)
        ref[H : H + W, :] = own
        ref[H - count : H, :] = jnp.where(wall == 0, 0.0, halo)
        ref[H + W : H + W + count, :] = jnp.where(wall == 0, halo, 0.0)
        return ref[...]

    def row_of(a, r):
        count, first = face_planes(a)
        halo = jnp.concatenate([wall_in[first + p, r : r + 1, :] for p in range(count)], 0)
        m = assembled(raw[a][pl.ds(r, W, stride=C), :], halo, count)
        own = strip_rows([strip[a, r : r + 1, :] for strip in strips], 0, W)
        halo = strip_rows([corner[r : r + 1, :] for corner in corners], first, 8)[:count]
        return m, assembled(own, halo, count)

    length_shift = jnp.where(length == 0, 0, H) if n_dir == 1 else H
    group = lane_of((8, LANES)) // (H * n_dir)
    for side, (out, order) in enumerate(((to_next, (C - 1, C - 2, C - 3, C - 4)), (to_prev, (0, 1, 2, 3)))):
        adj = [row_of(0, r) for r in order]
        mask = [row_of(2, r) for r in order[:3]]
        q = []
        for k in range(3):
            ion = row_of(1, order[k])
            moved = dense_apply(adj[k], adj[k + 1], adj[k - 1] if k else None, SI)
            q.append([adj[k][j] - DT * mask[k][j] * (moved[j] + ion[j] * adj[k][j]) for j in range(2)])
        near = dense_apply(q[0], q[1], None, SI)
        mis = row_of(3, order[0])
        near = [near[j] + mis[j] for j in range(2)]
        second = dense_apply(q[1], q[2], q[0], SI)[0] + row_of(3, order[1])[0]
        for value, (start, first, count) in zip((second, near[0], q[0][0], mask[0][0], adj[0][0]), near_rows(n_dir, W)):
            out[start : start + count, :] = value[first : first + count]
        packs = [jnp.zeros((8, LANES), F32) for _ in range(n_dir)]
        for t, tile in enumerate(rim_tiles((near[1], q[0][1], mask[0][1], adj[0][1]))):
            k, at = divmod(t, LANES // (H * n_dir))
            turned = pltpu.roll(tile, lax.rem(length_shift + H * n_dir * at, LANES), 1)
            packs[k] = jnp.where(group == at, turned, packs[k])
        for k in range(n_dir):
            out[8 * k : 8 * k + 8, :] = packs[k]
        for k, pair in enumerate((adj[0], mask[0], q[0])):
            own_rows[side, 2 * k] = pair[0]
            own_rows[side, 2 * k + 1] = pair[1]


def spots(m_ref, e_ref, i, rows, coef):
    m, e = plane(m_ref, i, rows), plane(e_ref, i, rows)
    wm = plane(m_ref, i - 1, rows) + plane(m_ref, i + 1, rows)
    we = plane(e_ref, i - 1, rows) + plane(e_ref, i + 1, rows)
    lm, le = beside_lanes(m, e)
    cm, ce = beside_rows(m, 0.0, 0.0), beside_rows(e, 0.0, 0.0)
    double = 2.0 * sum(coef)
    dm = double * m - coef[0] * wm - coef[1] * cm - coef[2] * lm
    de = double * e - coef[0] * we - coef[1] * ce - coef[2] * le
    return m, e, dm, de


def rim_lanes(lane, length, n_len):
    return jnp.logical_or(
        jnp.logical_and(lane < H, length < n_len - 1),
        jnp.logical_and(lane >= LANES - H, length > 0),
    )


def inside(i, wall, W, n_wall):
    w = wall * W + i - H
    return jnp.logical_and(w >= 0, w < n_wall * W)


def lanes_at(x, index):
    return jnp.take_along_axis(x, index, axis=1, mode="promise_in_bounds")


def rows_at(x, index):
    return jnp.take_along_axis(x, index, axis=0, mode="promise_in_bounds")


def halved(low, high):
    lane = lane_of(low.shape)
    even = 2 * lane % LANES
    pairs = [lanes_at(x, even) + lanes_at(x, even + 1) for x in (low, high)]
    return 0.125 * jnp.where(lane < LANES // 2, pairs[0], pairs[1])


def precise(a, b):
    return jnp.dot(a, b, precision=HIGHEST, preferred_element_type=F32)


def assemble(n_len, C, raw, wall_in, strips, corners, xm, xe):
    W = raw[0].shape[0] // C
    N = W + 2 * H
    wall, length = lax.axis_index("wall"), lax.axis_index("len")
    lane = lane_of((C, LANES))
    places = rim_places(n_len, length)
    seen = [jnp.logical_and(lax.rem(lane - off + LANES, LANES) < H, ok) for off, ok in places]

    def rim(packed, base):
        out = jnp.zeros((C, LANES), F32)
        for row, ok, (off, _) in zip(packed, seen, places):
            out = jnp.where(ok, pltpu.roll(row, lax.rem(off - base + LANES, LANES), 1), out)
        return out

    zero = jnp.zeros((C, LANES), F32)
    last = N - H
    for a, own in enumerate(raw):
        packed = [strip[a] for strip in strips]
        for w in range(W):
            set_plane(xm[a], w + H, C, plane(own, w, C))
            set_plane(xe[a], w + H, C, rim(packed, H * w))
        packed = [corner[...] for corner in corners]
        for i in range(H):
            for at in (i, last + i):
                set_plane(xm[a], at, C, zero)
                set_plane(xe[a], at, C, zero)
        count, first = face_planes(a)
        here = jnp.where(wall == 0, last, H - count)
        for p in range(count):
            set_plane(xm[a], here + p, C, wall_in[first + p])
            set_plane(xe[a], here + p, C, rim(packed, H * (first + p)))


def sector(n_len, n_wall, C, electrodes, *refs):
    n_dir = 1 if n_len == 2 else 2
    raw, wall_in, refs = refs[:4], refs[4], refs[5:]
    strips, corners, refs = refs[:n_dir], refs[n_dir : 2 * n_dir], refs[2 * n_dir :]
    owner, qm, bm, be, coarse, surface, patches, qe, pairs = refs[:9]
    xm, xe = refs[9:13], refs[13:17]
    assemble(n_len, C, raw, wall_in, strips, corners, xm, xe)
    N = qm.shape[0] // C
    W = N - 2 * H
    wall, length = lax.axis_index("wall"), lax.axis_index("len")
    rim = rim_lanes(lane_of((C, LANES)), length, n_len)
    zero = jnp.zeros((C, LANES), F32)
    for i in (0, N - 1):
        set_plane(qm, i, C, zero)
        set_plane(qe, i, C, zero)
    for i in (0, 1, N - 2, N - 1):
        set_plane(bm, i, C, zero)
        set_plane(be, i, C, zero)

    def parabolic(i):
        m, e, dm, de = spots(xm[0], xe[0], i, C, SI)
        set_plane(qm, i, C, m - DT * plane(xm[2], i, C) * (dm + plane(xm[1], i, C) * m))
        set_plane(qe, i, C, e - DT * plane(xe[2], i, C) * (de + plane(xe[1], i, C) * e))

    loop(1, N - 1, parabolic, 2)

    def elliptic_source(i):
        m, e, dm, de = spots(qm, qe, i, C, SI)
        ok = inside(i, wall, W, n_wall)
        set_plane(bm, i, C, jnp.where(ok, plane(xm[3], i, C) + dm, 0.0))
        set_plane(be, i, C, jnp.where(jnp.logical_and(rim, ok), plane(xe[3], i, C) + de, 0.0))

    loop(2, N - 2, elliptic_source, 2)

    coef, k0 = level_coef(0), level_step(0)

    def left(i):
        m, e = plane(bm, i, C), plane(be, i, C)
        wm = plane(bm, i - 1, C) + plane(bm, i + 1, C)
        cm = beside_rows(m, 0.0, 0.0)
        lm = beside_lanes_main(m, e)
        return m, (1.0 - OMEGA) * m + k0 * (coef[0] * wm + coef[1] * cm + coef[2] * lm)

    def pair(q):
        i = 2 * q + H
        m, first = left(i)
        n, second = left(i + 1)
        set_plane(pairs, q, C, first + second)

        @pl.when(jnp.logical_and(q == 0, wall == 0))
        def _():
            surface[...] = k0 * (m + first)

        @pl.when(jnp.logical_and(q == W // 2 - 1, wall == n_wall - 1))
        def _():
            surface[...] = k0 * (n + second)

    loop(0, W // 2, pair, 2)

    half = W * C // 8
    z = pairs[pl.ds(0, 2 * half, stride=2), :] + pairs[pl.ds(1, 2 * half, stride=2), :]
    coarse[...] = halved(z[:half], z[half:])

    blk = lax.axis_index("blk")
    me = (blk * n_len + length) * n_wall + wall
    which = lax.broadcasted_iota(jnp.int32, (1, electrodes), 1).astype(F32)
    mine = owner[...] == me
    patches[0:1, :] = jnp.full((1, LANES), jnp.min(jnp.where(mine, which, float(electrodes))))
    patches[1:2, :] = jnp.full((1, LANES), jnp.max(jnp.where(mine, which, -1.0)))
    patches[2:8, :] = jnp.zeros((6, LANES), F32)


def unpacked(ref, n_len, length, N):
    n_dir = 1 if n_len == 2 else 2
    mains = []
    for start, first, count in near_rows(n_dir, N - 2 * H):
        begin = min(start - first, ref.shape[0] - N)
        value = ref[begin : begin + N, :]
        behind = start - first - begin
        mains.append(pltpu.roll(value, N - behind, 0) if behind else value)
    rim = rim_lanes(lane_of((8, LANES)), length, n_len)
    shift = jnp.where(length == 0, 0, H) if n_dir == 1 else H
    rims = []
    for k in range(4):
        parts = []
        for s in range(N // 8):
            pack, at = divmod(k * (N // 8) + s, LANES // (H * n_dir))
            back = lax.rem(2 * LANES - shift - H * n_dir * at, LANES)
            parts.append(jnp.where(rim, pltpu.roll(ref[8 * pack : 8 * pack + 8, :], back, 1), 0.0))
        rims.append(jnp.concatenate(parts, 0))
    second, near, q, mask, adj = mains
    return (adj, rims[3]), (mask, rims[2]), (q, rims[1]), (near, rims[0]), second


def lateral(pair):
    return dense_apply(pair, None, None, SI)


def source_rows(own, other):
    adj_o, mask_o, q_o = own
    adj_n, mask_n, q_n, p_n, second_n = other
    step = DT * SI[1]
    delta_o = [step * mask_o[k] * adj_n[k] for k in range(2)]
    delta_n = [step * mask_n[k] * adj_o[k] for k in range(2)]
    lat_o, lat_n = lateral(delta_o), lateral(delta_n)
    near = [lat_o[k] - SI[1] * (q_n[k] + delta_n[k]) for k in range(2)]
    second = [-SI[1] * delta_o[k] for k in range(2)]
    halo = [p_n[k] + lat_n[k] - SI[1] * (q_o[k] + delta_o[k]) for k in range(2)]
    halo_second = second_n - SI[1] * delta_n[0]
    return near, second, halo, halo_second, delta_o[0]


def correct(electrodes, n_len, n_wall, own_rows, from_next, from_prev, coarse, surface, ids, *rest):
    rows_n, rows_p, message = rest[:3]
    lines, sums = rest[3:]
    _, C, L = ids.shape
    N = own_rows.shape[2]
    W = N - 2 * H
    wall, length = lax.axis_index("wall"), lax.axis_index("len")
    ok_m = inside(lax.broadcasted_iota(jnp.int32, (N, LANES), 0), wall, W, n_wall)
    ok_e = jnp.logical_and(ok_m, rim_lanes(lane_of((N, LANES)), length, n_len))
    coef, k0 = level_coef(0), level_step(0)
    y = surface[...]
    row = lax.broadcasted_iota(jnp.int32, (C, LANES), 0)
    at = pl.ds(jnp.where(wall == 0, H, W + H - 1), 1)
    lows, highs = [], []
    W1, C1 = W // 2, C // 2
    for side, (other, out, order) in enumerate(
        ((from_next, rows_n, (C - 1, C - 2, C - 3)), (from_prev, rows_p, (0, 1, 2)))
    ):
        own = [(own_rows[side, 2 * k], own_rows[side, 2 * k + 1]) for k in range(3)]
        near, second, halo, halo_second, delta = source_rows(own, unpacked(other, n_len, length, N))
        near = [jnp.where(ok_m, near[0], 0.0), jnp.where(ok_e, near[1], 0.0)]
        second = [jnp.where(ok_m, second[0], 0.0), jnp.where(ok_e, second[1], 0.0)]
        out[0] = halo_m = jnp.where(ok_m, halo[0], 0.0)
        out[1] = jnp.where(ok_e, halo[1], 0.0)
        out[2] = jnp.where(ok_m, halo_second, 0.0)
        out[3] = delta
        out[4], out[5] = near
        out[6], out[7] = second

        def turned(pair, beside):
            m, e = pair
            return (1.0 - OMEGA) * m + k0 * (
                coef[0] * beside_dense(m) + coef[2] * beside_lanes_main(m, e) + coef[1] * beside
            )

        first = turned(near, second[0] + halo_m)
        next_one = turned(second, near[0])
        third = k0 * coef[1] * second[0]
        for k, change in enumerate((near[0] + first, second[0] + next_one, third)):
            lines[0] = change
            y = y + jnp.where(row == order[k], k0 * lines[0, at, :], 0.0)
        for change in (first + next_one, third):
            lines[0] = change
            both = lines[0, pl.ds(H, W1, stride=2), :] + lines[0, pl.ds(H + 1, W1, stride=2), :]
            lows.append(both[: W1 // 2])
            highs.append(both[W1 // 2 :])
    add = halved(jnp.concatenate(lows, 0), jnp.concatenate(highs, 0))
    half = W * C // 8
    message[0:half, :] = coarse[...]
    for k, c1 in enumerate((C1 - 1, C1 - 2, 0, 1)):
        spot = pl.ds(c1, W1 // 2, stride=C1)
        message[spot, :] = message[spot, :] + add[k * (W1 // 2) : (k + 1) * (W1 // 2)]
    patch = ids[0]
    message[half : half + C, :] = patch.astype(F32)
    wide = sums.shape[0]
    if wide > electrodes:
        sums[...] = jnp.zeros(sums.shape, F32)

    def one(e):
        sums[pl.ds(e, 1), :] = jnp.sum(jnp.where(patch == e, y, 0.0), axis=0, keepdims=True)

    loop(0, electrodes, one, 8)
    totals = lax.dot_general(
        jnp.ones((8, LANES), F32), sums[...], (((1,), (1,)), ((), ())), precision=HIGHEST, preferred_element_type=F32
    )
    message[half + C : half + C + 8, :] = jnp.zeros((8, LANES), F32)
    for t in range(wide // LANES):
        message[half + C + t : half + C + t + 1, :] = totals[0:1, t * LANES : (t + 1) * LANES]


def source_part(n_len, n_wall, C, bm, be, rows_n, rows_p, qm, mask, base_adj, base_pot, fm, fe, tm, te, hp):
    N = bm.shape[0] // C
    W = N - 2 * H
    length, wall = lax.axis_index("len"), lax.axis_index("wall")
    fm[...] = bm[...]
    fe[...] = be[...]
    for rows, near, second in ((rows_n, C - 1, C - 2), (rows_p, 0, 1)):
        for k, at in ((4, near), (6, second)):
            spot = pl.ds(at, N, stride=C)
            fm[spot, :] = fm[spot, :] + rows[k]
            fe[spot, :] = fe[spot, :] + rows[k + 1]
    coef, k0 = level_coef(0), level_step(0)
    rim = rim_lanes(lane_of((C, LANES)), length, n_len)

    def part(i):
        m, e = plane(fm, i, C), plane(fe, i, C)
        wm = plane(fm, i - 1, C) + plane(fm, i + 1, C)
        we = plane(fe, i - 1, C) + plane(fe, i + 1, C)
        lm, le = beside_lanes(m, e)
        at = pl.ds(i, 1)
        cm = beside_rows(m, rows_p[0, at, :], rows_n[0, at, :])
        ce = beside_rows(e, rows_p[1, at, :], rows_n[1, at, :])
        pm = k0 * ((2.0 - OMEGA) * m + k0 * (coef[0] * wm + coef[1] * cm + coef[2] * lm))
        pe = k0 * ((2.0 - OMEGA) * e + k0 * (coef[0] * we + coef[1] * ce + coef[2] * le))
        set_plane(tm, i, C, jnp.where(inside(i, wall, W, n_wall), pm, 0.0))
        set_plane(te, i, C, jnp.where(rim, pe, 0.0))

    loop(H - 1, N - H + 1, part, 2)
    for side, (rows, at) in enumerate(((rows_n, C - 1), (rows_p, 0))):
        m = rows[0]
        total = (
            coef[0] * beside_dense(m)
            + coef[1] * (rows[2] + dense(fm, at, N, C))
            + coef[2] * beside_lanes_main(m, rows[1])
        )
        hp[side] = k0 * ((2.0 - OMEGA) * m + k0 * total)
    row = lax.broadcasted_iota(jnp.int32, (C, LANES), 0)

    def finish(w):
        i = w + H
        m, e = plane(tm, i, C), plane(te, i, C)
        at = pl.ds(i, 1)
        wm = plane(tm, i - 1, C) + plane(tm, i + 1, C)
        cm = beside_rows(m, hp[1, at, :], hp[0, at, :])
        lm = beside_lanes_main(m, e)
        lam = plane(qm, i, C)
        lam = lam + jnp.where(row == C - 1, rows_n[3, at, :], 0.0) + jnp.where(row == 0, rows_p[3, at, :], 0.0)
        moved = 2.0 * sum(SI) * m - SI[0] * wm - SI[1] * cm - SI[2] * lm
        set_plane(base_adj, w, C, lam - DT * plane(mask, w, C) * moved)
        set_plane(base_pot, w, C, m)

    loop(0, W, finish, 2)


def halves(shape):
    lane = lane_of(shape)
    return lane, lane % (LANES // 2)


def compact(C, W, blocks, out, wall_out, sheet1, coarse2):
    n_blk = blocks.shape[0]
    W1, C1 = W // 2, C // 2
    half, start, middle = W1 // 2, W1 // 2 * C1, LANES // 2
    blk, length, wall = lax.axis_index("blk"), lax.axis_index("len"), lax.axis_index("wall")
    sums = jnp.zeros((8, LANES), F32)
    for d in range(n_blk):
        b = lax.rem(blk - d + n_blk, n_blk)
        for i in range(half):
            sheet1[i, pl.ds(pl.multiple_of(C1 * b, C1), C1), :] = blocks[d, i * C1 : (i + 1) * C1, :]
        out[pl.ds(pl.multiple_of(96 + C * b, C), C), :] = blocks[d, start : start + C, :]
        sums = sums + blocks[d, start + C : start + C + 8, :]
    out[160:168, :] = sums
    NC1 = sheet1.shape[1]
    lane, at = halves((NC1, LANES))
    low = lane < middle
    coef, k1 = level_coef(1), level_step(1)
    ends = pltpu.roll(sheet1[half - 1], middle, 1), pltpu.roll(sheet1[0], middle, 1)
    for q in range(half // 2):
        both = sheet1[2 * q] + sheet1[2 * q + 1]
        prev = sheet1[2 * q - 1] if q else jnp.where(low, 0.0, ends[0])
        after_it = sheet1[2 * q + 2] if 2 * q + 2 < half else jnp.where(low, ends[1], 0.0)
        c = pltpu.roll(both, 1, 0) + pltpu.roll(both, NC1 - 1, 0)
        l = jnp.where(at == 0, 0.0, pltpu.roll(both, 1, 1)) + jnp.where(
            at == middle - 1, 0.0, pltpu.roll(both, LANES - 1, 1)
        )
        left = (1.0 - OMEGA) * both + k1 * (coef[0] * (prev + both + after_it) + coef[1] * c + coef[2] * l)
        coarse2[q] = 0.125 * twins(left, 1)
    coarse2[half // 2] = 0.125 * twins(jnp.where(wall == 0, sheet1[half - 1], sheet1[0]), 1)
    rows2 = NC1 // 2
    lane2, at2 = halves((rows2, LANES))
    pick = lane2 - at2 + 2 * (at2 % (middle // 2))
    for p in range(half // 4):
        pair = [lanes_at(coarse2[2 * p + k, pl.ds(0, rows2, stride=2), :], pick) for k in range(2)]
        out[rows2 * p : rows2 * (p + 1), :] = jnp.where(at2 < middle // 2, pair[0], pair[1])
    beside = jnp.zeros((NC1, LANES), F32)
    base = jnp.where(length == 0, middle - H, 0)
    for i in range(half):
        turned = pltpu.roll(sheet1[i], lax.rem(H * i - base + LANES, LANES), 1)
        beside = jnp.where(at // H == i, turned, beside)
    index = lax.broadcasted_iota(jnp.int32, (8, LANES), 0) ^ 1
    line = beside + jnp.concatenate([rows_at(beside[t : t + 8], index) for t in range(0, NC1, 8)], 0)
    line = 0.125 * (line + pltpu.roll(line, LANES - H, 1))
    m = lane - 96
    spot = jnp.where(m < H, 8 * m, middle + 8 * (m - H)) + jnp.where(length == 0, H - 1, 0)
    line = lanes_at(line, jnp.clip(spot, 0, LANES - 1))
    beside = jnp.where(jnp.logical_and(m >= 0, m < 8), line, beside)
    out[32 : 32 + NC1, :] = beside
    face = coarse2[half // 2, pl.ds(0, rows2, stride=2), :]
    face = lanes_at(face, jnp.where(wall == 0, middle, 0) + 2 * (at2 % (middle // 2)))
    inner = jnp.logical_and(lane2 >= middle // 2, lane2 < middle)
    out[32 : 32 + rows2, :] = jnp.where(inner, face, beside[:rows2])
    inner_surface = jnp.where(low, sheet1[0], pltpu.roll(sheet1[1], middle, 1))
    outer_surface = jnp.where(low, pltpu.roll(sheet1[half - 2], middle, 1), sheet1[half - 1])
    out[64 : 64 + NC1, :] = jnp.where(wall == 0, inner_surface, outer_surface)
    wall_out[0:168, :] = out[...]
    last = jnp.where(low, pltpu.roll(sheet1[half - 1], middle, 1), sheet1[half - 2])
    wall_out[168 : 168 + NC1, :] = jnp.where(wall == 0, last, inner_surface)


def around(x, by):
    rows, lanes = x.shape
    lane = lane_of(x.shape)
    c = pltpu.roll(x, by, 0) + pltpu.roll(x, rows - by, 0)
    l = jnp.where(lane < by, 0.0, pltpu.roll(x, by, 1)) + jnp.where(
        lane >= lanes - by, 0.0, pltpu.roll(x, lanes - by, 1)
    )
    return c, l


def twins(x, by):
    rows, lanes = x.shape
    if lanes == LANES:
        index = lax.broadcasted_iota(jnp.int32, (8, LANES), 0) ^ by
        x = x + jnp.concatenate([rows_at(x[t : t + 8], index) for t in range(0, rows, 8)], 0)
        return x + lanes_at(x, lane_of(x.shape) ^ by)
    row = lax.broadcasted_iota(jnp.int32, x.shape, 0)
    lane = lane_of(x.shape)
    x = x + jnp.where((row & by) == 0, pltpu.roll(x, rows - by, 0), pltpu.roll(x, by, 0))
    return x + jnp.where((lane & by) == 0, pltpu.roll(x, lanes - by, 1), pltpu.roll(x, by, 1))


def solve(sizes, relative, compacted, C, W, *refs):
    n_blk, n_len, n_wall = sizes
    count = n_len * n_wall + compacted
    blocks, refs = refs[:count], refs[count:]
    base_adj, base_pot, mask, patches, adj_prev, potential, patch_grad = refs[:7]
    b1, x1, b2, x2, b3, x3, near, pm, pe, tm, te, adj_out, pot_out, sheet, briefs, sems = refs[7:]
    L = LANES
    W1, C1 = W // 2, C // 2
    planes, NC1, NL1 = b1.shape
    planes -= 2
    blk, length, wall = lax.axis_index("blk"), lax.axis_index("len"), lax.axis_index("wall")
    half = W1 // 2
    middle = LANES // 2
    lane8 = lane_of((C1, LANES))
    often = 4 if NC1 * NL1 <= 4096 else 1

    def blk_of(d):
        return lax.rem(blk - d + n_blk, n_blk) if relative else d

    def length_of(j):
        return (length + j) % n_len if n_len == 2 else j

    def wall_of(v):
        return (wall + v) % n_wall

    zero1 = jnp.zeros((NC1, NL1), F32)
    for ref in (b1, x1, b2, x2, b3, x3):
        ref[0] = zero1
        ref[ref.shape[0] - 1] = zero1

    if not compacted:
        for v in range(n_wall):
            wall_s = wall_of(v)
            mine = blocks[v * n_len : (v + 1) * n_len]

            def unpack(d):
                at = pl.ds(pl.multiple_of(C1 * blk_of(d), C1), C1)
                for t in range(n_len // 2):
                    one, two = mine[2 * t], mine[2 * t + 1]
                    for i in range(half):
                        a, b = one[d, i * C1 : (i + 1) * C1, :], two[d, i * C1 : (i + 1) * C1, :]
                        if n_len == 2:
                            a, b = jnp.where(length == 0, a, b), jnp.where(length == 0, b, a)
                        spot = 1 + wall_s * W1 + i
                        lanes = slice(t * LANES, (t + 1) * LANES)
                        b1[spot, at, lanes] = jnp.where(lane8 < middle, a, pltpu.roll(b, middle, 1))
                        b1[spot + half, at, lanes] = jnp.where(lane8 < middle, pltpu.roll(a, middle, 1), b)

            loop(0, n_blk, unpack, 4)
    if compacted:
        stack, len_brief, wall_brief, both_brief, own_brief = blocks
        lane8 = lane_of((C1, LANES))
        here8 = lane8 // middle == length
        here = lane_of((NC1, LANES)) // middle == length
        face_lane = jnp.where(length == 0, middle, middle - H)
        near8 = jnp.logical_and(lane8 >= face_lane, lane8 < face_lane + H)
        at_face = jnp.logical_and(lane_of((NC1, LANES)) >= face_lane, lane_of((NC1, LANES)) < face_lane + H)
        def unpack_mine(d):
            row = pl.multiple_of(C1 * blk_of(d), C1)
            beside = len_brief[pl.ds(32 + row, C1), :]
            for i in range(half):
                a = stack[d, i * C1 : (i + 1) * C1, :]
                b = pltpu.roll(a, middle, 1)
                for k, value in enumerate((jnp.where(length == 0, a, b), jnp.where(length == 0, b, a))):
                    turn = lax.rem(face_lane - H * i - middle * k + 2 * LANES, LANES)
                    rest = jnp.where(near8, pltpu.roll(beside, turn, 1), 0.0)
                    b1[1 + wall * W1 + i + half * k, pl.ds(row, C1), :] = jnp.where(here8, value, rest)

        loop(0, n_blk, unpack_mine, 1)

        def two_planes(tile):
            turned = pltpu.roll(tile, middle, 1)
            return jnp.where(length == 0, tile, turned), jnp.where(length == 0, turned, tile)

        beyond = two_planes(wall_brief[168 : 168 + NC1, :])
        beside = both_brief[32 : 32 + NC1, :]
        for k in range(2):
            off = jnp.where(wall == 0, H * k, middle + H * (half - 1 - k))
            rest = jnp.where(at_face, pltpu.roll(beside, lax.rem(face_lane - off + 2 * LANES, LANES), 1), 0.0)
            b1[jnp.where(wall == 0, 1 + W1 + k, W1 - k)] = jnp.where(here, beyond[k], rest)
        for k in range(2):
            theirs = two_planes(len_brief[64 : 64 + NC1, :])[1 - k]
            spot = jnp.where(wall == 0, 1, planes - 1) + k
            b1[spot] = jnp.where(here, b1[spot], theirs)
            ours = two_planes(wall_brief[64 : 64 + NC1, :])[k]
            theirs = two_planes(both_brief[64 : 64 + NC1, :])[1 - k]
            b1[jnp.where(wall == 0, planes - 1, 1) + k] = jnp.where(here, ours, theirs)
        first_half = length == 0
        for k in range(2):
            ours = jnp.where(wall == k, own_brief[0:64, :], wall_brief[0:64, :])
            theirs = jnp.where(wall == k, len_brief[0:64, :], both_brief[0:64, :])
            briefs[0, k] = jnp.where(first_half, ours, theirs)
            briefs[1, k] = jnp.where(first_half, theirs, ours)
        lane_8 = lane_of((8, LANES))
        quarter = middle // 2
        left_quarter = lane_8 % middle < quarter
        pairs_index = [lane_8 // 2, middle + lane_8 // 2]
        facing = jnp.logical_and(lane_8 >= middle - 2, lane_8 < middle + 2)
        coef1 = [level_step(1) * x for x in level_coef(1)]
        rows2 = NC1 // 2

        def merged(w, start):
            at = pl.ds(pl.multiple_of(start, 8), 8)
            one, two = briefs[0, w, at, :], briefs[1, w, at, :]
            even = jnp.where(left_quarter, one, pltpu.roll(two, quarter, 1))
            odd = jnp.where(left_quarter, pltpu.roll(one, LANES - quarter, 1), two)
            return even, odd

        def fill(n):
            w, t = n // 2, n % 2
            lines = [briefs[h, w, pl.ds(32 + 16 * t, 8, stride=2), :] for h in range(2)]
            lines = [lanes_at(x, jnp.minimum(96 + lane_8 // 4, LANES - 1)) for x in lines]
            lines = coef1[2] * jnp.where(lane_8 % 4 < 2, lines[1], lines[0])
            for p in range(half // 4):
                tiles = merged(w, rows2 * p + 8 * t)
                for odd in range(2):
                    for high in range(2):
                        k = 2 * p + odd + half // 2 * high
                        value = lanes_at(tiles[odd], pairs_index[high])
                        value = value + jnp.where(facing, pltpu.roll(lines, middle - 2 - 4 * k, 1), 0.0)
                        for r in range(2):
                            b2[1 + w * half + k, pl.ds(16 * t + r, 8, stride=2), :] = value
            value = coef1[0] * lanes_at(merged(1 - w, 32 + 8 * t)[1], pairs_index[0])
            for r in range(2):
                at = pl.ds(16 * t + r, 8, stride=2)
                b2[half + w, at, :] = b2[half + w, at, :] + value

        assert rows2 == 16 and n_wall == 2
        loop(0, 4, fill, 1)

    def total_of(x, wsum, level, by):
        coef = level_coef(level)
        c, l = around(x, by)
        return level_step(level) * (coef[0] * wsum + coef[1] * c + coef[2] * l)

    def left_pair(ref, i, level):
        both = ref[i] + ref[i + 1]
        return (1.0 - OMEGA) * both + total_of(both, ref[i - 1] + both + ref[i + 2], level, 2 ** (level - 1))

    def sweep(x_ref, b_ref, i, level):
        x = x_ref[i]
        total = total_of(x, x_ref[i - 1] + x_ref[i + 1], level, 2 ** (level - 1))
        return (1.0 - OMEGA) * x + level_step(level) * b_ref[i] + total

    def down1(q):
        b2[1 + q] = 0.125 * twins(left_pair(b1, 2 * q + 1, 1), 1)

    if not compacted:
        loop(0, planes // 2, down1, often)

    def down2(q):
        b3[1 + q] = 0.125 * twins(left_pair(b2, 2 * q + 1, 2), 2)

    loop(0, planes // 4, down2, often)

    deep = planes // 4
    k3 = level_step(3)

    x2[1 + deep] = zero1

    def start3(q):
        b = b3[1 + q]
        x2[1 + q] = k3 * ((2.0 - OMEGA) * b + total_of(b, b3[q] + b3[2 + q], 3, 4))

    loop(0, deep, start3, often)

    def sweep3(q):
        x3[1 + q] = sweep(x2, b3, 1 + q, 3)

    loop(0, deep, sweep3, often)
    k2 = level_step(2)

    def up2(q):
        coarse = x3[1 + q]
        x2[1 + 2 * q] = k2 * b2[1 + 2 * q] + coarse
        x2[2 + 2 * q] = k2 * b2[2 + 2 * q] + coarse

    loop(0, planes // 4, up2, often)

    k1 = level_step(1)

    def up1(q):
        fine = sweep(x2, b2, 1 + q, 2)
        x1[1 + 2 * q] = k1 * b1[1 + 2 * q] + fine
        x1[2 + 2 * q] = k1 * b1[2 + 2 * q] + fine

    if compacted:
        loop(0, half, lambda q: up1(half * wall + q), often)
        up1(half - wall)
        up1((planes // 2 - 1) * (1 - wall))
    else:
        loop(0, planes // 2, up1, often)

    Q = W1 + 2
    sectors = (blk, lax.rem(blk + 1, n_blk), lax.rem(blk + n_blk - 1, n_blk))
    spots3 = [pl.ds(pl.multiple_of(s * C1, C1), C1) for s in sectors]
    row8 = lax.broadcasted_iota(jnp.int32, (C1, NL1), 0)

    def three(ref, i):
        return jnp.concatenate([ref[i, s, :] for s in spots3], 0)

    def finish1(q):
        i = wall * W1 + q
        x = three(x1, i)
        wsum = three(x1, jnp.maximum(i - 1, 0)) + three(x1, jnp.minimum(i + 1, planes + 1))
        value = (1.0 - OMEGA) * x + k1 * three(b1, i) + total_of(x, wsum, 1, 1)
        value = jnp.where(jnp.logical_and(i >= 1, i <= planes), value, 0.0)
        set_plane(near, 2 * q, C1, value[:C1])
        set_plane(near, 2 * q + 1, C1, jnp.where(row8 < 2, value[C1 : 2 * C1], value[2 * C1 :]))

    loop(0, Q, finish1, min(often, 6))

    first = length * middle
    R = C + 8
    row8 = lax.broadcasted_iota(jnp.int32, (8, LANES), 0)
    tile_lane = lane_of((8, LANES))
    at_e = jnp.where(tile_lane < H, middle + tile_lane // 2, tile_lane // 2 - middle)
    rim8 = rim_lanes(tile_lane, length, n_len)
    if NL1 == LANES:
        index_m, index_e = first + tile_lane // 2, jnp.clip(first + at_e, 0, LANES - 1)

        def spread(tile):
            return lanes_at(tile, index_m), jnp.where(rim8, lanes_at(tile, index_e), 0.0)

    else:
        source = lax.broadcasted_iota(jnp.int32, (NL1, LANES), 0)
        lane = lane_of((NL1, LANES))
        at_all = jnp.where(lane < H, middle + lane // 2, jnp.where(lane >= LANES - H, lane // 2 - middle, 4 * NL1))
        take_m = jnp.where(source == first + lane // 2, 1.0, 0.0).astype(F32)
        take_e = jnp.where(source == first + at_all, 1.0, 0.0).astype(F32)

        def spread(tile):
            return precise(tile, take_m), precise(tile, take_e)

    picks = (row8 // 2, H + row8 // 2)
    ends = jnp.where(row8 < H, 6 + row8 // 2, row8 // 2 - 2)

    def fine_rows(q):
        own = spread(plane(near, 2 * q, C1))
        beside = spread(plane(near, 2 * q + 1, C1))
        for out, a, b in ((pm, own[0], beside[0]), (pe, own[1], beside[1])):
            parts = (jnp.where(row8 < 6, a, b), a, jnp.where(row8 < 2, b, a))
            index = (ends, 2 + row8 // 2, ends)
            for k in range(3):
                out[pl.ds(pl.multiple_of(8 + R * q + 8 * k, 8), 8), :] = rows_at(parts[k], index[k])

    loop(0, Q, fine_rows, min(often, 6))
    for ref in (pm, pe):
        ref[0:8, :] = jnp.zeros((8, LANES), F32)
        ref[8 + R * Q : 16 + R * Q, :] = jnp.zeros((8, LANES), F32)
    coef, k0 = level_coef(0), level_step(0)
    def fine(ref, t, by=0, count=R):
        return ref[pl.ds(8 + R * t + by, count), :]

    def coarse_terms(q):
        out = []
        sides = beside_lanes(fine(pm, q), fine(pe, q))
        for ref, l in zip((pm, pe), sides):
            x = fine(ref, q)
            c = fine(ref, q, -1) + fine(ref, q, 1)
            out.append((1.0 - OMEGA) * x + k0 * (coef[0] * x + coef[1] * c + coef[2] * l))
        return out

    ks = k0 * coef[0]

    def set_fine(ref, t, value):
        ref[pl.ds(pl.multiple_of(8 + R * t, 8), R), :] = value

    def put_end(t, q, other, ok):
        set_fine(tm, t, jnp.where(ok, coarse_terms(q)[0] + ks * fine(pm, other), 0.0))

    put_end(0, 0, 1, wall > 0)
    put_end(W + 1, Q - 1, Q - 2, wall < n_wall - 1)
    rim = rim_lanes(lane_of((R, LANES)), length, n_len)

    def level0(q):
        gm, ge = coarse_terms(q)
        for t, other in ((2 * q - 1, q - 1), (2 * q, q + 1)):
            set_fine(tm, t, gm + ks * fine(pm, other))
            set_fine(te, t, jnp.where(rim, ge + ks * fine(pe, other), 0.0))

    loop(1, 1 + W1, level0, 4)

    def finish0(w):
        t = w + 1
        m, e = fine(tm, t, H, C), fine(te, t, H, C)
        cm = fine(tm, t, H - 1, C) + fine(tm, t, H + 1, C)
        wm = fine(tm, t - 1, H, C) + fine(tm, t + 1, H, C)
        lm = beside_lanes_main(m, e)
        moved = 2.0 * sum(SI) * m - SI[0] * wm - SI[1] * cm - SI[2] * lm
        set_plane(adj_out, w, C, plane(base_adj, w, C) - DT * plane(mask, w, C) * moved)
        set_plane(pot_out, w, C, plane(base_pot, w, C) + m)

    parts = 2
    size = W // parts
    copies = []
    for k in range(parts):
        loop(k * size, (k + 1) * size, finish0, 4)
        spot = pl.ds(k * size * C, size * C)
        for n, (src, dst) in enumerate(((adj_out, adj_prev), (pot_out, potential))):
            copies.append(pltpu.make_async_copy(src.at[spot], dst.at[spot], sems.at[n, k]))
            copies[-1].start()

    NC, NL = sheet.shape[1:]

    def whole_fine(x):
        if NL1 == LANES:
            parts = []
            for t in range(0, NC1, 8):
                wide8 = [lanes_at(x[t : t + 8], tile_lane // 2 + k * middle) for k in range(2)]
                for pick in picks[:2]:
                    parts.append(jnp.concatenate([rows_at(v, pick) for v in wide8], 1))
            return jnp.concatenate(parts, 0)
        along_c = lax.broadcasted_iota(jnp.int32, (NC, NC1), 0) // 2
        along_l = lax.broadcasted_iota(jnp.int32, (NL1, NL), 1) // 2
        twice_c = jnp.where(along_c == lax.broadcasted_iota(jnp.int32, (NC, NC1), 1), 1.0, 0.0).astype(F32)
        twice_l = jnp.where(along_l == lax.broadcasted_iota(jnp.int32, (NL1, NL), 0), 1.0, 0.0).astype(F32)
        return precise(precise(twice_c, x), twice_l)

    for s, i in enumerate((1, planes)):
        p = whole_fine(sweep(x1, b1, i, 1))
        c, l = around(p, 1)
        sheet[s] = (1.0 - OMEGA) * p + k0 * (coef[0] * p + coef[1] * c + coef[2] * l)

    owned = [patches[r : r + 1, :] for r in range(2)]
    spot = lax.broadcasted_iota(jnp.int32, (8, LANES), 0) * LANES + lane_of((8, LANES))
    spot = spot.astype(F32)
    start = half * C1
    totals = [jnp.zeros((C, LANES), F32) for _ in owned]
    small = [jnp.zeros((8, LANES), F32) for _ in owned]
    for v in range(n_wall):
        wall_s = wall_of(v)
        for j in range(n_len):
            ref = blocks[v * n_len + j]
            at_l = pl.ds(pl.multiple_of(length_of(j) * L, L), L)
            if compacted and v + j:
                for b in range(n_blk):
                    values = sheet[wall_s, b * C : (b + 1) * C, at_l]
                    ids = ref[96 + b * C : 96 + (b + 1) * C, :]
                    totals = [x + jnp.where(ids == e, values, 0.0) for x, e in zip(totals, owned)]
                small = [x + jnp.where(spot == e, ref[160:168, :], 0.0) for x, e in zip(small, owned)]
                continue

            def add(d, carry):
                big, little = carry
                values = sheet[wall_s, pl.ds(pl.multiple_of(blk_of(d) * C, C), C), at_l]
                ids = ref[d, start : start + C, :]
                parts = ref[d, start + C : start + C + 8, :]
                big = [x + jnp.where(ids == e, values, 0.0) for x, e in zip(big, owned)]
                little = [x + jnp.where(spot == e, parts, 0.0) for x, e in zip(little, owned)]
                return big, little

            totals, small = lax.fori_loop(0, n_blk, add, (totals, small), unroll=min(4, n_blk))
    factor = 1.0 / (2.0 * C * L / 2) ** 0.5
    for r in range(2):
        patch_grad[0, r] = (jnp.sum(totals[r]) + jnp.sum(small[r])) * factor
    for copy in copies:
        copy.wait()


def ring(x, axis, by):
    count = lax.axis_size(axis)
    return lax.ppermute(x, axis, [(i, (i + by) % count) for i in range(count)])


def across(x):
    n_wall = lax.axis_size("wall")
    pairs = [(l * n_wall + w, (1 - l) * n_wall + (w + 1) % n_wall) for l in range(2) for w in range(n_wall)]
    return lax.ppermute(x, ("len", "wall"), pairs)


def call(kernel, ins, outs, scratch, name, work=0, room=48):
    places = {"vmem": pltpu.VMEM, "smem": pltpu.SMEM, "any": pl.ANY, "hbm": pltpu.HBM}

    def specs(kinds):
        return [pl.BlockSpec(memory_space=places[kind]) for kind in kinds]

    cost = pl.CostEstimate(flops=work, bytes_accessed=work, transcendentals=0) if work else None
    return pl.pallas_call(
        kernel,
        out_shape=[jax.ShapeDtypeStruct(shape, F32) for shape, _ in outs],
        in_specs=specs(ins),
        out_specs=specs(kind for _, kind in outs),
        scratch_shapes=[pltpu.VMEM(shape, F32) if isinstance(shape, tuple) else shape for shape in scratch],
        compiler_params=pltpu.CompilerParams(vmem_limit_bytes=int(room * 2**20)),
        cost_estimate=cost,
        name=name,
    )


def body(adj_next, ion_slope, misfit, tissue_mask, patch_ids, owner_map):
    W, C, L = adj_next.shape
    n_blk, n_len, n_wall = lax.axis_size("blk"), lax.axis_size("len"), lax.axis_size("wall")
    electrodes = owner_map.shape[0]
    assert L == LANES and H * W == LANES and n_wall == 2 and electrodes == 2 * n_blk * n_len * n_wall
    N = W + 2 * H
    n_dir = 1 if n_len == 2 else 2
    cells = W * C
    vmem = "vmem"
    field, own = (N * C, L), (cells, L)
    raw = [x.reshape(cells, L) for x in (adj_next, ion_slope, tissue_mask, misfit)]

    *fields, wall_out = (faces := call(
        functools.partial(pack_faces, n_len),
        ["hbm"] * 4,
        [(own, vmem)] * 4
        + [((sum(FACES), C, L), vmem)]
        + [((4, C, L), vmem)] * n_dir
        + [((C, L), vmem)] * n_dir,
        [pltpu.VMEM(own, jnp.int32), pltpu.SemaphoreType.DMA((4, 4))],
        "faces",
        room=52.75,
    )(*raw))[:5]
    strip_out, corner_out = faces[5 : 5 + n_dir], faces[5 + n_dir :]
    wall_in = ring(wall_out, "wall", 1)
    if n_dir == 1:
        strips = [ring(strip_out[0], "len", 1)]
        corners = [across(corner_out[0])]
    else:
        strips = [ring(strip_out[1], "len", -1), ring(strip_out[0], "len", 1)]
        corners = [ring(ring(corner_out[1], "wall", 1), "len", -1), ring(ring(corner_out[0], "wall", 1), "len", 1)]

    near = (sum(near_rows(n_dir, W)[-1][::2]), L)
    halos = [wall_in, *strips, *corners]
    to_next, to_prev, own_rows = call(
        functools.partial(boundary, n_len, C),
        [vmem] * (5 + 2 * n_dir),
        [(near, vmem)] * 2 + [((2, 6, N, L), vmem)],
        [(48, N, L)],
        "boundary",
    )(*fields, *halos)
    from_next = ring(to_prev, "blk", -1)
    from_prev = ring(to_next, "blk", 1)
    qm, bm, be, coarse, surface, patches = call(
        functools.partial(sector, n_len, n_wall, C, electrodes),
        [vmem] * (6 + 2 * n_dir),
        [(field, vmem)] * 3 + [((cells // 8, L), vmem), ((C, L), vmem), ((8, L), vmem)],
        [field, (cells // 2, L)] + [field] * 8,
        "sector",
        work=16 * 10**6,
    )(*fields, *halos, owner_map.reshape(1, electrodes))

    rows = (8, N, L)
    wide = LANES * ((electrodes + LANES - 1) // LANES)
    message = (cells // 8 + C + 8, L)
    rows_n, rows_p, mine = call(
        functools.partial(correct, electrodes, n_len, n_wall),
        [vmem] * 6,
        [(rows, vmem), (rows, vmem), (message, vmem)],
        [(1, N, L), (wide, L)],
        "correct",
    )(own_rows, from_next, from_prev, coarse, surface, patch_ids)

    relative = n_blk <= 4
    moved = [ring(mine, "blk", d) for d in range(1, n_blk)] if relative else [lax.all_gather(mine, "blk")]
    base_adj, base_pot = call(
        functools.partial(source_part, n_len, n_wall, C),
        [vmem] * 6,
        [(own, vmem), (own, vmem)],
        [field] * 4 + [(2, N, L)],
        "source_part",
        work=12 * 10**6,
    )(bm, be, rows_n, rows_p, qm, fields[2])
    moved, base_adj = lax.optimization_barrier((moved, base_adj))
    sector_blocks = jnp.stack([mine] + moved) if relative else moved[0]
    compacted = (n_blk, n_len, C, W) == (4, 2, 16, 32)
    if compacted:
        brief, across_wall = call(
            functools.partial(compact, C, W),
            [vmem],
            [((168, L), vmem), ((200, L), vmem)],
            [(W // 4, n_blk * C // 2, L), (W // 8 + 1, n_blk * C // 2, L)],
            "compact",
        )(sector_blocks)
        len_brief = ring(brief, "len", 1)
        blocks = [sector_blocks, len_brief, ring(across_wall, "wall", 1), ring(len_brief, "wall", 1), brief]
    elif n_len == 2:
        here = [sector_blocks, ring(sector_blocks, "len", 1)]
    else:
        gathered = lax.all_gather(sector_blocks, "len")
        here = [gathered[j] for j in range(n_len)]
    if not compacted:
        blocks = here + [ring(x, "wall", 1) for x in here]

    NC1, NL1 = n_blk * C // 2, n_len * L // 2
    planes = n_wall * W // 2
    grids = [(planes // k + 2, NC1, NL1) for k in (1, 1, 2, 2, 4, 4)]
    Q = W // 2 + 2
    tall = (Q * (C + 8) + 16, L)
    taller = ((W + 2) * (C + 8) + 16, L)
    scratch = grids + [(Q * C, NL1), tall, tall, taller, taller, own, own]
    scratch += [(2, n_blk * C, n_len * L), (2, 2, 64, L), pltpu.SemaphoreType.DMA((2, 2))]
    adj_prev, potential, patch_grad = call(
        functools.partial(solve, (n_blk, n_len, n_wall), relative, compacted, C, W),
        [vmem] * (len(blocks) + 4),
        [(own, "any"), (own, "any"), ((1, 2), "smem")],
        scratch,
        "solve",
        room=48 if NC1 * NL1 <= 4096 else 58,
    )(*blocks, base_adj, base_pot, fields[2], patches)
    return adj_prev.reshape(W, C, L), potential.reshape(W, C, L), patch_grad


def solution(mesh):
    field = P(("groups", "wall"), "blk", "len")
    return jax.shard_map(
        body,
        mesh=mesh,
        in_specs=(field, field, field, field, field, P("groups")),
        out_specs=(field, field, P(("groups", "blk", "len", "wall"), None)),
        check_vma=False,
    )
```

```python
import functools

import jax
import jax.numpy as jnp
from jax import lax
from jax.experimental import pallas as pl
from jax.experimental.pallas import tpu as pltpu
from jax.sharding import PartitionSpec as P

SI = (0.6, 1.0, 3.0)
SE = (0.8, 1.2, 2.0)
SHIFT = 0.002
OMEGA = 0.8
DT = 0.1
H = 4
LANES = 128
HIGHEST = lax.Precision.HIGHEST
F32 = jnp.float32


def level_coef(level):
    return tuple((SI[i] + SE[i]) / 4.0**level for i in range(3))


def level_diag(level):
    return SHIFT + 2.0 * sum(level_coef(level))


def level_step(level):
    return OMEGA / level_diag(level)


def lane_of(shape):
    return lax.broadcasted_iota(jnp.int32, shape, len(shape) - 1)


def before(m, e):
    first = lane_of(m.shape) == 0
    rm, re = pltpu.roll(m, 1, 1), pltpu.roll(e, 1, 1)
    return jnp.where(first, re, rm), jnp.where(first, rm, re)


def after(m, e):
    last = lane_of(m.shape) == LANES - 1
    rm, re = pltpu.roll(m, LANES - 1, 1), pltpu.roll(e, LANES - 1, 1)
    return jnp.where(last, re, rm), jnp.where(last, rm, re)


def beside_lanes(m, e):
    bm, be = before(m, e)
    am, ae = after(m, e)
    return bm + am, be + ae


def beside_lanes_main(m, e):
    lane = lane_of(m.shape)
    ends = lanes_at(e, LANES - 1 - lane)
    left = jnp.where(lane == 0, ends, pltpu.roll(m, 1, 1))
    right = jnp.where(lane == LANES - 1, ends, pltpu.roll(m, LANES - 1, 1))
    return left + right


def beside_rows(x, row_before, row_after):
    rows = x.shape[0]
    row = lax.broadcasted_iota(jnp.int32, x.shape, 0)
    low = jnp.where(row == 0, row_before, pltpu.roll(x, 1, 0))
    high = jnp.where(row == rows - 1, row_after, pltpu.roll(x, rows - 1, 0))
    return low + high


def beside_dense(x):
    return pltpu.roll(x, 1, 0) + pltpu.roll(x, x.shape[0] - 1, 0)


def plane(ref, i, rows):
    return ref[pl.ds(pl.multiple_of(i * rows, rows), rows), :]


def set_plane(ref, i, rows, value):
    ref[pl.ds(pl.multiple_of(i * rows, rows), rows), :] = value


def loop(low, high, step, unroll):
    def wrapped(i, carry):
        step(i)
        return carry

    if unroll >= high - low:
        for i in range(low, high):
            step(i)
        return
    lax.fori_loop(low, high, wrapped, 0, unroll=unroll)


FACES = (H, H - 1, H - 1, H - 2)


def face_planes(array):
    return FACES[array], sum(FACES[:array])


def pack_faces(n_len, adj, ion, mask, mis, *rest):
    n_dir = 1 if n_len == 2 else 2
    fields, wall_out, rest = rest[:4], rest[4], rest[5:]
    strips, corners = rest[:n_dir], rest[n_dir : 2 * n_dir]
    whole_mask, sems = rest[2 * n_dir :]
    cells = adj.shape[0]
    C = wall_out.shape[1]
    W = cells // C
    wall, length = lax.axis_index("wall"), lax.axis_index("len")
    targets = (fields[0], fields[1], whole_mask, fields[3])
    copies = []
    for a, (src, dst) in enumerate(zip((adj, ion, mask, mis), targets)):
        part = cells // 4
        for k in range(4):
            spot = pl.ds(k * part, part)
            copies.append(pltpu.make_async_copy(src.at[spot], dst.at[spot], sems.at[a, k]))
            copies[-1].start()

    base = jnp.where(wall == 0, W - H, 0)
    group = lane_of((C, LANES)) // H
    turns = [jnp.where(length == 0, H, 0)] if n_dir == 1 else [H, 0]
    corner = [jnp.zeros((C, LANES), F32) for _ in range(n_dir)]
    for a in (0, 1, 3, 2):
        for k in range(4):
            copies[4 * a + k].wait()
        if a == 2:
            fields[2][...] = whole_mask[...].astype(F32)
        ref = fields[a]
        strip = [jnp.zeros((C, LANES), F32) for _ in range(n_dir)]
        for w in range(W):
            value = ref[w * C : (w + 1) * C, :]
            for d in range(n_dir):
                turned = pltpu.roll(value, lax.rem(H * w + turns[d], LANES), 1)
                strip[d] = jnp.where(group == w, turned, strip[d])
        for d in range(n_dir):
            strips[d][a] = strip[d]
        count, first = face_planes(a)
        for p in range(count):
            face = plane(ref, base + jnp.where(wall == 0, H - count, 0) + p, C)
            wall_out[first + p] = face
            slot = first + p
            for d in range(n_dir):
                turned = pltpu.roll(face, lax.rem(H * slot + turns[d], LANES), 1)
                corner[d] = jnp.where(group == slot, turned, corner[d])
    for d in range(n_dir):
        corners[d][...] = corner[d]


def dense(ref, row, N, C):
    return ref[pl.ds(row, N, stride=C), :]


def dense_pair(m, e, row, N, C):
    return dense(m, row, N, C), dense(e, row, N, C)


def dense_apply(pair, inner, outer, coef):
    m, e = pair
    lm, le = beside_lanes(m, e)
    double = 2.0 * sum(coef)
    out = [double * m - coef[0] * beside_dense(m) - coef[2] * lm, double * e - coef[0] * beside_dense(e) - coef[2] * le]
    for row in (inner, outer):
        if row is not None:
            out = [out[k] - coef[1] * row[k] for k in range(2)]
    return out


def near_rows(n_dir, W):
    start, places = 8 * n_dir, []
    for reach in (0, 1, 2, 2, 3):
        places.append((start, H - reach, W + 2 * reach))
        start += W + 2 * reach
    assert start % 8 == 0
    return places


def rim_tiles(values):
    return [value[s : s + 8] for value in values for s in range(0, value.shape[0], 8)]


def rim_places(n_len, length):
    if n_len == 2:
        return [(jnp.where(length == 0, 0, LANES - H), True)]
    return [(0, length < n_len - 1), (LANES - H, length > 0)]


def boundary(n_len, C, *refs):
    n_dir = 1 if n_len == 2 else 2
    raw, wall_in, refs = refs[:4], refs[4], refs[5:]
    strips, corners, refs = refs[:n_dir], refs[n_dir : 2 * n_dir], refs[2 * n_dir :]
    to_next, to_prev, own_rows, build = refs
    W = raw[0].shape[0] // C
    N = W + 2 * H
    wall, length = lax.axis_index("wall"), lax.axis_index("len")
    places = rim_places(n_len, length)

    def strip_rows(packed, first, count):
        lane, k = lane_of((count, LANES)), lax.broadcasted_iota(jnp.int32, (count, LANES), 0)
        out = jnp.zeros((count, LANES), F32)
        for row, (off, ok) in zip(packed, places):
            j = lax.rem(lane - off + LANES, LANES)
            index = jnp.clip(H * (first + k) + j, 0, LANES - 1)
            taken = lanes_at(jnp.broadcast_to(row, (count, LANES)), index)
            out = jnp.where(jnp.logical_and(j < H, ok), taken, out)
        return out

    slots = iter(range(build.shape[0]))

    def assembled(own, halo, count):
        ref = build.at[next(slots)]
        ref[0:8, :] = jnp.zeros((8, LANES), F32)
        ref[N - 8 : N, :] = jnp.zeros((8, LANES), F32)
        ref[H : H + W, :] = own
        ref[H - count : H, :] = jnp.where(wall == 0, 0.0, halo)
        ref[H + W : H + W + count, :] = jnp.where(wall == 0, halo, 0.0)
        return ref[...]

    def row_of(a, r):
        count, first = face_planes(a)
        halo = jnp.concatenate([wall_in[first + p, r : r + 1, :] for p in range(count)], 0)
        m = assembled(raw[a][pl.ds(r, W, stride=C), :], halo, count)
        own = strip_rows([strip[a, r : r + 1, :] for strip in strips], 0, W)
        halo = strip_rows([corner[r : r + 1, :] for corner in corners], first, 8)[:count]
        return m, assembled(own, halo, count)

    length_shift = jnp.where(length == 0, 0, H) if n_dir == 1 else H
    group = lane_of((8, LANES)) // (H * n_dir)
    for side, (out, order) in enumerate(((to_next, (C - 1, C - 2, C - 3, C - 4)), (to_prev, (0, 1, 2, 3)))):
        adj = [row_of(0, r) for r in order]
        mask = [row_of(2, r) for r in order[:3]]
        q = []
        for k in range(3):
            ion = row_of(1, order[k])
            moved = dense_apply(adj[k], adj[k + 1], adj[k - 1] if k else None, SI)
            q.append([adj[k][j] - DT * mask[k][j] * (moved[j] + ion[j] * adj[k][j]) for j in range(2)])
        near = dense_apply(q[0], q[1], None, SI)
        mis = row_of(3, order[0])
        near = [near[j] + mis[j] for j in range(2)]
        second = dense_apply(q[1], q[2], q[0], SI)[0] + row_of(3, order[1])[0]
        for value, (start, first, count) in zip((second, near[0], q[0][0], mask[0][0], adj[0][0]), near_rows(n_dir, W)):
            out[start : start + count, :] = value[first : first + count]
        packs = [jnp.zeros((8, LANES), F32) for _ in range(n_dir)]
        for t, tile in enumerate(rim_tiles((near[1], q[0][1], mask[0][1], adj[0][1]))):
            k, at = divmod(t, LANES // (H * n_dir))
            turned = pltpu.roll(tile, lax.rem(length_shift + H * n_dir * at, LANES), 1)
            packs[k] = jnp.where(group == at, turned, packs[k])
        for k in range(n_dir):
            out[8 * k : 8 * k + 8, :] = packs[k]
        for k, pair in enumerate((adj[0], mask[0], q[0])):
            own_rows[side, 2 * k] = pair[0]
            own_rows[side, 2 * k + 1] = pair[1]


def spots(m_ref, e_ref, i, rows, coef):
    m, e = plane(m_ref, i, rows), plane(e_ref, i, rows)
    wm = plane(m_ref, i - 1, rows) + plane(m_ref, i + 1, rows)
    we = plane(e_ref, i - 1, rows) + plane(e_ref, i + 1, rows)
    lm, le = beside_lanes(m, e)
    cm, ce = beside_rows(m, 0.0, 0.0), beside_rows(e, 0.0, 0.0)
    double = 2.0 * sum(coef)
    dm = double * m - coef[0] * wm - coef[1] * cm - coef[2] * lm
    de = double * e - coef[0] * we - coef[1] * ce - coef[2] * le
    return m, e, dm, de


def rim_lanes(lane, length, n_len):
    return jnp.logical_or(
        jnp.logical_and(lane < H, length < n_len - 1),
        jnp.logical_and(lane >= LANES - H, length > 0),
    )


def inside(i, wall, W, n_wall):
    w = wall * W + i - H
    return jnp.logical_and(w >= 0, w < n_wall * W)


def lanes_at(x, index):
    return jnp.take_along_axis(x, index, axis=1, mode="promise_in_bounds")


def rows_at(x, index):
    return jnp.take_along_axis(x, index, axis=0, mode="promise_in_bounds")


def halved(low, high):
    lane = lane_of(low.shape)
    even = 2 * lane % LANES
    pairs = [lanes_at(x, even) + lanes_at(x, even + 1) for x in (low, high)]
    return 0.125 * jnp.where(lane < LANES // 2, pairs[0], pairs[1])


def precise(a, b):
    return jnp.dot(a, b, precision=HIGHEST, preferred_element_type=F32)


def assemble(n_len, C, raw, wall_in, strips, corners, xm, xe):
    W = raw[0].shape[0] // C
    N = W + 2 * H
    wall, length = lax.axis_index("wall"), lax.axis_index("len")
    lane = lane_of((C, LANES))
    places = rim_places(n_len, length)
    seen = [jnp.logical_and(lax.rem(lane - off + LANES, LANES) < H, ok) for off, ok in places]

    def rim(packed, base):
        out = jnp.zeros((C, LANES), F32)
        for row, ok, (off, _) in zip(packed, seen, places):
            out = jnp.where(ok, pltpu.roll(row, lax.rem(off - base + LANES, LANES), 1), out)
        return out

    zero = jnp.zeros((C, LANES), F32)
    last = N - H
    for a, own in enumerate(raw):
        packed = [strip[a] for strip in strips]
        for w in range(W):
            set_plane(xm[a], w + H, C, plane(own, w, C))
            set_plane(xe[a], w + H, C, rim(packed, H * w))
        packed = [corner[...] for corner in corners]
        for i in range(H):
            for at in (i, last + i):
                set_plane(xm[a], at, C, zero)
                set_plane(xe[a], at, C, zero)
        count, first = face_planes(a)
        here = jnp.where(wall == 0, last, H - count)
        for p in range(count):
            set_plane(xm[a], here + p, C, wall_in[first + p])
            set_plane(xe[a], here + p, C, rim(packed, H * (first + p)))


def sector(n_len, n_wall, C, electrodes, *refs):
    n_dir = 1 if n_len == 2 else 2
    raw, wall_in, refs = refs[:4], refs[4], refs[5:]
    strips, corners, refs = refs[:n_dir], refs[n_dir : 2 * n_dir], refs[2 * n_dir :]
    owner, qm, bm, be, coarse, surface, patches, qe, pairs = refs[:9]
    xm, xe = refs[9:13], refs[13:17]
    assemble(n_len, C, raw, wall_in, strips, corners, xm, xe)
    N = qm.shape[0] // C
    W = N - 2 * H
    wall, length = lax.axis_index("wall"), lax.axis_index("len")
    rim = rim_lanes(lane_of((C, LANES)), length, n_len)
    zero = jnp.zeros((C, LANES), F32)
    for i in (0, N - 1):
        set_plane(qm, i, C, zero)
        set_plane(qe, i, C, zero)
    for i in (0, 1, N - 2, N - 1):
        set_plane(bm, i, C, zero)
        set_plane(be, i, C, zero)

    def parabolic(i):
        m, e, dm, de = spots(xm[0], xe[0], i, C, SI)
        set_plane(qm, i, C, m - DT * plane(xm[2], i, C) * (dm + plane(xm[1], i, C) * m))
        set_plane(qe, i, C, e - DT * plane(xe[2], i, C) * (de + plane(xe[1], i, C) * e))

    loop(1, N - 1, parabolic, 2)

    def elliptic_source(i):
        m, e, dm, de = spots(qm, qe, i, C, SI)
        ok = inside(i, wall, W, n_wall)
        set_plane(bm, i, C, jnp.where(ok, plane(xm[3], i, C) + dm, 0.0))
        set_plane(be, i, C, jnp.where(jnp.logical_and(rim, ok), plane(xe[3], i, C) + de, 0.0))

    loop(2, N - 2, elliptic_source, 2)

    coef, k0 = level_coef(0), level_step(0)

    def left(i):
        m, e = plane(bm, i, C), plane(be, i, C)
        wm = plane(bm, i - 1, C) + plane(bm, i + 1, C)
        cm = beside_rows(m, 0.0, 0.0)
        lm = beside_lanes_main(m, e)
        return m, (1.0 - OMEGA) * m + k0 * (coef[0] * wm + coef[1] * cm + coef[2] * lm)

    def pair(q):
        i = 2 * q + H
        m, first = left(i)
        n, second = left(i + 1)
        set_plane(pairs, q, C, first + second)

        @pl.when(jnp.logical_and(q == 0, wall == 0))
        def _():
            surface[...] = k0 * (m + first)

        @pl.when(jnp.logical_and(q == W // 2 - 1, wall == n_wall - 1))
        def _():
            surface[...] = k0 * (n + second)

    loop(0, W // 2, pair, 2)

    half = W * C // 8
    z = pairs[pl.ds(0, 2 * half, stride=2), :] + pairs[pl.ds(1, 2 * half, stride=2), :]
    coarse[...] = halved(z[:half], z[half:])

    blk = lax.axis_index("blk")
    me = (blk * n_len + length) * n_wall + wall
    which = lax.broadcasted_iota(jnp.int32, (1, electrodes), 1).astype(F32)
    mine = owner[...] == me
    patches[0:1, :] = jnp.full((1, LANES), jnp.min(jnp.where(mine, which, float(electrodes))))
    patches[1:2, :] = jnp.full((1, LANES), jnp.max(jnp.where(mine, which, -1.0)))
    patches[2:8, :] = jnp.zeros((6, LANES), F32)


def unpacked(ref, n_len, length, N):
    n_dir = 1 if n_len == 2 else 2
    mains = []
    for start, first, count in near_rows(n_dir, N - 2 * H):
        begin = min(start - first, ref.shape[0] - N)
        value = ref[begin : begin + N, :]
        behind = start - first - begin
        mains.append(pltpu.roll(value, N - behind, 0) if behind else value)
    rim = rim_lanes(lane_of((8, LANES)), length, n_len)
    shift = jnp.where(length == 0, 0, H) if n_dir == 1 else H
    rims = []
    for k in range(4):
        parts = []
        for s in range(N // 8):
            pack, at = divmod(k * (N // 8) + s, LANES // (H * n_dir))
            back = lax.rem(2 * LANES - shift - H * n_dir * at, LANES)
            parts.append(jnp.where(rim, pltpu.roll(ref[8 * pack : 8 * pack + 8, :], back, 1), 0.0))
        rims.append(jnp.concatenate(parts, 0))
    second, near, q, mask, adj = mains
    return (adj, rims[3]), (mask, rims[2]), (q, rims[1]), (near, rims[0]), second


def lateral(pair):
    return dense_apply(pair, None, None, SI)


def source_rows(own, other):
    adj_o, mask_o, q_o = own
    adj_n, mask_n, q_n, p_n, second_n = other
    step = DT * SI[1]
    delta_o = [step * mask_o[k] * adj_n[k] for k in range(2)]
    delta_n = [step * mask_n[k] * adj_o[k] for k in range(2)]
    lat_o, lat_n = lateral(delta_o), lateral(delta_n)
    near = [lat_o[k] - SI[1] * (q_n[k] + delta_n[k]) for k in range(2)]
    second = [-SI[1] * delta_o[k] for k in range(2)]
    halo = [p_n[k] + lat_n[k] - SI[1] * (q_o[k] + delta_o[k]) for k in range(2)]
    halo_second = second_n - SI[1] * delta_n[0]
    return near, second, halo, halo_second, delta_o[0]


def correct(electrodes, n_len, n_wall, own_rows, from_next, from_prev, coarse, surface, ids, *rest):
    rows_n, rows_p, message = rest[:3]
    lines, sums = rest[3:]
    _, C, L = ids.shape
    N = own_rows.shape[2]
    W = N - 2 * H
    wall, length = lax.axis_index("wall"), lax.axis_index("len")
    ok_m = inside(lax.broadcasted_iota(jnp.int32, (N, LANES), 0), wall, W, n_wall)
    ok_e = jnp.logical_and(ok_m, rim_lanes(lane_of((N, LANES)), length, n_len))
    coef, k0 = level_coef(0), level_step(0)
    y = surface[...]
    row = lax.broadcasted_iota(jnp.int32, (C, LANES), 0)
    at = pl.ds(jnp.where(wall == 0, H, W + H - 1), 1)
    lows, highs = [], []
    W1, C1 = W // 2, C // 2
    for side, (other, out, order) in enumerate(
        ((from_next, rows_n, (C - 1, C - 2, C - 3)), (from_prev, rows_p, (0, 1, 2)))
    ):
        own = [(own_rows[side, 2 * k], own_rows[side, 2 * k + 1]) for k in range(3)]
        near, second, halo, halo_second, delta = source_rows(own, unpacked(other, n_len, length, N))
        near = [jnp.where(ok_m, near[0], 0.0), jnp.where(ok_e, near[1], 0.0)]
        second = [jnp.where(ok_m, second[0], 0.0), jnp.where(ok_e, second[1], 0.0)]
        out[0] = halo_m = jnp.where(ok_m, halo[0], 0.0)
        out[1] = jnp.where(ok_e, halo[1], 0.0)
        out[2] = jnp.where(ok_m, halo_second, 0.0)
        out[3] = delta
        out[4], out[5] = near
        out[6], out[7] = second

        def turned(pair, beside):
            m, e = pair
            return (1.0 - OMEGA) * m + k0 * (
                coef[0] * beside_dense(m) + coef[2] * beside_lanes_main(m, e) + coef[1] * beside
            )

        first = turned(near, second[0] + halo_m)
        next_one = turned(second, near[0])
        third = k0 * coef[1] * second[0]
        for k, change in enumerate((near[0] + first, second[0] + next_one, third)):
            lines[0] = change
            y = y + jnp.where(row == order[k], k0 * lines[0, at, :], 0.0)
        for change in (first + next_one, third):
            lines[0] = change
            both = lines[0, pl.ds(H, W1, stride=2), :] + lines[0, pl.ds(H + 1, W1, stride=2), :]
            lows.append(both[: W1 // 2])
            highs.append(both[W1 // 2 :])
    add = halved(jnp.concatenate(lows, 0), jnp.concatenate(highs, 0))
    half = W * C // 8
    message[0:half, :] = coarse[...]
    for k, c1 in enumerate((C1 - 1, C1 - 2, 0, 1)):
        spot = pl.ds(c1, W1 // 2, stride=C1)
        message[spot, :] = message[spot, :] + add[k * (W1 // 2) : (k + 1) * (W1 // 2)]
    patch = ids[0]
    message[half : half + C, :] = patch.astype(F32)
    wide = sums.shape[0]
    if wide > electrodes:
        sums[...] = jnp.zeros(sums.shape, F32)

    def one(e):
        sums[pl.ds(e, 1), :] = jnp.sum(jnp.where(patch == e, y, 0.0), axis=0, keepdims=True)

    loop(0, electrodes, one, 8)
    totals = lax.dot_general(
        jnp.ones((8, LANES), F32), sums[...], (((1,), (1,)), ((), ())), precision=HIGHEST, preferred_element_type=F32
    )
    message[half + C : half + C + 8, :] = jnp.zeros((8, LANES), F32)
    for t in range(wide // LANES):
        message[half + C + t : half + C + t + 1, :] = totals[0:1, t * LANES : (t + 1) * LANES]


def source_part(n_len, n_wall, C, bm, be, rows_n, rows_p, qm, mask, base_adj, base_pot, fm, fe, tm, te, hp):
    N = bm.shape[0] // C
    W = N - 2 * H
    length, wall = lax.axis_index("len"), lax.axis_index("wall")
    fm[...] = bm[...]
    fe[...] = be[...]
    for rows, near, second in ((rows_n, C - 1, C - 2), (rows_p, 0, 1)):
        for k, at in ((4, near), (6, second)):
            spot = pl.ds(at, N, stride=C)
            fm[spot, :] = fm[spot, :] + rows[k]
            fe[spot, :] = fe[spot, :] + rows[k + 1]
    coef, k0 = level_coef(0), level_step(0)
    rim = rim_lanes(lane_of((C, LANES)), length, n_len)

    def part(i):
        m, e = plane(fm, i, C), plane(fe, i, C)
        wm = plane(fm, i - 1, C) + plane(fm, i + 1, C)
        we = plane(fe, i - 1, C) + plane(fe, i + 1, C)
        lm, le = beside_lanes(m, e)
        at = pl.ds(i, 1)
        cm = beside_rows(m, rows_p[0, at, :], rows_n[0, at, :])
        ce = beside_rows(e, rows_p[1, at, :], rows_n[1, at, :])
        pm = k0 * ((2.0 - OMEGA) * m + k0 * (coef[0] * wm + coef[1] * cm + coef[2] * lm))
        pe = k0 * ((2.0 - OMEGA) * e + k0 * (coef[0] * we + coef[1] * ce + coef[2] * le))
        set_plane(tm, i, C, jnp.where(inside(i, wall, W, n_wall), pm, 0.0))
        set_plane(te, i, C, jnp.where(rim, pe, 0.0))

    loop(H - 1, N - H + 1, part, 2)
    for side, (rows, at) in enumerate(((rows_n, C - 1), (rows_p, 0))):
        m = rows[0]
        total = (
            coef[0] * beside_dense(m)
            + coef[1] * (rows[2] + dense(fm, at, N, C))
            + coef[2] * beside_lanes_main(m, rows[1])
        )
        hp[side] = k0 * ((2.0 - OMEGA) * m + k0 * total)
    row = lax.broadcasted_iota(jnp.int32, (C, LANES), 0)

    def finish(w):
        i = w + H
        m, e = plane(tm, i, C), plane(te, i, C)
        at = pl.ds(i, 1)
        wm = plane(tm, i - 1, C) + plane(tm, i + 1, C)
        cm = beside_rows(m, hp[1, at, :], hp[0, at, :])
        lm = beside_lanes_main(m, e)
        lam = plane(qm, i, C)
        lam = lam + jnp.where(row == C - 1, rows_n[3, at, :], 0.0) + jnp.where(row == 0, rows_p[3, at, :], 0.0)
        moved = 2.0 * sum(SI) * m - SI[0] * wm - SI[1] * cm - SI[2] * lm
        set_plane(base_adj, w, C, lam - DT * plane(mask, w, C) * moved)
        set_plane(base_pot, w, C, m)

    loop(0, W, finish, 2)


def halves(shape):
    lane = lane_of(shape)
    return lane, lane % (LANES // 2)


def compact(C, W, blocks, out, wall_out, sheet1, coarse2):
    n_blk = blocks.shape[0]
    W1, C1 = W // 2, C // 2
    half, start, middle = W1 // 2, W1 // 2 * C1, LANES // 2
    blk, length, wall = lax.axis_index("blk"), lax.axis_index("len"), lax.axis_index("wall")
    sums = jnp.zeros((8, LANES), F32)
    for d in range(n_blk):
        b = lax.rem(blk - d + n_blk, n_blk)
        for i in range(half):
            sheet1[i, pl.ds(pl.multiple_of(C1 * b, C1), C1), :] = blocks[d, i * C1 : (i + 1) * C1, :]
        out[pl.ds(pl.multiple_of(96 + C * b, C), C), :] = blocks[d, start : start + C, :]
        sums = sums + blocks[d, start + C : start + C + 8, :]
    out[160:168, :] = sums
    NC1 = sheet1.shape[1]
    lane, at = halves((NC1, LANES))
    low = lane < middle
    coef, k1 = level_coef(1), level_step(1)
    ends = pltpu.roll(sheet1[half - 1], middle, 1), pltpu.roll(sheet1[0], middle, 1)
    for q in range(half // 2):
        both = sheet1[2 * q] + sheet1[2 * q + 1]
        prev = sheet1[2 * q - 1] if q else jnp.where(low, 0.0, ends[0])
        after_it = sheet1[2 * q + 2] if 2 * q + 2 < half else jnp.where(low, ends[1], 0.0)
        c = pltpu.roll(both, 1, 0) + pltpu.roll(both, NC1 - 1, 0)
        l = jnp.where(at == 0, 0.0, pltpu.roll(both, 1, 1)) + jnp.where(
            at == middle - 1, 0.0, pltpu.roll(both, LANES - 1, 1)
        )
        left = (1.0 - OMEGA) * both + k1 * (coef[0] * (prev + both + after_it) + coef[1] * c + coef[2] * l)
        coarse2[q] = 0.125 * twins(left, 1)
    coarse2[half // 2] = 0.125 * twins(jnp.where(wall == 0, sheet1[half - 1], sheet1[0]), 1)
    rows2 = NC1 // 2
    lane2, at2 = halves((rows2, LANES))
    pick = lane2 - at2 + 2 * (at2 % (middle // 2))
    for p in range(half // 4):
        pair = [lanes_at(coarse2[2 * p + k, pl.ds(0, rows2, stride=2), :], pick) for k in range(2)]
        out[rows2 * p : rows2 * (p + 1), :] = jnp.where(at2 < middle // 2, pair[0], pair[1])
    beside = jnp.zeros((NC1, LANES), F32)
    base = jnp.where(length == 0, middle - H, 0)
    for i in range(half):
        turned = pltpu.roll(sheet1[i], lax.rem(H * i - base + LANES, LANES), 1)
        beside = jnp.where(at // H == i, turned, beside)
    index = lax.broadcasted_iota(jnp.int32, (8, LANES), 0) ^ 1
    line = beside + jnp.concatenate([rows_at(beside[t : t + 8], index) for t in range(0, NC1, 8)], 0)
    line = 0.125 * (line + pltpu.roll(line, LANES - H, 1))
    m = lane - 96
    spot = jnp.where(m < H, 8 * m, middle + 8 * (m - H)) + jnp.where(length == 0, H - 1, 0)
    line = lanes_at(line, jnp.clip(spot, 0, LANES - 1))
    beside = jnp.where(jnp.logical_and(m >= 0, m < 8), line, beside)
    out[32 : 32 + NC1, :] = beside
    face = coarse2[half // 2, pl.ds(0, rows2, stride=2), :]
    face = lanes_at(face, jnp.where(wall == 0, middle, 0) + 2 * (at2 % (middle // 2)))
    inner = jnp.logical_and(lane2 >= middle // 2, lane2 < middle)
    out[32 : 32 + rows2, :] = jnp.where(inner, face, beside[:rows2])
    inner_surface = jnp.where(low, sheet1[0], pltpu.roll(sheet1[1], middle, 1))
    outer_surface = jnp.where(low, pltpu.roll(sheet1[half - 2], middle, 1), sheet1[half - 1])
    out[64 : 64 + NC1, :] = jnp.where(wall == 0, inner_surface, outer_surface)
    wall_out[0:168, :] = out[...]
    last = jnp.where(low, pltpu.roll(sheet1[half - 1], middle, 1), sheet1[half - 2])
    wall_out[168 : 168 + NC1, :] = jnp.where(wall == 0, last, inner_surface)


def around(x, by):
    rows, lanes = x.shape
    lane = lane_of(x.shape)
    c = pltpu.roll(x, by, 0) + pltpu.roll(x, rows - by, 0)
    l = jnp.where(lane < by, 0.0, pltpu.roll(x, by, 1)) + jnp.where(
        lane >= lanes - by, 0.0, pltpu.roll(x, lanes - by, 1)
    )
    return c, l


def twins(x, by):
    rows, lanes = x.shape
    if lanes == LANES:
        index = lax.broadcasted_iota(jnp.int32, (8, LANES), 0) ^ by
        x = x + jnp.concatenate([rows_at(x[t : t + 8], index) for t in range(0, rows, 8)], 0)
        return x + lanes_at(x, lane_of(x.shape) ^ by)
    row = lax.broadcasted_iota(jnp.int32, x.shape, 0)
    lane = lane_of(x.shape)
    x = x + jnp.where((row & by) == 0, pltpu.roll(x, rows - by, 0), pltpu.roll(x, by, 0))
    return x + jnp.where((lane & by) == 0, pltpu.roll(x, lanes - by, 1), pltpu.roll(x, by, 1))


def solve(sizes, relative, compacted, C, W, *refs):
    n_blk, n_len, n_wall = sizes
    count = n_len * n_wall + compacted
    blocks, refs = refs[:count], refs[count:]
    base_adj, base_pot, mask, patches, adj_prev, potential, patch_grad = refs[:7]
    b1, x1, b2, x2, b3, x3, near, pm, pe, tm, te, adj_out, pot_out, sheet, briefs, sems = refs[7:]
    L = LANES
    W1, C1 = W // 2, C // 2
    planes, NC1, NL1 = b1.shape
    planes -= 2
    blk, length, wall = lax.axis_index("blk"), lax.axis_index("len"), lax.axis_index("wall")
    half = W1 // 2
    middle = LANES // 2
    lane8 = lane_of((C1, LANES))
    often = 40 if NC1 * NL1 <= 4096 else 1

    def blk_of(d):
        return lax.rem(blk - d + n_blk, n_blk) if relative else d

    def length_of(j):
        return (length + j) % n_len if n_len == 2 else j

    def wall_of(v):
        return (wall + v) % n_wall

    zero1 = jnp.zeros((NC1, NL1), F32)
    for ref in (b1, x1, b2, x2, b3, x3):
        ref[0] = zero1
        ref[ref.shape[0] - 1] = zero1

    if not compacted:
        for v in range(n_wall):
            wall_s = wall_of(v)
            mine = blocks[v * n_len : (v + 1) * n_len]

            def unpack(d):
                at = pl.ds(pl.multiple_of(C1 * blk_of(d), C1), C1)
                for t in range(n_len // 2):
                    one, two = mine[2 * t], mine[2 * t + 1]
                    for i in range(half):
                        a, b = one[d, i * C1 : (i + 1) * C1, :], two[d, i * C1 : (i + 1) * C1, :]
                        if n_len == 2:
                            a, b = jnp.where(length == 0, a, b), jnp.where(length == 0, b, a)
                        spot = 1 + wall_s * W1 + i
                        lanes = slice(t * LANES, (t + 1) * LANES)
                        b1[spot, at, lanes] = jnp.where(lane8 < middle, a, pltpu.roll(b, middle, 1))
                        b1[spot + half, at, lanes] = jnp.where(lane8 < middle, pltpu.roll(a, middle, 1), b)

            loop(0, n_blk, unpack, 4)
    if compacted:
        stack, len_brief, wall_brief, both_brief, own_brief = blocks
        lane8 = lane_of((C1, LANES))
        here8 = lane8 // middle == length
        here = lane_of((NC1, LANES)) // middle == length
        face_lane = jnp.where(length == 0, middle, middle - H)
        near8 = jnp.logical_and(lane8 >= face_lane, lane8 < face_lane + H)
        at_face = jnp.logical_and(lane_of((NC1, LANES)) >= face_lane, lane_of((NC1, LANES)) < face_lane + H)
        for d in range(n_blk):
            row = pl.multiple_of(C1 * blk_of(d), C1)
            beside = len_brief[pl.ds(32 + row, C1), :]
            for i in range(half):
                a = stack[d, i * C1 : (i + 1) * C1, :]
                b = pltpu.roll(a, middle, 1)
                for k, value in enumerate((jnp.where(length == 0, a, b), jnp.where(length == 0, b, a))):
                    turn = lax.rem(face_lane - H * i - middle * k + 2 * LANES, LANES)
                    rest = jnp.where(near8, pltpu.roll(beside, turn, 1), 0.0)
                    b1[1 + wall * W1 + i + half * k, pl.ds(row, C1), :] = jnp.where(here8, value, rest)

        def two_planes(tile):
            turned = pltpu.roll(tile, middle, 1)
            return jnp.where(length == 0, tile, turned), jnp.where(length == 0, turned, tile)

        beyond = two_planes(wall_brief[168 : 168 + NC1, :])
        beside = both_brief[32 : 32 + NC1, :]
        for k in range(2):
            off = jnp.where(wall == 0, H * k, middle + H * (half - 1 - k))
            rest = jnp.where(at_face, pltpu.roll(beside, lax.rem(face_lane - off + 2 * LANES, LANES), 1), 0.0)
            b1[jnp.where(wall == 0, 1 + W1 + k, W1 - k)] = jnp.where(here, beyond[k], rest)
        for k in range(2):
            theirs = two_planes(len_brief[64 : 64 + NC1, :])[1 - k]
            spot = jnp.where(wall == 0, 1, planes - 1) + k
            b1[spot] = jnp.where(here, b1[spot], theirs)
            ours = two_planes(wall_brief[64 : 64 + NC1, :])[k]
            theirs = two_planes(both_brief[64 : 64 + NC1, :])[1 - k]
            b1[jnp.where(wall == 0, planes - 1, 1) + k] = jnp.where(here, ours, theirs)
        first_half = length == 0
        for k in range(2):
            ours = jnp.where(wall == k, own_brief[0:64, :], wall_brief[0:64, :])
            theirs = jnp.where(wall == k, len_brief[0:64, :], both_brief[0:64, :])
            briefs[0, k] = jnp.where(first_half, ours, theirs)
            briefs[1, k] = jnp.where(first_half, theirs, ours)
        lane_8 = lane_of((8, LANES))
        quarter = middle // 2
        left_quarter = lane_8 % middle < quarter
        pairs_index = [lane_8 // 2, middle + lane_8 // 2]
        facing = jnp.logical_and(lane_8 >= middle - 2, lane_8 < middle + 2)
        coef1 = [level_step(1) * x for x in level_coef(1)]
        rows2 = NC1 // 2

        def merged(w, start):
            one, two = briefs[0, w, start : start + 8, :], briefs[1, w, start : start + 8, :]
            even = jnp.where(left_quarter, one, pltpu.roll(two, quarter, 1))
            odd = jnp.where(left_quarter, pltpu.roll(one, LANES - quarter, 1), two)
            return even, odd

        for w in range(n_wall):
            for t in range(rows2 // 8):
                lines = [briefs[h, w, pl.ds(32 + 16 * t, 8, stride=2), :] for h in range(2)]
                lines = [lanes_at(x, jnp.minimum(96 + lane_8 // 4, LANES - 1)) for x in lines]
                lines = coef1[2] * jnp.where(lane_8 % 4 < 2, lines[1], lines[0])
                for p in range(half // 4):
                    tiles = merged(w, rows2 * p + 8 * t)
                    for odd in range(2):
                        for high in range(2):
                            k = 2 * p + odd + half // 2 * high
                            value = lanes_at(tiles[odd], pairs_index[high])
                            line = pltpu.roll(lines, middle - 2 - 4 * k, 1)
                            value = value + jnp.where(facing, line, 0.0)
                            if k == (half - 1 if w == 0 else 0):
                                value = value + coef1[0] * lanes_at(merged(1 - w, 32 + 8 * t)[1], pairs_index[0])
                            for r in range(2):
                                b2[1 + w * half + k, pl.ds(16 * t + r, 8, stride=2), :] = value

    def total_of(x, wsum, level, by):
        coef = level_coef(level)
        c, l = around(x, by)
        return level_step(level) * (coef[0] * wsum + coef[1] * c + coef[2] * l)

    def left_pair(ref, i, level):
        both = ref[i] + ref[i + 1]
        return (1.0 - OMEGA) * both + total_of(both, ref[i - 1] + both + ref[i + 2], level, 2 ** (level - 1))

    def sweep(x_ref, b_ref, i, level):
        x = x_ref[i]
        total = total_of(x, x_ref[i - 1] + x_ref[i + 1], level, 2 ** (level - 1))
        return (1.0 - OMEGA) * x + level_step(level) * b_ref[i] + total

    def down1(q):
        b2[1 + q] = 0.125 * twins(left_pair(b1, 2 * q + 1, 1), 1)

    if not compacted:
        loop(0, planes // 2, down1, often)

    def down2(q):
        b3[1 + q] = 0.125 * twins(left_pair(b2, 2 * q + 1, 2), 2)

    loop(0, planes // 4, down2, often)

    deep = planes // 4
    k3 = level_step(3)

    x2[1 + deep] = zero1

    def start3(q):
        b = b3[1 + q]
        x2[1 + q] = k3 * ((2.0 - OMEGA) * b + total_of(b, b3[q] + b3[2 + q], 3, 4))

    loop(0, deep, start3, often)

    def sweep3(q):
        x3[1 + q] = sweep(x2, b3, 1 + q, 3)

    loop(0, deep, sweep3, often)
    k2 = level_step(2)

    def up2(q):
        coarse = x3[1 + q]
        x2[1 + 2 * q] = k2 * b2[1 + 2 * q] + coarse
        x2[2 + 2 * q] = k2 * b2[2 + 2 * q] + coarse

    loop(0, planes // 4, up2, often)

    k1 = level_step(1)

    def up1(q):
        fine = sweep(x2, b2, 1 + q, 2)
        x1[1 + 2 * q] = k1 * b1[1 + 2 * q] + fine
        x1[2 + 2 * q] = k1 * b1[2 + 2 * q] + fine

    if compacted:
        loop(0, half, lambda q: up1(half * wall + q), often)
        up1(half - wall)
        up1((planes // 2 - 1) * (1 - wall))
    else:
        loop(0, planes // 2, up1, often)

    Q = W1 + 2
    sectors = (blk, lax.rem(blk + 1, n_blk), lax.rem(blk + n_blk - 1, n_blk))
    spots3 = [pl.ds(pl.multiple_of(s * C1, C1), C1) for s in sectors]
    row8 = lax.broadcasted_iota(jnp.int32, (C1, NL1), 0)

    def three(ref, i):
        return jnp.concatenate([ref[i, s, :] for s in spots3], 0)

    def finish1(q):
        i = wall * W1 + q
        x = three(x1, i)
        wsum = three(x1, jnp.maximum(i - 1, 0)) + three(x1, jnp.minimum(i + 1, planes + 1))
        value = (1.0 - OMEGA) * x + k1 * three(b1, i) + total_of(x, wsum, 1, 1)
        value = jnp.where(jnp.logical_and(i >= 1, i <= planes), value, 0.0)
        set_plane(near, 2 * q, C1, value[:C1])
        set_plane(near, 2 * q + 1, C1, jnp.where(row8 < 2, value[C1 : 2 * C1], value[2 * C1 :]))

    loop(0, Q, finish1, often)

    first = length * middle
    R = C + 8
    row8 = lax.broadcasted_iota(jnp.int32, (8, LANES), 0)
    tile_lane = lane_of((8, LANES))
    at_e = jnp.where(tile_lane < H, middle + tile_lane // 2, tile_lane // 2 - middle)
    rim8 = rim_lanes(tile_lane, length, n_len)
    if NL1 == LANES:
        index_m, index_e = first + tile_lane // 2, jnp.clip(first + at_e, 0, LANES - 1)

        def spread(tile):
            return lanes_at(tile, index_m), jnp.where(rim8, lanes_at(tile, index_e), 0.0)

    else:
        source = lax.broadcasted_iota(jnp.int32, (NL1, LANES), 0)
        lane = lane_of((NL1, LANES))
        at_all = jnp.where(lane < H, middle + lane // 2, jnp.where(lane >= LANES - H, lane // 2 - middle, 4 * NL1))
        take_m = jnp.where(source == first + lane // 2, 1.0, 0.0).astype(F32)
        take_e = jnp.where(source == first + at_all, 1.0, 0.0).astype(F32)

        def spread(tile):
            return precise(tile, take_m), precise(tile, take_e)

    picks = (row8 // 2, H + row8 // 2)
    ends = jnp.where(row8 < H, 6 + row8 // 2, row8 // 2 - 2)

    def fine_rows(q):
        own = spread(plane(near, 2 * q, C1))
        beside = spread(plane(near, 2 * q + 1, C1))
        for out, a, b in ((pm, own[0], beside[0]), (pe, own[1], beside[1])):
            parts = (jnp.where(row8 < 6, a, b), a, jnp.where(row8 < 2, b, a))
            index = (ends, 2 + row8 // 2, ends)
            for k in range(3):
                out[pl.ds(pl.multiple_of(8 + R * q + 8 * k, 8), 8), :] = rows_at(parts[k], index[k])

    loop(0, Q, fine_rows, often)
    for ref in (pm, pe):
        ref[0:8, :] = jnp.zeros((8, LANES), F32)
        ref[8 + R * Q : 16 + R * Q, :] = jnp.zeros((8, LANES), F32)
    coef, k0 = level_coef(0), level_step(0)
    def fine(ref, t, by=0, count=R):
        return ref[pl.ds(8 + R * t + by, count), :]

    def coarse_terms(q):
        out = []
        sides = beside_lanes(fine(pm, q), fine(pe, q))
        for ref, l in zip((pm, pe), sides):
            x = fine(ref, q)
            c = fine(ref, q, -1) + fine(ref, q, 1)
            out.append((1.0 - OMEGA) * x + k0 * (coef[0] * x + coef[1] * c + coef[2] * l))
        return out

    ks = k0 * coef[0]

    def set_fine(ref, t, value):
        ref[pl.ds(pl.multiple_of(8 + R * t, 8), R), :] = value

    def put_end(t, q, other, ok):
        set_fine(tm, t, jnp.where(ok, coarse_terms(q)[0] + ks * fine(pm, other), 0.0))

    put_end(0, 0, 1, wall > 0)
    put_end(W + 1, Q - 1, Q - 2, wall < n_wall - 1)
    rim = rim_lanes(lane_of((R, LANES)), length, n_len)

    def level0(q):
        gm, ge = coarse_terms(q)
        for t, other in ((2 * q - 1, q - 1), (2 * q, q + 1)):
            set_fine(tm, t, gm + ks * fine(pm, other))
            set_fine(te, t, jnp.where(rim, ge + ks * fine(pe, other), 0.0))

    loop(1, 1 + W1, level0, often)

    def finish0(w):
        t = w + 1
        m, e = fine(tm, t, H, C), fine(te, t, H, C)
        cm = fine(tm, t, H - 1, C) + fine(tm, t, H + 1, C)
        wm = fine(tm, t - 1, H, C) + fine(tm, t + 1, H, C)
        lm = beside_lanes_main(m, e)
        moved = 2.0 * sum(SI) * m - SI[0] * wm - SI[1] * cm - SI[2] * lm
        set_plane(adj_out, w, C, plane(base_adj, w, C) - DT * plane(mask, w, C) * moved)
        set_plane(pot_out, w, C, plane(base_pot, w, C) + m)

    parts = 2
    size = W // parts
    copies = []
    for k in range(parts):
        loop(k * size, (k + 1) * size, finish0, often)
        spot = pl.ds(k * size * C, size * C)
        for n, (src, dst) in enumerate(((adj_out, adj_prev), (pot_out, potential))):
            copies.append(pltpu.make_async_copy(src.at[spot], dst.at[spot], sems.at[n, k]))
            copies[-1].start()

    NC, NL = sheet.shape[1:]

    def whole_fine(x):
        if NL1 == LANES:
            parts = []
            for t in range(0, NC1, 8):
                wide8 = [lanes_at(x[t : t + 8], tile_lane // 2 + k * middle) for k in range(2)]
                for pick in picks[:2]:
                    parts.append(jnp.concatenate([rows_at(v, pick) for v in wide8], 1))
            return jnp.concatenate(parts, 0)
        along_c = lax.broadcasted_iota(jnp.int32, (NC, NC1), 0) // 2
        along_l = lax.broadcasted_iota(jnp.int32, (NL1, NL), 1) // 2
        twice_c = jnp.where(along_c == lax.broadcasted_iota(jnp.int32, (NC, NC1), 1), 1.0, 0.0).astype(F32)
        twice_l = jnp.where(along_l == lax.broadcasted_iota(jnp.int32, (NL1, NL), 0), 1.0, 0.0).astype(F32)
        return precise(precise(twice_c, x), twice_l)

    for s, i in enumerate((1, planes)):
        p = whole_fine(sweep(x1, b1, i, 1))
        c, l = around(p, 1)
        sheet[s] = (1.0 - OMEGA) * p + k0 * (coef[0] * p + coef[1] * c + coef[2] * l)

    owned = [patches[r : r + 1, :] for r in range(2)]
    spot = lax.broadcasted_iota(jnp.int32, (8, LANES), 0) * LANES + lane_of((8, LANES))
    spot = spot.astype(F32)
    start = half * C1
    totals = [jnp.zeros((C, LANES), F32) for _ in owned]
    small = [jnp.zeros((8, LANES), F32) for _ in owned]
    for v in range(n_wall):
        wall_s = wall_of(v)
        for j in range(n_len):
            ref = blocks[v * n_len + j]
            at_l = pl.ds(pl.multiple_of(length_of(j) * L, L), L)
            if compacted and v + j:
                for b in range(n_blk):
                    values = sheet[wall_s, b * C : (b + 1) * C, at_l]
                    ids = ref[96 + b * C : 96 + (b + 1) * C, :]
                    totals = [x + jnp.where(ids == e, values, 0.0) for x, e in zip(totals, owned)]
                small = [x + jnp.where(spot == e, ref[160:168, :], 0.0) for x, e in zip(small, owned)]
                continue

            def add(d, carry):
                big, little = carry
                values = sheet[wall_s, pl.ds(pl.multiple_of(blk_of(d) * C, C), C), at_l]
                ids = ref[d, start : start + C, :]
                parts = ref[d, start + C : start + C + 8, :]
                big = [x + jnp.where(ids == e, values, 0.0) for x, e in zip(big, owned)]
                little = [x + jnp.where(spot == e, parts, 0.0) for x, e in zip(little, owned)]
                return big, little

            totals, small = lax.fori_loop(0, n_blk, add, (totals, small), unroll=min(4, n_blk))
    factor = 1.0 / (2.0 * C * L / 2) ** 0.5
    for r in range(2):
        patch_grad[0, r] = (jnp.sum(totals[r]) + jnp.sum(small[r])) * factor
    for copy in copies:
        copy.wait()


def ring(x, axis, by):
    count = lax.axis_size(axis)
    return lax.ppermute(x, axis, [(i, (i + by) % count) for i in range(count)])


def across(x):
    n_wall = lax.axis_size("wall")
    pairs = [(l * n_wall + w, (1 - l) * n_wall + (w + 1) % n_wall) for l in range(2) for w in range(n_wall)]
    return lax.ppermute(x, ("len", "wall"), pairs)


def call(kernel, ins, outs, scratch, name, work=0, room=48):
    places = {"vmem": pltpu.VMEM, "smem": pltpu.SMEM, "any": pl.ANY, "hbm": pltpu.HBM}

    def specs(kinds):
        return [pl.BlockSpec(memory_space=places[kind]) for kind in kinds]

    cost = pl.CostEstimate(flops=work, bytes_accessed=work, transcendentals=0) if work else None
    return pl.pallas_call(
        kernel,
        out_shape=[jax.ShapeDtypeStruct(shape, F32) for shape, _ in outs],
        in_specs=specs(ins),
        out_specs=specs(kind for _, kind in outs),
        scratch_shapes=[pltpu.VMEM(shape, F32) if isinstance(shape, tuple) else shape for shape in scratch],
        compiler_params=pltpu.CompilerParams(vmem_limit_bytes=int(room * 2**20)),
        cost_estimate=cost,
        name=name,
    )


def body(adj_next, ion_slope, misfit, tissue_mask, patch_ids, owner_map):
    W, C, L = adj_next.shape
    n_blk, n_len, n_wall = lax.axis_size("blk"), lax.axis_size("len"), lax.axis_size("wall")
    electrodes = owner_map.shape[0]
    assert L == LANES and H * W == LANES and n_wall == 2 and electrodes == 2 * n_blk * n_len * n_wall
    N = W + 2 * H
    n_dir = 1 if n_len == 2 else 2
    cells = W * C
    vmem = "vmem"
    field, own = (N * C, L), (cells, L)
    raw = [x.reshape(cells, L) for x in (adj_next, ion_slope, tissue_mask, misfit)]

    *fields, wall_out = (faces := call(
        functools.partial(pack_faces, n_len),
        ["hbm"] * 4,
        [(own, vmem)] * 4
        + [((sum(FACES), C, L), vmem)]
        + [((4, C, L), vmem)] * n_dir
        + [((C, L), vmem)] * n_dir,
        [pltpu.VMEM(own, jnp.int32), pltpu.SemaphoreType.DMA((4, 4))],
        "faces",
        room=52.75,
    )(*raw))[:5]
    strip_out, corner_out = faces[5 : 5 + n_dir], faces[5 + n_dir :]
    wall_in = ring(wall_out, "wall", 1)
    if n_dir == 1:
        strips = [ring(strip_out[0], "len", 1)]
        corners = [across(corner_out[0])]
    else:
        strips = [ring(strip_out[1], "len", -1), ring(strip_out[0], "len", 1)]
        corners = [ring(ring(corner_out[1], "wall", 1), "len", -1), ring(ring(corner_out[0], "wall", 1), "len", 1)]

    near = (sum(near_rows(n_dir, W)[-1][::2]), L)
    halos = [wall_in, *strips, *corners]
    to_next, to_prev, own_rows = call(
        functools.partial(boundary, n_len, C),
        [vmem] * (5 + 2 * n_dir),
        [(near, vmem)] * 2 + [((2, 6, N, L), vmem)],
        [(48, N, L)],
        "boundary",
    )(*fields, *halos)
    from_next = ring(to_prev, "blk", -1)
    from_prev = ring(to_next, "blk", 1)
    qm, bm, be, coarse, surface, patches = call(
        functools.partial(sector, n_len, n_wall, C, electrodes),
        [vmem] * (6 + 2 * n_dir),
        [(field, vmem)] * 3 + [((cells // 8, L), vmem), ((C, L), vmem), ((8, L), vmem)],
        [field, (cells // 2, L)] + [field] * 8,
        "sector",
        work=16 * 10**6,
    )(*fields, *halos, owner_map.reshape(1, electrodes))

    rows = (8, N, L)
    wide = LANES * ((electrodes + LANES - 1) // LANES)
    message = (cells // 8 + C + 8, L)
    rows_n, rows_p, mine = call(
        functools.partial(correct, electrodes, n_len, n_wall),
        [vmem] * 6,
        [(rows, vmem), (rows, vmem), (message, vmem)],
        [(1, N, L), (wide, L)],
        "correct",
    )(own_rows, from_next, from_prev, coarse, surface, patch_ids)

    relative = n_blk <= 4
    moved = [ring(mine, "blk", d) for d in range(1, n_blk)] if relative else [lax.all_gather(mine, "blk")]
    base_adj, base_pot = call(
        functools.partial(source_part, n_len, n_wall, C),
        [vmem] * 6,
        [(own, vmem), (own, vmem)],
        [field] * 4 + [(2, N, L)],
        "source_part",
        work=12 * 10**6,
    )(bm, be, rows_n, rows_p, qm, fields[2])
    moved, base_adj = lax.optimization_barrier((moved, base_adj))
    sector_blocks = jnp.stack([mine] + moved) if relative else moved[0]
    compacted = (n_blk, n_len, C, W) == (4, 2, 16, 32)
    if compacted:
        brief, across_wall = call(
            functools.partial(compact, C, W),
            [vmem],
            [((168, L), vmem), ((200, L), vmem)],
            [(W // 4, n_blk * C // 2, L), (W // 8 + 1, n_blk * C // 2, L)],
            "compact",
        )(sector_blocks)
        len_brief = ring(brief, "len", 1)
        blocks = [sector_blocks, len_brief, ring(across_wall, "wall", 1), ring(len_brief, "wall", 1), brief]
    elif n_len == 2:
        here = [sector_blocks, ring(sector_blocks, "len", 1)]
    else:
        gathered = lax.all_gather(sector_blocks, "len")
        here = [gathered[j] for j in range(n_len)]
    if not compacted:
        blocks = here + [ring(x, "wall", 1) for x in here]

    NC1, NL1 = n_blk * C // 2, n_len * L // 2
    planes = n_wall * W // 2
    grids = [(planes // k + 2, NC1, NL1) for k in (1, 1, 2, 2, 4, 4)]
    Q = W // 2 + 2
    tall = (Q * (C + 8) + 16, L)
    taller = ((W + 2) * (C + 8) + 16, L)
    scratch = grids + [(Q * C, NL1), tall, tall, taller, taller, own, own]
    scratch += [(2, n_blk * C, n_len * L), (2, 2, 64, L), pltpu.SemaphoreType.DMA((2, 2))]
    adj_prev, potential, patch_grad = call(
        functools.partial(solve, (n_blk, n_len, n_wall), relative, compacted, C, W),
        [vmem] * (len(blocks) + 4),
        [(own, "any"), (own, "any"), ((1, 2), "smem")],
        scratch,
        "solve",
        room=48 if NC1 * NL1 <= 4096 else 58,
    )(*blocks, base_adj, base_pot, fields[2], patches)
    return adj_prev.reshape(W, C, L), potential.reshape(W, C, L), patch_grad


def solution(mesh):
    field = P(("groups", "wall"), "blk", "len")
    return jax.shard_map(
        body,
        mesh=mesh,
        in_specs=(field, field, field, field, field, P("groups")),
        out_specs=(field, field, P(("groups", "blk", "len", "wall"), None)),
        check_vma=False,
    )
```

```python
import functools

import jax
import jax.numpy as jnp
from jax import lax
from jax.experimental import pallas as pl
from jax.experimental.pallas import tpu as pltpu
from jax.sharding import PartitionSpec as P

SI = (0.6, 1.0, 3.0)
SE = (0.8, 1.2, 2.0)
SHIFT = 0.002
OMEGA = 0.8
DT = 0.1
H = 4
LANES = 128
HIGHEST = lax.Precision.HIGHEST
F32 = jnp.float32


def level_coef(level):
    return tuple((SI[i] + SE[i]) / 4.0**level for i in range(3))


def level_diag(level):
    return SHIFT + 2.0 * sum(level_coef(level))


def level_step(level):
    return OMEGA / level_diag(level)


def lane_of(shape):
    return lax.broadcasted_iota(jnp.int32, shape, len(shape) - 1)


def before(m, e):
    first = lane_of(m.shape) == 0
    rm, re = pltpu.roll(m, 1, 1), pltpu.roll(e, 1, 1)
    return jnp.where(first, re, rm), jnp.where(first, rm, re)


def after(m, e):
    last = lane_of(m.shape) == LANES - 1
    rm, re = pltpu.roll(m, LANES - 1, 1), pltpu.roll(e, LANES - 1, 1)
    return jnp.where(last, re, rm), jnp.where(last, rm, re)


def beside_lanes(m, e):
    bm, be = before(m, e)
    am, ae = after(m, e)
    return bm + am, be + ae


def beside_lanes_main(m, e):
    lane = lane_of(m.shape)
    ends = lanes_at(e, LANES - 1 - lane)
    left = jnp.where(lane == 0, ends, pltpu.roll(m, 1, 1))
    right = jnp.where(lane == LANES - 1, ends, pltpu.roll(m, LANES - 1, 1))
    return left + right


def beside_rows(x, row_before, row_after):
    rows = x.shape[0]
    row = lax.broadcasted_iota(jnp.int32, x.shape, 0)
    low = jnp.where(row == 0, row_before, pltpu.roll(x, 1, 0))
    high = jnp.where(row == rows - 1, row_after, pltpu.roll(x, rows - 1, 0))
    return low + high


def beside_dense(x):
    return pltpu.roll(x, 1, 0) + pltpu.roll(x, x.shape[0] - 1, 0)


def plane(ref, i, rows):
    return ref[pl.ds(pl.multiple_of(i * rows, rows), rows), :]


def set_plane(ref, i, rows, value):
    ref[pl.ds(pl.multiple_of(i * rows, rows), rows), :] = value


def loop(low, high, step, unroll):
    def wrapped(i, carry):
        step(i)
        return carry

    if unroll >= high - low:
        for i in range(low, high):
            step(i)
        return
    lax.fori_loop(low, high, wrapped, 0, unroll=unroll)


FACES = (H, H - 1, H - 1, H - 2)


def face_planes(array):
    return FACES[array], sum(FACES[:array])


def pack_faces(n_len, adj, ion, mask, mis, *rest):
    n_dir = 1 if n_len == 2 else 2
    fields, wall_out, rest = rest[:4], rest[4], rest[5:]
    strips, corners = rest[:n_dir], rest[n_dir : 2 * n_dir]
    whole_mask, sems = rest[2 * n_dir :]
    cells = adj.shape[0]
    C = wall_out.shape[1]
    W = cells // C
    wall, length = lax.axis_index("wall"), lax.axis_index("len")
    targets = (fields[0], fields[1], whole_mask, fields[3])
    copies = []
    for a, (src, dst) in enumerate(zip((adj, ion, mask, mis), targets)):
        part = cells // 4
        for k in range(4):
            spot = pl.ds(k * part, part)
            copies.append(pltpu.make_async_copy(src.at[spot], dst.at[spot], sems.at[a, k]))
            copies[-1].start()

    base = jnp.where(wall == 0, W - H, 0)
    group = lane_of((C, LANES)) // H
    turns = [jnp.where(length == 0, H, 0)] if n_dir == 1 else [H, 0]
    corner = [jnp.zeros((C, LANES), F32) for _ in range(n_dir)]
    for a in (0, 1, 3, 2):
        for k in range(4):
            copies[4 * a + k].wait()
        if a == 2:
            fields[2][...] = whole_mask[...].astype(F32)
        ref = fields[a]
        strip = [jnp.zeros((C, LANES), F32) for _ in range(n_dir)]
        for w in range(W):
            value = ref[w * C : (w + 1) * C, :]
            for d in range(n_dir):
                turned = pltpu.roll(value, lax.rem(H * w + turns[d], LANES), 1)
                strip[d] = jnp.where(group == w, turned, strip[d])
        for d in range(n_dir):
            strips[d][a] = strip[d]
        count, first = face_planes(a)
        for p in range(count):
            face = plane(ref, base + jnp.where(wall == 0, H - count, 0) + p, C)
            wall_out[first + p] = face
            slot = first + p
            for d in range(n_dir):
                turned = pltpu.roll(face, lax.rem(H * slot + turns[d], LANES), 1)
                corner[d] = jnp.where(group == slot, turned, corner[d])
    for d in range(n_dir):
        corners[d][...] = corner[d]


def dense(ref, row, N, C):
    return ref[pl.ds(row, N, stride=C), :]


def dense_pair(m, e, row, N, C):
    return dense(m, row, N, C), dense(e, row, N, C)


def dense_apply(pair, inner, outer, coef):
    m, e = pair
    lm, le = beside_lanes(m, e)
    double = 2.0 * sum(coef)
    out = [double * m - coef[0] * beside_dense(m) - coef[2] * lm, double * e - coef[0] * beside_dense(e) - coef[2] * le]
    for row in (inner, outer):
        if row is not None:
            out = [out[k] - coef[1] * row[k] for k in range(2)]
    return out


def near_rows(n_dir, W):
    start, places = 8 * n_dir, []
    for reach in (0, 1, 2, 2, 3):
        places.append((start, H - reach, W + 2 * reach))
        start += W + 2 * reach
    assert start % 8 == 0
    return places


def rim_tiles(values):
    return [value[s : s + 8] for value in values for s in range(0, value.shape[0], 8)]


def rim_places(n_len, length):
    if n_len == 2:
        return [(jnp.where(length == 0, 0, LANES - H), True)]
    return [(0, length < n_len - 1), (LANES - H, length > 0)]


def boundary(n_len, C, *refs):
    n_dir = 1 if n_len == 2 else 2
    raw, wall_in, refs = refs[:4], refs[4], refs[5:]
    strips, corners, refs = refs[:n_dir], refs[n_dir : 2 * n_dir], refs[2 * n_dir :]
    to_next, to_prev, own_rows, build = refs
    W = raw[0].shape[0] // C
    N = W + 2 * H
    wall, length = lax.axis_index("wall"), lax.axis_index("len")
    places = rim_places(n_len, length)

    def strip_rows(packed, first, count):
        lane, k = lane_of((count, LANES)), lax.broadcasted_iota(jnp.int32, (count, LANES), 0)
        out = jnp.zeros((count, LANES), F32)
        for row, (off, ok) in zip(packed, places):
            j = lax.rem(lane - off + LANES, LANES)
            index = jnp.clip(H * (first + k) + j, 0, LANES - 1)
            taken = lanes_at(jnp.broadcast_to(row, (count, LANES)), index)
            out = jnp.where(jnp.logical_and(j < H, ok), taken, out)
        return out

    slots = iter(range(build.shape[0]))

    def assembled(own, halo, count):
        ref = build.at[next(slots)]
        ref[0:8, :] = jnp.zeros((8, LANES), F32)
        ref[N - 8 : N, :] = jnp.zeros((8, LANES), F32)
        ref[H : H + W, :] = own
        ref[H - count : H, :] = jnp.where(wall == 0, 0.0, halo)
        ref[H + W : H + W + count, :] = jnp.where(wall == 0, halo, 0.0)
        return ref[...]

    def row_of(a, r):
        count, first = face_planes(a)
        halo = jnp.concatenate([wall_in[first + p, r : r + 1, :] for p in range(count)], 0)
        m = assembled(raw[a][pl.ds(r, W, stride=C), :], halo, count)
        own = strip_rows([strip[a, r : r + 1, :] for strip in strips], 0, W)
        halo = strip_rows([corner[r : r + 1, :] for corner in corners], first, 8)[:count]
        return m, assembled(own, halo, count)

    length_shift = jnp.where(length == 0, 0, H) if n_dir == 1 else H
    group = lane_of((8, LANES)) // (H * n_dir)
    for side, (out, order) in enumerate(((to_next, (C - 1, C - 2, C - 3, C - 4)), (to_prev, (0, 1, 2, 3)))):
        adj = [row_of(0, r) for r in order]
        mask = [row_of(2, r) for r in order[:3]]
        q = []
        for k in range(3):
            ion = row_of(1, order[k])
            moved = dense_apply(adj[k], adj[k + 1], adj[k - 1] if k else None, SI)
            q.append([adj[k][j] - DT * mask[k][j] * (moved[j] + ion[j] * adj[k][j]) for j in range(2)])
        near = dense_apply(q[0], q[1], None, SI)
        mis = row_of(3, order[0])
        near = [near[j] + mis[j] for j in range(2)]
        second = dense_apply(q[1], q[2], q[0], SI)[0] + row_of(3, order[1])[0]
        for value, (start, first, count) in zip((second, near[0], q[0][0], mask[0][0], adj[0][0]), near_rows(n_dir, W)):
            out[start : start + count, :] = value[first : first + count]
        packs = [jnp.zeros((8, LANES), F32) for _ in range(n_dir)]
        for t, tile in enumerate(rim_tiles((near[1], q[0][1], mask[0][1], adj[0][1]))):
            k, at = divmod(t, LANES // (H * n_dir))
            turned = pltpu.roll(tile, lax.rem(length_shift + H * n_dir * at, LANES), 1)
            packs[k] = jnp.where(group == at, turned, packs[k])
        for k in range(n_dir):
            out[8 * k : 8 * k + 8, :] = packs[k]
        for k, pair in enumerate((adj[0], mask[0], q[0])):
            own_rows[side, 2 * k] = pair[0]
            own_rows[side, 2 * k + 1] = pair[1]


def spots(m_ref, e_ref, i, rows, coef):
    m, e = plane(m_ref, i, rows), plane(e_ref, i, rows)
    wm = plane(m_ref, i - 1, rows) + plane(m_ref, i + 1, rows)
    we = plane(e_ref, i - 1, rows) + plane(e_ref, i + 1, rows)
    lm, le = beside_lanes(m, e)
    cm, ce = beside_rows(m, 0.0, 0.0), beside_rows(e, 0.0, 0.0)
    double = 2.0 * sum(coef)
    dm = double * m - coef[0] * wm - coef[1] * cm - coef[2] * lm
    de = double * e - coef[0] * we - coef[1] * ce - coef[2] * le
    return m, e, dm, de


def rim_lanes(lane, length, n_len):
    return jnp.logical_or(
        jnp.logical_and(lane < H, length < n_len - 1),
        jnp.logical_and(lane >= LANES - H, length > 0),
    )


def inside(i, wall, W, n_wall):
    w = wall * W + i - H
    return jnp.logical_and(w >= 0, w < n_wall * W)


def lanes_at(x, index):
    return jnp.take_along_axis(x, index, axis=1, mode="promise_in_bounds")


def rows_at(x, index):
    return jnp.take_along_axis(x, index, axis=0, mode="promise_in_bounds")


def halved(low, high):
    lane = lane_of(low.shape)
    even = 2 * lane % LANES
    pairs = [lanes_at(x, even) + lanes_at(x, even + 1) for x in (low, high)]
    return 0.125 * jnp.where(lane < LANES // 2, pairs[0], pairs[1])


def precise(a, b):
    return jnp.dot(a, b, precision=HIGHEST, preferred_element_type=F32)


def assemble(n_len, C, raw, wall_in, strips, corners, xm, xe):
    W = raw[0].shape[0] // C
    N = W + 2 * H
    wall, length = lax.axis_index("wall"), lax.axis_index("len")
    lane = lane_of((C, LANES))
    places = rim_places(n_len, length)
    seen = [jnp.logical_and(lax.rem(lane - off + LANES, LANES) < H, ok) for off, ok in places]

    def rim(packed, base):
        out = jnp.zeros((C, LANES), F32)
        for row, ok, (off, _) in zip(packed, seen, places):
            out = jnp.where(ok, pltpu.roll(row, lax.rem(off - base + LANES, LANES), 1), out)
        return out

    zero = jnp.zeros((C, LANES), F32)
    last = N - H
    for a, own in enumerate(raw):
        packed = [strip[a] for strip in strips]
        for w in range(W):
            set_plane(xm[a], w + H, C, plane(own, w, C))
            set_plane(xe[a], w + H, C, rim(packed, H * w))
        packed = [corner[...] for corner in corners]
        for i in range(H):
            for at in (i, last + i):
                set_plane(xm[a], at, C, zero)
                set_plane(xe[a], at, C, zero)
        count, first = face_planes(a)
        here = jnp.where(wall == 0, last, H - count)
        for p in range(count):
            set_plane(xm[a], here + p, C, wall_in[first + p])
            set_plane(xe[a], here + p, C, rim(packed, H * (first + p)))


def sector(n_len, n_wall, C, electrodes, *refs):
    n_dir = 1 if n_len == 2 else 2
    raw, wall_in, refs = refs[:4], refs[4], refs[5:]
    strips, corners, refs = refs[:n_dir], refs[n_dir : 2 * n_dir], refs[2 * n_dir :]
    owner, qm, bm, be, coarse, surface, patches, qe, pairs = refs[:9]
    xm, xe = refs[9:13], refs[13:17]
    assemble(n_len, C, raw, wall_in, strips, corners, xm, xe)
    N = qm.shape[0] // C
    W = N - 2 * H
    wall, length = lax.axis_index("wall"), lax.axis_index("len")
    rim = rim_lanes(lane_of((C, LANES)), length, n_len)
    zero = jnp.zeros((C, LANES), F32)
    for i in (0, N - 1):
        set_plane(qm, i, C, zero)
        set_plane(qe, i, C, zero)
    for i in (0, 1, N - 2, N - 1):
        set_plane(bm, i, C, zero)
        set_plane(be, i, C, zero)

    def parabolic(i):
        m, e, dm, de = spots(xm[0], xe[0], i, C, SI)
        set_plane(qm, i, C, m - DT * plane(xm[2], i, C) * (dm + plane(xm[1], i, C) * m))
        set_plane(qe, i, C, e - DT * plane(xe[2], i, C) * (de + plane(xe[1], i, C) * e))

    loop(1, N - 1, parabolic, N)

    def elliptic_source(i):
        m, e, dm, de = spots(qm, qe, i, C, SI)
        ok = inside(i, wall, W, n_wall)
        set_plane(bm, i, C, jnp.where(ok, plane(xm[3], i, C) + dm, 0.0))
        set_plane(be, i, C, jnp.where(jnp.logical_and(rim, ok), plane(xe[3], i, C) + de, 0.0))

    loop(2, N - 2, elliptic_source, N)

    coef, k0 = level_coef(0), level_step(0)

    def left(i):
        m, e = plane(bm, i, C), plane(be, i, C)
        wm = plane(bm, i - 1, C) + plane(bm, i + 1, C)
        cm = beside_rows(m, 0.0, 0.0)
        lm = beside_lanes_main(m, e)
        return m, (1.0 - OMEGA) * m + k0 * (coef[0] * wm + coef[1] * cm + coef[2] * lm)

    def pair(q):
        i = 2 * q + H
        m, first = left(i)
        n, second = left(i + 1)
        set_plane(pairs, q, C, first + second)

        @pl.when(jnp.logical_and(q == 0, wall == 0))
        def _():
            surface[...] = k0 * (m + first)

        @pl.when(jnp.logical_and(q == W // 2 - 1, wall == n_wall - 1))
        def _():
            surface[...] = k0 * (n + second)

    loop(0, W // 2, pair, W)

    half = W * C // 8
    z = pairs[pl.ds(0, 2 * half, stride=2), :] + pairs[pl.ds(1, 2 * half, stride=2), :]
    coarse[...] = halved(z[:half], z[half:])

    blk = lax.axis_index("blk")
    me = (blk * n_len + length) * n_wall + wall
    which = lax.broadcasted_iota(jnp.int32, (1, electrodes), 1).astype(F32)
    mine = owner[...] == me
    patches[0:1, :] = jnp.full((1, LANES), jnp.min(jnp.where(mine, which, float(electrodes))))
    patches[1:2, :] = jnp.full((1, LANES), jnp.max(jnp.where(mine, which, -1.0)))
    patches[2:8, :] = jnp.zeros((6, LANES), F32)


def unpacked(ref, n_len, length, N):
    n_dir = 1 if n_len == 2 else 2
    mains = []
    for start, first, count in near_rows(n_dir, N - 2 * H):
        begin = min(start - first, ref.shape[0] - N)
        value = ref[begin : begin + N, :]
        behind = start - first - begin
        mains.append(pltpu.roll(value, N - behind, 0) if behind else value)
    rim = rim_lanes(lane_of((8, LANES)), length, n_len)
    shift = jnp.where(length == 0, 0, H) if n_dir == 1 else H
    rims = []
    for k in range(4):
        parts = []
        for s in range(N // 8):
            pack, at = divmod(k * (N // 8) + s, LANES // (H * n_dir))
            back = lax.rem(2 * LANES - shift - H * n_dir * at, LANES)
            parts.append(jnp.where(rim, pltpu.roll(ref[8 * pack : 8 * pack + 8, :], back, 1), 0.0))
        rims.append(jnp.concatenate(parts, 0))
    second, near, q, mask, adj = mains
    return (adj, rims[3]), (mask, rims[2]), (q, rims[1]), (near, rims[0]), second


def lateral(pair):
    return dense_apply(pair, None, None, SI)


def source_rows(own, other):
    adj_o, mask_o, q_o = own
    adj_n, mask_n, q_n, p_n, second_n = other
    step = DT * SI[1]
    delta_o = [step * mask_o[k] * adj_n[k] for k in range(2)]
    delta_n = [step * mask_n[k] * adj_o[k] for k in range(2)]
    lat_o, lat_n = lateral(delta_o), lateral(delta_n)
    near = [lat_o[k] - SI[1] * (q_n[k] + delta_n[k]) for k in range(2)]
    second = [-SI[1] * delta_o[k] for k in range(2)]
    halo = [p_n[k] + lat_n[k] - SI[1] * (q_o[k] + delta_o[k]) for k in range(2)]
    halo_second = second_n - SI[1] * delta_n[0]
    return near, second, halo, halo_second, delta_o[0]


def correct(electrodes, n_len, n_wall, own_rows, from_next, from_prev, coarse, surface, ids, *rest):
    rows_n, rows_p, message = rest[:3]
    lines, sums = rest[3:]
    _, C, L = ids.shape
    N = own_rows.shape[2]
    W = N - 2 * H
    wall, length = lax.axis_index("wall"), lax.axis_index("len")
    ok_m = inside(lax.broadcasted_iota(jnp.int32, (N, LANES), 0), wall, W, n_wall)
    ok_e = jnp.logical_and(ok_m, rim_lanes(lane_of((N, LANES)), length, n_len))
    coef, k0 = level_coef(0), level_step(0)
    y = surface[...]
    row = lax.broadcasted_iota(jnp.int32, (C, LANES), 0)
    at = pl.ds(jnp.where(wall == 0, H, W + H - 1), 1)
    lows, highs = [], []
    W1, C1 = W // 2, C // 2
    for side, (other, out, order) in enumerate(
        ((from_next, rows_n, (C - 1, C - 2, C - 3)), (from_prev, rows_p, (0, 1, 2)))
    ):
        own = [(own_rows[side, 2 * k], own_rows[side, 2 * k + 1]) for k in range(3)]
        near, second, halo, halo_second, delta = source_rows(own, unpacked(other, n_len, length, N))
        near = [jnp.where(ok_m, near[0], 0.0), jnp.where(ok_e, near[1], 0.0)]
        second = [jnp.where(ok_m, second[0], 0.0), jnp.where(ok_e, second[1], 0.0)]
        out[0] = halo_m = jnp.where(ok_m, halo[0], 0.0)
        out[1] = jnp.where(ok_e, halo[1], 0.0)
        out[2] = jnp.where(ok_m, halo_second, 0.0)
        out[3] = delta
        out[4], out[5] = near
        out[6], out[7] = second

        def turned(pair, beside):
            m, e = pair
            return (1.0 - OMEGA) * m + k0 * (
                coef[0] * beside_dense(m) + coef[2] * beside_lanes_main(m, e) + coef[1] * beside
            )

        first = turned(near, second[0] + halo_m)
        next_one = turned(second, near[0])
        third = k0 * coef[1] * second[0]
        for k, change in enumerate((near[0] + first, second[0] + next_one, third)):
            lines[0] = change
            y = y + jnp.where(row == order[k], k0 * lines[0, at, :], 0.0)
        for change in (first + next_one, third):
            lines[0] = change
            both = lines[0, pl.ds(H, W1, stride=2), :] + lines[0, pl.ds(H + 1, W1, stride=2), :]
            lows.append(both[: W1 // 2])
            highs.append(both[W1 // 2 :])
    add = halved(jnp.concatenate(lows, 0), jnp.concatenate(highs, 0))
    half = W * C // 8
    message[0:half, :] = coarse[...]
    for k, c1 in enumerate((C1 - 1, C1 - 2, 0, 1)):
        spot = pl.ds(c1, W1 // 2, stride=C1)
        message[spot, :] = message[spot, :] + add[k * (W1 // 2) : (k + 1) * (W1 // 2)]
    patch = ids[0]
    message[half : half + C, :] = patch.astype(F32)
    wide = sums.shape[0]
    if wide > electrodes:
        sums[...] = jnp.zeros(sums.shape, F32)

    def one(e):
        sums[pl.ds(e, 1), :] = jnp.sum(jnp.where(patch == e, y, 0.0), axis=0, keepdims=True)

    loop(0, electrodes, one, 32 if electrodes <= 32 else 8)
    totals = lax.dot_general(
        jnp.ones((8, LANES), F32), sums[...], (((1,), (1,)), ((), ())), precision=HIGHEST, preferred_element_type=F32
    )
    message[half + C : half + C + 8, :] = jnp.zeros((8, LANES), F32)
    for t in range(wide // LANES):
        message[half + C + t : half + C + t + 1, :] = totals[0:1, t * LANES : (t + 1) * LANES]


def source_part(n_len, n_wall, C, bm, be, rows_n, rows_p, qm, mask, base_adj, base_pot, fm, fe, tm, te, hp):
    N = bm.shape[0] // C
    W = N - 2 * H
    length, wall = lax.axis_index("len"), lax.axis_index("wall")
    fm[...] = bm[...]
    fe[...] = be[...]
    for rows, near, second in ((rows_n, C - 1, C - 2), (rows_p, 0, 1)):
        for k, at in ((4, near), (6, second)):
            spot = pl.ds(at, N, stride=C)
            fm[spot, :] = fm[spot, :] + rows[k]
            fe[spot, :] = fe[spot, :] + rows[k + 1]
    coef, k0 = level_coef(0), level_step(0)
    rim = rim_lanes(lane_of((C, LANES)), length, n_len)

    def part(i):
        m, e = plane(fm, i, C), plane(fe, i, C)
        wm = plane(fm, i - 1, C) + plane(fm, i + 1, C)
        we = plane(fe, i - 1, C) + plane(fe, i + 1, C)
        lm, le = beside_lanes(m, e)
        at = pl.ds(i, 1)
        cm = beside_rows(m, rows_p[0, at, :], rows_n[0, at, :])
        ce = beside_rows(e, rows_p[1, at, :], rows_n[1, at, :])
        pm = k0 * ((2.0 - OMEGA) * m + k0 * (coef[0] * wm + coef[1] * cm + coef[2] * lm))
        pe = k0 * ((2.0 - OMEGA) * e + k0 * (coef[0] * we + coef[1] * ce + coef[2] * le))
        set_plane(tm, i, C, jnp.where(inside(i, wall, W, n_wall), pm, 0.0))
        set_plane(te, i, C, jnp.where(rim, pe, 0.0))

    loop(H - 1, N - H + 1, part, 2)
    for side, (rows, at) in enumerate(((rows_n, C - 1), (rows_p, 0))):
        m = rows[0]
        total = (
            coef[0] * beside_dense(m)
            + coef[1] * (rows[2] + dense(fm, at, N, C))
            + coef[2] * beside_lanes_main(m, rows[1])
        )
        hp[side] = k0 * ((2.0 - OMEGA) * m + k0 * total)
    row = lax.broadcasted_iota(jnp.int32, (C, LANES), 0)

    def finish(w):
        i = w + H
        m, e = plane(tm, i, C), plane(te, i, C)
        at = pl.ds(i, 1)
        wm = plane(tm, i - 1, C) + plane(tm, i + 1, C)
        cm = beside_rows(m, hp[1, at, :], hp[0, at, :])
        lm = beside_lanes_main(m, e)
        lam = plane(qm, i, C)
        lam = lam + jnp.where(row == C - 1, rows_n[3, at, :], 0.0) + jnp.where(row == 0, rows_p[3, at, :], 0.0)
        moved = 2.0 * sum(SI) * m - SI[0] * wm - SI[1] * cm - SI[2] * lm
        set_plane(base_adj, w, C, lam - DT * plane(mask, w, C) * moved)
        set_plane(base_pot, w, C, m)

    loop(0, W, finish, 2)


def halves(shape):
    lane = lane_of(shape)
    return lane, lane % (LANES // 2)


def compact(C, W, blocks, out, wall_out, sheet1, coarse2):
    n_blk = blocks.shape[0]
    W1, C1 = W // 2, C // 2
    half, start, middle = W1 // 2, W1 // 2 * C1, LANES // 2
    blk, length, wall = lax.axis_index("blk"), lax.axis_index("len"), lax.axis_index("wall")
    sums = jnp.zeros((8, LANES), F32)
    for d in range(n_blk):
        b = lax.rem(blk - d + n_blk, n_blk)
        for i in range(half):
            sheet1[i, pl.ds(pl.multiple_of(C1 * b, C1), C1), :] = blocks[d, i * C1 : (i + 1) * C1, :]
        out[pl.ds(pl.multiple_of(96 + C * b, C), C), :] = blocks[d, start : start + C, :]
        sums = sums + blocks[d, start + C : start + C + 8, :]
    out[160:168, :] = sums
    NC1 = sheet1.shape[1]
    lane, at = halves((NC1, LANES))
    low = lane < middle
    coef, k1 = level_coef(1), level_step(1)
    ends = pltpu.roll(sheet1[half - 1], middle, 1), pltpu.roll(sheet1[0], middle, 1)
    for q in range(half // 2):
        both = sheet1[2 * q] + sheet1[2 * q + 1]
        prev = sheet1[2 * q - 1] if q else jnp.where(low, 0.0, ends[0])
        after_it = sheet1[2 * q + 2] if 2 * q + 2 < half else jnp.where(low, ends[1], 0.0)
        c = pltpu.roll(both, 1, 0) + pltpu.roll(both, NC1 - 1, 0)
        l = jnp.where(at == 0, 0.0, pltpu.roll(both, 1, 1)) + jnp.where(
            at == middle - 1, 0.0, pltpu.roll(both, LANES - 1, 1)
        )
        left = (1.0 - OMEGA) * both + k1 * (coef[0] * (prev + both + after_it) + coef[1] * c + coef[2] * l)
        coarse2[q] = 0.125 * twins(left, 1)
    coarse2[half // 2] = 0.125 * twins(jnp.where(wall == 0, sheet1[half - 1], sheet1[0]), 1)
    rows2 = NC1 // 2
    lane2, at2 = halves((rows2, LANES))
    pick = lane2 - at2 + 2 * (at2 % (middle // 2))
    for p in range(half // 4):
        pair = [lanes_at(coarse2[2 * p + k, pl.ds(0, rows2, stride=2), :], pick) for k in range(2)]
        out[rows2 * p : rows2 * (p + 1), :] = jnp.where(at2 < middle // 2, pair[0], pair[1])
    beside = jnp.zeros((NC1, LANES), F32)
    base = jnp.where(length == 0, middle - H, 0)
    for i in range(half):
        turned = pltpu.roll(sheet1[i], lax.rem(H * i - base + LANES, LANES), 1)
        beside = jnp.where(at // H == i, turned, beside)
    index = lax.broadcasted_iota(jnp.int32, (8, LANES), 0) ^ 1
    line = beside + jnp.concatenate([rows_at(beside[t : t + 8], index) for t in range(0, NC1, 8)], 0)
    line = 0.125 * (line + pltpu.roll(line, LANES - H, 1))
    m = lane - 96
    spot = jnp.where(m < H, 8 * m, middle + 8 * (m - H)) + jnp.where(length == 0, H - 1, 0)
    line = lanes_at(line, jnp.clip(spot, 0, LANES - 1))
    beside = jnp.where(jnp.logical_and(m >= 0, m < 8), line, beside)
    out[32 : 32 + NC1, :] = beside
    face = coarse2[half // 2, pl.ds(0, rows2, stride=2), :]
    face = lanes_at(face, jnp.where(wall == 0, middle, 0) + 2 * (at2 % (middle // 2)))
    inner = jnp.logical_and(lane2 >= middle // 2, lane2 < middle)
    out[32 : 32 + rows2, :] = jnp.where(inner, face, beside[:rows2])
    inner_surface = jnp.where(low, sheet1[0], pltpu.roll(sheet1[1], middle, 1))
    outer_surface = jnp.where(low, pltpu.roll(sheet1[half - 2], middle, 1), sheet1[half - 1])
    out[64 : 64 + NC1, :] = jnp.where(wall == 0, inner_surface, outer_surface)
    wall_out[0:168, :] = out[...]
    last = jnp.where(low, pltpu.roll(sheet1[half - 1], middle, 1), sheet1[half - 2])
    wall_out[168 : 168 + NC1, :] = jnp.where(wall == 0, last, inner_surface)


def around(x, by):
    rows, lanes = x.shape
    lane = lane_of(x.shape)
    c = pltpu.roll(x, by, 0) + pltpu.roll(x, rows - by, 0)
    l = jnp.where(lane < by, 0.0, pltpu.roll(x, by, 1)) + jnp.where(
        lane >= lanes - by, 0.0, pltpu.roll(x, lanes - by, 1)
    )
    return c, l


def twins(x, by):
    rows, lanes = x.shape
    if lanes == LANES:
        index = lax.broadcasted_iota(jnp.int32, (8, LANES), 0) ^ by
        x = x + jnp.concatenate([rows_at(x[t : t + 8], index) for t in range(0, rows, 8)], 0)
        return x + lanes_at(x, lane_of(x.shape) ^ by)
    row = lax.broadcasted_iota(jnp.int32, x.shape, 0)
    lane = lane_of(x.shape)
    x = x + jnp.where((row & by) == 0, pltpu.roll(x, rows - by, 0), pltpu.roll(x, by, 0))
    return x + jnp.where((lane & by) == 0, pltpu.roll(x, lanes - by, 1), pltpu.roll(x, by, 1))


def solve(sizes, relative, compacted, C, W, *refs):
    n_blk, n_len, n_wall = sizes
    count = n_len * n_wall + compacted
    blocks, refs = refs[:count], refs[count:]
    base_adj, base_pot, mask, patches, adj_prev, potential, patch_grad = refs[:7]
    b1, x1, b2, x2, b3, x3, near, pm, pe, tm, te, adj_out, pot_out, sheet, briefs, sems = refs[7:]
    L = LANES
    W1, C1 = W // 2, C // 2
    planes, NC1, NL1 = b1.shape
    planes -= 2
    blk, length, wall = lax.axis_index("blk"), lax.axis_index("len"), lax.axis_index("wall")
    half = W1 // 2
    middle = LANES // 2
    lane8 = lane_of((C1, LANES))
    often = 40 if NC1 * NL1 <= 4096 else 1

    def blk_of(d):
        return lax.rem(blk - d + n_blk, n_blk) if relative else d

    def length_of(j):
        return (length + j) % n_len if n_len == 2 else j

    def wall_of(v):
        return (wall + v) % n_wall

    zero1 = jnp.zeros((NC1, NL1), F32)
    for ref in (b1, x1, b2, x2, b3, x3):
        ref[0] = zero1
        ref[ref.shape[0] - 1] = zero1

    if not compacted:
        for v in range(n_wall):
            wall_s = wall_of(v)
            mine = blocks[v * n_len : (v + 1) * n_len]

            def unpack(d):
                at = pl.ds(pl.multiple_of(C1 * blk_of(d), C1), C1)
                for t in range(n_len // 2):
                    one, two = mine[2 * t], mine[2 * t + 1]
                    for i in range(half):
                        a, b = one[d, i * C1 : (i + 1) * C1, :], two[d, i * C1 : (i + 1) * C1, :]
                        if n_len == 2:
                            a, b = jnp.where(length == 0, a, b), jnp.where(length == 0, b, a)
                        spot = 1 + wall_s * W1 + i
                        lanes = slice(t * LANES, (t + 1) * LANES)
                        b1[spot, at, lanes] = jnp.where(lane8 < middle, a, pltpu.roll(b, middle, 1))
                        b1[spot + half, at, lanes] = jnp.where(lane8 < middle, pltpu.roll(a, middle, 1), b)

            loop(0, n_blk, unpack, 4)
    if compacted:
        stack, len_brief, wall_brief, both_brief, own_brief = blocks
        lane8 = lane_of((C1, LANES))
        here8 = lane8 // middle == length
        here = lane_of((NC1, LANES)) // middle == length
        face_lane = jnp.where(length == 0, middle, middle - H)
        near8 = jnp.logical_and(lane8 >= face_lane, lane8 < face_lane + H)
        at_face = jnp.logical_and(lane_of((NC1, LANES)) >= face_lane, lane_of((NC1, LANES)) < face_lane + H)
        for d in range(n_blk):
            row = pl.multiple_of(C1 * blk_of(d), C1)
            beside = len_brief[pl.ds(32 + row, C1), :]
            for i in range(half):
                a = stack[d, i * C1 : (i + 1) * C1, :]
                b = pltpu.roll(a, middle, 1)
                for k, value in enumerate((jnp.where(length == 0, a, b), jnp.where(length == 0, b, a))):
                    turn = lax.rem(face_lane - H * i - middle * k + 2 * LANES, LANES)
                    rest = jnp.where(near8, pltpu.roll(beside, turn, 1), 0.0)
                    b1[1 + wall * W1 + i + half * k, pl.ds(row, C1), :] = jnp.where(here8, value, rest)

        def two_planes(tile):
            turned = pltpu.roll(tile, middle, 1)
            return jnp.where(length == 0, tile, turned), jnp.where(length == 0, turned, tile)

        beyond = two_planes(wall_brief[168 : 168 + NC1, :])
        beside = both_brief[32 : 32 + NC1, :]
        for k in range(2):
            off = jnp.where(wall == 0, H * k, middle + H * (half - 1 - k))
            rest = jnp.where(at_face, pltpu.roll(beside, lax.rem(face_lane - off + 2 * LANES, LANES), 1), 0.0)
            b1[jnp.where(wall == 0, 1 + W1 + k, W1 - k)] = jnp.where(here, beyond[k], rest)
        for k in range(2):
            theirs = two_planes(len_brief[64 : 64 + NC1, :])[1 - k]
            spot = jnp.where(wall == 0, 1, planes - 1) + k
            b1[spot] = jnp.where(here, b1[spot], theirs)
            ours = two_planes(wall_brief[64 : 64 + NC1, :])[k]
            theirs = two_planes(both_brief[64 : 64 + NC1, :])[1 - k]
            b1[jnp.where(wall == 0, planes - 1, 1) + k] = jnp.where(here, ours, theirs)
        first_half = length == 0
        for k in range(2):
            ours = jnp.where(wall == k, own_brief[0:64, :], wall_brief[0:64, :])
            theirs = jnp.where(wall == k, len_brief[0:64, :], both_brief[0:64, :])
            briefs[0, k] = jnp.where(first_half, ours, theirs)
            briefs[1, k] = jnp.where(first_half, theirs, ours)
        lane_8 = lane_of((8, LANES))
        quarter = middle // 2
        left_quarter = lane_8 % middle < quarter
        pairs_index = [lane_8 // 2, middle + lane_8 // 2]
        facing = jnp.logical_and(lane_8 >= middle - 2, lane_8 < middle + 2)
        coef1 = [level_step(1) * x for x in level_coef(1)]
        rows2 = NC1 // 2

        def merged(w, start):
            one, two = briefs[0, w, start : start + 8, :], briefs[1, w, start : start + 8, :]
            even = jnp.where(left_quarter, one, pltpu.roll(two, quarter, 1))
            odd = jnp.where(left_quarter, pltpu.roll(one, LANES - quarter, 1), two)
            return even, odd

        for w in range(n_wall):
            for t in range(rows2 // 8):
                lines = [briefs[h, w, pl.ds(32 + 16 * t, 8, stride=2), :] for h in range(2)]
                lines = [lanes_at(x, jnp.minimum(96 + lane_8 // 4, LANES - 1)) for x in lines]
                lines = coef1[2] * jnp.where(lane_8 % 4 < 2, lines[1], lines[0])
                for p in range(half // 4):
                    tiles = merged(w, rows2 * p + 8 * t)
                    for odd in range(2):
                        for high in range(2):
                            k = 2 * p + odd + half // 2 * high
                            value = lanes_at(tiles[odd], pairs_index[high])
                            line = pltpu.roll(lines, middle - 2 - 4 * k, 1)
                            value = value + jnp.where(facing, line, 0.0)
                            if k == (half - 1 if w == 0 else 0):
                                value = value + coef1[0] * lanes_at(merged(1 - w, 32 + 8 * t)[1], pairs_index[0])
                            for r in range(2):
                                b2[1 + w * half + k, pl.ds(16 * t + r, 8, stride=2), :] = value

    def total_of(x, wsum, level, by):
        coef = level_coef(level)
        c, l = around(x, by)
        return level_step(level) * (coef[0] * wsum + coef[1] * c + coef[2] * l)

    def left_pair(ref, i, level):
        both = ref[i] + ref[i + 1]
        return (1.0 - OMEGA) * both + total_of(both, ref[i - 1] + both + ref[i + 2], level, 2 ** (level - 1))

    def sweep(x_ref, b_ref, i, level):
        x = x_ref[i]
        total = total_of(x, x_ref[i - 1] + x_ref[i + 1], level, 2 ** (level - 1))
        return (1.0 - OMEGA) * x + level_step(level) * b_ref[i] + total

    def down1(q):
        b2[1 + q] = 0.125 * twins(left_pair(b1, 2 * q + 1, 1), 1)

    if not compacted:
        loop(0, planes // 2, down1, often)

    def down2(q):
        b3[1 + q] = 0.125 * twins(left_pair(b2, 2 * q + 1, 2), 2)

    loop(0, planes // 4, down2, often)

    deep = planes // 4
    k3 = level_step(3)

    x2[1 + deep] = zero1

    def start3(q):
        b = b3[1 + q]
        x2[1 + q] = k3 * ((2.0 - OMEGA) * b + total_of(b, b3[q] + b3[2 + q], 3, 4))

    loop(0, deep, start3, often)

    def sweep3(q):
        x3[1 + q] = sweep(x2, b3, 1 + q, 3)

    loop(0, deep, sweep3, often)
    k2 = level_step(2)

    def up2(q):
        coarse = x3[1 + q]
        x2[1 + 2 * q] = k2 * b2[1 + 2 * q] + coarse
        x2[2 + 2 * q] = k2 * b2[2 + 2 * q] + coarse

    loop(0, planes // 4, up2, often)

    k1 = level_step(1)

    def up1(q):
        fine = sweep(x2, b2, 1 + q, 2)
        x1[1 + 2 * q] = k1 * b1[1 + 2 * q] + fine
        x1[2 + 2 * q] = k1 * b1[2 + 2 * q] + fine

    if compacted:
        loop(0, half, lambda q: up1(half * wall + q), often)
        up1(half - wall)
        up1((planes // 2 - 1) * (1 - wall))
    else:
        loop(0, planes // 2, up1, often)

    Q = W1 + 2
    sectors = (blk, lax.rem(blk + 1, n_blk), lax.rem(blk + n_blk - 1, n_blk))
    spots3 = [pl.ds(pl.multiple_of(s * C1, C1), C1) for s in sectors]
    row8 = lax.broadcasted_iota(jnp.int32, (C1, NL1), 0)

    def three(ref, i):
        return jnp.concatenate([ref[i, s, :] for s in spots3], 0)

    def finish1(q):
        i = wall * W1 + q
        x = three(x1, i)
        wsum = three(x1, jnp.maximum(i - 1, 0)) + three(x1, jnp.minimum(i + 1, planes + 1))
        value = (1.0 - OMEGA) * x + k1 * three(b1, i) + total_of(x, wsum, 1, 1)
        value = jnp.where(jnp.logical_and(i >= 1, i <= planes), value, 0.0)
        set_plane(near, 2 * q, C1, value[:C1])
        set_plane(near, 2 * q + 1, C1, jnp.where(row8 < 2, value[C1 : 2 * C1], value[2 * C1 :]))

    loop(0, Q, finish1, often)

    first = length * middle
    R = C + 8
    row8 = lax.broadcasted_iota(jnp.int32, (8, LANES), 0)
    tile_lane = lane_of((8, LANES))
    at_e = jnp.where(tile_lane < H, middle + tile_lane // 2, tile_lane // 2 - middle)
    rim8 = rim_lanes(tile_lane, length, n_len)
    if NL1 == LANES:
        index_m, index_e = first + tile_lane // 2, jnp.clip(first + at_e, 0, LANES - 1)

        def spread(tile):
            return lanes_at(tile, index_m), jnp.where(rim8, lanes_at(tile, index_e), 0.0)

    else:
        source = lax.broadcasted_iota(jnp.int32, (NL1, LANES), 0)
        lane = lane_of((NL1, LANES))
        at_all = jnp.where(lane < H, middle + lane // 2, jnp.where(lane >= LANES - H, lane // 2 - middle, 4 * NL1))
        take_m = jnp.where(source == first + lane // 2, 1.0, 0.0).astype(F32)
        take_e = jnp.where(source == first + at_all, 1.0, 0.0).astype(F32)

        def spread(tile):
            return precise(tile, take_m), precise(tile, take_e)

    picks = (row8 // 2, H + row8 // 2)
    ends = jnp.where(row8 < H, 6 + row8 // 2, row8 // 2 - 2)

    def fine_rows(q):
        own = spread(plane(near, 2 * q, C1))
        beside = spread(plane(near, 2 * q + 1, C1))
        for out, a, b in ((pm, own[0], beside[0]), (pe, own[1], beside[1])):
            parts = (jnp.where(row8 < 6, a, b), a, jnp.where(row8 < 2, b, a))
            index = (ends, 2 + row8 // 2, ends)
            for k in range(3):
                out[pl.ds(pl.multiple_of(8 + R * q + 8 * k, 8), 8), :] = rows_at(parts[k], index[k])

    loop(0, Q, fine_rows, often)
    for ref in (pm, pe):
        ref[0:8, :] = jnp.zeros((8, LANES), F32)
        ref[8 + R * Q : 16 + R * Q, :] = jnp.zeros((8, LANES), F32)
    coef, k0 = level_coef(0), level_step(0)
    def fine(ref, t, by=0, count=R):
        return ref[pl.ds(8 + R * t + by, count), :]

    def coarse_terms(q):
        out = []
        sides = beside_lanes(fine(pm, q), fine(pe, q))
        for ref, l in zip((pm, pe), sides):
            x = fine(ref, q)
            c = fine(ref, q, -1) + fine(ref, q, 1)
            out.append((1.0 - OMEGA) * x + k0 * (coef[0] * x + coef[1] * c + coef[2] * l))
        return out

    ks = k0 * coef[0]

    def set_fine(ref, t, value):
        ref[pl.ds(pl.multiple_of(8 + R * t, 8), R), :] = value

    def put_end(t, q, other, ok):
        set_fine(tm, t, jnp.where(ok, coarse_terms(q)[0] + ks * fine(pm, other), 0.0))

    put_end(0, 0, 1, wall > 0)
    put_end(W + 1, Q - 1, Q - 2, wall < n_wall - 1)
    rim = rim_lanes(lane_of((R, LANES)), length, n_len)

    def level0(q):
        gm, ge = coarse_terms(q)
        for t, other in ((2 * q - 1, q - 1), (2 * q, q + 1)):
            set_fine(tm, t, gm + ks * fine(pm, other))
            set_fine(te, t, jnp.where(rim, ge + ks * fine(pe, other), 0.0))

    loop(1, 1 + W1, level0, often)

    def finish0(w):
        t = w + 1
        m, e = fine(tm, t, H, C), fine(te, t, H, C)
        cm = fine(tm, t, H - 1, C) + fine(tm, t, H + 1, C)
        wm = fine(tm, t - 1, H, C) + fine(tm, t + 1, H, C)
        lm = beside_lanes_main(m, e)
        moved = 2.0 * sum(SI) * m - SI[0] * wm - SI[1] * cm - SI[2] * lm
        set_plane(adj_out, w, C, plane(base_adj, w, C) - DT * plane(mask, w, C) * moved)
        set_plane(pot_out, w, C, plane(base_pot, w, C) + m)

    parts = 2
    size = W // parts
    copies = []
    for k in range(parts):
        loop(k * size, (k + 1) * size, finish0, often)
        spot = pl.ds(k * size * C, size * C)
        for n, (src, dst) in enumerate(((adj_out, adj_prev), (pot_out, potential))):
            copies.append(pltpu.make_async_copy(src.at[spot], dst.at[spot], sems.at[n, k]))
            copies[-1].start()

    NC, NL = sheet.shape[1:]

    def whole_fine(x):
        if NL1 == LANES:
            parts = []
            for t in range(0, NC1, 8):
                wide8 = [lanes_at(x[t : t + 8], tile_lane // 2 + k * middle) for k in range(2)]
                for pick in picks[:2]:
                    parts.append(jnp.concatenate([rows_at(v, pick) for v in wide8], 1))
            return jnp.concatenate(parts, 0)
        along_c = lax.broadcasted_iota(jnp.int32, (NC, NC1), 0) // 2
        along_l = lax.broadcasted_iota(jnp.int32, (NL1, NL), 1) // 2
        twice_c = jnp.where(along_c == lax.broadcasted_iota(jnp.int32, (NC, NC1), 1), 1.0, 0.0).astype(F32)
        twice_l = jnp.where(along_l == lax.broadcasted_iota(jnp.int32, (NL1, NL), 0), 1.0, 0.0).astype(F32)
        return precise(precise(twice_c, x), twice_l)

    for s, i in enumerate((1, planes)):
        p = whole_fine(sweep(x1, b1, i, 1))
        c, l = around(p, 1)
        sheet[s] = (1.0 - OMEGA) * p + k0 * (coef[0] * p + coef[1] * c + coef[2] * l)

    owned = [patches[r : r + 1, :] for r in range(2)]
    spot = lax.broadcasted_iota(jnp.int32, (8, LANES), 0) * LANES + lane_of((8, LANES))
    spot = spot.astype(F32)
    start = half * C1
    totals = [jnp.zeros((C, LANES), F32) for _ in owned]
    small = [jnp.zeros((8, LANES), F32) for _ in owned]
    for v in range(n_wall):
        wall_s = wall_of(v)
        for j in range(n_len):
            ref = blocks[v * n_len + j]
            at_l = pl.ds(pl.multiple_of(length_of(j) * L, L), L)
            if compacted and v + j:
                for b in range(n_blk):
                    values = sheet[wall_s, b * C : (b + 1) * C, at_l]
                    ids = ref[96 + b * C : 96 + (b + 1) * C, :]
                    totals = [x + jnp.where(ids == e, values, 0.0) for x, e in zip(totals, owned)]
                small = [x + jnp.where(spot == e, ref[160:168, :], 0.0) for x, e in zip(small, owned)]
                continue

            def add(d, carry):
                big, little = carry
                values = sheet[wall_s, pl.ds(pl.multiple_of(blk_of(d) * C, C), C), at_l]
                ids = ref[d, start : start + C, :]
                parts = ref[d, start + C : start + C + 8, :]
                big = [x + jnp.where(ids == e, values, 0.0) for x, e in zip(big, owned)]
                little = [x + jnp.where(spot == e, parts, 0.0) for x, e in zip(little, owned)]
                return big, little

            totals, small = lax.fori_loop(0, n_blk, add, (totals, small), unroll=min(4, n_blk))
    factor = 1.0 / (2.0 * C * L / 2) ** 0.5
    for r in range(2):
        patch_grad[0, r] = (jnp.sum(totals[r]) + jnp.sum(small[r])) * factor
    for copy in copies:
        copy.wait()


def ring(x, axis, by):
    count = lax.axis_size(axis)
    return lax.ppermute(x, axis, [(i, (i + by) % count) for i in range(count)])


def across(x):
    n_wall = lax.axis_size("wall")
    pairs = [(l * n_wall + w, (1 - l) * n_wall + (w + 1) % n_wall) for l in range(2) for w in range(n_wall)]
    return lax.ppermute(x, ("len", "wall"), pairs)


def call(kernel, ins, outs, scratch, name, work=0, room=48):
    places = {"vmem": pltpu.VMEM, "smem": pltpu.SMEM, "any": pl.ANY, "hbm": pltpu.HBM}

    def specs(kinds):
        return [pl.BlockSpec(memory_space=places[kind]) for kind in kinds]

    cost = pl.CostEstimate(flops=work, bytes_accessed=work, transcendentals=0) if work else None
    return pl.pallas_call(
        kernel,
        out_shape=[jax.ShapeDtypeStruct(shape, F32) for shape, _ in outs],
        in_specs=specs(ins),
        out_specs=specs(kind for _, kind in outs),
        scratch_shapes=[pltpu.VMEM(shape, F32) if isinstance(shape, tuple) else shape for shape in scratch],
        compiler_params=pltpu.CompilerParams(vmem_limit_bytes=int(room * 2**20)),
        cost_estimate=cost,
        name=name,
    )


def body(adj_next, ion_slope, misfit, tissue_mask, patch_ids, owner_map):
    W, C, L = adj_next.shape
    n_blk, n_len, n_wall = lax.axis_size("blk"), lax.axis_size("len"), lax.axis_size("wall")
    electrodes = owner_map.shape[0]
    assert L == LANES and H * W == LANES and n_wall == 2 and electrodes == 2 * n_blk * n_len * n_wall
    N = W + 2 * H
    n_dir = 1 if n_len == 2 else 2
    cells = W * C
    vmem = "vmem"
    field, own = (N * C, L), (cells, L)
    raw = [x.reshape(cells, L) for x in (adj_next, ion_slope, tissue_mask, misfit)]

    *fields, wall_out = (faces := call(
        functools.partial(pack_faces, n_len),
        ["hbm"] * 4,
        [(own, vmem)] * 4
        + [((sum(FACES), C, L), vmem)]
        + [((4, C, L), vmem)] * n_dir
        + [((C, L), vmem)] * n_dir,
        [pltpu.VMEM(own, jnp.int32), pltpu.SemaphoreType.DMA((4, 4))],
        "faces",
        room=52.75,
    )(*raw))[:5]
    strip_out, corner_out = faces[5 : 5 + n_dir], faces[5 + n_dir :]
    wall_in = ring(wall_out, "wall", 1)
    if n_dir == 1:
        strips = [ring(strip_out[0], "len", 1)]
        corners = [across(corner_out[0])]
    else:
        strips = [ring(strip_out[1], "len", -1), ring(strip_out[0], "len", 1)]
        corners = [ring(ring(corner_out[1], "wall", 1), "len", -1), ring(ring(corner_out[0], "wall", 1), "len", 1)]

    near = (sum(near_rows(n_dir, W)[-1][::2]), L)
    halos = [wall_in, *strips, *corners]
    to_next, to_prev, own_rows = call(
        functools.partial(boundary, n_len, C),
        [vmem] * (5 + 2 * n_dir),
        [(near, vmem)] * 2 + [((2, 6, N, L), vmem)],
        [(48, N, L)],
        "boundary",
    )(*fields, *halos)
    from_next = ring(to_prev, "blk", -1)
    from_prev = ring(to_next, "blk", 1)
    qm, bm, be, coarse, surface, patches = call(
        functools.partial(sector, n_len, n_wall, C, electrodes),
        [vmem] * (6 + 2 * n_dir),
        [(field, vmem)] * 3 + [((cells // 8, L), vmem), ((C, L), vmem), ((8, L), vmem)],
        [field, (cells // 2, L)] + [field] * 8,
        "sector",
        work=16 * 10**6,
    )(*fields, *halos, owner_map.reshape(1, electrodes))

    rows = (8, N, L)
    wide = LANES * ((electrodes + LANES - 1) // LANES)
    message = (cells // 8 + C + 8, L)
    rows_n, rows_p, mine = call(
        functools.partial(correct, electrodes, n_len, n_wall),
        [vmem] * 6,
        [(rows, vmem), (rows, vmem), (message, vmem)],
        [(1, N, L), (wide, L)],
        "correct",
    )(own_rows, from_next, from_prev, coarse, surface, patch_ids)

    relative = n_blk <= 4
    moved = [ring(mine, "blk", d) for d in range(1, n_blk)] if relative else [lax.all_gather(mine, "blk")]
    base_adj, base_pot = call(
        functools.partial(source_part, n_len, n_wall, C),
        [vmem] * 6,
        [(own, vmem), (own, vmem)],
        [field] * 4 + [(2, N, L)],
        "source_part",
        work=12 * 10**6,
    )(bm, be, rows_n, rows_p, qm, fields[2])
    moved, base_adj = lax.optimization_barrier((moved, base_adj))
    sector_blocks = jnp.stack([mine] + moved) if relative else moved[0]
    compacted = (n_blk, n_len, C, W) == (4, 2, 16, 32)
    if compacted:
        brief, across_wall = call(
            functools.partial(compact, C, W),
            [vmem],
            [((168, L), vmem), ((200, L), vmem)],
            [(W // 4, n_blk * C // 2, L), (W // 8 + 1, n_blk * C // 2, L)],
            "compact",
        )(sector_blocks)
        len_brief = ring(brief, "len", 1)
        blocks = [sector_blocks, len_brief, ring(across_wall, "wall", 1), across(brief), brief]
    elif n_len == 2:
        here = [sector_blocks, ring(sector_blocks, "len", 1)]
    else:
        gathered = lax.all_gather(sector_blocks, "len")
        here = [gathered[j] for j in range(n_len)]
    if not compacted:
        blocks = here + [ring(x, "wall", 1) for x in here]

    NC1, NL1 = n_blk * C // 2, n_len * L // 2
    planes = n_wall * W // 2
    grids = [(planes // k + 2, NC1, NL1) for k in (1, 1, 2, 2, 4, 4)]
    Q = W // 2 + 2
    tall = (Q * (C + 8) + 16, L)
    taller = ((W + 2) * (C + 8) + 16, L)
    scratch = grids + [(Q * C, NL1), tall, tall, taller, taller, own, own]
    scratch += [(2, n_blk * C, n_len * L), (2, 2, 64, L), pltpu.SemaphoreType.DMA((2, 2))]
    adj_prev, potential, patch_grad = call(
        functools.partial(solve, (n_blk, n_len, n_wall), relative, compacted, C, W),
        [vmem] * (len(blocks) + 4),
        [(own, "any"), (own, "any"), ((1, 2), "smem")],
        scratch,
        "solve",
        room=48 if NC1 * NL1 <= 4096 else 58,
    )(*blocks, base_adj, base_pot, fields[2], patches)
    return adj_prev.reshape(W, C, L), potential.reshape(W, C, L), patch_grad


def solution(mesh):
    field = P(("groups", "wall"), "blk", "len")
    return jax.shard_map(
        body,
        mesh=mesh,
        in_specs=(field, field, field, field, field, P("groups")),
        out_specs=(field, field, P(("groups", "blk", "len", "wall"), None)),
        check_vma=False,
    )
```

```python
import functools

import jax
import jax.numpy as jnp
from jax import lax
from jax.experimental import pallas as pl
from jax.experimental.pallas import tpu as pltpu
from jax.sharding import PartitionSpec as P

SI = (0.6, 1.0, 3.0)
SE = (0.8, 1.2, 2.0)
SHIFT = 0.002
OMEGA = 0.8
DT = 0.1
H = 4
LANES = 128
HIGHEST = lax.Precision.HIGHEST
F32 = jnp.float32


def level_coef(level):
    return tuple((SI[i] + SE[i]) / 4.0**level for i in range(3))


def level_diag(level):
    return SHIFT + 2.0 * sum(level_coef(level))


def level_step(level):
    return OMEGA / level_diag(level)


def lane_of(shape):
    return lax.broadcasted_iota(jnp.int32, shape, len(shape) - 1)


def before(m, e):
    first = lane_of(m.shape) == 0
    rm, re = pltpu.roll(m, 1, 1), pltpu.roll(e, 1, 1)
    return jnp.where(first, re, rm), jnp.where(first, rm, re)


def after(m, e):
    last = lane_of(m.shape) == LANES - 1
    rm, re = pltpu.roll(m, LANES - 1, 1), pltpu.roll(e, LANES - 1, 1)
    return jnp.where(last, re, rm), jnp.where(last, rm, re)


def beside_lanes(m, e):
    bm, be = before(m, e)
    am, ae = after(m, e)
    return bm + am, be + ae


def beside_lanes_main(m, e):
    lane = lane_of(m.shape)
    ends = lanes_at(e, LANES - 1 - lane)
    left = jnp.where(lane == 0, ends, pltpu.roll(m, 1, 1))
    right = jnp.where(lane == LANES - 1, ends, pltpu.roll(m, LANES - 1, 1))
    return left + right


def beside_rows(x, row_before, row_after):
    rows = x.shape[0]
    row = lax.broadcasted_iota(jnp.int32, x.shape, 0)
    low = jnp.where(row == 0, row_before, pltpu.roll(x, 1, 0))
    high = jnp.where(row == rows - 1, row_after, pltpu.roll(x, rows - 1, 0))
    return low + high


def beside_dense(x):
    return pltpu.roll(x, 1, 0) + pltpu.roll(x, x.shape[0] - 1, 0)


def plane(ref, i, rows):
    return ref[pl.ds(pl.multiple_of(i * rows, rows), rows), :]


def set_plane(ref, i, rows, value):
    ref[pl.ds(pl.multiple_of(i * rows, rows), rows), :] = value


def loop(low, high, step, unroll):
    def wrapped(i, carry):
        step(i)
        return carry

    if unroll >= high - low:
        for i in range(low, high):
            step(i)
        return
    lax.fori_loop(low, high, wrapped, 0, unroll=unroll)


FACES = (H, H - 1, H - 1, H - 2)


def face_planes(array):
    return FACES[array], sum(FACES[:array])


def pack_faces(n_len, adj, ion, mask, mis, *rest):
    n_dir = 1 if n_len == 2 else 2
    fields, wall_out, rest = rest[:4], rest[4], rest[5:]
    strips, corners = rest[:n_dir], rest[n_dir : 2 * n_dir]
    whole_mask, sems = rest[2 * n_dir :]
    cells = adj.shape[0]
    C = wall_out.shape[1]
    W = cells // C
    wall, length = lax.axis_index("wall"), lax.axis_index("len")
    targets = (fields[0], fields[1], whole_mask, fields[3])
    copies = []
    for a, (src, dst) in enumerate(zip((adj, ion, mask, mis), targets)):
        part = cells // 4
        for k in range(4):
            spot = pl.ds(k * part, part)
            copies.append(pltpu.make_async_copy(src.at[spot], dst.at[spot], sems.at[a, k]))
            copies[-1].start()

    base = jnp.where(wall == 0, W - H, 0)
    group = lane_of((C, LANES)) // H
    turns = [jnp.where(length == 0, H, 0)] if n_dir == 1 else [H, 0]
    corner = [jnp.zeros((C, LANES), F32) for _ in range(n_dir)]
    for a in (0, 1, 3, 2):
        for k in range(4):
            copies[4 * a + k].wait()
        if a == 2:
            fields[2][...] = whole_mask[...].astype(F32)
        ref = fields[a]
        strip = [jnp.zeros((C, LANES), F32) for _ in range(n_dir)]
        for w in range(W):
            value = ref[w * C : (w + 1) * C, :]
            for d in range(n_dir):
                turned = pltpu.roll(value, lax.rem(H * w + turns[d], LANES), 1)
                strip[d] = jnp.where(group == w, turned, strip[d])
        for d in range(n_dir):
            strips[d][a] = strip[d]
        count, first = face_planes(a)
        for p in range(count):
            face = plane(ref, base + jnp.where(wall == 0, H - count, 0) + p, C)
            wall_out[first + p] = face
            slot = first + p
            for d in range(n_dir):
                turned = pltpu.roll(face, lax.rem(H * slot + turns[d], LANES), 1)
                corner[d] = jnp.where(group == slot, turned, corner[d])
    for d in range(n_dir):
        corners[d][...] = corner[d]


def dense(ref, row, N, C):
    return ref[pl.ds(row, N, stride=C), :]


def dense_pair(m, e, row, N, C):
    return dense(m, row, N, C), dense(e, row, N, C)


def dense_apply(pair, inner, outer, coef):
    m, e = pair
    lm, le = beside_lanes(m, e)
    double = 2.0 * sum(coef)
    out = [double * m - coef[0] * beside_dense(m) - coef[2] * lm, double * e - coef[0] * beside_dense(e) - coef[2] * le]
    for row in (inner, outer):
        if row is not None:
            out = [out[k] - coef[1] * row[k] for k in range(2)]
    return out


def near_rows(n_dir, W):
    start, places = 8 * n_dir, []
    for reach in (0, 1, 2, 2, 3):
        places.append((start, H - reach, W + 2 * reach))
        start += W + 2 * reach
    assert start % 8 == 0
    return places


def rim_tiles(values):
    return [value[s : s + 8] for value in values for s in range(0, value.shape[0], 8)]


def rim_places(n_len, length):
    if n_len == 2:
        return [(jnp.where(length == 0, 0, LANES - H), True)]
    return [(0, length < n_len - 1), (LANES - H, length > 0)]


def boundary(n_len, C, *refs):
    n_dir = 1 if n_len == 2 else 2
    raw, wall_in, refs = refs[:4], refs[4], refs[5:]
    strips, corners, refs = refs[:n_dir], refs[n_dir : 2 * n_dir], refs[2 * n_dir :]
    to_next, to_prev, own_rows, build = refs
    W = raw[0].shape[0] // C
    N = W + 2 * H
    wall, length = lax.axis_index("wall"), lax.axis_index("len")
    places = rim_places(n_len, length)

    def strip_rows(packed, first, count):
        lane, k = lane_of((count, LANES)), lax.broadcasted_iota(jnp.int32, (count, LANES), 0)
        out = jnp.zeros((count, LANES), F32)
        for row, (off, ok) in zip(packed, places):
            j = lax.rem(lane - off + LANES, LANES)
            index = jnp.clip(H * (first + k) + j, 0, LANES - 1)
            taken = lanes_at(jnp.broadcast_to(row, (count, LANES)), index)
            out = jnp.where(jnp.logical_and(j < H, ok), taken, out)
        return out

    slots = iter(range(build.shape[0]))

    def assembled(own, halo, count):
        ref = build.at[next(slots)]
        ref[0:8, :] = jnp.zeros((8, LANES), F32)
        ref[N - 8 : N, :] = jnp.zeros((8, LANES), F32)
        ref[H : H + W, :] = own
        ref[H - count : H, :] = jnp.where(wall == 0, 0.0, halo)
        ref[H + W : H + W + count, :] = jnp.where(wall == 0, halo, 0.0)
        return ref[...]

    def row_of(a, r):
        count, first = face_planes(a)
        halo = jnp.concatenate([wall_in[first + p, r : r + 1, :] for p in range(count)], 0)
        m = assembled(raw[a][pl.ds(r, W, stride=C), :], halo, count)
        own = strip_rows([strip[a, r : r + 1, :] for strip in strips], 0, W)
        halo = strip_rows([corner[r : r + 1, :] for corner in corners], first, 8)[:count]
        return m, assembled(own, halo, count)

    length_shift = jnp.where(length == 0, 0, H) if n_dir == 1 else H
    group = lane_of((8, LANES)) // (H * n_dir)
    for side, (out, order) in enumerate(((to_next, (C - 1, C - 2, C - 3, C - 4)), (to_prev, (0, 1, 2, 3)))):
        adj = [row_of(0, r) for r in order]
        mask = [row_of(2, r) for r in order[:3]]
        q = []
        for k in range(3):
            ion = row_of(1, order[k])
            moved = dense_apply(adj[k], adj[k + 1], adj[k - 1] if k else None, SI)
            q.append([adj[k][j] - DT * mask[k][j] * (moved[j] + ion[j] * adj[k][j]) for j in range(2)])
        near = dense_apply(q[0], q[1], None, SI)
        mis = row_of(3, order[0])
        near = [near[j] + mis[j] for j in range(2)]
        second = dense_apply(q[1], q[2], q[0], SI)[0] + row_of(3, order[1])[0]
        for value, (start, first, count) in zip((second, near[0], q[0][0], mask[0][0], adj[0][0]), near_rows(n_dir, W)):
            out[start : start + count, :] = value[first : first + count]
        packs = [jnp.zeros((8, LANES), F32) for _ in range(n_dir)]
        for t, tile in enumerate(rim_tiles((near[1], q[0][1], mask[0][1], adj[0][1]))):
            k, at = divmod(t, LANES // (H * n_dir))
            turned = pltpu.roll(tile, lax.rem(length_shift + H * n_dir * at, LANES), 1)
            packs[k] = jnp.where(group == at, turned, packs[k])
        for k in range(n_dir):
            out[8 * k : 8 * k + 8, :] = packs[k]
        for k, pair in enumerate((adj[0], mask[0], q[0])):
            own_rows[side, 2 * k] = pair[0]
            own_rows[side, 2 * k + 1] = pair[1]


def spots(m_ref, e_ref, i, rows, coef):
    m, e = plane(m_ref, i, rows), plane(e_ref, i, rows)
    wm = plane(m_ref, i - 1, rows) + plane(m_ref, i + 1, rows)
    we = plane(e_ref, i - 1, rows) + plane(e_ref, i + 1, rows)
    lm, le = beside_lanes(m, e)
    cm, ce = beside_rows(m, 0.0, 0.0), beside_rows(e, 0.0, 0.0)
    double = 2.0 * sum(coef)
    dm = double * m - coef[0] * wm - coef[1] * cm - coef[2] * lm
    de = double * e - coef[0] * we - coef[1] * ce - coef[2] * le
    return m, e, dm, de


def rim_lanes(lane, length, n_len):
    return jnp.logical_or(
        jnp.logical_and(lane < H, length < n_len - 1),
        jnp.logical_and(lane >= LANES - H, length > 0),
    )


def inside(i, wall, W, n_wall):
    w = wall * W + i - H
    return jnp.logical_and(w >= 0, w < n_wall * W)


def lanes_at(x, index):
    return jnp.take_along_axis(x, index, axis=1, mode="promise_in_bounds")


def rows_at(x, index):
    return jnp.take_along_axis(x, index, axis=0, mode="promise_in_bounds")


def halved(low, high):
    lane = lane_of(low.shape)
    even = 2 * lane % LANES
    pairs = [lanes_at(x, even) + lanes_at(x, even + 1) for x in (low, high)]
    return 0.125 * jnp.where(lane < LANES // 2, pairs[0], pairs[1])


def precise(a, b):
    return jnp.dot(a, b, precision=HIGHEST, preferred_element_type=F32)


def assemble(n_len, C, raw, wall_in, strips, corners, xm, xe):
    W = raw[0].shape[0] // C
    N = W + 2 * H
    wall, length = lax.axis_index("wall"), lax.axis_index("len")
    lane = lane_of((C, LANES))
    places = rim_places(n_len, length)
    seen = [jnp.logical_and(lax.rem(lane - off + LANES, LANES) < H, ok) for off, ok in places]

    def rim(packed, base):
        out = jnp.zeros((C, LANES), F32)
        for row, ok, (off, _) in zip(packed, seen, places):
            out = jnp.where(ok, pltpu.roll(row, lax.rem(off - base + LANES, LANES), 1), out)
        return out

    zero = jnp.zeros((C, LANES), F32)
    last = N - H
    for a, own in enumerate(raw):
        packed = [strip[a] for strip in strips]
        for w in range(W):
            set_plane(xm[a], w + H, C, plane(own, w, C))
            set_plane(xe[a], w + H, C, rim(packed, H * w))
        packed = [corner[...] for corner in corners]
        for i in range(H):
            for at in (i, last + i):
                set_plane(xm[a], at, C, zero)
                set_plane(xe[a], at, C, zero)
        count, first = face_planes(a)
        here = jnp.where(wall == 0, last, H - count)
        for p in range(count):
            set_plane(xm[a], here + p, C, wall_in[first + p])
            set_plane(xe[a], here + p, C, rim(packed, H * (first + p)))


def sector(n_len, n_wall, C, electrodes, *refs):
    n_dir = 1 if n_len == 2 else 2
    raw, wall_in, refs = refs[:4], refs[4], refs[5:]
    strips, corners, refs = refs[:n_dir], refs[n_dir : 2 * n_dir], refs[2 * n_dir :]
    owner, qm, bm, be, coarse, surface, patches, qe, pairs = refs[:9]
    xm, xe = refs[9:13], refs[13:17]
    assemble(n_len, C, raw, wall_in, strips, corners, xm, xe)
    N = qm.shape[0] // C
    W = N - 2 * H
    wall, length = lax.axis_index("wall"), lax.axis_index("len")
    rim = rim_lanes(lane_of((C, LANES)), length, n_len)
    zero = jnp.zeros((C, LANES), F32)
    for i in (0, N - 1):
        set_plane(qm, i, C, zero)
        set_plane(qe, i, C, zero)
    for i in (0, 1, N - 2, N - 1):
        set_plane(bm, i, C, zero)
        set_plane(be, i, C, zero)

    def parabolic(i):
        m, e, dm, de = spots(xm[0], xe[0], i, C, SI)
        set_plane(qm, i, C, m - DT * plane(xm[2], i, C) * (dm + plane(xm[1], i, C) * m))
        set_plane(qe, i, C, e - DT * plane(xe[2], i, C) * (de + plane(xe[1], i, C) * e))

    loop(1, N - 1, parabolic, N)

    def elliptic_source(i):
        m, e, dm, de = spots(qm, qe, i, C, SI)
        ok = inside(i, wall, W, n_wall)
        set_plane(bm, i, C, jnp.where(ok, plane(xm[3], i, C) + dm, 0.0))
        set_plane(be, i, C, jnp.where(jnp.logical_and(rim, ok), plane(xe[3], i, C) + de, 0.0))

    loop(2, N - 2, elliptic_source, N)

    coef, k0 = level_coef(0), level_step(0)

    def left(i):
        m, e = plane(bm, i, C), plane(be, i, C)
        wm = plane(bm, i - 1, C) + plane(bm, i + 1, C)
        cm = beside_rows(m, 0.0, 0.0)
        lm = beside_lanes_main(m, e)
        return m, (1.0 - OMEGA) * m + k0 * (coef[0] * wm + coef[1] * cm + coef[2] * lm)

    def pair(q):
        i = 2 * q + H
        m, first = left(i)
        n, second = left(i + 1)
        set_plane(pairs, q, C, first + second)

        @pl.when(jnp.logical_and(q == 0, wall == 0))
        def _():
            surface[...] = k0 * (m + first)

        @pl.when(jnp.logical_and(q == W // 2 - 1, wall == n_wall - 1))
        def _():
            surface[...] = k0 * (n + second)

    loop(0, W // 2, pair, W)

    half = W * C // 8
    z = pairs[pl.ds(0, 2 * half, stride=2), :] + pairs[pl.ds(1, 2 * half, stride=2), :]
    coarse[...] = halved(z[:half], z[half:])

    blk = lax.axis_index("blk")
    me = (blk * n_len + length) * n_wall + wall
    which = lax.broadcasted_iota(jnp.int32, (1, electrodes), 1).astype(F32)
    mine = owner[...] == me
    patches[0:1, :] = jnp.full((1, LANES), jnp.min(jnp.where(mine, which, float(electrodes))))
    patches[1:2, :] = jnp.full((1, LANES), jnp.max(jnp.where(mine, which, -1.0)))
    patches[2:8, :] = jnp.zeros((6, LANES), F32)


def unpacked(ref, n_len, length, N):
    n_dir = 1 if n_len == 2 else 2
    mains = []
    for start, first, count in near_rows(n_dir, N - 2 * H):
        begin = min(start - first, ref.shape[0] - N)
        value = ref[begin : begin + N, :]
        behind = start - first - begin
        mains.append(pltpu.roll(value, N - behind, 0) if behind else value)
    rim = rim_lanes(lane_of((8, LANES)), length, n_len)
    shift = jnp.where(length == 0, 0, H) if n_dir == 1 else H
    rims = []
    for k in range(4):
        parts = []
        for s in range(N // 8):
            pack, at = divmod(k * (N // 8) + s, LANES // (H * n_dir))
            back = lax.rem(2 * LANES - shift - H * n_dir * at, LANES)
            parts.append(jnp.where(rim, pltpu.roll(ref[8 * pack : 8 * pack + 8, :], back, 1), 0.0))
        rims.append(jnp.concatenate(parts, 0))
    second, near, q, mask, adj = mains
    return (adj, rims[3]), (mask, rims[2]), (q, rims[1]), (near, rims[0]), second


def lateral(pair):
    return dense_apply(pair, None, None, SI)


def source_rows(own, other):
    adj_o, mask_o, q_o = own
    adj_n, mask_n, q_n, p_n, second_n = other
    step = DT * SI[1]
    delta_o = [step * mask_o[k] * adj_n[k] for k in range(2)]
    delta_n = [step * mask_n[k] * adj_o[k] for k in range(2)]
    lat_o, lat_n = lateral(delta_o), lateral(delta_n)
    near = [lat_o[k] - SI[1] * (q_n[k] + delta_n[k]) for k in range(2)]
    second = [-SI[1] * delta_o[k] for k in range(2)]
    halo = [p_n[k] + lat_n[k] - SI[1] * (q_o[k] + delta_o[k]) for k in range(2)]
    halo_second = second_n - SI[1] * delta_n[0]
    return near, second, halo, halo_second, delta_o[0]


def correct(electrodes, n_len, n_wall, own_rows, from_next, from_prev, coarse, surface, ids, *rest):
    rows_n, rows_p, message = rest[:3]
    lines, sums = rest[3:]
    _, C, L = ids.shape
    N = own_rows.shape[2]
    W = N - 2 * H
    wall, length = lax.axis_index("wall"), lax.axis_index("len")
    ok_m = inside(lax.broadcasted_iota(jnp.int32, (N, LANES), 0), wall, W, n_wall)
    ok_e = jnp.logical_and(ok_m, rim_lanes(lane_of((N, LANES)), length, n_len))
    coef, k0 = level_coef(0), level_step(0)
    y = surface[...]
    row = lax.broadcasted_iota(jnp.int32, (C, LANES), 0)
    at = pl.ds(jnp.where(wall == 0, H, W + H - 1), 1)
    lows, highs = [], []
    W1, C1 = W // 2, C // 2
    for side, (other, out, order) in enumerate(
        ((from_next, rows_n, (C - 1, C - 2, C - 3)), (from_prev, rows_p, (0, 1, 2)))
    ):
        own = [(own_rows[side, 2 * k], own_rows[side, 2 * k + 1]) for k in range(3)]
        near, second, halo, halo_second, delta = source_rows(own, unpacked(other, n_len, length, N))
        near = [jnp.where(ok_m, near[0], 0.0), jnp.where(ok_e, near[1], 0.0)]
        second = [jnp.where(ok_m, second[0], 0.0), jnp.where(ok_e, second[1], 0.0)]
        out[0] = halo_m = jnp.where(ok_m, halo[0], 0.0)
        out[1] = jnp.where(ok_e, halo[1], 0.0)
        out[2] = jnp.where(ok_m, halo_second, 0.0)
        out[3] = delta
        out[4], out[5] = near
        out[6], out[7] = second

        def turned(pair, beside):
            m, e = pair
            return (1.0 - OMEGA) * m + k0 * (
                coef[0] * beside_dense(m) + coef[2] * beside_lanes_main(m, e) + coef[1] * beside
            )

        first = turned(near, second[0] + halo_m)
        next_one = turned(second, near[0])
        third = k0 * coef[1] * second[0]
        for k, change in enumerate((near[0] + first, second[0] + next_one, third)):
            lines[0] = change
            y = y + jnp.where(row == order[k], k0 * lines[0, at, :], 0.0)
        for change in (first + next_one, third):
            lines[0] = change
            both = lines[0, pl.ds(H, W1, stride=2), :] + lines[0, pl.ds(H + 1, W1, stride=2), :]
            lows.append(both[: W1 // 2])
            highs.append(both[W1 // 2 :])
    add = halved(jnp.concatenate(lows, 0), jnp.concatenate(highs, 0))
    half = W * C // 8
    message[0:half, :] = coarse[...]
    for k, c1 in enumerate((C1 - 1, C1 - 2, 0, 1)):
        spot = pl.ds(c1, W1 // 2, stride=C1)
        message[spot, :] = message[spot, :] + add[k * (W1 // 2) : (k + 1) * (W1 // 2)]
    patch = ids[0]
    message[half : half + C, :] = patch.astype(F32)
    wide = sums.shape[0]
    if wide > electrodes:
        sums[...] = jnp.zeros(sums.shape, F32)

    def one(e):
        sums[pl.ds(e, 1), :] = jnp.sum(jnp.where(patch == e, y, 0.0), axis=0, keepdims=True)

    loop(0, electrodes, one, 32 if electrodes <= 32 else 8)
    totals = lax.dot_general(
        jnp.ones((8, LANES), F32), sums[...], (((1,), (1,)), ((), ())), precision=HIGHEST, preferred_element_type=F32
    )
    message[half + C : half + C + 8, :] = jnp.zeros((8, LANES), F32)
    for t in range(wide // LANES):
        message[half + C + t : half + C + t + 1, :] = totals[0:1, t * LANES : (t + 1) * LANES]


def source_part(n_len, n_wall, C, bm, be, rows_n, rows_p, qm, mask, base_adj, base_pot, fm, fe, tm, te, hp):
    N = bm.shape[0] // C
    W = N - 2 * H
    length, wall = lax.axis_index("len"), lax.axis_index("wall")
    fm[...] = bm[...]
    fe[...] = be[...]
    for rows, near, second in ((rows_n, C - 1, C - 2), (rows_p, 0, 1)):
        for k, at in ((4, near), (6, second)):
            spot = pl.ds(at, N, stride=C)
            fm[spot, :] = fm[spot, :] + rows[k]
            fe[spot, :] = fe[spot, :] + rows[k + 1]
    coef, k0 = level_coef(0), level_step(0)
    rim = rim_lanes(lane_of((C, LANES)), length, n_len)

    def part(i):
        m, e = plane(fm, i, C), plane(fe, i, C)
        wm = plane(fm, i - 1, C) + plane(fm, i + 1, C)
        we = plane(fe, i - 1, C) + plane(fe, i + 1, C)
        lm, le = beside_lanes(m, e)
        at = pl.ds(i, 1)
        cm = beside_rows(m, rows_p[0, at, :], rows_n[0, at, :])
        ce = beside_rows(e, rows_p[1, at, :], rows_n[1, at, :])
        pm = k0 * ((2.0 - OMEGA) * m + k0 * (coef[0] * wm + coef[1] * cm + coef[2] * lm))
        pe = k0 * ((2.0 - OMEGA) * e + k0 * (coef[0] * we + coef[1] * ce + coef[2] * le))
        set_plane(tm, i, C, jnp.where(inside(i, wall, W, n_wall), pm, 0.0))
        set_plane(te, i, C, jnp.where(rim, pe, 0.0))

    loop(H - 1, N - H + 1, part, N)
    for side, (rows, at) in enumerate(((rows_n, C - 1), (rows_p, 0))):
        m = rows[0]
        total = (
            coef[0] * beside_dense(m)
            + coef[1] * (rows[2] + dense(fm, at, N, C))
            + coef[2] * beside_lanes_main(m, rows[1])
        )
        hp[side] = k0 * ((2.0 - OMEGA) * m + k0 * total)
    row = lax.broadcasted_iota(jnp.int32, (C, LANES), 0)

    def finish(w):
        i = w + H
        m, e = plane(tm, i, C), plane(te, i, C)
        at = pl.ds(i, 1)
        wm = plane(tm, i - 1, C) + plane(tm, i + 1, C)
        cm = beside_rows(m, hp[1, at, :], hp[0, at, :])
        lm = beside_lanes_main(m, e)
        lam = plane(qm, i, C)
        lam = lam + jnp.where(row == C - 1, rows_n[3, at, :], 0.0) + jnp.where(row == 0, rows_p[3, at, :], 0.0)
        moved = 2.0 * sum(SI) * m - SI[0] * wm - SI[1] * cm - SI[2] * lm
        set_plane(base_adj, w, C, lam - DT * plane(mask, w, C) * moved)
        set_plane(base_pot, w, C, m)

    loop(0, W, finish, W)


def halves(shape):
    lane = lane_of(shape)
    return lane, lane % (LANES // 2)


def compact(C, W, blocks, out, wall_out, sheet1, coarse2):
    n_blk = blocks.shape[0]
    W1, C1 = W // 2, C // 2
    half, start, middle = W1 // 2, W1 // 2 * C1, LANES // 2
    blk, length, wall = lax.axis_index("blk"), lax.axis_index("len"), lax.axis_index("wall")
    sums = jnp.zeros((8, LANES), F32)
    for d in range(n_blk):
        b = lax.rem(blk - d + n_blk, n_blk)
        for i in range(half):
            sheet1[i, pl.ds(pl.multiple_of(C1 * b, C1), C1), :] = blocks[d, i * C1 : (i + 1) * C1, :]
        out[pl.ds(pl.multiple_of(96 + C * b, C), C), :] = blocks[d, start : start + C, :]
        sums = sums + blocks[d, start + C : start + C + 8, :]
    out[160:168, :] = sums
    NC1 = sheet1.shape[1]
    lane, at = halves((NC1, LANES))
    low = lane < middle
    coef, k1 = level_coef(1), level_step(1)
    ends = pltpu.roll(sheet1[half - 1], middle, 1), pltpu.roll(sheet1[0], middle, 1)
    for q in range(half // 2):
        both = sheet1[2 * q] + sheet1[2 * q + 1]
        prev = sheet1[2 * q - 1] if q else jnp.where(low, 0.0, ends[0])
        after_it = sheet1[2 * q + 2] if 2 * q + 2 < half else jnp.where(low, ends[1], 0.0)
        c = pltpu.roll(both, 1, 0) + pltpu.roll(both, NC1 - 1, 0)
        l = jnp.where(at == 0, 0.0, pltpu.roll(both, 1, 1)) + jnp.where(
            at == middle - 1, 0.0, pltpu.roll(both, LANES - 1, 1)
        )
        left = (1.0 - OMEGA) * both + k1 * (coef[0] * (prev + both + after_it) + coef[1] * c + coef[2] * l)
        coarse2[q] = 0.125 * twins(left, 1)
    coarse2[half // 2] = 0.125 * twins(jnp.where(wall == 0, sheet1[half - 1], sheet1[0]), 1)
    rows2 = NC1 // 2
    lane2, at2 = halves((rows2, LANES))
    pick = lane2 - at2 + 2 * (at2 % (middle // 2))
    for p in range(half // 4):
        pair = [lanes_at(coarse2[2 * p + k, pl.ds(0, rows2, stride=2), :], pick) for k in range(2)]
        out[rows2 * p : rows2 * (p + 1), :] = jnp.where(at2 < middle // 2, pair[0], pair[1])
    beside = jnp.zeros((NC1, LANES), F32)
    base = jnp.where(length == 0, middle - H, 0)
    for i in range(half):
        turned = pltpu.roll(sheet1[i], lax.rem(H * i - base + LANES, LANES), 1)
        beside = jnp.where(at // H == i, turned, beside)
    index = lax.broadcasted_iota(jnp.int32, (8, LANES), 0) ^ 1
    line = beside + jnp.concatenate([rows_at(beside[t : t + 8], index) for t in range(0, NC1, 8)], 0)
    line = 0.125 * (line + pltpu.roll(line, LANES - H, 1))
    m = lane - 96
    spot = jnp.where(m < H, 8 * m, middle + 8 * (m - H)) + jnp.where(length == 0, H - 1, 0)
    line = lanes_at(line, jnp.clip(spot, 0, LANES - 1))
    beside = jnp.where(jnp.logical_and(m >= 0, m < 8), line, beside)
    out[32 : 32 + NC1, :] = beside
    face = coarse2[half // 2, pl.ds(0, rows2, stride=2), :]
    face = lanes_at(face, jnp.where(wall == 0, middle, 0) + 2 * (at2 % (middle // 2)))
    inner = jnp.logical_and(lane2 >= middle // 2, lane2 < middle)
    out[32 : 32 + rows2, :] = jnp.where(inner, face, beside[:rows2])
    inner_surface = jnp.where(low, sheet1[0], pltpu.roll(sheet1[1], middle, 1))
    outer_surface = jnp.where(low, pltpu.roll(sheet1[half - 2], middle, 1), sheet1[half - 1])
    out[64 : 64 + NC1, :] = jnp.where(wall == 0, inner_surface, outer_surface)
    wall_out[0:168, :] = out[...]
    last = jnp.where(low, pltpu.roll(sheet1[half - 1], middle, 1), sheet1[half - 2])
    wall_out[168 : 168 + NC1, :] = jnp.where(wall == 0, last, inner_surface)


def around(x, by):
    rows, lanes = x.shape
    lane = lane_of(x.shape)
    c = pltpu.roll(x, by, 0) + pltpu.roll(x, rows - by, 0)
    l = jnp.where(lane < by, 0.0, pltpu.roll(x, by, 1)) + jnp.where(
        lane >= lanes - by, 0.0, pltpu.roll(x, lanes - by, 1)
    )
    return c, l


def twins(x, by):
    rows, lanes = x.shape
    if lanes == LANES:
        index = lax.broadcasted_iota(jnp.int32, (8, LANES), 0) ^ by
        x = x + jnp.concatenate([rows_at(x[t : t + 8], index) for t in range(0, rows, 8)], 0)
        return x + lanes_at(x, lane_of(x.shape) ^ by)
    row = lax.broadcasted_iota(jnp.int32, x.shape, 0)
    lane = lane_of(x.shape)
    x = x + jnp.where((row & by) == 0, pltpu.roll(x, rows - by, 0), pltpu.roll(x, by, 0))
    return x + jnp.where((lane & by) == 0, pltpu.roll(x, lanes - by, 1), pltpu.roll(x, by, 1))


def solve(sizes, relative, compacted, C, W, *refs):
    n_blk, n_len, n_wall = sizes
    count = n_len * n_wall + compacted
    blocks, refs = refs[:count], refs[count:]
    base_adj, base_pot, mask, patches, adj_prev, potential, patch_grad = refs[:7]
    b1, x1, b2, x2, b3, x3, near, pm, pe, tm, te, adj_out, pot_out, sheet, briefs, sems = refs[7:]
    L = LANES
    W1, C1 = W // 2, C // 2
    planes, NC1, NL1 = b1.shape
    planes -= 2
    blk, length, wall = lax.axis_index("blk"), lax.axis_index("len"), lax.axis_index("wall")
    half = W1 // 2
    middle = LANES // 2
    lane8 = lane_of((C1, LANES))
    often = 40 if NC1 * NL1 <= 4096 else 1

    def blk_of(d):
        return lax.rem(blk - d + n_blk, n_blk) if relative else d

    def length_of(j):
        return (length + j) % n_len if n_len == 2 else j

    def wall_of(v):
        return (wall + v) % n_wall

    zero1 = jnp.zeros((NC1, NL1), F32)
    for ref in (b1, x1, b2, x2, b3, x3):
        ref[0] = zero1
        ref[ref.shape[0] - 1] = zero1

    if not compacted:
        for v in range(n_wall):
            wall_s = wall_of(v)
            mine = blocks[v * n_len : (v + 1) * n_len]

            def unpack(d):
                at = pl.ds(pl.multiple_of(C1 * blk_of(d), C1), C1)
                for t in range(n_len // 2):
                    one, two = mine[2 * t], mine[2 * t + 1]
                    for i in range(half):
                        a, b = one[d, i * C1 : (i + 1) * C1, :], two[d, i * C1 : (i + 1) * C1, :]
                        if n_len == 2:
                            a, b = jnp.where(length == 0, a, b), jnp.where(length == 0, b, a)
                        spot = 1 + wall_s * W1 + i
                        lanes = slice(t * LANES, (t + 1) * LANES)
                        b1[spot, at, lanes] = jnp.where(lane8 < middle, a, pltpu.roll(b, middle, 1))
                        b1[spot + half, at, lanes] = jnp.where(lane8 < middle, pltpu.roll(a, middle, 1), b)

            loop(0, n_blk, unpack, 4)
    if compacted:
        stack, len_brief, wall_brief, both_brief, own_brief = blocks
        lane8 = lane_of((C1, LANES))
        here8 = lane8 // middle == length
        here = lane_of((NC1, LANES)) // middle == length
        face_lane = jnp.where(length == 0, middle, middle - H)
        near8 = jnp.logical_and(lane8 >= face_lane, lane8 < face_lane + H)
        at_face = jnp.logical_and(lane_of((NC1, LANES)) >= face_lane, lane_of((NC1, LANES)) < face_lane + H)
        for d in range(n_blk):
            row = pl.multiple_of(C1 * blk_of(d), C1)
            beside = len_brief[pl.ds(32 + row, C1), :]
            for i in range(half):
                a = stack[d, i * C1 : (i + 1) * C1, :]
                b = pltpu.roll(a, middle, 1)
                for k, value in enumerate((jnp.where(length == 0, a, b), jnp.where(length == 0, b, a))):
                    turn = lax.rem(face_lane - H * i - middle * k + 2 * LANES, LANES)
                    rest = jnp.where(near8, pltpu.roll(beside, turn, 1), 0.0)
                    b1[1 + wall * W1 + i + half * k, pl.ds(row, C1), :] = jnp.where(here8, value, rest)

        def two_planes(tile):
            turned = pltpu.roll(tile, middle, 1)
            return jnp.where(length == 0, tile, turned), jnp.where(length == 0, turned, tile)

        beyond = two_planes(wall_brief[168 : 168 + NC1, :])
        beside = both_brief[32 : 32 + NC1, :]
        for k in range(2):
            off = jnp.where(wall == 0, H * k, middle + H * (half - 1 - k))
            rest = jnp.where(at_face, pltpu.roll(beside, lax.rem(face_lane - off + 2 * LANES, LANES), 1), 0.0)
            b1[jnp.where(wall == 0, 1 + W1 + k, W1 - k)] = jnp.where(here, beyond[k], rest)
        for k in range(2):
            theirs = two_planes(len_brief[64 : 64 + NC1, :])[1 - k]
            spot = jnp.where(wall == 0, 1, planes - 1) + k
            b1[spot] = jnp.where(here, b1[spot], theirs)
            ours = two_planes(wall_brief[64 : 64 + NC1, :])[k]
            theirs = two_planes(both_brief[64 : 64 + NC1, :])[1 - k]
            b1[jnp.where(wall == 0, planes - 1, 1) + k] = jnp.where(here, ours, theirs)
        first_half = length == 0
        for k in range(2):
            ours = jnp.where(wall == k, own_brief[0:64, :], wall_brief[0:64, :])
            theirs = jnp.where(wall == k, len_brief[0:64, :], both_brief[0:64, :])
            briefs[0, k] = jnp.where(first_half, ours, theirs)
            briefs[1, k] = jnp.where(first_half, theirs, ours)
        lane_8 = lane_of((8, LANES))
        quarter = middle // 2
        left_quarter = lane_8 % middle < quarter
        pairs_index = [lane_8 // 2, middle + lane_8 // 2]
        facing = jnp.logical_and(lane_8 >= middle - 2, lane_8 < middle + 2)
        coef1 = [level_step(1) * x for x in level_coef(1)]
        rows2 = NC1 // 2

        def merged(w, start):
            one, two = briefs[0, w, start : start + 8, :], briefs[1, w, start : start + 8, :]
            even = jnp.where(left_quarter, one, pltpu.roll(two, quarter, 1))
            odd = jnp.where(left_quarter, pltpu.roll(one, LANES - quarter, 1), two)
            return even, odd

        for w in range(n_wall):
            for t in range(rows2 // 8):
                lines = [briefs[h, w, pl.ds(32 + 16 * t, 8, stride=2), :] for h in range(2)]
                lines = [lanes_at(x, jnp.minimum(96 + lane_8 // 4, LANES - 1)) for x in lines]
                lines = coef1[2] * jnp.where(lane_8 % 4 < 2, lines[1], lines[0])
                for p in range(half // 4):
                    tiles = merged(w, rows2 * p + 8 * t)
                    for odd in range(2):
                        for high in range(2):
                            k = 2 * p + odd + half // 2 * high
                            value = lanes_at(tiles[odd], pairs_index[high])
                            line = pltpu.roll(lines, middle - 2 - 4 * k, 1)
                            value = value + jnp.where(facing, line, 0.0)
                            if k == (half - 1 if w == 0 else 0):
                                value = value + coef1[0] * lanes_at(merged(1 - w, 32 + 8 * t)[1], pairs_index[0])
                            for r in range(2):
                                b2[1 + w * half + k, pl.ds(16 * t + r, 8, stride=2), :] = value

    def total_of(x, wsum, level, by):
        coef = level_coef(level)
        c, l = around(x, by)
        return level_step(level) * (coef[0] * wsum + coef[1] * c + coef[2] * l)

    def left_pair(ref, i, level):
        both = ref[i] + ref[i + 1]
        return (1.0 - OMEGA) * both + total_of(both, ref[i - 1] + both + ref[i + 2], level, 2 ** (level - 1))

    def sweep(x_ref, b_ref, i, level):
        x = x_ref[i]
        total = total_of(x, x_ref[i - 1] + x_ref[i + 1], level, 2 ** (level - 1))
        return (1.0 - OMEGA) * x + level_step(level) * b_ref[i] + total

    def down1(q):
        b2[1 + q] = 0.125 * twins(left_pair(b1, 2 * q + 1, 1), 1)

    if not compacted:
        loop(0, planes // 2, down1, often)

    def down2(q):
        b3[1 + q] = 0.125 * twins(left_pair(b2, 2 * q + 1, 2), 2)

    loop(0, planes // 4, down2, often)

    deep = planes // 4
    k3 = level_step(3)

    x2[1 + deep] = zero1

    def start3(q):
        b = b3[1 + q]
        x2[1 + q] = k3 * ((2.0 - OMEGA) * b + total_of(b, b3[q] + b3[2 + q], 3, 4))

    loop(0, deep, start3, often)

    def sweep3(q):
        x3[1 + q] = sweep(x2, b3, 1 + q, 3)

    loop(0, deep, sweep3, often)
    k2 = level_step(2)

    def up2(q):
        coarse = x3[1 + q]
        x2[1 + 2 * q] = k2 * b2[1 + 2 * q] + coarse
        x2[2 + 2 * q] = k2 * b2[2 + 2 * q] + coarse

    loop(0, planes // 4, up2, often)

    k1 = level_step(1)

    def up1(q):
        fine = sweep(x2, b2, 1 + q, 2)
        x1[1 + 2 * q] = k1 * b1[1 + 2 * q] + fine
        x1[2 + 2 * q] = k1 * b1[2 + 2 * q] + fine

    if compacted:
        loop(0, half, lambda q: up1(half * wall + q), often)
        up1(half - wall)
        up1((planes // 2 - 1) * (1 - wall))
    else:
        loop(0, planes // 2, up1, often)

    Q = W1 + 2
    sectors = (blk, lax.rem(blk + 1, n_blk), lax.rem(blk + n_blk - 1, n_blk))
    spots3 = [pl.ds(pl.multiple_of(s * C1, C1), C1) for s in sectors]
    row8 = lax.broadcasted_iota(jnp.int32, (C1, NL1), 0)

    def three(ref, i):
        return jnp.concatenate([ref[i, s, :] for s in spots3], 0)

    def finish1(q):
        i = wall * W1 + q
        x = three(x1, i)
        wsum = three(x1, jnp.maximum(i - 1, 0)) + three(x1, jnp.minimum(i + 1, planes + 1))
        value = (1.0 - OMEGA) * x + k1 * three(b1, i) + total_of(x, wsum, 1, 1)
        value = jnp.where(jnp.logical_and(i >= 1, i <= planes), value, 0.0)
        set_plane(near, 2 * q, C1, value[:C1])
        set_plane(near, 2 * q + 1, C1, jnp.where(row8 < 2, value[C1 : 2 * C1], value[2 * C1 :]))

    loop(0, Q, finish1, often)

    first = length * middle
    R = C + 8
    row8 = lax.broadcasted_iota(jnp.int32, (8, LANES), 0)
    tile_lane = lane_of((8, LANES))
    at_e = jnp.where(tile_lane < H, middle + tile_lane // 2, tile_lane // 2 - middle)
    rim8 = rim_lanes(tile_lane, length, n_len)
    if NL1 == LANES:
        index_m, index_e = first + tile_lane // 2, jnp.clip(first + at_e, 0, LANES - 1)

        def spread(tile):
            return lanes_at(tile, index_m), jnp.where(rim8, lanes_at(tile, index_e), 0.0)

    else:
        source = lax.broadcasted_iota(jnp.int32, (NL1, LANES), 0)
        lane = lane_of((NL1, LANES))
        at_all = jnp.where(lane < H, middle + lane // 2, jnp.where(lane >= LANES - H, lane // 2 - middle, 4 * NL1))
        take_m = jnp.where(source == first + lane // 2, 1.0, 0.0).astype(F32)
        take_e = jnp.where(source == first + at_all, 1.0, 0.0).astype(F32)

        def spread(tile):
            return precise(tile, take_m), precise(tile, take_e)

    picks = (row8 // 2, H + row8 // 2)
    ends = jnp.where(row8 < H, 6 + row8 // 2, row8 // 2 - 2)

    def fine_rows(q):
        own = spread(plane(near, 2 * q, C1))
        beside = spread(plane(near, 2 * q + 1, C1))
        for out, a, b in ((pm, own[0], beside[0]), (pe, own[1], beside[1])):
            parts = (jnp.where(row8 < 6, a, b), a, jnp.where(row8 < 2, b, a))
            index = (ends, 2 + row8 // 2, ends)
            for k in range(3):
                out[pl.ds(pl.multiple_of(8 + R * q + 8 * k, 8), 8), :] = rows_at(parts[k], index[k])

    loop(0, Q, fine_rows, often)
    for ref in (pm, pe):
        ref[0:8, :] = jnp.zeros((8, LANES), F32)
        ref[8 + R * Q : 16 + R * Q, :] = jnp.zeros((8, LANES), F32)
    coef, k0 = level_coef(0), level_step(0)
    def fine(ref, t, by=0, count=R):
        return ref[pl.ds(8 + R * t + by, count), :]

    def coarse_terms(q):
        out = []
        sides = beside_lanes(fine(pm, q), fine(pe, q))
        for ref, l in zip((pm, pe), sides):
            x = fine(ref, q)
            c = fine(ref, q, -1) + fine(ref, q, 1)
            out.append((1.0 - OMEGA) * x + k0 * (coef[0] * x + coef[1] * c + coef[2] * l))
        return out

    ks = k0 * coef[0]

    def set_fine(ref, t, value):
        ref[pl.ds(pl.multiple_of(8 + R * t, 8), R), :] = value

    def put_end(t, q, other, ok):
        set_fine(tm, t, jnp.where(ok, coarse_terms(q)[0] + ks * fine(pm, other), 0.0))

    put_end(0, 0, 1, wall > 0)
    put_end(W + 1, Q - 1, Q - 2, wall < n_wall - 1)
    rim = rim_lanes(lane_of((R, LANES)), length, n_len)

    def level0(q):
        gm, ge = coarse_terms(q)
        for t, other in ((2 * q - 1, q - 1), (2 * q, q + 1)):
            set_fine(tm, t, gm + ks * fine(pm, other))
            set_fine(te, t, jnp.where(rim, ge + ks * fine(pe, other), 0.0))

    loop(1, 1 + W1, level0, often)

    def finish0(w):
        t = w + 1
        m, e = fine(tm, t, H, C), fine(te, t, H, C)
        cm = fine(tm, t, H - 1, C) + fine(tm, t, H + 1, C)
        wm = fine(tm, t - 1, H, C) + fine(tm, t + 1, H, C)
        lm = beside_lanes_main(m, e)
        moved = 2.0 * sum(SI) * m - SI[0] * wm - SI[1] * cm - SI[2] * lm
        set_plane(adj_out, w, C, plane(base_adj, w, C) - DT * plane(mask, w, C) * moved)
        set_plane(pot_out, w, C, plane(base_pot, w, C) + m)

    parts = 2
    size = W // parts
    copies = []
    for k in range(parts):
        loop(k * size, (k + 1) * size, finish0, often)
        spot = pl.ds(k * size * C, size * C)
        for n, (src, dst) in enumerate(((adj_out, adj_prev), (pot_out, potential))):
            copies.append(pltpu.make_async_copy(src.at[spot], dst.at[spot], sems.at[n, k]))
            copies[-1].start()

    NC, NL = sheet.shape[1:]

    def whole_fine(x):
        if NL1 == LANES:
            parts = []
            for t in range(0, NC1, 8):
                wide8 = [lanes_at(x[t : t + 8], tile_lane // 2 + k * middle) for k in range(2)]
                for pick in picks[:2]:
                    parts.append(jnp.concatenate([rows_at(v, pick) for v in wide8], 1))
            return jnp.concatenate(parts, 0)
        along_c = lax.broadcasted_iota(jnp.int32, (NC, NC1), 0) // 2
        along_l = lax.broadcasted_iota(jnp.int32, (NL1, NL), 1) // 2
        twice_c = jnp.where(along_c == lax.broadcasted_iota(jnp.int32, (NC, NC1), 1), 1.0, 0.0).astype(F32)
        twice_l = jnp.where(along_l == lax.broadcasted_iota(jnp.int32, (NL1, NL), 0), 1.0, 0.0).astype(F32)
        return precise(precise(twice_c, x), twice_l)

    for s, i in enumerate((1, planes)):
        p = whole_fine(sweep(x1, b1, i, 1))
        c, l = around(p, 1)
        sheet[s] = (1.0 - OMEGA) * p + k0 * (coef[0] * p + coef[1] * c + coef[2] * l)

    owned = [patches[r : r + 1, :] for r in range(2)]
    spot = lax.broadcasted_iota(jnp.int32, (8, LANES), 0) * LANES + lane_of((8, LANES))
    spot = spot.astype(F32)
    start = half * C1
    totals = [jnp.zeros((C, LANES), F32) for _ in owned]
    small = [jnp.zeros((8, LANES), F32) for _ in owned]
    for v in range(n_wall):
        wall_s = wall_of(v)
        for j in range(n_len):
            ref = blocks[v * n_len + j]
            at_l = pl.ds(pl.multiple_of(length_of(j) * L, L), L)
            if compacted and v + j:
                for b in range(n_blk):
                    values = sheet[wall_s, b * C : (b + 1) * C, at_l]
                    ids = ref[96 + b * C : 96 + (b + 1) * C, :]
                    totals = [x + jnp.where(ids == e, values, 0.0) for x, e in zip(totals, owned)]
                small = [x + jnp.where(spot == e, ref[160:168, :], 0.0) for x, e in zip(small, owned)]
                continue

            def add(d, carry):
                big, little = carry
                values = sheet[wall_s, pl.ds(pl.multiple_of(blk_of(d) * C, C), C), at_l]
                ids = ref[d, start : start + C, :]
                parts = ref[d, start + C : start + C + 8, :]
                big = [x + jnp.where(ids == e, values, 0.0) for x, e in zip(big, owned)]
                little = [x + jnp.where(spot == e, parts, 0.0) for x, e in zip(little, owned)]
                return big, little

            totals, small = lax.fori_loop(0, n_blk, add, (totals, small), unroll=min(4, n_blk))
    factor = 1.0 / (2.0 * C * L / 2) ** 0.5
    for r in range(2):
        patch_grad[0, r] = (jnp.sum(totals[r]) + jnp.sum(small[r])) * factor
    for copy in copies:
        copy.wait()


def ring(x, axis, by):
    count = lax.axis_size(axis)
    return lax.ppermute(x, axis, [(i, (i + by) % count) for i in range(count)])


def across(x):
    n_wall = lax.axis_size("wall")
    pairs = [(l * n_wall + w, (1 - l) * n_wall + (w + 1) % n_wall) for l in range(2) for w in range(n_wall)]
    return lax.ppermute(x, ("len", "wall"), pairs)


def call(kernel, ins, outs, scratch, name, work=0, room=48):
    places = {"vmem": pltpu.VMEM, "smem": pltpu.SMEM, "any": pl.ANY, "hbm": pltpu.HBM}

    def specs(kinds):
        return [pl.BlockSpec(memory_space=places[kind]) for kind in kinds]

    cost = pl.CostEstimate(flops=work, bytes_accessed=work, transcendentals=0) if work else None
    return pl.pallas_call(
        kernel,
        out_shape=[jax.ShapeDtypeStruct(shape, F32) for shape, _ in outs],
        in_specs=specs(ins),
        out_specs=specs(kind for _, kind in outs),
        scratch_shapes=[pltpu.VMEM(shape, F32) if isinstance(shape, tuple) else shape for shape in scratch],
        compiler_params=pltpu.CompilerParams(vmem_limit_bytes=int(room * 2**20)),
        cost_estimate=cost,
        name=name,
    )


def body(adj_next, ion_slope, misfit, tissue_mask, patch_ids, owner_map):
    W, C, L = adj_next.shape
    n_blk, n_len, n_wall = lax.axis_size("blk"), lax.axis_size("len"), lax.axis_size("wall")
    electrodes = owner_map.shape[0]
    assert L == LANES and H * W == LANES and n_wall == 2 and electrodes == 2 * n_blk * n_len * n_wall
    N = W + 2 * H
    n_dir = 1 if n_len == 2 else 2
    cells = W * C
    vmem = "vmem"
    field, own = (N * C, L), (cells, L)
    raw = [x.reshape(cells, L) for x in (adj_next, ion_slope, tissue_mask, misfit)]

    *fields, wall_out = (faces := call(
        functools.partial(pack_faces, n_len),
        ["hbm"] * 4,
        [(own, vmem)] * 4
        + [((sum(FACES), C, L), vmem)]
        + [((4, C, L), vmem)] * n_dir
        + [((C, L), vmem)] * n_dir,
        [pltpu.VMEM(own, jnp.int32), pltpu.SemaphoreType.DMA((4, 4))],
        "faces",
        room=52.75,
    )(*raw))[:5]
    strip_out, corner_out = faces[5 : 5 + n_dir], faces[5 + n_dir :]
    wall_in = ring(wall_out, "wall", 1)
    if n_dir == 1:
        strips = [ring(strip_out[0], "len", 1)]
        corners = [across(corner_out[0])]
    else:
        strips = [ring(strip_out[1], "len", -1), ring(strip_out[0], "len", 1)]
        corners = [ring(ring(corner_out[1], "wall", 1), "len", -1), ring(ring(corner_out[0], "wall", 1), "len", 1)]

    near = (sum(near_rows(n_dir, W)[-1][::2]), L)
    halos = [wall_in, *strips, *corners]
    to_next, to_prev, own_rows = call(
        functools.partial(boundary, n_len, C),
        [vmem] * (5 + 2 * n_dir),
        [(near, vmem)] * 2 + [((2, 6, N, L), vmem)],
        [(48, N, L)],
        "boundary",
    )(*fields, *halos)
    from_next = ring(to_prev, "blk", -1)
    from_prev = ring(to_next, "blk", 1)
    qm, bm, be, coarse, surface, patches = call(
        functools.partial(sector, n_len, n_wall, C, electrodes),
        [vmem] * (6 + 2 * n_dir),
        [(field, vmem)] * 3 + [((cells // 8, L), vmem), ((C, L), vmem), ((8, L), vmem)],
        [field, (cells // 2, L)] + [field] * 8,
        "sector",
        work=16 * 10**6,
    )(*fields, *halos, owner_map.reshape(1, electrodes))

    rows = (8, N, L)
    wide = LANES * ((electrodes + LANES - 1) // LANES)
    message = (cells // 8 + C + 8, L)
    rows_n, rows_p, mine = call(
        functools.partial(correct, electrodes, n_len, n_wall),
        [vmem] * 6,
        [(rows, vmem), (rows, vmem), (message, vmem)],
        [(1, N, L), (wide, L)],
        "correct",
    )(own_rows, from_next, from_prev, coarse, surface, patch_ids)

    relative = n_blk <= 4
    moved = [ring(mine, "blk", d) for d in range(1, n_blk)] if relative else [lax.all_gather(mine, "blk")]
    base_adj, base_pot = call(
        functools.partial(source_part, n_len, n_wall, C),
        [vmem] * 6,
        [(own, vmem), (own, vmem)],
        [field] * 4 + [(2, N, L)],
        "source_part",
        work=12 * 10**6,
    )(bm, be, rows_n, rows_p, qm, fields[2])
    moved, base_adj = lax.optimization_barrier((moved, base_adj))
    sector_blocks = jnp.stack([mine] + moved) if relative else moved[0]
    compacted = (n_blk, n_len, C, W) == (4, 2, 16, 32)
    if compacted:
        brief, across_wall = call(
            functools.partial(compact, C, W),
            [vmem],
            [((168, L), vmem), ((200, L), vmem)],
            [(W // 4, n_blk * C // 2, L), (W // 8 + 1, n_blk * C // 2, L)],
            "compact",
        )(sector_blocks)
        len_brief = ring(brief, "len", 1)
        blocks = [sector_blocks, len_brief, ring(across_wall, "wall", 1), ring(len_brief, "wall", 1), brief]
    elif n_len == 2:
        here = [sector_blocks, ring(sector_blocks, "len", 1)]
    else:
        gathered = lax.all_gather(sector_blocks, "len")
        here = [gathered[j] for j in range(n_len)]
    if not compacted:
        blocks = here + [ring(x, "wall", 1) for x in here]

    NC1, NL1 = n_blk * C // 2, n_len * L // 2
    planes = n_wall * W // 2
    grids = [(planes // k + 2, NC1, NL1) for k in (1, 1, 2, 2, 4, 4)]
    Q = W // 2 + 2
    tall = (Q * (C + 8) + 16, L)
    taller = ((W + 2) * (C + 8) + 16, L)
    scratch = grids + [(Q * C, NL1), tall, tall, taller, taller, own, own]
    scratch += [(2, n_blk * C, n_len * L), (2, 2, 64, L), pltpu.SemaphoreType.DMA((2, 2))]
    adj_prev, potential, patch_grad = call(
        functools.partial(solve, (n_blk, n_len, n_wall), relative, compacted, C, W),
        [vmem] * (len(blocks) + 4),
        [(own, "any"), (own, "any"), ((1, 2), "smem")],
        scratch,
        "solve",
        room=48 if NC1 * NL1 <= 4096 else 58,
    )(*blocks, base_adj, base_pot, fields[2], patches)
    return adj_prev.reshape(W, C, L), potential.reshape(W, C, L), patch_grad


def solution(mesh):
    field = P(("groups", "wall"), "blk", "len")
    return jax.shard_map(
        body,
        mesh=mesh,
        in_specs=(field, field, field, field, field, P("groups")),
        out_specs=(field, field, P(("groups", "blk", "len", "wall"), None)),
        check_vma=False,
    )
```

```python
import functools

import jax
import jax.numpy as jnp
from jax import lax
from jax.experimental import pallas as pl
from jax.experimental.pallas import tpu as pltpu
from jax.sharding import PartitionSpec as P

SI = (0.6, 1.0, 3.0)
SE = (0.8, 1.2, 2.0)
SHIFT = 0.002
OMEGA = 0.8
DT = 0.1
H = 4
LANES = 128
HIGHEST = lax.Precision.HIGHEST
F32 = jnp.float32


def level_coef(level):
    return tuple((SI[i] + SE[i]) / 4.0**level for i in range(3))


def level_diag(level):
    return SHIFT + 2.0 * sum(level_coef(level))


def level_step(level):
    return OMEGA / level_diag(level)


def lane_of(shape):
    return lax.broadcasted_iota(jnp.int32, shape, len(shape) - 1)


def before(m, e):
    first = lane_of(m.shape) == 0
    rm, re = pltpu.roll(m, 1, 1), pltpu.roll(e, 1, 1)
    return jnp.where(first, re, rm), jnp.where(first, rm, re)


def after(m, e):
    last = lane_of(m.shape) == LANES - 1
    rm, re = pltpu.roll(m, LANES - 1, 1), pltpu.roll(e, LANES - 1, 1)
    return jnp.where(last, re, rm), jnp.where(last, rm, re)


def beside_lanes(m, e):
    bm, be = before(m, e)
    am, ae = after(m, e)
    return bm + am, be + ae


def beside_lanes_main(m, e):
    lane = lane_of(m.shape)
    ends = lanes_at(e, LANES - 1 - lane)
    left = jnp.where(lane == 0, ends, pltpu.roll(m, 1, 1))
    right = jnp.where(lane == LANES - 1, ends, pltpu.roll(m, LANES - 1, 1))
    return left + right


def beside_rows(x, row_before, row_after):
    rows = x.shape[0]
    row = lax.broadcasted_iota(jnp.int32, x.shape, 0)
    low = jnp.where(row == 0, row_before, pltpu.roll(x, 1, 0))
    high = jnp.where(row == rows - 1, row_after, pltpu.roll(x, rows - 1, 0))
    return low + high


def beside_dense(x):
    return pltpu.roll(x, 1, 0) + pltpu.roll(x, x.shape[0] - 1, 0)


def plane(ref, i, rows):
    return ref[pl.ds(pl.multiple_of(i * rows, rows), rows), :]


def set_plane(ref, i, rows, value):
    ref[pl.ds(pl.multiple_of(i * rows, rows), rows), :] = value


def loop(low, high, step, unroll):
    def wrapped(i, carry):
        step(i)
        return carry

    if unroll >= high - low:
        for i in range(low, high):
            step(i)
        return
    lax.fori_loop(low, high, wrapped, 0, unroll=unroll)


FACES = (H, H - 1, H - 1, H - 2)


def face_planes(array):
    return FACES[array], sum(FACES[:array])


def pack_faces(n_len, adj, ion, mask, mis, *rest):
    n_dir = 1 if n_len == 2 else 2
    fields, wall_out, rest = rest[:4], rest[4], rest[5:]
    strips, corners = rest[:n_dir], rest[n_dir : 2 * n_dir]
    whole_mask, sems = rest[2 * n_dir :]
    cells = adj.shape[0]
    C = wall_out.shape[1]
    W = cells // C
    wall, length = lax.axis_index("wall"), lax.axis_index("len")
    targets = (fields[0], fields[1], whole_mask, fields[3])
    copies = []
    for a, (src, dst) in enumerate(zip((adj, ion, mask, mis), targets)):
        part = cells // 4
        for k in range(4):
            spot = pl.ds(k * part, part)
            copies.append(pltpu.make_async_copy(src.at[spot], dst.at[spot], sems.at[a, k]))
            copies[-1].start()

    base = jnp.where(wall == 0, W - H, 0)
    group = lane_of((C, LANES)) // H
    turns = [jnp.where(length == 0, H, 0)] if n_dir == 1 else [H, 0]
    corner = [jnp.zeros((C, LANES), F32) for _ in range(n_dir)]
    for a in (0, 1, 3, 2):
        for k in range(4):
            copies[4 * a + k].wait()
        if a == 2:
            fields[2][...] = whole_mask[...].astype(F32)
        ref = fields[a]
        strip = [jnp.zeros((C, LANES), F32) for _ in range(n_dir)]
        for w in range(W):
            value = ref[w * C : (w + 1) * C, :]
            for d in range(n_dir):
                turned = pltpu.roll(value, lax.rem(H * w + turns[d], LANES), 1)
                strip[d] = jnp.where(group == w, turned, strip[d])
        for d in range(n_dir):
            strips[d][a] = strip[d]
        count, first = face_planes(a)
        for p in range(count):
            face = plane(ref, base + jnp.where(wall == 0, H - count, 0) + p, C)
            wall_out[first + p] = face
            slot = first + p
            for d in range(n_dir):
                turned = pltpu.roll(face, lax.rem(H * slot + turns[d], LANES), 1)
                corner[d] = jnp.where(group == slot, turned, corner[d])
    for d in range(n_dir):
        corners[d][...] = corner[d]


def dense(ref, row, N, C):
    return ref[pl.ds(row, N, stride=C), :]


def dense_pair(m, e, row, N, C):
    return dense(m, row, N, C), dense(e, row, N, C)


def dense_apply(pair, inner, outer, coef):
    m, e = pair
    lm, le = beside_lanes(m, e)
    double = 2.0 * sum(coef)
    out = [double * m - coef[0] * beside_dense(m) - coef[2] * lm, double * e - coef[0] * beside_dense(e) - coef[2] * le]
    for row in (inner, outer):
        if row is not None:
            out = [out[k] - coef[1] * row[k] for k in range(2)]
    return out


def near_rows(n_dir, W):
    start, places = 8 * n_dir, []
    for reach in (0, 1, 2, 2, 3):
        places.append((start, H - reach, W + 2 * reach))
        start += W + 2 * reach
    assert start % 8 == 0
    return places


def rim_tiles(values):
    return [value[s : s + 8] for value in values for s in range(0, value.shape[0], 8)]


def rim_places(n_len, length):
    if n_len == 2:
        return [(jnp.where(length == 0, 0, LANES - H), True)]
    return [(0, length < n_len - 1), (LANES - H, length > 0)]


def boundary(n_len, C, *refs):
    n_dir = 1 if n_len == 2 else 2
    raw, wall_in, refs = refs[:4], refs[4], refs[5:]
    strips, corners, refs = refs[:n_dir], refs[n_dir : 2 * n_dir], refs[2 * n_dir :]
    first_out, second_out, own_rows, build, to_next, to_prev = refs
    W = raw[0].shape[0] // C
    N = W + 2 * H
    wall, length = lax.axis_index("wall"), lax.axis_index("len")
    places = rim_places(n_len, length)

    def strip_rows(packed, first, count):
        lane, k = lane_of((count, LANES)), lax.broadcasted_iota(jnp.int32, (count, LANES), 0)
        out = jnp.zeros((count, LANES), F32)
        for row, (off, ok) in zip(packed, places):
            j = lax.rem(lane - off + LANES, LANES)
            index = jnp.clip(H * (first + k) + j, 0, LANES - 1)
            taken = lanes_at(jnp.broadcast_to(row, (count, LANES)), index)
            out = jnp.where(jnp.logical_and(j < H, ok), taken, out)
        return out

    slots = iter(range(build.shape[0]))

    def assembled(own, halo, count):
        ref = build.at[next(slots)]
        ref[0:8, :] = jnp.zeros((8, LANES), F32)
        ref[N - 8 : N, :] = jnp.zeros((8, LANES), F32)
        ref[H : H + W, :] = own
        ref[H - count : H, :] = jnp.where(wall == 0, 0.0, halo)
        ref[H + W : H + W + count, :] = jnp.where(wall == 0, halo, 0.0)
        return ref[...]

    def row_of(a, r):
        count, first = face_planes(a)
        halo = jnp.concatenate([wall_in[first + p, r : r + 1, :] for p in range(count)], 0)
        m = assembled(raw[a][pl.ds(r, W, stride=C), :], halo, count)
        own = strip_rows([strip[a, r : r + 1, :] for strip in strips], 0, W)
        halo = strip_rows([corner[r : r + 1, :] for corner in corners], first, 8)[:count]
        return m, assembled(own, halo, count)

    length_shift = jnp.where(length == 0, 0, H) if n_dir == 1 else H
    group = lane_of((8, LANES)) // (H * n_dir)
    for side, (out, order) in enumerate(((to_next, (C - 1, C - 2, C - 3, C - 4)), (to_prev, (0, 1, 2, 3)))):
        adj = [row_of(0, r) for r in order]
        mask = [row_of(2, r) for r in order[:3]]
        q = []
        for k in range(3):
            ion = row_of(1, order[k])
            moved = dense_apply(adj[k], adj[k + 1], adj[k - 1] if k else None, SI)
            q.append([adj[k][j] - DT * mask[k][j] * (moved[j] + ion[j] * adj[k][j]) for j in range(2)])
        near = dense_apply(q[0], q[1], None, SI)
        mis = row_of(3, order[0])
        near = [near[j] + mis[j] for j in range(2)]
        second = dense_apply(q[1], q[2], q[0], SI)[0] + row_of(3, order[1])[0]
        for value, (start, first, count) in zip((second, near[0], q[0][0], mask[0][0], adj[0][0]), near_rows(n_dir, W)):
            out[start : start + count, :] = value[first : first + count]
        packs = [jnp.zeros((8, LANES), F32) for _ in range(n_dir)]
        for t, tile in enumerate(rim_tiles((near[1], q[0][1], mask[0][1], adj[0][1]))):
            k, at = divmod(t, LANES // (H * n_dir))
            turned = pltpu.roll(tile, lax.rem(length_shift + H * n_dir * at, LANES), 1)
            packs[k] = jnp.where(group == at, turned, packs[k])
        for k in range(n_dir):
            out[8 * k : 8 * k + 8, :] = packs[k]
        for k, pair in enumerate((adj[0], mask[0], q[0])):
            own_rows[side, 2 * k] = pair[0]
            own_rows[side, 2 * k + 1] = pair[1]
    even = lax.rem(lax.axis_index("blk"), 2) == 0
    first_out[...] = jnp.where(even, to_prev[...], to_next[...])
    second_out[...] = jnp.where(even, to_next[...], to_prev[...])


def spots(m_ref, e_ref, i, rows, coef):
    m, e = plane(m_ref, i, rows), plane(e_ref, i, rows)
    wm = plane(m_ref, i - 1, rows) + plane(m_ref, i + 1, rows)
    we = plane(e_ref, i - 1, rows) + plane(e_ref, i + 1, rows)
    lm, le = beside_lanes(m, e)
    cm, ce = beside_rows(m, 0.0, 0.0), beside_rows(e, 0.0, 0.0)
    double = 2.0 * sum(coef)
    dm = double * m - coef[0] * wm - coef[1] * cm - coef[2] * lm
    de = double * e - coef[0] * we - coef[1] * ce - coef[2] * le
    return m, e, dm, de


def rim_lanes(lane, length, n_len):
    return jnp.logical_or(
        jnp.logical_and(lane < H, length < n_len - 1),
        jnp.logical_and(lane >= LANES - H, length > 0),
    )


def inside(i, wall, W, n_wall):
    w = wall * W + i - H
    return jnp.logical_and(w >= 0, w < n_wall * W)


def lanes_at(x, index):
    return jnp.take_along_axis(x, index, axis=1, mode="promise_in_bounds")


def rows_at(x, index):
    return jnp.take_along_axis(x, index, axis=0, mode="promise_in_bounds")


def halved(low, high):
    lane = lane_of(low.shape)
    even = 2 * lane % LANES
    pairs = [lanes_at(x, even) + lanes_at(x, even + 1) for x in (low, high)]
    return 0.125 * jnp.where(lane < LANES // 2, pairs[0], pairs[1])


def precise(a, b):
    return jnp.dot(a, b, precision=HIGHEST, preferred_element_type=F32)


def assemble(n_len, C, raw, wall_in, strips, corners, xm, xe):
    W = raw[0].shape[0] // C
    N = W + 2 * H
    wall, length = lax.axis_index("wall"), lax.axis_index("len")
    lane = lane_of((C, LANES))
    places = rim_places(n_len, length)
    seen = [jnp.logical_and(lax.rem(lane - off + LANES, LANES) < H, ok) for off, ok in places]

    def rim(packed, base):
        out = jnp.zeros((C, LANES), F32)
        for row, ok, (off, _) in zip(packed, seen, places):
            out = jnp.where(ok, pltpu.roll(row, lax.rem(off - base + LANES, LANES), 1), out)
        return out

    zero = jnp.zeros((C, LANES), F32)
    last = N - H
    for a, own in enumerate(raw):
        packed = [strip[a] for strip in strips]
        for w in range(W):
            set_plane(xm[a], w + H, C, plane(own, w, C))
            set_plane(xe[a], w + H, C, rim(packed, H * w))
        packed = [corner[...] for corner in corners]
        for i in range(H):
            for at in (i, last + i):
                set_plane(xm[a], at, C, zero)
                set_plane(xe[a], at, C, zero)
        count, first = face_planes(a)
        here = jnp.where(wall == 0, last, H - count)
        for p in range(count):
            set_plane(xm[a], here + p, C, wall_in[first + p])
            set_plane(xe[a], here + p, C, rim(packed, H * (first + p)))


def sector(n_len, n_wall, C, electrodes, *refs):
    n_dir = 1 if n_len == 2 else 2
    raw, wall_in, refs = refs[:4], refs[4], refs[5:]
    strips, corners, refs = refs[:n_dir], refs[n_dir : 2 * n_dir], refs[2 * n_dir :]
    owner, qm, bm, be, coarse, surface, patches, qe, pairs = refs[:9]
    xm, xe = refs[9:13], refs[13:17]
    assemble(n_len, C, raw, wall_in, strips, corners, xm, xe)
    N = qm.shape[0] // C
    W = N - 2 * H
    wall, length = lax.axis_index("wall"), lax.axis_index("len")
    rim = rim_lanes(lane_of((C, LANES)), length, n_len)
    zero = jnp.zeros((C, LANES), F32)
    for i in (0, N - 1):
        set_plane(qm, i, C, zero)
        set_plane(qe, i, C, zero)
    for i in (0, 1, N - 2, N - 1):
        set_plane(bm, i, C, zero)
        set_plane(be, i, C, zero)

    def parabolic(i):
        m, e, dm, de = spots(xm[0], xe[0], i, C, SI)
        set_plane(qm, i, C, m - DT * plane(xm[2], i, C) * (dm + plane(xm[1], i, C) * m))
        set_plane(qe, i, C, e - DT * plane(xe[2], i, C) * (de + plane(xe[1], i, C) * e))

    loop(1, N - 1, parabolic, N)

    def elliptic_source(i):
        m, e, dm, de = spots(qm, qe, i, C, SI)
        ok = inside(i, wall, W, n_wall)
        set_plane(bm, i, C, jnp.where(ok, plane(xm[3], i, C) + dm, 0.0))
        set_plane(be, i, C, jnp.where(jnp.logical_and(rim, ok), plane(xe[3], i, C) + de, 0.0))

    loop(2, N - 2, elliptic_source, N)

    coef, k0 = level_coef(0), level_step(0)

    def left(i):
        m, e = plane(bm, i, C), plane(be, i, C)
        wm = plane(bm, i - 1, C) + plane(bm, i + 1, C)
        cm = beside_rows(m, 0.0, 0.0)
        lm = beside_lanes_main(m, e)
        return m, (1.0 - OMEGA) * m + k0 * (coef[0] * wm + coef[1] * cm + coef[2] * lm)

    def pair(q):
        i = 2 * q + H
        m, first = left(i)
        n, second = left(i + 1)
        set_plane(pairs, q, C, first + second)

        @pl.when(jnp.logical_and(q == 0, wall == 0))
        def _():
            surface[...] = k0 * (m + first)

        @pl.when(jnp.logical_and(q == W // 2 - 1, wall == n_wall - 1))
        def _():
            surface[...] = k0 * (n + second)

    loop(0, W // 2, pair, W)

    half = W * C // 8
    z = pairs[pl.ds(0, 2 * half, stride=2), :] + pairs[pl.ds(1, 2 * half, stride=2), :]
    coarse[...] = halved(z[:half], z[half:])

    blk = lax.axis_index("blk")
    me = (blk * n_len + length) * n_wall + wall
    which = lax.broadcasted_iota(jnp.int32, (1, electrodes), 1).astype(F32)
    mine = owner[...] == me
    patches[0:1, :] = jnp.full((1, LANES), jnp.min(jnp.where(mine, which, float(electrodes))))
    patches[1:2, :] = jnp.full((1, LANES), jnp.max(jnp.where(mine, which, -1.0)))
    patches[2:8, :] = jnp.zeros((6, LANES), F32)


def unpacked(ref, n_len, length, N):
    n_dir = 1 if n_len == 2 else 2
    mains = []
    for start, first, count in near_rows(n_dir, N - 2 * H):
        begin = min(start - first, ref.shape[0] - N)
        value = ref[begin : begin + N, :]
        behind = start - first - begin
        mains.append(pltpu.roll(value, N - behind, 0) if behind else value)
    rim = rim_lanes(lane_of((8, LANES)), length, n_len)
    shift = jnp.where(length == 0, 0, H) if n_dir == 1 else H
    rims = []
    for k in range(4):
        parts = []
        for s in range(N // 8):
            pack, at = divmod(k * (N // 8) + s, LANES // (H * n_dir))
            back = lax.rem(2 * LANES - shift - H * n_dir * at, LANES)
            parts.append(jnp.where(rim, pltpu.roll(ref[8 * pack : 8 * pack + 8, :], back, 1), 0.0))
        rims.append(jnp.concatenate(parts, 0))
    second, near, q, mask, adj = mains
    return (adj, rims[3]), (mask, rims[2]), (q, rims[1]), (near, rims[0]), second


def lateral(pair):
    return dense_apply(pair, None, None, SI)


def source_rows(own, other):
    adj_o, mask_o, q_o = own
    adj_n, mask_n, q_n, p_n, second_n = other
    step = DT * SI[1]
    delta_o = [step * mask_o[k] * adj_n[k] for k in range(2)]
    delta_n = [step * mask_n[k] * adj_o[k] for k in range(2)]
    lat_o, lat_n = lateral(delta_o), lateral(delta_n)
    near = [lat_o[k] - SI[1] * (q_n[k] + delta_n[k]) for k in range(2)]
    second = [-SI[1] * delta_o[k] for k in range(2)]
    halo = [p_n[k] + lat_n[k] - SI[1] * (q_o[k] + delta_o[k]) for k in range(2)]
    halo_second = second_n - SI[1] * delta_n[0]
    return near, second, halo, halo_second, delta_o[0]


def correct(electrodes, n_len, n_wall, own_rows, first_in, second_in, coarse, surface, ids, *rest):
    rows_n, rows_p, message = rest[:3]
    lines, sums, from_next, from_prev = rest[3:]
    even = lax.rem(lax.axis_index("blk"), 2) == 0
    from_next[...] = jnp.where(even, second_in[...], first_in[...])
    from_prev[...] = jnp.where(even, first_in[...], second_in[...])
    _, C, L = ids.shape
    N = own_rows.shape[2]
    W = N - 2 * H
    wall, length = lax.axis_index("wall"), lax.axis_index("len")
    ok_m = inside(lax.broadcasted_iota(jnp.int32, (N, LANES), 0), wall, W, n_wall)
    ok_e = jnp.logical_and(ok_m, rim_lanes(lane_of((N, LANES)), length, n_len))
    coef, k0 = level_coef(0), level_step(0)
    y = surface[...]
    row = lax.broadcasted_iota(jnp.int32, (C, LANES), 0)
    at = pl.ds(jnp.where(wall == 0, H, W + H - 1), 1)
    lows, highs = [], []
    W1, C1 = W // 2, C // 2
    for side, (other, out, order) in enumerate(
        ((from_next, rows_n, (C - 1, C - 2, C - 3)), (from_prev, rows_p, (0, 1, 2)))
    ):
        own = [(own_rows[side, 2 * k], own_rows[side, 2 * k + 1]) for k in range(3)]
        near, second, halo, halo_second, delta = source_rows(own, unpacked(other, n_len, length, N))
        near = [jnp.where(ok_m, near[0], 0.0), jnp.where(ok_e, near[1], 0.0)]
        second = [jnp.where(ok_m, second[0], 0.0), jnp.where(ok_e, second[1], 0.0)]
        out[0] = halo_m = jnp.where(ok_m, halo[0], 0.0)
        out[1] = jnp.where(ok_e, halo[1], 0.0)
        out[2] = jnp.where(ok_m, halo_second, 0.0)
        out[3] = delta
        out[4], out[5] = near
        out[6], out[7] = second

        def turned(pair, beside):
            m, e = pair
            return (1.0 - OMEGA) * m + k0 * (
                coef[0] * beside_dense(m) + coef[2] * beside_lanes_main(m, e) + coef[1] * beside
            )

        first = turned(near, second[0] + halo_m)
        next_one = turned(second, near[0])
        third = k0 * coef[1] * second[0]
        for k, change in enumerate((near[0] + first, second[0] + next_one, third)):
            lines[0] = change
            y = y + jnp.where(row == order[k], k0 * lines[0, at, :], 0.0)
        for change in (first + next_one, third):
            lines[0] = change
            both = lines[0, pl.ds(H, W1, stride=2), :] + lines[0, pl.ds(H + 1, W1, stride=2), :]
            lows.append(both[: W1 // 2])
            highs.append(both[W1 // 2 :])
    add = halved(jnp.concatenate(lows, 0), jnp.concatenate(highs, 0))
    half = W * C // 8
    message[0:half, :] = coarse[...]
    for k, c1 in enumerate((C1 - 1, C1 - 2, 0, 1)):
        spot = pl.ds(c1, W1 // 2, stride=C1)
        message[spot, :] = message[spot, :] + add[k * (W1 // 2) : (k + 1) * (W1 // 2)]
    patch = ids[0]
    message[half : half + C, :] = patch.astype(F32)
    wide = sums.shape[0]
    if wide > electrodes:
        sums[...] = jnp.zeros(sums.shape, F32)

    def one(e):
        sums[pl.ds(e, 1), :] = jnp.sum(jnp.where(patch == e, y, 0.0), axis=0, keepdims=True)

    loop(0, electrodes, one, 32 if electrodes <= 32 else 8)
    totals = lax.dot_general(
        jnp.ones((8, LANES), F32), sums[...], (((1,), (1,)), ((), ())), precision=HIGHEST, preferred_element_type=F32
    )
    message[half + C : half + C + 8, :] = jnp.zeros((8, LANES), F32)
    for t in range(wide // LANES):
        message[half + C + t : half + C + t + 1, :] = totals[0:1, t * LANES : (t + 1) * LANES]


def source_part(n_len, n_wall, C, bm, be, rows_n, rows_p, qm, mask, base_adj, base_pot, fm, fe, tm, te, hp):
    N = bm.shape[0] // C
    W = N - 2 * H
    length, wall = lax.axis_index("len"), lax.axis_index("wall")
    fm[...] = bm[...]
    fe[...] = be[...]
    for rows, near, second in ((rows_n, C - 1, C - 2), (rows_p, 0, 1)):
        for k, at in ((4, near), (6, second)):
            spot = pl.ds(at, N, stride=C)
            fm[spot, :] = fm[spot, :] + rows[k]
            fe[spot, :] = fe[spot, :] + rows[k + 1]
    coef, k0 = level_coef(0), level_step(0)
    rim = rim_lanes(lane_of((C, LANES)), length, n_len)

    def part(i):
        m, e = plane(fm, i, C), plane(fe, i, C)
        wm = plane(fm, i - 1, C) + plane(fm, i + 1, C)
        we = plane(fe, i - 1, C) + plane(fe, i + 1, C)
        lm, le = beside_lanes(m, e)
        at = pl.ds(i, 1)
        cm = beside_rows(m, rows_p[0, at, :], rows_n[0, at, :])
        ce = beside_rows(e, rows_p[1, at, :], rows_n[1, at, :])
        pm = k0 * ((2.0 - OMEGA) * m + k0 * (coef[0] * wm + coef[1] * cm + coef[2] * lm))
        pe = k0 * ((2.0 - OMEGA) * e + k0 * (coef[0] * we + coef[1] * ce + coef[2] * le))
        set_plane(tm, i, C, jnp.where(inside(i, wall, W, n_wall), pm, 0.0))
        set_plane(te, i, C, jnp.where(rim, pe, 0.0))

    loop(H - 1, N - H + 1, part, N)
    for side, (rows, at) in enumerate(((rows_n, C - 1), (rows_p, 0))):
        m = rows[0]
        total = (
            coef[0] * beside_dense(m)
            + coef[1] * (rows[2] + dense(fm, at, N, C))
            + coef[2] * beside_lanes_main(m, rows[1])
        )
        hp[side] = k0 * ((2.0 - OMEGA) * m + k0 * total)
    row = lax.broadcasted_iota(jnp.int32, (C, LANES), 0)

    def finish(w):
        i = w + H
        m, e = plane(tm, i, C), plane(te, i, C)
        at = pl.ds(i, 1)
        wm = plane(tm, i - 1, C) + plane(tm, i + 1, C)
        cm = beside_rows(m, hp[1, at, :], hp[0, at, :])
        lm = beside_lanes_main(m, e)
        lam = plane(qm, i, C)
        lam = lam + jnp.where(row == C - 1, rows_n[3, at, :], 0.0) + jnp.where(row == 0, rows_p[3, at, :], 0.0)
        moved = 2.0 * sum(SI) * m - SI[0] * wm - SI[1] * cm - SI[2] * lm
        set_plane(base_adj, w, C, lam - DT * plane(mask, w, C) * moved)
        set_plane(base_pot, w, C, m)

    loop(0, W, finish, W)


def halves(shape):
    lane = lane_of(shape)
    return lane, lane % (LANES // 2)


def compact(C, W, blocks, out, wall_out, sheet1, coarse2):
    n_blk = blocks.shape[0]
    W1, C1 = W // 2, C // 2
    half, start, middle = W1 // 2, W1 // 2 * C1, LANES // 2
    blk, length, wall = lax.axis_index("blk"), lax.axis_index("len"), lax.axis_index("wall")
    sums = jnp.zeros((8, LANES), F32)
    for d in range(n_blk):
        b = blk ^ d
        for i in range(half):
            sheet1[i, pl.ds(pl.multiple_of(C1 * b, C1), C1), :] = blocks[d, i * C1 : (i + 1) * C1, :]
        out[pl.ds(pl.multiple_of(96 + C * b, C), C), :] = blocks[d, start : start + C, :]
        sums = sums + blocks[d, start + C : start + C + 8, :]
    out[160:168, :] = sums
    NC1 = sheet1.shape[1]
    lane, at = halves((NC1, LANES))
    low = lane < middle
    coef, k1 = level_coef(1), level_step(1)
    ends = pltpu.roll(sheet1[half - 1], middle, 1), pltpu.roll(sheet1[0], middle, 1)
    for q in range(half // 2):
        both = sheet1[2 * q] + sheet1[2 * q + 1]
        prev = sheet1[2 * q - 1] if q else jnp.where(low, 0.0, ends[0])
        after_it = sheet1[2 * q + 2] if 2 * q + 2 < half else jnp.where(low, ends[1], 0.0)
        c = pltpu.roll(both, 1, 0) + pltpu.roll(both, NC1 - 1, 0)
        l = jnp.where(at == 0, 0.0, pltpu.roll(both, 1, 1)) + jnp.where(
            at == middle - 1, 0.0, pltpu.roll(both, LANES - 1, 1)
        )
        left = (1.0 - OMEGA) * both + k1 * (coef[0] * (prev + both + after_it) + coef[1] * c + coef[2] * l)
        coarse2[q] = 0.125 * twins(left, 1)
    coarse2[half // 2] = 0.125 * twins(jnp.where(wall == 0, sheet1[half - 1], sheet1[0]), 1)
    rows2 = NC1 // 2
    lane2, at2 = halves((rows2, LANES))
    pick = lane2 - at2 + 2 * (at2 % (middle // 2))
    for p in range(half // 4):
        pair = [lanes_at(coarse2[2 * p + k, pl.ds(0, rows2, stride=2), :], pick) for k in range(2)]
        out[rows2 * p : rows2 * (p + 1), :] = jnp.where(at2 < middle // 2, pair[0], pair[1])
    beside = jnp.zeros((NC1, LANES), F32)
    base = jnp.where(length == 0, middle - H, 0)
    for i in range(half):
        turned = pltpu.roll(sheet1[i], lax.rem(H * i - base + LANES, LANES), 1)
        beside = jnp.where(at // H == i, turned, beside)
    index = lax.broadcasted_iota(jnp.int32, (8, LANES), 0) ^ 1
    line = beside + jnp.concatenate([rows_at(beside[t : t + 8], index) for t in range(0, NC1, 8)], 0)
    line = 0.125 * (line + pltpu.roll(line, LANES - H, 1))
    m = lane - 96
    spot = jnp.where(m < H, 8 * m, middle + 8 * (m - H)) + jnp.where(length == 0, H - 1, 0)
    line = lanes_at(line, jnp.clip(spot, 0, LANES - 1))
    beside = jnp.where(jnp.logical_and(m >= 0, m < 8), line, beside)
    out[32 : 32 + NC1, :] = beside
    face = coarse2[half // 2, pl.ds(0, rows2, stride=2), :]
    face = lanes_at(face, jnp.where(wall == 0, middle, 0) + 2 * (at2 % (middle // 2)))
    inner = jnp.logical_and(lane2 >= middle // 2, lane2 < middle)
    out[32 : 32 + rows2, :] = jnp.where(inner, face, beside[:rows2])
    inner_surface = jnp.where(low, sheet1[0], pltpu.roll(sheet1[1], middle, 1))
    outer_surface = jnp.where(low, pltpu.roll(sheet1[half - 2], middle, 1), sheet1[half - 1])
    out[64 : 64 + NC1, :] = jnp.where(wall == 0, inner_surface, outer_surface)
    wall_out[0:168, :] = out[...]
    last = jnp.where(low, pltpu.roll(sheet1[half - 1], middle, 1), sheet1[half - 2])
    wall_out[168 : 168 + NC1, :] = jnp.where(wall == 0, last, inner_surface)


def around(x, by):
    rows, lanes = x.shape
    lane = lane_of(x.shape)
    c = pltpu.roll(x, by, 0) + pltpu.roll(x, rows - by, 0)
    l = jnp.where(lane < by, 0.0, pltpu.roll(x, by, 1)) + jnp.where(
        lane >= lanes - by, 0.0, pltpu.roll(x, lanes - by, 1)
    )
    return c, l


def twins(x, by):
    rows, lanes = x.shape
    if lanes == LANES:
        index = lax.broadcasted_iota(jnp.int32, (8, LANES), 0) ^ by
        x = x + jnp.concatenate([rows_at(x[t : t + 8], index) for t in range(0, rows, 8)], 0)
        return x + lanes_at(x, lane_of(x.shape) ^ by)
    row = lax.broadcasted_iota(jnp.int32, x.shape, 0)
    lane = lane_of(x.shape)
    x = x + jnp.where((row & by) == 0, pltpu.roll(x, rows - by, 0), pltpu.roll(x, by, 0))
    return x + jnp.where((lane & by) == 0, pltpu.roll(x, lanes - by, 1), pltpu.roll(x, by, 1))


def solve(sizes, relative, compacted, C, W, *refs):
    n_blk, n_len, n_wall = sizes
    count = n_len * n_wall + compacted
    blocks, refs = refs[:count], refs[count:]
    base_adj, base_pot, mask, patches, adj_prev, potential, patch_grad = refs[:7]
    b1, x1, b2, x2, b3, x3, near, pm, pe, tm, te, adj_out, pot_out, sheet, briefs, sems = refs[7:]
    L = LANES
    W1, C1 = W // 2, C // 2
    planes, NC1, NL1 = b1.shape
    planes -= 2
    blk, length, wall = lax.axis_index("blk"), lax.axis_index("len"), lax.axis_index("wall")
    half = W1 // 2
    middle = LANES // 2
    lane8 = lane_of((C1, LANES))
    often = 40 if NC1 * NL1 <= 4096 else 1

    def blk_of(d):
        return blk ^ d if relative else d

    def length_of(j):
        return (length + j) % n_len if n_len == 2 else j

    def wall_of(v):
        return (wall + v) % n_wall

    zero1 = jnp.zeros((NC1, NL1), F32)
    for ref in (b1, x1, b2, x2, b3, x3):
        ref[0] = zero1
        ref[ref.shape[0] - 1] = zero1

    if not compacted:
        for v in range(n_wall):
            wall_s = wall_of(v)
            mine = blocks[v * n_len : (v + 1) * n_len]

            def unpack(d):
                at = pl.ds(pl.multiple_of(C1 * blk_of(d), C1), C1)
                for t in range(n_len // 2):
                    one, two = mine[2 * t], mine[2 * t + 1]
                    for i in range(half):
                        a, b = one[d, i * C1 : (i + 1) * C1, :], two[d, i * C1 : (i + 1) * C1, :]
                        if n_len == 2:
                            a, b = jnp.where(length == 0, a, b), jnp.where(length == 0, b, a)
                        spot = 1 + wall_s * W1 + i
                        lanes = slice(t * LANES, (t + 1) * LANES)
                        b1[spot, at, lanes] = jnp.where(lane8 < middle, a, pltpu.roll(b, middle, 1))
                        b1[spot + half, at, lanes] = jnp.where(lane8 < middle, pltpu.roll(a, middle, 1), b)

            loop(0, n_blk, unpack, 4)
    if compacted:
        stack, len_brief, wall_brief, both_brief, own_brief = blocks
        lane8 = lane_of((C1, LANES))
        here8 = lane8 // middle == length
        here = lane_of((NC1, LANES)) // middle == length
        face_lane = jnp.where(length == 0, middle, middle - H)
        near8 = jnp.logical_and(lane8 >= face_lane, lane8 < face_lane + H)
        at_face = jnp.logical_and(lane_of((NC1, LANES)) >= face_lane, lane_of((NC1, LANES)) < face_lane + H)
        for d in range(n_blk):
            row = pl.multiple_of(C1 * blk_of(d), C1)
            beside = len_brief[pl.ds(32 + row, C1), :]
            for i in range(half):
                a = stack[d, i * C1 : (i + 1) * C1, :]
                b = pltpu.roll(a, middle, 1)
                for k, value in enumerate((jnp.where(length == 0, a, b), jnp.where(length == 0, b, a))):
                    turn = lax.rem(face_lane - H * i - middle * k + 2 * LANES, LANES)
                    rest = jnp.where(near8, pltpu.roll(beside, turn, 1), 0.0)
                    b1[1 + wall * W1 + i + half * k, pl.ds(row, C1), :] = jnp.where(here8, value, rest)

        def two_planes(tile):
            turned = pltpu.roll(tile, middle, 1)
            return jnp.where(length == 0, tile, turned), jnp.where(length == 0, turned, tile)

        beyond = two_planes(wall_brief[168 : 168 + NC1, :])
        beside = both_brief[32 : 32 + NC1, :]
        for k in range(2):
            off = jnp.where(wall == 0, H * k, middle + H * (half - 1 - k))
            rest = jnp.where(at_face, pltpu.roll(beside, lax.rem(face_lane - off + 2 * LANES, LANES), 1), 0.0)
            b1[jnp.where(wall == 0, 1 + W1 + k, W1 - k)] = jnp.where(here, beyond[k], rest)
        for k in range(2):
            theirs = two_planes(len_brief[64 : 64 + NC1, :])[1 - k]
            spot = jnp.where(wall == 0, 1, planes - 1) + k
            b1[spot] = jnp.where(here, b1[spot], theirs)
            ours = two_planes(wall_brief[64 : 64 + NC1, :])[k]
            theirs = two_planes(both_brief[64 : 64 + NC1, :])[1 - k]
            b1[jnp.where(wall == 0, planes - 1, 1) + k] = jnp.where(here, ours, theirs)
        first_half = length == 0
        for k in range(2):
            ours = jnp.where(wall == k, own_brief[0:64, :], wall_brief[0:64, :])
            theirs = jnp.where(wall == k, len_brief[0:64, :], both_brief[0:64, :])
            briefs[0, k] = jnp.where(first_half, ours, theirs)
            briefs[1, k] = jnp.where(first_half, theirs, ours)
        lane_8 = lane_of((8, LANES))
        quarter = middle // 2
        left_quarter = lane_8 % middle < quarter
        pairs_index = [lane_8 // 2, middle + lane_8 // 2]
        facing = jnp.logical_and(lane_8 >= middle - 2, lane_8 < middle + 2)
        coef1 = [level_step(1) * x for x in level_coef(1)]
        rows2 = NC1 // 2

        def merged(w, start):
            one, two = briefs[0, w, start : start + 8, :], briefs[1, w, start : start + 8, :]
            even = jnp.where(left_quarter, one, pltpu.roll(two, quarter, 1))
            odd = jnp.where(left_quarter, pltpu.roll(one, LANES - quarter, 1), two)
            return even, odd

        for w in range(n_wall):
            for t in range(rows2 // 8):
                lines = [briefs[h, w, pl.ds(32 + 16 * t, 8, stride=2), :] for h in range(2)]
                lines = [lanes_at(x, jnp.minimum(96 + lane_8 // 4, LANES - 1)) for x in lines]
                lines = coef1[2] * jnp.where(lane_8 % 4 < 2, lines[1], lines[0])
                for p in range(half // 4):
                    tiles = merged(w, rows2 * p + 8 * t)
                    for odd in range(2):
                        for high in range(2):
                            k = 2 * p + odd + half // 2 * high
                            value = lanes_at(tiles[odd], pairs_index[high])
                            line = pltpu.roll(lines, middle - 2 - 4 * k, 1)
                            value = value + jnp.where(facing, line, 0.0)
                            if k == (half - 1 if w == 0 else 0):
                                value = value + coef1[0] * lanes_at(merged(1 - w, 32 + 8 * t)[1], pairs_index[0])
                            for r in range(2):
                                b2[1 + w * half + k, pl.ds(16 * t + r, 8, stride=2), :] = value

    def total_of(x, wsum, level, by):
        coef = level_coef(level)
        c, l = around(x, by)
        return level_step(level) * (coef[0] * wsum + coef[1] * c + coef[2] * l)

    def left_pair(ref, i, level):
        both = ref[i] + ref[i + 1]
        return (1.0 - OMEGA) * both + total_of(both, ref[i - 1] + both + ref[i + 2], level, 2 ** (level - 1))

    def sweep(x_ref, b_ref, i, level):
        x = x_ref[i]
        total = total_of(x, x_ref[i - 1] + x_ref[i + 1], level, 2 ** (level - 1))
        return (1.0 - OMEGA) * x + level_step(level) * b_ref[i] + total

    def down1(q):
        b2[1 + q] = 0.125 * twins(left_pair(b1, 2 * q + 1, 1), 1)

    if not compacted:
        loop(0, planes // 2, down1, often)

    def down2(q):
        b3[1 + q] = 0.125 * twins(left_pair(b2, 2 * q + 1, 2), 2)

    loop(0, planes // 4, down2, often)

    deep = planes // 4
    k3 = level_step(3)

    x2[1 + deep] = zero1

    def start3(q):
        b = b3[1 + q]
        x2[1 + q] = k3 * ((2.0 - OMEGA) * b + total_of(b, b3[q] + b3[2 + q], 3, 4))

    loop(0, deep, start3, often)

    def sweep3(q):
        x3[1 + q] = sweep(x2, b3, 1 + q, 3)

    loop(0, deep, sweep3, often)
    k2 = level_step(2)

    def up2(q):
        coarse = x3[1 + q]
        x2[1 + 2 * q] = k2 * b2[1 + 2 * q] + coarse
        x2[2 + 2 * q] = k2 * b2[2 + 2 * q] + coarse

    loop(0, planes // 4, up2, often)

    k1 = level_step(1)

    def up1(q):
        fine = sweep(x2, b2, 1 + q, 2)
        x1[1 + 2 * q] = k1 * b1[1 + 2 * q] + fine
        x1[2 + 2 * q] = k1 * b1[2 + 2 * q] + fine

    if compacted:
        loop(0, half, lambda q: up1(half * wall + q), often)
        up1(half - wall)
        up1((planes // 2 - 1) * (1 - wall))
    else:
        loop(0, planes // 2, up1, often)

    Q = W1 + 2
    sectors = (blk, lax.rem(blk + 1, n_blk), lax.rem(blk + n_blk - 1, n_blk))
    spots3 = [pl.ds(pl.multiple_of(s * C1, C1), C1) for s in sectors]
    row8 = lax.broadcasted_iota(jnp.int32, (C1, NL1), 0)

    def three(ref, i):
        return jnp.concatenate([ref[i, s, :] for s in spots3], 0)

    def finish1(q):
        i = wall * W1 + q
        x = three(x1, i)
        wsum = three(x1, jnp.maximum(i - 1, 0)) + three(x1, jnp.minimum(i + 1, planes + 1))
        value = (1.0 - OMEGA) * x + k1 * three(b1, i) + total_of(x, wsum, 1, 1)
        value = jnp.where(jnp.logical_and(i >= 1, i <= planes), value, 0.0)
        set_plane(near, 2 * q, C1, value[:C1])
        set_plane(near, 2 * q + 1, C1, jnp.where(row8 < 2, value[C1 : 2 * C1], value[2 * C1 :]))

    loop(0, Q, finish1, often)

    first = length * middle
    R = C + 8
    row8 = lax.broadcasted_iota(jnp.int32, (8, LANES), 0)
    tile_lane = lane_of((8, LANES))
    at_e = jnp.where(tile_lane < H, middle + tile_lane // 2, tile_lane // 2 - middle)
    rim8 = rim_lanes(tile_lane, length, n_len)
    if NL1 == LANES:
        index_m, index_e = first + tile_lane // 2, jnp.clip(first + at_e, 0, LANES - 1)

        def spread(tile):
            return lanes_at(tile, index_m), jnp.where(rim8, lanes_at(tile, index_e), 0.0)

    else:
        source = lax.broadcasted_iota(jnp.int32, (NL1, LANES), 0)
        lane = lane_of((NL1, LANES))
        at_all = jnp.where(lane < H, middle + lane // 2, jnp.where(lane >= LANES - H, lane // 2 - middle, 4 * NL1))
        take_m = jnp.where(source == first + lane // 2, 1.0, 0.0).astype(F32)
        take_e = jnp.where(source == first + at_all, 1.0, 0.0).astype(F32)

        def spread(tile):
            return precise(tile, take_m), precise(tile, take_e)

    picks = (row8 // 2, H + row8 // 2)
    ends = jnp.where(row8 < H, 6 + row8 // 2, row8 // 2 - 2)

    def fine_rows(q):
        own = spread(plane(near, 2 * q, C1))
        beside = spread(plane(near, 2 * q + 1, C1))
        for out, a, b in ((pm, own[0], beside[0]), (pe, own[1], beside[1])):
            parts = (jnp.where(row8 < 6, a, b), a, jnp.where(row8 < 2, b, a))
            index = (ends, 2 + row8 // 2, ends)
            for k in range(3):
                out[pl.ds(pl.multiple_of(8 + R * q + 8 * k, 8), 8), :] = rows_at(parts[k], index[k])

    loop(0, Q, fine_rows, often)
    for ref in (pm, pe):
        ref[0:8, :] = jnp.zeros((8, LANES), F32)
        ref[8 + R * Q : 16 + R * Q, :] = jnp.zeros((8, LANES), F32)
    coef, k0 = level_coef(0), level_step(0)
    def fine(ref, t, by=0, count=R):
        return ref[pl.ds(8 + R * t + by, count), :]

    def coarse_terms(q):
        out = []
        sides = beside_lanes(fine(pm, q), fine(pe, q))
        for ref, l in zip((pm, pe), sides):
            x = fine(ref, q)
            c = fine(ref, q, -1) + fine(ref, q, 1)
            out.append((1.0 - OMEGA) * x + k0 * (coef[0] * x + coef[1] * c + coef[2] * l))
        return out

    ks = k0 * coef[0]

    def set_fine(ref, t, value):
        ref[pl.ds(pl.multiple_of(8 + R * t, 8), R), :] = value

    def put_end(t, q, other, ok):
        set_fine(tm, t, jnp.where(ok, coarse_terms(q)[0] + ks * fine(pm, other), 0.0))

    put_end(0, 0, 1, wall > 0)
    put_end(W + 1, Q - 1, Q - 2, wall < n_wall - 1)
    rim = rim_lanes(lane_of((R, LANES)), length, n_len)

    def level0(q):
        gm, ge = coarse_terms(q)
        for t, other in ((2 * q - 1, q - 1), (2 * q, q + 1)):
            set_fine(tm, t, gm + ks * fine(pm, other))
            set_fine(te, t, jnp.where(rim, ge + ks * fine(pe, other), 0.0))

    loop(1, 1 + W1, level0, often)

    def finish0(w):
        t = w + 1
        m, e = fine(tm, t, H, C), fine(te, t, H, C)
        cm = fine(tm, t, H - 1, C) + fine(tm, t, H + 1, C)
        wm = fine(tm, t - 1, H, C) + fine(tm, t + 1, H, C)
        lm = beside_lanes_main(m, e)
        moved = 2.0 * sum(SI) * m - SI[0] * wm - SI[1] * cm - SI[2] * lm
        set_plane(adj_out, w, C, plane(base_adj, w, C) - DT * plane(mask, w, C) * moved)
        set_plane(pot_out, w, C, plane(base_pot, w, C) + m)

    parts = 2
    size = W // parts
    copies = []
    for k in range(parts):
        loop(k * size, (k + 1) * size, finish0, often)
        spot = pl.ds(k * size * C, size * C)
        for n, (src, dst) in enumerate(((adj_out, adj_prev), (pot_out, potential))):
            copies.append(pltpu.make_async_copy(src.at[spot], dst.at[spot], sems.at[n, k]))
            copies[-1].start()

    NC, NL = sheet.shape[1:]

    def whole_fine(x):
        if NL1 == LANES:
            parts = []
            for t in range(0, NC1, 8):
                wide8 = [lanes_at(x[t : t + 8], tile_lane // 2 + k * middle) for k in range(2)]
                for pick in picks[:2]:
                    parts.append(jnp.concatenate([rows_at(v, pick) for v in wide8], 1))
            return jnp.concatenate(parts, 0)
        along_c = lax.broadcasted_iota(jnp.int32, (NC, NC1), 0) // 2
        along_l = lax.broadcasted_iota(jnp.int32, (NL1, NL), 1) // 2
        twice_c = jnp.where(along_c == lax.broadcasted_iota(jnp.int32, (NC, NC1), 1), 1.0, 0.0).astype(F32)
        twice_l = jnp.where(along_l == lax.broadcasted_iota(jnp.int32, (NL1, NL), 0), 1.0, 0.0).astype(F32)
        return precise(precise(twice_c, x), twice_l)

    for s, i in enumerate((1, planes)):
        p = whole_fine(sweep(x1, b1, i, 1))
        c, l = around(p, 1)
        sheet[s] = (1.0 - OMEGA) * p + k0 * (coef[0] * p + coef[1] * c + coef[2] * l)

    owned = [patches[r : r + 1, :] for r in range(2)]
    spot = lax.broadcasted_iota(jnp.int32, (8, LANES), 0) * LANES + lane_of((8, LANES))
    spot = spot.astype(F32)
    start = half * C1
    totals = [jnp.zeros((C, LANES), F32) for _ in owned]
    small = [jnp.zeros((8, LANES), F32) for _ in owned]
    for v in range(n_wall):
        wall_s = wall_of(v)
        for j in range(n_len):
            ref = blocks[v * n_len + j]
            at_l = pl.ds(pl.multiple_of(length_of(j) * L, L), L)
            if compacted and v + j:
                for b in range(n_blk):
                    values = sheet[wall_s, b * C : (b + 1) * C, at_l]
                    ids = ref[96 + b * C : 96 + (b + 1) * C, :]
                    totals = [x + jnp.where(ids == e, values, 0.0) for x, e in zip(totals, owned)]
                small = [x + jnp.where(spot == e, ref[160:168, :], 0.0) for x, e in zip(small, owned)]
                continue

            def add(d, carry):
                big, little = carry
                values = sheet[wall_s, pl.ds(pl.multiple_of(blk_of(d) * C, C), C), at_l]
                ids = ref[d, start : start + C, :]
                parts = ref[d, start + C : start + C + 8, :]
                big = [x + jnp.where(ids == e, values, 0.0) for x, e in zip(big, owned)]
                little = [x + jnp.where(spot == e, parts, 0.0) for x, e in zip(little, owned)]
                return big, little

            totals, small = lax.fori_loop(0, n_blk, add, (totals, small), unroll=min(4, n_blk))
    factor = 1.0 / (2.0 * C * L / 2) ** 0.5
    for r in range(2):
        patch_grad[0, r] = (jnp.sum(totals[r]) + jnp.sum(small[r])) * factor
    for copy in copies:
        copy.wait()


def ring(x, axis, by):
    count = lax.axis_size(axis)
    return lax.ppermute(x, axis, [(i, (i + by) % count) for i in range(count)])


def paired(x, by):
    return lax.ppermute(x, "blk", [(i, i ^ by) for i in range(lax.axis_size("blk"))])


def neighbour_pairs(x, odd_first):
    count = lax.axis_size("blk")
    assert count % 2 == 0
    return lax.ppermute(x, "blk", [(i, (i + (1 if i % 2 == odd_first else -1)) % count) for i in range(count)])


def across(x):
    n_wall = lax.axis_size("wall")
    pairs = [(l * n_wall + w, (1 - l) * n_wall + (w + 1) % n_wall) for l in range(2) for w in range(n_wall)]
    return lax.ppermute(x, ("len", "wall"), pairs)


def call(kernel, ins, outs, scratch, name, work=0, room=48):
    places = {"vmem": pltpu.VMEM, "smem": pltpu.SMEM, "any": pl.ANY, "hbm": pltpu.HBM}

    def specs(kinds):
        return [pl.BlockSpec(memory_space=places[kind]) for kind in kinds]

    cost = pl.CostEstimate(flops=work, bytes_accessed=work, transcendentals=0) if work else None
    return pl.pallas_call(
        kernel,
        out_shape=[jax.ShapeDtypeStruct(shape, F32) for shape, _ in outs],
        in_specs=specs(ins),
        out_specs=specs(kind for _, kind in outs),
        scratch_shapes=[pltpu.VMEM(shape, F32) if isinstance(shape, tuple) else shape for shape in scratch],
        compiler_params=pltpu.CompilerParams(vmem_limit_bytes=int(room * 2**20)),
        cost_estimate=cost,
        name=name,
    )


def body(adj_next, ion_slope, misfit, tissue_mask, patch_ids, owner_map):
    W, C, L = adj_next.shape
    n_blk, n_len, n_wall = lax.axis_size("blk"), lax.axis_size("len"), lax.axis_size("wall")
    electrodes = owner_map.shape[0]
    assert L == LANES and H * W == LANES and n_wall == 2 and electrodes == 2 * n_blk * n_len * n_wall
    N = W + 2 * H
    n_dir = 1 if n_len == 2 else 2
    cells = W * C
    vmem = "vmem"
    field, own = (N * C, L), (cells, L)
    raw = [x.reshape(cells, L) for x in (adj_next, ion_slope, tissue_mask, misfit)]

    *fields, wall_out = (faces := call(
        functools.partial(pack_faces, n_len),
        ["hbm"] * 4,
        [(own, vmem)] * 4
        + [((sum(FACES), C, L), vmem)]
        + [((4, C, L), vmem)] * n_dir
        + [((C, L), vmem)] * n_dir,
        [pltpu.VMEM(own, jnp.int32), pltpu.SemaphoreType.DMA((4, 4))],
        "faces",
        room=52.75,
    )(*raw))[:5]
    strip_out, corner_out = faces[5 : 5 + n_dir], faces[5 + n_dir :]
    wall_in = ring(wall_out, "wall", 1)
    if n_dir == 1:
        strips = [ring(strip_out[0], "len", 1)]
        corners = [across(corner_out[0])]
    else:
        strips = [ring(strip_out[1], "len", -1), ring(strip_out[0], "len", 1)]
        corners = [ring(ring(corner_out[1], "wall", 1), "len", -1), ring(ring(corner_out[0], "wall", 1), "len", 1)]

    near = (sum(near_rows(n_dir, W)[-1][::2]), L)
    halos = [wall_in, *strips, *corners]
    first_out, second_out, own_rows = call(
        functools.partial(boundary, n_len, C),
        [vmem] * (5 + 2 * n_dir),
        [(near, vmem)] * 2 + [((2, 6, N, L), vmem)],
        [(48, N, L), near, near],
        "boundary",
    )(*fields, *halos)
    first_in = neighbour_pairs(first_out, 1)
    second_in = neighbour_pairs(second_out, 0)
    qm, bm, be, coarse, surface, patches = call(
        functools.partial(sector, n_len, n_wall, C, electrodes),
        [vmem] * (6 + 2 * n_dir),
        [(field, vmem)] * 3 + [((cells // 8, L), vmem), ((C, L), vmem), ((8, L), vmem)],
        [field, (cells // 2, L)] + [field] * 8,
        "sector",
        work=16 * 10**6,
    )(*fields, *halos, owner_map.reshape(1, electrodes))

    rows = (8, N, L)
    wide = LANES * ((electrodes + LANES - 1) // LANES)
    message = (cells // 8 + C + 8, L)
    rows_n, rows_p, mine = call(
        functools.partial(correct, electrodes, n_len, n_wall),
        [vmem] * 6,
        [(rows, vmem), (rows, vmem), (message, vmem)],
        [(1, N, L), (wide, L), near, near],
        "correct",
    )(own_rows, first_in, second_in, coarse, surface, patch_ids)

    relative = n_blk in (2, 4)
    moved = [paired(mine, d) for d in range(1, n_blk)] if relative else [lax.all_gather(mine, "blk")]
    base_adj, base_pot = call(
        functools.partial(source_part, n_len, n_wall, C),
        [vmem] * 6,
        [(own, vmem), (own, vmem)],
        [field] * 4 + [(2, N, L)],
        "source_part",
        work=12 * 10**6,
    )(bm, be, rows_n, rows_p, qm, fields[2])
    moved, base_adj = lax.optimization_barrier((moved, base_adj))
    sector_blocks = jnp.stack([mine] + moved) if relative else moved[0]
    compacted = (n_blk, n_len, C, W) == (4, 2, 16, 32)
    if compacted:
        brief, across_wall = call(
            functools.partial(compact, C, W),
            [vmem],
            [((168, L), vmem), ((200, L), vmem)],
            [(W // 4, n_blk * C // 2, L), (W // 8 + 1, n_blk * C // 2, L)],
            "compact",
        )(sector_blocks)
        len_brief = ring(brief, "len", 1)
        blocks = [sector_blocks, len_brief, ring(across_wall, "wall", 1), ring(len_brief, "wall", 1), brief]
    elif n_len == 2:
        here = [sector_blocks, ring(sector_blocks, "len", 1)]
    else:
        gathered = lax.all_gather(sector_blocks, "len")
        here = [gathered[j] for j in range(n_len)]
    if not compacted:
        blocks = here + [ring(x, "wall", 1) for x in here]

    NC1, NL1 = n_blk * C // 2, n_len * L // 2
    planes = n_wall * W // 2
    grids = [(planes // k + 2, NC1, NL1) for k in (1, 1, 2, 2, 4, 4)]
    Q = W // 2 + 2
    tall = (Q * (C + 8) + 16, L)
    taller = ((W + 2) * (C + 8) + 16, L)
    scratch = grids + [(Q * C, NL1), tall, tall, taller, taller, own, own]
    scratch += [(2, n_blk * C, n_len * L), (2, 2, 64, L), pltpu.SemaphoreType.DMA((2, 2))]
    adj_prev, potential, patch_grad = call(
        functools.partial(solve, (n_blk, n_len, n_wall), relative, compacted, C, W),
        [vmem] * (len(blocks) + 4),
        [(own, "any"), (own, "any"), ((1, 2), "smem")],
        scratch,
        "solve",
        room=48 if NC1 * NL1 <= 4096 else 58,
    )(*blocks, base_adj, base_pot, fields[2], patches)
    return adj_prev.reshape(W, C, L), potential.reshape(W, C, L), patch_grad


def solution(mesh):
    field = P(("groups", "wall"), "blk", "len")
    return jax.shard_map(
        body,
        mesh=mesh,
        in_specs=(field, field, field, field, field, P("groups")),
        out_specs=(field, field, P(("groups", "blk", "len", "wall"), None)),
        check_vma=False,
    )
```

```python
import functools

import jax
import jax.numpy as jnp
from jax import lax
from jax.experimental import pallas as pl
from jax.experimental.pallas import tpu as pltpu
from jax.sharding import PartitionSpec as P

SI = (0.6, 1.0, 3.0)
SE = (0.8, 1.2, 2.0)
SHIFT = 0.002
OMEGA = 0.8
DT = 0.1
H = 4
LANES = 128
HIGHEST = lax.Precision.HIGHEST
F32 = jnp.float32


def level_coef(level):
    return tuple((SI[i] + SE[i]) / 4.0**level for i in range(3))


def level_diag(level):
    return SHIFT + 2.0 * sum(level_coef(level))


def level_step(level):
    return OMEGA / level_diag(level)


def lane_of(shape):
    return lax.broadcasted_iota(jnp.int32, shape, len(shape) - 1)


def before(m, e):
    first = lane_of(m.shape) == 0
    rm, re = pltpu.roll(m, 1, 1), pltpu.roll(e, 1, 1)
    return jnp.where(first, re, rm), jnp.where(first, rm, re)


def after(m, e):
    last = lane_of(m.shape) == LANES - 1
    rm, re = pltpu.roll(m, LANES - 1, 1), pltpu.roll(e, LANES - 1, 1)
    return jnp.where(last, re, rm), jnp.where(last, rm, re)


def beside_lanes(m, e):
    bm, be = before(m, e)
    am, ae = after(m, e)
    return bm + am, be + ae


def beside_lanes_main(m, e):
    lane = lane_of(m.shape)
    ends = lanes_at(e, LANES - 1 - lane)
    left = jnp.where(lane == 0, ends, pltpu.roll(m, 1, 1))
    right = jnp.where(lane == LANES - 1, ends, pltpu.roll(m, LANES - 1, 1))
    return left + right


def beside_rows(x, row_before, row_after):
    rows = x.shape[0]
    row = lax.broadcasted_iota(jnp.int32, x.shape, 0)
    low = jnp.where(row == 0, row_before, pltpu.roll(x, 1, 0))
    high = jnp.where(row == rows - 1, row_after, pltpu.roll(x, rows - 1, 0))
    return low + high


def beside_dense(x):
    return pltpu.roll(x, 1, 0) + pltpu.roll(x, x.shape[0] - 1, 0)


def plane(ref, i, rows):
    return ref[pl.ds(pl.multiple_of(i * rows, rows), rows), :]


def set_plane(ref, i, rows, value):
    ref[pl.ds(pl.multiple_of(i * rows, rows), rows), :] = value


def loop(low, high, step, unroll):
    def wrapped(i, carry):
        step(i)
        return carry

    if unroll >= high - low:
        for i in range(low, high):
            step(i)
        return
    lax.fori_loop(low, high, wrapped, 0, unroll=unroll)


FACES = (H, H - 1, H - 1, H - 2)


def face_planes(array):
    return FACES[array], sum(FACES[:array])


def pack_faces(n_len, adj, ion, mask, mis, *rest):
    n_dir = 1 if n_len == 2 else 2
    fields, rest = rest[:4], rest[4:]
    corners, strips = rest[:n_dir], rest[n_dir : 2 * n_dir]
    wall_out, whole_mask, sems = rest[2 * n_dir :]
    cells = adj.shape[0]
    C = wall_out.shape[1]
    W = cells // C
    wall, length = lax.axis_index("wall"), lax.axis_index("len")
    targets = (fields[0], fields[1], whole_mask, fields[3])
    copies = []
    for a, (src, dst) in enumerate(zip((adj, ion, mask, mis), targets)):
        part = cells // 4
        for k in range(4):
            spot = pl.ds(k * part, part)
            copies.append(pltpu.make_async_copy(src.at[spot], dst.at[spot], sems.at[a, k]))
            copies[-1].start()

    base = jnp.where(wall == 0, W - H, 0)
    group = lane_of((C, LANES)) // H
    turns = [jnp.where(length == 0, H, 0)] if n_dir == 1 else [H, 0]
    corner = [jnp.zeros((C, LANES), F32) for _ in range(n_dir)]
    for a in (0, 1, 3, 2):
        for k in range(4):
            copies[4 * a + k].wait()
        if a == 2:
            fields[2][...] = whole_mask[...].astype(F32)
        ref = fields[a]
        strip = [jnp.zeros((C, LANES), F32) for _ in range(n_dir)]
        for w in range(W):
            value = ref[w * C : (w + 1) * C, :]
            for d in range(n_dir):
                turned = pltpu.roll(value, lax.rem(H * w + turns[d], LANES), 1)
                strip[d] = jnp.where(group == w, turned, strip[d])
        for d in range(n_dir):
            strips[d][a] = strip[d]
        count, first = face_planes(a)
        for p in range(count):
            face = plane(ref, base + jnp.where(wall == 0, H - count, 0) + p, C)
            wall_out[first + p] = face
            slot = first + p
            for d in range(n_dir):
                turned = pltpu.roll(face, lax.rem(H * slot + turns[d], LANES), 1)
                corner[d] = jnp.where(group == slot, turned, corner[d])
    for d in range(n_dir):
        corners[d][...] = corner[d]


def dense(ref, row, N, C):
    return ref[pl.ds(row, N, stride=C), :]


def dense_pair(m, e, row, N, C):
    return dense(m, row, N, C), dense(e, row, N, C)


def dense_apply(pair, inner, outer, coef):
    m, e = pair
    lm, le = beside_lanes(m, e)
    double = 2.0 * sum(coef)
    out = [double * m - coef[0] * beside_dense(m) - coef[2] * lm, double * e - coef[0] * beside_dense(e) - coef[2] * le]
    for row in (inner, outer):
        if row is not None:
            out = [out[k] - coef[1] * row[k] for k in range(2)]
    return out


def near_rows(n_dir, W):
    start, places = 8 * n_dir, []
    for reach in (0, 1, 2, 2, 3):
        places.append((start, H - reach, W + 2 * reach))
        start += W + 2 * reach
    assert start % 8 == 0
    return places


def rim_tiles(values):
    return [value[s : s + 8] for value in values for s in range(0, value.shape[0], 8)]


def rim_places(n_len, length):
    if n_len == 2:
        return [(jnp.where(length == 0, 0, LANES - H), True)]
    return [(0, length < n_len - 1), (LANES - H, length > 0)]


def boundary(n_len, C, *refs):
    n_dir = 1 if n_len == 2 else 2
    raw, refs = refs[:4], refs[4:]
    corners, strips, wall_in = refs[:n_dir], refs[n_dir : 2 * n_dir], refs[2 * n_dir]
    refs = refs[2 * n_dir + 1 :]
    first_out, second_out, own_rows, build, to_next, to_prev = refs
    W = raw[0].shape[0] // C
    N = W + 2 * H
    wall, length = lax.axis_index("wall"), lax.axis_index("len")
    places = rim_places(n_len, length)

    def strip_rows(packed, first, count):
        lane, k = lane_of((count, LANES)), lax.broadcasted_iota(jnp.int32, (count, LANES), 0)
        out = jnp.zeros((count, LANES), F32)
        for row, (off, ok) in zip(packed, places):
            j = lax.rem(lane - off + LANES, LANES)
            index = jnp.clip(H * (first + k) + j, 0, LANES - 1)
            taken = lanes_at(jnp.broadcast_to(row, (count, LANES)), index)
            out = jnp.where(jnp.logical_and(j < H, ok), taken, out)
        return out

    slots = iter(range(build.shape[0]))

    def assembled(own, halo, count):
        ref = build.at[next(slots)]
        ref[0:8, :] = jnp.zeros((8, LANES), F32)
        ref[N - 8 : N, :] = jnp.zeros((8, LANES), F32)
        ref[H : H + W, :] = own
        ref[H - count : H, :] = jnp.where(wall == 0, 0.0, halo)
        ref[H + W : H + W + count, :] = jnp.where(wall == 0, halo, 0.0)
        return ref[...]

    def row_of(a, r):
        count, first = face_planes(a)
        halo = jnp.concatenate([wall_in[first + p, r : r + 1, :] for p in range(count)], 0)
        m = assembled(raw[a][pl.ds(r, W, stride=C), :], halo, count)
        own = strip_rows([strip[a, r : r + 1, :] for strip in strips], 0, W)
        halo = strip_rows([corner[r : r + 1, :] for corner in corners], first, 8)[:count]
        return m, assembled(own, halo, count)

    length_shift = jnp.where(length == 0, 0, H) if n_dir == 1 else H
    group = lane_of((8, LANES)) // (H * n_dir)
    for side, (out, order) in enumerate(((to_next, (C - 1, C - 2, C - 3, C - 4)), (to_prev, (0, 1, 2, 3)))):
        adj = [row_of(0, r) for r in order]
        mask = [row_of(2, r) for r in order[:3]]
        q = []
        for k in range(3):
            ion = row_of(1, order[k])
            moved = dense_apply(adj[k], adj[k + 1], adj[k - 1] if k else None, SI)
            q.append([adj[k][j] - DT * mask[k][j] * (moved[j] + ion[j] * adj[k][j]) for j in range(2)])
        near = dense_apply(q[0], q[1], None, SI)
        mis = row_of(3, order[0])
        near = [near[j] + mis[j] for j in range(2)]
        second = dense_apply(q[1], q[2], q[0], SI)[0] + row_of(3, order[1])[0]
        for value, (start, first, count) in zip((second, near[0], q[0][0], mask[0][0], adj[0][0]), near_rows(n_dir, W)):
            out[start : start + count, :] = value[first : first + count]
        packs = [jnp.zeros((8, LANES), F32) for _ in range(n_dir)]
        for t, tile in enumerate(rim_tiles((near[1], q[0][1], mask[0][1], adj[0][1]))):
            k, at = divmod(t, LANES // (H * n_dir))
            turned = pltpu.roll(tile, lax.rem(length_shift + H * n_dir * at, LANES), 1)
            packs[k] = jnp.where(group == at, turned, packs[k])
        for k in range(n_dir):
            out[8 * k : 8 * k + 8, :] = packs[k]
        for k, pair in enumerate((adj[0], mask[0], q[0])):
            own_rows[side, 2 * k] = pair[0]
            own_rows[side, 2 * k + 1] = pair[1]
    even = lax.rem(lax.axis_index("blk"), 2) == 0
    first_out[...] = jnp.where(even, to_prev[...], to_next[...])
    second_out[...] = jnp.where(even, to_next[...], to_prev[...])


def spots(m_ref, e_ref, i, rows, coef):
    m, e = plane(m_ref, i, rows), plane(e_ref, i, rows)
    wm = plane(m_ref, i - 1, rows) + plane(m_ref, i + 1, rows)
    we = plane(e_ref, i - 1, rows) + plane(e_ref, i + 1, rows)
    lm, le = beside_lanes(m, e)
    cm, ce = beside_rows(m, 0.0, 0.0), beside_rows(e, 0.0, 0.0)
    double = 2.0 * sum(coef)
    dm = double * m - coef[0] * wm - coef[1] * cm - coef[2] * lm
    de = double * e - coef[0] * we - coef[1] * ce - coef[2] * le
    return m, e, dm, de


def rim_lanes(lane, length, n_len):
    return jnp.logical_or(
        jnp.logical_and(lane < H, length < n_len - 1),
        jnp.logical_and(lane >= LANES - H, length > 0),
    )


def inside(i, wall, W, n_wall):
    w = wall * W + i - H
    return jnp.logical_and(w >= 0, w < n_wall * W)


def lanes_at(x, index):
    return jnp.take_along_axis(x, index, axis=1, mode="promise_in_bounds")


def rows_at(x, index):
    return jnp.take_along_axis(x, index, axis=0, mode="promise_in_bounds")


def halved(low, high):
    lane = lane_of(low.shape)
    even = 2 * lane % LANES
    pairs = [lanes_at(x, even) + lanes_at(x, even + 1) for x in (low, high)]
    return 0.125 * jnp.where(lane < LANES // 2, pairs[0], pairs[1])


def precise(a, b):
    return jnp.dot(a, b, precision=HIGHEST, preferred_element_type=F32)


def assemble(n_len, C, raw, wall_in, strips, corners, xm, xe):
    W = raw[0].shape[0] // C
    N = W + 2 * H
    wall, length = lax.axis_index("wall"), lax.axis_index("len")
    lane = lane_of((C, LANES))
    places = rim_places(n_len, length)
    seen = [jnp.logical_and(lax.rem(lane - off + LANES, LANES) < H, ok) for off, ok in places]

    def rim(packed, base):
        out = jnp.zeros((C, LANES), F32)
        for row, ok, (off, _) in zip(packed, seen, places):
            out = jnp.where(ok, pltpu.roll(row, lax.rem(off - base + LANES, LANES), 1), out)
        return out

    zero = jnp.zeros((C, LANES), F32)
    last = N - H
    for a, own in enumerate(raw):
        packed = [strip[a] for strip in strips]
        for w in range(W):
            set_plane(xm[a], w + H, C, plane(own, w, C))
            set_plane(xe[a], w + H, C, rim(packed, H * w))
        packed = [corner[...] for corner in corners]
        for i in range(H):
            for at in (i, last + i):
                set_plane(xm[a], at, C, zero)
                set_plane(xe[a], at, C, zero)
        count, first = face_planes(a)
        here = jnp.where(wall == 0, last, H - count)
        for p in range(count):
            set_plane(xm[a], here + p, C, wall_in[first + p])
            set_plane(xe[a], here + p, C, rim(packed, H * (first + p)))


def sector(n_len, n_wall, C, electrodes, *refs):
    n_dir = 1 if n_len == 2 else 2
    raw, refs = refs[:4], refs[4:]
    corners, strips, wall_in = refs[:n_dir], refs[n_dir : 2 * n_dir], refs[2 * n_dir]
    refs = refs[2 * n_dir + 1 :]
    owner, qm, bm, be, coarse, surface, patches, qe, pairs = refs[:9]
    xm, xe = refs[9:13], refs[13:17]
    assemble(n_len, C, raw, wall_in, strips, corners, xm, xe)
    N = qm.shape[0] // C
    W = N - 2 * H
    wall, length = lax.axis_index("wall"), lax.axis_index("len")
    rim = rim_lanes(lane_of((C, LANES)), length, n_len)
    zero = jnp.zeros((C, LANES), F32)
    for i in (0, N - 1):
        set_plane(qm, i, C, zero)
        set_plane(qe, i, C, zero)
    for i in (0, 1, N - 2, N - 1):
        set_plane(bm, i, C, zero)
        set_plane(be, i, C, zero)

    def parabolic(i):
        m, e, dm, de = spots(xm[0], xe[0], i, C, SI)
        set_plane(qm, i, C, m - DT * plane(xm[2], i, C) * (dm + plane(xm[1], i, C) * m))
        set_plane(qe, i, C, e - DT * plane(xe[2], i, C) * (de + plane(xe[1], i, C) * e))

    loop(1, N - 1, parabolic, N)

    def elliptic_source(i):
        m, e, dm, de = spots(qm, qe, i, C, SI)
        ok = inside(i, wall, W, n_wall)
        set_plane(bm, i, C, jnp.where(ok, plane(xm[3], i, C) + dm, 0.0))
        set_plane(be, i, C, jnp.where(jnp.logical_and(rim, ok), plane(xe[3], i, C) + de, 0.0))

    loop(2, N - 2, elliptic_source, N)

    coef, k0 = level_coef(0), level_step(0)

    def left(i):
        m, e = plane(bm, i, C), plane(be, i, C)
        wm = plane(bm, i - 1, C) + plane(bm, i + 1, C)
        cm = beside_rows(m, 0.0, 0.0)
        lm = beside_lanes_main(m, e)
        return m, (1.0 - OMEGA) * m + k0 * (coef[0] * wm + coef[1] * cm + coef[2] * lm)

    def pair(q):
        i = 2 * q + H
        m, first = left(i)
        n, second = left(i + 1)
        set_plane(pairs, q, C, first + second)

        @pl.when(jnp.logical_and(q == 0, wall == 0))
        def _():
            surface[...] = k0 * (m + first)

        @pl.when(jnp.logical_and(q == W // 2 - 1, wall == n_wall - 1))
        def _():
            surface[...] = k0 * (n + second)

    loop(0, W // 2, pair, W)

    half = W * C // 8
    z = pairs[pl.ds(0, 2 * half, stride=2), :] + pairs[pl.ds(1, 2 * half, stride=2), :]
    coarse[...] = halved(z[:half], z[half:])

    blk = lax.axis_index("blk")
    me = (blk * n_len + length) * n_wall + wall
    which = lax.broadcasted_iota(jnp.int32, (1, electrodes), 1).astype(F32)
    mine = owner[...] == me
    patches[0:1, :] = jnp.full((1, LANES), jnp.min(jnp.where(mine, which, float(electrodes))))
    patches[1:2, :] = jnp.full((1, LANES), jnp.max(jnp.where(mine, which, -1.0)))
    patches[2:8, :] = jnp.zeros((6, LANES), F32)


def unpacked(ref, n_len, length, N):
    n_dir = 1 if n_len == 2 else 2
    mains = []
    for start, first, count in near_rows(n_dir, N - 2 * H):
        begin = min(start - first, ref.shape[0] - N)
        value = ref[begin : begin + N, :]
        behind = start - first - begin
        mains.append(pltpu.roll(value, N - behind, 0) if behind else value)
    rim = rim_lanes(lane_of((8, LANES)), length, n_len)
    shift = jnp.where(length == 0, 0, H) if n_dir == 1 else H
    rims = []
    for k in range(4):
        parts = []
        for s in range(N // 8):
            pack, at = divmod(k * (N // 8) + s, LANES // (H * n_dir))
            back = lax.rem(2 * LANES - shift - H * n_dir * at, LANES)
            parts.append(jnp.where(rim, pltpu.roll(ref[8 * pack : 8 * pack + 8, :], back, 1), 0.0))
        rims.append(jnp.concatenate(parts, 0))
    second, near, q, mask, adj = mains
    return (adj, rims[3]), (mask, rims[2]), (q, rims[1]), (near, rims[0]), second


def lateral(pair):
    return dense_apply(pair, None, None, SI)


def source_rows(own, other):
    adj_o, mask_o, q_o = own
    adj_n, mask_n, q_n, p_n, second_n = other
    step = DT * SI[1]
    delta_o = [step * mask_o[k] * adj_n[k] for k in range(2)]
    delta_n = [step * mask_n[k] * adj_o[k] for k in range(2)]
    lat_o, lat_n = lateral(delta_o), lateral(delta_n)
    near = [lat_o[k] - SI[1] * (q_n[k] + delta_n[k]) for k in range(2)]
    second = [-SI[1] * delta_o[k] for k in range(2)]
    halo = [p_n[k] + lat_n[k] - SI[1] * (q_o[k] + delta_o[k]) for k in range(2)]
    halo_second = second_n - SI[1] * delta_n[0]
    return near, second, halo, halo_second, delta_o[0]


def correct(electrodes, n_len, n_wall, own_rows, first_in, second_in, coarse, surface, ids, *rest):
    rows_n, rows_p, message = rest[:3]
    lines, sums, from_next, from_prev = rest[3:]
    even = lax.rem(lax.axis_index("blk"), 2) == 0
    from_next[...] = jnp.where(even, second_in[...], first_in[...])
    from_prev[...] = jnp.where(even, first_in[...], second_in[...])
    _, C, L = ids.shape
    N = own_rows.shape[2]
    W = N - 2 * H
    wall, length = lax.axis_index("wall"), lax.axis_index("len")
    ok_m = inside(lax.broadcasted_iota(jnp.int32, (N, LANES), 0), wall, W, n_wall)
    ok_e = jnp.logical_and(ok_m, rim_lanes(lane_of((N, LANES)), length, n_len))
    coef, k0 = level_coef(0), level_step(0)
    y = surface[...]
    row = lax.broadcasted_iota(jnp.int32, (C, LANES), 0)
    at = pl.ds(jnp.where(wall == 0, H, W + H - 1), 1)
    lows, highs = [], []
    W1, C1 = W // 2, C // 2
    for side, (other, out, order) in enumerate(
        ((from_next, rows_n, (C - 1, C - 2, C - 3)), (from_prev, rows_p, (0, 1, 2)))
    ):
        own = [(own_rows[side, 2 * k], own_rows[side, 2 * k + 1]) for k in range(3)]
        near, second, halo, halo_second, delta = source_rows(own, unpacked(other, n_len, length, N))
        near = [jnp.where(ok_m, near[0], 0.0), jnp.where(ok_e, near[1], 0.0)]
        second = [jnp.where(ok_m, second[0], 0.0), jnp.where(ok_e, second[1], 0.0)]
        out[0] = halo_m = jnp.where(ok_m, halo[0], 0.0)
        out[1] = jnp.where(ok_e, halo[1], 0.0)
        out[2] = jnp.where(ok_m, halo_second, 0.0)
        out[3] = delta
        out[4], out[5] = near
        out[6], out[7] = second

        def turned(pair, beside):
            m, e = pair
            return (1.0 - OMEGA) * m + k0 * (
                coef[0] * beside_dense(m) + coef[2] * beside_lanes_main(m, e) + coef[1] * beside
            )

        first = turned(near, second[0] + halo_m)
        next_one = turned(second, near[0])
        third = k0 * coef[1] * second[0]
        for k, change in enumerate((near[0] + first, second[0] + next_one, third)):
            lines[0] = change
            y = y + jnp.where(row == order[k], k0 * lines[0, at, :], 0.0)
        for change in (first + next_one, third):
            lines[0] = change
            both = lines[0, pl.ds(H, W1, stride=2), :] + lines[0, pl.ds(H + 1, W1, stride=2), :]
            lows.append(both[: W1 // 2])
            highs.append(both[W1 // 2 :])
    add = halved(jnp.concatenate(lows, 0), jnp.concatenate(highs, 0))
    half = W * C // 8
    message[0:half, :] = coarse[...]
    for k, c1 in enumerate((C1 - 1, C1 - 2, 0, 1)):
        spot = pl.ds(c1, W1 // 2, stride=C1)
        message[spot, :] = message[spot, :] + add[k * (W1 // 2) : (k + 1) * (W1 // 2)]
    patch = ids[0]
    message[half : half + C, :] = patch.astype(F32)
    wide = sums.shape[0]
    if wide > electrodes:
        sums[...] = jnp.zeros(sums.shape, F32)

    def one(e):
        sums[pl.ds(e, 1), :] = jnp.sum(jnp.where(patch == e, y, 0.0), axis=0, keepdims=True)

    loop(0, electrodes, one, 32 if electrodes <= 32 else 8)
    totals = lax.dot_general(
        jnp.ones((8, LANES), F32), sums[...], (((1,), (1,)), ((), ())), precision=HIGHEST, preferred_element_type=F32
    )
    message[half + C : half + C + 8, :] = jnp.zeros((8, LANES), F32)
    for t in range(wide // LANES):
        message[half + C + t : half + C + t + 1, :] = totals[0:1, t * LANES : (t + 1) * LANES]


def source_part(n_len, n_wall, C, bm, be, rows_n, rows_p, qm, mask, base_adj, base_pot, fm, fe, tm, te, hp):
    N = bm.shape[0] // C
    W = N - 2 * H
    length, wall = lax.axis_index("len"), lax.axis_index("wall")
    fm[...] = bm[...]
    fe[...] = be[...]
    for rows, near, second in ((rows_n, C - 1, C - 2), (rows_p, 0, 1)):
        for k, at in ((4, near), (6, second)):
            spot = pl.ds(at, N, stride=C)
            fm[spot, :] = fm[spot, :] + rows[k]
            fe[spot, :] = fe[spot, :] + rows[k + 1]
    coef, k0 = level_coef(0), level_step(0)
    rim = rim_lanes(lane_of((C, LANES)), length, n_len)

    def part(i):
        m, e = plane(fm, i, C), plane(fe, i, C)
        wm = plane(fm, i - 1, C) + plane(fm, i + 1, C)
        we = plane(fe, i - 1, C) + plane(fe, i + 1, C)
        lm, le = beside_lanes(m, e)
        at = pl.ds(i, 1)
        cm = beside_rows(m, rows_p[0, at, :], rows_n[0, at, :])
        ce = beside_rows(e, rows_p[1, at, :], rows_n[1, at, :])
        pm = k0 * ((2.0 - OMEGA) * m + k0 * (coef[0] * wm + coef[1] * cm + coef[2] * lm))
        pe = k0 * ((2.0 - OMEGA) * e + k0 * (coef[0] * we + coef[1] * ce + coef[2] * le))
        set_plane(tm, i, C, jnp.where(inside(i, wall, W, n_wall), pm, 0.0))
        set_plane(te, i, C, jnp.where(rim, pe, 0.0))

    loop(H - 1, N - H + 1, part, N)
    for side, (rows, at) in enumerate(((rows_n, C - 1), (rows_p, 0))):
        m = rows[0]
        total = (
            coef[0] * beside_dense(m)
            + coef[1] * (rows[2] + dense(fm, at, N, C))
            + coef[2] * beside_lanes_main(m, rows[1])
        )
        hp[side] = k0 * ((2.0 - OMEGA) * m + k0 * total)
    row = lax.broadcasted_iota(jnp.int32, (C, LANES), 0)

    def finish(w):
        i = w + H
        m, e = plane(tm, i, C), plane(te, i, C)
        at = pl.ds(i, 1)
        wm = plane(tm, i - 1, C) + plane(tm, i + 1, C)
        cm = beside_rows(m, hp[1, at, :], hp[0, at, :])
        lm = beside_lanes_main(m, e)
        lam = plane(qm, i, C)
        lam = lam + jnp.where(row == C - 1, rows_n[3, at, :], 0.0) + jnp.where(row == 0, rows_p[3, at, :], 0.0)
        moved = 2.0 * sum(SI) * m - SI[0] * wm - SI[1] * cm - SI[2] * lm
        set_plane(base_adj, w, C, lam - DT * plane(mask, w, C) * moved)
        set_plane(base_pot, w, C, m)

    loop(0, W, finish, W)


def halves(shape):
    lane = lane_of(shape)
    return lane, lane % (LANES // 2)


def compact(C, W, blocks, out, wall_out, sheet1, coarse2):
    n_blk = blocks.shape[0]
    W1, C1 = W // 2, C // 2
    half, start, middle = W1 // 2, W1 // 2 * C1, LANES // 2
    blk, length, wall = lax.axis_index("blk"), lax.axis_index("len"), lax.axis_index("wall")
    sums = jnp.zeros((8, LANES), F32)
    for d in range(n_blk):
        b = blk ^ d
        for i in range(half):
            sheet1[i, pl.ds(pl.multiple_of(C1 * b, C1), C1), :] = blocks[d, i * C1 : (i + 1) * C1, :]
        out[pl.ds(pl.multiple_of(96 + C * b, C), C), :] = blocks[d, start : start + C, :]
        sums = sums + blocks[d, start + C : start + C + 8, :]
    out[160:168, :] = sums
    NC1 = sheet1.shape[1]
    lane, at = halves((NC1, LANES))
    low = lane < middle
    coef, k1 = level_coef(1), level_step(1)
    ends = pltpu.roll(sheet1[half - 1], middle, 1), pltpu.roll(sheet1[0], middle, 1)
    for q in range(half // 2):
        both = sheet1[2 * q] + sheet1[2 * q + 1]
        prev = sheet1[2 * q - 1] if q else jnp.where(low, 0.0, ends[0])
        after_it = sheet1[2 * q + 2] if 2 * q + 2 < half else jnp.where(low, ends[1], 0.0)
        c = pltpu.roll(both, 1, 0) + pltpu.roll(both, NC1 - 1, 0)
        l = jnp.where(at == 0, 0.0, pltpu.roll(both, 1, 1)) + jnp.where(
            at == middle - 1, 0.0, pltpu.roll(both, LANES - 1, 1)
        )
        left = (1.0 - OMEGA) * both + k1 * (coef[0] * (prev + both + after_it) + coef[1] * c + coef[2] * l)
        coarse2[q] = 0.125 * twins(left, 1)
    coarse2[half // 2] = 0.125 * twins(jnp.where(wall == 0, sheet1[half - 1], sheet1[0]), 1)
    rows2 = NC1 // 2
    lane2, at2 = halves((rows2, LANES))
    pick = lane2 - at2 + 2 * (at2 % (middle // 2))
    for p in range(half // 4):
        pair = [lanes_at(coarse2[2 * p + k, pl.ds(0, rows2, stride=2), :], pick) for k in range(2)]
        out[rows2 * p : rows2 * (p + 1), :] = jnp.where(at2 < middle // 2, pair[0], pair[1])
    beside = jnp.zeros((NC1, LANES), F32)
    base = jnp.where(length == 0, middle - H, 0)
    for i in range(half):
        turned = pltpu.roll(sheet1[i], lax.rem(H * i - base + LANES, LANES), 1)
        beside = jnp.where(at // H == i, turned, beside)
    index = lax.broadcasted_iota(jnp.int32, (8, LANES), 0) ^ 1
    line = beside + jnp.concatenate([rows_at(beside[t : t + 8], index) for t in range(0, NC1, 8)], 0)
    line = 0.125 * (line + pltpu.roll(line, LANES - H, 1))
    m = lane - 96
    spot = jnp.where(m < H, 8 * m, middle + 8 * (m - H)) + jnp.where(length == 0, H - 1, 0)
    line = lanes_at(line, jnp.clip(spot, 0, LANES - 1))
    beside = jnp.where(jnp.logical_and(m >= 0, m < 8), line, beside)
    out[32 : 32 + NC1, :] = beside
    face = coarse2[half // 2, pl.ds(0, rows2, stride=2), :]
    face = lanes_at(face, jnp.where(wall == 0, middle, 0) + 2 * (at2 % (middle // 2)))
    inner = jnp.logical_and(lane2 >= middle // 2, lane2 < middle)
    out[32 : 32 + rows2, :] = jnp.where(inner, face, beside[:rows2])
    inner_surface = jnp.where(low, sheet1[0], pltpu.roll(sheet1[1], middle, 1))
    outer_surface = jnp.where(low, pltpu.roll(sheet1[half - 2], middle, 1), sheet1[half - 1])
    out[64 : 64 + NC1, :] = jnp.where(wall == 0, inner_surface, outer_surface)
    wall_out[0:168, :] = out[...]
    last = jnp.where(low, pltpu.roll(sheet1[half - 1], middle, 1), sheet1[half - 2])
    wall_out[168 : 168 + NC1, :] = jnp.where(wall == 0, last, inner_surface)


def around(x, by):
    rows, lanes = x.shape
    lane = lane_of(x.shape)
    c = pltpu.roll(x, by, 0) + pltpu.roll(x, rows - by, 0)
    l = jnp.where(lane < by, 0.0, pltpu.roll(x, by, 1)) + jnp.where(
        lane >= lanes - by, 0.0, pltpu.roll(x, lanes - by, 1)
    )
    return c, l


def twins(x, by):
    rows, lanes = x.shape
    if lanes == LANES:
        index = lax.broadcasted_iota(jnp.int32, (8, LANES), 0) ^ by
        x = x + jnp.concatenate([rows_at(x[t : t + 8], index) for t in range(0, rows, 8)], 0)
        return x + lanes_at(x, lane_of(x.shape) ^ by)
    row = lax.broadcasted_iota(jnp.int32, x.shape, 0)
    lane = lane_of(x.shape)
    x = x + jnp.where((row & by) == 0, pltpu.roll(x, rows - by, 0), pltpu.roll(x, by, 0))
    return x + jnp.where((lane & by) == 0, pltpu.roll(x, lanes - by, 1), pltpu.roll(x, by, 1))


def solve(sizes, relative, compacted, C, W, *refs):
    n_blk, n_len, n_wall = sizes
    count = n_len * n_wall + compacted
    blocks, refs = refs[:count], refs[count:]
    base_adj, base_pot, mask, patches, adj_prev, potential, patch_grad = refs[:7]
    b1, x1, b2, x2, b3, x3, near, pm, pe, tm, te, adj_out, pot_out, sheet, briefs, sems = refs[7:]
    L = LANES
    W1, C1 = W // 2, C // 2
    planes, NC1, NL1 = b1.shape
    planes -= 2
    blk, length, wall = lax.axis_index("blk"), lax.axis_index("len"), lax.axis_index("wall")
    half = W1 // 2
    middle = LANES // 2
    lane8 = lane_of((C1, LANES))
    often = 40 if NC1 * NL1 <= 4096 else 1

    def blk_of(d):
        return blk ^ d if relative else d

    def length_of(j):
        return (length + j) % n_len if n_len == 2 else j

    def wall_of(v):
        return (wall + v) % n_wall

    zero1 = jnp.zeros((NC1, NL1), F32)
    for ref in (b1, x1, b2, x2, b3, x3):
        ref[0] = zero1
        ref[ref.shape[0] - 1] = zero1

    if not compacted:
        for v in range(n_wall):
            wall_s = wall_of(v)
            mine = blocks[v * n_len : (v + 1) * n_len]

            def unpack(d):
                at = pl.ds(pl.multiple_of(C1 * blk_of(d), C1), C1)
                for t in range(n_len // 2):
                    one, two = mine[2 * t], mine[2 * t + 1]
                    for i in range(half):
                        a, b = one[d, i * C1 : (i + 1) * C1, :], two[d, i * C1 : (i + 1) * C1, :]
                        if n_len == 2:
                            a, b = jnp.where(length == 0, a, b), jnp.where(length == 0, b, a)
                        spot = 1 + wall_s * W1 + i
                        lanes = slice(t * LANES, (t + 1) * LANES)
                        b1[spot, at, lanes] = jnp.where(lane8 < middle, a, pltpu.roll(b, middle, 1))
                        b1[spot + half, at, lanes] = jnp.where(lane8 < middle, pltpu.roll(a, middle, 1), b)

            loop(0, n_blk, unpack, 4)
    if compacted:
        stack, len_brief, wall_brief, both_brief, own_brief = blocks
        lane8 = lane_of((C1, LANES))
        here8 = lane8 // middle == length
        here = lane_of((NC1, LANES)) // middle == length
        face_lane = jnp.where(length == 0, middle, middle - H)
        near8 = jnp.logical_and(lane8 >= face_lane, lane8 < face_lane + H)
        at_face = jnp.logical_and(lane_of((NC1, LANES)) >= face_lane, lane_of((NC1, LANES)) < face_lane + H)
        for d in range(n_blk):
            row = pl.multiple_of(C1 * blk_of(d), C1)
            beside = len_brief[pl.ds(32 + row, C1), :]
            for i in range(half):
                a = stack[d, i * C1 : (i + 1) * C1, :]
                b = pltpu.roll(a, middle, 1)
                for k, value in enumerate((jnp.where(length == 0, a, b), jnp.where(length == 0, b, a))):
                    turn = lax.rem(face_lane - H * i - middle * k + 2 * LANES, LANES)
                    rest = jnp.where(near8, pltpu.roll(beside, turn, 1), 0.0)
                    b1[1 + wall * W1 + i + half * k, pl.ds(row, C1), :] = jnp.where(here8, value, rest)

        def two_planes(tile):
            turned = pltpu.roll(tile, middle, 1)
            return jnp.where(length == 0, tile, turned), jnp.where(length == 0, turned, tile)

        beyond = two_planes(wall_brief[168 : 168 + NC1, :])
        beside = both_brief[32 : 32 + NC1, :]
        for k in range(2):
            off = jnp.where(wall == 0, H * k, middle + H * (half - 1 - k))
            rest = jnp.where(at_face, pltpu.roll(beside, lax.rem(face_lane - off + 2 * LANES, LANES), 1), 0.0)
            b1[jnp.where(wall == 0, 1 + W1 + k, W1 - k)] = jnp.where(here, beyond[k], rest)
        for k in range(2):
            theirs = two_planes(len_brief[64 : 64 + NC1, :])[1 - k]
            spot = jnp.where(wall == 0, 1, planes - 1) + k
            b1[spot] = jnp.where(here, b1[spot], theirs)
            ours = two_planes(wall_brief[64 : 64 + NC1, :])[k]
            theirs = two_planes(both_brief[64 : 64 + NC1, :])[1 - k]
            b1[jnp.where(wall == 0, planes - 1, 1) + k] = jnp.where(here, ours, theirs)
        first_half = length == 0
        for k in range(2):
            ours = jnp.where(wall == k, own_brief[0:64, :], wall_brief[0:64, :])
            theirs = jnp.where(wall == k, len_brief[0:64, :], both_brief[0:64, :])
            briefs[0, k] = jnp.where(first_half, ours, theirs)
            briefs[1, k] = jnp.where(first_half, theirs, ours)
        lane_8 = lane_of((8, LANES))
        quarter = middle // 2
        left_quarter = lane_8 % middle < quarter
        pairs_index = [lane_8 // 2, middle + lane_8 // 2]
        facing = jnp.logical_and(lane_8 >= middle - 2, lane_8 < middle + 2)
        coef1 = [level_step(1) * x for x in level_coef(1)]
        rows2 = NC1 // 2

        def merged(w, start):
            one, two = briefs[0, w, start : start + 8, :], briefs[1, w, start : start + 8, :]
            even = jnp.where(left_quarter, one, pltpu.roll(two, quarter, 1))
            odd = jnp.where(left_quarter, pltpu.roll(one, LANES - quarter, 1), two)
            return even, odd

        for w in range(n_wall):
            for t in range(rows2 // 8):
                lines = [briefs[h, w, pl.ds(32 + 16 * t, 8, stride=2), :] for h in range(2)]
                lines = [lanes_at(x, jnp.minimum(96 + lane_8 // 4, LANES - 1)) for x in lines]
                lines = coef1[2] * jnp.where(lane_8 % 4 < 2, lines[1], lines[0])
                for p in range(half // 4):
                    tiles = merged(w, rows2 * p + 8 * t)
                    for odd in range(2):
                        for high in range(2):
                            k = 2 * p + odd + half // 2 * high
                            value = lanes_at(tiles[odd], pairs_index[high])
                            line = pltpu.roll(lines, middle - 2 - 4 * k, 1)
                            value = value + jnp.where(facing, line, 0.0)
                            if k == (half - 1 if w == 0 else 0):
                                value = value + coef1[0] * lanes_at(merged(1 - w, 32 + 8 * t)[1], pairs_index[0])
                            for r in range(2):
                                b2[1 + w * half + k, pl.ds(16 * t + r, 8, stride=2), :] = value

    def total_of(x, wsum, level, by):
        coef = level_coef(level)
        c, l = around(x, by)
        return level_step(level) * (coef[0] * wsum + coef[1] * c + coef[2] * l)

    def left_pair(ref, i, level):
        both = ref[i] + ref[i + 1]
        return (1.0 - OMEGA) * both + total_of(both, ref[i - 1] + both + ref[i + 2], level, 2 ** (level - 1))

    def sweep(x_ref, b_ref, i, level):
        x = x_ref[i]
        total = total_of(x, x_ref[i - 1] + x_ref[i + 1], level, 2 ** (level - 1))
        return (1.0 - OMEGA) * x + level_step(level) * b_ref[i] + total

    def down1(q):
        b2[1 + q] = 0.125 * twins(left_pair(b1, 2 * q + 1, 1), 1)

    if not compacted:
        loop(0, planes // 2, down1, often)

    def down2(q):
        b3[1 + q] = 0.125 * twins(left_pair(b2, 2 * q + 1, 2), 2)

    loop(0, planes // 4, down2, often)

    deep = planes // 4
    k3 = level_step(3)

    x2[1 + deep] = zero1

    def start3(q):
        b = b3[1 + q]
        x2[1 + q] = k3 * ((2.0 - OMEGA) * b + total_of(b, b3[q] + b3[2 + q], 3, 4))

    loop(0, deep, start3, often)

    def sweep3(q):
        x3[1 + q] = sweep(x2, b3, 1 + q, 3)

    loop(0, deep, sweep3, often)
    k2 = level_step(2)

    def up2(q):
        coarse = x3[1 + q]
        x2[1 + 2 * q] = k2 * b2[1 + 2 * q] + coarse
        x2[2 + 2 * q] = k2 * b2[2 + 2 * q] + coarse

    loop(0, planes // 4, up2, often)

    k1 = level_step(1)

    def up1(q):
        fine = sweep(x2, b2, 1 + q, 2)
        x1[1 + 2 * q] = k1 * b1[1 + 2 * q] + fine
        x1[2 + 2 * q] = k1 * b1[2 + 2 * q] + fine

    if compacted:
        loop(0, half, lambda q: up1(half * wall + q), often)
        up1(half - wall)
        up1((planes // 2 - 1) * (1 - wall))
    else:
        loop(0, planes // 2, up1, often)

    Q = W1 + 2
    sectors = (blk, lax.rem(blk + 1, n_blk), lax.rem(blk + n_blk - 1, n_blk))
    spots3 = [pl.ds(pl.multiple_of(s * C1, C1), C1) for s in sectors]
    row8 = lax.broadcasted_iota(jnp.int32, (C1, NL1), 0)

    def three(ref, i):
        return jnp.concatenate([ref[i, s, :] for s in spots3], 0)

    def finish1(q):
        i = wall * W1 + q
        x = three(x1, i)
        wsum = three(x1, jnp.maximum(i - 1, 0)) + three(x1, jnp.minimum(i + 1, planes + 1))
        value = (1.0 - OMEGA) * x + k1 * three(b1, i) + total_of(x, wsum, 1, 1)
        value = jnp.where(jnp.logical_and(i >= 1, i <= planes), value, 0.0)
        set_plane(near, 2 * q, C1, value[:C1])
        set_plane(near, 2 * q + 1, C1, jnp.where(row8 < 2, value[C1 : 2 * C1], value[2 * C1 :]))

    loop(0, Q, finish1, often)

    first = length * middle
    R = C + 8
    row8 = lax.broadcasted_iota(jnp.int32, (8, LANES), 0)
    tile_lane = lane_of((8, LANES))
    at_e = jnp.where(tile_lane < H, middle + tile_lane // 2, tile_lane // 2 - middle)
    rim8 = rim_lanes(tile_lane, length, n_len)
    if NL1 == LANES:
        index_m, index_e = first + tile_lane // 2, jnp.clip(first + at_e, 0, LANES - 1)

        def spread(tile):
            return lanes_at(tile, index_m), jnp.where(rim8, lanes_at(tile, index_e), 0.0)

    else:
        source = lax.broadcasted_iota(jnp.int32, (NL1, LANES), 0)
        lane = lane_of((NL1, LANES))
        at_all = jnp.where(lane < H, middle + lane // 2, jnp.where(lane >= LANES - H, lane // 2 - middle, 4 * NL1))
        take_m = jnp.where(source == first + lane // 2, 1.0, 0.0).astype(F32)
        take_e = jnp.where(source == first + at_all, 1.0, 0.0).astype(F32)

        def spread(tile):
            return precise(tile, take_m), precise(tile, take_e)

    picks = (row8 // 2, H + row8 // 2)
    ends = jnp.where(row8 < H, 6 + row8 // 2, row8 // 2 - 2)

    def fine_rows(q):
        own = spread(plane(near, 2 * q, C1))
        beside = spread(plane(near, 2 * q + 1, C1))
        for out, a, b in ((pm, own[0], beside[0]), (pe, own[1], beside[1])):
            parts = (jnp.where(row8 < 6, a, b), a, jnp.where(row8 < 2, b, a))
            index = (ends, 2 + row8 // 2, ends)
            for k in range(3):
                out[pl.ds(pl.multiple_of(8 + R * q + 8 * k, 8), 8), :] = rows_at(parts[k], index[k])

    loop(0, Q, fine_rows, often)
    for ref in (pm, pe):
        ref[0:8, :] = jnp.zeros((8, LANES), F32)
        ref[8 + R * Q : 16 + R * Q, :] = jnp.zeros((8, LANES), F32)
    coef, k0 = level_coef(0), level_step(0)
    def fine(ref, t, by=0, count=R):
        return ref[pl.ds(8 + R * t + by, count), :]

    def coarse_terms(q):
        out = []
        sides = beside_lanes(fine(pm, q), fine(pe, q))
        for ref, l in zip((pm, pe), sides):
            x = fine(ref, q)
            c = fine(ref, q, -1) + fine(ref, q, 1)
            out.append((1.0 - OMEGA) * x + k0 * (coef[0] * x + coef[1] * c + coef[2] * l))
        return out

    ks = k0 * coef[0]

    def set_fine(ref, t, value):
        ref[pl.ds(pl.multiple_of(8 + R * t, 8), R), :] = value

    def put_end(t, q, other, ok):
        set_fine(tm, t, jnp.where(ok, coarse_terms(q)[0] + ks * fine(pm, other), 0.0))

    put_end(0, 0, 1, wall > 0)
    put_end(W + 1, Q - 1, Q - 2, wall < n_wall - 1)
    rim = rim_lanes(lane_of((R, LANES)), length, n_len)

    def level0(q):
        gm, ge = coarse_terms(q)
        for t, other in ((2 * q - 1, q - 1), (2 * q, q + 1)):
            set_fine(tm, t, gm + ks * fine(pm, other))
            set_fine(te, t, jnp.where(rim, ge + ks * fine(pe, other), 0.0))

    loop(1, 1 + W1, level0, often)

    def finish0(w):
        t = w + 1
        m, e = fine(tm, t, H, C), fine(te, t, H, C)
        cm = fine(tm, t, H - 1, C) + fine(tm, t, H + 1, C)
        wm = fine(tm, t - 1, H, C) + fine(tm, t + 1, H, C)
        lm = beside_lanes_main(m, e)
        moved = 2.0 * sum(SI) * m - SI[0] * wm - SI[1] * cm - SI[2] * lm
        set_plane(adj_out, w, C, plane(base_adj, w, C) - DT * plane(mask, w, C) * moved)
        set_plane(pot_out, w, C, plane(base_pot, w, C) + m)

    parts = 4
    size = W // parts
    copies = []
    for k in range(parts):
        loop(k * size, (k + 1) * size, finish0, often)
        spot = pl.ds(k * size * C, size * C)
        for n, (src, dst) in enumerate(((adj_out, adj_prev), (pot_out, potential))):
            copies.append(pltpu.make_async_copy(src.at[spot], dst.at[spot], sems.at[n, k]))
            copies[-1].start()

    NC, NL = sheet.shape[1:]

    def whole_fine(x):
        if NL1 == LANES:
            parts = []
            for t in range(0, NC1, 8):
                wide8 = [lanes_at(x[t : t + 8], tile_lane // 2 + k * middle) for k in range(2)]
                for pick in picks[:2]:
                    parts.append(jnp.concatenate([rows_at(v, pick) for v in wide8], 1))
            return jnp.concatenate(parts, 0)
        along_c = lax.broadcasted_iota(jnp.int32, (NC, NC1), 0) // 2
        along_l = lax.broadcasted_iota(jnp.int32, (NL1, NL), 1) // 2
        twice_c = jnp.where(along_c == lax.broadcasted_iota(jnp.int32, (NC, NC1), 1), 1.0, 0.0).astype(F32)
        twice_l = jnp.where(along_l == lax.broadcasted_iota(jnp.int32, (NL1, NL), 0), 1.0, 0.0).astype(F32)
        return precise(precise(twice_c, x), twice_l)

    for s, i in enumerate((1, planes)):
        p = whole_fine(sweep(x1, b1, i, 1))
        c, l = around(p, 1)
        sheet[s] = (1.0 - OMEGA) * p + k0 * (coef[0] * p + coef[1] * c + coef[2] * l)

    owned = [patches[r : r + 1, :] for r in range(2)]
    spot = lax.broadcasted_iota(jnp.int32, (8, LANES), 0) * LANES + lane_of((8, LANES))
    spot = spot.astype(F32)
    start = half * C1
    totals = [jnp.zeros((C, LANES), F32) for _ in owned]
    small = [jnp.zeros((8, LANES), F32) for _ in owned]
    for v in range(n_wall):
        wall_s = wall_of(v)
        for j in range(n_len):
            ref = blocks[v * n_len + j]
            at_l = pl.ds(pl.multiple_of(length_of(j) * L, L), L)
            if compacted and v + j:
                for b in range(n_blk):
                    values = sheet[wall_s, b * C : (b + 1) * C, at_l]
                    ids = ref[96 + b * C : 96 + (b + 1) * C, :]
                    totals = [x + jnp.where(ids == e, values, 0.0) for x, e in zip(totals, owned)]
                small = [x + jnp.where(spot == e, ref[160:168, :], 0.0) for x, e in zip(small, owned)]
                continue

            def add(d, carry):
                big, little = carry
                values = sheet[wall_s, pl.ds(pl.multiple_of(blk_of(d) * C, C), C), at_l]
                ids = ref[d, start : start + C, :]
                parts = ref[d, start + C : start + C + 8, :]
                big = [x + jnp.where(ids == e, values, 0.0) for x, e in zip(big, owned)]
                little = [x + jnp.where(spot == e, parts, 0.0) for x, e in zip(little, owned)]
                return big, little

            totals, small = lax.fori_loop(0, n_blk, add, (totals, small), unroll=min(4, n_blk))
    factor = 1.0 / (2.0 * C * L / 2) ** 0.5
    for r in range(2):
        patch_grad[0, r] = (jnp.sum(totals[r]) + jnp.sum(small[r])) * factor
    for copy in copies:
        copy.wait()


def ring(x, axis, by):
    count = lax.axis_size(axis)
    return lax.ppermute(x, axis, [(i, (i + by) % count) for i in range(count)])


def paired(x, by):
    return lax.ppermute(x, "blk", [(i, i ^ by) for i in range(lax.axis_size("blk"))])


def neighbour_pairs(x, odd_first):
    count = lax.axis_size("blk")
    assert count % 2 == 0
    return lax.ppermute(x, "blk", [(i, (i + (1 if i % 2 == odd_first else -1)) % count) for i in range(count)])


def across(x):
    n_wall = lax.axis_size("wall")
    pairs = [(l * n_wall + w, (1 - l) * n_wall + (w + 1) % n_wall) for l in range(2) for w in range(n_wall)]
    return lax.ppermute(x, ("len", "wall"), pairs)


def call(kernel, ins, outs, scratch, name, work=0, room=48):
    places = {"vmem": pltpu.VMEM, "smem": pltpu.SMEM, "any": pl.ANY, "hbm": pltpu.HBM}

    def specs(kinds):
        return [pl.BlockSpec(memory_space=places[kind]) for kind in kinds]

    cost = pl.CostEstimate(flops=work, bytes_accessed=work, transcendentals=0) if work else None
    return pl.pallas_call(
        kernel,
        out_shape=[jax.ShapeDtypeStruct(shape, F32) for shape, _ in outs],
        in_specs=specs(ins),
        out_specs=specs(kind for _, kind in outs),
        scratch_shapes=[pltpu.VMEM(shape, F32) if isinstance(shape, tuple) else shape for shape in scratch],
        compiler_params=pltpu.CompilerParams(vmem_limit_bytes=int(room * 2**20)),
        cost_estimate=cost,
        name=name,
    )


def body(adj_next, ion_slope, misfit, tissue_mask, patch_ids, owner_map):
    W, C, L = adj_next.shape
    n_blk, n_len, n_wall = lax.axis_size("blk"), lax.axis_size("len"), lax.axis_size("wall")
    electrodes = owner_map.shape[0]
    assert L == LANES and H * W == LANES and n_wall == 2 and electrodes == 2 * n_blk * n_len * n_wall
    N = W + 2 * H
    n_dir = 1 if n_len == 2 else 2
    cells = W * C
    vmem = "vmem"
    field, own = (N * C, L), (cells, L)
    raw = [x.reshape(cells, L) for x in (adj_next, ion_slope, tissue_mask, misfit)]

    faces = call(
        functools.partial(pack_faces, n_len),
        ["hbm"] * 4,
        [(own, vmem)] * 4
        + [((C, L), vmem)] * n_dir
        + [((4, C, L), vmem)] * n_dir
        + [((sum(FACES), C, L), vmem)],
        [pltpu.VMEM(own, jnp.int32), pltpu.SemaphoreType.DMA((4, 4))],
        "faces",
        room=52.75,
    )(*raw)
    fields, corner_out, strip_out, wall_out = faces[:4], faces[4 : 4 + n_dir], faces[4 + n_dir : -1], faces[-1]
    if n_dir == 1:
        corners = [across(corner_out[0])]
        strips = [ring(strip_out[0], "len", 1)]
    else:
        strips = [ring(strip_out[1], "len", -1), ring(strip_out[0], "len", 1)]
        corners = [ring(ring(corner_out[1], "wall", 1), "len", -1), ring(ring(corner_out[0], "wall", 1), "len", 1)]
    wall_in = ring(wall_out, "wall", 1)

    near = (sum(near_rows(n_dir, W)[-1][::2]), L)
    halos = [*corners, *strips, wall_in]
    first_out, second_out, own_rows = call(
        functools.partial(boundary, n_len, C),
        [vmem] * (5 + 2 * n_dir),
        [(near, vmem)] * 2 + [((2, 6, N, L), vmem)],
        [(48, N, L), near, near],
        "boundary",
    )(*fields, *halos)
    first_in = neighbour_pairs(first_out, 1)
    second_in = neighbour_pairs(second_out, 0)
    qm, bm, be, coarse, surface, patches = call(
        functools.partial(sector, n_len, n_wall, C, electrodes),
        [vmem] * (6 + 2 * n_dir),
        [(field, vmem)] * 3 + [((cells // 8, L), vmem), ((C, L), vmem), ((8, L), vmem)],
        [field, (cells // 2, L)] + [field] * 8,
        "sector",
        work=16 * 10**6,
    )(*fields, *halos, owner_map.reshape(1, electrodes))

    rows = (8, N, L)
    wide = LANES * ((electrodes + LANES - 1) // LANES)
    message = (cells // 8 + C + 8, L)
    rows_n, rows_p, mine = call(
        functools.partial(correct, electrodes, n_len, n_wall),
        [vmem] * 6,
        [(rows, vmem), (rows, vmem), (message, vmem)],
        [(1, N, L), (wide, L), near, near],
        "correct",
    )(own_rows, first_in, second_in, coarse, surface, patch_ids)

    relative = n_blk in (2, 4)
    moved = [paired(mine, d) for d in range(1, n_blk)] if relative else [lax.all_gather(mine, "blk")]
    base_adj, base_pot = call(
        functools.partial(source_part, n_len, n_wall, C),
        [vmem] * 6,
        [(own, vmem), (own, vmem)],
        [field] * 4 + [(2, N, L)],
        "source_part",
        work=12 * 10**6,
    )(bm, be, rows_n, rows_p, qm, fields[2])
    moved, base_adj = lax.optimization_barrier((moved, base_adj))
    sector_blocks = jnp.stack([mine] + moved) if relative else moved[0]
    compacted = (n_blk, n_len, C, W) == (4, 2, 16, 32)
    if compacted:
        brief, across_wall = call(
            functools.partial(compact, C, W),
            [vmem],
            [((168, L), vmem), ((200, L), vmem)],
            [(W // 4, n_blk * C // 2, L), (W // 8 + 1, n_blk * C // 2, L)],
            "compact",
        )(sector_blocks)
        len_brief = ring(brief, "len", 1)
        blocks = [sector_blocks, len_brief, ring(across_wall, "wall", 1), ring(len_brief, "wall", 1), brief]
    elif n_len == 2:
        here = [sector_blocks, ring(sector_blocks, "len", 1)]
    else:
        gathered = lax.all_gather(sector_blocks, "len")
        here = [gathered[j] for j in range(n_len)]
    if not compacted:
        blocks = here + [ring(x, "wall", 1) for x in here]

    NC1, NL1 = n_blk * C // 2, n_len * L // 2
    planes = n_wall * W // 2
    grids = [(planes // k + 2, NC1, NL1) for k in (1, 1, 2, 2, 4, 4)]
    Q = W // 2 + 2
    tall = (Q * (C + 8) + 16, L)
    taller = ((W + 2) * (C + 8) + 16, L)
    scratch = grids + [(Q * C, NL1), tall, tall, taller, taller, own, own]
    scratch += [(2, n_blk * C, n_len * L), (2, 2, 64, L), pltpu.SemaphoreType.DMA((2, 4))]
    adj_prev, potential, patch_grad = call(
        functools.partial(solve, (n_blk, n_len, n_wall), relative, compacted, C, W),
        [vmem] * (len(blocks) + 4),
        [(own, "any"), (own, "any"), ((1, 2), "smem")],
        scratch,
        "solve",
        room=48 if NC1 * NL1 <= 4096 else 58,
    )(*blocks, base_adj, base_pot, fields[2], patches)
    return adj_prev.reshape(W, C, L), potential.reshape(W, C, L), patch_grad


def solution(mesh):
    field = P(("groups", "wall"), "blk", "len")
    return jax.shard_map(
        body,
        mesh=mesh,
        in_specs=(field, field, field, field, field, P("groups")),
        out_specs=(field, field, P(("groups", "blk", "len", "wall"), None)),
        check_vma=False,
    )
```

```python
import functools

import jax
import jax.numpy as jnp
from jax import lax
from jax.experimental import pallas as pl
from jax.experimental.pallas import tpu as pltpu
from jax.sharding import PartitionSpec as P

SI = (0.6, 1.0, 3.0)
SE = (0.8, 1.2, 2.0)
SHIFT = 0.002
OMEGA = 0.8
DT = 0.1
H = 4
LANES = 128
HIGHEST = lax.Precision.HIGHEST
F32 = jnp.float32


def level_coef(level):
    return tuple((SI[i] + SE[i]) / 4.0**level for i in range(3))


def level_diag(level):
    return SHIFT + 2.0 * sum(level_coef(level))


def level_step(level):
    return OMEGA / level_diag(level)


def lane_of(shape):
    return lax.broadcasted_iota(jnp.int32, shape, len(shape) - 1)


def before(m, e):
    first = lane_of(m.shape) == 0
    rm, re = pltpu.roll(m, 1, 1), pltpu.roll(e, 1, 1)
    return jnp.where(first, re, rm), jnp.where(first, rm, re)


def after(m, e):
    last = lane_of(m.shape) == LANES - 1
    rm, re = pltpu.roll(m, LANES - 1, 1), pltpu.roll(e, LANES - 1, 1)
    return jnp.where(last, re, rm), jnp.where(last, rm, re)


def beside_lanes(m, e):
    bm, be = before(m, e)
    am, ae = after(m, e)
    return bm + am, be + ae


def beside_lanes_main(m, e):
    lane = lane_of(m.shape)
    ends = lanes_at(e, LANES - 1 - lane)
    left = jnp.where(lane == 0, ends, pltpu.roll(m, 1, 1))
    right = jnp.where(lane == LANES - 1, ends, pltpu.roll(m, LANES - 1, 1))
    return left + right


def beside_rows(x, row_before, row_after):
    rows = x.shape[0]
    row = lax.broadcasted_iota(jnp.int32, x.shape, 0)
    low = jnp.where(row == 0, row_before, pltpu.roll(x, 1, 0))
    high = jnp.where(row == rows - 1, row_after, pltpu.roll(x, rows - 1, 0))
    return low + high


def beside_dense(x):
    return pltpu.roll(x, 1, 0) + pltpu.roll(x, x.shape[0] - 1, 0)


def plane(ref, i, rows):
    return ref[pl.ds(pl.multiple_of(i * rows, rows), rows), :]


def set_plane(ref, i, rows, value):
    ref[pl.ds(pl.multiple_of(i * rows, rows), rows), :] = value


def loop(low, high, step, unroll):
    def wrapped(i, carry):
        step(i)
        return carry

    if unroll >= high - low:
        for i in range(low, high):
            step(i)
        return
    lax.fori_loop(low, high, wrapped, 0, unroll=unroll)


FACES = (H, H - 1, H - 1, H - 2)


def face_planes(array):
    return FACES[array], sum(FACES[:array])


def pack_faces(n_len, adj, ion, mask, mis, *rest):
    n_dir = 1 if n_len == 2 else 2
    fields, wall_out, rest = rest[:4], rest[4], rest[5:]
    strips, corners = rest[:n_dir], rest[n_dir : 2 * n_dir]
    whole_mask, sems = rest[2 * n_dir :]
    cells = adj.shape[0]
    C = wall_out.shape[1]
    W = cells // C
    wall, length = lax.axis_index("wall"), lax.axis_index("len")
    targets = (fields[0], fields[1], whole_mask, fields[3])
    copies = []
    for a, (src, dst) in enumerate(zip((adj, ion, mask, mis), targets)):
        part = cells // 4
        for k in range(4):
            spot = pl.ds(k * part, part)
            copies.append(pltpu.make_async_copy(src.at[spot], dst.at[spot], sems.at[a, k]))
            copies[-1].start()

    base = jnp.where(wall == 0, W - H, 0)
    group = lane_of((C, LANES)) // H
    turns = [jnp.where(length == 0, H, 0)] if n_dir == 1 else [H, 0]
    corner = [jnp.zeros((C, LANES), F32) for _ in range(n_dir)]
    for a in (0, 1, 3, 2):
        for k in range(4):
            copies[4 * a + k].wait()
        if a == 2:
            fields[2][...] = whole_mask[...].astype(F32)
        ref = fields[a]
        strip = [jnp.zeros((C, LANES), F32) for _ in range(n_dir)]
        for w in range(W):
            value = ref[w * C : (w + 1) * C, :]
            for d in range(n_dir):
                turned = pltpu.roll(value, lax.rem(H * w + turns[d], LANES), 1)
                strip[d] = jnp.where(group == w, turned, strip[d])
        for d in range(n_dir):
            strips[d][a] = strip[d]
        count, first = face_planes(a)
        for p in range(count):
            face = plane(ref, base + jnp.where(wall == 0, H - count, 0) + p, C)
            wall_out[first + p] = face
            slot = first + p
            for d in range(n_dir):
                turned = pltpu.roll(face, lax.rem(H * slot + turns[d], LANES), 1)
                corner[d] = jnp.where(group == slot, turned, corner[d])
    for d in range(n_dir):
        corners[d][...] = corner[d]


def dense(ref, row, N, C):
    return ref[pl.ds(row, N, stride=C), :]


def dense_pair(m, e, row, N, C):
    return dense(m, row, N, C), dense(e, row, N, C)


def dense_apply(pair, inner, outer, coef):
    m, e = pair
    lm, le = beside_lanes(m, e)
    double = 2.0 * sum(coef)
    out = [double * m - coef[0] * beside_dense(m) - coef[2] * lm, double * e - coef[0] * beside_dense(e) - coef[2] * le]
    for row in (inner, outer):
        if row is not None:
            out = [out[k] - coef[1] * row[k] for k in range(2)]
    return out


def near_rows(n_dir, W):
    start, places = 8 * n_dir, []
    for reach in (0, 1, 2, 2, 3):
        places.append((start, H - reach, W + 2 * reach))
        start += W + 2 * reach
    assert start % 8 == 0
    return places


def rim_tiles(values):
    return [value[s : s + 8] for value in values for s in range(0, value.shape[0], 8)]


def rim_places(n_len, length):
    if n_len == 2:
        return [(jnp.where(length == 0, 0, LANES - H), True)]
    return [(0, length < n_len - 1), (LANES - H, length > 0)]


def boundary(n_len, C, *refs):
    n_dir = 1 if n_len == 2 else 2
    raw, wall_in, refs = refs[:4], refs[4], refs[5:]
    strips, corners, refs = refs[:n_dir], refs[n_dir : 2 * n_dir], refs[2 * n_dir :]
    first_out, second_out, own_rows, build, to_next, to_prev = refs
    W = raw[0].shape[0] // C
    N = W + 2 * H
    wall, length = lax.axis_index("wall"), lax.axis_index("len")
    places = rim_places(n_len, length)

    def strip_rows(packed, first, count):
        lane, k = lane_of((count, LANES)), lax.broadcasted_iota(jnp.int32, (count, LANES), 0)
        out = jnp.zeros((count, LANES), F32)
        for row, (off, ok) in zip(packed, places):
            j = lax.rem(lane - off + LANES, LANES)
            index = jnp.clip(H * (first + k) + j, 0, LANES - 1)
            taken = lanes_at(jnp.broadcast_to(row, (count, LANES)), index)
            out = jnp.where(jnp.logical_and(j < H, ok), taken, out)
        return out

    slots = iter(range(build.shape[0]))

    def assembled(own, halo, count):
        ref = build.at[next(slots)]
        ref[0:8, :] = jnp.zeros((8, LANES), F32)
        ref[N - 8 : N, :] = jnp.zeros((8, LANES), F32)
        ref[H : H + W, :] = own
        ref[H - count : H, :] = jnp.where(wall == 0, 0.0, halo)
        ref[H + W : H + W + count, :] = jnp.where(wall == 0, halo, 0.0)
        return ref[...]

    def row_of(a, r):
        count, first = face_planes(a)
        halo = jnp.concatenate([wall_in[first + p, r : r + 1, :] for p in range(count)], 0)
        m = assembled(raw[a][pl.ds(r, W, stride=C), :], halo, count)
        own = strip_rows([strip[a, r : r + 1, :] for strip in strips], 0, W)
        halo = strip_rows([corner[r : r + 1, :] for corner in corners], first, 8)[:count]
        return m, assembled(own, halo, count)

    length_shift = jnp.where(length == 0, 0, H) if n_dir == 1 else H
    group = lane_of((8, LANES)) // (H * n_dir)
    for side, (out, order) in enumerate(((to_next, (C - 1, C - 2, C - 3, C - 4)), (to_prev, (0, 1, 2, 3)))):
        adj = [row_of(0, r) for r in order]
        mask = [row_of(2, r) for r in order[:3]]
        q = []
        for k in range(3):
            ion = row_of(1, order[k])
            moved = dense_apply(adj[k], adj[k + 1], adj[k - 1] if k else None, SI)
            q.append([adj[k][j] - DT * mask[k][j] * (moved[j] + ion[j] * adj[k][j]) for j in range(2)])
        near = dense_apply(q[0], q[1], None, SI)
        mis = row_of(3, order[0])
        near = [near[j] + mis[j] for j in range(2)]
        second = dense_apply(q[1], q[2], q[0], SI)[0] + row_of(3, order[1])[0]
        for value, (start, first, count) in zip((second, near[0], q[0][0], mask[0][0], adj[0][0]), near_rows(n_dir, W)):
            out[start : start + count, :] = value[first : first + count]
        packs = [jnp.zeros((8, LANES), F32) for _ in range(n_dir)]
        for t, tile in enumerate(rim_tiles((near[1], q[0][1], mask[0][1], adj[0][1]))):
            k, at = divmod(t, LANES // (H * n_dir))
            turned = pltpu.roll(tile, lax.rem(length_shift + H * n_dir * at, LANES), 1)
            packs[k] = jnp.where(group == at, turned, packs[k])
        for k in range(n_dir):
            out[8 * k : 8 * k + 8, :] = packs[k]
        for k, pair in enumerate((adj[0], mask[0], q[0])):
            own_rows[side, 2 * k] = pair[0]
            own_rows[side, 2 * k + 1] = pair[1]
    even = lax.rem(lax.axis_index("blk"), 2) == 0
    first_out[...] = jnp.where(even, to_prev[...], to_next[...])
    second_out[...] = jnp.where(even, to_next[...], to_prev[...])


def spots(m_ref, e_ref, i, rows, coef):
    m, e = plane(m_ref, i, rows), plane(e_ref, i, rows)
    wm = plane(m_ref, i - 1, rows) + plane(m_ref, i + 1, rows)
    we = plane(e_ref, i - 1, rows) + plane(e_ref, i + 1, rows)
    lm, le = beside_lanes(m, e)
    cm, ce = beside_rows(m, 0.0, 0.0), beside_rows(e, 0.0, 0.0)
    double = 2.0 * sum(coef)
    dm = double * m - coef[0] * wm - coef[1] * cm - coef[2] * lm
    de = double * e - coef[0] * we - coef[1] * ce - coef[2] * le
    return m, e, dm, de


def rim_lanes(lane, length, n_len):
    return jnp.logical_or(
        jnp.logical_and(lane < H, length < n_len - 1),
        jnp.logical_and(lane >= LANES - H, length > 0),
    )


def inside(i, wall, W, n_wall):
    w = wall * W + i - H
    return jnp.logical_and(w >= 0, w < n_wall * W)


def lanes_at(x, index):
    return jnp.take_along_axis(x, index, axis=1, mode="promise_in_bounds")


def rows_at(x, index):
    return jnp.take_along_axis(x, index, axis=0, mode="promise_in_bounds")


def halved(low, high):
    lane = lane_of(low.shape)
    even = 2 * lane % LANES
    pairs = [lanes_at(x, even) + lanes_at(x, even + 1) for x in (low, high)]
    return 0.125 * jnp.where(lane < LANES // 2, pairs[0], pairs[1])


def precise(a, b):
    return jnp.dot(a, b, precision=HIGHEST, preferred_element_type=F32)


def assemble(n_len, C, raw, wall_in, strips, corners, xm, xe):
    W = raw[0].shape[0] // C
    N = W + 2 * H
    wall, length = lax.axis_index("wall"), lax.axis_index("len")
    lane = lane_of((C, LANES))
    places = rim_places(n_len, length)
    seen = [jnp.logical_and(lax.rem(lane - off + LANES, LANES) < H, ok) for off, ok in places]

    def rim(packed, base):
        out = jnp.zeros((C, LANES), F32)
        for row, ok, (off, _) in zip(packed, seen, places):
            out = jnp.where(ok, pltpu.roll(row, lax.rem(off - base + LANES, LANES), 1), out)
        return out

    zero = jnp.zeros((C, LANES), F32)
    last = N - H
    for a, own in enumerate(raw):
        packed = [strip[a] for strip in strips]
        for w in range(W):
            set_plane(xm[a], w + H, C, plane(own, w, C))
            set_plane(xe[a], w + H, C, rim(packed, H * w))
        packed = [corner[...] for corner in corners]
        for i in range(H):
            for at in (i, last + i):
                set_plane(xm[a], at, C, zero)
                set_plane(xe[a], at, C, zero)
        count, first = face_planes(a)
        here = jnp.where(wall == 0, last, H - count)
        for p in range(count):
            set_plane(xm[a], here + p, C, wall_in[first + p])
            set_plane(xe[a], here + p, C, rim(packed, H * (first + p)))


def sector(n_len, n_wall, C, electrodes, *refs):
    n_dir = 1 if n_len == 2 else 2
    raw, wall_in, refs = refs[:4], refs[4], refs[5:]
    strips, corners, refs = refs[:n_dir], refs[n_dir : 2 * n_dir], refs[2 * n_dir :]
    owner, qm, bm, be, coarse, surface, patches, qe, pairs = refs[:9]
    xm, xe = refs[9:13], refs[13:17]
    assemble(n_len, C, raw, wall_in, strips, corners, xm, xe)
    N = qm.shape[0] // C
    W = N - 2 * H
    wall, length = lax.axis_index("wall"), lax.axis_index("len")
    rim = rim_lanes(lane_of((C, LANES)), length, n_len)
    zero = jnp.zeros((C, LANES), F32)
    for i in (0, N - 1):
        set_plane(qm, i, C, zero)
        set_plane(qe, i, C, zero)
    for i in (0, 1, N - 2, N - 1):
        set_plane(bm, i, C, zero)
        set_plane(be, i, C, zero)

    def parabolic(i):
        m, e, dm, de = spots(xm[0], xe[0], i, C, SI)
        set_plane(qm, i, C, m - DT * plane(xm[2], i, C) * (dm + plane(xm[1], i, C) * m))
        set_plane(qe, i, C, e - DT * plane(xe[2], i, C) * (de + plane(xe[1], i, C) * e))

    loop(1, N - 1, parabolic, N)

    def elliptic_source(i):
        m, e, dm, de = spots(qm, qe, i, C, SI)
        ok = inside(i, wall, W, n_wall)
        set_plane(bm, i, C, jnp.where(ok, plane(xm[3], i, C) + dm, 0.0))
        set_plane(be, i, C, jnp.where(jnp.logical_and(rim, ok), plane(xe[3], i, C) + de, 0.0))

    loop(2, N - 2, elliptic_source, N)

    coef, k0 = level_coef(0), level_step(0)

    def left(i):
        m, e = plane(bm, i, C), plane(be, i, C)
        wm = plane(bm, i - 1, C) + plane(bm, i + 1, C)
        cm = beside_rows(m, 0.0, 0.0)
        lm = beside_lanes_main(m, e)
        return m, (1.0 - OMEGA) * m + k0 * (coef[0] * wm + coef[1] * cm + coef[2] * lm)

    def pair(q):
        i = 2 * q + H
        m, first = left(i)
        n, second = left(i + 1)
        set_plane(pairs, q, C, first + second)

        @pl.when(jnp.logical_and(q == 0, wall == 0))
        def _():
            surface[...] = k0 * (m + first)

        @pl.when(jnp.logical_and(q == W // 2 - 1, wall == n_wall - 1))
        def _():
            surface[...] = k0 * (n + second)

    loop(0, W // 2, pair, W)

    half = W * C // 8
    z = pairs[pl.ds(0, 2 * half, stride=2), :] + pairs[pl.ds(1, 2 * half, stride=2), :]
    coarse[...] = halved(z[:half], z[half:])

    blk = lax.axis_index("blk")
    me = (blk * n_len + length) * n_wall + wall
    which = lax.broadcasted_iota(jnp.int32, (1, electrodes), 1).astype(F32)
    mine = owner[...] == me
    patches[0:1, :] = jnp.full((1, LANES), jnp.min(jnp.where(mine, which, float(electrodes))))
    patches[1:2, :] = jnp.full((1, LANES), jnp.max(jnp.where(mine, which, -1.0)))
    patches[2:8, :] = jnp.zeros((6, LANES), F32)


def unpacked(ref, n_len, length, N):
    n_dir = 1 if n_len == 2 else 2
    mains = []
    for start, first, count in near_rows(n_dir, N - 2 * H):
        begin = min(start - first, ref.shape[0] - N)
        value = ref[begin : begin + N, :]
        behind = start - first - begin
        mains.append(pltpu.roll(value, N - behind, 0) if behind else value)
    rim = rim_lanes(lane_of((8, LANES)), length, n_len)
    shift = jnp.where(length == 0, 0, H) if n_dir == 1 else H
    rims = []
    for k in range(4):
        parts = []
        for s in range(N // 8):
            pack, at = divmod(k * (N // 8) + s, LANES // (H * n_dir))
            back = lax.rem(2 * LANES - shift - H * n_dir * at, LANES)
            parts.append(jnp.where(rim, pltpu.roll(ref[8 * pack : 8 * pack + 8, :], back, 1), 0.0))
        rims.append(jnp.concatenate(parts, 0))
    second, near, q, mask, adj = mains
    return (adj, rims[3]), (mask, rims[2]), (q, rims[1]), (near, rims[0]), second


def lateral(pair):
    return dense_apply(pair, None, None, SI)


def source_rows(own, other):
    adj_o, mask_o, q_o = own
    adj_n, mask_n, q_n, p_n, second_n = other
    step = DT * SI[1]
    delta_o = [step * mask_o[k] * adj_n[k] for k in range(2)]
    delta_n = [step * mask_n[k] * adj_o[k] for k in range(2)]
    lat_o, lat_n = lateral(delta_o), lateral(delta_n)
    near = [lat_o[k] - SI[1] * (q_n[k] + delta_n[k]) for k in range(2)]
    second = [-SI[1] * delta_o[k] for k in range(2)]
    halo = [p_n[k] + lat_n[k] - SI[1] * (q_o[k] + delta_o[k]) for k in range(2)]
    halo_second = second_n - SI[1] * delta_n[0]
    return near, second, halo, halo_second, delta_o[0]


def correct(electrodes, n_len, n_wall, own_rows, first_in, second_in, coarse, surface, ids, *rest):
    rows_n, rows_p, message = rest[:3]
    lines, sums, from_next, from_prev = rest[3:]
    even = lax.rem(lax.axis_index("blk"), 2) == 0
    from_next[...] = jnp.where(even, second_in[...], first_in[...])
    from_prev[...] = jnp.where(even, first_in[...], second_in[...])
    _, C, L = ids.shape
    N = own_rows.shape[2]
    W = N - 2 * H
    wall, length = lax.axis_index("wall"), lax.axis_index("len")
    ok_m = inside(lax.broadcasted_iota(jnp.int32, (N, LANES), 0), wall, W, n_wall)
    ok_e = jnp.logical_and(ok_m, rim_lanes(lane_of((N, LANES)), length, n_len))
    coef, k0 = level_coef(0), level_step(0)
    y = surface[...]
    row = lax.broadcasted_iota(jnp.int32, (C, LANES), 0)
    at = pl.ds(jnp.where(wall == 0, H, W + H - 1), 1)
    lows, highs = [], []
    W1, C1 = W // 2, C // 2
    for side, (other, out, order) in enumerate(
        ((from_next, rows_n, (C - 1, C - 2, C - 3)), (from_prev, rows_p, (0, 1, 2)))
    ):
        own = [(own_rows[side, 2 * k], own_rows[side, 2 * k + 1]) for k in range(3)]
        near, second, halo, halo_second, delta = source_rows(own, unpacked(other, n_len, length, N))
        near = [jnp.where(ok_m, near[0], 0.0), jnp.where(ok_e, near[1], 0.0)]
        second = [jnp.where(ok_m, second[0], 0.0), jnp.where(ok_e, second[1], 0.0)]
        out[0] = halo_m = jnp.where(ok_m, halo[0], 0.0)
        out[1] = jnp.where(ok_e, halo[1], 0.0)
        out[2] = jnp.where(ok_m, halo_second, 0.0)
        out[3] = delta
        out[4], out[5] = near
        out[6], out[7] = second

        def turned(pair, beside):
            m, e = pair
            return (1.0 - OMEGA) * m + k0 * (
                coef[0] * beside_dense(m) + coef[2] * beside_lanes_main(m, e) + coef[1] * beside
            )

        first = turned(near, second[0] + halo_m)
        next_one = turned(second, near[0])
        third = k0 * coef[1] * second[0]
        for k, change in enumerate((near[0] + first, second[0] + next_one, third)):
            lines[0] = change
            y = y + jnp.where(row == order[k], k0 * lines[0, at, :], 0.0)
        for change in (first + next_one, third):
            lines[0] = change
            both = lines[0, pl.ds(H, W1, stride=2), :] + lines[0, pl.ds(H + 1, W1, stride=2), :]
            lows.append(both[: W1 // 2])
            highs.append(both[W1 // 2 :])
    add = halved(jnp.concatenate(lows, 0), jnp.concatenate(highs, 0))
    half = W * C // 8
    message[0:half, :] = coarse[...]
    for k, c1 in enumerate((C1 - 1, C1 - 2, 0, 1)):
        spot = pl.ds(c1, W1 // 2, stride=C1)
        message[spot, :] = message[spot, :] + add[k * (W1 // 2) : (k + 1) * (W1 // 2)]
    patch = ids[0]
    message[half : half + C, :] = patch.astype(F32)
    wide = sums.shape[0]
    if wide > electrodes:
        sums[...] = jnp.zeros(sums.shape, F32)

    def one(e):
        sums[pl.ds(e, 1), :] = jnp.sum(jnp.where(patch == e, y, 0.0), axis=0, keepdims=True)

    loop(0, electrodes, one, 32 if electrodes <= 32 else 8)
    totals = lax.dot_general(
        jnp.ones((8, LANES), F32), sums[...], (((1,), (1,)), ((), ())), precision=HIGHEST, preferred_element_type=F32
    )
    for t in range(wide // LANES):
        message[half + C + t : half + C + t + 1, :] = totals[0:1, t * LANES : (t + 1) * LANES]


def source_part(n_len, n_wall, C, bm, be, rows_n, rows_p, qm, mask, base_adj, base_pot, fm, fe, tm, te, hp):
    N = bm.shape[0] // C
    W = N - 2 * H
    length, wall = lax.axis_index("len"), lax.axis_index("wall")
    fm[...] = bm[...]
    fe[...] = be[...]
    for rows, near, second in ((rows_n, C - 1, C - 2), (rows_p, 0, 1)):
        for k, at in ((4, near), (6, second)):
            spot = pl.ds(at, N, stride=C)
            fm[spot, :] = fm[spot, :] + rows[k]
            fe[spot, :] = fe[spot, :] + rows[k + 1]
    coef, k0 = level_coef(0), level_step(0)
    rim = rim_lanes(lane_of((C, LANES)), length, n_len)

    def part(i):
        m, e = plane(fm, i, C), plane(fe, i, C)
        wm = plane(fm, i - 1, C) + plane(fm, i + 1, C)
        we = plane(fe, i - 1, C) + plane(fe, i + 1, C)
        lm, le = beside_lanes(m, e)
        at = pl.ds(i, 1)
        cm = beside_rows(m, rows_p[0, at, :], rows_n[0, at, :])
        ce = beside_rows(e, rows_p[1, at, :], rows_n[1, at, :])
        pm = k0 * ((2.0 - OMEGA) * m + k0 * (coef[0] * wm + coef[1] * cm + coef[2] * lm))
        pe = k0 * ((2.0 - OMEGA) * e + k0 * (coef[0] * we + coef[1] * ce + coef[2] * le))
        set_plane(tm, i, C, jnp.where(inside(i, wall, W, n_wall), pm, 0.0))
        set_plane(te, i, C, jnp.where(rim, pe, 0.0))

    loop(H - 1, N - H + 1, part, N)
    for side, (rows, at) in enumerate(((rows_n, C - 1), (rows_p, 0))):
        m = rows[0]
        total = (
            coef[0] * beside_dense(m)
            + coef[1] * (rows[2] + dense(fm, at, N, C))
            + coef[2] * beside_lanes_main(m, rows[1])
        )
        hp[side] = k0 * ((2.0 - OMEGA) * m + k0 * total)
    row = lax.broadcasted_iota(jnp.int32, (C, LANES), 0)

    def finish(w):
        i = w + H
        m, e = plane(tm, i, C), plane(te, i, C)
        at = pl.ds(i, 1)
        wm = plane(tm, i - 1, C) + plane(tm, i + 1, C)
        cm = beside_rows(m, hp[1, at, :], hp[0, at, :])
        lm = beside_lanes_main(m, e)
        lam = plane(qm, i, C)
        lam = lam + jnp.where(row == C - 1, rows_n[3, at, :], 0.0) + jnp.where(row == 0, rows_p[3, at, :], 0.0)
        moved = 2.0 * sum(SI) * m - SI[0] * wm - SI[1] * cm - SI[2] * lm
        set_plane(base_adj, w, C, lam - DT * plane(mask, w, C) * moved)
        set_plane(base_pot, w, C, m)

    loop(0, W, finish, W)


def halves(shape):
    lane = lane_of(shape)
    return lane, lane % (LANES // 2)


def compact(C, W, blocks, out, wall_out, sheet1, coarse2):
    n_blk = blocks.shape[0]
    W1, C1 = W // 2, C // 2
    half, start, middle = W1 // 2, W1 // 2 * C1, LANES // 2
    blk, length, wall = lax.axis_index("blk"), lax.axis_index("len"), lax.axis_index("wall")
    sums = jnp.zeros((1, LANES), F32)
    for d in range(n_blk):
        b = blk ^ d
        for i in range(half):
            sheet1[i, pl.ds(pl.multiple_of(C1 * b, C1), C1), :] = blocks[d, i * C1 : (i + 1) * C1, :]
        out[pl.ds(pl.multiple_of(96 + C * b, C), C), :] = blocks[d, start : start + C, :]
        sums = sums + blocks[d, start + C : start + C + 1, :]
    out[160:168, :] = jnp.zeros((8, LANES), F32)
    out[160:161, :] = sums
    NC1 = sheet1.shape[1]
    lane, at = halves((NC1, LANES))
    low = lane < middle
    coef, k1 = level_coef(1), level_step(1)
    ends = pltpu.roll(sheet1[half - 1], middle, 1), pltpu.roll(sheet1[0], middle, 1)
    for q in range(half // 2):
        both = sheet1[2 * q] + sheet1[2 * q + 1]
        prev = sheet1[2 * q - 1] if q else jnp.where(low, 0.0, ends[0])
        after_it = sheet1[2 * q + 2] if 2 * q + 2 < half else jnp.where(low, ends[1], 0.0)
        c = pltpu.roll(both, 1, 0) + pltpu.roll(both, NC1 - 1, 0)
        l = jnp.where(at == 0, 0.0, pltpu.roll(both, 1, 1)) + jnp.where(
            at == middle - 1, 0.0, pltpu.roll(both, LANES - 1, 1)
        )
        left = (1.0 - OMEGA) * both + k1 * (coef[0] * (prev + both + after_it) + coef[1] * c + coef[2] * l)
        coarse2[q] = 0.125 * twins(left, 1)
    coarse2[half // 2] = 0.125 * twins(jnp.where(wall == 0, sheet1[half - 1], sheet1[0]), 1)
    rows2 = NC1 // 2
    lane2, at2 = halves((rows2, LANES))
    pick = lane2 - at2 + 2 * (at2 % (middle // 2))
    for p in range(half // 4):
        pair = [lanes_at(coarse2[2 * p + k, pl.ds(0, rows2, stride=2), :], pick) for k in range(2)]
        out[rows2 * p : rows2 * (p + 1), :] = jnp.where(at2 < middle // 2, pair[0], pair[1])
    beside = jnp.zeros((NC1, LANES), F32)
    base = jnp.where(length == 0, middle - H, 0)
    for i in range(half):
        turned = pltpu.roll(sheet1[i], lax.rem(H * i - base + LANES, LANES), 1)
        beside = jnp.where(at // H == i, turned, beside)
    index = lax.broadcasted_iota(jnp.int32, (8, LANES), 0) ^ 1
    line = beside + jnp.concatenate([rows_at(beside[t : t + 8], index) for t in range(0, NC1, 8)], 0)
    line = 0.125 * (line + pltpu.roll(line, LANES - H, 1))
    m = lane - 96
    spot = jnp.where(m < H, 8 * m, middle + 8 * (m - H)) + jnp.where(length == 0, H - 1, 0)
    line = lanes_at(line, jnp.clip(spot, 0, LANES - 1))
    beside = jnp.where(jnp.logical_and(m >= 0, m < 8), line, beside)
    out[32 : 32 + NC1, :] = beside
    face = coarse2[half // 2, pl.ds(0, rows2, stride=2), :]
    face = lanes_at(face, jnp.where(wall == 0, middle, 0) + 2 * (at2 % (middle // 2)))
    inner = jnp.logical_and(lane2 >= middle // 2, lane2 < middle)
    out[32 : 32 + rows2, :] = jnp.where(inner, face, beside[:rows2])
    inner_surface = jnp.where(low, sheet1[0], pltpu.roll(sheet1[1], middle, 1))
    outer_surface = jnp.where(low, pltpu.roll(sheet1[half - 2], middle, 1), sheet1[half - 1])
    out[64 : 64 + NC1, :] = jnp.where(wall == 0, inner_surface, outer_surface)
    wall_out[0:168, :] = out[...]
    last = jnp.where(low, pltpu.roll(sheet1[half - 1], middle, 1), sheet1[half - 2])
    wall_out[168 : 168 + NC1, :] = jnp.where(wall == 0, last, inner_surface)


def around(x, by):
    rows, lanes = x.shape
    lane = lane_of(x.shape)
    c = pltpu.roll(x, by, 0) + pltpu.roll(x, rows - by, 0)
    l = jnp.where(lane < by, 0.0, pltpu.roll(x, by, 1)) + jnp.where(
        lane >= lanes - by, 0.0, pltpu.roll(x, lanes - by, 1)
    )
    return c, l


def twins(x, by):
    rows, lanes = x.shape
    if lanes == LANES:
        index = lax.broadcasted_iota(jnp.int32, (8, LANES), 0) ^ by
        x = x + jnp.concatenate([rows_at(x[t : t + 8], index) for t in range(0, rows, 8)], 0)
        return x + lanes_at(x, lane_of(x.shape) ^ by)
    row = lax.broadcasted_iota(jnp.int32, x.shape, 0)
    lane = lane_of(x.shape)
    x = x + jnp.where((row & by) == 0, pltpu.roll(x, rows - by, 0), pltpu.roll(x, by, 0))
    return x + jnp.where((lane & by) == 0, pltpu.roll(x, lanes - by, 1), pltpu.roll(x, by, 1))


def solve(sizes, relative, compacted, C, W, *refs):
    n_blk, n_len, n_wall = sizes
    count = n_len * n_wall + compacted
    blocks, refs = refs[:count], refs[count:]
    base_adj, base_pot, mask, patches, adj_prev, potential, patch_grad = refs[:7]
    b1, x1, b2, x2, b3, x3, near, pm, pe, tm, te, adj_out, pot_out, sheet, briefs, sems = refs[7:]
    L = LANES
    W1, C1 = W // 2, C // 2
    planes, NC1, NL1 = b1.shape
    planes -= 2
    blk, length, wall = lax.axis_index("blk"), lax.axis_index("len"), lax.axis_index("wall")
    half = W1 // 2
    middle = LANES // 2
    lane8 = lane_of((C1, LANES))
    often = 40 if NC1 * NL1 <= 4096 else 1

    def blk_of(d):
        return blk ^ d if relative else d

    def length_of(j):
        return (length + j) % n_len if n_len == 2 else j

    def wall_of(v):
        return (wall + v) % n_wall

    zero1 = jnp.zeros((NC1, NL1), F32)
    for ref in (b1, x1, b2, x2, b3, x3):
        ref[0] = zero1
        ref[ref.shape[0] - 1] = zero1

    if not compacted:
        for v in range(n_wall):
            wall_s = wall_of(v)
            mine = blocks[v * n_len : (v + 1) * n_len]

            def unpack(d):
                at = pl.ds(pl.multiple_of(C1 * blk_of(d), C1), C1)
                for t in range(n_len // 2):
                    one, two = mine[2 * t], mine[2 * t + 1]
                    for i in range(half):
                        a, b = one[d, i * C1 : (i + 1) * C1, :], two[d, i * C1 : (i + 1) * C1, :]
                        if n_len == 2:
                            a, b = jnp.where(length == 0, a, b), jnp.where(length == 0, b, a)
                        spot = 1 + wall_s * W1 + i
                        lanes = slice(t * LANES, (t + 1) * LANES)
                        b1[spot, at, lanes] = jnp.where(lane8 < middle, a, pltpu.roll(b, middle, 1))
                        b1[spot + half, at, lanes] = jnp.where(lane8 < middle, pltpu.roll(a, middle, 1), b)

            loop(0, n_blk, unpack, 4)
    if compacted:
        stack, len_brief, wall_brief, both_brief, own_brief = blocks
        lane8 = lane_of((C1, LANES))
        here8 = lane8 // middle == length
        here = lane_of((NC1, LANES)) // middle == length
        face_lane = jnp.where(length == 0, middle, middle - H)
        near8 = jnp.logical_and(lane8 >= face_lane, lane8 < face_lane + H)
        at_face = jnp.logical_and(lane_of((NC1, LANES)) >= face_lane, lane_of((NC1, LANES)) < face_lane + H)
        for d in range(n_blk):
            row = pl.multiple_of(C1 * blk_of(d), C1)
            beside = len_brief[pl.ds(32 + row, C1), :]
            for i in range(half):
                a = stack[d, i * C1 : (i + 1) * C1, :]
                b = pltpu.roll(a, middle, 1)
                for k, value in enumerate((jnp.where(length == 0, a, b), jnp.where(length == 0, b, a))):
                    turn = lax.rem(face_lane - H * i - middle * k + 2 * LANES, LANES)
                    rest = jnp.where(near8, pltpu.roll(beside, turn, 1), 0.0)
                    b1[1 + wall * W1 + i + half * k, pl.ds(row, C1), :] = jnp.where(here8, value, rest)

        def two_planes(tile):
            turned = pltpu.roll(tile, middle, 1)
            return jnp.where(length == 0, tile, turned), jnp.where(length == 0, turned, tile)

        beyond = two_planes(wall_brief[168 : 168 + NC1, :])
        beside = both_brief[32 : 32 + NC1, :]
        for k in range(2):
            off = jnp.where(wall == 0, H * k, middle + H * (half - 1 - k))
            rest = jnp.where(at_face, pltpu.roll(beside, lax.rem(face_lane - off + 2 * LANES, LANES), 1), 0.0)
            b1[jnp.where(wall == 0, 1 + W1 + k, W1 - k)] = jnp.where(here, beyond[k], rest)
        for k in range(2):
            theirs = two_planes(len_brief[64 : 64 + NC1, :])[1 - k]
            spot = jnp.where(wall == 0, 1, planes - 1) + k
            b1[spot] = jnp.where(here, b1[spot], theirs)
            ours = two_planes(wall_brief[64 : 64 + NC1, :])[k]
            theirs = two_planes(both_brief[64 : 64 + NC1, :])[1 - k]
            b1[jnp.where(wall == 0, planes - 1, 1) + k] = jnp.where(here, ours, theirs)
        first_half = length == 0
        for k in range(2):
            ours = jnp.where(wall == k, own_brief[0:64, :], wall_brief[0:64, :])
            theirs = jnp.where(wall == k, len_brief[0:64, :], both_brief[0:64, :])
            briefs[0, k] = jnp.where(first_half, ours, theirs)
            briefs[1, k] = jnp.where(first_half, theirs, ours)
        lane_8 = lane_of((8, LANES))
        quarter = middle // 2
        left_quarter = lane_8 % middle < quarter
        pairs_index = [lane_8 // 2, middle + lane_8 // 2]
        facing = jnp.logical_and(lane_8 >= middle - 2, lane_8 < middle + 2)
        coef1 = [level_step(1) * x for x in level_coef(1)]
        rows2 = NC1 // 2

        def merged(w, start):
            one, two = briefs[0, w, start : start + 8, :], briefs[1, w, start : start + 8, :]
            even = jnp.where(left_quarter, one, pltpu.roll(two, quarter, 1))
            odd = jnp.where(left_quarter, pltpu.roll(one, LANES - quarter, 1), two)
            return even, odd

        for w in range(n_wall):
            for t in range(rows2 // 8):
                lines = [briefs[h, w, pl.ds(32 + 16 * t, 8, stride=2), :] for h in range(2)]
                lines = [lanes_at(x, jnp.minimum(96 + lane_8 // 4, LANES - 1)) for x in lines]
                lines = coef1[2] * jnp.where(lane_8 % 4 < 2, lines[1], lines[0])
                for p in range(half // 4):
                    tiles = merged(w, rows2 * p + 8 * t)
                    for odd in range(2):
                        for high in range(2):
                            k = 2 * p + odd + half // 2 * high
                            value = lanes_at(tiles[odd], pairs_index[high])
                            line = pltpu.roll(lines, middle - 2 - 4 * k, 1)
                            value = value + jnp.where(facing, line, 0.0)
                            if k == (half - 1 if w == 0 else 0):
                                value = value + coef1[0] * lanes_at(merged(1 - w, 32 + 8 * t)[1], pairs_index[0])
                            for r in range(2):
                                b2[1 + w * half + k, pl.ds(16 * t + r, 8, stride=2), :] = value

    def total_of(x, wsum, level, by):
        coef = level_coef(level)
        c, l = around(x, by)
        return level_step(level) * (coef[0] * wsum + coef[1] * c + coef[2] * l)

    def left_pair(ref, i, level):
        both = ref[i] + ref[i + 1]
        return (1.0 - OMEGA) * both + total_of(both, ref[i - 1] + both + ref[i + 2], level, 2 ** (level - 1))

    def sweep(x_ref, b_ref, i, level):
        x = x_ref[i]
        total = total_of(x, x_ref[i - 1] + x_ref[i + 1], level, 2 ** (level - 1))
        return (1.0 - OMEGA) * x + level_step(level) * b_ref[i] + total

    def down1(q):
        b2[1 + q] = 0.125 * twins(left_pair(b1, 2 * q + 1, 1), 1)

    if not compacted:
        loop(0, planes // 2, down1, often)

    def down2(q):
        b3[1 + q] = 0.125 * twins(left_pair(b2, 2 * q + 1, 2), 2)

    loop(0, planes // 4, down2, often)

    deep = planes // 4
    k3 = level_step(3)

    x2[1 + deep] = zero1

    def start3(q):
        b = b3[1 + q]
        x2[1 + q] = k3 * ((2.0 - OMEGA) * b + total_of(b, b3[q] + b3[2 + q], 3, 4))

    loop(0, deep, start3, often)

    def sweep3(q):
        x3[1 + q] = sweep(x2, b3, 1 + q, 3)

    loop(0, deep, sweep3, often)
    k2 = level_step(2)

    def up2(q):
        coarse = x3[1 + q]
        x2[1 + 2 * q] = k2 * b2[1 + 2 * q] + coarse
        x2[2 + 2 * q] = k2 * b2[2 + 2 * q] + coarse

    loop(0, planes // 4, up2, often)

    k1 = level_step(1)

    def up1(q):
        fine = sweep(x2, b2, 1 + q, 2)
        x1[1 + 2 * q] = k1 * b1[1 + 2 * q] + fine
        x1[2 + 2 * q] = k1 * b1[2 + 2 * q] + fine

    if compacted:
        loop(0, half, lambda q: up1(half * wall + q), often)
        up1(half - wall)
        up1((planes // 2 - 1) * (1 - wall))
    else:
        loop(0, planes // 2, up1, often)

    Q = W1 + 2
    sectors = (blk, lax.rem(blk + 1, n_blk), lax.rem(blk + n_blk - 1, n_blk))
    spots3 = [pl.ds(pl.multiple_of(s * C1, C1), C1) for s in sectors]
    row8 = lax.broadcasted_iota(jnp.int32, (C1, NL1), 0)

    def three(ref, i):
        return jnp.concatenate([ref[i, s, :] for s in spots3], 0)

    def finish1(q):
        i = wall * W1 + q
        x = three(x1, i)
        wsum = three(x1, jnp.maximum(i - 1, 0)) + three(x1, jnp.minimum(i + 1, planes + 1))
        value = (1.0 - OMEGA) * x + k1 * three(b1, i) + total_of(x, wsum, 1, 1)
        value = jnp.where(jnp.logical_and(i >= 1, i <= planes), value, 0.0)
        set_plane(near, 2 * q, C1, value[:C1])
        set_plane(near, 2 * q + 1, C1, jnp.where(row8 < 2, value[C1 : 2 * C1], value[2 * C1 :]))

    loop(0, Q, finish1, often)

    first = length * middle
    R = C + 8
    row8 = lax.broadcasted_iota(jnp.int32, (8, LANES), 0)
    tile_lane = lane_of((8, LANES))
    at_e = jnp.where(tile_lane < H, middle + tile_lane // 2, tile_lane // 2 - middle)
    rim8 = rim_lanes(tile_lane, length, n_len)
    if NL1 == LANES:
        index_m, index_e = first + tile_lane // 2, jnp.clip(first + at_e, 0, LANES - 1)

        def spread(tile):
            return lanes_at(tile, index_m), jnp.where(rim8, lanes_at(tile, index_e), 0.0)

    else:
        source = lax.broadcasted_iota(jnp.int32, (NL1, LANES), 0)
        lane = lane_of((NL1, LANES))
        at_all = jnp.where(lane < H, middle + lane // 2, jnp.where(lane >= LANES - H, lane // 2 - middle, 4 * NL1))
        take_m = jnp.where(source == first + lane // 2, 1.0, 0.0).astype(F32)
        take_e = jnp.where(source == first + at_all, 1.0, 0.0).astype(F32)

        def spread(tile):
            return precise(tile, take_m), precise(tile, take_e)

    picks = (row8 // 2, H + row8 // 2)
    ends = jnp.where(row8 < H, 6 + row8 // 2, row8 // 2 - 2)

    def fine_rows(q):
        own = spread(plane(near, 2 * q, C1))
        beside = spread(plane(near, 2 * q + 1, C1))
        for out, a, b in ((pm, own[0], beside[0]), (pe, own[1], beside[1])):
            parts = (jnp.where(row8 < 6, a, b), a, jnp.where(row8 < 2, b, a))
            index = (ends, 2 + row8 // 2, ends)
            for k in range(3):
                out[pl.ds(pl.multiple_of(8 + R * q + 8 * k, 8), 8), :] = rows_at(parts[k], index[k])

    loop(0, Q, fine_rows, often)
    for ref in (pm, pe):
        ref[0:8, :] = jnp.zeros((8, LANES), F32)
        ref[8 + R * Q : 16 + R * Q, :] = jnp.zeros((8, LANES), F32)
    coef, k0 = level_coef(0), level_step(0)
    def fine(ref, t, by=0, count=R):
        return ref[pl.ds(8 + R * t + by, count), :]

    def coarse_terms(q):
        out = []
        sides = beside_lanes(fine(pm, q), fine(pe, q))
        for ref, l in zip((pm, pe), sides):
            x = fine(ref, q)
            c = fine(ref, q, -1) + fine(ref, q, 1)
            out.append((1.0 - OMEGA) * x + k0 * (coef[0] * x + coef[1] * c + coef[2] * l))
        return out

    ks = k0 * coef[0]

    def set_fine(ref, t, value):
        ref[pl.ds(pl.multiple_of(8 + R * t, 8), R), :] = value

    def put_end(t, q, other, ok):
        set_fine(tm, t, jnp.where(ok, coarse_terms(q)[0] + ks * fine(pm, other), 0.0))

    put_end(0, 0, 1, wall > 0)
    put_end(W + 1, Q - 1, Q - 2, wall < n_wall - 1)
    rim = rim_lanes(lane_of((R, LANES)), length, n_len)

    def level0(q):
        gm, ge = coarse_terms(q)
        for t, other in ((2 * q - 1, q - 1), (2 * q, q + 1)):
            set_fine(tm, t, gm + ks * fine(pm, other))
            set_fine(te, t, jnp.where(rim, ge + ks * fine(pe, other), 0.0))

    loop(1, 1 + W1, level0, often)

    def finish0(w):
        t = w + 1
        m, e = fine(tm, t, H, C), fine(te, t, H, C)
        cm = fine(tm, t, H - 1, C) + fine(tm, t, H + 1, C)
        wm = fine(tm, t - 1, H, C) + fine(tm, t + 1, H, C)
        lm = beside_lanes_main(m, e)
        moved = 2.0 * sum(SI) * m - SI[0] * wm - SI[1] * cm - SI[2] * lm
        set_plane(adj_out, w, C, plane(base_adj, w, C) - DT * plane(mask, w, C) * moved)
        set_plane(pot_out, w, C, plane(base_pot, w, C) + m)

    parts = 2
    size = W // parts
    copies = []
    for k in range(parts):
        loop(k * size, (k + 1) * size, finish0, often)
        spot = pl.ds(k * size * C, size * C)
        for n, (src, dst) in enumerate(((adj_out, adj_prev), (pot_out, potential))):
            copies.append(pltpu.make_async_copy(src.at[spot], dst.at[spot], sems.at[n, k]))
            copies[-1].start()

    NC, NL = sheet.shape[1:]

    def whole_fine(x):
        if NL1 == LANES:
            parts = []
            for t in range(0, NC1, 8):
                wide8 = [lanes_at(x[t : t + 8], tile_lane // 2 + k * middle) for k in range(2)]
                for pick in picks[:2]:
                    parts.append(jnp.concatenate([rows_at(v, pick) for v in wide8], 1))
            return jnp.concatenate(parts, 0)
        along_c = lax.broadcasted_iota(jnp.int32, (NC, NC1), 0) // 2
        along_l = lax.broadcasted_iota(jnp.int32, (NL1, NL), 1) // 2
        twice_c = jnp.where(along_c == lax.broadcasted_iota(jnp.int32, (NC, NC1), 1), 1.0, 0.0).astype(F32)
        twice_l = jnp.where(along_l == lax.broadcasted_iota(jnp.int32, (NL1, NL), 0), 1.0, 0.0).astype(F32)
        return precise(precise(twice_c, x), twice_l)

    for s, i in enumerate((1, planes)):
        p = whole_fine(sweep(x1, b1, i, 1))
        c, l = around(p, 1)
        sheet[s] = (1.0 - OMEGA) * p + k0 * (coef[0] * p + coef[1] * c + coef[2] * l)

    owned = [patches[r : r + 1, :] for r in range(2)]
    spot = lax.broadcasted_iota(jnp.int32, (8, LANES), 0) * LANES + lane_of((8, LANES))
    spot = spot.astype(F32)
    start = half * C1
    totals = [jnp.zeros((C, LANES), F32) for _ in owned]
    small = [jnp.zeros((8, LANES), F32) for _ in owned]
    lines = blocks[0].shape[1] - start - C
    thin = [jnp.zeros((lines, LANES), F32) for _ in owned]
    for v in range(n_wall):
        wall_s = wall_of(v)
        for j in range(n_len):
            ref = blocks[v * n_len + j]
            at_l = pl.ds(pl.multiple_of(length_of(j) * L, L), L)
            if compacted and v + j:
                for b in range(n_blk):
                    values = sheet[wall_s, b * C : (b + 1) * C, at_l]
                    ids = ref[96 + b * C : 96 + (b + 1) * C, :]
                    totals = [x + jnp.where(ids == e, values, 0.0) for x, e in zip(totals, owned)]
                small = [x + jnp.where(spot == e, ref[160:168, :], 0.0) for x, e in zip(small, owned)]
                continue

            def add(d, carry):
                big, little = carry
                values = sheet[wall_s, pl.ds(pl.multiple_of(blk_of(d) * C, C), C), at_l]
                ids = ref[d, start : start + C, :]
                parts = ref[d, start + C : start + C + lines, :]
                big = [x + jnp.where(ids == e, values, 0.0) for x, e in zip(big, owned)]
                little = [x + jnp.where(spot[:lines] == e, parts, 0.0) for x, e in zip(little, owned)]
                return big, little

            totals, thin = lax.fori_loop(0, n_blk, add, (totals, thin), unroll=min(4, n_blk))
    factor = 1.0 / (2.0 * C * L / 2) ** 0.5
    for r in range(2):
        patch_grad[0, r] = (jnp.sum(totals[r]) + jnp.sum(small[r]) + jnp.sum(thin[r])) * factor
    for copy in copies:
        copy.wait()


def ring(x, axis, by):
    count = lax.axis_size(axis)
    return lax.ppermute(x, axis, [(i, (i + by) % count) for i in range(count)])


def paired(x, by):
    return lax.ppermute(x, "blk", [(i, i ^ by) for i in range(lax.axis_size("blk"))])


def neighbour_pairs(x, odd_first):
    count = lax.axis_size("blk")
    assert count % 2 == 0
    return lax.ppermute(x, "blk", [(i, (i + (1 if i % 2 == odd_first else -1)) % count) for i in range(count)])


def across(x):
    n_wall = lax.axis_size("wall")
    pairs = [(l * n_wall + w, (1 - l) * n_wall + (w + 1) % n_wall) for l in range(2) for w in range(n_wall)]
    return lax.ppermute(x, ("len", "wall"), pairs)


def call(kernel, ins, outs, scratch, name, work=0, room=48):
    places = {"vmem": pltpu.VMEM, "smem": pltpu.SMEM, "any": pl.ANY, "hbm": pltpu.HBM}

    def specs(kinds):
        return [pl.BlockSpec(memory_space=places[kind]) for kind in kinds]

    cost = pl.CostEstimate(flops=work, bytes_accessed=work, transcendentals=0) if work else None
    return pl.pallas_call(
        kernel,
        out_shape=[jax.ShapeDtypeStruct(shape, F32) for shape, _ in outs],
        in_specs=specs(ins),
        out_specs=specs(kind for _, kind in outs),
        scratch_shapes=[pltpu.VMEM(shape, F32) if isinstance(shape, tuple) else shape for shape in scratch],
        compiler_params=pltpu.CompilerParams(vmem_limit_bytes=int(room * 2**20)),
        cost_estimate=cost,
        name=name,
    )


def body(adj_next, ion_slope, misfit, tissue_mask, patch_ids, owner_map):
    W, C, L = adj_next.shape
    n_blk, n_len, n_wall = lax.axis_size("blk"), lax.axis_size("len"), lax.axis_size("wall")
    electrodes = owner_map.shape[0]
    assert L == LANES and H * W == LANES and n_wall == 2 and electrodes == 2 * n_blk * n_len * n_wall
    N = W + 2 * H
    n_dir = 1 if n_len == 2 else 2
    cells = W * C
    vmem = "vmem"
    field, own = (N * C, L), (cells, L)
    raw = [x.reshape(cells, L) for x in (adj_next, ion_slope, tissue_mask, misfit)]

    *fields, wall_out = (faces := call(
        functools.partial(pack_faces, n_len),
        ["hbm"] * 4,
        [(own, vmem)] * 4
        + [((sum(FACES), C, L), vmem)]
        + [((4, C, L), vmem)] * n_dir
        + [((C, L), vmem)] * n_dir,
        [pltpu.VMEM(own, jnp.int32), pltpu.SemaphoreType.DMA((4, 4))],
        "faces",
        room=52.75,
    )(*raw))[:5]
    strip_out, corner_out = faces[5 : 5 + n_dir], faces[5 + n_dir :]
    wall_in = ring(wall_out, "wall", 1)
    if n_dir == 1:
        strips = [ring(strip_out[0], "len", 1)]
        corners = [across(corner_out[0])]
    else:
        strips = [ring(strip_out[1], "len", -1), ring(strip_out[0], "len", 1)]
        corners = [ring(ring(corner_out[1], "wall", 1), "len", -1), ring(ring(corner_out[0], "wall", 1), "len", 1)]

    near = (sum(near_rows(n_dir, W)[-1][::2]), L)
    halos = [wall_in, *strips, *corners]
    first_out, second_out, own_rows = call(
        functools.partial(boundary, n_len, C),
        [vmem] * (5 + 2 * n_dir),
        [(near, vmem)] * 2 + [((2, 6, N, L), vmem)],
        [(48, N, L), near, near],
        "boundary",
    )(*fields, *halos)
    first_in = neighbour_pairs(first_out, 1)
    second_in = neighbour_pairs(second_out, 0)
    qm, bm, be, coarse, surface, patches = call(
        functools.partial(sector, n_len, n_wall, C, electrodes),
        [vmem] * (6 + 2 * n_dir),
        [(field, vmem)] * 3 + [((cells // 8, L), vmem), ((C, L), vmem), ((8, L), vmem)],
        [field, (cells // 2, L)] + [field] * 8,
        "sector",
        work=16 * 10**6,
    )(*fields, *halos, owner_map.reshape(1, electrodes))

    rows = (8, N, L)
    wide = LANES * ((electrodes + LANES - 1) // LANES)
    message = (cells // 8 + C + wide // LANES, L)
    rows_n, rows_p, mine = call(
        functools.partial(correct, electrodes, n_len, n_wall),
        [vmem] * 6,
        [(rows, vmem), (rows, vmem), (message, vmem)],
        [(1, N, L), (wide, L), near, near],
        "correct",
    )(own_rows, first_in, second_in, coarse, surface, patch_ids)

    relative = n_blk in (2, 4)
    moved = [paired(mine, d) for d in range(1, n_blk)] if relative else [lax.all_gather(mine, "blk")]
    base_adj, base_pot = call(
        functools.partial(source_part, n_len, n_wall, C),
        [vmem] * 6,
        [(own, vmem), (own, vmem)],
        [field] * 4 + [(2, N, L)],
        "source_part",
        work=12 * 10**6,
    )(bm, be, rows_n, rows_p, qm, fields[2])
    moved, base_adj = lax.optimization_barrier((moved, base_adj))
    sector_blocks = jnp.stack([mine] + moved) if relative else moved[0]
    compacted = (n_blk, n_len, C, W) == (4, 2, 16, 32)
    if compacted:
        brief, across_wall = call(
            functools.partial(compact, C, W),
            [vmem],
            [((168, L), vmem), ((200, L), vmem)],
            [(W // 4, n_blk * C // 2, L), (W // 8 + 1, n_blk * C // 2, L)],
            "compact",
        )(sector_blocks)
        len_brief = ring(brief, "len", 1)
        blocks = [sector_blocks, len_brief, ring(across_wall, "wall", 1), ring(len_brief, "wall", 1), brief]
    elif n_len == 2:
        here = [sector_blocks, ring(sector_blocks, "len", 1)]
    else:
        gathered = lax.all_gather(sector_blocks, "len")
        here = [gathered[j] for j in range(n_len)]
    if not compacted:
        blocks = here + [ring(x, "wall", 1) for x in here]

    NC1, NL1 = n_blk * C // 2, n_len * L // 2
    planes = n_wall * W // 2
    grids = [(planes // k + 2, NC1, NL1) for k in (1, 1, 2, 2, 4, 4)]
    Q = W // 2 + 2
    tall = (Q * (C + 8) + 16, L)
    taller = ((W + 2) * (C + 8) + 16, L)
    scratch = grids + [(Q * C, NL1), tall, tall, taller, taller, own, own]
    scratch += [(2, n_blk * C, n_len * L), (2, 2, 64, L), pltpu.SemaphoreType.DMA((2, 2))]
    adj_prev, potential, patch_grad = call(
        functools.partial(solve, (n_blk, n_len, n_wall), relative, compacted, C, W),
        [vmem] * (len(blocks) + 4),
        [(own, "any"), (own, "any"), ((1, 2), "smem")],
        scratch,
        "solve",
        room=48 if NC1 * NL1 <= 4096 else 58,
    )(*blocks, base_adj, base_pot, fields[2], patches)
    return adj_prev.reshape(W, C, L), potential.reshape(W, C, L), patch_grad


def solution(mesh):
    field = P(("groups", "wall"), "blk", "len")
    return jax.shard_map(
        body,
        mesh=mesh,
        in_specs=(field, field, field, field, field, P("groups")),
        out_specs=(field, field, P(("groups", "blk", "len", "wall"), None)),
        check_vma=False,
    )
```
